32 devices in a mesh: dp: 2 (over x), blk: 16 (over z, y, core).
Axes of the slice: x: 2, y: 2, z: 4, core: 2. Of those that a mesh axis runs over, the one named last changes fastest.
Arguments:
- byte_embeds: bfloat16 [2, 8192, 768], P('dp', 'blk'), may hold values from -6 to 6
- segments: int32 [2, 8192], P('dp', 'blk'), may hold values from 0 to 7, as said below
- score_weight: bfloat16 [768], replicated, may hold values from -0.4375 to 0.4375
- norm_gain1: bfloat16 [768], replicated, may hold values from 0.5 to 1.5
- w_query: bfloat16 [768, 768], replicated, may hold values from -0.21875 to 0.21875
- w_key: bfloat16 [768, 768], replicated, may hold values from -0.21875 to 0.21875
- w_value: bfloat16 [768, 768], replicated, may hold values from -0.21875 to 0.21875
- w_out: bfloat16 [768, 768], replicated, may hold values from -0.875 to 0.875
- rel_bias: bfloat16 [32, 12], replicated, may hold values from -4 to 4
- norm_gain2: bfloat16 [768], replicated, may hold values from 0.5 to 1.5
- w_gate: bfloat16 [768, 2048], replicated, may hold values from -0.21875 to 0.21875
- w_up: bfloat16 [768, 2048], replicated, may hold values from -0.21875 to 0.21875
- w_down: bfloat16 [2048, 768], replicated, may hold values from -0.1875 to 0.1875
- cotangent: bfloat16 [2, 4096, 768], P('dp', 'blk'), may hold values from -6 to 6
Outputs:
- block_out: bfloat16 [2, 4096, 768], P('dp', 'blk')
- grad_bytes: bfloat16 [2, 8192, 768], P('dp', 'blk')
- grad_score: float32 [768], replicated
- grad_gain1: float32 [768], replicated
- grad_query: float32 [768, 768], P(('dp', 'blk'))
- grad_key: float32 [768, 768], P(('dp', 'blk'))
- grad_value: float32 [768, 768], P(('dp', 'blk'))
- grad_out: float32 [768, 768], P(('dp', 'blk'))
- grad_bias: float32 [32, 12], replicated
- grad_gain2: float32 [768], replicated
- grad_gate: float32 [768, 2048], P(('dp', 'blk'))
- grad_up: float32 [768, 2048], P(('dp', 'blk'))
- grad_down: float32 [2048, 768], P(('dp', 'blk'))
- block_share: float32 [4], replicated
The draws below stay inside these ranges and needn't reach their ends.
Inputs may be any that keep to these rules, and one draw needn't show every extreme that they name: `segments`: segment ids are 0 at each row's first byte and never fall along a row, by steps of one; of rows 2k and 2k + 1, one, chosen by the seed, is a single document and the other holds exactly 8 documents.
All inputs are finite; a program needn't handle non-finite values.
Results may differ from the reference program's by a relative error of at most 0.019.
Values may be sent and summed in bfloat16 or wider, within the bound.
A program may use at most 256 MiB of HBM per device.

```python
import math
from functools import partial
import jax
import jax.numpy as jnp
from jax import lax

D = 768
HEADS = 12
HEAD_DIM = 64
FF = 2048
BUCKETS = 32
MAX_BLOCK = 4
ROWS = 2
ROW_BYTES = 8192
ROW_TOK = 4096


def draw_segments(key, part):
    key = jax.random.fold_in(key, 11)
    start_key, choose_key = jax.random.split(key)
    stride = ROW_BYTES // 8
    offsets = jax.random.randint(start_key, (ROWS, 7), 0, stride)
    starts = jnp.arange(1, 8, dtype=jnp.int32)[None, :] * stride + offsets
    byte_pos = jnp.arange(ROW_BYTES, dtype=jnp.int32)
    segment_ids = jnp.sum((byte_pos[None, :, None] >= starts[:, None, :]).astype(jnp.int32), axis=-1)
    picked = jax.random.randint(choose_key, (ROWS // 2,), 0, 2)
    row_index = jnp.arange(ROWS, dtype=jnp.int32)
    single = row_index % 2 == jnp.repeat(picked, 2)
    return jnp.where(single[:, None], 0, segment_ids).astype(jnp.int32)


def steps_of(rng, dims, pieces, smallest, top_value):
    factor_of = 1.0
    for position, parts in pieces:
        heights = jax.random.uniform(jax.random.fold_in(jax.random.fold_in(rng, 6), position), (parts,), jnp.float32, smallest / len(pieces), top_value / len(pieces))
        factor_of = factor_of * jnp.repeat(jnp.exp(heights), dims[position] // parts).reshape((-1,) + (1,) * (len(dims) - 1 - position))
    return factor_of


def bell_draw(stream_key, dims, scale, reach, cuts=(), held_as=jnp.bfloat16):
    drawn = scale * jax.random.normal(stream_key, dims, jnp.float32)
    if cuts:
        drawn = drawn * steps_of(stream_key, dims, cuts, -0.22, 0.18)
    return jnp.clip(drawn, -reach, reach).astype(held_as)


def setup_inputs(seed: int = 0) -> dict:
    streams_of = jax.random.split(jax.random.key(seed), 15)
    byte_embeds = bell_draw(streams_of[0], (ROWS, ROW_BYTES, D), 1.0, 6.0, ((0, 2), (1, 16)))
    segments = draw_segments(jax.random.fold_in(streams_of[14], 71), 0)
    score_weight = bell_draw(streams_of[2], (D,), (D // 4) ** -0.5, 0.4375)
    norm_gain1 = jnp.clip(1.0 + 0.1 * jax.random.normal(streams_of[3], (D,), jnp.float32), 0.5, 1.5).astype(jnp.bfloat16)
    w_query = bell_draw(streams_of[4], (D, D), D ** -0.5, 0.21875)
    w_key = bell_draw(streams_of[5], (D, D), D ** -0.5, 0.21875)
    w_value = bell_draw(streams_of[6], (D, D), D ** -0.5, 0.21875)
    w_out = bell_draw(streams_of[7], (D, D), (D // 16) ** -0.5, 0.875)
    rel_bias = bell_draw(streams_of[8], (BUCKETS, HEADS), 1.0, 4.0)
    norm_gain2 = jnp.clip(1.0 + 0.1 * jax.random.normal(streams_of[9], (D,), jnp.float32), 0.5, 1.5).astype(jnp.bfloat16)
    w_gate = bell_draw(streams_of[10], (D, FF), D ** -0.5, 0.21875)
    w_up = bell_draw(streams_of[11], (D, FF), D ** -0.5, 0.21875)
    w_down = bell_draw(streams_of[12], (FF, D), (FF // 2) ** -0.5, 0.1875)
    cotangent = bell_draw(streams_of[13], (ROWS, ROW_TOK, D), 1.0, 6.0, ((0, 2), (1, 16)))
    return {"byte_embeds": byte_embeds, "segments": segments, "score_weight": score_weight, "norm_gain1": norm_gain1, "w_query": w_query, "w_key": w_key, "w_value": w_value, "w_out": w_out, "rel_bias": rel_bias, "norm_gain2": norm_gain2, "w_gate": w_gate, "w_up": w_up, "w_down": w_down, "cotangent": cotangent}


PRECISE = lax.Precision.HIGHEST

@jax.custom_vjp
def low(v):
    return lax.optimization_barrier(v.astype(jnp.bfloat16)).astype(jnp.float32)

@jax.custom_vjp
def low_back(v):
    return v

def low_keep(v):
    return (low(v), None)

def low_pass(kept, grad):
    return (grad,)

def back_keep(v):
    return (v, None)

def back_low(kept, grad):
    return (low(grad),)
low.defvjp(low_keep, low_pass)
low_back.defvjp(back_keep, back_low)

def low_both(tensor):
    return low(low_back(tensor))

def buckets_of(relative):
    distance = jnp.abs(relative)
    beyond = jnp.zeros_like(distance)
    for border in (12, 16, 23, 32, 46, 64, 91):
        beyond = beyond + (distance >= border).astype(jnp.int32)
    nearer = jnp.where(distance < 8, distance, 8 + beyond)
    return nearer + BUCKETS // 2 * (relative > 0).astype(jnp.int32)

def rms_norm(values, gain):
    return values * lax.rsqrt(lax.optimization_barrier(jnp.mean(values * values, axis=-1, keepdims=True)) + 1e-06) * gain

def pool_blocks(embeds, segments, block_width):
    row_count, length, width_d = embeds.shape
    padded_len = -(-length // block_width) * block_width
    extra = padded_len - length
    blocks = jnp.pad(embeds, ((0, 0), (0, extra), (0, 0))).reshape(row_count, padded_len // block_width, block_width, width_d)
    labels = jnp.pad(segments, ((0, 0), (0, extra)), constant_values=-1).reshape(row_count, padded_len // block_width, block_width)
    same = (labels[..., :, None] == labels[..., None, :]).astype(jnp.float32)
    weights = same / lax.optimization_barrier(jnp.sum(same, axis=-1, keepdims=True))
    pooled = jnp.einsum('rnij,rnjd->rnid', weights, blocks, precision=PRECISE)
    return pooled.reshape(row_count, padded_len, width_d)[:, :length]

def gbst(embeds, segments, score_weight):
    stacked = jnp.stack([pool_blocks(embeds, segments, block_width) for block_width in range(1, MAX_BLOCK + 1)], axis=2)
    scores = jnp.einsum('rlbd,d->rlb', stacked, score_weight, precision=PRECISE)
    chances = jax.nn.softmax(scores, axis=-1)
    mixed = jnp.einsum('rlb,rlbd->rld', chances, stacked, precision=PRECISE)
    return (0.5 * (mixed[:, 0::2] + mixed[:, 1::2]), chances)

def split_heads(tensor):
    return tensor.reshape(tensor.shape[0], tensor.shape[1], HEADS, HEAD_DIM)

def row_attention(inputs, bias_full):
    queries, key_rows, value_rows, labels = inputs
    raw_scores = jnp.einsum('qhd,khd->hqk', queries, key_rows, precision=PRECISE) * (1.0 / math.sqrt(HEAD_DIM)) + bias_full
    scores = low_back(raw_scores)
    allowed = labels[:, None] == labels[None, :]
    masked = jnp.where(allowed[None], scores, -1e+30)
    chances = low(jax.nn.softmax(masked, axis=-1))
    return jnp.einsum('hqk,khd->qhd', chances, value_rows, precision=PRECISE)

def project(tensor, weight):
    return jnp.einsum('rtd,de->rte', tensor, weight, precision=PRECISE)

def forward(embeds, score_weight, gain1, w_query, w_key, w_value, w_out, rel_bias, gain2, w_gate, w_up, w_down, segments):
    hidden, unused = gbst(embeds, segments, score_weight)
    normed = low(rms_norm(hidden, gain1))
    queries = low_both(project(normed, w_query))
    key_rows = low_both(project(normed, w_key))
    value_rows = low_both(project(normed, w_value))
    positions = jnp.arange(ROW_TOK, dtype=jnp.int32)
    buckets = buckets_of(positions[None, :] - positions[:, None])
    bias_full = jnp.transpose(rel_bias[buckets], (2, 0, 1))
    labels = segments[:, 0::2]
    attended = lax.map(jax.checkpoint(partial(row_attention, bias_full=bias_full)), (split_heads(queries), split_heads(key_rows), split_heads(value_rows), labels))
    attended = low_both(attended.reshape(ROWS, ROW_TOK, D))
    residual = hidden + low_back(project(attended, w_out))
    normed2 = low(rms_norm(residual, gain2))
    gate_proj = low_back(project(normed2, w_gate))
    up_proj = low_back(project(normed2, w_up))
    activated = low(jax.nn.gelu(gate_proj, approximate=True) * up_proj)
    return residual + low_back(project(activated, w_down))

def reference(byte_embeds, segments, score_weight, norm_gain1, w_query, w_key, w_value, w_out, rel_bias, norm_gain2, w_gate, w_up, w_down, cotangent):
    inputs = tuple((operand.astype(jnp.float32) for operand in (byte_embeds, score_weight, norm_gain1, w_query, w_key, w_value, w_out, rel_bias, norm_gain2, w_gate, w_up, w_down)))
    output, pullback = jax.vjp(partial(forward, segments=segments), *inputs)
    gradients = pullback(cotangent.astype(jnp.float32))
    unused, chances = gbst(inputs[0], segments, inputs[1])
    share = lax.optimization_barrier(jnp.mean(chances, axis=(0, 1)))
    return (output.astype(jnp.bfloat16), gradients[0].astype(jnp.bfloat16), gradients[1], gradients[2], gradients[3], gradients[4], gradients[5], gradients[6], gradients[7], gradients[8], gradients[9], gradients[10], gradients[11], share)
```

```python
import functools
import math

import jax
import jax.numpy as jnp
from jax import lax
from jax.experimental import pallas as pl
from jax.experimental.pallas import tpu as pltpu
from jax.sharding import PartitionSpec as P

BUCKETS = 32
MAX_BLOCK = 4
VMEM_BYTES = 60 * 2**20


def extended(shard, sides, width):
    for axis, dim in sides:
        peers, length = (lax.axis_size(axis), shard.shape[dim])
        up = [(i, (i + 1) % peers) for i in range(peers - 1)]
        down = [(j, i) for i, j in up]
        last = lax.slice_in_dim(shard, length - width, length, axis=dim)
        leading = lax.slice_in_dim(shard, 0, width, axis=dim)
        before = lax.ppermute(last, axis, up)
        after = lax.ppermute(leading, axis, down)
        shard = jnp.concatenate([before, shard, after], axis=dim)
    return shard


def buckets_of(relative):
    distance = jnp.abs(relative)
    beyond = jnp.zeros_like(distance)
    for border in (12, 16, 23, 32, 46, 64, 91):
        beyond = beyond + (distance >= border).astype(jnp.int32)
    nearer = jnp.where(distance < 8, distance, 8 + beyond)
    return nearer + BUCKETS // 2 * (relative > 0).astype(jnp.int32)


def rms_norm(values, gain):
    return values * lax.rsqrt(jnp.mean(values * values, axis=-1, keepdims=True) + 1e-06) * gain


def geglu(gate_proj, up_proj):
    return jax.nn.gelu(gate_proj, approximate=True) * up_proj


def pool_masks(labels, base, length):
    positions = jnp.arange(length + 6, dtype=jnp.int32) + base - 3
    centre = labels[:, 3 : 3 + length]
    centre_pos = positions[3 : 3 + length]
    result = []
    for block_width in range(1, MAX_BLOCK + 1):
        pool_terms = []
        for offset in range(1 - block_width, block_width):
            near_labels = labels[:, 3 + offset : 3 + offset + length]
            near_pos = positions[3 + offset : 3 + offset + length]
            same_block = near_pos // block_width == centre_pos // block_width
            keep_mask = jnp.logical_and(near_labels == centre, same_block[None, :])
            pool_terms.append((offset, keep_mask.astype(jnp.float32)))
        counts = sum((entry[1] for entry in pool_terms))
        result.append((pool_terms, counts))
    return result


MESH_ID = pl.DeviceIdType.MESH
GROUPS = 4


def bits_of(size):
    return [1 << p for p in reversed(range(size.bit_length() - 1))]


def bit(value, mask):
    return (value // mask) % 2


def flipped(value, mask):
    return value + mask * (1 - 2 * bit(value, mask))


class Place:
    def __init__(self, shards):
        self.shards = shards
        self.rest_size = shards // GROUPS
        self.dp = lax.axis_index("dp")
        self.blk = lax.axis_index("blk")
        self.row = self.dp % 2
        self.group = self.blk // self.rest_size
        self.rest = self.blk % self.rest_size

    def at(self, row, group, rest):
        return (self.dp - self.row + row, group * self.rest_size + rest)

    def chunk(self, group, rest):
        return group * self.rest_size + rest

    def other_row(self):
        return self.at(1 - self.row, self.group, self.rest)

    def other_rest(self, mask):
        return self.at(self.row, self.group, flipped(self.rest, mask))

    def other_group(self, step):
        return self.at(self.row, (self.group + step) % GROUPS, self.rest)


def greet(targets):
    barrier = pltpu.get_barrier_semaphore()
    for target in targets:
        pl.semaphore_signal(barrier, inc=1, device_id=target, device_id_type=MESH_ID)
    pl.semaphore_wait(barrier, len(targets))


def remote(src, dst, send_sem, recv_sem, target):
    return pltpu.make_async_remote_copy(
        src_ref=src,
        dst_ref=dst,
        send_sem=send_sem,
        recv_sem=recv_sem,
        device_id=target,
        device_id_type=MESH_ID,
    )


def line_and_row(place):
    found = []
    for step in range(GROUPS):
        for flip in range(2):
            if step or flip:
                row = 1 - place.row if flip else place.row
                found.append(place.at(row, (place.group + step) % GROUPS, place.rest))
    return found


def spread_heads(place, q_ref, out_ref, send_sem, recv_sem):
    row_to = place.group // 2
    slot = place.group % 2
    dst = out_ref.at[place.row, slot]
    mine = recv_sem.at[place.row * 2 + slot]
    at_home = row_to == place.row
    for step in range(GROUPS):
        group = (place.group + step) % GROUPS
        src = q_ref.at[group]
        copy = remote(src, dst, send_sem.at[step], mine, place.at(row_to, group, place.rest))
        if step:
            copy.start()
        else:
            pl.when(jnp.logical_not(at_home))(copy.start)
            pl.when(at_home)(pltpu.make_async_copy(src, dst, mine).start)


def spread_heads_wait(place, q_ref, out_ref, send_sem, recv_sem):
    at_home = place.group // 2 == place.row
    for row in range(2):
        for slot in range(2):
            pltpu.make_async_copy(q_ref.at[0], out_ref.at[row, slot], recv_sem.at[row * 2 + slot]).wait()
    for step in range(GROUPS):
        copy = remote(q_ref.at[0], out_ref.at[0, 0], send_sem.at[step], recv_sem.at[0], place.other_row())
        if step:
            copy.wait_send()
        else:
            pl.when(jnp.logical_not(at_home))(copy.wait_send)


def return_heads(place, o_ref, out_ref, send_sem, recv_sem):
    for row in range(2):
        for slot in range(2):
            group = place.row * 2 + slot
            src = o_ref.at[row, slot]
            dst = out_ref.at[place.group]
            mine = recv_sem.at[place.group]
            at_home = jnp.logical_and(place.row == row, place.group == group)
            copy = remote(src, dst, send_sem.at[row * 2 + slot], mine, place.at(row, group, place.rest))
            pl.when(jnp.logical_not(at_home))(copy.start)
            pl.when(at_home)(pltpu.make_async_copy(src, dst, mine).start)


def return_heads_wait(place, o_ref, out_ref, send_sem, recv_sem):
    for group in range(GROUPS):
        pltpu.make_async_copy(o_ref.at[0, 0], out_ref.at[group], recv_sem.at[group]).wait()
    for row in range(2):
        for slot in range(2):
            group = place.row * 2 + slot
            at_home = jnp.logical_and(place.row == row, place.group == group)
            copy = remote(o_ref.at[0, 0], out_ref.at[0], send_sem.at[row * 2 + slot], recv_sem.at[0], place.other_row())
            pl.when(jnp.logical_not(at_home))(copy.wait_send)


def spread_kernel(shards, q_ref, out_ref, send_sem, recv_sem):
    place = Place(shards)
    greet(line_and_row(place))
    spread_heads(place, q_ref, out_ref, send_sem, recv_sem)
    spread_heads_wait(place, q_ref, out_ref, send_sem, recv_sem)


def return_kernel(shards, o_ref, out_ref, send_sem, recv_sem):
    place = Place(shards)
    greet(line_and_row(place))
    return_heads(place, o_ref, out_ref, send_sem, recv_sem)
    return_heads_wait(place, o_ref, out_ref, send_sem, recv_sem)


def move_heads(kernel, lead, shards, ident, packed):
    rows, lanes = packed.shape[-2:]
    return pl.pallas_call(
        functools.partial(kernel, shards),
        out_shape=jax.ShapeDtypeStruct(lead + (rows, lanes), packed.dtype),
        in_specs=[pl.BlockSpec(memory_space=pltpu.VMEM)],
        out_specs=pl.BlockSpec(memory_space=pltpu.VMEM),
        scratch_shapes=[pltpu.SemaphoreType.DMA((4,)), pltpu.SemaphoreType.DMA((4,))],
        compiler_params=pltpu.CompilerParams(collective_id=ident, has_side_effects=True, vmem_limit_bytes=VMEM_BYTES),
        name="move_heads_%d" % ident,
    )(packed)


def gather_kernel(shards, q_ref, kv_ref, label_ref, qo_ref, kvo_ref, labo_ref, q_send, q_recv, z_send, far_send, core_send, kv_recv, own_sem, lab_send, lab_recv):
    place = Place(shards)
    tokens = kv_ref.shape[1]
    rest_bits = bits_of(place.rest_size)
    core, far = rest_bits[-1], ["row"] + rest_bits[:-1]
    greet(line_and_row(place) + [place.other_rest(mask) for mask in rest_bits])

    dims = [("row", 1)] + [("blk", m) for m in bits_of(shards)]
    lab_index = [place.row] + [bit(place.blk, m) for _, m in dims[1:]]
    lab_order = list(range(len(dims)))

    def lab_copy(stage):
        index = tuple(slice(None) if p in lab_order[:stage] else lab_index[p] for p in range(len(dims)))
        axis, mask = dims[lab_order[stage]]
        target = place.other_row() if axis == "row" else (place.dp, flipped(place.blk, mask))
        there = labo_ref.at[index]
        return remote(there, there, lab_send.at[stage], lab_recv.at[stage], target)

    labo_ref[tuple(lab_index)] = label_ref[...]
    lab_copy(0).start()
    lab_stage = 0

    def slot(row, group, rest):
        start = pl.multiple_of(place.chunk(group, rest) * tokens, tokens)
        return kvo_ref.at[row, pl.ds(start, tokens)]

    def held(dz, offset, core_off):
        row = 1 - place.row if offset & 1 else place.row
        rest = place.rest
        for p, mask in enumerate(far[1:]):
            if offset >> (p + 1) & 1:
                rest = flipped(rest, mask)
        if core_off:
            rest = flipped(rest, core)
        return slot(row, (place.group + dz) % GROUPS, rest)

    count = 1 << len(far)

    def sem_of(dz, offset, core_off):
        return kv_recv.at[(core_off * count + offset) * GROUPS + dz]

    own = pltpu.make_async_copy(kv_ref.at[place.group], held(0, 0, 0), own_sem)
    own.start()
    waits = []
    for step in (1, 3, 2):
        copy = remote(kv_ref.at[(place.group + step) % GROUPS], held(0, 0, 0), z_send.at[step], sem_of((GROUPS - step) % GROUPS, 0, 0), place.other_group(step))
        copy.start()
        waits.append(copy)
    spread_heads(place, q_ref, qo_ref, q_send, q_recv)

    used = 0
    events = sorted(((dz, off) for dz in range(GROUPS) for off in range(count)), key=lambda e: (bin(e[1]).count("1"), (0, 1, 3, 2).index(e[0])))
    core_target = place.other_rest(core)
    for dz, off in events:
        here = held(dz, off, 0)
        if dz == 0 and off == 0:
            src = kv_ref.at[place.group]
        else:
            remote(here, here, z_send.at[0], sem_of(dz, off, 0), core_target).wait_recv()
            src = here
        order = [(p + dz) % len(far) for p in range(len(far))]
        last = max([order.index(p) for p in range(len(far)) if off >> p & 1], default=-1)
        for p in order[last + 1 :]:
            target = place.other_row() if p == 0 else place.other_rest(far[p])
            copy = remote(src, here, far_send.at[used], sem_of(dz, off | 1 << p, 0), target)
            copy.start()
            waits.append(copy)
            used += 1
        copy = remote(src, here, core_send.at[off * GROUPS + dz], sem_of(dz, off, 1), core_target)
        copy.start()
        waits.append(copy)
        if lab_stage < len(dims):
            lab_copy(lab_stage).wait()
            lab_stage += 1
            if lab_stage < len(dims):
                lab_copy(lab_stage).start()
    for dz, off in events:
        here = held(dz, off, 1)
        remote(here, here, z_send.at[0], sem_of(dz, off, 1), core_target).wait_recv()
    own.wait()
    for copy in waits:
        copy.wait_send()
    spread_heads_wait(place, q_ref, qo_ref, q_send, q_recv)


def gather_all(shards, q_packed, kv_parts, labels):
    tokens, width = kv_parts.shape[1:]
    far = 1 + len(bits_of(shards // GROUPS)) - 1
    count = 1 << far
    nbits = 1 + len(bits_of(shards))
    sem = pltpu.SemaphoreType.DMA
    return pl.pallas_call(
        functools.partial(gather_kernel, shards),
        out_shape=(
            jax.ShapeDtypeStruct((2, 2) + q_packed.shape[1:], q_packed.dtype),
            jax.ShapeDtypeStruct((2, shards * tokens, width), kv_parts.dtype),
            jax.ShapeDtypeStruct((2,) * nbits + labels.shape, labels.dtype),
        ),
        in_specs=[pl.BlockSpec(memory_space=pltpu.VMEM)] * 3,
        out_specs=(pl.BlockSpec(memory_space=pltpu.VMEM),) * 3,
        scratch_shapes=[
            sem((4,)), sem((4,)), sem((GROUPS,)), sem((GROUPS * (count - 1),)), sem((GROUPS * count,)), sem((GROUPS * count * 2,)),
            sem, sem((nbits,)), sem((nbits,)),
        ],
        compiler_params=pltpu.CompilerParams(collective_id=1, has_side_effects=True, vmem_limit_bytes=VMEM_BYTES),
        name="gather_keys",
    )(q_packed, kv_parts, labels)


def add_blocks(dst_ref, src_ref, index, shape):
    lead = shape[:-2]
    total = math.prod(lead)

    def one(step, _):
        place, left = [], step
        for size in reversed(lead):
            place.append(left % size)
            left = left // size
        place = tuple(reversed(place))
        full, k = [], 0
        for entry in index:
            if entry is None:
                full.append(place[k])
                k += 1
            else:
                full.append(entry)
        mine = src_ref[tuple(full)].astype(jnp.float32)
        dst_ref[place] = (dst_ref[place].astype(jnp.float32) + mine).astype(dst_ref.dtype)
        return 0

    lax.fori_loop(0, total, one, 0)


def reduce_kernel(shards, q_ref, kv_ref, qo_ref, kvo_ref, q_send, q_recv, send_sem, recv_sem, z_send, z_recv, *bufs):
    place = Place(shards)
    rest_bits = bits_of(place.rest_size)
    greet(line_and_row(place) + [place.other_rest(mask) for mask in rest_bits])
    return_heads(place, q_ref, qo_ref, q_send, q_recv)
    ndim = 1 + len(rest_bits)
    own = [place.row] + [bit(place.rest, m) for m in rest_bits]
    targets = [place.other_row()] + [place.other_rest(m) for m in rest_bits]
    state = {}

    def plan(group_step):
        far = list(range(ndim - 1))
        turn = group_step % len(far)
        return [ndim - 1] + far[turn:] + far[:turn]

    def copy_of(step, stage):
        order = plan(step)
        group = (place.group + step) % GROUPS
        done = order[:stage]
        p_now = order[stage]
        buf = bufs[stage].at[step]
        if stage == 0:
            index = (p_index(group, done, p_now))
            src = kv_ref.at[index]
        else:
            kept = [p for p in range(ndim) if p not in done]
            src = bufs[stage - 1].at[(step,) + tuple(1 - own[p] if p == p_now else slice(None) for p in kept)]
        return remote(src, buf, send_sem.at[stage, step], recv_sem.at[stage, step], targets[p_now])

    def p_index(group, done, p_now):
        index = [slice(None)] * ndim
        index[p_now] = 1 - own[p_now]
        return (index[0], group) + tuple(index[1:])

    def absorb(step, stage):
        order = plan(step)
        done, p_now = order[:stage], order[stage]
        buf = bufs[stage].at[step]
        group = (place.group + step) % GROUPS
        if stage == 0:
            index = [None] * ndim
            index[p_now] = own[p_now]
            add_blocks(buf, kv_ref, (index[0], group) + tuple(index[1:]), buf.shape)
        else:
            kept = [p for p in range(ndim) if p not in done]
            index = tuple(own[p] if p == p_now else None for p in kept)
            add_blocks(buf, bufs[stage - 1].at[step], index, buf.shape)

    steps = (2, 1, 3, 0)
    for step in steps:
        copy_of(step, 0).start()
    for stage in range(ndim):
        for step in steps:
            copy_of(step, stage).wait()
            absorb(step, stage)
            if stage < ndim - 1:
                copy_of(step, stage + 1).start()
            elif step:
                remote(bufs[stage].at[step], kvo_ref.at[place.group], z_send.at[step], z_recv.at[(GROUPS - step) % GROUPS], place.other_group(step)).start()
            else:
                kvo_ref[place.group] = bufs[stage][step]
    for step in (1, 3, 2):
        there = kvo_ref.at[(place.group + step) % GROUPS]
        remote(bufs[ndim - 1].at[step], there, z_send.at[step], z_recv.at[step], place.other_group(step)).wait()
    return_heads_wait(place, q_ref, qo_ref, q_send, q_recv)


def reduce_all(shards, q_packed, kv_sums):
    tokens_all, width = kv_sums.shape[1:]
    tokens = tokens_all // shards
    rest_bits = bits_of(shards // GROUPS)
    ndim = 1 + len(rest_bits)
    sem = pltpu.SemaphoreType.DMA
    return pl.pallas_call(
        functools.partial(reduce_kernel, shards),
        out_shape=(
            jax.ShapeDtypeStruct((GROUPS,) + q_packed.shape[2:], q_packed.dtype),
            jax.ShapeDtypeStruct((GROUPS, tokens, width), kv_sums.dtype),
        ),
        in_specs=[pl.BlockSpec(memory_space=pltpu.VMEM)] * 2,
        out_specs=(pl.BlockSpec(memory_space=pltpu.VMEM),) * 2,
        scratch_shapes=[sem((4,)), sem((4,)), sem((ndim, GROUPS)), sem((ndim, GROUPS)), sem((GROUPS,)), sem((GROUPS,))]
        + [pltpu.VMEM((GROUPS,) + (2,) * (ndim - 1 - s) + (tokens, width), kv_sums.dtype) for s in range(ndim)],
        compiler_params=pltpu.CompilerParams(collective_id=2, has_side_effects=True, vmem_limit_bytes=VMEM_BYTES),
        name="reduce_keys",
    )(q_packed, kv_sums.reshape((2, GROUPS) + (2,) * len(rest_bits) + (tokens, width)))


def weights_kernel(orders, axes, *refs):
    streams = len(orders) - 1
    ins, small_ref = refs[:streams], refs[streams]
    outs, small_out = refs[streams + 1 : 2 * streams + 1], refs[2 * streams + 1]
    send_sem, recv_sem = refs[2 * streams + 2 : 2 * streams + 4]
    bufs = refs[2 * streams + 4 :]
    ndim = len(axes)
    at = {"dp": lax.axis_index("dp"), "blk": lax.axis_index("blk")}
    own = [bit(at[axis], mask) for axis, mask in axes]

    def target(p):
        axis, mask = axes[p]
        moved = dict(at)
        moved[axis] = flipped(at[axis], mask)
        return (moved["dp"], moved["blk"])

    greet([target(p) for p in range(ndim)])
    small_bufs = bufs[streams * ndim]
    small_out[...] = small_ref[...]

    def parts(s, stage):
        order = orders[s]
        if s == streams:
            src = small_ref if stage == 0 else small_bufs.at[1, stage - 1]
            return src, small_bufs.at[0, stage], None
        kept = [p for p in range(ndim) if p not in order[:stage]]
        src = ins[s] if stage == 0 else bufs[s * ndim + stage - 1]
        return src, bufs[s * ndim + stage], kept

    def copy_of(s, stage):
        src, buf, kept = parts(s, stage)
        p_now = orders[s][stage]
        if kept is not None:
            src = src.at[tuple(1 - own[p] if p == p_now else slice(None) for p in kept)]
        return remote(src, buf, send_sem.at[s, stage], recv_sem.at[s, stage], target(p_now))

    def absorb(s, stage):
        src, buf, kept = parts(s, stage)
        if kept is None:
            total = src[...] + buf[...]
            if stage == ndim - 1:
                small_out[...] = total
            else:
                small_bufs[1, stage] = total
            return
        p_now = orders[s][stage]
        index = tuple(own[p] if p == p_now else None for p in kept)
        if stage == ndim - 1:
            outs[s][...] = buf[...].astype(jnp.float32) + src[index[0]].astype(jnp.float32)
        else:
            add_blocks(buf, src, index, buf.shape)

    for s in range(streams + 1):
        copy_of(s, 0).start()
    for stage in range(ndim):
        for s in range(streams + 1):
            copy_of(s, stage).wait()
            absorb(s, stage)
            if stage < ndim - 1:
                copy_of(s, stage + 1).start()


def reduce_weights(shape, blocks, small):
    axes = [("dp", m) for m in bits_of(shape["dp"])] + [("blk", m) for m in bits_of(shape["blk"])]
    ndim = len(axes)
    rest_bits = bits_of(shape["blk"] // GROUPS)
    core = ndim - 1
    across = list(range(len(bits_of(shape["dp"]))))
    up = [ndim - len(rest_bits) + p for p in range(len(rest_bits) - 1)]
    along = [ndim - len(rest_bits) - 1, ndim - len(rest_bits) - 2]
    first = [core] + across + up + along
    second = [core] + up + across + along
    orders = [first if s % 2 == 0 else second for s in range(len(blocks))] + [first]
    sem = pltpu.SemaphoreType.DMA
    scratch = []
    for block in blocks:
        rows, cols = block.shape[-2:]
        scratch += [pltpu.VMEM((2,) * (ndim - 1 - s) + (rows, cols), block.dtype) for s in range(ndim)]
    scratch.append(pltpu.VMEM((2, ndim) + small.shape, small.dtype))
    wide = [block.reshape((2,) * ndim + block.shape[-2:]) for block in blocks]
    found = pl.pallas_call(
        functools.partial(weights_kernel, orders, axes),
        out_shape=tuple(jax.ShapeDtypeStruct(b.shape[-2:], jnp.float32) for b in blocks) + (jax.ShapeDtypeStruct(small.shape, small.dtype),),
        in_specs=[pl.BlockSpec(memory_space=pltpu.VMEM)] * (len(blocks) + 1),
        out_specs=(pl.BlockSpec(memory_space=pltpu.VMEM),) * (len(blocks) + 1),
        scratch_shapes=[sem((len(blocks) + 1, ndim)), sem((len(blocks) + 1, ndim))] + scratch,
        compiler_params=pltpu.CompilerParams(collective_id=3, has_side_effects=True, vmem_limit_bytes=VMEM_BYTES),
        name="reduce_weights",
    )(*wide, small)
    return found[:-1], found[-1]


TQ = 256
TK = 512
NEAR_ROWS = 448
NEG = -1e30
FIRST_MAX = -1e29
NT = (((1,), (1,)), ((), ()))
NN = (((1,), (0,)), ((), ()))
BORDERS = (12, 16, 23, 32, 46, 64, 91)


def mxu(left, right, dims=NN):
    return lax.dot_general(left, right, dims, preferred_element_type=jnp.float32)


def turned(tile):
    return jnp.concatenate([tile[:, 64:], tile[:, :64]], axis=1)


def spread_lanes(packed, high):
    lane = lax.broadcasted_iota(jnp.int32, (1, 128), 1)
    keep = lane >= 64 if high else lane < 64
    zero = jnp.zeros((), packed.dtype)
    pair, last = packed[0:TQ], packed[TQ:]
    pick = lambda tile: jnp.where(keep, tile, zero)
    if high:
        return [pick(turned(pair)), pick(pair), jnp.concatenate([pick(turned(last)), pick(last)], axis=0)]
    return [pick(pair), pick(turned(pair)), jnp.concatenate([pick(last), pick(turned(last))], axis=0)]


def join_heads(parts):
    half = TQ // 2
    top = jnp.concatenate([parts[0], parts[1]], axis=1)
    low = jnp.concatenate([parts[2][:half], parts[2][half:]], axis=1)
    return jnp.concatenate([top, low], axis=0)


def valid_mask(se_ref, r, i, k0):
    kpos = k0 + lax.broadcasted_iota(jnp.int32, (TK, TQ), 0)
    return jnp.logical_and(kpos >= se_ref[r, i, 0:1, :], kpos < se_ref[r, i, 1:2, :])


def near_buckets(first, rows, parity):
    relative = (
        first - TK + TQ * parity
        + lax.broadcasted_iota(jnp.int32, (rows, TQ), 0)
        - lax.broadcasted_iota(jnp.int32, (rows, TQ), 1)
    )
    return buckets_of(relative)


def make_bias(table, parity, bias_ref):
    heads = bias_ref.shape[0]
    for h in range(heads):
        bias_ref[h, 0] = jnp.full((TK, TQ), table[h, 15], jnp.float32).astype(jnp.bfloat16)
        bias_ref[h, 3] = jnp.full((TK, TQ), table[h, 31], jnp.float32).astype(jnp.bfloat16)
    for tile in range(2):
        def rows(step, _):
            start = pl.multiple_of(step * 32, 32)
            which = near_buckets(tile * TK + start, 32, parity)
            for h in range(heads):
                value = jnp.zeros((32, TQ), jnp.float32)
                for b in range(BUCKETS):
                    value = jnp.where(which == b, table[h, b], value)
                bias_ref[h, tile + 1, pl.ds(start, 32)] = value.astype(jnp.bfloat16)
            return 0
        lax.fori_loop(0, TK // 32, rows, 0)


def tile_kind(bounds, r, i, t):
    slot = jnp.clip(t - bounds[r, i, 2] + 1, 0, 3)
    away = jnp.logical_or(slot == 0, slot == 3)
    inside = jnp.logical_and(t >= bounds[r, i, 3], t < bounds[r, i, 4])
    return slot, jnp.logical_and(away, inside)


def fwd_kernel(bounds, table, q_ref, kv_ref, se_ref, o_ref, keep_ref, lse_ref, bias_ref, vt, acc, mx, qp):
    heads = lse_ref.shape[2]
    make_bias(table, bounds[0, 0, 5], bias_ref)
    for r in range(2):
        for i in range(2):
            for h, tile in enumerate(spread_lanes(q_ref[r, i], False)):
                qp[r, i, h] = tile

    def row_body(r, _):
        lo_all = jnp.minimum(bounds[r, 0, 0], bounds[r, 1, 0])
        hi_all = jnp.maximum(bounds[r, 0, 1], bounds[r, 1, 1])

        def turn(t, _):
            k0 = pl.multiple_of(t * TK, TK)
            for h in range(heads):
                tile = kv_ref[r, pl.ds(k0, TK), h * 128 : h * 128 + 128]
                vt[h, 0:64, pl.ds(k0, TK)] = tile.T[64:128, :]
                vt[h, 64:80, pl.ds(k0, TK)] = jnp.ones((16, TK), jnp.bfloat16)
            return 0

        lax.fori_loop(lo_all, hi_all, turn, 0)

        def q_body(i, _):
            acc[...] = jnp.zeros_like(acc)
            mx[...] = jnp.full_like(mx, FIRST_MAX)

            def tile_body(t, _):
                k0 = pl.multiple_of(t * TK, TK)
                slot, plain = tile_kind(bounds, r, i, t)

                def scores(h):
                    return mxu(kv_ref[r, pl.ds(k0, TK), h * 128 : h * 128 + 128], qp[r, i, h], NT)

                def finish(h, s, b):
                    m_old = mx[h]
                    m_new = jnp.maximum(m_old, jnp.max(s, axis=0, keepdims=True) + b)
                    p = jnp.exp(s - (m_new - b)).astype(jnp.bfloat16)
                    mx[h] = m_new
                    acc[h] = acc[h] * jnp.exp(m_old - m_new) + mxu(vt[h, :, pl.ds(k0, TK)], p)

                @pl.when(plain)
                def _():
                    found = [scores(h) for h in range(heads)]
                    for h in range(heads):
                        finish(h, found[h], jnp.where(slot == 0, table[h, 15], table[h, 31]))

                @pl.when(jnp.logical_not(plain))
                def _():
                    ok = valid_mask(se_ref, r, i, k0)
                    for h in range(heads):
                        s = scores(h) + bias_ref[h, slot].astype(jnp.float32)
                        finish(h, jnp.where(ok, s, NEG), 0.0)

                return 0

            lax.fori_loop(bounds[r, i, 0], bounds[r, i, 1], tile_body, 0)
            parts = []
            for h in range(heads):
                total = acc[h, 64:65, :]
                parts.append((acc[h, 0:64, :] / total).T)
                lse_ref[r, i, h] = mx[h] + jnp.log(total)
            joined = join_heads(parts)
            o_ref[r, i] = joined.astype(jnp.bfloat16)
            keep_ref[r, i] = joined
            return 0

        lax.fori_loop(0, 2, q_body, 0)
        return 0

    lax.fori_loop(0, 2, row_body, 0)


SMEM_SPEC = pl.BlockSpec(memory_space=pltpu.SMEM)
VMEM_SPEC = pl.BlockSpec(memory_space=pltpu.VMEM)


def attention(bounds, table, q, kv, se):
    heads, n = kv.shape[2] // 128, kv.shape[1]
    packed = q.shape
    return pl.pallas_call(
        fwd_kernel,
        out_shape=(
            jax.ShapeDtypeStruct(packed, jnp.bfloat16),
            jax.ShapeDtypeStruct(packed, jnp.float32),
            jax.ShapeDtypeStruct((2, 2, heads, 1, TQ), jnp.float32),
            jax.ShapeDtypeStruct((heads, 4, TK, TQ), jnp.bfloat16),
        ),
        in_specs=[SMEM_SPEC] * 2 + [VMEM_SPEC] * 3,
        out_specs=(VMEM_SPEC,) * 4,
        scratch_shapes=[
            pltpu.VMEM((heads, 80, n), jnp.bfloat16),
            pltpu.VMEM((heads, 80, TQ), jnp.float32),
            pltpu.VMEM((heads, 1, TQ), jnp.float32),
            pltpu.VMEM((2, 2, heads, TQ, 128), jnp.bfloat16),
        ],
        compiler_params=pltpu.CompilerParams(vmem_limit_bytes=VMEM_BYTES),
        name="attention",
    )(bounds, table, q, kv, se)


def bwd_kernel(bounds, table, q_ref, do_ref, keep_ref, kv_ref, bias_ref, se_ref, lse_ref,
               dq_ref, dkv_ref, tab_ref, kt, dqt, dkv, grid, side, qp, dp_ref, delta):
    heads = lse_ref.shape[2]
    n = kv_ref.shape[1]
    grid[...] = jnp.zeros_like(grid)
    side[...] = jnp.zeros_like(side)
    for r in range(2):
        for i in range(2):
            for h, tile in enumerate(spread_lanes(q_ref[r, i], False)):
                qp[r, i, h] = tile
            for h, tile in enumerate(spread_lanes(do_ref[r, i], True)):
                dp_ref[r, i, h] = tile
            prod = (do_ref[r, i].astype(jnp.float32) * keep_ref[r, i]).T
            top, low = prod[:, 0:TQ], prod[:, TQ:]
            delta[r, i, 0] = jnp.sum(top[0:64], axis=0, keepdims=True)
            delta[r, i, 1] = jnp.sum(top[64:128], axis=0, keepdims=True)
            delta[r, i, 2] = jnp.concatenate(
                [jnp.sum(low[0:64], axis=0, keepdims=True), jnp.sum(low[64:128], axis=0, keepdims=True)], axis=1
            )

    def row_body(r, _):
        lo_all = jnp.minimum(bounds[r, 0, 0], bounds[r, 1, 0])
        hi_all = jnp.maximum(bounds[r, 0, 1], bounds[r, 1, 1])

        def clear(t, _):
            k0 = pl.multiple_of(t * TK, TK)
            for h in range(heads):
                dkv[h, pl.ds(k0, TK), :] = jnp.zeros((TK, 128), jnp.float32)
            return 0

        lax.fori_loop(0, n // TK, clear, 0)

        def turn(t, _):
            k0 = pl.multiple_of(t * TK, TK)
            for h in range(heads):
                tile = kv_ref[r, pl.ds(k0, TK), h * 128 : h * 128 + 128]
                kt[h, 0:64, pl.ds(k0, TK)] = tile.T[0:64, :]
                kt[h, 64:80, pl.ds(k0, TK)] = jnp.ones((16, TK), jnp.bfloat16)
            return 0

        lax.fori_loop(lo_all, hi_all, turn, 0)

        def q_body(i, _):
            dqt[...] = jnp.zeros_like(dqt)

            def tile_body(t, _):
                k0 = pl.multiple_of(t * TK, TK)
                slot, plain = tile_kind(bounds, r, i, t)

                def finish(h, p, ds, where):
                    ds_low = ds.astype(jnp.bfloat16)
                    two = jnp.concatenate([ds_low, p.astype(jnp.bfloat16)], axis=1)
                    both = jnp.concatenate([qp[r, i, h], dp_ref[r, i, h]], axis=0)
                    dkv[h, pl.ds(k0, TK), :] += mxu(two, both)
                    dqt[h, where] += mxu(kt[h, :, pl.ds(k0, TK)], ds_low)

                def products(h):
                    tile = kv_ref[r, pl.ds(k0, TK), h * 128 : h * 128 + 128]
                    return mxu(tile, qp[r, i, h], NT), mxu(tile, dp_ref[r, i, h], NT)

                @pl.when(plain)
                def _():
                    for h in range(heads):
                        s, d_probs = products(h)
                        p = jnp.exp(s - (lse_ref[r, i, h] - jnp.where(slot == 0, table[h, 15], table[h, 31])))
                        finish(h, p, p * (d_probs - delta[r, i, h]), jnp.where(slot == 0, 0, 2))

                @pl.when(jnp.logical_not(plain))
                def _():
                    ok = valid_mask(se_ref, r, i, k0)
                    for h in range(heads):
                        s, d_probs = products(h)
                        s = s + bias_ref[h, slot].astype(jnp.float32)
                        p = jnp.where(ok, jnp.exp(jnp.where(ok, s, NEG) - lse_ref[r, i, h]), 0.0)
                        ds = p * (d_probs - delta[r, i, h])
                        grid[h, slot] += ds
                        finish(h, p, ds, 1)

                return 0

            lax.fori_loop(bounds[r, i, 0], bounds[r, i, 1], tile_body, 0)
            parts = []
            for h in range(heads):
                parts.append((dqt[h, 0, 0:64] + dqt[h, 1, 0:64] + dqt[h, 2, 0:64]).T * 0.125)
                side[h, 0:1] += dqt[h, 0, 64:65]
                side[h, 1:2] += dqt[h, 2, 64:65]
            dq_ref[r, i] = join_heads(parts).astype(jnp.bfloat16)
            return 0

        lax.fori_loop(0, 2, q_body, 0)

        def put(t, _):
            k0 = pl.multiple_of(t * TK, TK)
            for h in range(heads):
                dkv_ref[r, pl.ds(k0, TK), h * 128 : h * 128 + 128] = dkv[h, pl.ds(k0, TK), :].astype(jnp.bfloat16)
            return 0

        lax.fori_loop(0, n // TK, put, 0)
        return 0

    lax.fori_loop(0, 2, row_body, 0)

    parity = bounds[0, 0, 5]
    tab_ref[...] = jnp.zeros_like(tab_ref)
    for h in range(heads):
        tab_ref[h, 15:16] = side[h, 0:1] + jnp.sum(grid[h, 0], axis=0, keepdims=True)
        tab_ref[h, 31:32] = side[h, 1:2] + jnp.sum(grid[h, 3], axis=0, keepdims=True)

    first = 13 - 8 * parity
    count = NEAR_ROWS // 32

    def block(h, step):
        tile = step // (TK // 32)
        start = pl.multiple_of((step % (TK // 32)) * 32, 32)
        return grid[h, tile + 1, pl.ds(start, 32)]

    def outer(bucket):
        def one(step, _):
            for h in range(heads):
                tab_ref[h, bucket : bucket + 1] += jnp.sum(block(h, step), axis=0, keepdims=True)
            return 0
        return one

    lax.fori_loop(0, first, outer(15), 0)
    lax.fori_loop(first + count, 2 * TK // 32, outer(31), 0)

    def inner(step, _):
        which = near_buckets(step * 32, 32, parity)
        for b in range(BUCKETS):
            here = which == b
            for h in range(heads):
                tab_ref[h, b : b + 1] += jnp.sum(jnp.where(here, block(h, step), 0.0), axis=0, keepdims=True)
        return 0

    lax.fori_loop(first, first + count, inner, 0)


def attention_back(bounds, table, q, do, keep, kv, bias, se, lse):
    heads, n = kv.shape[2] // 128, kv.shape[1]
    return pl.pallas_call(
        bwd_kernel,
        out_shape=(
            jax.ShapeDtypeStruct(q.shape, jnp.bfloat16),
            jax.ShapeDtypeStruct(kv.shape, jnp.bfloat16),
            jax.ShapeDtypeStruct((heads, BUCKETS, TQ), jnp.float32),
        ),
        in_specs=[SMEM_SPEC] * 2 + [VMEM_SPEC] * 7,
        out_specs=(VMEM_SPEC,) * 3,
        scratch_shapes=[
            pltpu.VMEM((heads, 80, n), jnp.bfloat16),
            pltpu.VMEM((heads, 3, 80, TQ), jnp.float32),
            pltpu.VMEM((heads, n, 128), jnp.float32),
            pltpu.VMEM((heads, 4, TK, TQ), jnp.float32),
            pltpu.VMEM((heads, 2, TQ), jnp.float32),
            pltpu.VMEM((2, 2, heads, TQ, 128), jnp.bfloat16),
            pltpu.VMEM((2, 2, heads, TQ, 128), jnp.bfloat16),
            pltpu.VMEM((2, 2, heads, 1, TQ), jnp.float32),
        ],
        compiler_params=pltpu.CompilerParams(vmem_limit_bytes=VMEM_BYTES),
        name="attention_back",
    )(bounds, table, q, do, keep, kv, bias, se, lse)


def pack_heads(array):
    tokens, width = array.shape
    parts = jnp.transpose(array.reshape(tokens, GROUPS, width // GROUPS), (1, 0, 2))
    half = tokens // 2
    last = jnp.concatenate([parts[:, :half, 128:], parts[:, half:, 128:]], axis=2)
    return jnp.concatenate([parts[:, :, :128], last], axis=1)


def unpack_heads(packed):
    rows = packed.shape[1]
    tokens = rows * 2 // 3
    last = packed[:, tokens:]
    last = jnp.concatenate([last[:, :, :64], last[:, :, 64:]], axis=1)
    parts = jnp.concatenate([packed[:, :tokens], last], axis=2)
    return jnp.transpose(parts, (1, 0, 2)).reshape(tokens, -1)


def body(
    byte_embeds,
    segments,
    score_weight,
    norm_gain1,
    w_query,
    w_key,
    w_value,
    w_out,
    rel_bias,
    norm_gain2,
    w_gate,
    w_up,
    w_down,
    cotangent,
):
    row_count, length, width_d = byte_embeds.shape
    tokens = length // 2
    shards = lax.axis_size("blk")
    devices_all = shards * lax.axis_size("dp")
    position = lax.axis_index("blk")
    base = position * length
    head_count = rel_bias.shape[1]
    head_dim = width_d // head_count
    score_scale = 1.0 / math.sqrt(head_dim)
    bias_table = rel_bias.astype(jnp.float32)
    score_vec = score_weight.astype(jnp.float32)
    rim_bytes = extended(byte_embeds, (("blk", 1),), 2)
    padded = jnp.pad(rim_bytes.astype(jnp.float32), ((0, 0), (1, 1), (0, 0)))
    rim_labels = extended(segments + 1, (("blk", 1),), 2)
    labels_pad = jnp.pad(rim_labels, ((0, 0), (1, 1)))
    masks_all = pool_masks(labels_pad, base, length)
    pools = []
    for pool_terms, counts in masks_all:
        summed = sum(
            (
                keep_mask[:, :, None] * padded[:, 3 + offset : 3 + offset + length]
                for offset, keep_mask in pool_terms
            )
        )
        pools.append(summed / counts[:, :, None])
    stacked = jnp.stack(pools, axis=2)
    block_scores = jnp.sum(stacked * score_vec, axis=-1)
    block_probs = jax.nn.softmax(block_scores, axis=-1)
    mixed = jnp.sum(block_probs[..., None] * stacked, axis=2)
    hidden = 0.5 * (mixed[:, 0::2] + mixed[:, 1::2])
    tok_labels = segments[:, 0::2]
    gain_one = norm_gain1.astype(jnp.float32)
    normed1, norm1_back = jax.vjp(rms_norm, hidden, gain_one)
    n1_low = normed1.astype(jnp.bfloat16)
    query_low = jnp.dot(n1_low, w_query, preferred_element_type=jnp.float32).astype(jnp.bfloat16)
    key_low = jnp.dot(n1_low, w_key, preferred_element_type=jnp.float32).astype(jnp.bfloat16)
    value_low = jnp.dot(n1_low, w_value, preferred_element_type=jnp.float32).astype(jnp.bfloat16)
    shape = {"dp": lax.axis_size("dp"), "blk": shards}
    group = position // (shards // GROUPS)
    rest = position % (shards // GROUPS)
    row = lax.axis_index("dp") % 2
    group_heads = head_count // GROUPS
    q_packed = pack_heads(query_low[0] * jnp.bfloat16(score_scale))
    kv_parts = jnp.stack([key_low.reshape(tokens, head_count, head_dim), value_low.reshape(tokens, head_count, head_dim)], axis=2)
    kv_parts = jnp.transpose(kv_parts.reshape(tokens, GROUPS, group_heads * 2 * head_dim), (1, 0, 2))
    label_block = jnp.pad(tok_labels.reshape(tokens // 128, 128), ((0, 8 - tokens // 128), (0, 0)))
    q_all, kv_all, labels_all = gather_all(shards, q_packed, kv_parts, label_block)
    labels_all = labels_all.reshape(2, shards, 8, 128)[:, :, : tokens // 128].reshape(2, shards * tokens)
    ids = jnp.arange(8, dtype=jnp.int32)
    counts = jnp.sum((labels_all[:, None, :] == ids[None, :, None]).astype(jnp.int32), axis=2)
    ends = jnp.sum(jnp.where(ids[None, :] <= ids[:, None], counts[:, None, :], 0), axis=2)
    begins = ends - counts
    rest_size = shards // GROUPS
    query_labels = jnp.stack(
        [lax.dynamic_slice_in_dim(labels_all, ((2 * row + i) * rest_size + rest) * tokens, tokens, 1) for i in range(2)],
        axis=1,
    )
    chosen = query_labels[:, :, None, :] == ids[None, None, :, None]
    span = jnp.stack(
        [jnp.sum(jnp.where(chosen, edge[:, None, :, None], 0), axis=2) for edge in (begins, ends)], axis=2
    )
    parity = rest % 2
    firsts = jnp.stack([((2 * row + i) * rest_size + rest) * tokens for i in range(2)])
    near = jnp.broadcast_to((firsts // TK - 1 + parity)[None], (2, 2))
    bounds = jnp.stack(
        [
            jnp.min(span[:, :, 0], axis=-1) // TK,
            -(-jnp.max(span[:, :, 1], axis=-1) // TK),
            near,
            -(-jnp.max(span[:, :, 0], axis=-1) // TK),
            jnp.min(span[:, :, 1], axis=-1) // TK,
            jnp.broadcast_to(parity, (2, 2)),
        ],
        axis=-1,
    ).astype(jnp.int32)
    table = lax.dynamic_slice_in_dim(bias_table.T, group * group_heads, group_heads, 0)
    o_packed, o_kept, log_total, bias_tiles = attention(bounds, table, q_all, kv_all, span)
    o_home = move_heads(return_kernel, (GROUPS,), shards, 4, o_packed)
    attended_low = unpack_heads(o_home)[None]
    residual = hidden + jnp.dot(attended_low, w_out, preferred_element_type=jnp.float32)
    gain_two = norm_gain2.astype(jnp.float32)
    normed2, norm2_back = jax.vjp(rms_norm, residual, gain_two)
    n2_low = normed2.astype(jnp.bfloat16)
    gate_proj = jnp.dot(n2_low, w_gate, preferred_element_type=jnp.float32)
    up_proj = jnp.dot(n2_low, w_up, preferred_element_type=jnp.float32)
    activated, geglu_back = jax.vjp(geglu, gate_proj, up_proj)
    act_low = activated.astype(jnp.bfloat16)
    block_out = (residual + jnp.dot(act_low, w_down, preferred_element_type=jnp.float32)).astype(
        jnp.bfloat16
    )
    grad_down = jnp.einsum("rtf,rtd->fd", act_low, cotangent, preferred_element_type=jnp.float32)
    d_act = jnp.einsum("rtd,fd->rtf", cotangent, w_down, preferred_element_type=jnp.float32)
    d_gate, d_up = geglu_back(d_act)
    d_gate_low = d_gate.astype(jnp.bfloat16)
    d_up_low = d_up.astype(jnp.bfloat16)
    grad_gate = jnp.einsum("rtd,rtf->df", n2_low, d_gate_low, preferred_element_type=jnp.float32)
    grad_up = jnp.einsum("rtd,rtf->df", n2_low, d_up_low, preferred_element_type=jnp.float32)
    d_normed2 = jnp.einsum(
        "rtf,df->rtd", d_gate_low, w_gate, preferred_element_type=jnp.float32
    ) + jnp.einsum("rtf,df->rtd", d_up_low, w_up, preferred_element_type=jnp.float32)
    d_res_part, d_gain_two = norm2_back(d_normed2)
    d_residual = cotangent.astype(jnp.float32) + d_res_part
    d_branch = d_residual.astype(jnp.bfloat16)
    grad_out = jnp.einsum("rtd,rte->de", attended_low, d_branch, preferred_element_type=jnp.float32)
    d_attended = jnp.einsum(
        "rte,de->rtd", d_branch, w_out, preferred_element_type=jnp.float32
    ).astype(jnp.bfloat16)
    do_all = move_heads(spread_kernel, (2, 2), shards, 5, pack_heads(d_attended[0]))
    dq_packed, dkv_all, d_table_lanes = attention_back(
        bounds, table, q_all, do_all, o_kept, kv_all, bias_tiles, span, log_total
    )
    dq_home, dkv_home = reduce_all(shards, dq_packed, dkv_all)
    d_query_low = unpack_heads(dq_home)[None]
    dkv_home = jnp.transpose(dkv_home, (1, 0, 2)).reshape(1, tokens, head_count, 2, head_dim)
    d_key_low = dkv_home[:, :, :, 0].reshape(1, tokens, width_d)
    d_value_low = dkv_home[:, :, :, 1].reshape(1, tokens, width_d)
    d_table = jnp.zeros((head_count, BUCKETS), jnp.float32)
    d_table = lax.dynamic_update_slice_in_dim(d_table, jnp.sum(d_table_lanes, axis=-1), group * group_heads, 0).T
    grad_query = jnp.einsum("rtd,rte->de", n1_low, d_query_low, preferred_element_type=jnp.float32)
    grad_key = jnp.einsum("rtd,rte->de", n1_low, d_key_low, preferred_element_type=jnp.float32)
    grad_value = jnp.einsum("rtd,rte->de", n1_low, d_value_low, preferred_element_type=jnp.float32)
    d_normed1 = (
        jnp.einsum("rte,de->rtd", d_query_low, w_query, preferred_element_type=jnp.float32)
        + jnp.einsum("rte,de->rtd", d_key_low, w_key, preferred_element_type=jnp.float32)
        + jnp.einsum("rte,de->rtd", d_value_low, w_value, preferred_element_type=jnp.float32)
    )
    d_hid_part, d_gain_one = norm1_back(d_normed1)
    d_hidden = d_residual + d_hid_part
    d_mixed = 0.5 * jnp.repeat(d_hidden, 2, axis=1)
    d_block = jnp.sum(d_mixed[:, :, None, :] * stacked, axis=-1)
    d_block_scores = block_probs * (
        d_block - jnp.sum(block_probs * d_block, axis=-1, keepdims=True)
    )
    grad_score_local = jnp.sum(d_block_scores[..., None] * stacked, axis=(0, 1, 2))
    d_pools = (
        block_probs[..., None] * d_mixed[:, :, None, :] + d_block_scores[..., None] * score_vec
    )
    spread = jnp.stack(
        [
            d_pools[:, :, width_index] / masks_all[width_index][1][:, :, None]
            for width_index in range(MAX_BLOCK)
        ],
        axis=2,
    ).reshape(row_count, length, MAX_BLOCK * width_d)
    rim_spread = extended(spread.astype(jnp.bfloat16), (("blk", 1),), 2).astype(spread.dtype)
    spread_pad = jnp.pad(rim_spread, ((0, 0), (1, 1), (0, 0))).reshape(
        row_count, length + 6, MAX_BLOCK, width_d
    )
    d_bytes = jnp.zeros((row_count, length, width_d), jnp.float32)
    for width_index in range(MAX_BLOCK):
        for offset, keep_mask in masks_all[width_index][0]:
            d_bytes = (
                d_bytes
                + keep_mask[:, :, None]
                * spread_pad[:, 3 + offset : 3 + offset + length, width_index]
            )
    share_local = jnp.sum(block_probs, axis=(0, 1)) / (row_count * length * devices_all)
    small = (grad_score_local, d_gain_one, d_gain_two, d_table, share_local)
    if devices_all <= 32:
        def blocks(grad):
            return grad.reshape(devices_all, grad.shape[0] // devices_all, grad.shape[1]).astype(jnp.bfloat16)

        wide = jnp.concatenate([blocks(grad_gate), blocks(grad_up)], axis=1)
        slim = jnp.concatenate([blocks(g) for g in (grad_query, grad_key, grad_value, grad_out, grad_down)], axis=1)
        flat = jnp.concatenate([part.reshape(-1) for part in small])
        flat = jnp.pad(flat, (0, -flat.shape[0] % 1024)).reshape(-1, 128)
        (wide, slim), flat = reduce_weights(shape, (wide, slim), flat)
        per = width_d // devices_all
        summed_weights = [slim[p * per : (p + 1) * per] for p in range(4)]
        summed_weights += [wide[:per], wide[per:], slim[4 * per :]]
        flat, summed_small = flat.reshape(-1), []
        for part in small:
            summed_small.append(flat[: part.size].reshape(part.shape))
            flat = flat[part.size :]
    else:
        summed_weights = [
            lax.psum_scatter(grad, ("dp", "blk"), scatter_dimension=0, tiled=True)
            for grad in (grad_query, grad_key, grad_value, grad_out, grad_gate, grad_up, grad_down)
        ]
        summed_small = lax.psum(small, ("dp", "blk"))
    return (
        block_out,
        d_bytes.astype(jnp.bfloat16),
        summed_small[0],
        summed_small[1],
        summed_weights[0],
        summed_weights[1],
        summed_weights[2],
        summed_weights[3],
        summed_small[3],
        summed_small[2],
        summed_weights[4],
        summed_weights[5],
        summed_weights[6],
        summed_small[4],
    )


def solution(mesh):
    placed = (
        P("dp", "blk", None),
        P("dp", "blk"),
        P(),
        P(),
        P(),
        P(),
        P(),
        P(),
        P(),
        P(),
        P(),
        P(),
        P(),
        P("dp", "blk", None),
    )
    return jax.shard_map(
        body,
        mesh=mesh,
        in_specs=placed,
        out_specs=(
            P("dp", "blk", None),
            P("dp", "blk", None),
            P(),
            P(),
            P(("dp", "blk"), None),
            P(("dp", "blk"), None),
            P(("dp", "blk"), None),
            P(("dp", "blk"), None),
            P(),
            P(),
            P(("dp", "blk"), None),
            P(("dp", "blk"), None),
            P(("dp", "blk"), None),
            P(),
        ),
        check_vma=False,
    )
```

```python
import functools
import math

import jax
import jax.numpy as jnp
from jax import lax
from jax.experimental import pallas as pl
from jax.experimental.pallas import tpu as pltpu
from jax.sharding import PartitionSpec as P

BUCKETS = 32
MAX_BLOCK = 4
VMEM_BYTES = 60 * 2**20


def buckets_of(relative):
    distance = jnp.abs(relative)
    beyond = jnp.zeros_like(distance)
    for border in (12, 16, 23, 32, 46, 64, 91):
        beyond = beyond + (distance >= border).astype(jnp.int32)
    nearer = jnp.where(distance < 8, distance, 8 + beyond)
    return nearer + BUCKETS // 2 * (relative > 0).astype(jnp.int32)


MESH_ID = pl.DeviceIdType.MESH
GROUPS = 4


def bits_of(size):
    return [1 << p for p in reversed(range(size.bit_length() - 1))]


def bit(value, mask):
    return (value // mask) % 2


def flipped(value, mask):
    return value + mask * (1 - 2 * bit(value, mask))


class Place:
    def __init__(self, shards):
        self.shards = shards
        self.rest_size = shards // GROUPS
        self.dp = lax.axis_index("dp")
        self.blk = lax.axis_index("blk")
        self.row = self.dp % 2
        self.group = self.blk // self.rest_size
        self.rest = self.blk % self.rest_size

    def at(self, row, group, rest):
        return (self.dp - self.row + row, group * self.rest_size + rest)

    def chunk(self, group, rest):
        return group * self.rest_size + rest

    def other_row(self):
        return self.at(1 - self.row, self.group, self.rest)

    def other_rest(self, mask):
        return self.at(self.row, self.group, flipped(self.rest, mask))

    def other_group(self, step):
        return self.at(self.row, (self.group + step) % GROUPS, self.rest)


def greet(targets):
    barrier = pltpu.get_barrier_semaphore()
    for target in targets:
        pl.semaphore_signal(barrier, inc=1, device_id=target, device_id_type=MESH_ID)
    pl.semaphore_wait(barrier, len(targets))


def remote(src, dst, send_sem, recv_sem, target):
    return pltpu.make_async_remote_copy(
        src_ref=src,
        dst_ref=dst,
        send_sem=send_sem,
        recv_sem=recv_sem,
        device_id=target,
        device_id_type=MESH_ID,
    )


def line_and_row(place):
    found = []
    for step in range(GROUPS):
        for flip in range(2):
            if step or flip:
                row = 1 - place.row if flip else place.row
                found.append(place.at(row, (place.group + step) % GROUPS, place.rest))
    return found


def spread_heads(place, q_ref, out_ref, send_sem, recv_sem):
    row_to = place.group // 2
    slot = place.group % 2
    dst = out_ref.at[place.row, slot]
    mine = recv_sem.at[place.row * 2 + slot]
    at_home = row_to == place.row
    for step in range(GROUPS):
        group = (place.group + step) % GROUPS
        src = q_ref.at[group]
        copy = remote(src, dst, send_sem.at[step], mine, place.at(row_to, group, place.rest))
        if step:
            copy.start()
        else:
            pl.when(jnp.logical_not(at_home))(copy.start)
            pl.when(at_home)(pltpu.make_async_copy(src, dst, mine).start)


def spread_heads_wait(place, q_ref, out_ref, send_sem, recv_sem):
    at_home = place.group // 2 == place.row
    for row in range(2):
        for slot in range(2):
            pltpu.make_async_copy(q_ref.at[0], out_ref.at[row, slot], recv_sem.at[row * 2 + slot]).wait()
    for step in range(GROUPS):
        copy = remote(q_ref.at[0], out_ref.at[0, 0], send_sem.at[step], recv_sem.at[0], place.other_row())
        if step:
            copy.wait_send()
        else:
            pl.when(jnp.logical_not(at_home))(copy.wait_send)


def return_heads(place, o_ref, out_ref, send_sem, recv_sem):
    for row in range(2):
        for slot in range(2):
            group = place.row * 2 + slot
            src = o_ref.at[row, slot]
            dst = out_ref.at[place.group]
            mine = recv_sem.at[place.group]
            at_home = jnp.logical_and(place.row == row, place.group == group)
            copy = remote(src, dst, send_sem.at[row * 2 + slot], mine, place.at(row, group, place.rest))
            pl.when(jnp.logical_not(at_home))(copy.start)
            pl.when(at_home)(pltpu.make_async_copy(src, dst, mine).start)


def return_heads_wait(place, o_ref, out_ref, send_sem, recv_sem):
    for group in range(GROUPS):
        pltpu.make_async_copy(o_ref.at[0, 0], out_ref.at[group], recv_sem.at[group]).wait()
    for row in range(2):
        for slot in range(2):
            group = place.row * 2 + slot
            at_home = jnp.logical_and(place.row == row, place.group == group)
            copy = remote(o_ref.at[0, 0], out_ref.at[0], send_sem.at[row * 2 + slot], recv_sem.at[0], place.other_row())
            pl.when(jnp.logical_not(at_home))(copy.wait_send)


def spread_kernel(shards, q_ref, out_ref, send_sem, recv_sem):
    place = Place(shards)
    greet(line_and_row(place))
    spread_heads(place, q_ref, out_ref, send_sem, recv_sem)
    spread_heads_wait(place, q_ref, out_ref, send_sem, recv_sem)


def return_kernel(shards, o_ref, out_ref, send_sem, recv_sem):
    place = Place(shards)
    greet(line_and_row(place))
    return_heads(place, o_ref, out_ref, send_sem, recv_sem)
    return_heads_wait(place, o_ref, out_ref, send_sem, recv_sem)


SMEM_SPEC = pl.BlockSpec(memory_space=pltpu.SMEM)
VMEM_SPEC = pl.BlockSpec(memory_space=pltpu.VMEM)


def move_heads(kernel, lead, shards, ident, packed):
    rows, lanes = packed.shape[-2:]
    return pl.pallas_call(
        functools.partial(kernel, shards),
        out_shape=jax.ShapeDtypeStruct(lead + (rows, lanes), packed.dtype),
        in_specs=[pl.BlockSpec(memory_space=pltpu.VMEM)],
        out_specs=pl.BlockSpec(memory_space=pltpu.VMEM),
        scratch_shapes=[pltpu.SemaphoreType.DMA((4,)), pltpu.SemaphoreType.DMA((4,))],
        compiler_params=pltpu.CompilerParams(collective_id=ident, has_side_effects=True, vmem_limit_bytes=VMEM_BYTES),
        name="move_heads_%d" % ident,
    )(packed)


def gather_kernel(shards, q_ref, kv_ref, label_ref, qo_ref, kvo_ref, labo_ref, q_send, q_recv, z_send, far_send, core_send, kv_recv, own_sem, lab_send, lab_recv):
    place = Place(shards)
    tokens = kv_ref.shape[1]
    rest_bits = bits_of(place.rest_size)
    core, far = rest_bits[-1], ["row"] + rest_bits[:-1]
    greet(line_and_row(place) + [place.other_rest(mask) for mask in rest_bits])

    dims = [("row", 1)] + [("blk", m) for m in bits_of(shards)]
    lab_index = [place.row] + [bit(place.blk, m) for _, m in dims[1:]]
    lab_order = list(range(len(dims)))

    def lab_copy(stage):
        index = tuple(slice(None) if p in lab_order[:stage] else lab_index[p] for p in range(len(dims)))
        axis, mask = dims[lab_order[stage]]
        target = place.other_row() if axis == "row" else (place.dp, flipped(place.blk, mask))
        there = labo_ref.at[index]
        return remote(there, there, lab_send.at[stage], lab_recv.at[stage], target)

    labo_ref[tuple(lab_index)] = label_ref[...]
    lab_copy(0).start()
    lab_stage = 0

    def slot(row, group, rest):
        start = pl.multiple_of(place.chunk(group, rest) * tokens, tokens)
        return kvo_ref.at[row, pl.ds(start, tokens)]

    def held(dz, offset, core_off):
        row = 1 - place.row if offset & 1 else place.row
        rest = place.rest
        for p, mask in enumerate(far[1:]):
            if offset >> (p + 1) & 1:
                rest = flipped(rest, mask)
        if core_off:
            rest = flipped(rest, core)
        return slot(row, (place.group + dz) % GROUPS, rest)

    count = 1 << len(far)

    def sem_of(dz, offset, core_off):
        return kv_recv.at[(core_off * count + offset) * GROUPS + dz]

    own = pltpu.make_async_copy(kv_ref.at[place.group], held(0, 0, 0), own_sem)
    own.start()
    waits = []
    for step in (1, 3, 2):
        copy = remote(kv_ref.at[(place.group + step) % GROUPS], held(0, 0, 0), z_send.at[step], sem_of((GROUPS - step) % GROUPS, 0, 0), place.other_group(step))
        copy.start()
        waits.append(copy)
    spread_heads(place, q_ref, qo_ref, q_send, q_recv)

    used = 0
    events = sorted(((dz, off) for dz in range(GROUPS) for off in range(count)), key=lambda e: (bin(e[1]).count("1"), (0, 1, 3, 2).index(e[0])))
    core_target = place.other_rest(core)
    for dz, off in events:
        here = held(dz, off, 0)
        if dz == 0 and off == 0:
            src = kv_ref.at[place.group]
        else:
            remote(here, here, z_send.at[0], sem_of(dz, off, 0), core_target).wait_recv()
            src = here
        order = [(p + dz) % len(far) for p in range(len(far))]
        last = max([order.index(p) for p in range(len(far)) if off >> p & 1], default=-1)
        for p in order[last + 1 :]:
            target = place.other_row() if p == 0 else place.other_rest(far[p])
            copy = remote(src, here, far_send.at[used], sem_of(dz, off | 1 << p, 0), target)
            copy.start()
            waits.append(copy)
            used += 1
        copy = remote(src, here, core_send.at[off * GROUPS + dz], sem_of(dz, off, 1), core_target)
        copy.start()
        waits.append(copy)
        if lab_stage < len(dims):
            lab_copy(lab_stage).wait()
            lab_stage += 1
            if lab_stage < len(dims):
                lab_copy(lab_stage).start()
    for dz, off in events:
        here = held(dz, off, 1)
        remote(here, here, z_send.at[0], sem_of(dz, off, 1), core_target).wait_recv()
    own.wait()
    for copy in waits:
        copy.wait_send()
    spread_heads_wait(place, q_ref, qo_ref, q_send, q_recv)


def gather_all(shards, q_packed, kv_parts, labels):
    tokens, width = kv_parts.shape[1:]
    far = 1 + len(bits_of(shards // GROUPS)) - 1
    count = 1 << far
    nbits = 1 + len(bits_of(shards))
    sem = pltpu.SemaphoreType.DMA
    return pl.pallas_call(
        functools.partial(gather_kernel, shards),
        out_shape=(
            jax.ShapeDtypeStruct((2, 2) + q_packed.shape[1:], q_packed.dtype),
            jax.ShapeDtypeStruct((2, shards * tokens, width), kv_parts.dtype),
            jax.ShapeDtypeStruct((2,) * nbits + labels.shape, labels.dtype),
        ),
        in_specs=[pl.BlockSpec(memory_space=pltpu.VMEM)] * 3,
        out_specs=(pl.BlockSpec(memory_space=pltpu.VMEM),) * 3,
        scratch_shapes=[
            sem((4,)), sem((4,)), sem((GROUPS,)), sem((GROUPS * (count - 1),)), sem((GROUPS * count,)), sem((GROUPS * count * 2,)),
            sem, sem((nbits,)), sem((nbits,)),
        ],
        compiler_params=pltpu.CompilerParams(collective_id=1, has_side_effects=True, vmem_limit_bytes=VMEM_BYTES),
        name="gather_keys",
    )(q_packed, kv_parts, labels)


def add_blocks(dst_ref, src_ref, index, shape):
    lead = shape[:-2]
    total = math.prod(lead)

    def one(step, _):
        place, left = [], step
        for size in reversed(lead):
            place.append(left % size)
            left = left // size
        place = tuple(reversed(place))
        full, k = [], 0
        for entry in index:
            if entry is None:
                full.append(place[k])
                k += 1
            else:
                full.append(entry)
        mine = src_ref[tuple(full)].astype(jnp.float32)
        dst_ref[place] = (dst_ref[place].astype(jnp.float32) + mine).astype(dst_ref.dtype)
        return 0

    lax.fori_loop(0, total, one, 0)


class Stream:
    def __init__(self, axes, at, kept, order, src, bufs, out, send_sem, recv_sem):
        self.axes, self.at, self.kept, self.order = axes, at, kept, order
        self.src, self.bufs, self.out = src, bufs, out
        self.send_sem, self.recv_sem = send_sem, recv_sem

    def own(self, p):
        axis, mask = self.axes[p]
        return bit(self.at[axis], mask)

    def target(self, p):
        axis, mask = self.axes[p]
        moved = dict(self.at)
        moved[axis] = flipped(self.at[axis], mask)
        return (moved["dp"], moved["blk"])

    def stage(self, k):
        kept = [p for p in self.kept if p not in self.order[:k]]
        return kept, self.src if k == 0 else self.bufs[k - 1], self.order[k]

    def copy(self, k):
        kept, src, now = self.stage(k)
        index = tuple(1 - self.own(p) if p == now else slice(None) for p in kept)
        return remote(src.at[index], self.bufs[k], self.send_sem.at[k], self.recv_sem.at[k], self.target(now))

    def absorb(self, k):
        kept, src, now = self.stage(k)
        buf = self.bufs[k]
        if k == len(self.order) - 1:
            mine = src[self.own(now)].astype(jnp.float32)
            self.out[...] = buf[...].astype(jnp.float32) + mine
        else:
            add_blocks(buf, src, tuple(self.own(p) if p == now else None for p in kept), buf.shape)


class Whole:
    def __init__(self, axes, at, order, src, bufs, out, send_sem, recv_sem):
        self.stream = Stream(axes, at, order, order, src, bufs, out, send_sem, recv_sem)
        self.order, self.src, self.bufs, self.out = order, src, bufs, out

    def held(self, k):
        return self.src if k == 0 else self.bufs.at[1, k - 1]

    def copy(self, k):
        s = self.stream
        return remote(self.held(k), self.bufs.at[0, k], s.send_sem.at[k], s.recv_sem.at[k], s.target(self.order[k]))

    def absorb(self, k):
        total = self.held(k)[...] + self.bufs[0, k]
        if k == len(self.order) - 1:
            self.out[...] = total
        else:
            self.bufs[1, k] = total


def run_streams(streams, first=0):
    for stage in range(max(len(s.order) for s in streams)):
        for s in streams:
            if stage < len(s.order):
                s.copy(stage).wait()
                s.absorb(stage)
                if stage < len(s.order) - 1:
                    s.copy(stage + 1).start()


def bit_axes(shape):
    return [("dp", m) for m in bits_of(shape["dp"])] + [("blk", m) for m in bits_of(shape["blk"])]


def stream_scratch(lead, order, rows, cols):
    return [pltpu.VMEM((2,) * (lead - 1 - k) + (rows, cols), jnp.bfloat16) for k in range(len(order))]


def weights_kernel(shards, da_ref, n2_ref, att_ref, act_ref, dg_ref, du_ref, ct_ref, db_ref,
                   do_ref, keep_a, send_a, keep_b, send_b, keep_c, send_c,
                   q_send, q_recv, core_send, core_recv, gate, up, down, out, wide_out, slim_out, wide_in, slim_in):
    place = Place(shards)
    core_target = place.other_rest(1)
    greet(line_and_row(place) + [core_target])
    spread_heads(place, da_ref, do_ref, q_send, q_recv)
    per = gate.shape[0] // 32
    per_ff = down.shape[0] // 32
    half = wide_out.shape[2] // 2
    core = place.rest % 2

    n2_t = n2_ref[...].T
    step = 512
    for j in range(gate.shape[1] // step):
        cols = slice(j * step, j * step + step)
        gate[:, cols] = mxu(n2_t, dg_ref[:, cols])
        up[:, cols] = mxu(n2_t, du_ref[:, cols])

    def wide_rows(block):
        rows = pl.ds(pl.multiple_of(block * per, 8), per)
        return jnp.concatenate([gate[rows, :], up[rows, :]], axis=0)

    def slim_rows(block):
        rows, more = pl.ds(pl.multiple_of(block * per, 8), per), pl.ds(pl.multiple_of(block * per_ff, 8), per_ff)
        empty = jnp.zeros((32 - per, out.shape[1]), jnp.float32)
        return jnp.concatenate([out[rows, :], empty, down[more, :]], axis=0)

    def send_wide(m, _):
        wide_out[m] = wide_rows(2 * m + 1 - core).astype(jnp.bfloat16)
        return 0

    lax.fori_loop(0, 16, send_wide, 0)
    wide_copy = remote(wide_out, wide_in, core_send.at[0], core_recv.at[0], core_target)
    wide_copy.start()
    out[...] = mxu(att_ref[...].T, db_ref[...])
    for j in range(down.shape[0] // step):
        rows = slice(j * step, j * step + step)
        down[rows, :] = mxu(act_ref[:, rows].T, ct_ref[...])

    def send_slim(m, _):
        slim_out[m] = slim_rows(2 * m + 1 - core).astype(jnp.bfloat16)
        return 0

    lax.fori_loop(0, 16, send_slim, 0)
    slim_copy = remote(slim_out, slim_in, core_send.at[1], core_recv.at[1], core_target)
    slim_copy.start()

    def number(j, bit_at, value):
        return j // bit_at * (2 * bit_at) + value * bit_at + j % bit_at

    wide_copy.wait()
    for (keep, send), bit_at, mine, cols in (
        ((keep_a, send_a), 8, place.row, slice(0, half)),
        ((keep_b, send_b), 1, bit(place.rest, 2), slice(half, 2 * half)),
    ):
        for ref, value in ((send, 1 - mine), (keep, mine)):
            def one(j, _):
                m = number(j, bit_at, value)
                ref[j] = (wide_rows(2 * m + core)[:, cols] + wide_in[m, :, cols].astype(jnp.float32)).astype(jnp.bfloat16)
                return 0
            lax.fori_loop(0, 8, one, 0)
    slim_copy.wait()
    mine = bit(place.group, 1)
    for ref, value in ((send_c, 1 - mine), (keep_c, mine)):
        def one(j, _):
            m = number(j, 2, value)
            ref[j] = (slim_rows(2 * m + core) + slim_in[m].astype(jnp.float32)).astype(jnp.bfloat16)
            return 0
        lax.fori_loop(0, 8, one, 0)
    spread_heads_wait(place, da_ref, do_ref, q_send, q_recv)


def spread_and_weights(shards, da, n2, att, act, dg, du, ct, db):
    width, ff = n2.shape[1], act.shape[1]
    per, per_ff = width // 32, ff // 32
    sem, low = pltpu.SemaphoreType.DMA, jnp.bfloat16
    wide, slim = (2 * per, ff), (32 + per_ff, width)
    halves = [jax.ShapeDtypeStruct((8, 2 * per, ff // 2), low)] * 4 + [jax.ShapeDtypeStruct((8,) + slim, low)] * 2
    return pl.pallas_call(
        functools.partial(weights_kernel, shards),
        out_shape=(jax.ShapeDtypeStruct((2, 2) + da.shape[1:], da.dtype),) + tuple(halves),
        in_specs=[VMEM_SPEC] * 8,
        out_specs=(VMEM_SPEC,) * 7,
        scratch_shapes=[
            sem((4,)), sem((4,)), sem((2,)), sem((2,)),
            pltpu.VMEM((width, ff), jnp.float32), pltpu.VMEM((width, ff), jnp.float32),
            pltpu.VMEM((ff, width), jnp.float32), pltpu.VMEM((width, width), jnp.float32),
            pltpu.VMEM((16,) + wide, low), pltpu.VMEM((16,) + slim, low),
            pltpu.VMEM((16,) + wide, low), pltpu.VMEM((16,) + slim, low),
        ],
        compiler_params=pltpu.CompilerParams(collective_id=5, has_side_effects=True, vmem_limit_bytes=VMEM_BYTES),
        name="spread_and_weights",
    )(da, n2, att, act, dg, du, ct, db)


def reduce_kernel(shards, axes, orders, *refs):
    count = len(orders)
    q_ref, kv_ref = refs[:2]
    pairs = refs[2 : 2 + 2 * count]
    qo_ref, kvo_ref = refs[2 + 2 * count : 4 + 2 * count]
    sums = refs[4 + 2 * count : 4 + 3 * count]
    q_send, q_recv, send_sem, recv_sem, z_send, z_recv, w_send, w_recv = refs[4 + 3 * count : 12 + 3 * count]
    bufs = refs[12 + 3 * count :]
    place = Place(shards)
    rest_bits = bits_of(place.rest_size)
    greet(line_and_row(place) + [place.other_rest(mask) for mask in rest_bits])
    return_heads(place, q_ref, qo_ref, q_send, q_recv)
    ndim = 1 + len(rest_bits)
    at = {"dp": place.dp, "blk": place.blk}
    streams, used = [], ndim
    for s, (kept, order) in enumerate(orders):
        src, more = bufs[used], bufs[used + 1 : used + 1 + len(order)]
        used += 1 + len(order)
        streams.append(Stream(axes, at, kept, order, src, more, sums[s], w_send.at[s], w_recv.at[s]))
    own = [place.row] + [bit(place.rest, m) for m in rest_bits]
    targets = [place.other_row()] + [place.other_rest(m) for m in rest_bits]
    state = {}

    def plan(group_step):
        far = list(range(ndim - 1))
        turn = group_step % len(far)
        return [ndim - 1] + far[turn:] + far[:turn]

    def copy_of(step, stage):
        order = plan(step)
        group = (place.group + step) % GROUPS
        done = order[:stage]
        p_now = order[stage]
        buf = bufs[stage].at[step]
        if stage == 0:
            index = (p_index(group, done, p_now))
            src = kv_ref.at[index]
        else:
            kept = [p for p in range(ndim) if p not in done]
            src = bufs[stage - 1].at[(step,) + tuple(1 - own[p] if p == p_now else slice(None) for p in kept)]
        return remote(src, buf, send_sem.at[stage, step], recv_sem.at[stage, step], targets[p_now])

    def p_index(group, done, p_now):
        index = [slice(None)] * ndim
        index[p_now] = 1 - own[p_now]
        return (index[0], group) + tuple(index[1:])

    def absorb(step, stage):
        order = plan(step)
        done, p_now = order[:stage], order[stage]
        buf = bufs[stage].at[step]
        group = (place.group + step) % GROUPS
        if stage == 0:
            index = [None] * ndim
            index[p_now] = own[p_now]
            add_blocks(buf, kv_ref, (index[0], group) + tuple(index[1:]), buf.shape)
        else:
            kept = [p for p in range(ndim) if p not in done]
            index = tuple(own[p] if p == p_now else None for p in kept)
            add_blocks(buf, bufs[stage - 1].at[step], index, buf.shape)

    steps = (2, 1, 3, 0)
    for step in steps:
        copy_of(step, 0).start()
    for s, stream in enumerate(streams):
        add_two(stream.src, pairs[2 * s], pairs[2 * s + 1])
        stream.copy(0).start()
    for stage in range(ndim):
        for step in steps:
            copy_of(step, stage).wait()
            absorb(step, stage)
            if stage < ndim - 1:
                copy_of(step, stage + 1).start()
            elif step:
                remote(bufs[stage].at[step], kvo_ref.at[place.group], z_send.at[step], z_recv.at[(GROUPS - step) % GROUPS], place.other_group(step)).start()
            else:
                kvo_ref[place.group] = bufs[stage][step]
        for stream in streams:
            if stage < len(stream.order):
                stream.copy(stage).wait()
                stream.absorb(stage)
                if stage < len(stream.order) - 1:
                    stream.copy(stage + 1).start()
    for step in (1, 3, 2):
        there = kvo_ref.at[(place.group + step) % GROUPS]
        remote(bufs[ndim - 1].at[step], there, z_send.at[step], z_recv.at[step], place.other_group(step)).wait()
    return_heads_wait(place, q_ref, qo_ref, q_send, q_recv)


def add_two(dst_ref, one_ref, two_ref):
    lead = dst_ref.shape[:-2]

    def one(step, _):
        place, left = [], step
        for size in reversed(lead):
            place.append(left % size)
            left = left // size
        place = tuple(reversed(place))
        dst_ref[place] = (one_ref[place].astype(jnp.float32) + two_ref[place].astype(jnp.float32)).astype(dst_ref.dtype)
        return 0

    lax.fori_loop(0, math.prod(lead), one, 0)


def reduce_all(shape, q_packed, kv_sums, orders, pairs):
    shards = shape["blk"]
    tokens_all, width = kv_sums.shape[1:]
    tokens = tokens_all // shards
    rest_bits = bits_of(shards // GROUPS)
    ndim = 1 + len(rest_bits)
    sem = pltpu.SemaphoreType.DMA
    scratch = [pltpu.VMEM((GROUPS,) + (2,) * (ndim - 1 - s) + (tokens, width), kv_sums.dtype) for s in range(ndim)]
    flat, sums = [], []
    for (kept, order), pair in zip(orders, pairs):
        rows, cols = pair[0].shape[-2:]
        flat += [part.reshape((2,) * len(kept) + (rows, cols)) for part in pair]
        sums.append(jax.ShapeDtypeStruct((rows, cols), jnp.float32))
        scratch.append(pltpu.VMEM((2,) * len(kept) + (rows, cols), jnp.bfloat16))
        scratch += stream_scratch(len(kept), order, rows, cols)
    stages = max([len(order) for _, order in orders], default=1)
    return pl.pallas_call(
        functools.partial(reduce_kernel, shards, bit_axes(shape), orders),
        out_shape=(
            jax.ShapeDtypeStruct((GROUPS,) + q_packed.shape[2:], q_packed.dtype),
            jax.ShapeDtypeStruct((GROUPS, tokens, width), kv_sums.dtype),
        ) + tuple(sums),
        in_specs=[VMEM_SPEC] * (2 + len(flat)),
        out_specs=(VMEM_SPEC,) * (2 + len(sums)),
        scratch_shapes=[sem((4,)), sem((4,)), sem((ndim, GROUPS)), sem((ndim, GROUPS)), sem((GROUPS,)), sem((GROUPS,)),
                        sem((max(len(orders), 1), stages)), sem((max(len(orders), 1), stages))] + scratch,
        compiler_params=pltpu.CompilerParams(collective_id=2, has_side_effects=True, vmem_limit_bytes=VMEM_BYTES),
        name="reduce_keys",
    )(q_packed, kv_sums.reshape((2, GROUPS) + (2,) * len(rest_bits) + (tokens, width)), *flat)


def sums_kernel(shards, axes, orders, *refs):
    count = len(orders) - 1
    ins, small_ref, spill_ref = refs[:count], refs[count], refs[count + 1]
    outs, small_out, spill_out = refs[count + 2 : 2 * count + 2], refs[2 * count + 2], refs[2 * count + 3]
    w_send, w_recv, s_send, s_recv = refs[2 * count + 4 : 2 * count + 8]
    bufs = refs[2 * count + 8 :]
    at = {"dp": lax.axis_index("dp"), "blk": lax.axis_index("blk")}
    whole = Whole(axes, at, orders[-1], small_ref, bufs[-1], small_out, w_send.at[count], w_recv.at[count])
    streams, used = [], 0
    for s in range(count):
        more = bufs[used : used + len(orders[s])]
        used += len(orders[s])
        streams.append(Stream(axes, at, sorted(orders[s]), orders[s], ins[s], more, outs[s], w_send.at[s], w_recv.at[s]))
    left = (at["dp"], (at["blk"] + shards - 1) % shards)
    right = (at["dp"], (at["blk"] + 1) % shards)
    greet([whole.stream.target(p) for p in range(len(axes))] + [left, right])
    spills = [
        remote(spill_ref.at[0], spill_out.at[1], s_send.at[0], s_recv.at[1], left),
        remote(spill_ref.at[1], spill_out.at[0], s_send.at[1], s_recv.at[0], right),
    ]
    streams.append(whole)
    for stream in streams:
        stream.copy(0).start()
    for copy in spills:
        copy.start()
    run_streams(streams)
    for copy in spills:
        copy.wait()


def last_sums(shape, blocks, orders, small, spill):
    axes = bit_axes(shape)
    ndim = len(axes)
    sem = pltpu.SemaphoreType.DMA
    scratch, sums = [], []
    for block, order in zip(blocks, orders):
        rows, cols = block.shape[-2:]
        scratch += stream_scratch(ndim, order, rows, cols)
        sums.append(jax.ShapeDtypeStruct((rows, cols), jnp.float32))
    count = len(blocks)
    scratch.append(pltpu.VMEM((2, ndim) + small.shape, small.dtype))
    found = pl.pallas_call(
        functools.partial(sums_kernel, shape["blk"], axes, orders),
        out_shape=tuple(sums) + (jax.ShapeDtypeStruct(small.shape, small.dtype), jax.ShapeDtypeStruct(spill.shape, spill.dtype)),
        in_specs=[VMEM_SPEC] * (count + 2),
        out_specs=(VMEM_SPEC,) * (count + 2),
        scratch_shapes=[sem((count + 1, ndim)), sem((count + 1, ndim)), sem((2,)), sem((2,))] + scratch,
        compiler_params=pltpu.CompilerParams(collective_id=3, has_side_effects=True, vmem_limit_bytes=VMEM_BYTES),
        name="last_sums",
    )(*[b.reshape((2,) * ndim + b.shape[-2:]) for b in blocks], small, spill)
    return found[:count], found[count], found[count + 1]


TQ = 256
TK = 512
NEAR_ROWS = 448
NEG = -1e30
FIRST_MAX = -1e29
NT = (((1,), (1,)), ((), ()))
NN = (((1,), (0,)), ((), ()))
BORDERS = (12, 16, 23, 32, 46, 64, 91)


def mxu(left, right, dims=NN):
    return lax.dot_general(left, right, dims, preferred_element_type=jnp.float32)


def turned(tile):
    return jnp.concatenate([tile[:, 64:], tile[:, :64]], axis=1)


def spread_lanes(packed, high):
    lane = lax.broadcasted_iota(jnp.int32, (1, 128), 1)
    keep = lane >= 64 if high else lane < 64
    zero = jnp.zeros((), packed.dtype)
    pair, last = packed[0:TQ], packed[TQ:]
    pick = lambda tile: jnp.where(keep, tile, zero)
    if high:
        return [pick(turned(pair)), pick(pair), jnp.concatenate([pick(turned(last)), pick(last)], axis=0)]
    return [pick(pair), pick(turned(pair)), jnp.concatenate([pick(last), pick(turned(last))], axis=0)]


def join_heads(parts):
    half = TQ // 2
    top = jnp.concatenate([parts[0], parts[1]], axis=1)
    low = jnp.concatenate([parts[2][:half], parts[2][half:]], axis=1)
    return jnp.concatenate([top, low], axis=0)


def valid_mask(se_ref, r, i, k0):
    kpos = k0 + lax.broadcasted_iota(jnp.int32, (TK, TQ), 0)
    return jnp.logical_and(kpos >= se_ref[r, i, 0:1, :], kpos < se_ref[r, i, 1:2, :])


def near_buckets(first, rows, parity):
    relative = (
        first - TK + TQ * parity
        + lax.broadcasted_iota(jnp.int32, (rows, TQ), 0)
        - lax.broadcasted_iota(jnp.int32, (rows, TQ), 1)
    )
    return buckets_of(relative)


def make_bias(table, parity, bias_ref):
    heads = bias_ref.shape[0]
    for h in range(heads):
        bias_ref[h, 0] = jnp.full((TK, TQ), table[h, 15], jnp.float32).astype(jnp.bfloat16)
        bias_ref[h, 3] = jnp.full((TK, TQ), table[h, 31], jnp.float32).astype(jnp.bfloat16)
    for tile in range(2):
        def rows(step, _):
            start = pl.multiple_of(step * 32, 32)
            which = near_buckets(tile * TK + start, 32, parity)
            for h in range(heads):
                value = jnp.zeros((32, TQ), jnp.float32)
                for b in range(BUCKETS):
                    value = jnp.where(which == b, table[h, b], value)
                bias_ref[h, tile + 1, pl.ds(start, 32)] = value.astype(jnp.bfloat16)
            return 0
        lax.fori_loop(0, TK // 32, rows, 0)


def tile_kind(bounds, r, i, t):
    slot = jnp.clip(t - bounds[r, i, 2] + 1, 0, 3)
    away = jnp.logical_or(slot == 0, slot == 3)
    inside = jnp.logical_and(t >= bounds[r, i, 3], t < bounds[r, i, 4])
    return slot, jnp.logical_and(away, inside)


def fwd_kernel(bounds, table, q_ref, kv_ref, se_ref, o_ref, keep_ref, lse_ref, bias_ref, vt, acc, mx, qp):
    heads = lse_ref.shape[2]
    make_bias(table, bounds[0, 0, 5], bias_ref)
    for r in range(2):
        for i in range(2):
            for h, tile in enumerate(spread_lanes(q_ref[r, i], False)):
                qp[r, i, h] = tile

    def row_body(r, _):
        lo_all = jnp.minimum(bounds[r, 0, 0], bounds[r, 1, 0])
        hi_all = jnp.maximum(bounds[r, 0, 1], bounds[r, 1, 1])

        def turn(t, _):
            k0 = pl.multiple_of(t * TK, TK)
            for h in range(heads):
                tile = kv_ref[r, pl.ds(k0, TK), h * 128 : h * 128 + 128]
                vt[h, 0:64, pl.ds(k0, TK)] = tile.T[64:128, :]
                vt[h, 64:80, pl.ds(k0, TK)] = jnp.ones((16, TK), jnp.bfloat16)
            return 0

        lax.fori_loop(lo_all, hi_all, turn, 0)

        def q_body(i, _):
            acc[...] = jnp.zeros_like(acc)
            mx[...] = jnp.full_like(mx, FIRST_MAX)

            def tile_body(t, _):
                k0 = pl.multiple_of(t * TK, TK)
                slot, plain = tile_kind(bounds, r, i, t)

                def scores(h):
                    return mxu(kv_ref[r, pl.ds(k0, TK), h * 128 : h * 128 + 128], qp[r, i, h], NT)

                def finish(h, s, b):
                    m_old = mx[h]
                    m_new = jnp.maximum(m_old, jnp.max(s, axis=0, keepdims=True) + b)
                    p = jnp.exp(s - (m_new - b)).astype(jnp.bfloat16)
                    mx[h] = m_new
                    acc[h] = acc[h] * jnp.exp(m_old - m_new) + mxu(vt[h, :, pl.ds(k0, TK)], p)

                @pl.when(plain)
                def _():
                    found = [scores(h) for h in range(heads)]
                    for h in range(heads):
                        finish(h, found[h], jnp.where(slot == 0, table[h, 15], table[h, 31]))

                @pl.when(jnp.logical_not(plain))
                def _():
                    ok = valid_mask(se_ref, r, i, k0)
                    for h in range(heads):
                        s = scores(h) + bias_ref[h, slot].astype(jnp.float32)
                        finish(h, jnp.where(ok, s, NEG), 0.0)

                return 0

            lax.fori_loop(bounds[r, i, 0], bounds[r, i, 1], tile_body, 0)
            parts = []
            for h in range(heads):
                total = acc[h, 64:65, :]
                parts.append((acc[h, 0:64, :] / total).T)
                lse_ref[r, i, h] = mx[h] + jnp.log(total)
            joined = join_heads(parts)
            o_ref[r, i] = joined.astype(jnp.bfloat16)
            keep_ref[r, i] = joined
            return 0

        lax.fori_loop(0, 2, q_body, 0)
        return 0

    lax.fori_loop(0, 2, row_body, 0)


def attention(bounds, table, q, kv, se):
    heads, n = kv.shape[2] // 128, kv.shape[1]
    packed = q.shape
    return pl.pallas_call(
        fwd_kernel,
        out_shape=(
            jax.ShapeDtypeStruct(packed, jnp.bfloat16),
            jax.ShapeDtypeStruct(packed, jnp.float32),
            jax.ShapeDtypeStruct((2, 2, heads, 1, TQ), jnp.float32),
            jax.ShapeDtypeStruct((heads, 4, TK, TQ), jnp.bfloat16),
        ),
        in_specs=[SMEM_SPEC] * 2 + [VMEM_SPEC] * 3,
        out_specs=(VMEM_SPEC,) * 4,
        scratch_shapes=[
            pltpu.VMEM((heads, 80, n), jnp.bfloat16),
            pltpu.VMEM((heads, 80, TQ), jnp.float32),
            pltpu.VMEM((heads, 1, TQ), jnp.float32),
            pltpu.VMEM((2, 2, heads, TQ, 128), jnp.bfloat16),
        ],
        compiler_params=pltpu.CompilerParams(vmem_limit_bytes=VMEM_BYTES),
        name="attention",
    )(bounds, table, q, kv, se)


def bwd_kernel(bounds, table, q_ref, do_ref, keep_ref, kv_ref, bias_ref, se_ref, lse_ref,
               dq_ref, dkv_ref, tab_ref, kt, dqt, dkv, grid, side, qp, dp_ref, delta):
    heads = lse_ref.shape[2]
    n = kv_ref.shape[1]
    grid[...] = jnp.zeros_like(grid)
    side[...] = jnp.zeros_like(side)
    for r in range(2):
        for i in range(2):
            for h, tile in enumerate(spread_lanes(q_ref[r, i], False)):
                qp[r, i, h] = tile
            for h, tile in enumerate(spread_lanes(do_ref[r, i], True)):
                dp_ref[r, i, h] = tile
            prod = (do_ref[r, i].astype(jnp.float32) * keep_ref[r, i]).T
            top, low = prod[:, 0:TQ], prod[:, TQ:]
            delta[r, i, 0] = jnp.sum(top[0:64], axis=0, keepdims=True)
            delta[r, i, 1] = jnp.sum(top[64:128], axis=0, keepdims=True)
            delta[r, i, 2] = jnp.concatenate(
                [jnp.sum(low[0:64], axis=0, keepdims=True), jnp.sum(low[64:128], axis=0, keepdims=True)], axis=1
            )

    def row_body(r, _):
        lo_all = jnp.minimum(bounds[r, 0, 0], bounds[r, 1, 0])
        hi_all = jnp.maximum(bounds[r, 0, 1], bounds[r, 1, 1])

        def clear(t, _):
            k0 = pl.multiple_of(t * TK, TK)
            for h in range(heads):
                dkv[h, pl.ds(k0, TK), :] = jnp.zeros((TK, 128), jnp.float32)
            return 0

        lax.fori_loop(0, n // TK, clear, 0)

        def turn(t, _):
            k0 = pl.multiple_of(t * TK, TK)
            for h in range(heads):
                tile = kv_ref[r, pl.ds(k0, TK), h * 128 : h * 128 + 128]
                kt[h, 0:64, pl.ds(k0, TK)] = tile.T[0:64, :]
                kt[h, 64:80, pl.ds(k0, TK)] = jnp.ones((16, TK), jnp.bfloat16)
            return 0

        lax.fori_loop(lo_all, hi_all, turn, 0)

        def q_body(i, _):
            dqt[...] = jnp.zeros_like(dqt)

            def tile_body(t, _):
                k0 = pl.multiple_of(t * TK, TK)
                slot, plain = tile_kind(bounds, r, i, t)

                def finish(h, p, ds, where):
                    ds_low = ds.astype(jnp.bfloat16)
                    two = jnp.concatenate([ds_low, p.astype(jnp.bfloat16)], axis=1)
                    both = jnp.concatenate([qp[r, i, h], dp_ref[r, i, h]], axis=0)
                    dkv[h, pl.ds(k0, TK), :] += mxu(two, both)
                    dqt[h, where] += mxu(kt[h, :, pl.ds(k0, TK)], ds_low)

                def products(h):
                    tile = kv_ref[r, pl.ds(k0, TK), h * 128 : h * 128 + 128]
                    return mxu(tile, qp[r, i, h], NT), mxu(tile, dp_ref[r, i, h], NT)

                @pl.when(plain)
                def _():
                    for h in range(heads):
                        s, d_probs = products(h)
                        p = jnp.exp(s - (lse_ref[r, i, h] - jnp.where(slot == 0, table[h, 15], table[h, 31])))
                        finish(h, p, p * (d_probs - delta[r, i, h]), jnp.where(slot == 0, 0, 2))

                @pl.when(jnp.logical_not(plain))
                def _():
                    ok = valid_mask(se_ref, r, i, k0)
                    for h in range(heads):
                        s, d_probs = products(h)
                        s = s + bias_ref[h, slot].astype(jnp.float32)
                        p = jnp.where(ok, jnp.exp(jnp.where(ok, s, NEG) - lse_ref[r, i, h]), 0.0)
                        ds = p * (d_probs - delta[r, i, h])
                        grid[h, slot] += ds
                        finish(h, p, ds, 1)

                return 0

            lax.fori_loop(bounds[r, i, 0], bounds[r, i, 1], tile_body, 0)
            parts = []
            for h in range(heads):
                parts.append((dqt[h, 0, 0:64] + dqt[h, 1, 0:64] + dqt[h, 2, 0:64]).T * 0.125)
                side[h, 0:1] += dqt[h, 0, 64:65]
                side[h, 1:2] += dqt[h, 2, 64:65]
            dq_ref[r, i] = join_heads(parts).astype(jnp.bfloat16)
            return 0

        lax.fori_loop(0, 2, q_body, 0)

        def put(t, _):
            k0 = pl.multiple_of(t * TK, TK)
            for h in range(heads):
                dkv_ref[r, pl.ds(k0, TK), h * 128 : h * 128 + 128] = dkv[h, pl.ds(k0, TK), :].astype(jnp.bfloat16)
            return 0

        lax.fori_loop(0, n // TK, put, 0)
        return 0

    lax.fori_loop(0, 2, row_body, 0)

    parity = bounds[0, 0, 5]
    tab_ref[...] = jnp.zeros_like(tab_ref)
    for h in range(heads):
        tab_ref[h, 15:16] = side[h, 0:1] + jnp.sum(grid[h, 0], axis=0, keepdims=True)
        tab_ref[h, 31:32] = side[h, 1:2] + jnp.sum(grid[h, 3], axis=0, keepdims=True)

    first = 13 - 8 * parity
    count = NEAR_ROWS // 32

    def block(h, step):
        tile = step // (TK // 32)
        start = pl.multiple_of((step % (TK // 32)) * 32, 32)
        return grid[h, tile + 1, pl.ds(start, 32)]

    def outer(bucket):
        def one(step, _):
            for h in range(heads):
                tab_ref[h, bucket : bucket + 1] += jnp.sum(block(h, step), axis=0, keepdims=True)
            return 0
        return one

    lax.fori_loop(0, first, outer(15), 0)
    lax.fori_loop(first + count, 2 * TK // 32, outer(31), 0)

    def inner(step, _):
        which = near_buckets(step * 32, 32, parity)
        for b in range(BUCKETS):
            here = which == b
            for h in range(heads):
                tab_ref[h, b : b + 1] += jnp.sum(jnp.where(here, block(h, step), 0.0), axis=0, keepdims=True)
        return 0

    lax.fori_loop(first, first + count, inner, 0)


def attention_back(bounds, table, q, do, keep, kv, bias, se, lse):
    heads, n = kv.shape[2] // 128, kv.shape[1]
    return pl.pallas_call(
        bwd_kernel,
        out_shape=(
            jax.ShapeDtypeStruct(q.shape, jnp.bfloat16),
            jax.ShapeDtypeStruct(kv.shape, jnp.bfloat16),
            jax.ShapeDtypeStruct((heads, BUCKETS, TQ), jnp.float32),
        ),
        in_specs=[SMEM_SPEC] * 2 + [VMEM_SPEC] * 7,
        out_specs=(VMEM_SPEC,) * 3,
        scratch_shapes=[
            pltpu.VMEM((heads, 80, n), jnp.bfloat16),
            pltpu.VMEM((heads, 3, 80, TQ), jnp.float32),
            pltpu.VMEM((heads, n, 128), jnp.float32),
            pltpu.VMEM((heads, 4, TK, TQ), jnp.float32),
            pltpu.VMEM((heads, 2, TQ), jnp.float32),
            pltpu.VMEM((2, 2, heads, TQ, 128), jnp.bfloat16),
            pltpu.VMEM((2, 2, heads, TQ, 128), jnp.bfloat16),
            pltpu.VMEM((2, 2, heads, 1, TQ), jnp.float32),
        ],
        compiler_params=pltpu.CompilerParams(vmem_limit_bytes=VMEM_BYTES),
        name="attention_back",
    )(bounds, table, q, do, keep, kv, bias, se, lse)


TAPS = tuple(range(-3, 5))
LEAD = 8


def pool_scalars(y_rows, lab_rows, first):
    tokens = y_rows[0].shape[1]
    t = lax.broadcasted_iota(jnp.int32, (1, tokens), 1)
    at = lambda rows, k: rows[k + 3]
    found = []
    for p in range(2):
        inside = {1: 0 * t, 2: 0 * t + p, 3: (first + 2 * t + p) % 3, 4: 2 * (t % 2) + p}
        weights, scores = {}, []
        for b in range(1, MAX_BLOCK + 1):
            keep = {}
            for o in range(1 - b, b):
                same = jnp.logical_and(inside[b] + o >= 0, inside[b] + o < b)
                same = jnp.logical_and(same, at(lab_rows, p + o) == at(lab_rows, p))
                keep[o] = same.astype(jnp.float32)
            inverse = 1.0 / sum(keep.values())
            for o in keep:
                weights[b, o] = keep[o] * inverse
            scores.append(sum(weights[b, o] * at(y_rows, p + o) for o in keep))
        top = functools.reduce(jnp.maximum, scores)
        grown = [jnp.exp(s - top) for s in scores]
        total = sum(grown)
        found.append(([g / total for g in grown], weights))
    return found


def tap_weights(found):
    rows = []
    for k in TAPS:
        row = 0.0
        for p, (probs, weights) in enumerate(found):
            for b in range(1, MAX_BLOCK + 1):
                if (b, k - p) in weights:
                    row = row + probs[b - 1] * weights[b, k - p]
        rows.append(0.5 * row)
    return rows


def as_columns(rows):
    tokens = rows[0].shape[1]
    return jnp.concatenate(list(rows) + [jnp.zeros((128 - len(rows), tokens), jnp.float32)], axis=0).T


def load_bytes(x_ref, before_ref, after_ref, xs):
    length, width = x_ref.shape
    for j in range(width // 128):
        cols = slice(j * 128, j * 128 + 128)
        xs[j, 0:LEAD, :] = jnp.zeros((LEAD, 128), jnp.float32)
        xs[j, LEAD + length :, :] = jnp.zeros((LEAD, 128), jnp.float32)
        xs[j, LEAD - 2 : LEAD, :] = before_ref[0:2, cols].astype(jnp.float32)
        xs[j, LEAD + length : LEAD + length + 2, :] = after_ref[0:2, cols].astype(jnp.float32)
        xs[j, LEAD : LEAD + length, :] = x_ref[:, cols].astype(jnp.float32)


def tap(xs, k, tokens):
    return jnp.concatenate([xs[j, pl.ds(LEAD + k, tokens, stride=2), :] for j in range(xs.shape[0])], axis=1)


def strips(buf, first, rows):
    return jnp.concatenate([buf[j, first : first + rows, :] for j in range(buf.shape[0])], axis=1)


def unit_rows(values):
    return lax.rsqrt(jnp.mean(values * values, axis=-1, keepdims=True) + 1e-06)


def pool_kernel(shards, scale, x_ref, before_ref, after_ref, lab_ref, score_ref, gain_ref, wq_ref, wk_ref, wv_ref,
                hidden_ref, n1_ref, y_ref, share_ref, q_ref, kv_ref, xs):
    tokens = hidden_ref.shape[0]
    width = hidden_ref.shape[1]
    load_bytes(x_ref, before_ref, after_ref, xs)
    score = jnp.broadcast_to(score_ref[...], (8, width))
    for k in TAPS:
        y_ref[k + 3 : k + 4, :] = mxu(score, tap(xs, k, tokens).astype(jnp.bfloat16), NT)[0:1]
    rows = [y_ref[j : j + 1, :] for j in range(8)]
    labels = [lab_ref[j : j + 1, :] for j in range(8)]
    first = (lax.axis_index("blk") * x_ref.shape[0]) % 3
    found = pool_scalars(rows, labels, first)
    lane = lax.broadcasted_iota(jnp.int32, (1, 128), 1)
    share = jnp.zeros((1, 128), jnp.float32)
    for b in range(MAX_BLOCK):
        share = jnp.where(lane == b, jnp.sum(found[0][0][b] + found[1][0][b], axis=1, keepdims=True) * scale, share)
    share_ref[...] = share
    columns = as_columns(tap_weights(found))
    hidden = sum(columns[:, k + 3 : k + 4] * tap(xs, k, tokens) for k in TAPS)
    hidden_ref[...] = hidden
    n1 = (hidden * unit_rows(hidden) * gain_ref[...].astype(jnp.float32)).astype(jnp.bfloat16)
    n1_ref[...] = n1
    keys = mxu(n1, wk_ref[...]).astype(jnp.bfloat16)
    values = mxu(n1, wv_ref[...]).astype(jnp.bfloat16)
    low = lane < 64
    for j in range(width // 128):
        k_pair, v_pair = keys[:, j * 128 : j * 128 + 128], values[:, j * 128 : j * 128 + 128]
        one = jnp.where(low, k_pair, turned(v_pair))
        two = jnp.where(low, turned(k_pair), v_pair)
        for head, tile in ((2 * j, one), (2 * j + 1, two)):
            kv_ref[head // 3, :, head % 3 * 128 : head % 3 * 128 + 128] = tile
    queries = mxu(n1, wq_ref[...]).astype(jnp.bfloat16) * jnp.bfloat16(0.125)
    put_packed(queries, q_ref)


def put_packed(array, out_ref):
    tokens = array.shape[0]
    half = tokens // 2
    for g in range(GROUPS):
        part = array[:, g * 192 : g * 192 + 192]
        out_ref[g, 0:tokens, :] = part[:, 0:128]
        out_ref[g, tokens:, :] = jnp.concatenate([part[:half, 128:], part[half:, 128:]], axis=1)


def get_packed(packed_ref):
    tokens = packed_ref.shape[1] * 2 // 3
    parts = []
    for g in range(GROUPS):
        last = packed_ref[g, tokens:, :]
        parts += [packed_ref[g, 0:tokens, :], jnp.concatenate([last[:, :64], last[:, 64:]], axis=0)]
    return jnp.concatenate(parts, axis=1)


def pool_and_project(shards, scale, x, before, after, labels, score, gain, wq, wk, wv):
    length, width = x.shape
    tokens = length // 2
    return pl.pallas_call(
        functools.partial(pool_kernel, shards, scale),
        out_shape=(
            jax.ShapeDtypeStruct((tokens, width), jnp.float32),
            jax.ShapeDtypeStruct((tokens, width), jnp.bfloat16),
            jax.ShapeDtypeStruct((8, tokens), jnp.float32),
            jax.ShapeDtypeStruct((1, 128), jnp.float32),
            jax.ShapeDtypeStruct((GROUPS, tokens * 3 // 2, 128), jnp.bfloat16),
            jax.ShapeDtypeStruct((GROUPS, tokens, width * 2 // GROUPS), jnp.bfloat16),
        ),
        in_specs=[VMEM_SPEC] * 9,
        out_specs=(VMEM_SPEC,) * 6,
        scratch_shapes=[pltpu.VMEM((width // 128, length + 2 * LEAD, 128), jnp.float32)],
        compiler_params=pltpu.CompilerParams(vmem_limit_bytes=VMEM_BYTES),
        name="pool_and_project",
    )(x, before, after, labels, score, gain, wq, wk, wv)


GELU_A = math.sqrt(2.0 / math.pi)
GELU_B = 0.044715


def norm_back(d_out, rows, gain):
    unit = unit_rows(rows)
    flat = rows * unit
    scaled = d_out * gain
    d_rows = unit * (scaled - flat * jnp.mean(scaled * flat, axis=-1, keepdims=True))
    return d_rows, jnp.sum(d_out * flat, axis=0, keepdims=True)


def feed_kernel(o_ref, hidden_ref, ct_ref, gain_ref, wo_ref, wg_ref, wu_ref, wd_ref,
                out_ref, dres_ref, da_ref, dgain_ref, n2_ref, att_ref, act_ref, dg_ref, du_ref, db_ref, acc, dn2):
    ff = wg_ref.shape[1]
    step = 512
    att = get_packed(o_ref)
    att_ref[...] = att
    residual = hidden_ref[...] + mxu(att, wo_ref[...])
    gain = gain_ref[...].astype(jnp.float32)
    n2_ref[...] = (residual * unit_rows(residual) * gain).astype(jnp.bfloat16)
    acc[...] = residual
    dn2[...] = jnp.zeros_like(dn2)

    for j in range(ff // step):
        cols = slice(j * step, j * step + step)
        n2 = n2_ref[...]
        gate = mxu(n2, wg_ref[:, cols])
        up = mxu(n2, wu_ref[:, cols])
        d_act = mxu(ct_ref[...], wd_ref[cols, :], NT)
        square = gate * gate
        curve = jnp.tanh(GELU_A * gate * (1.0 + GELU_B * square))
        half = 0.5 * (1.0 + curve)
        grown = gate * half
        slope = half + 0.5 * gate * (1.0 - curve * curve) * (GELU_A * (1.0 + 3.0 * GELU_B * square))
        act = (grown * up).astype(jnp.bfloat16)
        d_gate = (d_act * up * slope).astype(jnp.bfloat16)
        d_up = (d_act * grown).astype(jnp.bfloat16)
        act_ref[:, cols] = act
        dg_ref[:, cols] = d_gate
        du_ref[:, cols] = d_up
        acc[...] += mxu(act, wd_ref[cols, :])
        dn2[...] += mxu(d_gate, wg_ref[:, cols], NT) + mxu(d_up, wu_ref[:, cols], NT)

    out_ref[...] = acc[...].astype(jnp.bfloat16)
    residual = hidden_ref[...] + mxu(att_ref[...], wo_ref[...])
    d_rows, d_gain = norm_back(dn2[...], residual, gain)
    dgain_ref[...] = d_gain
    d_res = ct_ref[...].astype(jnp.float32) + d_rows
    dres_ref[...] = d_res
    d_branch = d_res.astype(jnp.bfloat16)
    db_ref[...] = d_branch
    put_packed(mxu(d_branch, wo_ref[...], NT).astype(jnp.bfloat16), da_ref)


def feed_forward(o_home, hidden, ct, gain, wo, wg, wu, wd):
    tokens, width = hidden.shape
    ff = wg.shape[1]
    low = lambda cols: jax.ShapeDtypeStruct((tokens, cols), jnp.bfloat16)
    return pl.pallas_call(
        feed_kernel,
        out_shape=(
            low(width),
            jax.ShapeDtypeStruct((tokens, width), jnp.float32),
            jax.ShapeDtypeStruct(o_home.shape, jnp.bfloat16),
            jax.ShapeDtypeStruct((1, width), jnp.float32),
            low(width), low(width), low(ff), low(ff), low(ff), low(width),
        ),
        in_specs=[VMEM_SPEC] * 8,
        out_specs=(VMEM_SPEC,) * 10,
        scratch_shapes=[pltpu.VMEM((tokens, width), jnp.float32)] * 2,
        compiler_params=pltpu.CompilerParams(vmem_limit_bytes=VMEM_BYTES),
        name="feed_forward",
    )(o_home, hidden, ct, gain, wo, wg, wu, wd)


def last_kernel(with_blocks, dq_ref, dkv_ref, hidden_ref, dres_ref, n1_ref, x_ref, before_ref, after_ref, lab_ref, y_ref, score_ref,
                gain_ref, wq_ref, wk_ref, wv_ref, dgain2_ref, share_ref, tab_ref,
                gb_ref, edge_ref, spill_ref, small_ref, w_ref, xs, gbuf, *grads):
    tokens, width = hidden_ref.shape
    length = x_ref.shape[0]
    lane = lax.broadcasted_iota(jnp.int32, (1, 128), 1)
    low = lane < 64
    dq = get_packed(dq_ref)
    dk_parts, dv_parts = [], []
    for j in range(width // 128):
        one, two = [dkv_ref[h // 3, :, h % 3 * 128 : h % 3 * 128 + 128] for h in (2 * j, 2 * j + 1)]
        dk_parts.append(jnp.where(low, one, turned(two)))
        dv_parts.append(jnp.where(low, turned(one), two))
    dk, dv = jnp.concatenate(dk_parts, axis=1), jnp.concatenate(dv_parts, axis=1)
    d_n1 = mxu(dq, wq_ref[...], NT) + mxu(dk, wk_ref[...], NT) + mxu(dv, wv_ref[...], NT)
    d_rows, d_gain1 = norm_back(d_n1, hidden_ref[...], gain_ref[...].astype(jnp.float32))
    d_hidden = dres_ref[...] + d_rows

    load_bytes(x_ref, before_ref, after_ref, xs)
    met = jnp.zeros((tokens, 128), jnp.float32)
    for k in TAPS:
        met = jnp.where(lane == k + 3, jnp.sum(d_hidden * tap(xs, k, tokens), axis=-1, keepdims=True), met)
    met = met.T
    first = (lax.axis_index("blk") * length) % 3
    found = pool_scalars([y_ref[j : j + 1, :] for j in range(8)], [lab_ref[j : j + 1, :] for j in range(8)], first)
    touch = [0.0] * 8
    for p, (probs, weights) in enumerate(found):
        d_block = []
        for b in range(1, MAX_BLOCK + 1):
            d_block.append(0.5 * sum(weights[b, o] * met[p + o + 3 : p + o + 4] for o in range(1 - b, b)))
        mean = sum(q * d for q, d in zip(probs, d_block))
        for b in range(1, MAX_BLOCK + 1):
            d_score = probs[b - 1] * (d_block[b - 1] - mean)
            for o in range(1 - b, b):
                touch[p + o + 3] = touch[p + o + 3] + d_score * weights[b, o]
    share_cols = as_columns(tap_weights(found) + touch)
    score = score_ref[...].astype(jnp.float32)
    gbuf[...] = jnp.zeros_like(gbuf)
    d_score_vec = jnp.zeros((1, width), jnp.float32)
    for k in TAPS:
        own, via = share_cols[:, k + 3 : k + 4], share_cols[:, k + 11 : k + 12]
        added = own * d_hidden + via * score
        for j in range(gbuf.shape[0]):
            gbuf[j, pl.ds(LEAD + k, tokens, stride=2), :] += added[:, j * 128 : j * 128 + 128]
        d_score_vec = d_score_vec + jnp.sum(via * tap(xs, k, tokens), axis=0, keepdims=True)
    gb_ref[...] = strips(gbuf, LEAD, length).astype(jnp.bfloat16)
    edge_ref[0] = strips(gbuf, LEAD, 16)
    edge_ref[1] = strips(gbuf, LEAD + length - 16, 16)
    spill_ref[0] = strips(gbuf, 0, LEAD)
    spill_ref[1] = strips(gbuf, LEAD + length, LEAD)

    small_ref[...] = jnp.zeros_like(small_ref)
    for row, vector in ((0, d_score_vec), (6, d_gain1), (12, dgain2_ref[...])):
        for j in range(width // 128):
            small_ref[row + j : row + j + 1, :] = vector[:, j * 128 : j * 128 + 128]
    heads = tab_ref.shape[0]
    group = lax.axis_index("blk") // (lax.axis_size("blk") // GROUPS)
    for h in range(heads):
        total = lax.dot_general(
            jnp.ones((8, tab_ref.shape[2]), jnp.float32), tab_ref[h], NT,
            precision=lax.Precision.HIGHEST, preferred_element_type=jnp.float32,
        )
        small_ref[pl.ds(18 + group * heads + h, 1), 0:BUCKETS] = total[0:1]
    small_ref[30:31, :] = share_ref[...]

    if with_blocks:
        (whole,) = grads
        n1_t = n1_ref[...].T
        for j, part in enumerate((dq, dk, dv)):
            whole[j] = mxu(n1_t, part)
        per = width // w_ref.shape[0]

        def block(d, _):
            start = pl.multiple_of(d * per, 8)
            parts = [whole[j, pl.ds(start, per), :] for j in range(3)]
            parts.append(jnp.zeros((w_ref.shape[1] - 3 * per, width), jnp.float32))
            w_ref[d] = jnp.concatenate(parts, axis=0).astype(jnp.bfloat16)
            return 0

        lax.fori_loop(0, w_ref.shape[0], block, 0)
    else:
        w_ref[0] = dq
        w_ref[1] = dk
        w_ref[2] = dv


def last_part(devices, dq, dkv, hidden, dres, n1, x, before, after, labels, y, score, gain, wq, wk, wv, dgain2, share, tab):
    tokens, width = hidden.shape
    length = x.shape[0]
    with_blocks = devices <= 32
    full = jax.ShapeDtypeStruct
    blocks = (devices, -(-3 * (width // devices) // 16) * 16, width) if with_blocks else (3, tokens, width)
    scratch = [pltpu.VMEM((width // 128, length + 2 * LEAD, 128), jnp.float32)] * 2
    if with_blocks:
        scratch.append(pltpu.VMEM((3, width, width), jnp.float32))
    return pl.pallas_call(
        functools.partial(last_kernel, with_blocks),
        out_shape=(
            full((length, width), jnp.bfloat16),
            full((2, 16, width), jnp.float32),
            full((2, LEAD, width), jnp.float32),
            full((32, 128), jnp.float32),
            full(blocks, jnp.bfloat16),
        ),
        in_specs=[VMEM_SPEC] * 18,
        out_specs=(VMEM_SPEC,) * 5,
        scratch_shapes=scratch,
        compiler_params=pltpu.CompilerParams(vmem_limit_bytes=VMEM_BYTES),
        name="last_part",
    )(dq, dkv, hidden, dres, n1, x, before, after, labels, y, score, gain, wq, wk, wv, dgain2, share, tab)


def finish_kernel(shards, heads_all, gb_ref, edge_ref, spill_ref, small_ref, *refs):
    position = lax.axis_index("blk")
    streams, outs = refs[: len(refs) - (5 if len(refs) == 5 else 12)], refs[len(refs) - (5 if len(refs) == 5 else 12) :]
    bytes_ref, score_ref, gain1_ref, gain2_ref, tab_ref = outs[:5]
    length = gb_ref.shape[0]
    bytes_ref[...] = gb_ref[...]
    zero = jnp.zeros((16 - LEAD, gb_ref.shape[1]), jnp.float32)
    left = jnp.where(position > 0, spill_ref[0], 0.0)
    right = jnp.where(position < shards - 1, spill_ref[1], 0.0)
    bytes_ref[0:16, :] = (edge_ref[0] + jnp.concatenate([left, zero], axis=0)).astype(jnp.bfloat16)
    bytes_ref[length - 16 :, :] = (edge_ref[1] + jnp.concatenate([zero, right], axis=0)).astype(jnp.bfloat16)
    for row, ref in ((0, score_ref), (6, gain1_ref), (12, gain2_ref)):
        for j in range(6):
            ref[:, j * 128 : j * 128 + 128] = small_ref[row + j : row + j + 1, :]
    tab_ref[...] = small_ref[16:32, :]
    if streams:
        gq, gk, gv, go, gg, gu, gd = outs[5:]
        per = gq.shape[0]
        wide_a, wide_b, slim, *thirds = streams
        for j, ref in enumerate((gq, gk, gv)):
            for c, third in enumerate(thirds):
                ref[:, c * 256 : c * 256 + 256] = third[j * per : j * per + per, :]
        half = wide_a.shape[1]
        for c, ref in ((0, wide_a), (1, wide_b)):
            gg[:, c * half : c * half + half] = ref[0:per, :]
            gu[:, c * half : c * half + half] = ref[per : 2 * per, :]
        go[...] = slim[0:per, :]
        gd[...] = slim[32:, :]


def finish(shards, heads_all, per, ff, gb, edge, spill, small, streams):
    width = gb.shape[1]
    full = jax.ShapeDtypeStruct
    line = full((1, width), jnp.float32)
    outs = [full(gb.shape, jnp.bfloat16), line, line, line, full((16, 128), jnp.float32)]
    if streams:
        square, broad = full((per, width), jnp.float32), full((per, ff), jnp.float32)
        outs += [square] * 4 + [broad] * 2 + [full((streams[2].shape[0] - 32, width), jnp.float32)]
    return pl.pallas_call(
        functools.partial(finish_kernel, shards, heads_all),
        out_shape=tuple(outs),
        in_specs=[VMEM_SPEC] * (4 + len(streams)),
        out_specs=(VMEM_SPEC,) * len(outs),
        compiler_params=pltpu.CompilerParams(vmem_limit_bytes=VMEM_BYTES),
        name="finish",
    )(gb, edge, spill, small, *streams)


def neighbours(rows):
    peers = lax.axis_size("blk")
    up = [(i, i + 1) for i in range(peers - 1)]
    last, leading = rows
    return lax.ppermute(last, "blk", up), lax.ppermute(leading, "blk", [(j, i) for i, j in up])


def body(
    byte_embeds,
    segments,
    score_weight,
    norm_gain1,
    w_query,
    w_key,
    w_value,
    w_out,
    rel_bias,
    norm_gain2,
    w_gate,
    w_up,
    w_down,
    cotangent,
):
    row_count, length, width = byte_embeds.shape
    tokens = length // 2
    shards = lax.axis_size("blk")
    shape = {"dp": lax.axis_size("dp"), "blk": shards}
    devices = shards * shape["dp"]
    heads = rel_bias.shape[1] // GROUPS
    position = lax.axis_index("blk")
    rest_size = shards // GROUPS
    group, rest = position // rest_size, position % rest_size
    row = lax.axis_index("dp") % 2
    x, ids_here = byte_embeds[0], segments[0]

    marks = (ids_here + 1).astype(jnp.bfloat16)
    with_marks = lambda part, two: jnp.concatenate([part, jnp.pad(two, (0, width - 2))[None]], axis=0)
    before, after = neighbours((with_marks(x[-2:], marks[-2:]), with_marks(x[:2], marks[:2])))
    line = jnp.concatenate([before[2, :2], marks, after[2, :2]])
    line = jnp.pad(line, (1, 1)).astype(jnp.int32).reshape(tokens + 3, 2).T
    labels = jnp.stack([line[j % 2, j // 2 : j // 2 + tokens] for j in range(8)])

    score_row, gain1, gain2 = score_weight[None], norm_gain1[None], norm_gain2[None]
    hidden, n1, y, share, q_packed, kv_parts = pool_and_project(
        shards, 1.0 / (row_count * length * devices), x, before, after, labels, score_row, gain1, w_query, w_key, w_value
    )

    label_block = jnp.pad(ids_here[0::2].reshape(tokens // 128, 128), ((0, 8 - tokens // 128), (0, 0)))
    q_all, kv_all, labels_all = gather_all(shards, q_packed, kv_parts, label_block)
    labels_all = labels_all.reshape(2, shards, 8, 128)[:, :, : tokens // 128].reshape(2, shards * tokens)
    ids = jnp.arange(8, dtype=jnp.int32)
    counts = jnp.sum((labels_all[:, None, :] == ids[None, :, None]).astype(jnp.int32), axis=2)
    ends = jnp.sum(jnp.where(ids[None, :] <= ids[:, None], counts[:, None, :], 0), axis=2)
    begins = ends - counts
    query_labels = jnp.stack(
        [lax.dynamic_slice_in_dim(labels_all, ((2 * row + i) * rest_size + rest) * tokens, tokens, 1) for i in range(2)],
        axis=1,
    )
    chosen = query_labels[:, :, None, :] == ids[None, None, :, None]
    span = jnp.stack(
        [jnp.sum(jnp.where(chosen, edge[:, None, :, None], 0), axis=2) for edge in (begins, ends)], axis=2
    )
    parity = rest % 2
    firsts = jnp.stack([((2 * row + i) * rest_size + rest) * tokens for i in range(2)])
    near = jnp.broadcast_to((firsts // TK - 1 + parity)[None], (2, 2))
    bounds = jnp.stack(
        [
            jnp.min(span[:, :, 0], axis=-1) // TK,
            -(-jnp.max(span[:, :, 1], axis=-1) // TK),
            near,
            -(-jnp.max(span[:, :, 0], axis=-1) // TK),
            jnp.min(span[:, :, 1], axis=-1) // TK,
            jnp.broadcast_to(parity, (2, 2)),
        ],
        axis=-1,
    ).astype(jnp.int32)
    table = lax.dynamic_slice_in_dim(rel_bias.astype(jnp.float32).T, group * heads, heads, 0)

    o_packed, o_kept, log_total, bias_tiles = attention(bounds, table, q_all, kv_all, span)
    o_home = move_heads(return_kernel, (GROUPS,), shards, 4, o_packed)
    ct = cotangent[0]
    block_out, d_res, da_packed, d_gain2, n2, att, act, d_gate, d_up, d_branch = feed_forward(
        o_home, hidden, ct, gain2, w_out, w_gate, w_up, w_down
    )

    orders, pairs = [], []
    if devices == 32:
        do_all, keep_a, send_a, keep_b, send_b, keep_c, send_c = spread_and_weights(
            shards, da_packed, n2, att, act, d_gate, d_up, ct, d_branch
        )
        swap = lambda part, axis, mask: lax.ppermute(part, axis, [(i, i ^ mask) for i in range(lax.axis_size(axis))])
        orders = [((1, 2, 3), (3, 2, 1)), ((0, 1, 2), (0, 2, 1)), ((0, 1, 3), (3, 0, 1))]
        pairs = [(keep_a, swap(send_a, "dp", 1)), (keep_b, swap(send_b, "blk", 2)), (keep_c, swap(send_c, "blk", 4))]
    else:
        do_all = move_heads(spread_kernel, (2, 2), shards, 5, da_packed)

    dq_packed, dkv_all, d_table_lanes = attention_back(
        bounds, table, q_all, do_all, o_kept, kv_all, bias_tiles, span, log_total
    )
    dq_home, dkv_home, *sums = reduce_all(shape, dq_packed, dkv_all, orders, pairs)
    grad_bytes, edge, spill, small, last_blocks = last_part(
        devices, dq_home, dkv_home, hidden, d_res, n1, x, before, after, labels, y, score_row, gain1,
        w_query, w_key, w_value, d_gain2, share, d_table_lanes,
    )
    across = len(bits_of(shape["dp"]))
    ndim = across + len(bits_of(shards))
    small_order = tuple(reversed(range(ndim)))
    if devices == 32:
        third = width // 3
        blocks = [last_blocks[:, :, c * third : c * third + third] for c in range(3)]
        thirds, small, spill = last_sums(
            shape, blocks, [(4, 0, 3, 2, 1), (4, 3, 2, 1, 0), (4, 2, 0, 3, 1), small_order], small, spill
        )
        sums = list(sums) + list(thirds)
    else:
        _, small, spill = last_sums(shape, [], [small_order], small, spill)
    per = width // devices
    grad_bytes, g_score, g_gain1, g_gain2, rows, *grads = finish(
        shards, rel_bias.shape[1], per, w_gate.shape[1], grad_bytes, edge, spill, small, sums
    )
    if devices != 32:
        product = lambda left, right: jnp.einsum("td,te->de", left, right, preferred_element_type=jnp.float32)
        grads = [product(n1, last_blocks[j]) for j in range(3)]
        grads += [product(att, d_branch), product(n2, d_gate), product(n2, d_up), product(act, ct)]
        grads = [lax.psum_scatter(grad, ("dp", "blk"), scatter_dimension=0, tiled=True) for grad in grads]
    return (
        block_out[None],
        grad_bytes[None],
        g_score[0],
        g_gain1[0],
        *grads[:4],
        rows[2 : 2 + rel_bias.shape[1], :BUCKETS].T,
        g_gain2[0],
        *grads[4:],
        rows[14, :MAX_BLOCK],
    )


def solution(mesh):
    placed = (
        P("dp", "blk", None),
        P("dp", "blk"),
        P(),
        P(),
        P(),
        P(),
        P(),
        P(),
        P(),
        P(),
        P(),
        P(),
        P(),
        P("dp", "blk", None),
    )
    return jax.shard_map(
        body,
        mesh=mesh,
        in_specs=placed,
        out_specs=(
            P("dp", "blk", None),
            P("dp", "blk", None),
            P(),
            P(),
            P(("dp", "blk"), None),
            P(("dp", "blk"), None),
            P(("dp", "blk"), None),
            P(("dp", "blk"), None),
            P(),
            P(),
            P(("dp", "blk"), None),
            P(("dp", "blk"), None),
            P(("dp", "blk"), None),
            P(),
        ),
        check_vma=False,
    )
```

```python
import functools
import math

import jax
import jax.numpy as jnp
from jax import lax
from jax.experimental import pallas as pl
from jax.experimental.pallas import tpu as pltpu
from jax.sharding import PartitionSpec as P

BUCKETS = 32
MAX_BLOCK = 4
VMEM_BYTES = 60 * 2**20


def buckets_of(relative):
    distance = jnp.abs(relative)
    beyond = jnp.zeros_like(distance)
    for border in (12, 16, 23, 32, 46, 64, 91):
        beyond = beyond + (distance >= border).astype(jnp.int32)
    nearer = jnp.where(distance < 8, distance, 8 + beyond)
    return nearer + BUCKETS // 2 * (relative > 0).astype(jnp.int32)


MESH_ID = pl.DeviceIdType.MESH
GROUPS = 4


def bits_of(size):
    return [1 << p for p in reversed(range(size.bit_length() - 1))]


def bit(value, mask):
    return (value // mask) % 2


def flipped(value, mask):
    return value + mask * (1 - 2 * bit(value, mask))


class Place:
    def __init__(self, shards):
        self.shards = shards
        self.rest_size = shards // GROUPS
        self.dp = lax.axis_index("dp")
        self.blk = lax.axis_index("blk")
        self.row = self.dp % 2
        self.group = self.blk // self.rest_size
        self.rest = self.blk % self.rest_size

    def at(self, row, group, rest):
        return (self.dp - self.row + row, group * self.rest_size + rest)

    def chunk(self, group, rest):
        return group * self.rest_size + rest

    def other_row(self):
        return self.at(1 - self.row, self.group, self.rest)

    def other_rest(self, mask):
        return self.at(self.row, self.group, flipped(self.rest, mask))

    def other_group(self, step):
        return self.at(self.row, (self.group + step) % GROUPS, self.rest)


def hail(targets):
    barrier = pltpu.get_barrier_semaphore()
    for target in targets:
        pl.semaphore_signal(barrier, inc=1, device_id=target, device_id_type=MESH_ID)
    return len(targets)


def await_all(count):
    pl.semaphore_wait(pltpu.get_barrier_semaphore(), count)


def greet(targets):
    await_all(hail(targets))


def remote(src, dst, send_sem, recv_sem, target):
    return pltpu.make_async_remote_copy(
        src_ref=src,
        dst_ref=dst,
        send_sem=send_sem,
        recv_sem=recv_sem,
        device_id=target,
        device_id_type=MESH_ID,
    )


def line_and_row(place):
    found = []
    for step in range(GROUPS):
        for flip in range(2):
            if step or flip:
                row = 1 - place.row if flip else place.row
                found.append(place.at(row, (place.group + step) % GROUPS, place.rest))
    return found


def spread_heads(place, q_ref, out_ref, send_sem, recv_sem):
    row_to = place.group // 2
    slot = place.group % 2
    dst = out_ref.at[place.row, slot]
    mine = recv_sem.at[place.row * 2 + slot]
    at_home = row_to == place.row
    for step in range(GROUPS):
        group = (place.group + step) % GROUPS
        src = q_ref.at[group]
        copy = remote(src, dst, send_sem.at[step], mine, place.at(row_to, group, place.rest))
        if step:
            copy.start()
        else:
            pl.when(jnp.logical_not(at_home))(copy.start)
            pl.when(at_home)(pltpu.make_async_copy(src, dst, mine).start)


def spread_heads_wait(place, q_ref, out_ref, send_sem, recv_sem):
    at_home = place.group // 2 == place.row
    for row in range(2):
        for slot in range(2):
            pltpu.make_async_copy(q_ref.at[0], out_ref.at[row, slot], recv_sem.at[row * 2 + slot]).wait()
    for step in range(GROUPS):
        copy = remote(q_ref.at[0], out_ref.at[0, 0], send_sem.at[step], recv_sem.at[0], place.other_row())
        if step:
            copy.wait_send()
        else:
            pl.when(jnp.logical_not(at_home))(copy.wait_send)


def return_heads(place, o_ref, out_ref, send_sem, recv_sem):
    for row in range(2):
        for slot in range(2):
            group = place.row * 2 + slot
            src = o_ref.at[row, slot]
            dst = out_ref.at[place.group]
            mine = recv_sem.at[place.group]
            at_home = jnp.logical_and(place.row == row, place.group == group)
            copy = remote(src, dst, send_sem.at[row * 2 + slot], mine, place.at(row, group, place.rest))
            pl.when(jnp.logical_not(at_home))(copy.start)
            pl.when(at_home)(pltpu.make_async_copy(src, dst, mine).start)


def return_heads_wait(place, o_ref, out_ref, send_sem, recv_sem):
    for group in range(GROUPS):
        pltpu.make_async_copy(o_ref.at[0, 0], out_ref.at[group], recv_sem.at[group]).wait()
    for row in range(2):
        for slot in range(2):
            group = place.row * 2 + slot
            at_home = jnp.logical_and(place.row == row, place.group == group)
            copy = remote(o_ref.at[0, 0], out_ref.at[0], send_sem.at[row * 2 + slot], recv_sem.at[0], place.other_row())
            pl.when(jnp.logical_not(at_home))(copy.wait_send)


def spread_kernel(shards, q_ref, out_ref, send_sem, recv_sem):
    place = Place(shards)
    greet(line_and_row(place))
    spread_heads(place, q_ref, out_ref, send_sem, recv_sem)
    spread_heads_wait(place, q_ref, out_ref, send_sem, recv_sem)


def return_kernel(shards, o_ref, out_ref, send_sem, recv_sem):
    place = Place(shards)
    greet(line_and_row(place))
    return_heads(place, o_ref, out_ref, send_sem, recv_sem)
    return_heads_wait(place, o_ref, out_ref, send_sem, recv_sem)


SMEM_SPEC = pl.BlockSpec(memory_space=pltpu.SMEM)
VMEM_SPEC = pl.BlockSpec(memory_space=pltpu.VMEM)


def move_heads(kernel, lead, shards, ident, packed):
    rows, lanes = packed.shape[-2:]
    return pl.pallas_call(
        functools.partial(kernel, shards),
        out_shape=jax.ShapeDtypeStruct(lead + (rows, lanes), packed.dtype),
        in_specs=[pl.BlockSpec(memory_space=pltpu.VMEM)],
        out_specs=pl.BlockSpec(memory_space=pltpu.VMEM),
        scratch_shapes=[pltpu.SemaphoreType.DMA((4,)), pltpu.SemaphoreType.DMA((4,))],
        compiler_params=pltpu.CompilerParams(collective_id=ident, has_side_effects=True, vmem_limit_bytes=VMEM_BYTES),
        name="move_heads_%d" % ident,
    )(packed)


def gather_kernel(shards, q_ref, kv_ref, label_ref, qo_ref, kvo_ref, labo_ref, q_send, q_recv, z_send, far_send, core_send, kv_recv, own_sem, lab_send, lab_recv):
    place = Place(shards)
    tokens = kv_ref.shape[1]
    rest_bits = bits_of(place.rest_size)
    core, far = rest_bits[-1], ["row"] + rest_bits[:-1]
    greet(line_and_row(place) + [place.other_rest(mask) for mask in rest_bits])

    dims = [("row", 1)] + [("blk", m) for m in bits_of(shards)]
    lab_index = [place.row] + [bit(place.blk, m) for _, m in dims[1:]]
    lab_order = list(range(len(dims)))

    def lab_copy(stage):
        index = tuple(slice(None) if p in lab_order[:stage] else lab_index[p] for p in range(len(dims)))
        axis, mask = dims[lab_order[stage]]
        target = place.other_row() if axis == "row" else (place.dp, flipped(place.blk, mask))
        there = labo_ref.at[index]
        return remote(there, there, lab_send.at[stage], lab_recv.at[stage], target)

    labo_ref[tuple(lab_index)] = label_ref[...]
    lab_copy(0).start()
    lab_stage = 0

    def slot(row, group, rest):
        start = pl.multiple_of(place.chunk(group, rest) * tokens, tokens)
        return kvo_ref.at[row, pl.ds(start, tokens)]

    def held(dz, offset, core_off):
        row = 1 - place.row if offset & 1 else place.row
        rest = place.rest
        for p, mask in enumerate(far[1:]):
            if offset >> (p + 1) & 1:
                rest = flipped(rest, mask)
        if core_off:
            rest = flipped(rest, core)
        return slot(row, (place.group + dz) % GROUPS, rest)

    count = 1 << len(far)

    def sem_of(dz, offset, core_off):
        return kv_recv.at[(core_off * count + offset) * GROUPS + dz]

    own = pltpu.make_async_copy(kv_ref.at[place.group], held(0, 0, 0), own_sem)
    own.start()
    waits = []
    for step in (1, 3, 2):
        copy = remote(kv_ref.at[(place.group + step) % GROUPS], held(0, 0, 0), z_send.at[step], sem_of((GROUPS - step) % GROUPS, 0, 0), place.other_group(step))
        copy.start()
        waits.append(copy)

    used = 0
    events = sorted(((dz, off) for dz in range(GROUPS) for off in range(count)), key=lambda e: (bin(e[1]).count("1"), (0, 1, 3, 2).index(e[0])))
    core_target = place.other_rest(core)
    for step, (dz, off) in enumerate(events):
        if step == GROUPS:
            spread_heads(place, q_ref, qo_ref, q_send, q_recv)
        here = held(dz, off, 0)
        if dz == 0 and off == 0:
            src = kv_ref.at[place.group]
        else:
            remote(here, here, z_send.at[0], sem_of(dz, off, 0), core_target).wait_recv()
            src = here
        order = [(p + dz) % len(far) for p in range(len(far))]
        last = max([order.index(p) for p in range(len(far)) if off >> p & 1], default=-1)
        for p in order[last + 1 :]:
            target = place.other_row() if p == 0 else place.other_rest(far[p])
            copy = remote(src, here, far_send.at[used], sem_of(dz, off | 1 << p, 0), target)
            copy.start()
            waits.append(copy)
            used += 1
        copy = remote(src, here, core_send.at[off * GROUPS + dz], sem_of(dz, off, 1), core_target)
        copy.start()
        waits.append(copy)
        if lab_stage < len(dims):
            lab_copy(lab_stage).wait()
            lab_stage += 1
            if lab_stage < len(dims):
                lab_copy(lab_stage).start()
    for dz, off in events:
        here = held(dz, off, 1)
        remote(here, here, z_send.at[0], sem_of(dz, off, 1), core_target).wait_recv()
    own.wait()
    for copy in waits:
        copy.wait_send()
    spread_heads_wait(place, q_ref, qo_ref, q_send, q_recv)


def gather_all(shards, q_packed, kv_parts, labels):
    tokens, width = kv_parts.shape[1:]
    far = 1 + len(bits_of(shards // GROUPS)) - 1
    count = 1 << far
    nbits = 1 + len(bits_of(shards))
    sem = pltpu.SemaphoreType.DMA
    return pl.pallas_call(
        functools.partial(gather_kernel, shards),
        out_shape=(
            jax.ShapeDtypeStruct((2, 2) + q_packed.shape[1:], q_packed.dtype),
            jax.ShapeDtypeStruct((2, shards * tokens, width), kv_parts.dtype),
            jax.ShapeDtypeStruct((2,) * nbits + labels.shape, labels.dtype),
        ),
        in_specs=[pl.BlockSpec(memory_space=pltpu.VMEM)] * 3,
        out_specs=(pl.BlockSpec(memory_space=pltpu.VMEM),) * 3,
        scratch_shapes=[
            sem((4,)), sem((4,)), sem((GROUPS,)), sem((GROUPS * (count - 1),)), sem((GROUPS * count,)), sem((GROUPS * count * 2,)),
            sem, sem((nbits,)), sem((nbits,)),
        ],
        compiler_params=pltpu.CompilerParams(collective_id=1, has_side_effects=True, vmem_limit_bytes=VMEM_BYTES),
        name="gather_keys",
    )(q_packed, kv_parts, labels)


def add_blocks(dst_ref, src_ref, index, shape):
    lead = shape[:-2]
    total = math.prod(lead)

    def one(step, _):
        place, left = [], step
        for size in reversed(lead):
            place.append(left % size)
            left = left // size
        place = tuple(reversed(place))
        full, k = [], 0
        for entry in index:
            if entry is None:
                full.append(place[k])
                k += 1
            else:
                full.append(entry)
        mine = src_ref[tuple(full)].astype(jnp.float32)
        dst_ref[place] = (dst_ref[place].astype(jnp.float32) + mine).astype(dst_ref.dtype)
        return 0

    lax.fori_loop(0, total, one, 0)


class Stream:
    def __init__(self, axes, at, kept, order, src, bufs, out, send_sem, recv_sem):
        self.axes, self.at, self.kept, self.order = axes, at, kept, order
        self.src, self.bufs, self.out = src, bufs, out
        self.send_sem, self.recv_sem = send_sem, recv_sem

    def own(self, p):
        axis, mask = self.axes[p]
        return bit(self.at[axis], mask)

    def target(self, p):
        axis, mask = self.axes[p]
        moved = dict(self.at)
        moved[axis] = flipped(self.at[axis], mask)
        return (moved["dp"], moved["blk"])

    def stage(self, k):
        kept = [p for p in self.kept if p not in self.order[:k]]
        return kept, self.src if k == 0 else self.bufs[k - 1], self.order[k]

    def copy(self, k):
        kept, src, now = self.stage(k)
        index = tuple(1 - self.own(p) if p == now else slice(None) for p in kept)
        return remote(src.at[index], self.bufs[k], self.send_sem.at[k], self.recv_sem.at[k], self.target(now))

    def absorb(self, k):
        kept, src, now = self.stage(k)
        buf = self.bufs[k]
        if k == len(self.order) - 1 and self.out is not None:
            mine = src[self.own(now)].astype(jnp.float32)
            self.out[...] = buf[...].astype(jnp.float32) + mine
        else:
            add_blocks(buf, src, tuple(self.own(p) if p == now else None for p in kept), buf.shape)


class Whole:
    def __init__(self, axes, at, order, src, bufs, out, send_sem, recv_sem):
        self.stream = Stream(axes, at, order, order, src, bufs, out, send_sem, recv_sem)
        self.order, self.src, self.bufs, self.out = order, src, bufs, out

    def held(self, k):
        return self.src if k == 0 else self.bufs.at[1, k - 1]

    def copy(self, k):
        s = self.stream
        return remote(self.held(k), self.bufs.at[0, k], s.send_sem.at[k], s.recv_sem.at[k], s.target(self.order[k]))

    def absorb(self, k):
        total = self.held(k)[...] + self.bufs[0, k]
        if k == len(self.order) - 1:
            self.out[...] = total
        else:
            self.bufs[1, k] = total


def advance(stream, stage):
    if stage < len(stream.order):
        stream.copy(stage).wait()
        stream.absorb(stage)
        if stage < len(stream.order) - 1:
            stream.copy(stage + 1).start()


def bit_axes(shape):
    return [("dp", m) for m in bits_of(shape["dp"])] + [("blk", m) for m in bits_of(shape["blk"])]


def stream_scratch(lead, order, rows, cols):
    return [pltpu.VMEM((2,) * (lead - 1 - k) + (rows, cols), jnp.bfloat16) for k in range(len(order))]


def weights_kernel(shards, da_ref, n2_ref, act_ref, dg_ref, du_ref, ct_ref,
                   do_ref, left_ref, right_ref, slim_ref,
                   q_send, q_recv, core_send, core_recv, gate, up, down, wide_out, slim_out, wide_in, slim_in):
    place = Place(shards)
    core_target = place.other_rest(1)
    greet(line_and_row(place) + [core_target])
    spread_heads(place, da_ref, do_ref, q_send, q_recv)
    per = gate.shape[0] // 32
    per_ff = down.shape[0] // 32
    half = wide_out.shape[2] // 2
    core = place.rest % 2

    n2_t = n2_ref[...].T
    step = 512
    for j in range(gate.shape[1] // step):
        cols = slice(j * step, j * step + step)
        gate[:, cols] = mxu(n2_t, dg_ref[:, cols])
        up[:, cols] = mxu(n2_t, du_ref[:, cols])

    def wide_rows(block):
        rows = pl.ds(pl.multiple_of(block * per, 8), per)
        return jnp.concatenate([gate[rows, :], up[rows, :]], axis=0)

    def slim_rows(block):
        return down[pl.ds(pl.multiple_of(block * per_ff, 8), per_ff), :]

    def send_wide(m, _):
        wide_out[m] = wide_rows(2 * m + 1 - core).astype(jnp.bfloat16)
        return 0

    lax.fori_loop(0, 16, send_wide, 0)
    wide_copy = remote(wide_out, wide_in, core_send.at[0], core_recv.at[0], core_target)
    wide_copy.start()
    for j in range(down.shape[0] // step):
        rows = slice(j * step, j * step + step)
        down[rows, :] = mxu(act_ref[:, rows].T, ct_ref[...])

    def send_slim(m, _):
        slim_out[m] = slim_rows(2 * m + 1 - core).astype(jnp.bfloat16)
        return 0

    lax.fori_loop(0, 16, send_slim, 0)
    slim_copy = remote(slim_out, slim_in, core_send.at[1], core_recv.at[1], core_target)
    slim_copy.start()

    wide_copy.wait()

    def sum_wide(m, _):
        total = wide_rows(2 * m + core) + wide_in[m].astype(jnp.float32)
        left_ref[m] = total[:, :half].astype(jnp.bfloat16)
        right_ref[m] = total[:, half:].astype(jnp.bfloat16)
        return 0

    lax.fori_loop(0, 16, sum_wide, 0)
    slim_copy.wait()

    def sum_slim(m, _):
        slim_ref[m] = (slim_rows(2 * m + core) + slim_in[m].astype(jnp.float32)).astype(jnp.bfloat16)
        return 0

    lax.fori_loop(0, 16, sum_slim, 0)
    spread_heads_wait(place, da_ref, do_ref, q_send, q_recv)


def spread_and_weights(shards, da, n2, act, dg, du, ct):
    width, ff = n2.shape[1], act.shape[1]
    per, per_ff = width // 32, ff // 32
    sem, low = pltpu.SemaphoreType.DMA, jnp.bfloat16
    wide, slim = (2 * per, ff), (per_ff, width)
    sums = [jax.ShapeDtypeStruct((16, 2 * per, ff // 2), low)] * 2 + [jax.ShapeDtypeStruct((16,) + slim, low)]
    return pl.pallas_call(
        functools.partial(weights_kernel, shards),
        out_shape=(jax.ShapeDtypeStruct((2, 2) + da.shape[1:], da.dtype),) + tuple(sums),
        in_specs=[VMEM_SPEC] * 6,
        out_specs=(VMEM_SPEC,) * 4,
        scratch_shapes=[
            sem((4,)), sem((4,)), sem((2,)), sem((2,)),
            pltpu.VMEM((width, ff), jnp.float32), pltpu.VMEM((width, ff), jnp.float32),
            pltpu.VMEM((ff, width), jnp.float32),
            pltpu.VMEM((16,) + wide, low), pltpu.VMEM((16,) + slim, low),
            pltpu.VMEM((16,) + wide, low), pltpu.VMEM((16,) + slim, low),
        ],
        compiler_params=pltpu.CompilerParams(collective_id=5, has_side_effects=True, vmem_limit_bytes=VMEM_BYTES),
        name="spread_and_weights",
    )(da, n2, act, dg, du, ct)


def reduce_kernel(shards, axes, orders, *refs):
    count = len(orders)
    q_ref, kv_ref = refs[:2]
    pairs = refs[2 : 2 + 2 * count]
    qo_ref, kvo_ref = refs[2 + 2 * count : 4 + 2 * count]
    sums = refs[4 + 2 * count : 4 + 3 * count]
    q_send, q_recv, send_sem, recv_sem, z_send, z_recv, w_send, w_recv = refs[4 + 3 * count : 12 + 3 * count]
    bufs = refs[12 + 3 * count :]
    place = Place(shards)
    rest_bits = bits_of(place.rest_size)
    greet(line_and_row(place) + [place.other_rest(mask) for mask in rest_bits])
    return_heads(place, q_ref, qo_ref, q_send, q_recv)
    ndim = 1 + len(rest_bits)
    at = {"dp": place.dp, "blk": place.blk}
    streams, used = [], ndim
    for s, (kept, order) in enumerate(orders):
        src, more = bufs[used], bufs[used + 1 : used + 1 + len(order)]
        used += 1 + len(order)
        streams.append(Stream(axes, at, kept, order, src, more, sums[s], w_send.at[s], w_recv.at[s]))
    own = [place.row] + [bit(place.rest, m) for m in rest_bits]
    targets = [place.other_row()] + [place.other_rest(m) for m in rest_bits]
    state = {}

    def plan(group_step):
        far = list(range(ndim - 1))
        turn = group_step % len(far)
        return [ndim - 1] + far[turn:] + far[:turn]

    def copy_of(step, stage):
        order = plan(step)
        group = (place.group + step) % GROUPS
        done = order[:stage]
        p_now = order[stage]
        buf = bufs[stage].at[step]
        if stage == 0:
            index = (p_index(group, done, p_now))
            src = kv_ref.at[index]
        else:
            kept = [p for p in range(ndim) if p not in done]
            src = bufs[stage - 1].at[(step,) + tuple(1 - own[p] if p == p_now else slice(None) for p in kept)]
        return remote(src, buf, send_sem.at[stage, step], recv_sem.at[stage, step], targets[p_now])

    def p_index(group, done, p_now):
        index = [slice(None)] * ndim
        index[p_now] = 1 - own[p_now]
        return (index[0], group) + tuple(index[1:])

    def absorb(step, stage):
        order = plan(step)
        done, p_now = order[:stage], order[stage]
        buf = bufs[stage].at[step]
        group = (place.group + step) % GROUPS
        if stage == 0:
            index = [None] * ndim
            index[p_now] = own[p_now]
            add_blocks(buf, kv_ref, (index[0], group) + tuple(index[1:]), buf.shape)
        else:
            kept = [p for p in range(ndim) if p not in done]
            index = tuple(own[p] if p == p_now else None for p in kept)
            add_blocks(buf, bufs[stage - 1].at[step], index, buf.shape)

    steps = (2, 1, 3, 0)
    for step in steps:
        copy_of(step, 0).start()
    for s, stream in enumerate(streams):
        add_two(stream.src, pairs[2 * s], pairs[2 * s + 1])
        stream.copy(0).start()
    for stage in range(ndim):
        for step in steps:
            copy_of(step, stage).wait()
            absorb(step, stage)
            if stage < ndim - 1:
                copy_of(step, stage + 1).start()
            elif step:
                remote(bufs[stage].at[step], kvo_ref.at[place.group], z_send.at[step], z_recv.at[(GROUPS - step) % GROUPS], place.other_group(step)).start()
            else:
                kvo_ref[place.group] = bufs[stage][step]
        for stream in streams:
            if stage < len(stream.order):
                stream.copy(stage).wait()
                stream.absorb(stage)
                if stage < len(stream.order) - 1:
                    stream.copy(stage + 1).start()
    for step in (1, 3, 2):
        there = kvo_ref.at[(place.group + step) % GROUPS]
        remote(bufs[ndim - 1].at[step], there, z_send.at[step], z_recv.at[step], place.other_group(step)).wait()
    return_heads_wait(place, q_ref, qo_ref, q_send, q_recv)


def add_two(dst_ref, one_ref, two_ref):
    lead = dst_ref.shape[:-2]

    def one(step, _):
        place, left = [], step
        for size in reversed(lead):
            place.append(left % size)
            left = left // size
        place = tuple(reversed(place))
        dst_ref[place] = (one_ref[place].astype(jnp.float32) + two_ref[place].astype(jnp.float32)).astype(dst_ref.dtype)
        return 0

    lax.fori_loop(0, math.prod(lead), one, 0)


def reduce_all(shape, q_packed, kv_sums, orders, pairs):
    shards = shape["blk"]
    tokens_all, width = kv_sums.shape[1:]
    tokens = tokens_all // shards
    rest_bits = bits_of(shards // GROUPS)
    ndim = 1 + len(rest_bits)
    sem = pltpu.SemaphoreType.DMA
    scratch = [pltpu.VMEM((GROUPS,) + (2,) * (ndim - 1 - s) + (tokens, width), kv_sums.dtype) for s in range(ndim)]
    flat, sums = [], []
    for (kept, order), pair in zip(orders, pairs):
        rows, cols = pair[0].shape[-2:]
        flat += [part.reshape((2,) * len(kept) + (rows, cols)) for part in pair]
        sums.append(jax.ShapeDtypeStruct((rows, cols), jnp.float32))
        scratch.append(pltpu.VMEM((2,) * len(kept) + (rows, cols), jnp.bfloat16))
        scratch += stream_scratch(len(kept), order, rows, cols)
    stages = max([len(order) for _, order in orders], default=1)
    return pl.pallas_call(
        functools.partial(reduce_kernel, shards, bit_axes(shape), orders),
        out_shape=(
            jax.ShapeDtypeStruct((GROUPS,) + q_packed.shape[2:], q_packed.dtype),
            jax.ShapeDtypeStruct((GROUPS, tokens, width), kv_sums.dtype),
        ) + tuple(sums),
        in_specs=[VMEM_SPEC] * (2 + len(flat)),
        out_specs=(VMEM_SPEC,) * (2 + len(sums)),
        scratch_shapes=[sem((4,)), sem((4,)), sem((ndim, GROUPS)), sem((ndim, GROUPS)), sem((GROUPS,)), sem((GROUPS,)),
                        sem((max(len(orders), 1), stages)), sem((max(len(orders), 1), stages))] + scratch,
        compiler_params=pltpu.CompilerParams(collective_id=2, has_side_effects=True, vmem_limit_bytes=VMEM_BYTES),
        name="reduce_keys",
    )(q_packed, kv_sums.reshape((2, GROUPS) + (2,) * len(rest_bits) + (tokens, width)), *flat)


TQ = 256
TK = 512
NEAR_ROWS = 448
NEG = -1e30
FIRST_MAX = -1e29
NT = (((1,), (1,)), ((), ()))
NN = (((1,), (0,)), ((), ()))
BORDERS = (12, 16, 23, 32, 46, 64, 91)


def mxu(left, right, dims=NN):
    return lax.dot_general(left, right, dims, preferred_element_type=jnp.float32)


def turned(tile):
    return jnp.concatenate([tile[:, 64:], tile[:, :64]], axis=1)


def spread_lanes(packed, high):
    lane = lax.broadcasted_iota(jnp.int32, (1, 128), 1)
    keep = lane >= 64 if high else lane < 64
    zero = jnp.zeros((), packed.dtype)
    pair, last = packed[0:TQ], packed[TQ:]
    pick = lambda tile: jnp.where(keep, tile, zero)
    if high:
        return [pick(turned(pair)), pick(pair), jnp.concatenate([pick(turned(last)), pick(last)], axis=0)]
    return [pick(pair), pick(turned(pair)), jnp.concatenate([pick(last), pick(turned(last))], axis=0)]


def join_heads(parts):
    half = TQ // 2
    top = jnp.concatenate([parts[0], parts[1]], axis=1)
    low = jnp.concatenate([parts[2][:half], parts[2][half:]], axis=1)
    return jnp.concatenate([top, low], axis=0)


def valid_mask(se_ref, r, i, k0):
    kpos = k0 + lax.broadcasted_iota(jnp.int32, (TK, TQ), 0)
    return jnp.logical_and(kpos >= se_ref[r, i, 0:1, :], kpos < se_ref[r, i, 1:2, :])


def near_buckets(first, rows, parity):
    relative = (
        first - TK + TQ * parity
        + lax.broadcasted_iota(jnp.int32, (rows, TQ), 0)
        - lax.broadcasted_iota(jnp.int32, (rows, TQ), 1)
    )
    return buckets_of(relative)


def make_bias(table, parity, bias_ref):
    heads = bias_ref.shape[0]
    for h in range(heads):
        bias_ref[h, 0] = jnp.full((TK, TQ), table[h, 15], jnp.float32).astype(jnp.bfloat16)
        bias_ref[h, 3] = jnp.full((TK, TQ), table[h, 31], jnp.float32).astype(jnp.bfloat16)
    for tile in range(2):
        def rows(step, _):
            start = pl.multiple_of(step * 32, 32)
            which = near_buckets(tile * TK + start, 32, parity)
            for h in range(heads):
                value = jnp.zeros((32, TQ), jnp.float32)
                for b in range(BUCKETS):
                    value = jnp.where(which == b, table[h, b], value)
                bias_ref[h, tile + 1, pl.ds(start, 32)] = value.astype(jnp.bfloat16)
            return 0
        lax.fori_loop(0, TK // 32, rows, 0)


def tile_kind(bounds, r, i, t):
    slot = jnp.clip(t - bounds[r, i, 2] + 1, 0, 3)
    away = jnp.logical_or(slot == 0, slot == 3)
    inside = jnp.logical_and(t >= bounds[r, i, 3], t < bounds[r, i, 4])
    return slot, jnp.logical_and(away, inside)


def fwd_kernel(bounds, table, q_ref, kv_ref, se_ref, o_ref, keep_ref, lse_ref, bias_ref, vt, acc, mx, qp):
    heads = lse_ref.shape[2]
    make_bias(table, bounds[0, 0, 5], bias_ref)
    for r in range(2):
        for i in range(2):
            for h, tile in enumerate(spread_lanes(q_ref[r, i], False)):
                qp[r, i, h] = tile

    def row_body(r, _):
        lo_all = jnp.minimum(bounds[r, 0, 0], bounds[r, 1, 0])
        hi_all = jnp.maximum(bounds[r, 0, 1], bounds[r, 1, 1])

        def turn(t, _):
            k0 = pl.multiple_of(t * TK, TK)
            for h in range(heads):
                tile = kv_ref[r, pl.ds(k0, TK), h * 128 : h * 128 + 128]
                vt[h, 0:64, pl.ds(k0, TK)] = tile.T[64:128, :]
                vt[h, 64:80, pl.ds(k0, TK)] = jnp.ones((16, TK), jnp.bfloat16)
            return 0

        lax.fori_loop(lo_all, hi_all, turn, 0)

        def q_body(i, _):
            acc[...] = jnp.zeros_like(acc)
            mx[...] = jnp.full_like(mx, FIRST_MAX)

            def tile_body(t, _):
                k0 = pl.multiple_of(t * TK, TK)
                slot, plain = tile_kind(bounds, r, i, t)

                def scores(h):
                    return mxu(kv_ref[r, pl.ds(k0, TK), h * 128 : h * 128 + 128], qp[r, i, h], NT)

                def finish(h, s, b):
                    m_old = mx[h]
                    m_new = jnp.maximum(m_old, jnp.max(s, axis=0, keepdims=True) + b)
                    p = jnp.exp(s - (m_new - b)).astype(jnp.bfloat16)
                    mx[h] = m_new
                    acc[h] = acc[h] * jnp.exp(m_old - m_new) + mxu(vt[h, :, pl.ds(k0, TK)], p)

                @pl.when(plain)
                def _():
                    found = [scores(h) for h in range(heads)]
                    for h in range(heads):
                        finish(h, found[h], jnp.where(slot == 0, table[h, 15], table[h, 31]))

                @pl.when(jnp.logical_not(plain))
                def _():
                    ok = valid_mask(se_ref, r, i, k0)
                    for h in range(heads):
                        s = scores(h) + bias_ref[h, slot].astype(jnp.float32)
                        finish(h, jnp.where(ok, s, NEG), 0.0)

                return 0

            lax.fori_loop(bounds[r, i, 0], bounds[r, i, 1], tile_body, 0)
            parts = []
            for h in range(heads):
                total = acc[h, 64:65, :]
                parts.append((acc[h, 0:64, :] / total).T)
                lse_ref[r, i, h] = mx[h] + jnp.log(total)
            joined = join_heads(parts)
            o_ref[r, i] = joined.astype(jnp.bfloat16)
            keep_ref[r, i] = joined
            return 0

        lax.fori_loop(0, 2, q_body, 0)
        return 0

    lax.fori_loop(0, 2, row_body, 0)


def attention(bounds, table, q, kv, se):
    heads, n = kv.shape[2] // 128, kv.shape[1]
    packed = q.shape
    return pl.pallas_call(
        fwd_kernel,
        out_shape=(
            jax.ShapeDtypeStruct(packed, jnp.bfloat16),
            jax.ShapeDtypeStruct(packed, jnp.float32),
            jax.ShapeDtypeStruct((2, 2, heads, 1, TQ), jnp.float32),
            jax.ShapeDtypeStruct((heads, 4, TK, TQ), jnp.bfloat16),
        ),
        in_specs=[SMEM_SPEC] * 2 + [VMEM_SPEC] * 3,
        out_specs=(VMEM_SPEC,) * 4,
        scratch_shapes=[
            pltpu.VMEM((heads, 80, n), jnp.bfloat16),
            pltpu.VMEM((heads, 80, TQ), jnp.float32),
            pltpu.VMEM((heads, 1, TQ), jnp.float32),
            pltpu.VMEM((2, 2, heads, TQ, 128), jnp.bfloat16),
        ],
        compiler_params=pltpu.CompilerParams(vmem_limit_bytes=VMEM_BYTES),
        name="attention",
    )(bounds, table, q, kv, se)


def prepare(q, do, keep, q_out, do_out, delta):
    for h, tile in enumerate(spread_lanes(q, False)):
        q_out[h] = tile
    for h, tile in enumerate(spread_lanes(do, True)):
        do_out[h] = tile
    prod = (do.astype(jnp.float32) * keep).T
    top, low = prod[:, 0:TQ], prod[:, TQ:]
    delta[0] = jnp.sum(top[0:64], axis=0, keepdims=True)
    delta[1] = jnp.sum(top[64:128], axis=0, keepdims=True)
    delta[2] = jnp.concatenate(
        [jnp.sum(low[0:64], axis=0, keepdims=True), jnp.sum(low[64:128], axis=0, keepdims=True)], axis=1
    )


def near_start(parity):
    return 416 - TQ * parity


def far_sums(grid, h, first, end):
    def one(step, total):
        rows = grid[h, pl.ds(pl.multiple_of(step * 32, 32), 32)]
        return total + jnp.sum(rows.reshape(4, 8, TQ), axis=0)
    total = lax.fori_loop(first // 32, end // 32, one, jnp.zeros((8, TQ), jnp.float32))
    return jnp.sum(total, axis=0, keepdims=True)


def bucket_sums(parity, near, side, tab_ref, tab8):
    heads = near.shape[0]
    tab8[...] = jnp.zeros_like(tab8)

    def inner(step, _):
        start = pl.multiple_of(step * 32, 32)
        which = near_buckets(near_start(parity) + start, 32, parity)
        for b in range(BUCKETS):
            here = which == b
            for h in range(heads):
                rows = jnp.where(here, near[h, pl.ds(start, 32)], 0.0)
                tab8[h, b] += jnp.sum(rows.reshape(4, 8, TQ), axis=0)
        return 0

    lax.fori_loop(0, NEAR_ROWS // 32, inner, 0)
    for h in range(heads):
        tab_ref[h] = jnp.sum(tab8[h], axis=1)
        tab_ref[h, 15:16] += side[h, 0:1]
        tab_ref[h, 31:32] += side[h, 1:2]


def bwd_kernel(alone, bounds, table, q_ref, do_ref, keep_ref, kv_ref, bias_ref, se_ref, lse_ref,
               dq_ref, dkv_ref, near_ref, side, *rest):
    tab_ref, tab8, rest = (None, None, rest) if alone else (rest[0], rest[-1], rest[1:-1])
    kt, dqt, dkv, grid, qp, dp_ref, delta = rest
    heads = lse_ref.shape[2]
    n = kv_ref.shape[1]
    grid[...] = jnp.zeros_like(grid)
    side[...] = jnp.zeros_like(side)
    base = 1 - bounds[0, 0, 6] if alone else 0
    for at in range(1 if alone else 2):
        for i in range(2):
            prepare(q_ref[base + at, i], do_ref[base + at, i], keep_ref[base + at, i], qp.at[at, i], dp_ref.at[at, i], delta.at[at, i])

    def row_body(at, _):
        r = base + at
        lo_all = jnp.minimum(bounds[r, 0, 0], bounds[r, 1, 0])
        hi_all = jnp.maximum(bounds[r, 0, 1], bounds[r, 1, 1])

        def clear(t, _):
            k0 = pl.multiple_of(t * TK, TK)
            for h in range(heads):
                dkv[h, pl.ds(k0, TK), :] = jnp.zeros((TK, 128), jnp.float32)
            return 0

        lax.fori_loop(0, n // TK, clear, 0)

        def turn(t, _):
            k0 = pl.multiple_of(t * TK, TK)
            for h in range(heads):
                tile = kv_ref[r, pl.ds(k0, TK), h * 128 : h * 128 + 128]
                kt[h, 0:64, pl.ds(k0, TK)] = tile.T[0:64, :]
                kt[h, 64:80, pl.ds(k0, TK)] = jnp.ones((16, TK), jnp.bfloat16)
            return 0

        lax.fori_loop(lo_all, hi_all, turn, 0)

        def q_body(i, _):
            dqt[...] = jnp.zeros_like(dqt)

            def tile_body(t, _):
                k0 = pl.multiple_of(t * TK, TK)
                slot, plain = tile_kind(bounds, r, i, t)

                def finish(h, p, ds, where):
                    ds_low = ds.astype(jnp.bfloat16)
                    two = jnp.concatenate([ds_low, p.astype(jnp.bfloat16)], axis=1)
                    both = jnp.concatenate([qp[at, i, h], dp_ref[at, i, h]], axis=0)
                    dkv[h, pl.ds(k0, TK), :] += mxu(two, both)
                    dqt[h, where] += mxu(kt[h, :, pl.ds(k0, TK)], ds_low)

                def products(h):
                    tile = kv_ref[r, pl.ds(k0, TK), h * 128 : h * 128 + 128]
                    return mxu(tile, qp[at, i, h], NT), mxu(tile, dp_ref[at, i, h], NT)

                @pl.when(plain)
                def _():
                    for h in range(heads):
                        s, d_probs = products(h)
                        p = jnp.exp(s - (lse_ref[r, i, h] - jnp.where(slot == 0, table[h, 15], table[h, 31])))
                        finish(h, p, p * (d_probs - delta[at, i, h]), jnp.where(slot == 0, 0, 2))

                @pl.when(jnp.logical_not(plain))
                def _():
                    ok = valid_mask(se_ref, r, i, k0)
                    for h in range(heads):
                        s, d_probs = products(h)
                        s = s + bias_ref[h, slot].astype(jnp.float32)
                        p = jnp.where(ok, jnp.exp(jnp.where(ok, s, NEG) - lse_ref[r, i, h]), 0.0)
                        ds = p * (d_probs - delta[at, i, h])
                        grid[h, pl.ds(pl.multiple_of(slot * TK, TK), TK)] += ds
                        finish(h, p, ds, 1)

                return 0

            lax.fori_loop(bounds[r, i, 0], bounds[r, i, 1], tile_body, 0)
            parts = []
            for h in range(heads):
                parts.append((dqt[h, 0, 0:64] + dqt[h, 1, 0:64] + dqt[h, 2, 0:64]).T * 0.125)
                side[h, 0:1] += dqt[h, 0, 64:65]
                side[h, 1:2] += dqt[h, 2, 64:65]
            dq_ref[at, i] = join_heads(parts).astype(jnp.bfloat16)
            return 0

        lax.fori_loop(0, 2, q_body, 0)

        def put(t, _):
            k0 = pl.multiple_of(t * TK, TK)
            for h in range(heads):
                dkv_ref[at, pl.ds(k0, TK), h * 128 : h * 128 + 128] = dkv[h, pl.ds(k0, TK), :].astype(jnp.bfloat16)
            return 0

        lax.fori_loop(0, n // TK, put, 0)
        return 0

    lax.fori_loop(0, 1 if alone else 2, row_body, 0)

    parity = bounds[0, 0, 5]
    first = TK + near_start(parity)
    for h in range(heads):
        near_ref[h] = grid[h, pl.ds(pl.multiple_of(first, 32), NEAR_ROWS)]
        side[h, 0:1] += far_sums(grid, h, 0, first)
        side[h, 1:2] += far_sums(grid, h, first + NEAR_ROWS, 4 * TK)
    if not alone:
        bucket_sums(parity, near_ref, side, tab_ref, tab8)


def attention_back(alone, bounds, table, q, do, keep, kv, bias, se, lse):
    heads, n = kv.shape[2] // 128, kv.shape[1]
    count = 1 if alone else 2
    table_out = [] if alone else [jax.ShapeDtypeStruct((heads, BUCKETS, TQ), jnp.float32)]
    return pl.pallas_call(
        functools.partial(bwd_kernel, alone),
        out_shape=(
            jax.ShapeDtypeStruct((count,) + q.shape[1:], jnp.bfloat16),
            jax.ShapeDtypeStruct((count,) + kv.shape[1:], jnp.bfloat16),
            jax.ShapeDtypeStruct((heads, NEAR_ROWS, TQ), jnp.float32),
            jax.ShapeDtypeStruct((heads, 2, TQ), jnp.float32),
        ) + tuple(table_out),
        in_specs=[SMEM_SPEC] * 2 + [VMEM_SPEC] * 7,
        out_specs=(VMEM_SPEC,) * (4 + len(table_out)),
        scratch_shapes=[
            pltpu.VMEM((heads, 80, n), jnp.bfloat16),
            pltpu.VMEM((heads, 3, 80, TQ), jnp.float32),
            pltpu.VMEM((heads, n, 128), jnp.float32),
            pltpu.VMEM((heads, 4 * TK, TQ), jnp.float32),
            pltpu.VMEM((count, 2, heads, TQ, 128), jnp.bfloat16),
            pltpu.VMEM((count, 2, heads, TQ, 128), jnp.bfloat16),
            pltpu.VMEM((count, 2, heads, 1, TQ), jnp.float32),
        ] + [pltpu.VMEM((heads, BUCKETS, 8, TQ), jnp.float32) for _ in table_out],
        compiler_params=pltpu.CompilerParams(vmem_limit_bytes=VMEM_BYTES),
        name="attention_back",
    )(bounds, table, q, do, keep, kv, bias, se, lse)


def dense_kernel(shards, axes, orders, bounds, table, q_ref, do_ref, keep_ref, kv_ref, bias_ref, lse_ref, dqs_ref, dkvs_ref, nears_ref, sides_ref, *refs):
    count = len(orders)
    weights, refs = refs[:count], refs[count:]
    dq_out, kvo_ref, tab_ref, refs = refs[0], refs[1], refs[2], refs[3:]
    more, refs = refs[:count], refs[count:]
    (kt, dqt, acc, grid, side, tab8, qp, dp_ref, delta, held, core_in, s_in, s_sum, x_out, x_in, y_out, y_in, kept, z_out, dq_rows,
     core_send, core_recv, x_send, x_recv, y_send, y_recv, z_send, z_recv, s_send, s_recv, q_send, q_recv, w_send, w_recv) = refs
    place = Place(shards)
    heads = lse_ref.shape[2]
    tokens = TQ
    across, core_to, row_to = place.other_rest(2), place.other_rest(1), place.other_row()
    y, core = bit(place.rest, 2), place.rest % 2
    met = hail(line_and_row(place) + [across, core_to])
    at = {"dp": place.dp, "blk": place.blk}
    streams = [
        Stream(axes, at, kept_bits, order, weights[s], [more[s]], None, w_send.at[s], w_recv.at[s])
        for s, (kept_bits, order) in enumerate(orders)
    ]
    s_core = remote(dkvs_ref.at[:, :, 1 - core], s_in, s_send, s_recv, core_to)

    dense = bounds[0, 0, 6]
    mine_dense = dense == place.row
    parity = core
    for i in range(2):
        prepare(q_ref[dense, i], do_ref[dense, i], keep_ref[dense, i], qp.at[i], dp_ref.at[i], delta.at[i])
    dqt[...] = jnp.zeros_like(dqt)
    grid[...] = jnp.zeros_like(grid)
    await_all(met)
    s_core.start()
    for stream in streams:
        stream.copy(0).start()

    wide = lambda value: value.astype(jnp.float32)
    slim = lambda value: value.astype(jnp.bfloat16)

    def group_of(n):
        return (place.group + 1 + n) % GROUPS

    def core_copy(n, j):
        return remote(held.at[n, j, 1 - core], core_in.at[n, j], core_send.at[n, j], core_recv.at[n, j], core_to)

    def x_copy(n, j):
        return remote(x_out.at[n, j], x_in.at[n, j], x_send.at[n, j], x_recv.at[n, j], row_to)

    def y_copy(n, j):
        return remote(y_out.at[n, j], y_in.at[n, j], y_send.at[n, j], y_recv.at[n, j], across)

    def z_copy(n):
        return remote(z_out.at[n], kvo_ref.at[place.group], z_send.at[n], z_recv.at[n], place.at(place.row, group_of(n), place.rest))

    def over_cores(n, j):
        core_copy(n, j).wait()
        return wide(held[n, j, core]) + wide(core_in[n, j])

    def send_x(n, j, one, two):
        x_out[n, j] = slim(jnp.where(mine_dense, two, one))
        x_copy(n, j).start()
        return jnp.where(mine_dense, one, two)

    def deliver(n, total):
        if isinstance(n, int):
            if n == GROUPS - 1:
                kvo_ref[place.group] = slim(total)
            else:
                z_out[n] = slim(total)
                z_copy(n).start()
            return

        z_out[n] = slim(total)

        @pl.when(n < GROUPS - 1)
        def _():
            z_copy(n).start()

        @pl.when(n == GROUPS - 1)
        def _():
            kvo_ref[place.group] = z_out[n]

    def y_first_1(n):
        y_out[n, 0] = slim(over_cores(n, 0))
        y_out[n, 1] = s_sum[n, 0]
        y_copy(n, 0).start()
        y_copy(n, 1).start()

    def y_first_3(n):
        y_copy(n, 0).wait()
        y_copy(n, 1).wait()
        kept[n, 0] = send_x(n, 0, over_cores(n, 1) + wide(y_in[n, 0]), wide(s_sum[n, 1]) + wide(y_in[n, 1]))

    def y_first_5(n):
        x_copy(n, 0).wait()
        deliver(n, kept[n, 0] + wide(x_in[n, 0]))

    def x_first_1(n):
        kept[n, 0] = send_x(n, 0, over_cores(n, 0), wide(s_sum[n, 0]))

    def x_first_2(n):
        kept[n, 1] = send_x(n, 1, over_cores(n, 1), wide(s_sum[n, 1]))

    def x_first_3(n):
        x_copy(n, 0).wait()
        y_out[n, 0] = slim(kept[n, 0] + wide(x_in[n, 0]))
        y_copy(n, 0).start()

    def x_first_5(n):
        x_copy(n, 1).wait()
        y_copy(n, 0).wait()
        deliver(n, kept[n, 1] + wide(x_in[n, 1]) + wide(y_in[n, 0]))

    actions = ((1, 0, y_first_1), (1, 1, x_first_1), (2, 1, x_first_2), (6, 0, y_first_3), (5, 1, x_first_3))

    def tile_body(m, _):
        n, j = m // 2, m % 2
        place_y = jnp.where(j == 0, 1 - y, y)
        t = group_of(n) * 2 + place_y
        k0 = pl.multiple_of(t * TK, TK)
        acc[...] = jnp.zeros_like(acc)
        for h in range(heads):
            kt[h, 0:64] = kv_ref[dense, pl.ds(k0, TK), h * 128 : h * 128 + 128].T[0:64]
            kt[h, 64:80] = jnp.ones((16, TK), jnp.bfloat16)

        def part(i, _):
            first = ((2 * place.row + i) * place.rest_size + place.rest) * tokens
            slot = jnp.clip(t - (first // TK - 1 + parity) + 1, 0, 3)
            away = jnp.logical_or(slot == 0, slot == 3)

            def finish(h, p, ds, where):
                ds_low = ds.astype(jnp.bfloat16)
                two = jnp.concatenate([ds_low, p.astype(jnp.bfloat16)], axis=1)
                both = jnp.concatenate([qp[i, h], dp_ref[i, h]], axis=0)
                acc[:, h * 128 : h * 128 + 128] += mxu(two, both)
                dqt[i, h, where] += mxu(kt[h], ds_low)

            def products(h):
                tile = kv_ref[dense, pl.ds(k0, TK), h * 128 : h * 128 + 128]
                return mxu(tile, qp[i, h], NT), mxu(tile, dp_ref[i, h], NT)

            @pl.when(away)
            def _():
                for h in range(heads):
                    s, d_probs = products(h)
                    p = jnp.exp(s - (lse_ref[dense, i, h] - jnp.where(slot == 0, table[h, 15], table[h, 31])))
                    finish(h, p, p * (d_probs - delta[i, h]), jnp.where(slot == 0, 0, 2))

            @pl.when(jnp.logical_not(away))
            def _():
                for h in range(heads):
                    s, d_probs = products(h)
                    p = jnp.exp(s + bias_ref[h, slot].astype(jnp.float32) - lse_ref[dense, i, h])
                    ds = p * (d_probs - delta[i, h])
                    grid[h, pl.ds(pl.multiple_of((slot - 1) * TK, TK), TK)] += ds
                    finish(h, p, ds, 1)

            return 0

        lax.fori_loop(0, 2, part, 0)
        for half in range(2):
            held[n, j, half] = acc[half * tokens : half * tokens + tokens].astype(jnp.bfloat16)
        core_copy(n, j).start()

        @pl.when(m == 0)
        def _():
            s_core.wait()

            def one(step, _):
                n_s, far = step // 2, step % 2
                row = jnp.where(far == 0, 1 - y, y)
                group = group_of(n_s)
                s_sum[n_s, far] = slim(wide(dkvs_ref[group, row, core]) + wide(s_in[group, row]))
                return 0

            lax.fori_loop(0, 2 * GROUPS, one, 0)

        for delay, odd, action in actions:
            back = m - delay + 2 * GROUPS
            n_then = back // 2 - GROUPS

            @pl.when(jnp.logical_and(back % 2 == 0, jnp.logical_and(n_then >= 0, n_then % 2 == odd)))
            def _():
                action(n_then)

        return 0

    lax.fori_loop(0, 2 * GROUPS, tile_body, 0)
    x_first_2(GROUPS - 1)

    for i in range(2):
        parts = []
        for h in range(heads):
            parts.append((dqt[i, h, 0, 0:64] + dqt[i, h, 1, 0:64] + dqt[i, h, 2, 0:64]).T * 0.125)
        mine = join_heads(parts)
        other = dqs_ref[0, i].astype(jnp.float32)
        for r in range(2):
            dq_rows[r, i] = jnp.where(dense == r, mine, other).astype(jnp.bfloat16)
    return_heads(place, dq_rows, dq_out, q_send, q_recv)
    y_first_5(0)
    x_first_3(3)
    y_first_3(2)
    first = near_start(parity)
    for h in range(heads):
        side[h, 0:1] = dqt[0, h, 0, 64:65] + dqt[1, h, 0, 64:65] + sides_ref[h, 0:1] + far_sums(grid, h, 0, first)
        side[h, 1:2] = dqt[0, h, 2, 64:65] + dqt[1, h, 2, 64:65] + sides_ref[h, 1:2] + far_sums(grid, h, first + NEAR_ROWS, 2 * TK)
        rows = pl.ds(pl.multiple_of(first, 32), NEAR_ROWS)
        grid[h, rows] += nears_ref[h]
    bucket_sums(parity, NearRows(grid, first), side, tab_ref, tab8)
    x_first_5(1)
    for stream in streams:
        stream.copy(0).wait()
        stream.absorb(0)
    y_first_5(2)
    x_first_5(3)
    for n in range(GROUPS - 1):
        remote(z_out.at[n], kvo_ref.at[(place.group - 1 - n + GROUPS) % GROUPS], z_send.at[n], z_recv.at[n], row_to).wait()
    return_heads_wait(place, dq_rows, dq_out, q_send, q_recv)


class NearRows:
    def __init__(self, grid, first):
        self.grid, self.first, self.shape = grid, first, grid.shape

    def __getitem__(self, index):
        h, rows = index
        return self.grid[h, pl.ds(pl.multiple_of(self.first + rows.start, 32), rows.size)]


def dense_back(shape, bounds, table, q, do, keep, kv, bias, lse, dq_other, dkv_other, near_other, side_other, orders, blocks):
    shards = shape["blk"]
    heads, n, width = kv.shape[2] // 128, kv.shape[1], kv.shape[2]
    tokens = n // shards
    sem, low = pltpu.SemaphoreType.DMA, jnp.bfloat16
    chunk = (tokens, width)
    flat, outs = [], []
    for (kept, _), block in zip(orders, blocks):
        rows, cols = block.shape[-2:]
        flat.append(block.reshape((2,) * len(kept) + (rows, cols)))
        outs.append(jax.ShapeDtypeStruct((2,) * (len(kept) - 1) + (rows, cols), low))
    count = len(orders)
    pairs = lambda: sem((GROUPS, 2))
    return pl.pallas_call(
        functools.partial(dense_kernel, shards, bit_axes(shape), orders),
        out_shape=(
            jax.ShapeDtypeStruct((GROUPS,) + q.shape[2:], low),
            jax.ShapeDtypeStruct((GROUPS,) + chunk, low),
            jax.ShapeDtypeStruct((heads, BUCKETS, TQ), jnp.float32),
        ) + tuple(outs),
        in_specs=[SMEM_SPEC] * 2 + [VMEM_SPEC] * (10 + count),
        out_specs=(VMEM_SPEC,) * (3 + count),
        scratch_shapes=[
            pltpu.VMEM((heads, 80, TK), low),
            pltpu.VMEM((2, heads, 3, 80, TQ), jnp.float32),
            pltpu.VMEM((TK, width), jnp.float32),
            pltpu.VMEM((heads, 2 * TK, TQ), jnp.float32),
            pltpu.VMEM((heads, 2, TQ), jnp.float32),
            pltpu.VMEM((heads, BUCKETS, 8, TQ), jnp.float32),
            pltpu.VMEM((2, heads, TQ, 128), low),
            pltpu.VMEM((2, heads, TQ, 128), low),
            pltpu.VMEM((2, heads, 1, TQ), jnp.float32),
            pltpu.VMEM((GROUPS, 2, 2) + chunk, low),
            pltpu.VMEM((GROUPS, 2) + chunk, low),
            pltpu.VMEM((GROUPS, 2) + chunk, low),
            pltpu.VMEM((GROUPS, 2) + chunk, low),
            pltpu.VMEM((GROUPS, 2) + chunk, low),
            pltpu.VMEM((GROUPS, 2) + chunk, low),
            pltpu.VMEM((GROUPS, 2) + chunk, low),
            pltpu.VMEM((GROUPS, 2) + chunk, low),
            pltpu.VMEM((GROUPS, 2) + chunk, jnp.float32),
            pltpu.VMEM((GROUPS,) + chunk, low),
            pltpu.VMEM((2, 2) + q.shape[2:], low),
            pairs(), pairs(), pairs(), pairs(), pairs(), pairs(), sem((GROUPS,)), sem((GROUPS,)),
            sem, sem, sem((4,)), sem((4,)), sem((count, 1)), sem((count, 1)),
        ],
        compiler_params=pltpu.CompilerParams(collective_id=2, has_side_effects=True, vmem_limit_bytes=VMEM_BYTES),
        name="dense_back",
    )(bounds, table, q, do, keep, kv, bias, lse, dq_other, dkv_other.reshape((GROUPS, 2, 2) + chunk), near_other, side_other, *flat)


TAPS = tuple(range(-3, 5))
LEAD = 8


def pool_scalars(y_rows, lab_rows, first):
    tokens = y_rows[0].shape[1]
    t = lax.broadcasted_iota(jnp.int32, (1, tokens), 1)
    at = lambda rows, k: rows[k + 3]
    found = []
    for p in range(2):
        inside = {1: 0 * t, 2: 0 * t + p, 3: (first + 2 * t + p) % 3, 4: 2 * (t % 2) + p}
        weights, scores = {}, []
        for b in range(1, MAX_BLOCK + 1):
            keep = {}
            for o in range(1 - b, b):
                same = jnp.logical_and(inside[b] + o >= 0, inside[b] + o < b)
                same = jnp.logical_and(same, at(lab_rows, p + o) == at(lab_rows, p))
                keep[o] = same.astype(jnp.float32)
            inverse = 1.0 / sum(keep.values())
            for o in keep:
                weights[b, o] = keep[o] * inverse
            scores.append(sum(weights[b, o] * at(y_rows, p + o) for o in keep))
        top = functools.reduce(jnp.maximum, scores)
        grown = [jnp.exp(s - top) for s in scores]
        total = sum(grown)
        found.append(([g / total for g in grown], weights))
    return found


def tap_weights(found):
    rows = []
    for k in TAPS:
        row = 0.0
        for p, (probs, weights) in enumerate(found):
            for b in range(1, MAX_BLOCK + 1):
                if (b, k - p) in weights:
                    row = row + probs[b - 1] * weights[b, k - p]
        rows.append(0.5 * row)
    return rows


def as_columns(rows):
    tokens = rows[0].shape[1]
    return jnp.concatenate(list(rows) + [jnp.zeros((128 - len(rows), tokens), jnp.float32)], axis=0).T


def load_bytes(x_ref, before_ref, after_ref, xs):
    length, width = x_ref.shape
    for j in range(width // 128):
        cols = slice(j * 128, j * 128 + 128)
        xs[j, 0:LEAD, :] = jnp.zeros((LEAD, 128), jnp.float32)
        xs[j, LEAD + length :, :] = jnp.zeros((LEAD, 128), jnp.float32)
        xs[j, LEAD - 2 : LEAD, :] = before_ref[0:2, cols].astype(jnp.float32)
        xs[j, LEAD + length : LEAD + length + 2, :] = after_ref[0:2, cols].astype(jnp.float32)
        xs[j, LEAD : LEAD + length, :] = x_ref[:, cols].astype(jnp.float32)


def tap(xs, k, tokens):
    return jnp.concatenate([xs[j, pl.ds(LEAD + k, tokens, stride=2), :] for j in range(xs.shape[0])], axis=1)


def strips(buf, first, rows):
    return jnp.concatenate([buf[j, first : first + rows, :] for j in range(buf.shape[0])], axis=1)


def unit_rows(values):
    return lax.rsqrt(jnp.mean(values * values, axis=-1, keepdims=True) + 1e-06)


def pool_kernel(shards, scale, x_ref, before_ref, after_ref, lab_ref, score_ref, gain_ref, wq_ref, wk_ref, wv_ref,
                hidden_ref, n1_ref, y_ref, share_ref, q_ref, kv_ref, xs):
    tokens = hidden_ref.shape[0]
    width = hidden_ref.shape[1]
    load_bytes(x_ref, before_ref, after_ref, xs)
    score = jnp.broadcast_to(score_ref[...], (8, width))
    for k in TAPS:
        y_ref[k + 3 : k + 4, :] = mxu(score, tap(xs, k, tokens).astype(jnp.bfloat16), NT)[0:1]
    rows = [y_ref[j : j + 1, :] for j in range(8)]
    labels = [lab_ref[j : j + 1, :] for j in range(8)]
    first = (lax.axis_index("blk") * x_ref.shape[0]) % 3
    found = pool_scalars(rows, labels, first)
    lane = lax.broadcasted_iota(jnp.int32, (1, 128), 1)
    share = jnp.zeros((1, 128), jnp.float32)
    for b in range(MAX_BLOCK):
        share = jnp.where(lane == b, jnp.sum(found[0][0][b] + found[1][0][b], axis=1, keepdims=True) * scale, share)
    share_ref[...] = share
    columns = as_columns(tap_weights(found))
    hidden = sum(columns[:, k + 3 : k + 4] * tap(xs, k, tokens) for k in TAPS)
    hidden_ref[...] = hidden
    n1 = (hidden * unit_rows(hidden) * gain_ref[...].astype(jnp.float32)).astype(jnp.bfloat16)
    n1_ref[...] = n1
    keys = mxu(n1, wk_ref[...]).astype(jnp.bfloat16)
    values = mxu(n1, wv_ref[...]).astype(jnp.bfloat16)
    low = lane < 64
    for j in range(width // 128):
        k_pair, v_pair = keys[:, j * 128 : j * 128 + 128], values[:, j * 128 : j * 128 + 128]
        one = jnp.where(low, k_pair, turned(v_pair))
        two = jnp.where(low, turned(k_pair), v_pair)
        for head, tile in ((2 * j, one), (2 * j + 1, two)):
            kv_ref[head // 3, :, head % 3 * 128 : head % 3 * 128 + 128] = tile
    queries = mxu(n1, wq_ref[...]).astype(jnp.bfloat16) * jnp.bfloat16(0.125)
    put_packed(queries, q_ref)


def put_packed(array, out_ref):
    tokens = array.shape[0]
    half = tokens // 2
    for g in range(GROUPS):
        part = array[:, g * 192 : g * 192 + 192]
        out_ref[g, 0:tokens, :] = part[:, 0:128]
        out_ref[g, tokens:, :] = jnp.concatenate([part[:half, 128:], part[half:, 128:]], axis=1)


def get_packed(packed_ref):
    tokens = packed_ref.shape[1] * 2 // 3
    parts = []
    for g in range(GROUPS):
        last = packed_ref[g, tokens:, :]
        parts += [packed_ref[g, 0:tokens, :], jnp.concatenate([last[:, :64], last[:, 64:]], axis=0)]
    return jnp.concatenate(parts, axis=1)


def pool_and_project(shards, scale, x, before, after, labels, score, gain, wq, wk, wv):
    length, width = x.shape
    tokens = length // 2
    return pl.pallas_call(
        functools.partial(pool_kernel, shards, scale),
        out_shape=(
            jax.ShapeDtypeStruct((tokens, width), jnp.float32),
            jax.ShapeDtypeStruct((tokens, width), jnp.bfloat16),
            jax.ShapeDtypeStruct((8, tokens), jnp.float32),
            jax.ShapeDtypeStruct((1, 128), jnp.float32),
            jax.ShapeDtypeStruct((GROUPS, tokens * 3 // 2, 128), jnp.bfloat16),
            jax.ShapeDtypeStruct((GROUPS, tokens, width * 2 // GROUPS), jnp.bfloat16),
        ),
        in_specs=[VMEM_SPEC] * 9,
        out_specs=(VMEM_SPEC,) * 6,
        scratch_shapes=[pltpu.VMEM((width // 128, length + 2 * LEAD, 128), jnp.float32)],
        compiler_params=pltpu.CompilerParams(vmem_limit_bytes=VMEM_BYTES),
        name="pool_and_project",
    )(x, before, after, labels, score, gain, wq, wk, wv)


GELU_A = math.sqrt(2.0 / math.pi)
GELU_B = 0.044715


def norm_back(d_out, rows, gain):
    unit = unit_rows(rows)
    flat = rows * unit
    scaled = d_out * gain
    d_rows = unit * (scaled - flat * jnp.mean(scaled * flat, axis=-1, keepdims=True))
    return d_rows, jnp.sum(d_out * flat, axis=0, keepdims=True)


def feed_kernel(o_ref, hidden_ref, ct_ref, gain_ref, wo_ref, wg_ref, wu_ref, wd_ref,
                out_ref, dres_ref, da_ref, dgain_ref, n2_ref, att_ref, act_ref, dg_ref, du_ref, db_ref, acc, dn2):
    ff = wg_ref.shape[1]
    step = 512
    att = get_packed(o_ref)
    att_ref[...] = att
    residual = hidden_ref[...] + mxu(att, wo_ref[...])
    gain = gain_ref[...].astype(jnp.float32)
    n2_ref[...] = (residual * unit_rows(residual) * gain).astype(jnp.bfloat16)
    acc[...] = residual
    dn2[...] = jnp.zeros_like(dn2)

    for j in range(ff // step):
        cols = slice(j * step, j * step + step)
        n2 = n2_ref[...]
        gate = mxu(n2, wg_ref[:, cols])
        up = mxu(n2, wu_ref[:, cols])
        d_act = mxu(ct_ref[...], wd_ref[cols, :], NT)
        square = gate * gate
        curve = jnp.tanh(GELU_A * gate * (1.0 + GELU_B * square))
        half = 0.5 * (1.0 + curve)
        grown = gate * half
        slope = half + 0.5 * gate * (1.0 - curve * curve) * (GELU_A * (1.0 + 3.0 * GELU_B * square))
        act = (grown * up).astype(jnp.bfloat16)
        d_gate = (d_act * up * slope).astype(jnp.bfloat16)
        d_up = (d_act * grown).astype(jnp.bfloat16)
        act_ref[:, cols] = act
        dg_ref[:, cols] = d_gate
        du_ref[:, cols] = d_up
        acc[...] += mxu(act, wd_ref[cols, :])
        dn2[...] += mxu(d_gate, wg_ref[:, cols], NT) + mxu(d_up, wu_ref[:, cols], NT)

    out_ref[...] = acc[...].astype(jnp.bfloat16)
    residual = hidden_ref[...] + mxu(att_ref[...], wo_ref[...])
    d_rows, d_gain = norm_back(dn2[...], residual, gain)
    dgain_ref[...] = d_gain
    d_res = ct_ref[...].astype(jnp.float32) + d_rows
    dres_ref[...] = d_res
    d_branch = d_res.astype(jnp.bfloat16)
    db_ref[...] = d_branch
    put_packed(mxu(d_branch, wo_ref[...], NT).astype(jnp.bfloat16), da_ref)


def feed_forward(o_home, hidden, ct, gain, wo, wg, wu, wd):
    tokens, width = hidden.shape
    ff = wg.shape[1]
    low = lambda cols: jax.ShapeDtypeStruct((tokens, cols), jnp.bfloat16)
    return pl.pallas_call(
        feed_kernel,
        out_shape=(
            low(width),
            jax.ShapeDtypeStruct((tokens, width), jnp.float32),
            jax.ShapeDtypeStruct(o_home.shape, jnp.bfloat16),
            jax.ShapeDtypeStruct((1, width), jnp.float32),
            low(width), low(width), low(ff), low(ff), low(ff), low(width),
        ),
        in_specs=[VMEM_SPEC] * 8,
        out_specs=(VMEM_SPEC,) * 10,
        scratch_shapes=[pltpu.VMEM((tokens, width), jnp.float32)] * 2,
        compiler_params=pltpu.CompilerParams(vmem_limit_bytes=VMEM_BYTES),
        name="feed_forward",
    )(o_home, hidden, ct, gain, wo, wg, wu, wd)


def unpack_pairs(dkv_ref, width):
    low = lax.broadcasted_iota(jnp.int32, (1, 128), 1) < 64
    dk_parts, dv_parts = [], []
    for j in range(width // 128):
        one, two = [dkv_ref[h // 3, :, h % 3 * 128 : h % 3 * 128 + 128] for h in (2 * j, 2 * j + 1)]
        dk_parts.append(jnp.where(low, one, turned(two)))
        dv_parts.append(jnp.where(low, turned(one), two))
    return jnp.concatenate(dk_parts, axis=1), jnp.concatenate(dv_parts, axis=1)


def pool_back(d_hidden, x_refs, lab_ref, y_ref, score_ref, gb_ref, edge_ref, spill_ref, xs, gbuf):
    x_ref = x_refs[0]
    tokens, width = d_hidden.shape
    length = x_ref.shape[0]
    lane = lax.broadcasted_iota(jnp.int32, (1, 128), 1)
    met = jnp.zeros((tokens, 128), jnp.float32)
    for k in TAPS:
        met = jnp.where(lane == k + 3, jnp.sum(d_hidden * tap(xs, k, tokens), axis=-1, keepdims=True), met)
    met = met.T
    first = (lax.axis_index("blk") * length) % 3
    found = pool_scalars([y_ref[j : j + 1, :] for j in range(8)], [lab_ref[j : j + 1, :] for j in range(8)], first)
    touch = [0.0] * 8
    for p, (probs, weights) in enumerate(found):
        d_block = []
        for b in range(1, MAX_BLOCK + 1):
            d_block.append(0.5 * sum(weights[b, o] * met[p + o + 3 : p + o + 4] for o in range(1 - b, b)))
        mean = sum(q * d for q, d in zip(probs, d_block))
        for b in range(1, MAX_BLOCK + 1):
            d_score = probs[b - 1] * (d_block[b - 1] - mean)
            for o in range(1 - b, b):
                touch[p + o + 3] = touch[p + o + 3] + d_score * weights[b, o]
    share_cols = as_columns(tap_weights(found) + touch)
    score = score_ref[...].astype(jnp.float32)
    gbuf[...] = jnp.zeros_like(gbuf)
    d_score_vec = jnp.zeros((1, width), jnp.float32)
    for k in TAPS:
        own, via = share_cols[:, k + 3 : k + 4], share_cols[:, k + 11 : k + 12]
        added = own * d_hidden + via * score
        for j in range(gbuf.shape[0]):
            gbuf[j, pl.ds(LEAD + k, tokens, stride=2), :] += added[:, j * 128 : j * 128 + 128]
        d_score_vec = d_score_vec + jnp.sum(via * tap(xs, k, tokens), axis=0, keepdims=True)
    gb_ref[...] = strips(gbuf, LEAD, length).astype(jnp.bfloat16)
    edge_ref[0] = strips(gbuf, LEAD, 16)
    edge_ref[1] = strips(gbuf, LEAD + length - 16, 16)
    spill_ref[0] = strips(gbuf, 0, LEAD)
    spill_ref[1] = strips(gbuf, LEAD + length, LEAD)
    return d_score_vec


def put_small(small_ref, vectors, tab_ref, share_ref):
    small_ref[...] = jnp.zeros_like(small_ref)
    for row, vector in zip((0, 6, 12), vectors):
        for j in range(6):
            small_ref[row + j : row + j + 1, :] = vector[:, j * 128 : j * 128 + 128]
    heads = tab_ref.shape[0]
    group = lax.axis_index("blk") // (lax.axis_size("blk") // GROUPS)
    for h in range(heads):
        total = lax.dot_general(
            jnp.ones((8, tab_ref.shape[2]), jnp.float32), tab_ref[h], NT,
            precision=lax.Precision.HIGHEST, preferred_element_type=jnp.float32,
        )
        small_ref[pl.ds(18 + group * heads + h, 1), 0:BUCKETS] = total[0:1]
    small_ref[30:31, :] = share_ref[...]


def last_kernel(shards, axes, kepts, orders, *refs):
    with_weights = len(orders) > 1
    (dq_ref, dkv_ref, hidden_ref, dres_ref, n1_ref, att_ref, db_ref, x_ref, before_ref, after_ref, lab_ref, y_ref, score_ref,
     gain_ref, wq_ref, wk_ref, wv_ref, dgain2_ref, share_ref, tab_ref), refs = refs[:20], refs[20:]
    firsts = len(orders) - 3 if with_weights else 0
    halves, refs = refs[:firsts], refs[firsts:]
    (gb_ref, edge_ref, spill_out, small_out, parts_ref), refs = refs[:5], refs[5:]
    count = len(orders) - 1
    outs, refs = refs[:count], refs[count:]
    (w_send, w_recv, s_send, s_recv, xs, gbuf, spill_ref, small_ref, small_bufs), refs = refs[:9], refs[9:]
    at = {"dp": lax.axis_index("dp"), "blk": lax.axis_index("blk")}
    tokens, width = hidden_ref.shape
    whole = Whole(axes, at, orders[-1], small_ref, small_bufs, small_out, w_send.at[count], w_recv.at[count])
    left = (at["dp"], (at["blk"] + shards - 1) % shards)
    right = (at["dp"], (at["blk"] + 1) % shards)
    met = hail([whole.stream.target(p) for p in range(len(axes))] + [left, right])
    streams, used = [], 0
    if with_weights:
        total, blocks, refs = refs[0], refs[1:3], refs[3:]
        sources = list(halves) + list(blocks)
        for s in range(count):
            more = refs[used : used + len(orders[s])]
            used += len(orders[s])
            streams.append(Stream(axes, at, kepts[s], orders[s], sources[s], more, outs[s], w_send.at[s], w_recv.at[s]))
    load_bytes(x_ref, before_ref, after_ref, xs)
    dq = get_packed(dq_ref)
    dk, dv = unpack_pairs(dkv_ref, width)
    await_all(met)
    for stream in streams[:firsts]:
        stream.copy(0).start()
    if with_weights:
        n1_t = n1_ref[...].T
        for j, part in enumerate((dq, dk, dv)):
            total[j] = mxu(n1_t, part)
        total[3] = mxu(att_ref[...].T, db_ref[...])
        devices = 1 << len(axes)
        per = width // devices
        half = width // 2

        def block(d, _):
            start = pl.multiple_of(d * per, 8)
            rows = jnp.concatenate([total[j, pl.ds(start, per), :] for j in range(4)], axis=0).astype(jnp.bfloat16)
            place, rest = [], d
            for _ in axes:
                place.append(rest % 2)
                rest = rest // 2
            place = tuple(reversed(place))
            blocks[0][place] = rows[:, :half]
            blocks[1][place] = rows[:, half:]
            return 0

        lax.fori_loop(0, devices, block, 0)
        for stream in streams[firsts:]:
            stream.copy(0).start()
    else:
        parts_ref[0], parts_ref[1], parts_ref[2] = dq, dk, dv
    d_n1 = mxu(dq, wq_ref[...], NT) + mxu(dk, wk_ref[...], NT) + mxu(dv, wv_ref[...], NT)
    d_rows, d_gain1 = norm_back(d_n1, hidden_ref[...], gain_ref[...].astype(jnp.float32))
    d_hidden = dres_ref[...] + d_rows
    for stream in streams[firsts:] + streams[:firsts]:
        advance(stream, 0)
    d_score = pool_back(d_hidden, (x_ref, before_ref, after_ref), lab_ref, y_ref, score_ref, gb_ref, edge_ref, spill_ref, xs, gbuf)
    put_small(small_ref, (d_score, d_gain1, dgain2_ref[...]), tab_ref, share_ref)
    whole.copy(0).start()
    spills = [
        remote(spill_ref.at[0], spill_out.at[1], s_send.at[0], s_recv.at[1], left),
        remote(spill_ref.at[1], spill_out.at[0], s_send.at[1], s_recv.at[0], right),
    ]
    for copy in spills:
        copy.start()
    for stage in range(1, len(axes)):
        for stream in streams[firsts:]:
            advance(stream, stage)
        advance(whole, stage - 1)
        for stream in streams[:firsts]:
            advance(stream, stage)
    advance(whole, len(axes) - 1)
    for copy in spills:
        copy.wait()
    if with_weights:
        parts_ref[...] = jnp.zeros_like(parts_ref)


def last_part(shape, halves, kepts, orders, dq, dkv, hidden, dres, n1, att, db, x, before, after, labels, y, score, gain, wq, wk, wv, dgain2, share, tab):
    tokens, width = hidden.shape
    length = x.shape[0]
    axes = bit_axes(shape)
    ndim = len(axes)
    devices = 1 << ndim
    full, sem, low = jax.ShapeDtypeStruct, pltpu.SemaphoreType.DMA, jnp.bfloat16
    count = len(orders) - 1
    strip = pltpu.VMEM((width // 128, length + 2 * LEAD, 128), jnp.float32)
    scratch = [
        sem((count + 1, ndim)), sem((count + 1, ndim)), sem((2,)), sem((2,)), strip, strip,
        pltpu.VMEM((2, LEAD, width), jnp.float32), pltpu.VMEM((32, 128), jnp.float32), pltpu.VMEM((2, ndim, 32, 128), jnp.float32),
    ]
    sums = []
    if count:
        per = width // devices
        own = (4 * per, width // 2)
        scratch += [pltpu.VMEM((4, width, width), jnp.float32)] + [pltpu.VMEM((2,) * ndim + own, low)] * 2
        for rows, cols, order in [h.shape[-2:] + (o,) for h, o in zip(halves, orders)] + [own + (o,) for o in orders[-3:-1]]:
            scratch += stream_scratch(len(order), order, rows, cols)
            sums.append(full((rows, cols), jnp.float32))
    return pl.pallas_call(
        functools.partial(last_kernel, shape["blk"], axes, kepts, orders),
        out_shape=(
            full((length, width), low),
            full((2, 16, width), jnp.float32),
            full((2, LEAD, width), jnp.float32),
            full((32, 128), jnp.float32),
            full((16, 128) if count else (3, tokens, width), low),
        ) + tuple(sums),
        in_specs=[VMEM_SPEC] * (20 + len(halves)),
        out_specs=(VMEM_SPEC,) * (5 + count),
        scratch_shapes=scratch,
        compiler_params=pltpu.CompilerParams(collective_id=3, has_side_effects=True, vmem_limit_bytes=VMEM_BYTES),
        name="last_part",
    )(dq, dkv, hidden, dres, n1, att, db, x, before, after, labels, y, score, gain, wq, wk, wv, dgain2, share, tab, *halves)


def finish_kernel(shards, heads_all, gb_ref, edge_ref, spill_ref, small_ref, *refs):
    position = lax.axis_index("blk")
    streams, outs = refs[: len(refs) - (5 if len(refs) == 5 else 12)], refs[len(refs) - (5 if len(refs) == 5 else 12) :]
    bytes_ref, score_ref, gain1_ref, gain2_ref, tab_ref = outs[:5]
    length = gb_ref.shape[0]
    bytes_ref[...] = gb_ref[...]
    zero = jnp.zeros((16 - LEAD, gb_ref.shape[1]), jnp.float32)
    left = jnp.where(position > 0, spill_ref[0], 0.0)
    right = jnp.where(position < shards - 1, spill_ref[1], 0.0)
    bytes_ref[0:16, :] = (edge_ref[0] + jnp.concatenate([left, zero], axis=0)).astype(jnp.bfloat16)
    bytes_ref[length - 16 :, :] = (edge_ref[1] + jnp.concatenate([zero, right], axis=0)).astype(jnp.bfloat16)
    for row, ref in ((0, score_ref), (6, gain1_ref), (12, gain2_ref)):
        for j in range(6):
            ref[j * 128 : j * 128 + 128] = small_ref[row + j, :]
    tab_ref[...] = small_ref[16:32, :]
    if streams:
        gq, gk, gv, go, gg, gu, gd = outs[5:]
        per = gq.shape[0]
        wide_a, wide_b, slim, *thirds = streams
        third_width = thirds[0].shape[1]
        for j, ref in enumerate((gq, gk, gv, go)):
            for c, third in enumerate(thirds):
                ref[:, c * third_width : (c + 1) * third_width] = third[j * per : j * per + per, :]
        half = wide_a.shape[1]
        for c, ref in ((0, wide_a), (1, wide_b)):
            gg[:, c * half : c * half + half] = ref[0:per, :]
            gu[:, c * half : c * half + half] = ref[per : 2 * per, :]
        gd[...] = slim[...]


def finish(shards, heads_all, per, ff, gb, edge, spill, small, streams):
    width = gb.shape[1]
    full = jax.ShapeDtypeStruct
    line = full((width,), jnp.float32)
    outs = [full(gb.shape, jnp.bfloat16), line, line, line, full((16, 128), jnp.float32)]
    if streams:
        square, broad = full((per, width), jnp.float32), full((per, ff), jnp.float32)
        outs += [square] * 4 + [broad] * 2 + [full((streams[2].shape[0], width), jnp.float32)]
    return pl.pallas_call(
        functools.partial(finish_kernel, shards, heads_all),
        out_shape=tuple(outs),
        in_specs=[VMEM_SPEC] * (4 + len(streams)),
        out_specs=(VMEM_SPEC,) * len(outs),
        compiler_params=pltpu.CompilerParams(vmem_limit_bytes=VMEM_BYTES),
        name="finish",
    )(gb, edge, spill, small, *streams)


def neighbours(rows):
    peers = lax.axis_size("blk")
    up = [(i, i + 1) for i in range(peers - 1)]
    last, leading = rows
    return lax.ppermute(last, "blk", up), lax.ppermute(leading, "blk", [(j, i) for i, j in up])


def body(
    byte_embeds,
    segments,
    score_weight,
    norm_gain1,
    w_query,
    w_key,
    w_value,
    w_out,
    rel_bias,
    norm_gain2,
    w_gate,
    w_up,
    w_down,
    cotangent,
):
    row_count, length, width = byte_embeds.shape
    tokens = length // 2
    shards = lax.axis_size("blk")
    shape = {"dp": lax.axis_size("dp"), "blk": shards}
    devices = shards * shape["dp"]
    heads = rel_bias.shape[1] // GROUPS
    position = lax.axis_index("blk")
    rest_size = shards // GROUPS
    group, rest = position // rest_size, position % rest_size
    row = lax.axis_index("dp") % 2
    x, ids_here = byte_embeds[0], segments[0]

    marks = (ids_here + 1).astype(jnp.bfloat16)
    with_marks = lambda part, two: jnp.concatenate([part, jnp.pad(two, (0, width - 2))[None]], axis=0)
    before, after = neighbours((with_marks(x[-2:], marks[-2:]), with_marks(x[:2], marks[:2])))
    line = jnp.concatenate([before[2, :2], marks, after[2, :2]])
    line = jnp.pad(line, (1, 1)).astype(jnp.int32).reshape(tokens + 3, 2).T
    labels = jnp.stack([line[j % 2, j // 2 : j // 2 + tokens] for j in range(8)])

    score_row, gain1, gain2 = score_weight[None], norm_gain1[None], norm_gain2[None]
    hidden, n1, y, share, q_packed, kv_parts = pool_and_project(
        shards, 1.0 / (row_count * length * devices), x, before, after, labels, score_row, gain1, w_query, w_key, w_value
    )

    label_block = jnp.pad(ids_here[0::2].reshape(tokens // 128, 128), ((0, 8 - tokens // 128), (0, 0)))
    q_all, kv_all, labels_all = gather_all(shards, q_packed, kv_parts, label_block)
    labels_all = labels_all.reshape(2, shards, 8, 128)[:, :, : tokens // 128].reshape(2, shards * tokens)
    ids = jnp.arange(8, dtype=jnp.int32)
    counts = jnp.sum((labels_all[:, None, :] == ids[None, :, None]).astype(jnp.int32), axis=2)
    ends = jnp.sum(jnp.where(ids[None, :] <= ids[:, None], counts[:, None, :], 0), axis=2)
    begins = ends - counts
    query_labels = jnp.stack(
        [lax.dynamic_slice_in_dim(labels_all, ((2 * row + i) * rest_size + rest) * tokens, tokens, 1) for i in range(2)],
        axis=1,
    )
    chosen = query_labels[:, :, None, :] == ids[None, None, :, None]
    span = jnp.stack(
        [jnp.sum(jnp.where(chosen, edge[:, None, :, None], 0), axis=2) for edge in (begins, ends)], axis=2
    )
    parity = rest % 2
    firsts = jnp.stack([((2 * row + i) * rest_size + rest) * tokens for i in range(2)])
    near = jnp.broadcast_to((firsts // TK - 1 + parity)[None], (2, 2))
    bounds = jnp.stack(
        [
            jnp.min(span[:, :, 0], axis=-1) // TK,
            -(-jnp.max(span[:, :, 1], axis=-1) // TK),
            near,
            -(-jnp.max(span[:, :, 0], axis=-1) // TK),
            jnp.min(span[:, :, 1], axis=-1) // TK,
            jnp.broadcast_to(parity, (2, 2)),
            jnp.broadcast_to((labels_all[0, -1] > 0).astype(jnp.int32), (2, 2)),
        ],
        axis=-1,
    ).astype(jnp.int32)
    table = lax.dynamic_slice_in_dim(rel_bias.astype(jnp.float32).T, group * heads, heads, 0)

    o_packed, o_kept, log_total, bias_tiles = attention(bounds, table, q_all, kv_all, span)
    o_home = move_heads(return_kernel, (GROUPS,), shards, 4, o_packed)
    ct = cotangent[0]
    block_out, d_res, da_packed, d_gain2, n2, att, act, d_gate, d_up, d_branch = feed_forward(
        o_home, hidden, ct, gain2, w_out, w_gate, w_up, w_down
    )

    if devices == 32:
        do_all, *blocks = spread_and_weights(shards, da_packed, n2, act, d_gate, d_up, ct)
        dq_other, dkv_other, near_other, side_other = attention_back(
            True, bounds, table, q_all, do_all, o_kept, kv_all, bias_tiles, span, log_total
        )
        orders = [((0, 1, 2, 3), (0,)), ((0, 1, 2, 3), (3,)), ((0, 1, 2, 3), (2,))]
        dq_home, dkv_home, d_table_lanes, *sums = dense_back(
            shape, bounds, table, q_all, do_all, o_kept, kv_all, bias_tiles, log_total, dq_other, dkv_other, near_other, side_other,
            orders, blocks,
        )
    else:
        do_all = move_heads(spread_kernel, (2, 2), shards, 5, da_packed)
        dq_packed, dkv_all, _, _, d_table_lanes = attention_back(
            False, bounds, table, q_all, do_all, o_kept, kv_all, bias_tiles, span, log_total
        )
        dq_home, dkv_home = reduce_all(shape, dq_packed, dkv_all, [], [])
        sums = []
    across = len(bits_of(shape["dp"]))
    ndim = across + len(bits_of(shards))
    orders, kepts = [tuple(reversed(range(ndim)))], []
    if devices == 32:
        every = (0, 1, 2, 3, 4)
        kepts = [(1, 2, 3), (0, 1, 2), (0, 1, 3), every, every]
        orders = [(3, 2, 1), (0, 2, 1), (3, 0, 1), (4, 0, 3, 2, 1), (4, 3, 0, 2, 1)] + orders
    grad_bytes, edge, spill, small, last_parts, *sums = last_part(
        shape, sums, kepts, orders, dq_home, dkv_home, hidden, d_res, n1, att, d_branch, x, before, after, labels, y,
        score_row, gain1, w_query, w_key, w_value, d_gain2, share, d_table_lanes,
    )
    per = width // devices
    grad_bytes, g_score, g_gain1, g_gain2, rows, *grads = finish(
        shards, rel_bias.shape[1], per, w_gate.shape[1], grad_bytes, edge, spill, small, sums
    )
    if devices != 32:
        product = lambda left, right: jnp.einsum("td,te->de", left, right, preferred_element_type=jnp.float32)
        grads = [product(n1, last_parts[j]) for j in range(3)]
        grads += [product(att, d_branch), product(n2, d_gate), product(n2, d_up), product(act, ct)]
        grads = [lax.psum_scatter(grad, ("dp", "blk"), scatter_dimension=0, tiled=True) for grad in grads]
    return (
        block_out[None],
        grad_bytes[None],
        g_score,
        g_gain1,
        *grads[:4],
        rows[2 : 2 + rel_bias.shape[1], :BUCKETS].T,
        g_gain2,
        *grads[4:],
        rows[14, :MAX_BLOCK],
    )


def solution(mesh):
    placed = (
        P("dp", "blk", None),
        P("dp", "blk"),
        P(),
        P(),
        P(),
        P(),
        P(),
        P(),
        P(),
        P(),
        P(),
        P(),
        P(),
        P("dp", "blk", None),
    )
    return jax.shard_map(
        body,
        mesh=mesh,
        in_specs=placed,
        out_specs=(
            P("dp", "blk", None),
            P("dp", "blk", None),
            P(),
            P(),
            P(("dp", "blk"), None),
            P(("dp", "blk"), None),
            P(("dp", "blk"), None),
            P(("dp", "blk"), None),
            P(),
            P(),
            P(("dp", "blk"), None),
            P(("dp", "blk"), None),
            P(("dp", "blk"), None),
            P(),
        ),
        check_vma=False,
    )
```

```python
import functools
import math

import jax
import jax.numpy as jnp
from jax import lax
from jax.experimental import pallas as pl
from jax.experimental.pallas import tpu as pltpu
from jax.sharding import PartitionSpec as P

BUCKETS = 32
MAX_BLOCK = 4
VMEM_BYTES = 61 * 2**20


def buckets_of(relative):
    distance = jnp.abs(relative)
    beyond = jnp.zeros_like(distance)
    for border in (12, 16, 23, 32, 46, 64, 91):
        beyond = beyond + (distance >= border).astype(jnp.int32)
    nearer = jnp.where(distance < 8, distance, 8 + beyond)
    return nearer + BUCKETS // 2 * (relative > 0).astype(jnp.int32)


MESH_ID = pl.DeviceIdType.MESH
GROUPS = 4


def bits_of(size):
    return [1 << p for p in reversed(range(size.bit_length() - 1))]


def bit(value, mask):
    return (value // mask) % 2


def flipped(value, mask):
    return value + mask * (1 - 2 * bit(value, mask))


class Place:
    def __init__(self, shards):
        self.shards = shards
        self.rest_size = shards // GROUPS
        self.dp = lax.axis_index("dp")
        self.blk = lax.axis_index("blk")
        self.row = self.dp % 2
        self.group = self.blk // self.rest_size
        self.rest = self.blk % self.rest_size

    def at(self, row, group, rest):
        return (self.dp - self.row + row, group * self.rest_size + rest)

    def chunk(self, group, rest):
        return group * self.rest_size + rest

    def other_row(self):
        return self.at(1 - self.row, self.group, self.rest)

    def other_rest(self, mask):
        return self.at(self.row, self.group, flipped(self.rest, mask))

    def other_group(self, step):
        return self.at(self.row, (self.group + step) % GROUPS, self.rest)


def hail(targets):
    barrier = pltpu.get_barrier_semaphore()
    for target in targets:
        pl.semaphore_signal(barrier, inc=1, device_id=target, device_id_type=MESH_ID)
    return len(targets)


def await_all(count):
    pl.semaphore_wait(pltpu.get_barrier_semaphore(), count)


def greet(targets):
    await_all(hail(targets))


def remote(src, dst, send_sem, recv_sem, target):
    return pltpu.make_async_remote_copy(
        src_ref=src,
        dst_ref=dst,
        send_sem=send_sem,
        recv_sem=recv_sem,
        device_id=target,
        device_id_type=MESH_ID,
    )


def line_and_row(place):
    found = []
    for step in range(GROUPS):
        for flip in range(2):
            if step or flip:
                row = 1 - place.row if flip else place.row
                found.append(place.at(row, (place.group + step) % GROUPS, place.rest))
    return found


def spread_heads(place, q_ref, out_ref, send_sem, recv_sem):
    row_to = place.group // 2
    slot = place.group % 2
    dst = out_ref.at[place.row, slot]
    mine = recv_sem.at[place.row * 2 + slot]
    at_home = row_to == place.row
    for step in range(GROUPS):
        group = (place.group + step) % GROUPS
        src = q_ref.at[group]
        copy = remote(src, dst, send_sem.at[step], mine, place.at(row_to, group, place.rest))
        if step:
            copy.start()
        else:
            pl.when(jnp.logical_not(at_home))(copy.start)
            pl.when(at_home)(pltpu.make_async_copy(src, dst, mine).start)


def spread_heads_wait(place, q_ref, out_ref, send_sem, recv_sem):
    at_home = place.group // 2 == place.row
    for row in range(2):
        for slot in range(2):
            pltpu.make_async_copy(q_ref.at[0], out_ref.at[row, slot], recv_sem.at[row * 2 + slot]).wait()
    for step in range(GROUPS):
        copy = remote(q_ref.at[0], out_ref.at[0, 0], send_sem.at[step], recv_sem.at[0], place.other_row())
        if step:
            copy.wait_send()
        else:
            pl.when(jnp.logical_not(at_home))(copy.wait_send)


def return_heads(place, o_ref, out_ref, send_sem, recv_sem):
    for row in range(2):
        for slot in range(2):
            group = place.row * 2 + slot
            src = o_ref.at[row, slot]
            dst = out_ref.at[place.group]
            mine = recv_sem.at[place.group]
            at_home = jnp.logical_and(place.row == row, place.group == group)
            copy = remote(src, dst, send_sem.at[row * 2 + slot], mine, place.at(row, group, place.rest))
            pl.when(jnp.logical_not(at_home))(copy.start)
            pl.when(at_home)(pltpu.make_async_copy(src, dst, mine).start)


def return_heads_wait(place, o_ref, out_ref, send_sem, recv_sem):
    for group in range(GROUPS):
        pltpu.make_async_copy(o_ref.at[0, 0], out_ref.at[group], recv_sem.at[group]).wait()
    for row in range(2):
        for slot in range(2):
            group = place.row * 2 + slot
            at_home = jnp.logical_and(place.row == row, place.group == group)
            copy = remote(o_ref.at[0, 0], out_ref.at[0], send_sem.at[row * 2 + slot], recv_sem.at[0], place.other_row())
            pl.when(jnp.logical_not(at_home))(copy.wait_send)


def spread_kernel(shards, q_ref, out_ref, send_sem, recv_sem):
    place = Place(shards)
    greet(line_and_row(place))
    spread_heads(place, q_ref, out_ref, send_sem, recv_sem)
    spread_heads_wait(place, q_ref, out_ref, send_sem, recv_sem)


def return_kernel(shards, o_ref, out_ref, send_sem, recv_sem):
    place = Place(shards)
    greet(line_and_row(place))
    return_heads(place, o_ref, out_ref, send_sem, recv_sem)
    return_heads_wait(place, o_ref, out_ref, send_sem, recv_sem)


SMEM_SPEC = pl.BlockSpec(memory_space=pltpu.SMEM)
VMEM_SPEC = pl.BlockSpec(memory_space=pltpu.VMEM)


def move_heads(kernel, lead, shards, ident, packed):
    rows, lanes = packed.shape[-2:]
    return pl.pallas_call(
        functools.partial(kernel, shards),
        out_shape=jax.ShapeDtypeStruct(lead + (rows, lanes), packed.dtype),
        in_specs=[pl.BlockSpec(memory_space=pltpu.VMEM)],
        out_specs=pl.BlockSpec(memory_space=pltpu.VMEM),
        scratch_shapes=[pltpu.SemaphoreType.DMA((4,)), pltpu.SemaphoreType.DMA((4,))],
        compiler_params=pltpu.CompilerParams(collective_id=ident, has_side_effects=True, vmem_limit_bytes=VMEM_BYTES),
        name="move_heads_%d" % ident,
    )(packed)


def gather_kernel(shards, q_ref, kv_ref, label_ref, qo_ref, kvo_ref, labo_ref, q_send, q_recv, z_send, far_send, core_send, kv_recv, own_sem, lab_send, lab_recv):
    place = Place(shards)
    tokens = kv_ref.shape[1]
    rest_bits = bits_of(place.rest_size)
    core, far = rest_bits[-1], ["row"] + rest_bits[:-1]
    greet(line_and_row(place) + [place.other_rest(mask) for mask in rest_bits])

    dims = [("row", 1)] + [("blk", m) for m in bits_of(shards)]
    lab_index = [place.row] + [bit(place.blk, m) for _, m in dims[1:]]
    lab_order = list(range(len(dims)))

    def lab_copy(stage):
        index = tuple(slice(None) if p in lab_order[:stage] else lab_index[p] for p in range(len(dims)))
        axis, mask = dims[lab_order[stage]]
        target = place.other_row() if axis == "row" else (place.dp, flipped(place.blk, mask))
        there = labo_ref.at[index]
        return remote(there, there, lab_send.at[stage], lab_recv.at[stage], target)

    labo_ref[tuple(lab_index)] = label_ref[...]
    lab_copy(0).start()
    lab_stage = 0

    def slot(row, group, rest):
        start = pl.multiple_of(place.chunk(group, rest) * tokens, tokens)
        return kvo_ref.at[row, pl.ds(start, tokens)]

    def held(dz, offset, core_off):
        row = 1 - place.row if offset & 1 else place.row
        rest = place.rest
        for p, mask in enumerate(far[1:]):
            if offset >> (p + 1) & 1:
                rest = flipped(rest, mask)
        if core_off:
            rest = flipped(rest, core)
        return slot(row, (place.group + dz) % GROUPS, rest)

    count = 1 << len(far)

    def sem_of(dz, offset, core_off):
        return kv_recv.at[(core_off * count + offset) * GROUPS + dz]

    own = pltpu.make_async_copy(kv_ref.at[place.group], held(0, 0, 0), own_sem)
    own.start()
    waits = []
    for step in (1, 3, 2):
        copy = remote(kv_ref.at[(place.group + step) % GROUPS], held(0, 0, 0), z_send.at[step], sem_of((GROUPS - step) % GROUPS, 0, 0), place.other_group(step))
        copy.start()
        waits.append(copy)

    used = 0
    events = sorted(((dz, off) for dz in range(GROUPS) for off in range(count)), key=lambda e: (bin(e[1]).count("1"), (0, 1, 3, 2).index(e[0])))
    core_target = place.other_rest(core)
    for step, (dz, off) in enumerate(events):
        if step == GROUPS:
            spread_heads(place, q_ref, qo_ref, q_send, q_recv)
        here = held(dz, off, 0)
        if dz == 0 and off == 0:
            src = kv_ref.at[place.group]
        else:
            remote(here, here, z_send.at[0], sem_of(dz, off, 0), core_target).wait_recv()
            src = here
        order = [(p + dz) % len(far) for p in range(len(far))]
        last = max([order.index(p) for p in range(len(far)) if off >> p & 1], default=-1)
        for p in order[last + 1 :]:
            target = place.other_row() if p == 0 else place.other_rest(far[p])
            copy = remote(src, here, far_send.at[used], sem_of(dz, off | 1 << p, 0), target)
            copy.start()
            waits.append(copy)
            used += 1
        copy = remote(src, here, core_send.at[off * GROUPS + dz], sem_of(dz, off, 1), core_target)
        copy.start()
        waits.append(copy)
        if lab_stage < len(dims):
            lab_copy(lab_stage).wait()
            lab_stage += 1
            if lab_stage < len(dims):
                lab_copy(lab_stage).start()
    for dz, off in events:
        here = held(dz, off, 1)
        remote(here, here, z_send.at[0], sem_of(dz, off, 1), core_target).wait_recv()
    own.wait()
    for copy in waits:
        copy.wait_send()
    spread_heads_wait(place, q_ref, qo_ref, q_send, q_recv)


def gather_all(shards, q_packed, kv_parts, labels):
    tokens, width = kv_parts.shape[1:]
    far = 1 + len(bits_of(shards // GROUPS)) - 1
    count = 1 << far
    nbits = 1 + len(bits_of(shards))
    sem = pltpu.SemaphoreType.DMA
    return pl.pallas_call(
        functools.partial(gather_kernel, shards),
        out_shape=(
            jax.ShapeDtypeStruct((2, 2) + q_packed.shape[1:], q_packed.dtype),
            jax.ShapeDtypeStruct((2, shards * tokens, width), kv_parts.dtype),
            jax.ShapeDtypeStruct((2,) * nbits + labels.shape, labels.dtype),
        ),
        in_specs=[pl.BlockSpec(memory_space=pltpu.VMEM)] * 3,
        out_specs=(pl.BlockSpec(memory_space=pltpu.VMEM),) * 3,
        scratch_shapes=[
            sem((4,)), sem((4,)), sem((GROUPS,)), sem((GROUPS * (count - 1),)), sem((GROUPS * count,)), sem((GROUPS * count * 2,)),
            sem, sem((nbits,)), sem((nbits,)),
        ],
        compiler_params=pltpu.CompilerParams(collective_id=1, has_side_effects=True, vmem_limit_bytes=VMEM_BYTES),
        name="gather_keys",
    )(q_packed, kv_parts, labels)


def add_blocks(dst_ref, src_ref, index, shape):
    lead = shape[:-2]
    total = math.prod(lead)

    def one(step, _):
        place, left = [], step
        for size in reversed(lead):
            place.append(left % size)
            left = left // size
        place = tuple(reversed(place))
        full, k = [], 0
        for entry in index:
            if entry is None:
                full.append(place[k])
                k += 1
            else:
                full.append(entry)
        mine = src_ref[tuple(full)].astype(jnp.float32)
        dst_ref[place] = (dst_ref[place].astype(jnp.float32) + mine).astype(dst_ref.dtype)
        return 0

    lax.fori_loop(0, total, one, 0)


class Stream:
    def __init__(self, axes, at, kept, order, src, bufs, out, send_sem, recv_sem):
        self.axes, self.at, self.kept, self.order = axes, at, kept, order
        self.src, self.bufs, self.out = src, bufs, out
        self.send_sem, self.recv_sem = send_sem, recv_sem

    def own(self, p):
        axis, mask = self.axes[p]
        return bit(self.at[axis], mask)

    def target(self, p):
        axis, mask = self.axes[p]
        moved = dict(self.at)
        moved[axis] = flipped(self.at[axis], mask)
        return (moved["dp"], moved["blk"])

    def stage(self, k):
        kept = [p for p in self.kept if p not in self.order[:k]]
        return kept, self.src if k == 0 else self.bufs[k - 1], self.order[k]

    def copy(self, k):
        kept, src, now = self.stage(k)
        index = tuple(1 - self.own(p) if p == now else slice(None) for p in kept)
        return remote(src.at[index], self.bufs[k], self.send_sem.at[k], self.recv_sem.at[k], self.target(now))

    def absorb(self, k):
        kept, src, now = self.stage(k)
        buf = self.bufs[k]
        if k == len(self.order) - 1 and self.out is not None:
            mine = src[self.own(now)].astype(jnp.float32)
            self.out[...] = buf[...].astype(jnp.float32) + mine
        else:
            add_blocks(buf, src, tuple(self.own(p) if p == now else None for p in kept), buf.shape)


class Whole:
    def __init__(self, axes, at, order, src, bufs, out, send_sem, recv_sem):
        self.stream = Stream(axes, at, order, order, src, bufs, out, send_sem, recv_sem)
        self.order, self.src, self.bufs, self.out = order, src, bufs, out

    def held(self, k):
        return self.src if k == 0 else self.bufs.at[1, k - 1]

    def copy(self, k):
        s = self.stream
        return remote(self.held(k), self.bufs.at[0, k], s.send_sem.at[k], s.recv_sem.at[k], s.target(self.order[k]))

    def absorb(self, k):
        total = self.held(k)[...] + self.bufs[0, k]
        if k == len(self.order) - 1:
            self.out[...] = total
        else:
            self.bufs[1, k] = total


def advance(stream, stage):
    if stage < len(stream.order):
        stream.copy(stage).wait()
        stream.absorb(stage)
        if stage < len(stream.order) - 1:
            stream.copy(stage + 1).start()


def bit_axes(shape):
    return [("dp", m) for m in bits_of(shape["dp"])] + [("blk", m) for m in bits_of(shape["blk"])]


def stream_scratch(lead, order, rows, cols):
    return [pltpu.VMEM((2,) * (lead - 1 - k) + (rows, cols), jnp.bfloat16) for k in range(len(order))]


def weights_kernel(shards, da_ref, n2_ref, att_ref, act_ref, dg_ref, du_ref, ct_ref, db_ref,
                   do_ref, keep_a, send_a, keep_b, send_b, keep_c, send_c,
                   q_send, q_recv, core_send, core_recv, gate, up, down, out, wide_out, slim_out, wide_in, slim_in):
    place = Place(shards)
    core_target = place.other_rest(1)
    greet(line_and_row(place) + [core_target])
    spread_heads(place, da_ref, do_ref, q_send, q_recv)
    per = gate.shape[0] // 32
    per_ff = down.shape[0] // 32
    first = keep_a.shape[2]
    half = out.shape[1] // 2
    core = place.rest % 2

    n2_t = n2_ref[...].T
    step = 512
    for j in range(gate.shape[1] // step):
        cols = slice(j * step, j * step + step)
        gate[:, cols] = mxu(n2_t, dg_ref[:, cols])
        up[:, cols] = mxu(n2_t, du_ref[:, cols])
    out[...] = mxu(att_ref[...].T, db_ref[...])

    def wide_rows(block):
        rows = pl.ds(pl.multiple_of(block * per, 8), per)
        last = jnp.concatenate([out[rows, :half], out[rows, half:]], axis=0)
        return jnp.concatenate([jnp.concatenate([gate[rows, :], up[rows, :]], axis=0), last], axis=1)

    def slim_rows(block):
        return down[pl.ds(pl.multiple_of(block * per_ff, 8), per_ff), :]

    def send_wide(m, _):
        wide_out[m] = wide_rows(2 * m + 1 - core).astype(jnp.bfloat16)
        return 0

    lax.fori_loop(0, 16, send_wide, 0)
    wide_copy = remote(wide_out, wide_in, core_send.at[0], core_recv.at[0], core_target)
    wide_copy.start()
    for j in range(down.shape[0] // step):
        rows = slice(j * step, j * step + step)
        down[rows, :] = mxu(act_ref[:, rows].T, ct_ref[...])

    def send_slim(m, _):
        slim_out[m] = slim_rows(2 * m + 1 - core).astype(jnp.bfloat16)
        return 0

    lax.fori_loop(0, 16, send_slim, 0)
    slim_copy = remote(slim_out, slim_in, core_send.at[1], core_recv.at[1], core_target)
    slim_copy.start()

    def number(j, bit_at, value):
        return j // bit_at * (2 * bit_at) + value * bit_at + j % bit_at

    wide_copy.wait()
    for (keep, send), bit_at, mine, cols in (
        ((keep_a, send_a), 8, place.row, slice(0, first)),
        ((keep_b, send_b), 1, bit(place.rest, 2), slice(first, wide_out.shape[2])),
    ):
        for ref, value in ((send, 1 - mine), (keep, mine)):
            def one(j, _):
                m = number(j, bit_at, value)
                ref[j] = (wide_rows(2 * m + core)[:, cols] + wide_in[m, :, cols].astype(jnp.float32)).astype(jnp.bfloat16)
                return 0
            lax.fori_loop(0, 8, one, 0)
    slim_copy.wait()
    mine = bit(place.group, 1)
    for ref, value in ((send_c, 1 - mine), (keep_c, mine)):
        def one(j, _):
            m = number(j, 2, value)
            ref[j] = (slim_rows(2 * m + core) + slim_in[m].astype(jnp.float32)).astype(jnp.bfloat16)
            return 0
        lax.fori_loop(0, 8, one, 0)
    spread_heads_wait(place, da_ref, do_ref, q_send, q_recv)


def spread_and_weights(shards, da, n2, att, act, dg, du, ct, db):
    width, ff = n2.shape[1], act.shape[1]
    per, per_ff = width // 32, ff // 32
    sem, low = pltpu.SemaphoreType.DMA, jnp.bfloat16
    wide, slim = (2 * per, ff + width // 2), (per_ff, width)
    first = (wide[1] // 256 + 1) * 128
    sums = [jax.ShapeDtypeStruct((8, 2 * per, cols), low) for cols in (first, first, wide[1] - first, wide[1] - first)]
    sums += [jax.ShapeDtypeStruct((8,) + slim, low)] * 2
    return pl.pallas_call(
        functools.partial(weights_kernel, shards),
        out_shape=(jax.ShapeDtypeStruct((2, 2) + da.shape[1:], da.dtype),) + tuple(sums),
        in_specs=[VMEM_SPEC] * 8,
        out_specs=(VMEM_SPEC,) * 7,
        scratch_shapes=[
            sem((4,)), sem((4,)), sem((2,)), sem((2,)),
            pltpu.VMEM((width, ff), jnp.float32), pltpu.VMEM((width, ff), jnp.float32),
            pltpu.VMEM((ff, width), jnp.float32), pltpu.VMEM((width, width), jnp.float32),
            pltpu.VMEM((16,) + wide, low), pltpu.VMEM((16,) + slim, low),
            pltpu.VMEM((16,) + wide, low), pltpu.VMEM((16,) + slim, low),
        ],
        compiler_params=pltpu.CompilerParams(collective_id=5, has_side_effects=True, vmem_limit_bytes=VMEM_BYTES),
        name="spread_and_weights",
    )(da, n2, att, act, dg, du, ct, db)


def reduce_kernel(shards, axes, orders, *refs):
    count = len(orders)
    q_ref, kv_ref = refs[:2]
    pairs = refs[2 : 2 + 2 * count]
    qo_ref, kvo_ref = refs[2 + 2 * count : 4 + 2 * count]
    sums = refs[4 + 2 * count : 4 + 3 * count]
    q_send, q_recv, send_sem, recv_sem, z_send, z_recv, w_send, w_recv = refs[4 + 3 * count : 12 + 3 * count]
    bufs = refs[12 + 3 * count :]
    place = Place(shards)
    rest_bits = bits_of(place.rest_size)
    greet(line_and_row(place) + [place.other_rest(mask) for mask in rest_bits])
    return_heads(place, q_ref, qo_ref, q_send, q_recv)
    ndim = 1 + len(rest_bits)
    at = {"dp": place.dp, "blk": place.blk}
    streams, used = [], ndim
    for s, (kept, order) in enumerate(orders):
        src, more = bufs[used], bufs[used + 1 : used + 1 + len(order)]
        used += 1 + len(order)
        streams.append(Stream(axes, at, kept, order, src, more, sums[s], w_send.at[s], w_recv.at[s]))
    own = [place.row] + [bit(place.rest, m) for m in rest_bits]
    targets = [place.other_row()] + [place.other_rest(m) for m in rest_bits]
    state = {}

    def plan(group_step):
        far = list(range(ndim - 1))
        turn = group_step % len(far)
        return [ndim - 1] + far[turn:] + far[:turn]

    def copy_of(step, stage):
        order = plan(step)
        group = (place.group + step) % GROUPS
        done = order[:stage]
        p_now = order[stage]
        buf = bufs[stage].at[step]
        if stage == 0:
            index = (p_index(group, done, p_now))
            src = kv_ref.at[index]
        else:
            kept = [p for p in range(ndim) if p not in done]
            src = bufs[stage - 1].at[(step,) + tuple(1 - own[p] if p == p_now else slice(None) for p in kept)]
        return remote(src, buf, send_sem.at[stage, step], recv_sem.at[stage, step], targets[p_now])

    def p_index(group, done, p_now):
        index = [slice(None)] * ndim
        index[p_now] = 1 - own[p_now]
        return (index[0], group) + tuple(index[1:])

    def absorb(step, stage):
        order = plan(step)
        done, p_now = order[:stage], order[stage]
        buf = bufs[stage].at[step]
        group = (place.group + step) % GROUPS
        if stage == 0:
            index = [None] * ndim
            index[p_now] = own[p_now]
            add_blocks(buf, kv_ref, (index[0], group) + tuple(index[1:]), buf.shape)
        else:
            kept = [p for p in range(ndim) if p not in done]
            index = tuple(own[p] if p == p_now else None for p in kept)
            add_blocks(buf, bufs[stage - 1].at[step], index, buf.shape)

    steps = (2, 1, 3, 0)
    for step in steps:
        copy_of(step, 0).start()
    for s, stream in enumerate(streams):
        add_two(stream.src, pairs[2 * s], pairs[2 * s + 1])
        stream.copy(0).start()
    for stage in range(ndim):
        for step in steps:
            copy_of(step, stage).wait()
            absorb(step, stage)
            if stage < ndim - 1:
                copy_of(step, stage + 1).start()
            elif step:
                remote(bufs[stage].at[step], kvo_ref.at[place.group], z_send.at[step], z_recv.at[(GROUPS - step) % GROUPS], place.other_group(step)).start()
            else:
                kvo_ref[place.group] = bufs[stage][step]
        for stream in streams:
            if stage < len(stream.order):
                stream.copy(stage).wait()
                stream.absorb(stage)
                if stage < len(stream.order) - 1:
                    stream.copy(stage + 1).start()
    for step in (1, 3, 2):
        there = kvo_ref.at[(place.group + step) % GROUPS]
        remote(bufs[ndim - 1].at[step], there, z_send.at[step], z_recv.at[step], place.other_group(step)).wait()
    return_heads_wait(place, q_ref, qo_ref, q_send, q_recv)


def add_two(dst_ref, one_ref, two_ref):
    lead = dst_ref.shape[:-2]

    def one(step, _):
        place, left = [], step
        for size in reversed(lead):
            place.append(left % size)
            left = left // size
        place = tuple(reversed(place))
        dst_ref[place] = (one_ref[place].astype(jnp.float32) + two_ref[place].astype(jnp.float32)).astype(dst_ref.dtype)
        return 0

    lax.fori_loop(0, math.prod(lead), one, 0)


def reduce_all(shape, q_packed, kv_sums, orders, pairs):
    shards = shape["blk"]
    tokens_all, width = kv_sums.shape[1:]
    tokens = tokens_all // shards
    rest_bits = bits_of(shards // GROUPS)
    ndim = 1 + len(rest_bits)
    sem = pltpu.SemaphoreType.DMA
    scratch = [pltpu.VMEM((GROUPS,) + (2,) * (ndim - 1 - s) + (tokens, width), kv_sums.dtype) for s in range(ndim)]
    flat, sums = [], []
    for (kept, order), pair in zip(orders, pairs):
        rows, cols = pair[0].shape[-2:]
        flat += [part.reshape((2,) * len(kept) + (rows, cols)) for part in pair]
        sums.append(jax.ShapeDtypeStruct((rows, cols), jnp.float32))
        scratch.append(pltpu.VMEM((2,) * len(kept) + (rows, cols), jnp.bfloat16))
        scratch += stream_scratch(len(kept), order, rows, cols)
    stages = max([len(order) for _, order in orders], default=1)
    return pl.pallas_call(
        functools.partial(reduce_kernel, shards, bit_axes(shape), orders),
        out_shape=(
            jax.ShapeDtypeStruct((GROUPS,) + q_packed.shape[2:], q_packed.dtype),
            jax.ShapeDtypeStruct((GROUPS, tokens, width), kv_sums.dtype),
        ) + tuple(sums),
        in_specs=[VMEM_SPEC] * (2 + len(flat)),
        out_specs=(VMEM_SPEC,) * (2 + len(sums)),
        scratch_shapes=[sem((4,)), sem((4,)), sem((ndim, GROUPS)), sem((ndim, GROUPS)), sem((GROUPS,)), sem((GROUPS,)),
                        sem((max(len(orders), 1), stages)), sem((max(len(orders), 1), stages))] + scratch,
        compiler_params=pltpu.CompilerParams(collective_id=2, has_side_effects=True, vmem_limit_bytes=VMEM_BYTES),
        name="reduce_keys",
    )(q_packed, kv_sums.reshape((2, GROUPS) + (2,) * len(rest_bits) + (tokens, width)), *flat)


TQ = 256
TK = 512
NEAR_ROWS = 448
NEG = -1e30
FIRST_MAX = -1e29
NT = (((1,), (1,)), ((), ()))
NN = (((1,), (0,)), ((), ()))
BORDERS = (12, 16, 23, 32, 46, 64, 91)


def mxu(left, right, dims=NN):
    return lax.dot_general(left, right, dims, preferred_element_type=jnp.float32)


def turned(tile):
    return jnp.concatenate([tile[:, 64:], tile[:, :64]], axis=1)


def spread_lanes(packed, high):
    lane = lax.broadcasted_iota(jnp.int32, (1, 128), 1)
    keep = lane >= 64 if high else lane < 64
    zero = jnp.zeros((), packed.dtype)
    pair, last = packed[0:TQ], packed[TQ:]
    pick = lambda tile: jnp.where(keep, tile, zero)
    if high:
        return [pick(turned(pair)), pick(pair), jnp.concatenate([pick(turned(last)), pick(last)], axis=0)]
    return [pick(pair), pick(turned(pair)), jnp.concatenate([pick(last), pick(turned(last))], axis=0)]


def join_heads(parts):
    half = TQ // 2
    top = jnp.concatenate([parts[0], parts[1]], axis=1)
    low = jnp.concatenate([parts[2][:half], parts[2][half:]], axis=1)
    return jnp.concatenate([top, low], axis=0)


def valid_mask(se_ref, r, i, k0):
    kpos = k0 + lax.broadcasted_iota(jnp.int32, (TK, TQ), 0)
    return jnp.logical_and(kpos >= se_ref[r, i, 0:1, :], kpos < se_ref[r, i, 1:2, :])


def near_buckets(first, rows, parity):
    relative = (
        first - TK + TQ * parity
        + lax.broadcasted_iota(jnp.int32, (rows, TQ), 0)
        - lax.broadcasted_iota(jnp.int32, (rows, TQ), 1)
    )
    return buckets_of(relative)


def make_bias(table, parity, bias_ref, near_ref):
    heads = bias_ref.shape[0]
    for h in range(heads):
        bias_ref[h, 0] = jnp.full((TK, TQ), table[h, 15], jnp.float32).astype(jnp.bfloat16)
        bias_ref[h, 3] = jnp.full((TK, TQ), table[h, 31], jnp.float32).astype(jnp.bfloat16)
    for tile in range(2):
        def rows(step, _):
            start = pl.multiple_of(step * 32, 32)
            which = near_buckets(tile * TK + start, 32, parity)
            for h in range(heads):
                value = jnp.zeros((32, TQ), jnp.float32)
                for b in range(BUCKETS):
                    value = jnp.where(which == b, table[h, b], value)
                bias_ref[h, tile + 1, pl.ds(start, 32)] = value.astype(jnp.bfloat16)
                near_ref[h, tile, pl.ds(start, 32)] = value.astype(jnp.bfloat16)
            return 0
        lax.fori_loop(0, TK // 32, rows, 0)


def tile_kind(bounds, r, i, t):
    slot = jnp.clip(t - bounds[r, i, 2] + 1, 0, 3)
    away = jnp.logical_or(slot == 0, slot == 3)
    inside = jnp.logical_and(t >= bounds[r, i, 3], t < bounds[r, i, 4])
    return slot, jnp.logical_and(away, inside)


def fwd_kernel(bounds, table, q_ref, kv_ref, se_ref, o_ref, keep_ref, lse_ref, bias_ref, near_ref, vt, acc, mx, qp):
    heads = lse_ref.shape[2]
    make_bias(table, bounds[0, 0, 5], bias_ref, near_ref)
    for r in range(2):
        for i in range(2):
            for h, tile in enumerate(spread_lanes(q_ref[r, i], False)):
                qp[r, i, h] = tile

    def row_body(r, _):
        lo_all = jnp.minimum(bounds[r, 0, 0], bounds[r, 1, 0])
        hi_all = jnp.maximum(bounds[r, 0, 1], bounds[r, 1, 1])

        def turn(t, _):
            k0 = pl.multiple_of(t * TK, TK)
            for h in range(heads):
                tile = kv_ref[r, pl.ds(k0, TK), h * 128 : h * 128 + 128]
                vt[h, 0:64, pl.ds(k0, TK)] = tile.T[64:128, :]
                vt[h, 64:80, pl.ds(k0, TK)] = jnp.ones((16, TK), jnp.bfloat16)
            return 0

        lax.fori_loop(lo_all, hi_all, turn, 0)

        def q_body(i, _):
            acc[...] = jnp.zeros_like(acc)
            mx[...] = jnp.full_like(mx, FIRST_MAX)

            def tile_body(t, _):
                k0 = pl.multiple_of(t * TK, TK)
                slot, plain = tile_kind(bounds, r, i, t)

                def scores(h):
                    return mxu(kv_ref[r, pl.ds(k0, TK), h * 128 : h * 128 + 128], qp[r, i, h], NT)

                def finish(h, s, b):
                    m_old = mx[h]
                    m_new = jnp.maximum(m_old, jnp.max(s, axis=0, keepdims=True) + b)
                    p = jnp.exp(s - (m_new - b)).astype(jnp.bfloat16)
                    mx[h] = m_new
                    acc[h] = acc[h] * jnp.exp(m_old - m_new) + mxu(vt[h, :, pl.ds(k0, TK)], p)

                @pl.when(plain)
                def _():
                    found = [scores(h) for h in range(heads)]
                    for h in range(heads):
                        finish(h, found[h], jnp.where(slot == 0, table[h, 15], table[h, 31]))

                @pl.when(jnp.logical_not(plain))
                def _():
                    ok = valid_mask(se_ref, r, i, k0)
                    for h in range(heads):
                        s = scores(h) + bias_ref[h, slot].astype(jnp.float32)
                        finish(h, jnp.where(ok, s, NEG), 0.0)

                return 0

            lax.fori_loop(bounds[r, i, 0], bounds[r, i, 1], tile_body, 0)
            parts = []
            for h in range(heads):
                total = acc[h, 64:65, :]
                parts.append((acc[h, 0:64, :] / total).T)
                lse_ref[r, i, h] = mx[h] + jnp.log(total)
            joined = join_heads(parts)
            o_ref[r, i] = joined.astype(jnp.bfloat16)
            keep_ref[r, i] = joined
            return 0

        lax.fori_loop(0, 2, q_body, 0)
        return 0

    lax.fori_loop(0, 2, row_body, 0)


def attention(bounds, table, q, kv, se):
    heads, n = kv.shape[2] // 128, kv.shape[1]
    packed = q.shape
    return pl.pallas_call(
        fwd_kernel,
        out_shape=(
            jax.ShapeDtypeStruct(packed, jnp.bfloat16),
            jax.ShapeDtypeStruct(packed, jnp.float32),
            jax.ShapeDtypeStruct((2, 2, heads, 1, TQ), jnp.float32),
            jax.ShapeDtypeStruct((heads, 4, TK, TQ), jnp.bfloat16),
            jax.ShapeDtypeStruct((heads, 2, TK, TQ), jnp.bfloat16),
        ),
        in_specs=[SMEM_SPEC] * 2 + [VMEM_SPEC] * 3,
        out_specs=(VMEM_SPEC,) * 5,
        scratch_shapes=[
            pltpu.VMEM((heads, 80, n), jnp.bfloat16),
            pltpu.VMEM((heads, 80, TQ), jnp.float32),
            pltpu.VMEM((heads, 1, TQ), jnp.float32),
            pltpu.VMEM((2, 2, heads, TQ, 128), jnp.bfloat16),
        ],
        compiler_params=pltpu.CompilerParams(vmem_limit_bytes=VMEM_BYTES),
        name="attention",
    )(bounds, table, q, kv, se)


def prepare(q, do, q_out, do_out):
    for h, tile in enumerate(spread_lanes(q, False)):
        q_out[h] = tile
    for h, tile in enumerate(spread_lanes(do, True)):
        do_out[h] = tile


def row_deltas(do, keep, delta):
    prod = (do.astype(jnp.float32) * keep).T
    top, low = prod[:, 0:TQ], prod[:, TQ:]
    delta[0] = jnp.sum(top[0:64], axis=0, keepdims=True)
    delta[1] = jnp.sum(top[64:128], axis=0, keepdims=True)
    delta[2] = jnp.concatenate(
        [jnp.sum(low[0:64], axis=0, keepdims=True), jnp.sum(low[64:128], axis=0, keepdims=True)], axis=1
    )


def near_start(parity):
    return 416 - TQ * parity


def far_sums(grid, h, first, end):
    def one(step, total):
        rows = grid[h, pl.ds(pl.multiple_of(step * 32, 32), 32)]
        return total + jnp.sum(rows.reshape(4, 8, TQ), axis=0)
    total = lax.fori_loop(first // 32, end // 32, one, jnp.zeros((8, TQ), jnp.float32))
    return jnp.sum(total, axis=0, keepdims=True)


def bucket_sums(parity, near, side, tab_ref, tab8):
    heads = near.shape[0]
    tab8[...] = jnp.zeros_like(tab8)

    def inner(step, _):
        start = pl.multiple_of(step * 32, 32)
        which = near_buckets(near_start(parity) + start, 32, parity)
        for b in range(BUCKETS):
            here = which == b
            for h in range(heads):
                rows = jnp.where(here, near[h, pl.ds(start, 32)], 0.0)
                tab8[h, b] += jnp.sum(rows.reshape(4, 8, TQ), axis=0)
        return 0

    lax.fori_loop(0, NEAR_ROWS // 32, inner, 0)
    for h in range(heads):
        tab_ref[h] = jnp.sum(tab8[h], axis=1)
        tab_ref[h, 15:16] += side[h, 0:1]
        tab_ref[h, 31:32] += side[h, 1:2]


def bwd_kernel(alone, bounds, table, q_ref, do_ref, keep_ref, kv_ref, bias_ref, se_ref, lse_ref,
               dq_ref, dkv_ref, near_ref, side, delta, *rest):
    tab_ref, tab8, rest = (None, None, rest) if alone else (rest[0], rest[-1], rest[1:-1])
    kt, dqt, dkv, grid, qp, dp_ref = rest
    heads = lse_ref.shape[2]
    n = kv_ref.shape[1]
    grid[...] = jnp.zeros_like(grid)
    side[...] = jnp.zeros_like(side)
    base = 1 - bounds[0, 0, 6] if alone else 0
    for at in range(1 if alone else 2):
        for i in range(2):
            prepare(q_ref[base + at, i], do_ref[base + at, i], qp.at[at, i], dp_ref.at[at, i])
    for r in range(2):
        for i in range(2):
            row_deltas(do_ref[r, i], keep_ref[r, i], delta.at[r, i])

    def row_body(at, _):
        r = base + at
        lo_all = jnp.minimum(bounds[r, 0, 0], bounds[r, 1, 0])
        hi_all = jnp.maximum(bounds[r, 0, 1], bounds[r, 1, 1])

        def clear(t, _):
            k0 = pl.multiple_of(t * TK, TK)
            for h in range(heads):
                dkv[h, pl.ds(k0, TK), :] = jnp.zeros((TK, 128), jnp.float32)
            return 0

        lax.fori_loop(0, n // TK, clear, 0)

        def turn(t, _):
            k0 = pl.multiple_of(t * TK, TK)
            for h in range(heads):
                tile = kv_ref[r, pl.ds(k0, TK), h * 128 : h * 128 + 128]
                kt[h, 0:64, pl.ds(k0, TK)] = tile.T[0:64, :]
                kt[h, 64:80, pl.ds(k0, TK)] = jnp.ones((16, TK), jnp.bfloat16)
            return 0

        lax.fori_loop(lo_all, hi_all, turn, 0)

        def q_body(i, _):
            dqt[...] = jnp.zeros_like(dqt)

            def tile_body(t, _):
                k0 = pl.multiple_of(t * TK, TK)
                slot, plain = tile_kind(bounds, r, i, t)

                def finish(h, p, ds, where):
                    ds_low = ds.astype(jnp.bfloat16)
                    two = jnp.concatenate([ds_low, p.astype(jnp.bfloat16)], axis=1)
                    both = jnp.concatenate([qp[at, i, h], dp_ref[at, i, h]], axis=0)
                    dkv[h, pl.ds(k0, TK), :] += mxu(two, both)
                    dqt[h, where] += mxu(kt[h, :, pl.ds(k0, TK)], ds_low)

                def products(h):
                    tile = kv_ref[r, pl.ds(k0, TK), h * 128 : h * 128 + 128]
                    return mxu(tile, qp[at, i, h], NT), mxu(tile, dp_ref[at, i, h], NT)

                @pl.when(plain)
                def _():
                    for h in range(heads):
                        s, d_probs = products(h)
                        p = jnp.exp(s - (lse_ref[r, i, h] - jnp.where(slot == 0, table[h, 15], table[h, 31])))
                        finish(h, p, p * (d_probs - delta[r, i, h]), jnp.where(slot == 0, 0, 2))

                @pl.when(jnp.logical_not(plain))
                def _():
                    ok = valid_mask(se_ref, r, i, k0)
                    for h in range(heads):
                        s, d_probs = products(h)
                        s = s + bias_ref[h, slot].astype(jnp.float32)
                        p = jnp.where(ok, jnp.exp(jnp.where(ok, s, NEG) - lse_ref[r, i, h]), 0.0)
                        ds = p * (d_probs - delta[r, i, h])
                        grid[h, pl.ds(pl.multiple_of(slot * TK, TK), TK)] += ds
                        finish(h, p, ds, 1)

                return 0

            lax.fori_loop(bounds[r, i, 0], bounds[r, i, 1], tile_body, 0)
            parts = []
            for h in range(heads):
                parts.append((dqt[h, 0, 0:64] + dqt[h, 1, 0:64] + dqt[h, 2, 0:64]).T * 0.125)
                side[h, 0:1] += dqt[h, 0, 64:65]
                side[h, 1:2] += dqt[h, 2, 64:65]
            dq_ref[at, i] = join_heads(parts).astype(jnp.bfloat16)
            return 0

        lax.fori_loop(0, 2, q_body, 0)

        def put(t, _):
            k0 = pl.multiple_of(t * TK, TK)
            for h in range(heads):
                dkv_ref[at, pl.ds(k0, TK), h * 128 : h * 128 + 128] = dkv[h, pl.ds(k0, TK), :].astype(jnp.bfloat16)
            return 0

        lax.fori_loop(0, n // TK, put, 0)
        return 0

    lax.fori_loop(0, 1 if alone else 2, row_body, 0)

    parity = bounds[0, 0, 5]
    first = TK + near_start(parity)
    for h in range(heads):
        near_ref[h] = grid[h, pl.ds(pl.multiple_of(first, 32), NEAR_ROWS)]
        side[h, 0:1] += far_sums(grid, h, 0, first)
        side[h, 1:2] += far_sums(grid, h, first + NEAR_ROWS, 4 * TK)
    if not alone:
        bucket_sums(parity, near_ref, side, tab_ref, tab8)


def attention_back(alone, bounds, table, q, do, keep, kv, bias, se, lse):
    heads, n = kv.shape[2] // 128, kv.shape[1]
    count = 1 if alone else 2
    table_out = [] if alone else [jax.ShapeDtypeStruct((heads, BUCKETS, TQ), jnp.float32)]
    return pl.pallas_call(
        functools.partial(bwd_kernel, alone),
        out_shape=(
            jax.ShapeDtypeStruct((count,) + q.shape[1:], jnp.bfloat16),
            jax.ShapeDtypeStruct((count,) + kv.shape[1:], jnp.bfloat16),
            jax.ShapeDtypeStruct((heads, NEAR_ROWS, TQ), jnp.float32),
            jax.ShapeDtypeStruct((heads, 2, TQ), jnp.float32),
            jax.ShapeDtypeStruct((2, 2, heads, 1, TQ), jnp.float32),
        ) + tuple(table_out),
        in_specs=[SMEM_SPEC] * 2 + [VMEM_SPEC] * 7,
        out_specs=(VMEM_SPEC,) * (5 + len(table_out)),
        scratch_shapes=[
            pltpu.VMEM((heads, 80, n), jnp.bfloat16),
            pltpu.VMEM((heads, 3, 80, TQ), jnp.float32),
            pltpu.VMEM((heads, n, 128), jnp.float32),
            pltpu.VMEM((heads, 4 * TK, TQ), jnp.float32),
            pltpu.VMEM((count, 2, heads, TQ, 128), jnp.bfloat16),
            pltpu.VMEM((count, 2, heads, TQ, 128), jnp.bfloat16),
        ] + [pltpu.VMEM((heads, BUCKETS, 8, TQ), jnp.float32) for _ in table_out],
        compiler_params=pltpu.CompilerParams(vmem_limit_bytes=VMEM_BYTES),
        name="attention_back",
    )(bounds, table, q, do, keep, kv, bias, se, lse)


TAPS = tuple(range(-3, 5))
LEAD = 8


def pool_scalars(y_rows, lab_rows, first):
    tokens = y_rows[0].shape[1]
    t = lax.broadcasted_iota(jnp.int32, (1, tokens), 1)
    at = lambda rows, k: rows[k + 3]
    found = []
    for p in range(2):
        inside = {1: 0 * t, 2: 0 * t + p, 3: (first + 2 * t + p) % 3, 4: 2 * (t % 2) + p}
        weights, scores = {}, []
        for b in range(1, MAX_BLOCK + 1):
            keep = {}
            for o in range(1 - b, b):
                same = jnp.logical_and(inside[b] + o >= 0, inside[b] + o < b)
                same = jnp.logical_and(same, at(lab_rows, p + o) == at(lab_rows, p))
                keep[o] = same.astype(jnp.float32)
            inverse = 1.0 / sum(keep.values())
            for o in keep:
                weights[b, o] = keep[o] * inverse
            scores.append(sum(weights[b, o] * at(y_rows, p + o) for o in keep))
        top = functools.reduce(jnp.maximum, scores)
        grown = [jnp.exp(s - top) for s in scores]
        total = sum(grown)
        found.append(([g / total for g in grown], weights))
    return found


def tap_weights(found):
    rows = []
    for k in TAPS:
        row = 0.0
        for p, (probs, weights) in enumerate(found):
            for b in range(1, MAX_BLOCK + 1):
                if (b, k - p) in weights:
                    row = row + probs[b - 1] * weights[b, k - p]
        rows.append(0.5 * row)
    return rows


def as_columns(rows):
    tokens = rows[0].shape[1]
    return jnp.concatenate(list(rows) + [jnp.zeros((128 - len(rows), tokens), jnp.float32)], axis=0).T


def load_bytes(x_ref, before_ref, after_ref, xs):
    length, width = x_ref.shape
    for j in range(width // 128):
        cols = slice(j * 128, j * 128 + 128)
        xs[j, 0:LEAD, :] = jnp.zeros((LEAD, 128), jnp.float32)
        xs[j, LEAD + length :, :] = jnp.zeros((LEAD, 128), jnp.float32)
        xs[j, LEAD - 2 : LEAD, :] = before_ref[0:2, cols].astype(jnp.float32)
        xs[j, LEAD + length : LEAD + length + 2, :] = after_ref[0:2, cols].astype(jnp.float32)
        xs[j, LEAD : LEAD + length, :] = x_ref[:, cols].astype(jnp.float32)


def tap(xs, k, tokens):
    return jnp.concatenate([xs[j, pl.ds(LEAD + k, tokens, stride=2), :] for j in range(xs.shape[0])], axis=1)


def strips(buf, first, rows):
    return jnp.concatenate([buf[j, first : first + rows, :] for j in range(buf.shape[0])], axis=1)


def unit_rows(values):
    return lax.rsqrt(jnp.mean(values * values, axis=-1, keepdims=True) + 1e-06)


def pool_kernel(shards, scale, x_ref, before_ref, after_ref, lab_ref, score_ref, gain_ref, wq_ref, wk_ref, wv_ref,
                hidden_ref, n1_ref, y_ref, share_ref, q_ref, kv_ref, xs):
    tokens = hidden_ref.shape[0]
    width = hidden_ref.shape[1]
    load_bytes(x_ref, before_ref, after_ref, xs)
    score = jnp.broadcast_to(score_ref[...], (8, width))
    for k in TAPS:
        y_ref[k + 3 : k + 4, :] = mxu(score, tap(xs, k, tokens).astype(jnp.bfloat16), NT)[0:1]
    rows = [y_ref[j : j + 1, :] for j in range(8)]
    labels = [lab_ref[j : j + 1, :] for j in range(8)]
    first = (lax.axis_index("blk") * x_ref.shape[0]) % 3
    found = pool_scalars(rows, labels, first)
    lane = lax.broadcasted_iota(jnp.int32, (1, 128), 1)
    share = jnp.zeros((1, 128), jnp.float32)
    for b in range(MAX_BLOCK):
        share = jnp.where(lane == b, jnp.sum(found[0][0][b] + found[1][0][b], axis=1, keepdims=True) * scale, share)
    share_ref[...] = share
    columns = as_columns(tap_weights(found))
    hidden = sum(columns[:, k + 3 : k + 4] * tap(xs, k, tokens) for k in TAPS)
    hidden_ref[...] = hidden
    n1 = (hidden * unit_rows(hidden) * gain_ref[...].astype(jnp.float32)).astype(jnp.bfloat16)
    n1_ref[...] = n1
    keys = mxu(n1, wk_ref[...]).astype(jnp.bfloat16)
    values = mxu(n1, wv_ref[...]).astype(jnp.bfloat16)
    low = lane < 64
    for j in range(width // 128):
        k_pair, v_pair = keys[:, j * 128 : j * 128 + 128], values[:, j * 128 : j * 128 + 128]
        one = jnp.where(low, k_pair, turned(v_pair))
        two = jnp.where(low, turned(k_pair), v_pair)
        for head, tile in ((2 * j, one), (2 * j + 1, two)):
            kv_ref[head // 3, :, head % 3 * 128 : head % 3 * 128 + 128] = tile
    queries = mxu(n1, wq_ref[...]).astype(jnp.bfloat16) * jnp.bfloat16(0.125)
    put_packed(queries, q_ref)


def put_packed(array, out_ref):
    tokens = array.shape[0]
    half = tokens // 2
    for g in range(GROUPS):
        part = array[:, g * 192 : g * 192 + 192]
        out_ref[g, 0:tokens, :] = part[:, 0:128]
        out_ref[g, tokens:, :] = jnp.concatenate([part[:half, 128:], part[half:, 128:]], axis=1)


def get_packed(packed_ref):
    tokens = packed_ref.shape[1] * 2 // 3
    parts = []
    for g in range(GROUPS):
        last = packed_ref[g, tokens:, :]
        parts += [packed_ref[g, 0:tokens, :], jnp.concatenate([last[:, :64], last[:, 64:]], axis=0)]
    return jnp.concatenate(parts, axis=1)


def pool_and_project(shards, scale, x, before, after, labels, score, gain, wq, wk, wv):
    length, width = x.shape
    tokens = length // 2
    return pl.pallas_call(
        functools.partial(pool_kernel, shards, scale),
        out_shape=(
            jax.ShapeDtypeStruct((tokens, width), jnp.float32),
            jax.ShapeDtypeStruct((tokens, width), jnp.bfloat16),
            jax.ShapeDtypeStruct((8, tokens), jnp.float32),
            jax.ShapeDtypeStruct((1, 128), jnp.float32),
            jax.ShapeDtypeStruct((GROUPS, tokens * 3 // 2, 128), jnp.bfloat16),
            jax.ShapeDtypeStruct((GROUPS, tokens, width * 2 // GROUPS), jnp.bfloat16),
        ),
        in_specs=[VMEM_SPEC] * 9,
        out_specs=(VMEM_SPEC,) * 6,
        scratch_shapes=[pltpu.VMEM((width // 128, length + 2 * LEAD, 128), jnp.float32)],
        compiler_params=pltpu.CompilerParams(vmem_limit_bytes=VMEM_BYTES),
        name="pool_and_project",
    )(x, before, after, labels, score, gain, wq, wk, wv)


GELU_A = math.sqrt(2.0 / math.pi)
GELU_B = 0.044715


def norm_back(d_out, rows, gain):
    unit = unit_rows(rows)
    flat = rows * unit
    scaled = d_out * gain
    d_rows = unit * (scaled - flat * jnp.mean(scaled * flat, axis=-1, keepdims=True))
    return d_rows, jnp.sum(d_out * flat, axis=0, keepdims=True)


def feed_kernel(o_ref, hidden_ref, ct_ref, gain_ref, wo_ref, wg_ref, wu_ref, wd_ref,
                out_ref, dres_ref, da_ref, dgain_ref, n2_ref, att_ref, act_ref, dg_ref, du_ref, db_ref, acc, dn2):
    ff = wg_ref.shape[1]
    step = 512
    att = get_packed(o_ref)
    att_ref[...] = att
    residual = hidden_ref[...] + mxu(att, wo_ref[...])
    gain = gain_ref[...].astype(jnp.float32)
    n2_ref[...] = (residual * unit_rows(residual) * gain).astype(jnp.bfloat16)
    acc[...] = residual
    dn2[...] = jnp.zeros_like(dn2)

    for j in range(ff // step):
        cols = slice(j * step, j * step + step)
        n2 = n2_ref[...]
        gate = mxu(n2, wg_ref[:, cols])
        up = mxu(n2, wu_ref[:, cols])
        d_act = mxu(ct_ref[...], wd_ref[cols, :], NT)
        square = gate * gate
        curve = jnp.tanh(GELU_A * gate * (1.0 + GELU_B * square))
        half = 0.5 * (1.0 + curve)
        grown = gate * half
        slope = half + 0.5 * gate * (1.0 - curve * curve) * (GELU_A * (1.0 + 3.0 * GELU_B * square))
        act = (grown * up).astype(jnp.bfloat16)
        d_gate = (d_act * up * slope).astype(jnp.bfloat16)
        d_up = (d_act * grown).astype(jnp.bfloat16)
        act_ref[:, cols] = act
        dg_ref[:, cols] = d_gate
        du_ref[:, cols] = d_up
        acc[...] += mxu(act, wd_ref[cols, :])
        dn2[...] += mxu(d_gate, wg_ref[:, cols], NT) + mxu(d_up, wu_ref[:, cols], NT)

    out_ref[...] = acc[...].astype(jnp.bfloat16)
    residual = hidden_ref[...] + mxu(att_ref[...], wo_ref[...])
    d_rows, d_gain = norm_back(dn2[...], residual, gain)
    dgain_ref[...] = d_gain
    d_res = ct_ref[...].astype(jnp.float32) + d_rows
    dres_ref[...] = d_res
    d_branch = d_res.astype(jnp.bfloat16)
    db_ref[...] = d_branch
    put_packed(mxu(d_branch, wo_ref[...], NT).astype(jnp.bfloat16), da_ref)


def feed_forward(o_home, hidden, ct, gain, wo, wg, wu, wd):
    tokens, width = hidden.shape
    ff = wg.shape[1]
    low = lambda cols: jax.ShapeDtypeStruct((tokens, cols), jnp.bfloat16)
    return pl.pallas_call(
        feed_kernel,
        out_shape=(
            low(width),
            jax.ShapeDtypeStruct((tokens, width), jnp.float32),
            jax.ShapeDtypeStruct(o_home.shape, jnp.bfloat16),
            jax.ShapeDtypeStruct((1, width), jnp.float32),
            low(width), low(width), low(ff), low(ff), low(ff), low(width),
        ),
        in_specs=[VMEM_SPEC] * 8,
        out_specs=(VMEM_SPEC,) * 10,
        scratch_shapes=[pltpu.VMEM((tokens, width), jnp.float32)] * 2,
        compiler_params=pltpu.CompilerParams(vmem_limit_bytes=VMEM_BYTES),
        name="feed_forward",
    )(o_home, hidden, ct, gain, wo, wg, wu, wd)


def unpack_pairs(dkv_ref, width):
    low = lax.broadcasted_iota(jnp.int32, (1, 128), 1) < 64
    dk_parts, dv_parts = [], []
    for j in range(width // 128):
        one, two = [dkv_ref[h // 3, :, h % 3 * 128 : h % 3 * 128 + 128] for h in (2 * j, 2 * j + 1)]
        dk_parts.append(jnp.where(low, one, turned(two)))
        dv_parts.append(jnp.where(low, turned(one), two))
    return jnp.concatenate(dk_parts, axis=1), jnp.concatenate(dv_parts, axis=1)


def pool_back(d_hidden, x_refs, lab_ref, y_ref, score_ref, gb_ref, edge_ref, spill_ref, xs, gbuf):
    x_ref = x_refs[0]
    tokens, width = d_hidden.shape
    length = x_ref.shape[0]
    lane = lax.broadcasted_iota(jnp.int32, (1, 128), 1)
    met = jnp.zeros((tokens, 128), jnp.float32)
    for k in TAPS:
        met = jnp.where(lane == k + 3, jnp.sum(d_hidden * tap(xs, k, tokens), axis=-1, keepdims=True), met)
    met = met.T
    first = (lax.axis_index("blk") * length) % 3
    found = pool_scalars([y_ref[j : j + 1, :] for j in range(8)], [lab_ref[j : j + 1, :] for j in range(8)], first)
    touch = [0.0] * 8
    for p, (probs, weights) in enumerate(found):
        d_block = []
        for b in range(1, MAX_BLOCK + 1):
            d_block.append(0.5 * sum(weights[b, o] * met[p + o + 3 : p + o + 4] for o in range(1 - b, b)))
        mean = sum(q * d for q, d in zip(probs, d_block))
        for b in range(1, MAX_BLOCK + 1):
            d_score = probs[b - 1] * (d_block[b - 1] - mean)
            for o in range(1 - b, b):
                touch[p + o + 3] = touch[p + o + 3] + d_score * weights[b, o]
    share_cols = as_columns(tap_weights(found) + touch)
    score = score_ref[...].astype(jnp.float32)
    gbuf[...] = jnp.zeros_like(gbuf)
    d_score_vec = jnp.zeros((1, width), jnp.float32)
    for k in TAPS:
        own, via = share_cols[:, k + 3 : k + 4], share_cols[:, k + 11 : k + 12]
        added = own * d_hidden + via * score
        for j in range(gbuf.shape[0]):
            gbuf[j, pl.ds(LEAD + k, tokens, stride=2), :] += added[:, j * 128 : j * 128 + 128]
        d_score_vec = d_score_vec + jnp.sum(via * tap(xs, k, tokens), axis=0, keepdims=True)
    gb_ref[...] = strips(gbuf, LEAD, length).astype(jnp.bfloat16)
    edge_ref[0] = strips(gbuf, LEAD, 16)
    edge_ref[1] = strips(gbuf, LEAD + length - 16, 16)
    spill_ref[0] = strips(gbuf, 0, LEAD)
    spill_ref[1] = strips(gbuf, LEAD + length, LEAD)
    return d_score_vec


def put_small(small_ref, vectors, tab_ref, share_ref):
    small_ref[...] = jnp.zeros_like(small_ref)
    for row, vector in zip((0, 6, 12), vectors):
        for j in range(6):
            small_ref[row + j : row + j + 1, :] = vector[:, j * 128 : j * 128 + 128]
    heads = tab_ref.shape[0]
    group = lax.axis_index("blk") // (lax.axis_size("blk") // GROUPS)
    for h in range(heads):
        total = lax.dot_general(
            jnp.ones((8, tab_ref.shape[2]), jnp.float32), tab_ref[h], NT,
            precision=lax.Precision.HIGHEST, preferred_element_type=jnp.float32,
        )
        small_ref[pl.ds(18 + group * heads + h, 1), 0:BUCKETS] = total[0:1]
    small_ref[30:31, :] = share_ref[...]


def last_kernel(shards, axes, order, dq_ref, dkv_ref, hidden_ref, dres_ref, x_ref, before_ref, after_ref, lab_ref, y_ref, score_ref,
                gain_ref, wq_ref, wk_ref, wv_ref, dgain2_ref, share_ref, tab_ref, gb_ref, edge_ref, spill_out, small_out, parts_ref,
                w_send, w_recv, s_send, s_recv, xs, gbuf, spill_ref, small_ref, small_bufs):
    at = {"dp": lax.axis_index("dp"), "blk": lax.axis_index("blk")}
    width = hidden_ref.shape[1]
    whole = Whole(axes, at, order, small_ref, small_bufs, small_out, w_send, w_recv)
    left = (at["dp"], (at["blk"] + shards - 1) % shards)
    right = (at["dp"], (at["blk"] + 1) % shards)
    greet([whole.stream.target(p) for p in range(len(axes))] + [left, right])
    load_bytes(x_ref, before_ref, after_ref, xs)
    dq = get_packed(dq_ref)
    dk, dv = unpack_pairs(dkv_ref, width)
    parts_ref[0], parts_ref[1], parts_ref[2] = dq, dk, dv
    d_n1 = mxu(dq, wq_ref[...], NT) + mxu(dk, wk_ref[...], NT) + mxu(dv, wv_ref[...], NT)
    d_rows, d_gain1 = norm_back(d_n1, hidden_ref[...], gain_ref[...].astype(jnp.float32))
    d_hidden = dres_ref[...] + d_rows
    d_score = pool_back(d_hidden, (x_ref, before_ref, after_ref), lab_ref, y_ref, score_ref, gb_ref, edge_ref, spill_ref, xs, gbuf)
    put_small(small_ref, (d_score, d_gain1, dgain2_ref[...]), tab_ref, share_ref)
    spills = [
        remote(spill_ref.at[0], spill_out.at[1], s_send.at[0], s_recv.at[1], left),
        remote(spill_ref.at[1], spill_out.at[0], s_send.at[1], s_recv.at[0], right),
    ]
    whole.copy(0).start()
    for copy in spills:
        copy.start()
    for stage in range(len(axes)):
        advance(whole, stage)
    for copy in spills:
        copy.wait()


def last_part(shape, dq, dkv, hidden, dres, x, before, after, labels, y, score, gain, wq, wk, wv, dgain2, share, tab):
    tokens, width = hidden.shape
    length = x.shape[0]
    axes = bit_axes(shape)
    ndim = len(axes)
    full, sem, low = jax.ShapeDtypeStruct, pltpu.SemaphoreType.DMA, jnp.bfloat16
    strip = pltpu.VMEM((width // 128, length + 2 * LEAD, 128), jnp.float32)
    return pl.pallas_call(
        functools.partial(last_kernel, shape["blk"], axes, tuple(reversed(range(ndim)))),
        out_shape=(
            full((length, width), low),
            full((2, 16, width), jnp.float32),
            full((2, LEAD, width), jnp.float32),
            full((32, 128), jnp.float32),
            full((3, tokens, width), low),
        ),
        in_specs=[VMEM_SPEC] * 17,
        out_specs=(VMEM_SPEC,) * 5,
        scratch_shapes=[
            sem((ndim,)), sem((ndim,)), sem((2,)), sem((2,)), strip, strip,
            pltpu.VMEM((2, LEAD, width), jnp.float32), pltpu.VMEM((32, 128), jnp.float32), pltpu.VMEM((2, ndim, 32, 128), jnp.float32),
        ],
        compiler_params=pltpu.CompilerParams(collective_id=3, has_side_effects=True, vmem_limit_bytes=VMEM_BYTES),
        name="last_part",
    )(dq, dkv, hidden, dres, x, before, after, labels, y, score, gain, wq, wk, wv, dgain2, share, tab)


def finish_kernel(shards, heads_all, gb_ref, edge_ref, spill_ref, small_ref, *refs):
    position = lax.axis_index("blk")
    streams, outs = refs[: len(refs) - (5 if len(refs) == 5 else 12)], refs[len(refs) - (5 if len(refs) == 5 else 12) :]
    bytes_ref, score_ref, gain1_ref, gain2_ref, tab_ref = outs[:5]
    length = gb_ref.shape[0]
    bytes_ref[...] = gb_ref[...]
    zero = jnp.zeros((16 - LEAD, gb_ref.shape[1]), jnp.float32)
    left = jnp.where(position > 0, spill_ref[0], 0.0)
    right = jnp.where(position < shards - 1, spill_ref[1], 0.0)
    bytes_ref[0:16, :] = (edge_ref[0] + jnp.concatenate([left, zero], axis=0)).astype(jnp.bfloat16)
    bytes_ref[length - 16 :, :] = (edge_ref[1] + jnp.concatenate([zero, right], axis=0)).astype(jnp.bfloat16)
    for row, ref in ((0, score_ref), (6, gain1_ref), (12, gain2_ref)):
        for j in range(6):
            ref[j * 128 : j * 128 + 128] = small_ref[row + j, :]
    tab_ref[...] = small_ref[16:32, :]
    if streams:
        gq, gk, gv, go, gg, gu, gd = outs[5:]
        per, width = gq.shape
        half, ff = width // 2, gg.shape[1]
        one, two, down, *thirds = streams
        for ref, third in zip((gq, gk, gv), thirds):
            ref[:, :half] = third[:per, :]
            ref[:, half:] = third[per:, :]
        first = one.shape[1]
        for ref, rows in ((gg, slice(0, per)), (gu, slice(per, 2 * per))):
            ref[:, :first] = one[rows, :]
            ref[:, first:] = two[rows, : ff - first]
        go[:, :half] = two[:per, ff - first :]
        go[:, half:] = two[per:, ff - first :]
        gd[...] = down[...]


def finish(shards, heads_all, per, ff, gb, edge, spill, small, streams):
    width = gb.shape[1]
    full = jax.ShapeDtypeStruct
    line = full((width,), jnp.float32)
    outs = [full(gb.shape, jnp.bfloat16), line, line, line, full((16, 128), jnp.float32)]
    if streams:
        square, broad = full((per, width), jnp.float32), full((per, ff), jnp.float32)
        outs += [square] * 4 + [broad] * 2 + [full((streams[2].shape[0], width), jnp.float32)]
    return pl.pallas_call(
        functools.partial(finish_kernel, shards, heads_all),
        out_shape=tuple(outs),
        in_specs=[VMEM_SPEC] * (4 + len(streams)),
        out_specs=(VMEM_SPEC,) * len(outs),
        compiler_params=pltpu.CompilerParams(vmem_limit_bytes=VMEM_BYTES),
        name="finish",
    )(gb, edge, spill, small, *streams)


class NearRows:
    def __init__(self, grid, first):
        self.grid, self.first, self.shape = grid, first, grid.shape

    def __getitem__(self, index):
        h, rows = index
        return self.grid[h, pl.ds(pl.multiple_of(self.first + rows.start, 32), rows.size)]


class Refs:
    def __init__(self, names, refs):
        for name, ref in zip(names, refs, strict=True):
            setattr(self, name, ref)


wide = lambda value: value.astype(jnp.float32)
slim = lambda value: value.astype(jnp.bfloat16)


class DenseBack:
    def __init__(self, place, r):
        self.place, self.r = place, r
        self.heads = r.lse.shape[2]
        self.tokens = TQ
        self.across, self.core_to, self.row_to = place.other_rest(2), place.other_rest(1), place.other_row()
        self.y, self.core = bit(place.rest, 2), place.rest % 2
        self.s_core = remote(r.dkvs_hbm.at[:, :, 1 - self.core], r.s_in, r.s_send, r.s_recv, self.core_to)
        self.own_rows = pltpu.make_async_copy(r.dkvs_hbm.at[:, :, self.core], r.dkvs, r.own_sem)
        self.near_rows = pltpu.make_async_copy(r.nears_hbm, r.nears, r.near_sem)

    def group_of(self, n):
        return (self.place.group + 1 + n) % GROUPS

    def tile_start(self, m):
        place_y = jnp.where(m % 2 == 0, 1 - self.y, self.y)
        return pl.multiple_of((self.group_of(m // 2) * 2 + place_y) * TK, TK)

    def fetch(self, m):
        r = self.r
        return pltpu.make_async_copy(r.kv_hbm.at[:, pl.ds(self.tile_start(m), TK)], r.kv.at[m % 4], r.kv_sem.at[m % 4])

    def prepare(self):
        r = self.r
        for m in range(4):
            self.fetch(m).start()
        self.own_rows.start()
        self.near_rows.start()
        self.dense = r.bounds[0, 0, 6]
        self.mine_dense = self.dense == self.place.row
        for i in range(2):
            for h, tile in enumerate(spread_lanes(r.q[self.dense, i], False)):
                r.qp[i, h] = tile
            for h, tile in enumerate(spread_lanes(r.do[self.dense, i], True)):
                r.dp[i, h] = tile
        r.dqt[...] = jnp.zeros_like(r.dqt)
        r.grid[...] = jnp.zeros_like(r.grid)

    def core_copy(self, n, j):
        r = self.r
        return remote(r.held.at[n, j, 1 - self.core], r.core_in.at[n, j], r.core_send.at[n, j], r.core_recv.at[n, j], self.core_to)

    def x_copy(self, n, j):
        r = self.r
        return remote(r.x_out.at[n, j], r.x_in.at[n, j], r.x_send.at[n, j], r.x_recv.at[n, j], self.row_to)

    def y_copy(self, n, j):
        r = self.r
        return remote(r.y_out.at[n, j], r.y_in.at[n, j], r.y_send.at[n, j], r.y_recv.at[n, j], self.across)

    def z_copy(self, n):
        r, place = self.r, self.place
        return remote(r.z_out.at[n], r.dkv_home.at[place.group], r.z_send.at[n], r.z_recv.at[n], place.at(place.row, self.group_of(n), place.rest))

    def by_rows(self, one):
        def step(k, _):
            one(pl.ds(pl.multiple_of(k * 32, 32), 32))
            return 0
        lax.fori_loop(0, self.tokens // 32, step, 0)

    def own_sum(self, n, j, rows):
        return wide(self.r.held[n, j, self.core, rows]) + wide(self.r.core_in[n, j, rows])

    def split_rows(self, one, two):
        return slim(jnp.where(self.mine_dense, two, one)), slim(jnp.where(self.mine_dense, one, two))

    def other_sums(self):
        r = self.r
        self.s_core.wait()
        self.own_rows.wait()

        def one(step, _):
            n, far = step // 2, step % 2
            row = jnp.where(far == 0, 1 - self.y, self.y)
            group = self.group_of(n)

            def some(rows):
                r.s_in[group, row, rows] = slim(wide(r.dkvs[group, row, rows]) + wide(r.s_in[group, row, rows]))

            self.by_rows(some)
            pl.when(jnp.logical_and(far == 0, n % 2 == 0))(self.y_other(n).start)
            return 0

        lax.fori_loop(0, 2 * GROUPS, one, 0)

    def other(self, n, j):
        return self.r.s_in.at[self.group_of(n), 1 - self.y if j == 0 else self.y]

    def y_other(self, n):
        r = self.r
        return remote(self.other(n, 0), r.y_in.at[n, 1], r.y_send.at[n, 1], r.y_recv.at[n, 1], self.across)

    def y_first_1(self, n):
        r = self.r
        self.core_copy(n, 0).wait()

        def one(rows):
            r.y_out[n, 0, rows] = slim(self.own_sum(n, 0, rows))

        self.by_rows(one)
        self.y_copy(n, 0).start()

    def y_first_3(self, n):
        r = self.r
        self.core_copy(n, 1).wait()
        self.y_other(n).wait()
        self.y_copy(n, 0).wait()

        def one(rows):
            first = self.own_sum(n, 1, rows) + wide(r.y_in[n, 0, rows])
            second = wide(self.other(n, 1)[rows]) + wide(r.y_in[n, 1, rows])
            r.x_out[n, 0, rows], r.kept[n, 0, rows] = self.split_rows(first, second)

        self.by_rows(one)
        self.x_copy(n, 0).start()

    def y_first_5(self, n):
        r = self.r
        self.x_copy(n, 0).wait()

        def one(rows):
            r.z_out[n, rows] = slim(wide(r.kept[n, 0, rows]) + wide(r.x_in[n, 0, rows]))

        self.by_rows(one)
        self.z_copy(n).start()

    def x_first_1(self, n, j=0):
        r = self.r
        self.core_copy(n, j).wait()

        def one(rows):
            r.x_out[n, j, rows], r.kept[n, j, rows] = self.split_rows(self.own_sum(n, j, rows), wide(self.other(n, j)[rows]))

        self.by_rows(one)
        self.x_copy(n, j).start()

    def x_first_2(self, n):
        self.x_first_1(n, 1)

    def x_first_3(self, n):
        r = self.r
        self.x_copy(n, 0).wait()

        def one(rows):
            r.y_out[n, 0, rows] = slim(wide(r.kept[n, 0, rows]) + wide(r.x_in[n, 0, rows]))

        self.by_rows(one)
        self.y_copy(n, 0).start()

    def x_first_5(self, n):
        r = self.r
        self.x_copy(n, 1).wait()
        self.y_copy(n, 0).wait()

        def one(rows):
            total = slim(wide(r.kept[n, 1, rows]) + wide(r.x_in[n, 1, rows]) + wide(r.y_in[n, 0, rows]))
            if n == GROUPS - 1:
                r.dkv_home[self.place.group, rows] = total
            else:
                r.z_out[n, rows] = total

        self.by_rows(one)
        if n < GROUPS - 1:
            self.z_copy(n).start()

    def tile(self, m):
        r, place, heads = self.r, self.place, self.heads
        n, j = m // 2, m % 2
        t = self.tile_start(m) // TK
        self.fetch(m).wait()
        r.acc[...] = jnp.zeros_like(r.acc)
        r.keys[...] = jnp.where(self.dense == 0, r.kv[m % 4, 0], r.kv[m % 4, 1])
        keys = lambda h: r.keys[:, h * 128 : h * 128 + 128]
        for h in range(heads):
            r.kt[h, 0:64] = keys(h).T[0:64]
            r.kt[h, 64:80] = jnp.ones((16, TK), jnp.bfloat16)

        def part(i, _):
            first = ((2 * place.row + i) * place.rest_size + place.rest) * self.tokens
            slot = jnp.clip(t - (first // TK - 1 + self.core) + 1, 0, 3)
            away = jnp.logical_or(slot == 0, slot == 3)

            def finish(h, p, ds, where):
                ds_low = ds.astype(jnp.bfloat16)
                two = jnp.concatenate([ds_low, p.astype(jnp.bfloat16)], axis=1)
                both = jnp.concatenate([r.qp[i, h], r.dp[i, h]], axis=0)
                r.acc[:, h * 128 : h * 128 + 128] += mxu(two, both)
                r.dqt[i, h, where] += mxu(r.kt[h], ds_low)

            def products(h):
                return mxu(keys(h), r.qp[i, h], NT), mxu(keys(h), r.dp[i, h], NT)

            @pl.when(away)
            def _():
                for h in range(heads):
                    s, d_probs = products(h)
                    p = jnp.exp(s - (r.lse[self.dense, i, h] - jnp.where(slot == 0, r.table[h, 15], r.table[h, 31])))
                    finish(h, p, p * (d_probs - r.delta[self.dense, i, h]), jnp.where(slot == 0, 0, 2))

            @pl.when(jnp.logical_not(away))
            def _():
                for h in range(heads):
                    s, d_probs = products(h)
                    p = jnp.exp(s + r.bias[h, slot - 1].astype(jnp.float32) - r.lse[self.dense, i, h])
                    ds = p * (d_probs - r.delta[self.dense, i, h])
                    r.grid[h, pl.ds(pl.multiple_of((slot - 1) * TK, TK), TK)] += ds
                    finish(h, p, ds, 1)

            return 0

        lax.fori_loop(0, 2, part, 0)
        for half in range(2):
            r.held[n, j, half] = r.acc[half * self.tokens : half * self.tokens + self.tokens].astype(jnp.bfloat16)
        self.core_copy(n, j).start()
        pl.when(m < 4)(lambda: self.fetch(m + 4).start())

    def queries(self):
        r = self.r
        for i in range(2):
            parts = []
            for h in range(self.heads):
                parts.append((r.dqt[i, h, 0, 0:64] + r.dqt[i, h, 1, 0:64] + r.dqt[i, h, 2, 0:64]).T * 0.125)
            mine = join_heads(parts)
            other = r.dqs[0, i].astype(jnp.float32)
            for row in range(2):
                r.dq_rows[row, i] = jnp.where(self.dense == row, mine, other).astype(jnp.bfloat16)

    def buckets(self):
        r = self.r
        self.near_rows.wait()
        first = near_start(self.core)
        for h in range(self.heads):
            r.side[h, 0:1] = r.dqt[0, h, 0, 64:65] + r.dqt[1, h, 0, 64:65] + r.sides[h, 0:1] + far_sums(r.grid, h, 0, first)
            r.side[h, 1:2] = r.dqt[0, h, 2, 64:65] + r.dqt[1, h, 2, 64:65] + r.sides[h, 1:2] + far_sums(r.grid, h, first + NEAR_ROWS, 2 * TK)
            rows = pl.ds(pl.multiple_of(first, 32), NEAR_ROWS)
            r.grid[h, rows] += r.nears[h]
        bucket_sums(self.core, NearRows(r.grid, first), r.side, r.tab, r.tab8)

    def wait_home(self):
        r, place = self.r, self.place
        for n in range(GROUPS - 1):
            there = r.dkv_home.at[(place.group - 1 - n + GROUPS) % GROUPS]
            remote(r.z_out.at[n], there, r.z_send.at[n], r.z_recv.at[n], self.row_to).wait()


def back_kernel(shards, axes, names, plans, *refs):
    r = Refs(names, refs)
    place = Place(shards)
    at = {"dp": place.dp, "blk": place.blk}
    tokens, width = r.hidden.shape
    back = DenseBack(place, r)
    streams = []
    for s, (kept, order) in enumerate(plans):
        bufs = [getattr(r, "buf%d_%d" % (s, k)) for k in range(len(order))]
        streams.append(Stream(axes, at, kept, order, getattr(r, "src%d" % s), bufs, getattr(r, "sum%d" % s), r.w_send.at[s], r.w_recv.at[s]))
    early, late = streams[:3], streams[3:]
    whole = Whole(axes, at, (4, 0, 3, 2, 1), r.small, r.small_bufs, r.small_out, r.w_send.at[len(plans)], r.w_recv.at[len(plans)])
    left, right = (place.dp, (place.blk + shards - 1) % shards), (place.dp, (place.blk + 1) % shards)

    met = hail(line_and_row(place) + [back.across, back.core_to, left, right])
    fetches = [pltpu.make_async_copy(getattr(r, "came%d_hbm" % s), early[s].src, r.came_sem.at[s]) for s in range(3)]
    for copy in fetches:
        copy.start()
    back.prepare()
    for s in range(3):
        fetches[s].wait()
        add_two(early[s].src, early[s].src, getattr(r, "keep%d" % s))
    await_all(met)
    back.s_core.start()
    for stream in early:
        stream.copy(0).start()

    def step(m, _):
        back.tile(m)
        pl.when(m == 0)(back.other_sums)
        for when, n, action in (
            (1, 0, back.y_first_1), (3, 1, back.x_first_1), (4, 1, back.x_first_2), (5, 2, back.y_first_1),
            (6, 0, back.y_first_3), (6, 1, back.x_first_3), (7, 3, back.x_first_1),
        ):
            pl.when(m == when)(functools.partial(action, n))
        return 0

    lax.fori_loop(0, 2 * GROUPS, step, 0)
    back.x_first_2(3)
    back.queries()
    return_heads(place, r.dq_rows, r.dq_home, r.q_send, r.q_recv)
    for stream in early:
        advance(stream, 0)
    back.y_first_5(0)
    back.x_first_3(3)
    back.x_first_5(1)
    back.y_first_3(2)
    back.buckets()
    for stream in early:
        advance(stream, 1)
    back.y_first_5(2)
    back.x_first_5(3)
    load_bytes(r.x, r.before, r.after, r.xs)
    n1_t = r.n1[...].T
    return_heads_wait(place, r.dq_rows, r.dq_home, r.q_send, r.q_recv)
    dq = get_packed(r.dq_home)
    devices = 1 << len(axes)
    per = width // devices
    half = width // 2

    def weights(stream, part):
        r.total[...] = mxu(n1_t, part)

        def block(d, _):
            rows = pl.ds(pl.multiple_of(d * per, 8), per)
            index, rest = [], d
            for _ in axes:
                index.append(rest % 2)
                rest = rest // 2
            part = r.total[rows, :]
            stream.src[tuple(reversed(index))] = jnp.concatenate([part[:, :half], part[:, half:]], axis=0).astype(jnp.bfloat16)
            return 0

        lax.fori_loop(0, devices, block, 0)
        stream.copy(0).start()

    weights(late[0], dq)
    back.wait_home()
    dk, dv = unpack_pairs(r.dkv_home, width)
    weights(late[1], dk)
    weights(late[2], dv)
    d_n1 = mxu(dq, r.wq[...], NT) + mxu(dk, r.wk[...], NT) + mxu(dv, r.wv[...], NT)
    d_rows, d_gain1 = norm_back(d_n1, r.hidden[...], r.gain[...].astype(jnp.float32))
    d_hidden = r.dres[...] + d_rows
    for stream in late:
        advance(stream, 0)
    for stream in early:
        advance(stream, 2)
    d_score = pool_back(d_hidden, (r.x, r.before, r.after), r.labels, r.y, r.score, r.gb, r.edge, r.spill, r.xs, r.gbuf)
    put_small(r.small, (d_score, d_gain1, r.dgain2[...]), r.tab, r.share)
    whole.copy(0).start()
    spills = [
        remote(r.spill.at[0], r.spill_out.at[1], r.s2_send.at[0], r.s2_recv.at[1], left),
        remote(r.spill.at[1], r.spill_out.at[0], r.s2_send.at[1], r.s2_recv.at[0], right),
    ]
    for copy in spills:
        copy.start()
    for stage in range(1, len(axes)):
        for stream in late:
            advance(stream, stage)
        advance(whole, stage - 1)
    advance(whole, len(axes) - 1)
    for copy in spills:
        copy.wait()


def back_and_last(shape, halves, inputs):
    shards = shape["blk"]
    axes = bit_axes(shape)
    ndim = len(axes)
    named = dict(inputs)
    kv, q, hidden = named["kv_hbm"], named["q"], named["hidden"]
    heads, n, width = kv.shape[2] // 128, kv.shape[1], kv.shape[2]
    tokens, features = hidden.shape
    length = named["x"].shape[0]
    f32, low, sem = jnp.float32, jnp.bfloat16, pltpu.SemaphoreType.DMA
    chunk = (tokens, width)
    every = (0, 1, 2, 3, 4)
    plans = [
        ((1, 2, 3), (3, 2, 1)), ((0, 1, 2), (2, 0, 1)), ((0, 1, 3), (0, 3, 1)),
        (every, (4, 0, 3, 2, 1)), (every, (4, 3, 2, 0, 1)), (every, (4, 2, 0, 3, 1)),
    ]
    own = (2 * (features // (1 << ndim)), features // 2)
    blocks = [h.shape[-2:] for h in halves[::2]] + [own] * 3
    ins = list(inputs)
    for s in range(3):
        for k, kind in enumerate(("keep%d", "came%d_hbm")):
            part = halves[2 * s + k]
            ins.append((kind % s, part.reshape((2, 2, 2) + part.shape[-2:])))
    spec_of = lambda name: pl.BlockSpec(memory_space=pl.ANY) if name.endswith("_hbm") else SMEM_SPEC if name in ("bounds", "table") else VMEM_SPEC
    outs = [
        ("gb", (length, features), low), ("edge", (2, 16, features), f32), ("spill_out", (2, LEAD, features), f32),
        ("small_out", (32, 128), f32),
    ] + [("sum%d" % s, block, f32) for s, block in enumerate(blocks)]
    mem = lambda shape, dtype=low: pltpu.VMEM(shape, dtype)
    pairs, fours = sem((GROUPS, 2)), sem((GROUPS,))
    strip = mem((features // 128, length + 2 * LEAD, 128), f32)
    scratch = [
        ("kt", mem((heads, 80, TK))), ("dqt", mem((2, heads, 3, 80, TQ), f32)), ("acc", mem((TK, width), f32)),
        ("grid", mem((heads, 2 * TK, TQ), f32)), ("side", mem((heads, 2, TQ), f32)), ("tab8", mem((heads, BUCKETS, 8, TQ), f32)),
        ("tab", mem((heads, BUCKETS, TQ), f32)),
        ("qp", mem((2, heads, TQ, 128))), ("dp", mem((2, heads, TQ, 128))),
        ("kv", mem((4, 2, TK, width))), ("keys", mem((TK, width))), ("dkvs", mem((GROUPS, 2) + chunk)), ("nears", mem((heads, NEAR_ROWS, TQ), f32)),
        ("held", mem((GROUPS, 2, 2) + chunk)), ("core_in", mem((GROUPS, 2) + chunk)), ("s_in", mem((GROUPS, 2) + chunk)),
        ("x_out", mem((GROUPS, 2) + chunk)), ("x_in", mem((GROUPS, 2) + chunk)),
        ("y_out", mem((GROUPS, 1) + chunk)), ("y_in", mem((GROUPS, 2) + chunk)), ("kept", mem((GROUPS, 2) + chunk)),
        ("z_out", mem((GROUPS,) + chunk)), ("dkv_home", mem((GROUPS,) + chunk)),
        ("dq_rows", mem((2, 2) + q.shape[2:])), ("dq_home", mem((GROUPS,) + q.shape[2:])),
        ("core_send", pairs), ("core_recv", pairs), ("x_send", pairs), ("x_recv", pairs), ("y_send", pairs), ("y_recv", pairs),
        ("z_send", fours), ("z_recv", fours), ("s_send", sem), ("s_recv", sem), ("q_send", fours), ("q_recv", fours),
        ("kv_sem", fours), ("came_sem", sem((3,))), ("own_sem", sem), ("near_sem", sem),
        ("w_send", sem((len(plans) + 1, ndim))), ("w_recv", sem((len(plans) + 1, ndim))), ("s2_send", sem((2,))), ("s2_recv", sem((2,))),
        ("xs", strip), ("gbuf", strip), ("spill", mem((2, LEAD, features), f32)), ("small", mem((32, 128), f32)),
        ("small_bufs", mem((2, ndim, 32, 128), f32)), ("total", mem((features, features), f32)),
    ]
    for s, ((kept, order), block) in enumerate(zip(plans, blocks)):
        scratch.append(("src%d" % s, mem((2,) * len(kept) + block)))
        for k, buf in enumerate(stream_scratch(len(kept), order, *block)):
            scratch.append(("buf%d_%d" % (s, k), buf))
    names = [name for name, _ in ins] + [name for name, _, _ in outs] + [name for name, _ in scratch]
    return pl.pallas_call(
        functools.partial(back_kernel, shards, axes, names, plans),
        out_shape=tuple(jax.ShapeDtypeStruct(shape, dtype) for _, shape, dtype in outs),
        in_specs=[spec_of(name) for name, _ in ins],
        out_specs=(VMEM_SPEC,) * len(outs),
        scratch_shapes=[kind for _, kind in scratch],
        compiler_params=pltpu.CompilerParams(collective_id=6, has_side_effects=True, vmem_limit_bytes=VMEM_BYTES),
        name="back_and_last",
    )(*[array for _, array in ins])


def neighbours(rows):
    peers = lax.axis_size("blk")
    up = [(i, i + 1) for i in range(peers - 1)]
    last, leading = rows
    return lax.ppermute(last, "blk", up), lax.ppermute(leading, "blk", [(j, i) for i, j in up])


def body(
    byte_embeds,
    segments,
    score_weight,
    norm_gain1,
    w_query,
    w_key,
    w_value,
    w_out,
    rel_bias,
    norm_gain2,
    w_gate,
    w_up,
    w_down,
    cotangent,
):
    row_count, length, width = byte_embeds.shape
    tokens = length // 2
    shards = lax.axis_size("blk")
    shape = {"dp": lax.axis_size("dp"), "blk": shards}
    devices = shards * shape["dp"]
    heads = rel_bias.shape[1] // GROUPS
    position = lax.axis_index("blk")
    rest_size = shards // GROUPS
    group, rest = position // rest_size, position % rest_size
    row = lax.axis_index("dp") % 2
    x, ids_here = byte_embeds[0], segments[0]

    marks = (ids_here + 1).astype(jnp.bfloat16)
    with_marks = lambda part, two: jnp.concatenate([part, jnp.pad(two, (0, width - 2))[None]], axis=0)
    before, after = neighbours((with_marks(x[-2:], marks[-2:]), with_marks(x[:2], marks[:2])))
    line = jnp.concatenate([before[2, :2], marks, after[2, :2]])
    line = jnp.pad(line, (1, 1)).astype(jnp.int32).reshape(tokens + 3, 2).T
    labels = jnp.stack([line[j % 2, j // 2 : j // 2 + tokens] for j in range(8)])

    score_row, gain1, gain2 = score_weight[None], norm_gain1[None], norm_gain2[None]
    hidden, n1, y, share, q_packed, kv_parts = pool_and_project(
        shards, 1.0 / (row_count * length * devices), x, before, after, labels, score_row, gain1, w_query, w_key, w_value
    )

    label_block = jnp.pad(ids_here[0::2].reshape(tokens // 128, 128), ((0, 8 - tokens // 128), (0, 0)))
    q_all, kv_all, labels_all = gather_all(shards, q_packed, kv_parts, label_block)
    labels_all = labels_all.reshape(2, shards, 8, 128)[:, :, : tokens // 128].reshape(2, shards * tokens)
    ids = jnp.arange(8, dtype=jnp.int32)
    counts = jnp.sum((labels_all[:, None, :] == ids[None, :, None]).astype(jnp.int32), axis=2)
    ends = jnp.sum(jnp.where(ids[None, :] <= ids[:, None], counts[:, None, :], 0), axis=2)
    begins = ends - counts
    query_labels = jnp.stack(
        [lax.dynamic_slice_in_dim(labels_all, ((2 * row + i) * rest_size + rest) * tokens, tokens, 1) for i in range(2)],
        axis=1,
    )
    chosen = query_labels[:, :, None, :] == ids[None, None, :, None]
    span = jnp.stack(
        [jnp.sum(jnp.where(chosen, edge[:, None, :, None], 0), axis=2) for edge in (begins, ends)], axis=2
    )
    parity = rest % 2
    firsts = jnp.stack([((2 * row + i) * rest_size + rest) * tokens for i in range(2)])
    near = jnp.broadcast_to((firsts // TK - 1 + parity)[None], (2, 2))
    bounds = jnp.stack(
        [
            jnp.min(span[:, :, 0], axis=-1) // TK,
            -(-jnp.max(span[:, :, 1], axis=-1) // TK),
            near,
            -(-jnp.max(span[:, :, 0], axis=-1) // TK),
            jnp.min(span[:, :, 1], axis=-1) // TK,
            jnp.broadcast_to(parity, (2, 2)),
            jnp.broadcast_to((labels_all[0, -1] > 0).astype(jnp.int32), (2, 2)),
        ],
        axis=-1,
    ).astype(jnp.int32)
    table = lax.dynamic_slice_in_dim(rel_bias.astype(jnp.float32).T, group * heads, heads, 0)

    o_packed, o_kept, log_total, bias_tiles, near_bias = attention(bounds, table, q_all, kv_all, span)
    o_home = move_heads(return_kernel, (GROUPS,), shards, 4, o_packed)
    ct = cotangent[0]
    block_out, d_res, da_packed, d_gain2, n2, att, act, d_gate, d_up, d_branch = feed_forward(
        o_home, hidden, ct, gain2, w_out, w_gate, w_up, w_down
    )

    if devices == 32:
        do_all, keep_a, send_a, keep_b, send_b, keep_c, send_c = spread_and_weights(
            shards, da_packed, n2, att, act, d_gate, d_up, ct, d_branch
        )
        swap = lambda part, axis, mask: lax.ppermute(part, axis, [(i, i ^ mask) for i in range(lax.axis_size(axis))])
        halves = [keep_a, swap(send_a, "dp", 1), keep_b, swap(send_b, "blk", 2), keep_c, swap(send_c, "blk", 4)]
        dq_other, dkv_other, near_other, side_other, deltas = attention_back(
            True, bounds, table, q_all, do_all, o_kept, kv_all, bias_tiles, span, log_total
        )
        grad_bytes, edge, spill, small, *sums = back_and_last(
            shape,
            halves,
            (
                ("bounds", bounds), ("table", table), ("q", q_all), ("do", do_all), ("delta", deltas), ("kv_hbm", kv_all),
                ("bias", near_bias), ("lse", log_total), ("dqs", dq_other),
                ("dkvs_hbm", dkv_other.reshape((GROUPS, 2, 2) + kv_parts.shape[1:])), ("nears_hbm", near_other), ("sides", side_other),
                ("hidden", hidden), ("dres", d_res), ("n1", n1), ("x", x), ("before", before), ("after", after),
                ("labels", labels), ("y", y), ("score", score_row), ("gain", gain1), ("wq", w_query), ("wk", w_key),
                ("wv", w_value), ("dgain2", d_gain2), ("share", share),
            ),
        )
    else:
        do_all = move_heads(spread_kernel, (2, 2), shards, 5, da_packed)
        dq_packed, dkv_all, _, _, _, d_table_lanes = attention_back(
            False, bounds, table, q_all, do_all, o_kept, kv_all, bias_tiles, span, log_total
        )
        dq_home, dkv_home = reduce_all(shape, dq_packed, dkv_all, [], [])
        grad_bytes, edge, spill, small, last_parts = last_part(
            shape, dq_home, dkv_home, hidden, d_res, x, before, after, labels, y,
            score_row, gain1, w_query, w_key, w_value, d_gain2, share, d_table_lanes,
        )
        sums = []
    per = width // devices
    grad_bytes, g_score, g_gain1, g_gain2, rows, *grads = finish(
        shards, rel_bias.shape[1], per, w_gate.shape[1], grad_bytes, edge, spill, small, sums
    )
    if devices != 32:
        product = lambda left, right: jnp.einsum("td,te->de", left, right, preferred_element_type=jnp.float32)
        grads = [product(n1, last_parts[j]) for j in range(3)]
        grads += [product(att, d_branch), product(n2, d_gate), product(n2, d_up), product(act, ct)]
        grads = [lax.psum_scatter(grad, ("dp", "blk"), scatter_dimension=0, tiled=True) for grad in grads]
    return (
        block_out[None],
        grad_bytes[None],
        g_score,
        g_gain1,
        *grads[:4],
        rows[2 : 2 + rel_bias.shape[1], :BUCKETS].T,
        g_gain2,
        *grads[4:],
        rows[14, :MAX_BLOCK],
    )


def solution(mesh):
    placed = (
        P("dp", "blk", None),
        P("dp", "blk"),
        P(),
        P(),
        P(),
        P(),
        P(),
        P(),
        P(),
        P(),
        P(),
        P(),
        P(),
        P("dp", "blk", None),
    )
    return jax.shard_map(
        body,
        mesh=mesh,
        in_specs=placed,
        out_specs=(
            P("dp", "blk", None),
            P("dp", "blk", None),
            P(),
            P(),
            P(("dp", "blk"), None),
            P(("dp", "blk"), None),
            P(("dp", "blk"), None),
            P(("dp", "blk"), None),
            P(),
            P(),
            P(("dp", "blk"), None),
            P(("dp", "blk"), None),
            P(("dp", "blk"), None),
            P(),
        ),
        check_vma=False,
    )
```

```python
import functools
import math

import jax
import jax.numpy as jnp
from jax import lax
from jax.experimental import pallas as pl
from jax.experimental.pallas import tpu as pltpu
from jax.sharding import PartitionSpec as P

BUCKETS = 32
MAX_BLOCK = 4
VMEM_BYTES = 61 * 2**20


def buckets_of(relative):
    distance = jnp.abs(relative)
    beyond = jnp.zeros_like(distance)
    for border in (12, 16, 23, 32, 46, 64, 91):
        beyond = beyond + (distance >= border).astype(jnp.int32)
    nearer = jnp.where(distance < 8, distance, 8 + beyond)
    return nearer + BUCKETS // 2 * (relative > 0).astype(jnp.int32)


MESH_ID = pl.DeviceIdType.MESH
GROUPS = 4


def bits_of(size):
    return [1 << p for p in reversed(range(size.bit_length() - 1))]


def bit(value, mask):
    return (value // mask) % 2


def flipped(value, mask):
    return value + mask * (1 - 2 * bit(value, mask))


class Place:
    def __init__(self, shards):
        self.shards = shards
        self.rest_size = shards // GROUPS
        self.dp = lax.axis_index("dp")
        self.blk = lax.axis_index("blk")
        self.row = self.dp % 2
        self.group = self.blk // self.rest_size
        self.rest = self.blk % self.rest_size

    def at(self, row, group, rest):
        return (self.dp - self.row + row, group * self.rest_size + rest)

    def chunk(self, group, rest):
        return group * self.rest_size + rest

    def other_row(self):
        return self.at(1 - self.row, self.group, self.rest)

    def other_rest(self, mask):
        return self.at(self.row, self.group, flipped(self.rest, mask))

    def other_group(self, step):
        return self.at(self.row, (self.group + step) % GROUPS, self.rest)


def hail(targets):
    barrier = pltpu.get_barrier_semaphore()
    for target in targets:
        pl.semaphore_signal(barrier, inc=1, device_id=target, device_id_type=MESH_ID)
    return len(targets)


def await_all(count):
    pl.semaphore_wait(pltpu.get_barrier_semaphore(), count)


def greet(targets):
    await_all(hail(targets))


def remote(src, dst, send_sem, recv_sem, target):
    return pltpu.make_async_remote_copy(
        src_ref=src,
        dst_ref=dst,
        send_sem=send_sem,
        recv_sem=recv_sem,
        device_id=target,
        device_id_type=MESH_ID,
    )


def line_and_row(place):
    found = []
    for step in range(GROUPS):
        for flip in range(2):
            if step or flip:
                row = 1 - place.row if flip else place.row
                found.append(place.at(row, (place.group + step) % GROUPS, place.rest))
    return found


def spread_heads(place, q_ref, out_ref, send_sem, recv_sem):
    row_to = place.group // 2
    slot = place.group % 2
    dst = out_ref.at[place.row, slot]
    mine = recv_sem.at[place.row * 2 + slot]
    at_home = row_to == place.row
    for step in range(GROUPS):
        group = (place.group + step) % GROUPS
        src = q_ref.at[group]
        copy = remote(src, dst, send_sem.at[step], mine, place.at(row_to, group, place.rest))
        if step:
            copy.start()
        else:
            pl.when(jnp.logical_not(at_home))(copy.start)
            pl.when(at_home)(pltpu.make_async_copy(src, dst, mine).start)


def spread_heads_come(q_ref, out_ref, recv_sem):
    for row in range(2):
        for slot in range(2):
            pltpu.make_async_copy(q_ref.at[0], out_ref.at[row, slot], recv_sem.at[row * 2 + slot]).wait()


def spread_heads_gone(place, q_ref, out_ref, send_sem, recv_sem):
    at_home = place.group // 2 == place.row
    for step in range(GROUPS):
        copy = remote(q_ref.at[0], out_ref.at[0, 0], send_sem.at[step], recv_sem.at[0], place.other_row())
        if step:
            copy.wait_send()
        else:
            pl.when(jnp.logical_not(at_home))(copy.wait_send)


def spread_heads_wait(place, q_ref, out_ref, send_sem, recv_sem):
    spread_heads_come(q_ref, out_ref, recv_sem)
    spread_heads_gone(place, q_ref, out_ref, send_sem, recv_sem)


def return_heads(place, o_ref, out_ref, send_sem, recv_sem):
    for row in range(2):
        for slot in range(2):
            group = place.row * 2 + slot
            src = o_ref.at[row, slot]
            dst = out_ref.at[place.group]
            mine = recv_sem.at[place.group]
            at_home = jnp.logical_and(place.row == row, place.group == group)
            copy = remote(src, dst, send_sem.at[row * 2 + slot], mine, place.at(row, group, place.rest))
            pl.when(jnp.logical_not(at_home))(copy.start)
            pl.when(at_home)(pltpu.make_async_copy(src, dst, mine).start)


def return_heads_wait(place, o_ref, out_ref, send_sem, recv_sem):
    for group in range(GROUPS):
        pltpu.make_async_copy(o_ref.at[0, 0], out_ref.at[group], recv_sem.at[group]).wait()
    for row in range(2):
        for slot in range(2):
            group = place.row * 2 + slot
            at_home = jnp.logical_and(place.row == row, place.group == group)
            copy = remote(o_ref.at[0, 0], out_ref.at[0], send_sem.at[row * 2 + slot], recv_sem.at[0], place.other_row())
            pl.when(jnp.logical_not(at_home))(copy.wait_send)


def spread_kernel(shards, q_ref, out_ref, send_sem, recv_sem):
    place = Place(shards)
    greet(line_and_row(place))
    spread_heads(place, q_ref, out_ref, send_sem, recv_sem)
    spread_heads_wait(place, q_ref, out_ref, send_sem, recv_sem)


def return_kernel(shards, o_ref, out_ref, send_sem, recv_sem):
    place = Place(shards)
    greet(line_and_row(place))
    return_heads(place, o_ref, out_ref, send_sem, recv_sem)
    return_heads_wait(place, o_ref, out_ref, send_sem, recv_sem)


SMEM_SPEC = pl.BlockSpec(memory_space=pltpu.SMEM)
VMEM_SPEC = pl.BlockSpec(memory_space=pltpu.VMEM)
ANY_SPEC = pl.BlockSpec(memory_space=pl.ANY)


def move_heads(kernel, lead, shards, ident, packed):
    rows, lanes = packed.shape[-2:]
    return pl.pallas_call(
        functools.partial(kernel, shards),
        out_shape=jax.ShapeDtypeStruct(lead + (rows, lanes), packed.dtype),
        in_specs=[pl.BlockSpec(memory_space=pltpu.VMEM)],
        out_specs=pl.BlockSpec(memory_space=pltpu.VMEM),
        scratch_shapes=[pltpu.SemaphoreType.DMA((4,)), pltpu.SemaphoreType.DMA((4,))],
        compiler_params=pltpu.CompilerParams(collective_id=ident, has_side_effects=True, vmem_limit_bytes=VMEM_BYTES),
        name="move_heads_%d" % ident,
    )(packed)


def gather_kernel(shards, q_ref, kv_ref, label_ref, qo_ref, kvo_ref, labo_ref, q_send, q_recv, z_send, far_send, core_send, kv_recv, own_sem, lab_send, lab_recv):
    place = Place(shards)
    tokens = kv_ref.shape[1]
    rest_bits = bits_of(place.rest_size)
    core, far = rest_bits[-1], ["row"] + rest_bits[:-1]
    greet(line_and_row(place) + [place.other_rest(mask) for mask in rest_bits])

    dims = [("row", 1)] + [("blk", m) for m in bits_of(shards)]
    lab_index = [place.row] + [bit(place.blk, m) for _, m in dims[1:]]
    lab_order = list(range(len(dims)))

    def lab_copy(stage):
        index = tuple(slice(None) if p in lab_order[:stage] else lab_index[p] for p in range(len(dims)))
        axis, mask = dims[lab_order[stage]]
        target = place.other_row() if axis == "row" else (place.dp, flipped(place.blk, mask))
        there = labo_ref.at[index]
        return remote(there, there, lab_send.at[stage], lab_recv.at[stage], target)

    labo_ref[tuple(lab_index)] = label_ref[...]
    lab_copy(0).start()
    lab_stage = 0

    def slot(row, group, rest):
        start = pl.multiple_of(place.chunk(group, rest) * tokens, tokens)
        return kvo_ref.at[row, pl.ds(start, tokens)]

    def held(dz, offset, core_off):
        row = 1 - place.row if offset & 1 else place.row
        rest = place.rest
        for p, mask in enumerate(far[1:]):
            if offset >> (p + 1) & 1:
                rest = flipped(rest, mask)
        if core_off:
            rest = flipped(rest, core)
        return slot(row, (place.group + dz) % GROUPS, rest)

    count = 1 << len(far)

    def sem_of(dz, offset, core_off):
        return kv_recv.at[(core_off * count + offset) * GROUPS + dz]

    own = pltpu.make_async_copy(kv_ref.at[place.group], held(0, 0, 0), own_sem)
    own.start()
    waits = []
    for step in (1, 3, 2):
        copy = remote(kv_ref.at[(place.group + step) % GROUPS], held(0, 0, 0), z_send.at[step], sem_of((GROUPS - step) % GROUPS, 0, 0), place.other_group(step))
        copy.start()
        waits.append(copy)

    used = 0
    events = sorted(((dz, off) for dz in range(GROUPS) for off in range(count)), key=lambda e: (bin(e[1]).count("1"), (0, 1, 3, 2).index(e[0])))
    core_target = place.other_rest(core)
    for step, (dz, off) in enumerate(events):
        if step == GROUPS:
            spread_heads(place, q_ref, qo_ref, q_send, q_recv)
        here = held(dz, off, 0)
        if dz == 0 and off == 0:
            src = kv_ref.at[place.group]
        else:
            remote(here, here, z_send.at[0], sem_of(dz, off, 0), core_target).wait_recv()
            src = here
        order = [(p + dz) % len(far) for p in range(len(far))]
        last = max([order.index(p) for p in range(len(far)) if off >> p & 1], default=-1)
        for p in order[last + 1 :]:
            target = place.other_row() if p == 0 else place.other_rest(far[p])
            copy = remote(src, here, far_send.at[used], sem_of(dz, off | 1 << p, 0), target)
            copy.start()
            waits.append(copy)
            used += 1
        copy = remote(src, here, core_send.at[off * GROUPS + dz], sem_of(dz, off, 1), core_target)
        copy.start()
        waits.append(copy)
        if lab_stage < len(dims):
            lab_copy(lab_stage).wait()
            lab_stage += 1
            if lab_stage < len(dims):
                lab_copy(lab_stage).start()
    for dz, off in events:
        here = held(dz, off, 1)
        remote(here, here, z_send.at[0], sem_of(dz, off, 1), core_target).wait_recv()
    own.wait()
    for copy in waits:
        copy.wait_send()
    spread_heads_wait(place, q_ref, qo_ref, q_send, q_recv)


def gather_all(shards, q_packed, kv_parts, labels):
    tokens, width = kv_parts.shape[1:]
    far = 1 + len(bits_of(shards // GROUPS)) - 1
    count = 1 << far
    nbits = 1 + len(bits_of(shards))
    sem = pltpu.SemaphoreType.DMA
    return pl.pallas_call(
        functools.partial(gather_kernel, shards),
        out_shape=(
            jax.ShapeDtypeStruct((2, 2) + q_packed.shape[1:], q_packed.dtype),
            jax.ShapeDtypeStruct((2, shards * tokens, width), kv_parts.dtype),
            jax.ShapeDtypeStruct((2,) * nbits + labels.shape, labels.dtype),
        ),
        in_specs=[pl.BlockSpec(memory_space=pltpu.VMEM)] * 3,
        out_specs=(pl.BlockSpec(memory_space=pltpu.VMEM),) * 3,
        scratch_shapes=[
            sem((4,)), sem((4,)), sem((GROUPS,)), sem((GROUPS * (count - 1),)), sem((GROUPS * count,)), sem((GROUPS * count * 2,)),
            sem, sem((nbits,)), sem((nbits,)),
        ],
        compiler_params=pltpu.CompilerParams(collective_id=1, has_side_effects=True, vmem_limit_bytes=VMEM_BYTES),
        name="gather_keys",
    )(q_packed, kv_parts, labels)


def add_blocks(dst_ref, src_ref, index, shape):
    lead = shape[:-2]
    total = math.prod(lead)

    def one(step, _):
        place, left = [], step
        for size in reversed(lead):
            place.append(left % size)
            left = left // size
        place = tuple(reversed(place))
        full, k = [], 0
        for entry in index:
            if entry is None:
                full.append(place[k])
                k += 1
            else:
                full.append(entry)
        mine = src_ref[tuple(full)].astype(jnp.float32)
        dst_ref[place] = (dst_ref[place].astype(jnp.float32) + mine).astype(dst_ref.dtype)
        return 0

    lax.fori_loop(0, total, one, 0)


class Stream:
    def __init__(self, axes, at, kept, order, src, bufs, out, send_sem, recv_sem):
        self.axes, self.at, self.kept, self.order = axes, at, kept, order
        self.src, self.bufs, self.out = src, bufs, out
        self.send_sem, self.recv_sem = send_sem, recv_sem

    def own(self, p):
        axis, mask = self.axes[p]
        return bit(self.at[axis], mask)

    def target(self, p):
        axis, mask = self.axes[p]
        moved = dict(self.at)
        moved[axis] = flipped(self.at[axis], mask)
        return (moved["dp"], moved["blk"])

    def stage(self, k):
        kept = [p for p in self.kept if p not in self.order[:k]]
        return kept, self.src if k == 0 else self.bufs[k - 1], self.order[k]

    def copy(self, k):
        kept, src, now = self.stage(k)
        index = tuple(1 - self.own(p) if p == now else slice(None) for p in kept)
        return remote(src.at[index], self.bufs[k], self.send_sem.at[k], self.recv_sem.at[k], self.target(now))

    def absorb(self, k):
        kept, src, now = self.stage(k)
        buf = self.bufs[k]
        if k == len(self.order) - 1 and self.out is not None:
            mine = src[self.own(now)].astype(jnp.float32)
            self.out[...] = buf[...].astype(jnp.float32) + mine
        else:
            add_blocks(buf, src, tuple(self.own(p) if p == now else None for p in kept), buf.shape)


class Whole:
    def __init__(self, axes, at, order, src, bufs, out, send_sem, recv_sem):
        self.stream = Stream(axes, at, order, order, src, bufs, out, send_sem, recv_sem)
        self.order, self.src, self.bufs, self.out = order, src, bufs, out

    def held(self, k):
        return self.src if k == 0 else self.bufs.at[1, k - 1]

    def copy(self, k):
        s = self.stream
        return remote(self.held(k), self.bufs.at[0, k], s.send_sem.at[k], s.recv_sem.at[k], s.target(self.order[k]))

    def absorb(self, k):
        total = self.held(k)[...] + self.bufs[0, k]
        if k == len(self.order) - 1:
            self.out[...] = total
        else:
            self.bufs[1, k] = total


def advance(stream, stage):
    if stage < len(stream.order):
        stream.copy(stage).wait()
        stream.absorb(stage)
        if stage < len(stream.order) - 1:
            stream.copy(stage + 1).start()


def bit_axes(shape):
    return [("dp", m) for m in bits_of(shape["dp"])] + [("blk", m) for m in bits_of(shape["blk"])]


def stream_scratch(lead, order, rows, cols):
    return [pltpu.VMEM((2,) * (lead - 1 - k) + (rows, cols), jnp.bfloat16) for k in range(len(order))]


def feed_weights(place, n2_ref, att_ref, act_ref, dg_ref, du_ref, ct_ref, db_ref,
                 keep_a, send_a, keep_b, send_b, keep_c, send_c,
                 core_send, core_recv, gate, up, down, out, wide_out, slim_out, wide_in, slim_in):
    core_target = place.other_rest(1)
    per = gate.shape[0] // 32
    per_ff = down.shape[0] // 32
    first = keep_a.shape[2]
    half = out.shape[1] // 2
    core = place.rest % 2

    n2_t = n2_ref[...].T
    step = 512
    for j in range(gate.shape[1] // step):
        cols = slice(j * step, j * step + step)
        gate[:, cols] = mxu(n2_t, dg_ref[:, cols])
        up[:, cols] = mxu(n2_t, du_ref[:, cols])
    out[...] = mxu(att_ref[...].T, db_ref[...])

    def wide_rows(block):
        rows = pl.ds(pl.multiple_of(block * per, 8), per)
        last = jnp.concatenate([out[rows, :half], out[rows, half:]], axis=0)
        return jnp.concatenate([jnp.concatenate([gate[rows, :], up[rows, :]], axis=0), last], axis=1)

    def slim_rows(block):
        return down[pl.ds(pl.multiple_of(block * per_ff, 8), per_ff), :]

    def send_wide(m, _):
        wide_out[m] = wide_rows(2 * m + 1 - core).astype(jnp.bfloat16)
        return 0

    lax.fori_loop(0, 16, send_wide, 0)
    wide_copy = remote(wide_out, wide_in, core_send.at[0], core_recv.at[0], core_target)
    wide_copy.start()
    for j in range(down.shape[0] // step):
        rows = slice(j * step, j * step + step)
        down[rows, :] = mxu(act_ref[:, rows].T, ct_ref[...])

    def send_slim(m, _):
        slim_out[m] = slim_rows(2 * m + 1 - core).astype(jnp.bfloat16)
        return 0

    lax.fori_loop(0, 16, send_slim, 0)
    slim_copy = remote(slim_out, slim_in, core_send.at[1], core_recv.at[1], core_target)
    slim_copy.start()

    def number(j, bit_at, value):
        return j // bit_at * (2 * bit_at) + value * bit_at + j % bit_at

    wide_copy.wait()
    for (keep, send), bit_at, mine, cols in (
        ((keep_a, send_a), 8, place.row, slice(0, first)),
        ((keep_b, send_b), 1, bit(place.rest, 2), slice(first, wide_out.shape[2])),
    ):
        for ref, value in ((send, 1 - mine), (keep, mine)):
            def one(j, _):
                m = number(j, bit_at, value)
                ref[j] = (wide_rows(2 * m + core)[:, cols] + wide_in[m, :, cols].astype(jnp.float32)).astype(jnp.bfloat16)
                return 0
            lax.fori_loop(0, 8, one, 0)
    slim_copy.wait()
    mine = bit(place.group, 1)
    for ref, value in ((send_c, 1 - mine), (keep_c, mine)):
        def one(j, _):
            m = number(j, 2, value)
            ref[j] = (slim_rows(2 * m + core) + slim_in[m].astype(jnp.float32)).astype(jnp.bfloat16)
            return 0
        lax.fori_loop(0, 8, one, 0)


def reduce_kernel(shards, axes, orders, *refs):
    count = len(orders)
    q_ref, kv_ref = refs[:2]
    pairs = refs[2 : 2 + 2 * count]
    qo_ref, kvo_ref = refs[2 + 2 * count : 4 + 2 * count]
    sums = refs[4 + 2 * count : 4 + 3 * count]
    q_send, q_recv, send_sem, recv_sem, z_send, z_recv, w_send, w_recv = refs[4 + 3 * count : 12 + 3 * count]
    bufs = refs[12 + 3 * count :]
    place = Place(shards)
    rest_bits = bits_of(place.rest_size)
    greet(line_and_row(place) + [place.other_rest(mask) for mask in rest_bits])
    return_heads(place, q_ref, qo_ref, q_send, q_recv)
    ndim = 1 + len(rest_bits)
    at = {"dp": place.dp, "blk": place.blk}
    streams, used = [], ndim
    for s, (kept, order) in enumerate(orders):
        src, more = bufs[used], bufs[used + 1 : used + 1 + len(order)]
        used += 1 + len(order)
        streams.append(Stream(axes, at, kept, order, src, more, sums[s], w_send.at[s], w_recv.at[s]))
    own = [place.row] + [bit(place.rest, m) for m in rest_bits]
    targets = [place.other_row()] + [place.other_rest(m) for m in rest_bits]
    state = {}

    def plan(group_step):
        far = list(range(ndim - 1))
        turn = group_step % len(far)
        return [ndim - 1] + far[turn:] + far[:turn]

    def copy_of(step, stage):
        order = plan(step)
        group = (place.group + step) % GROUPS
        done = order[:stage]
        p_now = order[stage]
        buf = bufs[stage].at[step]
        if stage == 0:
            index = (p_index(group, done, p_now))
            src = kv_ref.at[index]
        else:
            kept = [p for p in range(ndim) if p not in done]
            src = bufs[stage - 1].at[(step,) + tuple(1 - own[p] if p == p_now else slice(None) for p in kept)]
        return remote(src, buf, send_sem.at[stage, step], recv_sem.at[stage, step], targets[p_now])

    def p_index(group, done, p_now):
        index = [slice(None)] * ndim
        index[p_now] = 1 - own[p_now]
        return (index[0], group) + tuple(index[1:])

    def absorb(step, stage):
        order = plan(step)
        done, p_now = order[:stage], order[stage]
        buf = bufs[stage].at[step]
        group = (place.group + step) % GROUPS
        if stage == 0:
            index = [None] * ndim
            index[p_now] = own[p_now]
            add_blocks(buf, kv_ref, (index[0], group) + tuple(index[1:]), buf.shape)
        else:
            kept = [p for p in range(ndim) if p not in done]
            index = tuple(own[p] if p == p_now else None for p in kept)
            add_blocks(buf, bufs[stage - 1].at[step], index, buf.shape)

    steps = (2, 1, 3, 0)
    for step in steps:
        copy_of(step, 0).start()
    for s, stream in enumerate(streams):
        add_two(stream.src, pairs[2 * s], pairs[2 * s + 1])
        stream.copy(0).start()
    for stage in range(ndim):
        for step in steps:
            copy_of(step, stage).wait()
            absorb(step, stage)
            if stage < ndim - 1:
                copy_of(step, stage + 1).start()
            elif step:
                remote(bufs[stage].at[step], kvo_ref.at[place.group], z_send.at[step], z_recv.at[(GROUPS - step) % GROUPS], place.other_group(step)).start()
            else:
                kvo_ref[place.group] = bufs[stage][step]
        for stream in streams:
            if stage < len(stream.order):
                stream.copy(stage).wait()
                stream.absorb(stage)
                if stage < len(stream.order) - 1:
                    stream.copy(stage + 1).start()
    for step in (1, 3, 2):
        there = kvo_ref.at[(place.group + step) % GROUPS]
        remote(bufs[ndim - 1].at[step], there, z_send.at[step], z_recv.at[step], place.other_group(step)).wait()
    return_heads_wait(place, q_ref, qo_ref, q_send, q_recv)


def add_two(dst_ref, one_ref, two_ref):
    lead = dst_ref.shape[:-2]

    def one(step, _):
        place, left = [], step
        for size in reversed(lead):
            place.append(left % size)
            left = left // size
        place = tuple(reversed(place))
        dst_ref[place] = (one_ref[place].astype(jnp.float32) + two_ref[place].astype(jnp.float32)).astype(dst_ref.dtype)
        return 0

    lax.fori_loop(0, math.prod(lead), one, 0)


def reduce_all(shape, q_packed, kv_sums, orders, pairs):
    shards = shape["blk"]
    tokens_all, width = kv_sums.shape[1:]
    tokens = tokens_all // shards
    rest_bits = bits_of(shards // GROUPS)
    ndim = 1 + len(rest_bits)
    sem = pltpu.SemaphoreType.DMA
    scratch = [pltpu.VMEM((GROUPS,) + (2,) * (ndim - 1 - s) + (tokens, width), kv_sums.dtype) for s in range(ndim)]
    flat, sums = [], []
    for (kept, order), pair in zip(orders, pairs):
        rows, cols = pair[0].shape[-2:]
        flat += [part.reshape((2,) * len(kept) + (rows, cols)) for part in pair]
        sums.append(jax.ShapeDtypeStruct((rows, cols), jnp.float32))
        scratch.append(pltpu.VMEM((2,) * len(kept) + (rows, cols), jnp.bfloat16))
        scratch += stream_scratch(len(kept), order, rows, cols)
    stages = max([len(order) for _, order in orders], default=1)
    return pl.pallas_call(
        functools.partial(reduce_kernel, shards, bit_axes(shape), orders),
        out_shape=(
            jax.ShapeDtypeStruct((GROUPS,) + q_packed.shape[2:], q_packed.dtype),
            jax.ShapeDtypeStruct((GROUPS, tokens, width), kv_sums.dtype),
        ) + tuple(sums),
        in_specs=[VMEM_SPEC] * (2 + len(flat)),
        out_specs=(VMEM_SPEC,) * (2 + len(sums)),
        scratch_shapes=[sem((4,)), sem((4,)), sem((ndim, GROUPS)), sem((ndim, GROUPS)), sem((GROUPS,)), sem((GROUPS,)),
                        sem((max(len(orders), 1), stages)), sem((max(len(orders), 1), stages))] + scratch,
        compiler_params=pltpu.CompilerParams(collective_id=2, has_side_effects=True, vmem_limit_bytes=VMEM_BYTES),
        name="reduce_keys",
    )(q_packed, kv_sums.reshape((2, GROUPS) + (2,) * len(rest_bits) + (tokens, width)), *flat)


TQ = 256
TK = 512
NEAR_ROWS = 448
NEG = -1e30
FIRST_MAX = -1e29
NT = (((1,), (1,)), ((), ()))
NN = (((1,), (0,)), ((), ()))
BORDERS = (12, 16, 23, 32, 46, 64, 91)


def mxu(left, right, dims=NN):
    return lax.dot_general(left, right, dims, preferred_element_type=jnp.float32)


def turned(tile):
    return jnp.concatenate([tile[:, 64:], tile[:, :64]], axis=1)


def spread_lanes(packed, high):
    lane = lax.broadcasted_iota(jnp.int32, (1, 128), 1)
    keep = lane >= 64 if high else lane < 64
    zero = jnp.zeros((), packed.dtype)
    pair, last = packed[0:TQ], packed[TQ:]
    pick = lambda tile: jnp.where(keep, tile, zero)
    if high:
        return [pick(turned(pair)), pick(pair), jnp.concatenate([pick(turned(last)), pick(last)], axis=0)]
    return [pick(pair), pick(turned(pair)), jnp.concatenate([pick(last), pick(turned(last))], axis=0)]


def join_heads(parts):
    half = TQ // 2
    top = jnp.concatenate([parts[0], parts[1]], axis=1)
    low = jnp.concatenate([parts[2][:half], parts[2][half:]], axis=1)
    return jnp.concatenate([top, low], axis=0)


def valid_mask(se_ref, r, i, k0):
    kpos = k0 + lax.broadcasted_iota(jnp.int32, (TK, TQ), 0)
    return jnp.logical_and(kpos >= se_ref[r, i, 0:1, :], kpos < se_ref[r, i, 1:2, :])


def near_buckets(first, rows, parity):
    relative = (
        first - TK + TQ * parity
        + lax.broadcasted_iota(jnp.int32, (rows, TQ), 0)
        - lax.broadcasted_iota(jnp.int32, (rows, TQ), 1)
    )
    return buckets_of(relative)


def make_bias(table, parity, near_ref, tiles=(0, 1)):
    heads = near_ref.shape[0]
    for tile in tiles:
        def rows(step, _):
            start = pl.multiple_of(step * 32, 32)
            place = tile * TK + start
            after = place - near_start(parity)
            inside = jnp.logical_and(after >= 0, after < NEAR_ROWS)

            @pl.when(inside)
            def _():
                which = near_buckets(place, 32, parity)
                for h in range(heads):
                    value = jnp.zeros((32, TQ), jnp.float32)
                    for b in range(BUCKETS):
                        value = jnp.where(which == b, table[h, b], value)
                    near_ref[h, tile, pl.ds(start, 32)] = value.astype(jnp.bfloat16)

            @pl.when(jnp.logical_not(inside))
            def _():
                for h in range(heads):
                    value = jnp.where(after < 0, table[h, 15], table[h, 31])
                    near_ref[h, tile, pl.ds(start, 32)] = jnp.full((32, TQ), value, jnp.float32).astype(jnp.bfloat16)

            return 0
        lax.fori_loop(0, TK // 32, rows, 0)


def tile_kind(bounds, r, i, t):
    slot = jnp.clip(t - bounds[r, i, 2] + 1, 0, 3)
    away = jnp.logical_or(slot == 0, slot == 3)
    inside = jnp.logical_and(t >= bounds[r, i, 3], t < bounds[r, i, 4])
    return slot, jnp.logical_and(away, inside)


def fwd_kernel(alone, bounds, table, q_ref, kv_hbm, se_ref, *refs):
    if alone:
        near_ref, o_in, keep_in, lse_in, o_ref, keep_ref, lse_ref, vt, acc, mx, qp, kv_ref, kv_sem = refs
    else:
        o_ref, keep_ref, lse_ref, near_ref, vt, acc, mx, qp, kv_ref, kv_sem = refs
        make_bias(table, bounds[0, 0, 5], near_ref)
    heads = lse_ref.shape[2]
    base = 1 - bounds[0, 0, 6] if alone else 0

    def row_body(at, _):
        r = base + at
        lo_all = jnp.minimum(bounds[r, 0, 0], bounds[r, 1, 0])
        hi_all = jnp.maximum(bounds[r, 0, 1], bounds[r, 1, 1])

        def fetch(t):
            rows = pl.ds(pl.multiple_of(t * TK, TK), TK)
            return pltpu.make_async_copy(kv_hbm.at[r, rows], kv_ref.at[rows], kv_sem.at[t])

        def begin(t, _):
            fetch(t).start()
            return 0

        lax.fori_loop(lo_all, hi_all, begin, 0)
        for i in range(2):
            for h, tile in enumerate(spread_lanes(q_ref[r, i], False)):
                qp[i, h] = tile

        def turn(t, _):
            fetch(t).wait()
            k0 = pl.multiple_of(t * TK, TK)
            for h in range(heads):
                tile = kv_ref[pl.ds(k0, TK), h * 128 : h * 128 + 128]
                vt[h, 0:64, pl.ds(k0, TK)] = tile.T[64:128, :]
                vt[h, 64:80, pl.ds(k0, TK)] = jnp.ones((16, TK), jnp.bfloat16)
            return 0

        lax.fori_loop(lo_all, hi_all, turn, 0)

        def q_body(i, _):
            acc[...] = jnp.zeros_like(acc)
            mx[...] = jnp.full_like(mx, FIRST_MAX)

            def tile_body(t, _):
                k0 = pl.multiple_of(t * TK, TK)
                slot, plain = tile_kind(bounds, r, i, t)
                near = jnp.logical_and(slot > 0, slot < 3)

                def scores(h):
                    return mxu(kv_ref[pl.ds(k0, TK), h * 128 : h * 128 + 128], qp[i, h], NT)

                def finish(h, s, b):
                    m_old = mx[h]
                    m_new = jnp.maximum(m_old, jnp.max(s, axis=0, keepdims=True) + b)
                    p = jnp.exp(s - (m_new - b)).astype(jnp.bfloat16)
                    mx[h] = m_new
                    acc[h] = acc[h] * jnp.exp(m_old - m_new) + mxu(vt[h, :, pl.ds(k0, TK)], p)

                @pl.when(plain)
                def _():
                    found = [scores(h) for h in range(heads)]
                    for h in range(heads):
                        finish(h, found[h], jnp.where(slot == 0, table[h, 15], table[h, 31]))

                @pl.when(near)
                def _():
                    ok = valid_mask(se_ref, r, i, k0)
                    for h in range(heads):
                        s = scores(h) + near_ref[h, slot - 1].astype(jnp.float32)
                        finish(h, jnp.where(ok, s, NEG), 0.0)

                @pl.when(jnp.logical_not(jnp.logical_or(plain, near)))
                def _():
                    ok = valid_mask(se_ref, r, i, k0)
                    for h in range(heads):
                        s = scores(h) + jnp.where(slot == 0, table[h, 15], table[h, 31])
                        finish(h, jnp.where(ok, s, NEG), 0.0)

                return 0

            lax.fori_loop(bounds[r, i, 0], bounds[r, i, 1], tile_body, 0)
            parts = []
            for h in range(heads):
                total = acc[h, 64:65, :]
                parts.append((acc[h, 0:64, :] / total).T)
                lse_ref[r, i, h] = mx[h] + jnp.log(total)
            joined = join_heads(parts)
            o_ref[r, i] = joined.astype(jnp.bfloat16)
            keep_ref[r, i] = joined
            return 0

        lax.fori_loop(0, 2, q_body, 0)
        return 0

    lax.fori_loop(0, 1 if alone else 2, row_body, 0)
    if alone:
        o_ref[1 - base] = o_in[...]
        keep_ref[1 - base] = keep_in[...]
        lse_ref[1 - base] = lse_in[...]


def attention(bounds, table, q, kv, se, ready=()):
    heads, n = kv.shape[2] // 128, kv.shape[1]
    packed = q.shape
    outs = [
        jax.ShapeDtypeStruct(packed, jnp.bfloat16),
        jax.ShapeDtypeStruct(packed, jnp.float32),
        jax.ShapeDtypeStruct((2, 2, heads, 1, TQ), jnp.float32),
    ]
    if not ready:
        outs.append(jax.ShapeDtypeStruct((heads, 2, TK, TQ), jnp.bfloat16))
    return pl.pallas_call(
        functools.partial(fwd_kernel, bool(ready)),
        out_shape=tuple(outs),
        in_specs=[SMEM_SPEC] * 2 + [VMEM_SPEC, ANY_SPEC, VMEM_SPEC] + [VMEM_SPEC] * len(ready),
        out_specs=(VMEM_SPEC,) * len(outs),
        scratch_shapes=[
            pltpu.VMEM((heads, 80, n), jnp.bfloat16),
            pltpu.VMEM((heads, 80, TQ), jnp.float32),
            pltpu.VMEM((heads, 1, TQ), jnp.float32),
            pltpu.VMEM((2, heads, TQ, 128), jnp.bfloat16),
            pltpu.VMEM(kv.shape[1:], jnp.bfloat16),
            pltpu.SemaphoreType.DMA((n // TK,)),
        ],
        compiler_params=pltpu.CompilerParams(vmem_limit_bytes=VMEM_BYTES),
        name="attention",
    )(bounds, table, q, kv, se, *ready)


def prepare(q, do, q_out, do_out):
    for h, tile in enumerate(spread_lanes(q, False)):
        q_out[h] = tile
    for h, tile in enumerate(spread_lanes(do, True)):
        do_out[h] = tile


def row_deltas(do, keep, delta):
    prod = (do.astype(jnp.float32) * keep).T
    top, low = prod[:, 0:TQ], prod[:, TQ:]
    delta[0] = jnp.sum(top[0:64], axis=0, keepdims=True)
    delta[1] = jnp.sum(top[64:128], axis=0, keepdims=True)
    delta[2] = jnp.concatenate(
        [jnp.sum(low[0:64], axis=0, keepdims=True), jnp.sum(low[64:128], axis=0, keepdims=True)], axis=1
    )


def near_start(parity):
    return 416 - TQ * parity


def far_sums(grid, h, first, end):
    def one(step, total):
        rows = grid[h, pl.ds(pl.multiple_of(step * 32, 32), 32)]
        return total + jnp.sum(rows.reshape(4, 8, TQ), axis=0)
    total = lax.fori_loop(first // 32, end // 32, one, jnp.zeros((8, TQ), jnp.float32))
    return jnp.sum(total, axis=0, keepdims=True)


def bucket_sums(parity, near, side, tab_ref, tab8):
    heads = near.shape[0]
    tab8[...] = jnp.zeros_like(tab8)

    def inner(step, _):
        start = pl.multiple_of(step * 32, 32)
        which = near_buckets(near_start(parity) + start, 32, parity)
        for b in range(BUCKETS):
            here = which == b
            for h in range(heads):
                rows = jnp.where(here, near[h, pl.ds(start, 32)], 0.0)
                tab8[h, b] += jnp.sum(rows.reshape(4, 8, TQ), axis=0)
        return 0

    lax.fori_loop(0, NEAR_ROWS // 32, inner, 0)
    for h in range(heads):
        tab_ref[h] = jnp.sum(tab8[h], axis=1)
        tab_ref[h, 15:16] += side[h, 0:1]
        tab_ref[h, 31:32] += side[h, 1:2]


def bwd_kernel(alone, bounds, table, q_ref, do_ref, keep_ref, kv_hbm, bias_ref, se_ref, lse_ref,
               dq_ref, dkv_ref, near_ref, side, delta, *rest):
    tab_ref, tab8, rest = (None, None, rest) if alone else (rest[0], rest[-1], rest[1:-1])
    kt, dqt, dkv, grid, qp, dp_ref, kv_ref, kv_sem = rest
    heads = lse_ref.shape[2]
    n = kv_hbm.shape[1]
    grid[...] = jnp.zeros_like(grid)
    side[...] = jnp.zeros_like(side)
    base = 1 - bounds[0, 0, 6] if alone else 0
    for at in range(1 if alone else 2):
        for i in range(2):
            prepare(q_ref[base + at, i], do_ref[base + at, i], qp.at[at, i], dp_ref.at[at, i])
    for r in range(2):
        for i in range(2):
            row_deltas(do_ref[r, i], keep_ref[r, i], delta.at[r, i])

    def row_body(at, _):
        r = base + at
        lo_all = jnp.minimum(bounds[r, 0, 0], bounds[r, 1, 0])
        hi_all = jnp.maximum(bounds[r, 0, 1], bounds[r, 1, 1])

        def fetch(t):
            rows = pl.ds(pl.multiple_of(t * TK, TK), TK)
            return pltpu.make_async_copy(kv_hbm.at[r, rows], kv_ref.at[rows], kv_sem.at[t])

        def begin(t, _):
            fetch(t).start()
            return 0

        lax.fori_loop(lo_all, hi_all, begin, 0)

        def clear(t, _):
            k0 = pl.multiple_of(t * TK, TK)
            for h in range(heads):
                dkv[h, pl.ds(k0, TK), :] = jnp.zeros((TK, 128), jnp.float32)
            return 0

        lax.fori_loop(0, n // TK, clear, 0)

        def turn(t, _):
            fetch(t).wait()
            k0 = pl.multiple_of(t * TK, TK)
            for h in range(heads):
                tile = kv_ref[pl.ds(k0, TK), h * 128 : h * 128 + 128]
                kt[h, 0:64, pl.ds(k0, TK)] = tile.T[0:64, :]
                kt[h, 64:80, pl.ds(k0, TK)] = jnp.ones((16, TK), jnp.bfloat16)
            return 0

        lax.fori_loop(lo_all, hi_all, turn, 0)

        def q_body(i, _):
            dqt[...] = jnp.zeros_like(dqt)

            def tile_body(t, _):
                k0 = pl.multiple_of(t * TK, TK)
                slot, plain = tile_kind(bounds, r, i, t)

                def finish(h, p, ds, where):
                    ds_low = ds.astype(jnp.bfloat16)
                    two = jnp.concatenate([ds_low, p.astype(jnp.bfloat16)], axis=1)
                    both = jnp.concatenate([qp[at, i, h], dp_ref[at, i, h]], axis=0)
                    dkv[h, pl.ds(k0, TK), :] += mxu(two, both)
                    dqt[h, where] += mxu(kt[h, :, pl.ds(k0, TK)], ds_low)

                def products(h):
                    tile = kv_ref[pl.ds(k0, TK), h * 128 : h * 128 + 128]
                    return mxu(tile, qp[at, i, h], NT), mxu(tile, dp_ref[at, i, h], NT)

                @pl.when(plain)
                def _():
                    for h in range(heads):
                        s, d_probs = products(h)
                        p = jnp.exp(s - (lse_ref[r, i, h] - jnp.where(slot == 0, table[h, 15], table[h, 31])))
                        finish(h, p, p * (d_probs - delta[r, i, h]), jnp.where(slot == 0, 0, 2))

                def general(bias):
                    ok = valid_mask(se_ref, r, i, k0)
                    for h in range(heads):
                        s, d_probs = products(h)
                        s = s + bias(h)
                        p = jnp.where(ok, jnp.exp(jnp.where(ok, s, NEG) - lse_ref[r, i, h]), 0.0)
                        ds = p * (d_probs - delta[r, i, h])
                        grid[h, pl.ds(pl.multiple_of(slot * TK, TK), TK)] += ds
                        finish(h, p, ds, 1)

                near = jnp.logical_and(slot > 0, slot < 3)
                pl.when(near)(lambda: general(lambda h: bias_ref[h, slot - 1].astype(jnp.float32)))
                away = jnp.logical_not(jnp.logical_or(plain, near))
                pl.when(away)(lambda: general(lambda h: jnp.where(slot == 0, table[h, 15], table[h, 31])))
                return 0

            lax.fori_loop(bounds[r, i, 0], bounds[r, i, 1], tile_body, 0)
            parts = []
            for h in range(heads):
                parts.append((dqt[h, 0, 0:64] + dqt[h, 1, 0:64] + dqt[h, 2, 0:64]).T * 0.125)
                side[h, 0:1] += dqt[h, 0, 64:65]
                side[h, 1:2] += dqt[h, 2, 64:65]
            dq_ref[at, i] = join_heads(parts).astype(jnp.bfloat16)
            return 0

        lax.fori_loop(0, 2, q_body, 0)

        def put(t, _):
            k0 = pl.multiple_of(t * TK, TK)
            for h in range(heads):
                dkv_ref[at, pl.ds(k0, TK), h * 128 : h * 128 + 128] = dkv[h, pl.ds(k0, TK), :].astype(jnp.bfloat16)
            return 0

        lax.fori_loop(0, n // TK, put, 0)
        return 0

    lax.fori_loop(0, 1 if alone else 2, row_body, 0)

    parity = bounds[0, 0, 5]
    first = TK + near_start(parity)
    for h in range(heads):
        near_ref[h] = grid[h, pl.ds(pl.multiple_of(first, 32), NEAR_ROWS)]
        side[h, 0:1] += far_sums(grid, h, 0, first)
        side[h, 1:2] += far_sums(grid, h, first + NEAR_ROWS, 4 * TK)
    if not alone:
        bucket_sums(parity, near_ref, side, tab_ref, tab8)


def attention_back(alone, bounds, table, q, do, keep, kv, bias, se, lse):
    heads, n = kv.shape[2] // 128, kv.shape[1]
    count = 1 if alone else 2
    table_out = [] if alone else [jax.ShapeDtypeStruct((heads, BUCKETS, TQ), jnp.float32)]
    return pl.pallas_call(
        functools.partial(bwd_kernel, alone),
        out_shape=(
            jax.ShapeDtypeStruct((count,) + q.shape[1:], jnp.bfloat16),
            jax.ShapeDtypeStruct((count,) + kv.shape[1:], jnp.bfloat16),
            jax.ShapeDtypeStruct((heads, NEAR_ROWS, TQ), jnp.float32),
            jax.ShapeDtypeStruct((heads, 2, TQ), jnp.float32),
            jax.ShapeDtypeStruct((2, 2, heads, 1, TQ), jnp.float32),
        ) + tuple(table_out),
        in_specs=[SMEM_SPEC] * 2 + [VMEM_SPEC] * 3 + [ANY_SPEC] + [VMEM_SPEC] * 3,
        out_specs=(VMEM_SPEC,) * (5 + len(table_out)),
        scratch_shapes=[
            pltpu.VMEM((heads, 80, n), jnp.bfloat16),
            pltpu.VMEM((heads, 3, 80, TQ), jnp.float32),
            pltpu.VMEM((heads, n, 128), jnp.float32),
            pltpu.VMEM((heads, 4 * TK, TQ), jnp.float32),
            pltpu.VMEM((count, 2, heads, TQ, 128), jnp.bfloat16),
            pltpu.VMEM((count, 2, heads, TQ, 128), jnp.bfloat16),
            pltpu.VMEM(kv.shape[1:], jnp.bfloat16),
            pltpu.SemaphoreType.DMA((n // TK,)),
        ] + [pltpu.VMEM((heads, BUCKETS, 8, TQ), jnp.float32) for _ in table_out],
        compiler_params=pltpu.CompilerParams(vmem_limit_bytes=VMEM_BYTES),
        name="attention_back",
    )(bounds, table, q, do, keep, kv, bias, se, lse)


TAPS = tuple(range(-3, 5))
LEAD = 8


def pool_scalars(y_rows, lab_rows, first):
    tokens = y_rows[0].shape[1]
    t = lax.broadcasted_iota(jnp.int32, (1, tokens), 1)
    at = lambda rows, k: rows[k + 3]
    found = []
    for p in range(2):
        inside = {1: 0 * t, 2: 0 * t + p, 3: (first + 2 * t + p) % 3, 4: 2 * (t % 2) + p}
        weights, scores = {}, []
        for b in range(1, MAX_BLOCK + 1):
            keep = {}
            for o in range(1 - b, b):
                same = jnp.logical_and(inside[b] + o >= 0, inside[b] + o < b)
                same = jnp.logical_and(same, at(lab_rows, p + o) == at(lab_rows, p))
                keep[o] = same.astype(jnp.float32)
            inverse = 1.0 / sum(keep.values())
            for o in keep:
                weights[b, o] = keep[o] * inverse
            scores.append(sum(weights[b, o] * at(y_rows, p + o) for o in keep))
        top = functools.reduce(jnp.maximum, scores)
        grown = [jnp.exp(s - top) for s in scores]
        total = sum(grown)
        found.append(([g / total for g in grown], weights))
    return found


def tap_weights(found):
    rows = []
    for k in TAPS:
        row = 0.0
        for p, (probs, weights) in enumerate(found):
            for b in range(1, MAX_BLOCK + 1):
                if (b, k - p) in weights:
                    row = row + probs[b - 1] * weights[b, k - p]
        rows.append(0.5 * row)
    return rows


def as_columns(rows):
    tokens = rows[0].shape[1]
    return jnp.concatenate(list(rows) + [jnp.zeros((128 - len(rows), tokens), jnp.float32)], axis=0).T


def load_bytes(x_ref, before_ref, after_ref, xs):
    length, width = x_ref.shape
    for j in range(width // 128):
        cols = slice(j * 128, j * 128 + 128)
        xs[j, 0:LEAD, :] = jnp.zeros((LEAD, 128), jnp.float32)
        xs[j, LEAD + length :, :] = jnp.zeros((LEAD, 128), jnp.float32)
        xs[j, LEAD - 2 : LEAD, :] = before_ref[0:2, cols].astype(jnp.float32)
        xs[j, LEAD + length : LEAD + length + 2, :] = after_ref[0:2, cols].astype(jnp.float32)
        xs[j, LEAD : LEAD + length, :] = x_ref[:, cols].astype(jnp.float32)


def tap(xs, k, tokens):
    return jnp.concatenate([xs[j, pl.ds(LEAD + k, tokens, stride=2), :] for j in range(xs.shape[0])], axis=1)


def strips(buf, first, rows):
    return jnp.concatenate([buf[j, first : first + rows, :] for j in range(buf.shape[0])], axis=1)


def unit_rows(values):
    return lax.rsqrt(jnp.mean(values * values, axis=-1, keepdims=True) + 1e-06)


def pool_kernel(shards, scale, x_ref, before_ref, after_ref, lab_ref, score_ref, gain_ref, wq_ref, wk_ref, wv_ref,
                hidden_ref, n1_ref, y_ref, share_ref, q_ref, kv_ref, xs):
    tokens = hidden_ref.shape[0]
    width = hidden_ref.shape[1]
    load_bytes(x_ref, before_ref, after_ref, xs)
    score = jnp.broadcast_to(score_ref[...], (8, width))
    for k in TAPS:
        y_ref[k + 3 : k + 4, :] = mxu(score, tap(xs, k, tokens).astype(jnp.bfloat16), NT)[0:1]
    rows = [y_ref[j : j + 1, :] for j in range(8)]
    labels = [lab_ref[j : j + 1, :] for j in range(8)]
    first = (lax.axis_index("blk") * x_ref.shape[0]) % 3
    found = pool_scalars(rows, labels, first)
    lane = lax.broadcasted_iota(jnp.int32, (1, 128), 1)
    share = jnp.zeros((1, 128), jnp.float32)
    for b in range(MAX_BLOCK):
        share = jnp.where(lane == b, jnp.sum(found[0][0][b] + found[1][0][b], axis=1, keepdims=True) * scale, share)
    share_ref[...] = share
    columns = as_columns(tap_weights(found))
    hidden = sum(columns[:, k + 3 : k + 4] * tap(xs, k, tokens) for k in TAPS)
    hidden_ref[...] = hidden
    n1 = (hidden * unit_rows(hidden) * gain_ref[...].astype(jnp.float32)).astype(jnp.bfloat16)
    n1_ref[...] = n1
    keys = mxu(n1, wk_ref[...]).astype(jnp.bfloat16)
    values = mxu(n1, wv_ref[...]).astype(jnp.bfloat16)
    low = lane < 64
    for j in range(width // 128):
        k_pair, v_pair = keys[:, j * 128 : j * 128 + 128], values[:, j * 128 : j * 128 + 128]
        one = jnp.where(low, k_pair, turned(v_pair))
        two = jnp.where(low, turned(k_pair), v_pair)
        for head, tile in ((2 * j, one), (2 * j + 1, two)):
            kv_ref[head // 3, :, head % 3 * 128 : head % 3 * 128 + 128] = tile
    queries = mxu(n1, wq_ref[...]).astype(jnp.bfloat16) * jnp.bfloat16(0.125)
    put_packed(queries, q_ref)


def put_packed(array, out_ref):
    tokens = array.shape[0]
    half = tokens // 2
    for g in range(GROUPS):
        part = array[:, g * 192 : g * 192 + 192]
        out_ref[g, 0:tokens, :] = part[:, 0:128]
        out_ref[g, tokens:, :] = jnp.concatenate([part[:half, 128:], part[half:, 128:]], axis=1)


def get_packed(packed_ref):
    tokens = packed_ref.shape[1] * 2 // 3
    parts = []
    for g in range(GROUPS):
        last = packed_ref[g, tokens:, :]
        parts += [packed_ref[g, 0:tokens, :], jnp.concatenate([last[:, :64], last[:, 64:]], axis=0)]
    return jnp.concatenate(parts, axis=1)


def pool_and_project(shards, scale, x, before, after, labels, score, gain, wq, wk, wv):
    length, width = x.shape
    tokens = length // 2
    return pl.pallas_call(
        functools.partial(pool_kernel, shards, scale),
        out_shape=(
            jax.ShapeDtypeStruct((tokens, width), jnp.float32),
            jax.ShapeDtypeStruct((tokens, width), jnp.bfloat16),
            jax.ShapeDtypeStruct((8, tokens), jnp.float32),
            jax.ShapeDtypeStruct((1, 128), jnp.float32),
            jax.ShapeDtypeStruct((GROUPS, tokens * 3 // 2, 128), jnp.bfloat16),
            jax.ShapeDtypeStruct((GROUPS, tokens, width * 2 // GROUPS), jnp.bfloat16),
        ),
        in_specs=[VMEM_SPEC] * 9,
        out_specs=(VMEM_SPEC,) * 6,
        scratch_shapes=[pltpu.VMEM((width // 128, length + 2 * LEAD, 128), jnp.float32)],
        compiler_params=pltpu.CompilerParams(vmem_limit_bytes=VMEM_BYTES),
        name="pool_and_project",
    )(x, before, after, labels, score, gain, wq, wk, wv)


GELU_A = math.sqrt(2.0 / math.pi)
GELU_B = 0.044715


def norm_back(d_out, rows, gain):
    unit = unit_rows(rows)
    flat = rows * unit
    scaled = d_out * gain
    d_rows = unit * (scaled - flat * jnp.mean(scaled * flat, axis=-1, keepdims=True))
    return d_rows, jnp.sum(d_out * flat, axis=0, keepdims=True)


def feed_kernel(o_ref, hidden_ref, ct_ref, gain_ref, wo_ref, wg_ref, wu_ref, wd_ref,
                out_ref, dres_ref, da_ref, dgain_ref, n2_ref, att_ref, act_ref, dg_ref, du_ref, db_ref, acc, dn2):
    ff = wg_ref.shape[1]
    step = 512
    att = get_packed(o_ref)
    att_ref[...] = att
    residual = hidden_ref[...] + mxu(att, wo_ref[...])
    gain = gain_ref[...].astype(jnp.float32)
    n2_ref[...] = (residual * unit_rows(residual) * gain).astype(jnp.bfloat16)
    acc[...] = residual
    dn2[...] = jnp.zeros_like(dn2)

    for j in range(ff // step):
        cols = slice(j * step, j * step + step)
        n2 = n2_ref[...]
        gate = mxu(n2, wg_ref[:, cols])
        up = mxu(n2, wu_ref[:, cols])
        d_act = mxu(ct_ref[...], wd_ref[cols, :], NT)
        square = gate * gate
        curve = jnp.tanh(GELU_A * gate * (1.0 + GELU_B * square))
        half = 0.5 * (1.0 + curve)
        grown = gate * half
        slope = half + 0.5 * gate * (1.0 - curve * curve) * (GELU_A * (1.0 + 3.0 * GELU_B * square))
        act = (grown * up).astype(jnp.bfloat16)
        d_gate = (d_act * up * slope).astype(jnp.bfloat16)
        d_up = (d_act * grown).astype(jnp.bfloat16)
        act_ref[:, cols] = act
        dg_ref[:, cols] = d_gate
        du_ref[:, cols] = d_up
        acc[...] += mxu(act, wd_ref[cols, :])
        dn2[...] += mxu(d_gate, wg_ref[:, cols], NT) + mxu(d_up, wu_ref[:, cols], NT)

    out_ref[...] = acc[...].astype(jnp.bfloat16)
    residual = hidden_ref[...] + mxu(att_ref[...], wo_ref[...])
    d_rows, d_gain = norm_back(dn2[...], residual, gain)
    dgain_ref[...] = d_gain
    d_res = ct_ref[...].astype(jnp.float32) + d_rows
    dres_ref[...] = d_res
    d_branch = d_res.astype(jnp.bfloat16)
    db_ref[...] = d_branch
    put_packed(mxu(d_branch, wo_ref[...], NT).astype(jnp.bfloat16), da_ref)


def feed_forward(o_home, hidden, ct, gain, wo, wg, wu, wd):
    tokens, width = hidden.shape
    ff = wg.shape[1]
    low = lambda cols: jax.ShapeDtypeStruct((tokens, cols), jnp.bfloat16)
    return pl.pallas_call(
        feed_kernel,
        out_shape=(
            low(width),
            jax.ShapeDtypeStruct((tokens, width), jnp.float32),
            jax.ShapeDtypeStruct(o_home.shape, jnp.bfloat16),
            jax.ShapeDtypeStruct((1, width), jnp.float32),
            low(width), low(width), low(ff), low(ff), low(ff), low(width),
        ),
        in_specs=[VMEM_SPEC] * 8,
        out_specs=(VMEM_SPEC,) * 10,
        scratch_shapes=[pltpu.VMEM((tokens, width), jnp.float32)] * 2,
        compiler_params=pltpu.CompilerParams(vmem_limit_bytes=VMEM_BYTES),
        name="feed_forward",
    )(o_home, hidden, ct, gain, wo, wg, wu, wd)


def unpack_pairs(dkv_ref, width):
    low = lax.broadcasted_iota(jnp.int32, (1, 128), 1) < 64
    dk_parts, dv_parts = [], []
    for j in range(width // 128):
        one, two = [dkv_ref[h // 3, :, h % 3 * 128 : h % 3 * 128 + 128] for h in (2 * j, 2 * j + 1)]
        dk_parts.append(jnp.where(low, one, turned(two)))
        dv_parts.append(jnp.where(low, turned(one), two))
    return jnp.concatenate(dk_parts, axis=1), jnp.concatenate(dv_parts, axis=1)


def pool_back(d_hidden, x_refs, lab_ref, y_ref, score_ref, gb_ref, edge_ref, spill_ref, xs, gbuf):
    x_ref = x_refs[0]
    tokens, width = d_hidden.shape
    length = x_ref.shape[0]
    lane = lax.broadcasted_iota(jnp.int32, (1, 128), 1)
    met = jnp.zeros((tokens, 128), jnp.float32)
    for k in TAPS:
        met = jnp.where(lane == k + 3, jnp.sum(d_hidden * tap(xs, k, tokens), axis=-1, keepdims=True), met)
    met = met.T
    first = (lax.axis_index("blk") * length) % 3
    found = pool_scalars([y_ref[j : j + 1, :] for j in range(8)], [lab_ref[j : j + 1, :] for j in range(8)], first)
    touch = [0.0] * 8
    for p, (probs, weights) in enumerate(found):
        d_block = []
        for b in range(1, MAX_BLOCK + 1):
            d_block.append(0.5 * sum(weights[b, o] * met[p + o + 3 : p + o + 4] for o in range(1 - b, b)))
        mean = sum(q * d for q, d in zip(probs, d_block))
        for b in range(1, MAX_BLOCK + 1):
            d_score = probs[b - 1] * (d_block[b - 1] - mean)
            for o in range(1 - b, b):
                touch[p + o + 3] = touch[p + o + 3] + d_score * weights[b, o]
    share_cols = as_columns(tap_weights(found) + touch)
    score = score_ref[...].astype(jnp.float32)
    gbuf[...] = jnp.zeros_like(gbuf)
    d_score_vec = jnp.zeros((1, width), jnp.float32)
    for k in TAPS:
        own, via = share_cols[:, k + 3 : k + 4], share_cols[:, k + 11 : k + 12]
        added = own * d_hidden + via * score
        for j in range(gbuf.shape[0]):
            gbuf[j, pl.ds(LEAD + k, tokens, stride=2), :] += added[:, j * 128 : j * 128 + 128]
        d_score_vec = d_score_vec + jnp.sum(via * tap(xs, k, tokens), axis=0, keepdims=True)
    gb_ref[...] = strips(gbuf, LEAD, length).astype(jnp.bfloat16)
    edge_ref[0] = strips(gbuf, LEAD, 16)
    edge_ref[1] = strips(gbuf, LEAD + length - 16, 16)
    spill_ref[0] = strips(gbuf, 0, LEAD)
    spill_ref[1] = strips(gbuf, LEAD + length, LEAD)
    return d_score_vec


def put_small(small_ref, vectors, tab_ref, share_ref):
    small_ref[...] = jnp.zeros_like(small_ref)
    for row, vector in zip((0, 6, 12), vectors):
        for j in range(6):
            small_ref[row + j : row + j + 1, :] = vector[:, j * 128 : j * 128 + 128]
    heads = tab_ref.shape[0]
    group = lax.axis_index("blk") // (lax.axis_size("blk") // GROUPS)
    for h in range(heads):
        total = lax.dot_general(
            jnp.ones((8, tab_ref.shape[2]), jnp.float32), tab_ref[h], NT,
            precision=lax.Precision.HIGHEST, preferred_element_type=jnp.float32,
        )
        small_ref[pl.ds(18 + group * heads + h, 1), 0:BUCKETS] = total[0:1]
    small_ref[30:31, :] = share_ref[...]


def last_kernel(shards, axes, order, dq_ref, dkv_ref, hidden_ref, dres_ref, x_ref, before_ref, after_ref, lab_ref, y_ref, score_ref,
                gain_ref, wq_ref, wk_ref, wv_ref, dgain2_ref, share_ref, tab_ref, gb_ref, edge_ref, spill_out, small_out, parts_ref,
                w_send, w_recv, s_send, s_recv, xs, gbuf, spill_ref, small_ref, small_bufs):
    at = {"dp": lax.axis_index("dp"), "blk": lax.axis_index("blk")}
    width = hidden_ref.shape[1]
    whole = Whole(axes, at, order, small_ref, small_bufs, small_out, w_send, w_recv)
    left = (at["dp"], (at["blk"] + shards - 1) % shards)
    right = (at["dp"], (at["blk"] + 1) % shards)
    greet([whole.stream.target(p) for p in range(len(axes))] + [left, right])
    load_bytes(x_ref, before_ref, after_ref, xs)
    dq = get_packed(dq_ref)
    dk, dv = unpack_pairs(dkv_ref, width)
    parts_ref[0], parts_ref[1], parts_ref[2] = dq, dk, dv
    d_n1 = mxu(dq, wq_ref[...], NT) + mxu(dk, wk_ref[...], NT) + mxu(dv, wv_ref[...], NT)
    d_rows, d_gain1 = norm_back(d_n1, hidden_ref[...], gain_ref[...].astype(jnp.float32))
    d_hidden = dres_ref[...] + d_rows
    d_score = pool_back(d_hidden, (x_ref, before_ref, after_ref), lab_ref, y_ref, score_ref, gb_ref, edge_ref, spill_ref, xs, gbuf)
    put_small(small_ref, (d_score, d_gain1, dgain2_ref[...]), tab_ref, share_ref)
    spills = [
        remote(spill_ref.at[0], spill_out.at[1], s_send.at[0], s_recv.at[1], left),
        remote(spill_ref.at[1], spill_out.at[0], s_send.at[1], s_recv.at[0], right),
    ]
    whole.copy(0).start()
    for copy in spills:
        copy.start()
    for stage in range(len(axes)):
        advance(whole, stage)
    for copy in spills:
        copy.wait()


def last_part(shape, dq, dkv, hidden, dres, x, before, after, labels, y, score, gain, wq, wk, wv, dgain2, share, tab):
    tokens, width = hidden.shape
    length = x.shape[0]
    axes = bit_axes(shape)
    ndim = len(axes)
    full, sem, low = jax.ShapeDtypeStruct, pltpu.SemaphoreType.DMA, jnp.bfloat16
    strip = pltpu.VMEM((width // 128, length + 2 * LEAD, 128), jnp.float32)
    return pl.pallas_call(
        functools.partial(last_kernel, shape["blk"], axes, tuple(reversed(range(ndim)))),
        out_shape=(
            full((length, width), low),
            full((2, 16, width), jnp.float32),
            full((2, LEAD, width), jnp.float32),
            full((32, 128), jnp.float32),
            full((3, tokens, width), low),
        ),
        in_specs=[VMEM_SPEC] * 17,
        out_specs=(VMEM_SPEC,) * 5,
        scratch_shapes=[
            sem((ndim,)), sem((ndim,)), sem((2,)), sem((2,)), strip, strip,
            pltpu.VMEM((2, LEAD, width), jnp.float32), pltpu.VMEM((32, 128), jnp.float32), pltpu.VMEM((2, ndim, 32, 128), jnp.float32),
        ],
        compiler_params=pltpu.CompilerParams(collective_id=3, has_side_effects=True, vmem_limit_bytes=VMEM_BYTES),
        name="last_part",
    )(dq, dkv, hidden, dres, x, before, after, labels, y, score, gain, wq, wk, wv, dgain2, share, tab)


def finish_kernel(shards, heads_all, gb_ref, edge_ref, spill_ref, small_ref, *refs):
    position = lax.axis_index("blk")
    streams, outs = refs[: len(refs) - (5 if len(refs) == 5 else 12)], refs[len(refs) - (5 if len(refs) == 5 else 12) :]
    bytes_ref, score_ref, gain1_ref, gain2_ref, tab_ref = outs[:5]
    length = gb_ref.shape[0]
    bytes_ref[...] = gb_ref[...]
    zero = jnp.zeros((16 - LEAD, gb_ref.shape[1]), jnp.float32)
    left = jnp.where(position > 0, spill_ref[0], 0.0)
    right = jnp.where(position < shards - 1, spill_ref[1], 0.0)
    bytes_ref[0:16, :] = (edge_ref[0] + jnp.concatenate([left, zero], axis=0)).astype(jnp.bfloat16)
    bytes_ref[length - 16 :, :] = (edge_ref[1] + jnp.concatenate([zero, right], axis=0)).astype(jnp.bfloat16)
    for row, ref in ((0, score_ref), (6, gain1_ref), (12, gain2_ref)):
        for j in range(6):
            ref[j * 128 : j * 128 + 128] = small_ref[row + j, :]
    tab_ref[...] = small_ref[16:32, :]
    if streams:
        gq, gk, gv, go, gg, gu, gd = outs[5:]
        per, width = gq.shape
        half, ff = width // 2, gg.shape[1]
        one, two, down, *thirds = streams
        for ref, third in zip((gq, gk, gv), thirds):
            ref[:, :half] = third[:per, :]
            ref[:, half:] = third[per:, :]
        first = one.shape[1]
        for ref, rows in ((gg, slice(0, per)), (gu, slice(per, 2 * per))):
            ref[:, :first] = one[rows, :]
            ref[:, first:] = two[rows, : ff - first]
        go[:, :half] = two[:per, ff - first :]
        go[:, half:] = two[per:, ff - first :]
        gd[...] = down[...]


def finish(shards, heads_all, per, ff, gb, edge, spill, small, streams):
    width = gb.shape[1]
    full = jax.ShapeDtypeStruct
    line = full((width,), jnp.float32)
    outs = [full(gb.shape, jnp.bfloat16), line, line, line, full((16, 128), jnp.float32)]
    if streams:
        square, broad = full((per, width), jnp.float32), full((per, ff), jnp.float32)
        outs += [square] * 4 + [broad] * 2 + [full((streams[2].shape[0], width), jnp.float32)]
    return pl.pallas_call(
        functools.partial(finish_kernel, shards, heads_all),
        out_shape=tuple(outs),
        in_specs=[VMEM_SPEC] * (4 + len(streams)),
        out_specs=(VMEM_SPEC,) * len(outs),
        compiler_params=pltpu.CompilerParams(vmem_limit_bytes=VMEM_BYTES),
        name="finish",
    )(gb, edge, spill, small, *streams)


class NearRows:
    def __init__(self, grid, first):
        self.grid, self.first, self.shape = grid, first, grid.shape

    def __getitem__(self, index):
        h, rows = index
        return self.grid[h, pl.ds(pl.multiple_of(self.first + rows.start, 32), rows.size)]


class Refs:
    def __init__(self, **refs):
        self.__dict__.update(refs)


class Held:
    def __init__(self, array, space):
        self.array, self.space = array, space


def call(kernel, ident, ins, outs, scratch):
    leaf = lambda entry: isinstance(entry, Held) or isinstance(entry, tuple) or not isinstance(entry, (dict, list))
    parts = [jax.tree.flatten(part, is_leaf=leaf) for part in (ins, outs, scratch)]
    counts = [len(part[0]) for part in parts]
    given, wanted, kept = [part[0] for part in parts]

    def run(*refs):
        named, start = {}, 0
        for count, (_, tree) in zip(counts, parts):
            named.update(jax.tree.unflatten(tree, refs[start : start + count]))
            start += count
        kernel(Refs(**named))

    space = lambda entry, at: entry.space if isinstance(entry, Held) else entry[2] if isinstance(entry, tuple) and len(entry) > 2 else at
    found = pl.pallas_call(
        run,
        out_shape=tuple(jax.ShapeDtypeStruct(entry[0], entry[1]) for entry in wanted),
        in_specs=[pl.BlockSpec(memory_space=space(entry, pltpu.VMEM)) for entry in given],
        out_specs=tuple(pl.BlockSpec(memory_space=space(entry, pltpu.VMEM)) for entry in wanted),
        scratch_shapes=kept,
        compiler_params=pltpu.CompilerParams(collective_id=ident, has_side_effects=True, vmem_limit_bytes=VMEM_BYTES),
        name=kernel.func.__name__,
    )(*[entry.array if isinstance(entry, Held) else entry for entry in given])
    return Refs(**jax.tree.unflatten(parts[1][1], found))


wide = lambda value: value.astype(jnp.float32)
slim = lambda value: value.astype(jnp.bfloat16)


class DenseBack:
    def __init__(self, place, r):
        self.place, self.r = place, r
        self.heads = r.lse.shape[2]
        self.tokens = TQ
        self.across, self.core_to, self.row_to = place.other_rest(2), place.other_rest(1), place.other_row()
        self.y, self.core = bit(place.rest, 2), place.rest % 2
        self.s_core = remote(r.dkvs_hbm.at[:, :, 1 - self.core], r.s_in, r.s_send, r.s_recv, self.core_to)
        self.own_rows = pltpu.make_async_copy(r.dkvs_hbm.at[:, :, self.core], r.dkvs, r.own_sem)
        self.near_rows = pltpu.make_async_copy(r.nears_hbm, r.nears, r.near_sem)

    def group_of(self, n):
        return (self.place.group + 1 + n) % GROUPS

    def tile_start(self, m):
        place_y = jnp.where(m % 2 == 0, 1 - self.y, self.y)
        return pl.multiple_of((self.group_of(m // 2) * 2 + place_y) * TK, TK)

    def fetch(self, m):
        r = self.r
        return pltpu.make_async_copy(r.kv_hbm.at[:, pl.ds(self.tile_start(m), TK)], r.kv.at[m % 4], r.kv_sem.at[m % 4])

    def prepare(self):
        r = self.r
        for m in range(4):
            self.fetch(m).start()
        self.own_rows.start()
        self.near_rows.start()
        self.dense = r.bounds[0, 0, 6]
        self.mine_dense = self.dense == self.place.row
        for i in range(2):
            for h, tile in enumerate(spread_lanes(r.q[self.dense, i], False)):
                r.qp[i, h] = tile
            for h, tile in enumerate(spread_lanes(r.do[self.dense, i], True)):
                r.dp[i, h] = tile
        r.dqt[...] = jnp.zeros_like(r.dqt)
        r.grid[...] = jnp.zeros_like(r.grid)

    def core_copy(self, n, j):
        r = self.r
        return remote(r.held.at[n, j, 1 - self.core], r.core_in.at[n, j], r.core_send.at[n, j], r.core_recv.at[n, j], self.core_to)

    def x_copy(self, n, j):
        r = self.r
        return remote(r.x_out.at[n, j], r.x_in.at[n, j], r.x_send.at[n, j], r.x_recv.at[n, j], self.row_to)

    def y_copy(self, n, j):
        r = self.r
        return remote(r.y_out.at[n, j], r.y_in.at[n, j], r.y_send.at[n, j], r.y_recv.at[n, j], self.across)

    def z_copy(self, n):
        r, place = self.r, self.place
        return remote(r.z_out.at[n], r.dkv_home.at[place.group], r.z_send.at[n], r.z_recv.at[n], place.at(place.row, self.group_of(n), place.rest))

    def by_rows(self, one):
        def step(k, _):
            one(pl.ds(pl.multiple_of(k * 32, 32), 32))
            return 0
        lax.fori_loop(0, self.tokens // 32, step, 0)

    def own_sum(self, n, j, rows):
        return wide(self.r.held[n, j, self.core, rows]) + wide(self.r.core_in[n, j, rows])

    def split_rows(self, one, two):
        return slim(jnp.where(self.mine_dense, two, one)), slim(jnp.where(self.mine_dense, one, two))

    def other_sums(self):
        r = self.r
        self.s_core.wait()
        self.own_rows.wait()

        def one(step, _):
            n, far = step // 2, step % 2
            row = jnp.where(far == 0, 1 - self.y, self.y)
            group = self.group_of(n)

            def some(rows):
                r.s_in[group, row, rows] = slim(wide(r.dkvs[group, row, rows]) + wide(r.s_in[group, row, rows]))

            self.by_rows(some)
            pl.when(jnp.logical_and(far == 0, n % 2 == 0))(self.y_other(n).start)
            return 0

        lax.fori_loop(0, 2 * GROUPS, one, 0)

    def other(self, n, j):
        return self.r.s_in.at[self.group_of(n), 1 - self.y if j == 0 else self.y]

    def y_other(self, n):
        r = self.r
        return remote(self.other(n, 0), r.y_in.at[n, 1], r.y_send.at[n, 1], r.y_recv.at[n, 1], self.across)

    def y_first_1(self, n):
        r = self.r
        self.core_copy(n, 0).wait()

        def one(rows):
            r.y_out[n, 0, rows] = slim(self.own_sum(n, 0, rows))

        self.by_rows(one)
        self.y_copy(n, 0).start()

    def y_first_3(self, n):
        r = self.r
        self.core_copy(n, 1).wait()
        self.y_other(n).wait()
        self.y_copy(n, 0).wait()

        def one(rows):
            first = self.own_sum(n, 1, rows) + wide(r.y_in[n, 0, rows])
            second = wide(self.other(n, 1)[rows]) + wide(r.y_in[n, 1, rows])
            r.x_out[n, 0, rows], r.kept[n, 0, rows] = self.split_rows(first, second)

        self.by_rows(one)
        self.x_copy(n, 0).start()

    def y_first_5(self, n):
        r = self.r
        self.x_copy(n, 0).wait()

        def one(rows):
            r.z_out[n, rows] = slim(wide(r.kept[n, 0, rows]) + wide(r.x_in[n, 0, rows]))

        self.by_rows(one)
        self.z_copy(n).start()

    def x_first_1(self, n, j=0):
        r = self.r
        self.core_copy(n, j).wait()

        def one(rows):
            r.x_out[n, j, rows], r.kept[n, j, rows] = self.split_rows(self.own_sum(n, j, rows), wide(self.other(n, j)[rows]))

        self.by_rows(one)
        self.x_copy(n, j).start()

    def x_first_2(self, n):
        self.x_first_1(n, 1)

    def x_first_3(self, n):
        r = self.r
        self.x_copy(n, 0).wait()

        def one(rows):
            r.y_out[n, 0, rows] = slim(wide(r.kept[n, 0, rows]) + wide(r.x_in[n, 0, rows]))

        self.by_rows(one)
        self.y_copy(n, 0).start()

    def x_first_5(self, n):
        r = self.r
        self.x_copy(n, 1).wait()
        self.y_copy(n, 0).wait()

        def one(rows):
            total = slim(wide(r.kept[n, 1, rows]) + wide(r.x_in[n, 1, rows]) + wide(r.y_in[n, 0, rows]))
            if n == GROUPS - 1:
                r.dkv_home[self.place.group, rows] = total
            else:
                r.z_out[n, rows] = total

        self.by_rows(one)
        if n < GROUPS - 1:
            self.z_copy(n).start()

    def tile(self, m):
        r, place, heads = self.r, self.place, self.heads
        n, j = m // 2, m % 2
        t = self.tile_start(m) // TK
        self.fetch(m).wait()
        r.acc[...] = jnp.zeros_like(r.acc)
        r.keys[...] = jnp.where(self.dense == 0, r.kv[m % 4, 0], r.kv[m % 4, 1])
        keys = lambda h: r.keys[:, h * 128 : h * 128 + 128]
        for h in range(heads):
            r.kt[h, 0:64] = keys(h).T[0:64]
            r.kt[h, 64:80] = jnp.ones((16, TK), jnp.bfloat16)

        def part(i, _):
            first = ((2 * place.row + i) * place.rest_size + place.rest) * self.tokens
            slot = jnp.clip(t - (first // TK - 1 + self.core) + 1, 0, 3)
            away = jnp.logical_or(slot == 0, slot == 3)

            def finish(h, p, ds, where):
                ds_low = ds.astype(jnp.bfloat16)
                two = jnp.concatenate([ds_low, p.astype(jnp.bfloat16)], axis=1)
                both = jnp.concatenate([r.qp[i, h], r.dp[i, h]], axis=0)
                r.acc[:, h * 128 : h * 128 + 128] += mxu(two, both)
                r.dqt[i, h, where] += mxu(r.kt[h], ds_low)

            def products(h):
                return mxu(keys(h), r.qp[i, h], NT), mxu(keys(h), r.dp[i, h], NT)

            @pl.when(away)
            def _():
                for h in range(heads):
                    s, d_probs = products(h)
                    p = jnp.exp(s - (r.lse[self.dense, i, h] - jnp.where(slot == 0, r.table[h, 15], r.table[h, 31])))
                    finish(h, p, p * (d_probs - r.delta[self.dense, i, h]), jnp.where(slot == 0, 0, 2))

            @pl.when(jnp.logical_not(away))
            def _():
                for h in range(heads):
                    s, d_probs = products(h)
                    p = jnp.exp(s + r.bias[h, slot - 1].astype(jnp.float32) - r.lse[self.dense, i, h])
                    ds = p * (d_probs - r.delta[self.dense, i, h])
                    r.grid[h, pl.ds(pl.multiple_of((slot - 1) * TK, TK), TK)] += ds
                    finish(h, p, ds, 1)

            return 0

        lax.fori_loop(0, 2, part, 0)
        for half in range(2):
            r.held[n, j, half] = r.acc[half * self.tokens : half * self.tokens + self.tokens].astype(jnp.bfloat16)
        self.core_copy(n, j).start()
        pl.when(m < 4)(lambda: self.fetch(m + 4).start())

    def queries(self):
        r = self.r
        for i in range(2):
            parts = []
            for h in range(self.heads):
                parts.append((r.dqt[i, h, 0, 0:64] + r.dqt[i, h, 1, 0:64] + r.dqt[i, h, 2, 0:64]).T * 0.125)
            mine = join_heads(parts)
            other = r.dqs[0, i].astype(jnp.float32)
            for row in range(2):
                r.dq_rows[row, i] = jnp.where(self.dense == row, mine, other).astype(jnp.bfloat16)

    def buckets(self):
        r = self.r
        self.near_rows.wait()
        first = near_start(self.core)
        for h in range(self.heads):
            r.side[h, 0:1] = r.dqt[0, h, 0, 64:65] + r.dqt[1, h, 0, 64:65] + r.sides[h, 0:1] + far_sums(r.grid, h, 0, first)
            r.side[h, 1:2] = r.dqt[0, h, 2, 64:65] + r.dqt[1, h, 2, 64:65] + r.sides[h, 1:2] + far_sums(r.grid, h, first + NEAR_ROWS, 2 * TK)
            rows = pl.ds(pl.multiple_of(first, 32), NEAR_ROWS)
            r.grid[h, rows] += r.nears[h]
        bucket_sums(self.core, NearRows(r.grid, first), r.side, r.tab, r.tab8)

    def wait_home(self):
        r, place = self.r, self.place
        for n in range(GROUPS - 1):
            there = r.dkv_home.at[(place.group - 1 - n + GROUPS) % GROUPS]
            remote(r.z_out.at[n], there, r.z_send.at[n], r.z_recv.at[n], self.row_to).wait()


def back_kernel(shards, axes, plans, r):
    place = Place(shards)
    at = {"dp": place.dp, "blk": place.blk}
    tokens, width = r.hidden.shape
    back = DenseBack(place, r)
    streams = []
    for s, (kept, order) in enumerate(plans):
        streams.append(Stream(axes, at, kept, order, r.src[s], r.bufs[s], r.sums[s], r.w_send.at[s], r.w_recv.at[s]))
    early, late = streams[:3], streams[3:]
    whole = Whole(axes, at, (4, 0, 3, 2, 1), r.small, r.small_bufs, r.small_out, r.w_send.at[len(plans)], r.w_recv.at[len(plans)])
    left, right = (place.dp, (place.blk + shards - 1) % shards), (place.dp, (place.blk + 1) % shards)

    met = hail(line_and_row(place) + [back.across, back.core_to, left, right])
    fetches = [pltpu.make_async_copy(r.came_hbm[s], early[s].src, r.came_sem.at[s]) for s in range(3)]
    for copy in fetches:
        copy.start()
    back.prepare()
    for s in range(3):
        fetches[s].wait()
        add_two(early[s].src, early[s].src, r.keeps[s])
    await_all(met)
    back.s_core.start()
    for stream in early:
        stream.copy(0).start()

    def step(m, _):
        back.tile(m)
        pl.when(m == 0)(back.other_sums)
        for when, n, action in (
            (1, 0, back.y_first_1), (3, 1, back.x_first_1), (4, 1, back.x_first_2), (5, 2, back.y_first_1),
            (6, 0, back.y_first_3), (6, 1, back.x_first_3), (7, 3, back.x_first_1),
        ):
            pl.when(m == when)(functools.partial(action, n))
        return 0

    lax.fori_loop(0, 2 * GROUPS, step, 0)
    back.x_first_2(3)
    back.queries()
    return_heads(place, r.dq_rows, r.dq_home, r.q_send, r.q_recv)
    for stream in early:
        advance(stream, 0)
    back.y_first_5(0)
    back.x_first_3(3)
    back.x_first_5(1)
    back.y_first_3(2)
    back.buckets()
    for stream in early:
        advance(stream, 1)
    back.y_first_5(2)
    back.x_first_5(3)
    load_bytes(r.x, r.before, r.after, r.xs)
    n1_t = r.n1[...].T
    return_heads_wait(place, r.dq_rows, r.dq_home, r.q_send, r.q_recv)
    dq = get_packed(r.dq_home)
    devices = 1 << len(axes)
    per = width // devices
    half = width // 2

    def weights(stream, part):
        r.total[...] = mxu(n1_t, part)

        def block(d, _):
            rows = pl.ds(pl.multiple_of(d * per, 8), per)
            index, rest = [], d
            for _ in axes:
                index.append(rest % 2)
                rest = rest // 2
            part = r.total[rows, :]
            stream.src[tuple(reversed(index))] = jnp.concatenate([part[:, :half], part[:, half:]], axis=0).astype(jnp.bfloat16)
            return 0

        lax.fori_loop(0, devices, block, 0)
        stream.copy(0).start()

    weights(late[0], dq)
    back.wait_home()
    dk, dv = unpack_pairs(r.dkv_home, width)
    weights(late[1], dk)
    weights(late[2], dv)
    d_n1 = mxu(dq, r.wq[...], NT) + mxu(dk, r.wk[...], NT) + mxu(dv, r.wv[...], NT)
    d_rows, d_gain1 = norm_back(d_n1, r.hidden[...], r.gain[...].astype(jnp.float32))
    d_hidden = r.dres[...] + d_rows
    for stream in late:
        advance(stream, 0)
    for stream in early:
        advance(stream, 2)
    d_score = pool_back(d_hidden, (r.x, r.before, r.after), r.labels, r.y, r.score, r.gb, r.edge, r.spill, r.xs, r.gbuf)
    put_small(r.small, (d_score, d_gain1, r.dgain2[...]), r.tab, r.share)
    whole.copy(0).start()
    spills = [
        remote(r.spill.at[0], r.spill_out.at[1], r.s2_send.at[0], r.s2_recv.at[1], left),
        remote(r.spill.at[1], r.spill_out.at[0], r.s2_send.at[1], r.s2_recv.at[0], right),
    ]
    for copy in spills:
        copy.start()
    for stage in range(1, len(axes)):
        for stream in late:
            advance(stream, stage)
        advance(whole, stage - 1)
    advance(whole, len(axes) - 1)
    for copy in spills:
        copy.wait()


def back_and_last(shape, keeps, came, inputs):
    shards = shape["blk"]
    axes = bit_axes(shape)
    ndim = len(axes)
    kv, q, hidden = inputs["kv_hbm"].array, inputs["q"], inputs["hidden"]
    heads, n, width = kv.shape[2] // 128, kv.shape[1], kv.shape[2]
    tokens, features = hidden.shape
    length = inputs["x"].shape[0]
    f32, low, sem = jnp.float32, jnp.bfloat16, pltpu.SemaphoreType.DMA
    chunk = (tokens, width)
    every = (0, 1, 2, 3, 4)
    plans = [
        ((1, 2, 3), (3, 2, 1)), ((0, 1, 2), (2, 0, 1)), ((0, 1, 3), (0, 3, 1)),
        (every, (4, 0, 3, 2, 1)), (every, (4, 3, 2, 0, 1)), (every, (4, 2, 0, 3, 1)),
    ]
    own = (2 * (features // (1 << ndim)), features // 2)
    blocks = [part.shape[-2:] for part in keeps] + [own] * 3
    bits = lambda part: part.reshape((2, 2, 2) + part.shape[-2:])
    ins = dict(inputs, keeps=[bits(part) for part in keeps], came_hbm=[Held(bits(part), pl.ANY) for part in came])
    outs = dict(
        gb=((length, features), low), edge=((2, 16, features), f32), spill_out=((2, LEAD, features), f32),
        small_out=((32, 128), f32), sums=[(block, f32) for block in blocks],
    )
    mem = lambda shape, dtype=low: pltpu.VMEM(shape, dtype)
    pairs, fours = sem((GROUPS, 2)), sem((GROUPS,))
    strip = mem((features // 128, length + 2 * LEAD, 128), f32)
    scratch = dict(
        kt=mem((heads, 80, TK)), dqt=mem((2, heads, 3, 80, TQ), f32), acc=mem((TK, width), f32),
        grid=mem((heads, 2 * TK, TQ), f32), side=mem((heads, 2, TQ), f32), tab8=mem((heads, BUCKETS, 8, TQ), f32),
        tab=mem((heads, BUCKETS, TQ), f32),
        qp=mem((2, heads, TQ, 128)), dp=mem((2, heads, TQ, 128)),
        kv=mem((4, 2, TK, width)), keys=mem((TK, width)), dkvs=mem((GROUPS, 2) + chunk), nears=mem((heads, NEAR_ROWS, TQ), f32),
        held=mem((GROUPS, 2, 2) + chunk), core_in=mem((GROUPS, 2) + chunk), s_in=mem((GROUPS, 2) + chunk),
        x_out=mem((GROUPS, 2) + chunk), x_in=mem((GROUPS, 2) + chunk),
        y_out=mem((GROUPS, 1) + chunk), y_in=mem((GROUPS, 2) + chunk), kept=mem((GROUPS, 2) + chunk),
        z_out=mem((GROUPS,) + chunk), dkv_home=mem((GROUPS,) + chunk),
        dq_rows=mem((2, 2) + q.shape[2:]), dq_home=mem((GROUPS,) + q.shape[2:]),
        core_send=pairs, core_recv=pairs, x_send=pairs, x_recv=pairs, y_send=pairs, y_recv=pairs,
        z_send=fours, z_recv=fours, s_send=sem, s_recv=sem, q_send=fours, q_recv=fours,
        kv_sem=fours, came_sem=sem((3,)), own_sem=sem, near_sem=sem,
        w_send=sem((len(plans) + 1, ndim)), w_recv=sem((len(plans) + 1, ndim)), s2_send=sem((2,)), s2_recv=sem((2,)),
        xs=strip, gbuf=strip, spill=mem((2, LEAD, features), f32), small=mem((32, 128), f32),
        small_bufs=mem((2, ndim, 32, 128), f32), total=mem((features, features), f32),
    )
    scratch["src"] = [mem((2,) * len(kept) + block) for (kept, _), block in zip(plans, blocks)]
    scratch["bufs"] = [stream_scratch(len(kept), order, *block) for (kept, order), block in zip(plans, blocks)]
    return call(functools.partial(back_kernel, shards, axes, plans), 6, ins, outs, scratch)


class DenseForward:
    def __init__(self, place, r):
        self.place, self.r, self.heads = place, r, r.lse.shape[1]

    def prepare(self, dense):
        r = self.r
        self.dense = dense
        for i in range(2):
            for h, tile in enumerate(spread_lanes(jnp.where(dense == 0, r.q_all[0, i], r.q_all[1, i]), False)):
                r.qp[i, h] = tile
        r.acc[...] = jnp.zeros_like(r.acc)
        r.mx[...] = jnp.full_like(r.mx, FIRST_MAX)

    def tile(self, group, place_y):
        r, place = self.r, self.place
        t = group * 2 + place_y
        rows = pl.ds(pl.multiple_of(t * TK, TK), TK)
        r.keys[...] = jnp.where(self.dense == 0, r.kv_all[0, rows], r.kv_all[1, rows])
        for h in range(self.heads):
            r.vt[h, 0:64] = r.keys[:, h * 128 : h * 128 + 128].T[64:128]
            r.vt[h, 64:80] = jnp.ones((16, TK), jnp.bfloat16)

        def part(i, _):
            first = ((2 * place.row + i) * place.rest_size + place.rest) * TQ
            slot = jnp.clip(t - (first // TK - 1 + place.rest % 2) + 1, 0, 3)
            away = jnp.logical_or(slot == 0, slot == 3)

            def scores(h):
                return mxu(r.keys[:, h * 128 : h * 128 + 128], r.qp[i, h], NT)

            def finish(h, s, b):
                m_old = r.mx[i, h]
                m_new = jnp.maximum(m_old, jnp.max(s, axis=0, keepdims=True) + b)
                p = jnp.exp(s - (m_new - b)).astype(jnp.bfloat16)
                r.mx[i, h] = m_new
                r.acc[i, h] = r.acc[i, h] * jnp.exp(m_old - m_new) + mxu(r.vt[h], p)

            @pl.when(away)
            def _():
                found = [scores(h) for h in range(self.heads)]
                for h in range(self.heads):
                    finish(h, found[h], jnp.where(slot == 0, r.table[h, 15], r.table[h, 31]))

            @pl.when(jnp.logical_not(away))
            def _():
                for h in range(self.heads):
                    finish(h, scores(h) + r.near[h, slot - 1].astype(jnp.float32), 0.0)

            return 0

        lax.fori_loop(0, 2, part, 0)

    def end(self):
        r = self.r
        for i in range(2):
            parts = []
            for h in range(self.heads):
                total = r.acc[i, h, 64:65, :]
                parts.append((r.acc[i, h, 0:64, :] / total).T)
                r.lse[i, h] = r.mx[i, h] + jnp.log(total)
            joined = join_heads(parts)
            r.o[i] = joined.astype(jnp.bfloat16)
            r.keep[i] = joined


def label_spans(place, r):
    ids = range(8)
    shards = place.shards
    blocks = r.labels_all[...].reshape(2, shards, 8, 128)
    ends = []
    for row in range(2):
        here = blocks[row]
        ends.append([jnp.sum(jnp.logical_and(here >= 0, here <= k).astype(jnp.int32)) for k in ids])
    dense = (ends[0][0] < shards * TQ).astype(jnp.int32)
    for row in range(2):
        for i in range(2):
            group = 2 * place.row + i
            chunk = r.labels_all[tuple([row] + [bit(group * place.rest_size + place.rest, m) for m in bits_of(shards)])]
            line = jnp.concatenate([chunk[0:1], chunk[1:2]], axis=1)
            begin, end = jnp.zeros((1, TQ), jnp.int32), jnp.zeros((1, TQ), jnp.int32)
            for k in ids:
                begin = jnp.where(line == k, ends[row][k - 1] if k else 0, begin)
                end = jnp.where(line == k, ends[row][k], end)
            r.span[row, i, 0:1] = begin
            r.span[row, i, 1:2] = end
            first = (group * place.rest_size + place.rest) * TQ
            r.bounds[row, i, 0] = jnp.min(begin) // TK
            r.bounds[row, i, 1] = (jnp.max(end) + TK - 1) // TK
            r.bounds[row, i, 2] = first // TK - 1 + place.rest % 2
            r.bounds[row, i, 3] = (jnp.max(begin) + TK - 1) // TK
            r.bounds[row, i, 4] = jnp.min(end) // TK
            r.bounds[row, i, 5] = place.rest % 2
            r.bounds[row, i, 6] = dense
    return dense


def front_kernel(shards, r):
    place = Place(shards)
    tokens = r.kv.shape[1]
    y, core = bit(place.rest, 2), place.rest % 2
    core_to, across, row_to = place.other_rest(1), place.other_rest(2), place.other_row()
    met = hail(line_and_row(place) + [core_to, across])
    dims = [("row", 1)] + [("blk", m) for m in bits_of(shards)]
    lab_index = [place.row] + [bit(place.blk, m) for _, m in dims[1:]]

    def lab_copy(stage):
        index = tuple(slice(None) if p < stage else lab_index[p] for p in range(len(dims)))
        axis, mask = dims[stage]
        target = row_to if axis == "row" else (place.dp, flipped(place.blk, mask))
        there = r.labels_all.at[index]
        return remote(there, there, r.lab_send.at[stage], r.lab_recv.at[stage], target)

    def held(dz, off, core_off):
        row = 1 - place.row if off & 1 else place.row
        rest = flipped(place.rest, 2) if off & 2 else place.rest
        rest = flipped(rest, 1) if core_off else rest
        start = pl.multiple_of(place.chunk((place.group + dz) % GROUPS, rest) * tokens, tokens)
        return r.kv_all.at[row, pl.ds(start, tokens)]

    def sem_of(dz, off, core_off):
        return r.kv_recv.at[(core_off * 4 + off) * GROUPS + dz]

    waits = []

    def send(src, dz, off, core_off, target):
        copy = remote(src, held(dz, off & 3, 0), r.kv_send.at[len(waits)], sem_of(*core_off), target)
        copy.start()
        waits.append(copy)

    def arrived(dz, off, core_off=0):
        here = held(dz, off, core_off)
        remote(here, here, r.kv_send.at[0], sem_of(dz, off, core_off), core_to).wait_recv()

    def pass_on(dz, off):
        src = r.kv.at[place.group] if dz == 0 and off == 0 else held(dz, off, 0)
        if not (dz == 0 and off == 0):
            arrived(dz, off)
        order = (0, 1) if dz % 2 == 0 else (1, 0)
        last = max([order.index(p) for p in range(2) if off >> p & 1], default=-1)
        for p in order[last + 1 :]:
            send(src, dz, off, (dz, off | 1 << p, 0), across if p else row_to)
        send(src, dz, off, (dz, off, 1), core_to)

    r.labels_all[tuple(lab_index)] = r.label[...]
    await_all(met)
    lab_copy(0).start()
    own = pltpu.make_async_copy(r.kv.at[place.group], held(0, 0, 0), r.own_sem)
    own.start()

    def along(step):
        copy = remote(r.kv.at[(place.group + step) % GROUPS], held(0, 0, 0), r.z_send.at[step], sem_of((GROUPS - step) % GROUPS, 0, 0), place.other_group(step))
        copy.start()
        return copy

    def label_stage(stage):
        lab_copy(stage).wait()
        if stage + 1 < len(dims):
            lab_copy(stage + 1).start()

    work = DenseForward(place, r)

    def tile(dz, off_y):
        for off in (2 * off_y, 2 * off_y + 1):
            arrived(dz, off, 1)
        work.tile((place.group + dz) % GROUPS, 1 - y if off_y else y)

    first = [along(1), along(3)]
    pass_on(0, 0)
    make_bias(r.table, core, r.near, (0,))
    label_stage(0)
    pass_on(0, 1)
    pass_on(0, 2)
    make_bias(r.table, core, r.near, (1,))
    label_stage(1)
    for copy in first:
        copy.wait_send()
    spread_heads(place, r.q, r.q_all, r.q_send, r.q_recv)
    pass_on(1, 0)
    label_stage(2)
    pass_on(3, 0)
    label_stage(3)
    pass_on(0, 3)
    spread_heads_gone(place, r.q, r.q_all, r.q_send, r.q_recv)
    last = along(2)
    label_stage(4)
    dense = label_spans(place, r)
    pass_on(1, 1)
    pass_on(1, 2)
    spread_heads_come(r.q, r.q_all, r.q_recv)
    own.wait()
    work.prepare(dense)
    pass_on(3, 1)
    pass_on(3, 2)
    tile(0, 0)
    pass_on(1, 3)
    tile(0, 1)
    pass_on(3, 3)
    tile(1, 0)
    pass_on(2, 0)
    tile(1, 1)
    pass_on(2, 1)
    pass_on(2, 2)
    tile(3, 0)
    pass_on(2, 3)
    tile(3, 1)
    tile(2, 0)
    tile(2, 1)
    last.wait_send()
    work.end()
    for copy in waits:
        copy.wait_send()


def front(shards, table, q_packed, kv_parts, label):
    tokens, width = kv_parts.shape[1:]
    heads = width // 128
    nbits = 1 + len(bits_of(shards))
    sem, f32, low = pltpu.SemaphoreType.DMA, jnp.float32, jnp.bfloat16
    half = q_packed.shape[1:]
    ins = dict(table=Held(table, pltpu.SMEM), q=q_packed, kv=kv_parts, label=label)
    outs = dict(
        q_all=((2, 2) + half, low), kv_all=((2, shards * tokens, width), low), bounds=((2, 2, 7), jnp.int32, pltpu.SMEM),
        span=((2, 2, 2, TQ), jnp.int32), near=((heads, 2, TK, TQ), low),
        o=((2,) + half, low), keep=((2,) + half, f32), lse=((2, heads, 1, TQ), f32),
    )
    scratch = dict(
        labels_all=pltpu.VMEM((2,) * nbits + label.shape, label.dtype),
        qp=pltpu.VMEM((2, heads, TQ, 128), low), acc=pltpu.VMEM((2, heads, 80, TQ), f32),
        mx=pltpu.VMEM((2, heads, 1, TQ), f32), keys=pltpu.VMEM((TK, width), low), vt=pltpu.VMEM((heads, 80, TK), low),
        q_send=sem((4,)), q_recv=sem((4,)), kv_send=sem((28,)), z_send=sem((GROUPS,)), kv_recv=sem((32,)), own_sem=sem,
        lab_send=sem((nbits,)), lab_recv=sem((nbits,)),
    )
    return call(functools.partial(front_kernel, shards), 7, ins, outs, scratch)


def middle_kernel(shards, r):
    place = Place(shards)
    met = hail(line_and_row(place) + [place.other_rest(1)])
    pairs = ((r.wo_hbm, r.wo), (r.wg_hbm, r.wg), (r.wu_hbm, r.wu), (r.wd_hbm, r.wd))
    fetches = [pltpu.make_async_copy(src, dst, r.w_sem.at[k]) for k, (src, dst) in enumerate(pairs)]
    for copy in fetches:
        copy.start()
    await_all(met)
    return_heads(place, r.o, r.o_home, r.o_send, r.o_recv)
    for copy in fetches:
        copy.wait()
    return_heads_wait(place, r.o, r.o_home, r.o_send, r.o_recv)
    feed_kernel(r.o_home, r.hidden, r.ct, r.gain, r.wo, r.wg, r.wu, r.wd, r.block_out, r.dres, r.da, r.dgain,
                r.n2, r.att, r.act, r.dg, r.du, r.db, r.acc, r.dn2)
    spread_heads(place, r.da, r.do, r.q_send, r.q_recv)
    feed_weights(place, r.n2, r.att, r.act, r.dg, r.du, r.ct, r.db, r.keep_a, r.send_a, r.keep_b, r.send_b, r.keep_c, r.send_c,
                 r.core_send, r.core_recv, r.gate, r.up, r.down, r.out, r.wide_out, r.slim_out, r.wide_in, r.slim_in)
    spread_heads_wait(place, r.da, r.do, r.q_send, r.q_recv)


def middle(shards, o_packed, hidden, ct, gain, wo, wg, wu, wd):
    tokens, width = hidden.shape
    ff = wg.shape[1]
    per, per_ff = width // 32, ff // 32
    sem, low, f32 = pltpu.SemaphoreType.DMA, jnp.bfloat16, jnp.float32
    half = o_packed.shape[2:]
    wide_cols = ff + width // 2
    first = (wide_cols // 256 + 1) * 128
    ins = dict(o=o_packed, hidden=hidden, ct=ct, gain=gain, wo_hbm=Held(wo, pl.ANY), wg_hbm=Held(wg, pl.ANY), wu_hbm=Held(wu, pl.ANY), wd_hbm=Held(wd, pl.ANY))
    outs = dict(
        block_out=((tokens, width), low), dres=((tokens, width), f32), dgain=((1, width), f32), do=((2, 2) + half, low),
        keep_a=((8, 2 * per, first), low), send_a=((8, 2 * per, first), low),
        keep_b=((8, 2 * per, wide_cols - first), low), send_b=((8, 2 * per, wide_cols - first), low),
        keep_c=((8, per_ff, width), low), send_c=((8, per_ff, width), low),
    )
    mem = lambda shape, dtype=low: pltpu.VMEM(shape, dtype)
    scratch = dict(
        o_home=mem((GROUPS,) + half), da=mem((GROUPS,) + half),
        n2=mem((tokens, width)), att=mem((tokens, width)), db=mem((tokens, width)),
        act=mem((tokens, ff)), dg=mem((tokens, ff)), du=mem((tokens, ff)),
        acc=mem((tokens, width), f32), dn2=mem((tokens, width), f32),
        wo=mem(wo.shape), wg=mem(wg.shape), wu=mem(wu.shape), wd=mem(wd.shape),
        gate=mem((width, ff), f32), up=mem((width, ff), f32), down=mem((ff, width), f32), out=mem((width, width), f32),
        wide_out=mem((16, 2 * per, wide_cols)), slim_out=mem((16, per_ff, width)),
        wide_in=mem((16, 2 * per, wide_cols)), slim_in=mem((16, per_ff, width)),
        w_sem=sem((4,)), o_send=sem((4,)), o_recv=sem((4,)), q_send=sem((4,)), q_recv=sem((4,)),
        core_send=sem((2,)), core_recv=sem((2,)),
    )
    return call(functools.partial(middle_kernel, shards), 8, ins, outs, scratch)


def neighbours(rows):
    peers = lax.axis_size("blk")
    up = [(i, i + 1) for i in range(peers - 1)]
    last, leading = rows
    return lax.ppermute(last, "blk", up), lax.ppermute(leading, "blk", [(j, i) for i, j in up])


def body(
    byte_embeds,
    segments,
    score_weight,
    norm_gain1,
    w_query,
    w_key,
    w_value,
    w_out,
    rel_bias,
    norm_gain2,
    w_gate,
    w_up,
    w_down,
    cotangent,
):
    row_count, length, width = byte_embeds.shape
    tokens = length // 2
    shards = lax.axis_size("blk")
    shape = {"dp": lax.axis_size("dp"), "blk": shards}
    devices = shards * shape["dp"]
    heads = rel_bias.shape[1] // GROUPS
    position = lax.axis_index("blk")
    rest_size = shards // GROUPS
    group, rest = position // rest_size, position % rest_size
    row = lax.axis_index("dp") % 2
    x, ids_here = byte_embeds[0], segments[0]

    marks = (ids_here + 1).astype(jnp.bfloat16)
    with_marks = lambda part, two: jnp.concatenate([part, jnp.pad(two, (0, width - 2))[None]], axis=0)
    before, after = neighbours((with_marks(x[-2:], marks[-2:]), with_marks(x[:2], marks[:2])))
    line = jnp.concatenate([before[2, :2], marks, after[2, :2]])
    line = jnp.pad(line, (1, 1)).astype(jnp.int32).reshape(tokens + 3, 2).T
    labels = jnp.stack([line[j % 2, j // 2 : j // 2 + tokens] for j in range(8)])

    score_row, gain1, gain2 = score_weight[None], norm_gain1[None], norm_gain2[None]
    hidden, n1, y, share, q_packed, kv_parts = pool_and_project(
        shards, 1.0 / (row_count * length * devices), x, before, after, labels, score_row, gain1, w_query, w_key, w_value
    )

    label_block = jnp.pad(ids_here[0::2].reshape(tokens // 128, 128), ((0, 8 - tokens // 128), (0, 0)), constant_values=-1)
    table = lax.dynamic_slice_in_dim(rel_bias.astype(jnp.float32).T, group * heads, heads, 0)
    if devices == 32:
        got = front(shards, table, q_packed, kv_parts, label_block)
        bounds, span, q_all, kv_all, near_bias = got.bounds, got.span, got.q_all, got.kv_all, got.near
        o_packed, o_kept, log_total = attention(
            bounds, table, q_all, kv_all, span, (near_bias, got.o, got.keep, got.lse)
        )
    else:
        q_all, kv_all, labels_all = gather_all(shards, q_packed, kv_parts, label_block)
        labels_all = labels_all.reshape(2, shards, 8, 128)[:, :, : tokens // 128].reshape(2, shards * tokens)
        ids = jnp.arange(8, dtype=jnp.int32)
        counts = jnp.sum((labels_all[:, None, :] == ids[None, :, None]).astype(jnp.int32), axis=2)
        ends = jnp.sum(jnp.where(ids[None, :] <= ids[:, None], counts[:, None, :], 0), axis=2)
        begins = ends - counts
        query_labels = jnp.stack(
            [lax.dynamic_slice_in_dim(labels_all, ((2 * row + i) * rest_size + rest) * tokens, tokens, 1) for i in range(2)],
            axis=1,
        )
        chosen = query_labels[:, :, None, :] == ids[None, None, :, None]
        span = jnp.stack(
            [jnp.sum(jnp.where(chosen, edge[:, None, :, None], 0), axis=2) for edge in (begins, ends)], axis=2
        )
        parity = rest % 2
        firsts = jnp.stack([((2 * row + i) * rest_size + rest) * tokens for i in range(2)])
        near = jnp.broadcast_to((firsts // TK - 1 + parity)[None], (2, 2))
        bounds = jnp.stack(
            [
                jnp.min(span[:, :, 0], axis=-1) // TK,
                -(-jnp.max(span[:, :, 1], axis=-1) // TK),
                near,
                -(-jnp.max(span[:, :, 0], axis=-1) // TK),
                jnp.min(span[:, :, 1], axis=-1) // TK,
                jnp.broadcast_to(parity, (2, 2)),
                jnp.broadcast_to((labels_all[0, -1] > 0).astype(jnp.int32), (2, 2)),
            ],
            axis=-1,
        ).astype(jnp.int32)
        o_packed, o_kept, log_total, near_bias = attention(bounds, table, q_all, kv_all, span)
    ct = cotangent[0]
    if devices == 32:
        mid = middle(shards, o_packed, hidden, ct, gain2, w_out, w_gate, w_up, w_down)
        block_out, d_res, d_gain2, do_all = mid.block_out, mid.dres, mid.dgain, mid.do
        swap = lambda part, axis, mask: lax.ppermute(part, axis, [(i, i ^ mask) for i in range(lax.axis_size(axis))])
        came = [swap(mid.send_a, "dp", 1), swap(mid.send_b, "blk", 2), swap(mid.send_c, "blk", 4)]
        dq_other, dkv_other, near_other, side_other, deltas = attention_back(
            True, bounds, table, q_all, do_all, o_kept, kv_all, near_bias, span, log_total
        )
        last = back_and_last(
            shape,
            [mid.keep_a, mid.keep_b, mid.keep_c],
            came,
            dict(
                bounds=Held(bounds, pltpu.SMEM), table=Held(table, pltpu.SMEM), q=q_all, do=do_all, delta=deltas, kv_hbm=Held(kv_all, pl.ANY),
                bias=near_bias, lse=log_total, dqs=dq_other,
                dkvs_hbm=Held(dkv_other.reshape((GROUPS, 2, 2) + kv_parts.shape[1:]), pl.ANY), nears_hbm=Held(near_other, pl.ANY),
                sides=side_other, hidden=hidden, dres=d_res, n1=n1, x=x, before=before, after=after,
                labels=labels, y=y, score=score_row, gain=gain1, wq=w_query, wk=w_key, wv=w_value, dgain2=d_gain2, share=share,
            ),
        )
        grad_bytes, edge, spill, small, sums = last.gb, last.edge, last.spill_out, last.small_out, last.sums
    else:
        o_home = move_heads(return_kernel, (GROUPS,), shards, 4, o_packed)
        block_out, d_res, da_packed, d_gain2, n2, att, act, d_gate, d_up, d_branch = feed_forward(
            o_home, hidden, ct, gain2, w_out, w_gate, w_up, w_down
        )
        do_all = move_heads(spread_kernel, (2, 2), shards, 5, da_packed)
        dq_packed, dkv_all, _, _, _, d_table_lanes = attention_back(
            False, bounds, table, q_all, do_all, o_kept, kv_all, near_bias, span, log_total
        )
        dq_home, dkv_home = reduce_all(shape, dq_packed, dkv_all, [], [])
        grad_bytes, edge, spill, small, last_parts = last_part(
            shape, dq_home, dkv_home, hidden, d_res, x, before, after, labels, y,
            score_row, gain1, w_query, w_key, w_value, d_gain2, share, d_table_lanes,
        )
        sums = []
    per = width // devices
    grad_bytes, g_score, g_gain1, g_gain2, rows, *grads = finish(
        shards, rel_bias.shape[1], per, w_gate.shape[1], grad_bytes, edge, spill, small, sums
    )
    if devices != 32:
        product = lambda left, right: jnp.einsum("td,te->de", left, right, preferred_element_type=jnp.float32)
        grads = [product(n1, last_parts[j]) for j in range(3)]
        grads += [product(att, d_branch), product(n2, d_gate), product(n2, d_up), product(act, ct)]
        grads = [lax.psum_scatter(grad, ("dp", "blk"), scatter_dimension=0, tiled=True) for grad in grads]
    return (
        block_out[None],
        grad_bytes[None],
        g_score,
        g_gain1,
        *grads[:4],
        rows[2 : 2 + rel_bias.shape[1], :BUCKETS].T,
        g_gain2,
        *grads[4:],
        rows[14, :MAX_BLOCK],
    )


def solution(mesh):
    placed = (
        P("dp", "blk", None),
        P("dp", "blk"),
        P(),
        P(),
        P(),
        P(),
        P(),
        P(),
        P(),
        P(),
        P(),
        P(),
        P(),
        P("dp", "blk", None),
    )
    return jax.shard_map(
        body,
        mesh=mesh,
        in_specs=placed,
        out_specs=(
            P("dp", "blk", None),
            P("dp", "blk", None),
            P(),
            P(),
            P(("dp", "blk"), None),
            P(("dp", "blk"), None),
            P(("dp", "blk"), None),
            P(("dp", "blk"), None),
            P(),
            P(),
            P(("dp", "blk"), None),
            P(("dp", "blk"), None),
            P(("dp", "blk"), None),
            P(),
        ),
        check_vma=False,
    )
```

```python
import functools
import math

import jax
import jax.numpy as jnp
from jax import lax
from jax.experimental import pallas as pl
from jax.experimental.pallas import tpu as pltpu
from jax.sharding import PartitionSpec as P

BUCKETS = 32
MAX_BLOCK = 4
VMEM_BYTES = 61 * 2**20


def buckets_of(relative):
    distance = jnp.abs(relative)
    beyond = jnp.zeros_like(distance)
    for border in (12, 16, 23, 32, 46, 64, 91):
        beyond = beyond + (distance >= border).astype(jnp.int32)
    nearer = jnp.where(distance < 8, distance, 8 + beyond)
    return nearer + BUCKETS // 2 * (relative > 0).astype(jnp.int32)


MESH_ID = pl.DeviceIdType.MESH
GROUPS = 4


def bits_of(size):
    return [1 << p for p in reversed(range(size.bit_length() - 1))]


def bit(value, mask):
    return (value // mask) % 2


def flipped(value, mask):
    return value + mask * (1 - 2 * bit(value, mask))


class Place:
    def __init__(self, shards):
        self.shards = shards
        self.rest_size = shards // GROUPS
        self.dp = lax.axis_index("dp")
        self.blk = lax.axis_index("blk")
        self.row = self.dp % 2
        self.group = self.blk // self.rest_size
        self.rest = self.blk % self.rest_size

    def at(self, row, group, rest):
        return (self.dp - self.row + row, group * self.rest_size + rest)

    def chunk(self, group, rest):
        return group * self.rest_size + rest

    def other_row(self):
        return self.at(1 - self.row, self.group, self.rest)

    def other_rest(self, mask):
        return self.at(self.row, self.group, flipped(self.rest, mask))

    def other_group(self, step):
        return self.at(self.row, (self.group + step) % GROUPS, self.rest)


def hail(targets):
    barrier = pltpu.get_barrier_semaphore()
    for target in targets:
        pl.semaphore_signal(barrier, inc=1, device_id=target, device_id_type=MESH_ID)
    return len(targets)


def await_all(count):
    pl.semaphore_wait(pltpu.get_barrier_semaphore(), count)


def greet(targets):
    await_all(hail(targets))


def remote(src, dst, send_sem, recv_sem, target):
    return pltpu.make_async_remote_copy(
        src_ref=src,
        dst_ref=dst,
        send_sem=send_sem,
        recv_sem=recv_sem,
        device_id=target,
        device_id_type=MESH_ID,
    )


def line_and_row(place):
    found = []
    for step in range(GROUPS):
        for flip in range(2):
            if step or flip:
                row = 1 - place.row if flip else place.row
                found.append(place.at(row, (place.group + step) % GROUPS, place.rest))
    return found


def spread_heads(place, q_ref, out_ref, send_sem, recv_sem):
    row_to = place.group // 2
    slot = place.group % 2
    dst = out_ref.at[place.row, slot]
    mine = recv_sem.at[place.row * 2 + slot]
    at_home = row_to == place.row
    for step in range(GROUPS):
        group = (place.group + step) % GROUPS
        src = q_ref.at[group]
        copy = remote(src, dst, send_sem.at[step], mine, place.at(row_to, group, place.rest))
        if step:
            copy.start()
        else:
            pl.when(jnp.logical_not(at_home))(copy.start)
            pl.when(at_home)(pltpu.make_async_copy(src, dst, mine).start)


def spread_heads_come(q_ref, out_ref, recv_sem):
    for row in range(2):
        for slot in range(2):
            pltpu.make_async_copy(q_ref.at[0], out_ref.at[row, slot], recv_sem.at[row * 2 + slot]).wait()


def spread_heads_gone(place, q_ref, out_ref, send_sem, recv_sem):
    at_home = place.group // 2 == place.row
    for step in range(GROUPS):
        copy = remote(q_ref.at[0], out_ref.at[0, 0], send_sem.at[step], recv_sem.at[0], place.other_row())
        if step:
            copy.wait_send()
        else:
            pl.when(jnp.logical_not(at_home))(copy.wait_send)


def spread_heads_wait(place, q_ref, out_ref, send_sem, recv_sem):
    spread_heads_come(q_ref, out_ref, recv_sem)
    spread_heads_gone(place, q_ref, out_ref, send_sem, recv_sem)


def return_heads(place, o_ref, out_ref, send_sem, recv_sem):
    for row in range(2):
        for slot in range(2):
            group = place.row * 2 + slot
            src = o_ref.at[row, slot]
            dst = out_ref.at[place.group]
            mine = recv_sem.at[place.group]
            at_home = jnp.logical_and(place.row == row, place.group == group)
            copy = remote(src, dst, send_sem.at[row * 2 + slot], mine, place.at(row, group, place.rest))
            pl.when(jnp.logical_not(at_home))(copy.start)
            pl.when(at_home)(pltpu.make_async_copy(src, dst, mine).start)


def return_heads_wait(place, o_ref, out_ref, send_sem, recv_sem):
    for group in range(GROUPS):
        pltpu.make_async_copy(o_ref.at[0, 0], out_ref.at[group], recv_sem.at[group]).wait()
    for row in range(2):
        for slot in range(2):
            group = place.row * 2 + slot
            at_home = jnp.logical_and(place.row == row, place.group == group)
            copy = remote(o_ref.at[0, 0], out_ref.at[0], send_sem.at[row * 2 + slot], recv_sem.at[0], place.other_row())
            pl.when(jnp.logical_not(at_home))(copy.wait_send)


def spread_kernel(shards, q_ref, out_ref, send_sem, recv_sem):
    place = Place(shards)
    greet(line_and_row(place))
    spread_heads(place, q_ref, out_ref, send_sem, recv_sem)
    spread_heads_wait(place, q_ref, out_ref, send_sem, recv_sem)


def return_kernel(shards, o_ref, out_ref, send_sem, recv_sem):
    place = Place(shards)
    greet(line_and_row(place))
    return_heads(place, o_ref, out_ref, send_sem, recv_sem)
    return_heads_wait(place, o_ref, out_ref, send_sem, recv_sem)


SMEM_SPEC = pl.BlockSpec(memory_space=pltpu.SMEM)
VMEM_SPEC = pl.BlockSpec(memory_space=pltpu.VMEM)
ANY_SPEC = pl.BlockSpec(memory_space=pl.ANY)


def move_heads(kernel, lead, shards, ident, packed):
    rows, lanes = packed.shape[-2:]
    return pl.pallas_call(
        functools.partial(kernel, shards),
        out_shape=jax.ShapeDtypeStruct(lead + (rows, lanes), packed.dtype),
        in_specs=[pl.BlockSpec(memory_space=pltpu.VMEM)],
        out_specs=pl.BlockSpec(memory_space=pltpu.VMEM),
        scratch_shapes=[pltpu.SemaphoreType.DMA((4,)), pltpu.SemaphoreType.DMA((4,))],
        compiler_params=pltpu.CompilerParams(collective_id=ident, has_side_effects=True, vmem_limit_bytes=VMEM_BYTES),
        name="move_heads_%d" % ident,
    )(packed)


def gather_kernel(shards, q_ref, kv_ref, label_ref, qo_ref, kvo_ref, labo_ref, q_send, q_recv, z_send, far_send, core_send, kv_recv, own_sem, lab_send, lab_recv):
    place = Place(shards)
    tokens = kv_ref.shape[1]
    rest_bits = bits_of(place.rest_size)
    core, far = rest_bits[-1], ["row"] + rest_bits[:-1]
    greet(line_and_row(place) + [place.other_rest(mask) for mask in rest_bits])

    dims = [("row", 1)] + [("blk", m) for m in bits_of(shards)]
    lab_index = [place.row] + [bit(place.blk, m) for _, m in dims[1:]]
    lab_order = list(range(len(dims)))

    def lab_copy(stage):
        index = tuple(slice(None) if p in lab_order[:stage] else lab_index[p] for p in range(len(dims)))
        axis, mask = dims[lab_order[stage]]
        target = place.other_row() if axis == "row" else (place.dp, flipped(place.blk, mask))
        there = labo_ref.at[index]
        return remote(there, there, lab_send.at[stage], lab_recv.at[stage], target)

    labo_ref[tuple(lab_index)] = label_ref[...]
    lab_copy(0).start()
    lab_stage = 0

    def slot(row, group, rest):
        start = pl.multiple_of(place.chunk(group, rest) * tokens, tokens)
        return kvo_ref.at[row, pl.ds(start, tokens)]

    def held(dz, offset, core_off):
        row = 1 - place.row if offset & 1 else place.row
        rest = place.rest
        for p, mask in enumerate(far[1:]):
            if offset >> (p + 1) & 1:
                rest = flipped(rest, mask)
        if core_off:
            rest = flipped(rest, core)
        return slot(row, (place.group + dz) % GROUPS, rest)

    count = 1 << len(far)

    def sem_of(dz, offset, core_off):
        return kv_recv.at[(core_off * count + offset) * GROUPS + dz]

    own = pltpu.make_async_copy(kv_ref.at[place.group], held(0, 0, 0), own_sem)
    own.start()
    waits = []
    for step in (1, 3, 2):
        copy = remote(kv_ref.at[(place.group + step) % GROUPS], held(0, 0, 0), z_send.at[step], sem_of((GROUPS - step) % GROUPS, 0, 0), place.other_group(step))
        copy.start()
        waits.append(copy)

    used = 0
    events = sorted(((dz, off) for dz in range(GROUPS) for off in range(count)), key=lambda e: (bin(e[1]).count("1"), (0, 1, 3, 2).index(e[0])))
    core_target = place.other_rest(core)
    for step, (dz, off) in enumerate(events):
        if step == GROUPS:
            spread_heads(place, q_ref, qo_ref, q_send, q_recv)
        here = held(dz, off, 0)
        if dz == 0 and off == 0:
            src = kv_ref.at[place.group]
        else:
            remote(here, here, z_send.at[0], sem_of(dz, off, 0), core_target).wait_recv()
            src = here
        order = [(p + dz) % len(far) for p in range(len(far))]
        last = max([order.index(p) for p in range(len(far)) if off >> p & 1], default=-1)
        for p in order[last + 1 :]:
            target = place.other_row() if p == 0 else place.other_rest(far[p])
            copy = remote(src, here, far_send.at[used], sem_of(dz, off | 1 << p, 0), target)
            copy.start()
            waits.append(copy)
            used += 1
        copy = remote(src, here, core_send.at[off * GROUPS + dz], sem_of(dz, off, 1), core_target)
        copy.start()
        waits.append(copy)
        if lab_stage < len(dims):
            lab_copy(lab_stage).wait()
            lab_stage += 1
            if lab_stage < len(dims):
                lab_copy(lab_stage).start()
    for dz, off in events:
        here = held(dz, off, 1)
        remote(here, here, z_send.at[0], sem_of(dz, off, 1), core_target).wait_recv()
    own.wait()
    for copy in waits:
        copy.wait_send()
    spread_heads_wait(place, q_ref, qo_ref, q_send, q_recv)


def gather_all(shards, q_packed, kv_parts, labels):
    tokens, width = kv_parts.shape[1:]
    far = 1 + len(bits_of(shards // GROUPS)) - 1
    count = 1 << far
    nbits = 1 + len(bits_of(shards))
    sem = pltpu.SemaphoreType.DMA
    return pl.pallas_call(
        functools.partial(gather_kernel, shards),
        out_shape=(
            jax.ShapeDtypeStruct((2, 2) + q_packed.shape[1:], q_packed.dtype),
            jax.ShapeDtypeStruct((2, shards * tokens, width), kv_parts.dtype),
            jax.ShapeDtypeStruct((2,) * nbits + labels.shape, labels.dtype),
        ),
        in_specs=[pl.BlockSpec(memory_space=pltpu.VMEM)] * 3,
        out_specs=(pl.BlockSpec(memory_space=pltpu.VMEM),) * 3,
        scratch_shapes=[
            sem((4,)), sem((4,)), sem((GROUPS,)), sem((GROUPS * (count - 1),)), sem((GROUPS * count,)), sem((GROUPS * count * 2,)),
            sem, sem((nbits,)), sem((nbits,)),
        ],
        compiler_params=pltpu.CompilerParams(collective_id=1, has_side_effects=True, vmem_limit_bytes=VMEM_BYTES),
        name="gather_keys",
    )(q_packed, kv_parts, labels)


def add_blocks(dst_ref, src_ref, index, shape):
    lead = shape[:-2]
    total = math.prod(lead)

    def one(step, _):
        place, left = [], step
        for size in reversed(lead):
            place.append(left % size)
            left = left // size
        place = tuple(reversed(place))
        full, k = [], 0
        for entry in index:
            if entry is None:
                full.append(place[k])
                k += 1
            else:
                full.append(entry)
        mine = src_ref[tuple(full)].astype(jnp.float32)
        dst_ref[place] = (dst_ref[place].astype(jnp.float32) + mine).astype(dst_ref.dtype)
        return 0

    lax.fori_loop(0, total, one, 0)


class Stream:
    def __init__(self, axes, at, kept, order, src, bufs, out, send_sem, recv_sem):
        self.axes, self.at, self.kept, self.order = axes, at, kept, order
        self.src, self.bufs, self.out = src, bufs, out
        self.send_sem, self.recv_sem = send_sem, recv_sem

    def own(self, p):
        axis, mask = self.axes[p]
        return bit(self.at[axis], mask)

    def target(self, p):
        axis, mask = self.axes[p]
        moved = dict(self.at)
        moved[axis] = flipped(self.at[axis], mask)
        return (moved["dp"], moved["blk"])

    def stage(self, k):
        kept = [p for p in self.kept if p not in self.order[:k]]
        return kept, self.src if k == 0 else self.bufs[k - 1], self.order[k]

    def copy(self, k):
        kept, src, now = self.stage(k)
        index = tuple(1 - self.own(p) if p == now else slice(None) for p in kept)
        return remote(src.at[index], self.bufs[k], self.send_sem.at[k], self.recv_sem.at[k], self.target(now))

    def absorb(self, k):
        kept, src, now = self.stage(k)
        buf = self.bufs[k]
        if k == len(self.order) - 1 and self.out is not None:
            mine = src[self.own(now)].astype(jnp.float32)
            self.out[...] = buf[...].astype(jnp.float32) + mine
        else:
            add_blocks(buf, src, tuple(self.own(p) if p == now else None for p in kept), buf.shape)


class Whole:
    def __init__(self, axes, at, order, src, bufs, out, send_sem, recv_sem):
        self.stream = Stream(axes, at, order, order, src, bufs, out, send_sem, recv_sem)
        self.order, self.src, self.bufs, self.out = order, src, bufs, out

    def held(self, k):
        return self.src if k == 0 else self.bufs.at[1, k - 1]

    def copy(self, k):
        s = self.stream
        return remote(self.held(k), self.bufs.at[0, k], s.send_sem.at[k], s.recv_sem.at[k], s.target(self.order[k]))

    def absorb(self, k):
        total = self.held(k)[...] + self.bufs[0, k]
        if k == len(self.order) - 1:
            self.out[...] = total
        else:
            self.bufs[1, k] = total


def advance(stream, stage):
    if stage < len(stream.order):
        stream.copy(stage).wait()
        stream.absorb(stage)
        if stage < len(stream.order) - 1:
            stream.copy(stage + 1).start()


def bit_axes(shape):
    return [("dp", m) for m in bits_of(shape["dp"])] + [("blk", m) for m in bits_of(shape["blk"])]


def stream_scratch(lead, order, rows, cols):
    return [pltpu.VMEM((2,) * (lead - 1 - k) + (rows, cols), jnp.bfloat16) for k in range(len(order))]


def feed_weights(place, n2_ref, att_ref, act_ref, dg_ref, du_ref, ct_ref, db_ref, sums,
                 core_send, core_recv, gate, up, down, out, wide_out, slim_out, wide_in, slim_in):
    core_target = place.other_rest(1)
    per = gate.shape[0] // 32
    per_ff = down.shape[0] // 32
    first = sums[0].shape[2]
    half = out.shape[1] // 2
    core = place.rest % 2

    n2_t = n2_ref[...].T
    step = 512
    for j in range(gate.shape[1] // step):
        cols = slice(j * step, j * step + step)
        gate[:, cols] = mxu(n2_t, dg_ref[:, cols])
        up[:, cols] = mxu(n2_t, du_ref[:, cols])
    out[...] = mxu(att_ref[...].T, db_ref[...])

    def wide_rows(block):
        rows = pl.ds(pl.multiple_of(block * per, 8), per)
        last = jnp.concatenate([out[rows, :half], out[rows, half:]], axis=0)
        return jnp.concatenate([jnp.concatenate([gate[rows, :], up[rows, :]], axis=0), last], axis=1)

    def slim_rows(block):
        return down[pl.ds(pl.multiple_of(block * per_ff, 8), per_ff), :]

    def send_wide(m, _):
        wide_out[m] = wide_rows(2 * m + 1 - core).astype(jnp.bfloat16)
        return 0

    lax.fori_loop(0, 16, send_wide, 0)
    wide_copy = remote(wide_out, wide_in, core_send.at[0], core_recv.at[0], core_target)
    wide_copy.start()
    for j in range(down.shape[0] // step):
        rows = slice(j * step, j * step + step)
        down[rows, :] = mxu(act_ref[:, rows].T, ct_ref[...])

    def send_slim(m, _):
        slim_out[m] = slim_rows(2 * m + 1 - core).astype(jnp.bfloat16)
        return 0

    lax.fori_loop(0, 16, send_slim, 0)
    slim_copy = remote(slim_out, slim_in, core_send.at[1], core_recv.at[1], core_target)
    slim_copy.start()

    wide_copy.wait()

    def sum_wide(m, _):
        total = wide_rows(2 * m + core) + wide_in[m].astype(jnp.float32)
        sums[0][m] = total[:, :first].astype(jnp.bfloat16)
        sums[1][m] = total[:, first:].astype(jnp.bfloat16)
        return 0

    lax.fori_loop(0, 16, sum_wide, 0)
    slim_copy.wait()

    def sum_slim(m, _):
        sums[2][m] = (slim_rows(2 * m + core) + slim_in[m].astype(jnp.float32)).astype(jnp.bfloat16)
        return 0

    lax.fori_loop(0, 16, sum_slim, 0)


def reduce_kernel(shards, axes, orders, *refs):
    count = len(orders)
    q_ref, kv_ref = refs[:2]
    pairs = refs[2 : 2 + 2 * count]
    qo_ref, kvo_ref = refs[2 + 2 * count : 4 + 2 * count]
    sums = refs[4 + 2 * count : 4 + 3 * count]
    q_send, q_recv, send_sem, recv_sem, z_send, z_recv, w_send, w_recv = refs[4 + 3 * count : 12 + 3 * count]
    bufs = refs[12 + 3 * count :]
    place = Place(shards)
    rest_bits = bits_of(place.rest_size)
    greet(line_and_row(place) + [place.other_rest(mask) for mask in rest_bits])
    return_heads(place, q_ref, qo_ref, q_send, q_recv)
    ndim = 1 + len(rest_bits)
    at = {"dp": place.dp, "blk": place.blk}
    streams, used = [], ndim
    for s, (kept, order) in enumerate(orders):
        src, more = bufs[used], bufs[used + 1 : used + 1 + len(order)]
        used += 1 + len(order)
        streams.append(Stream(axes, at, kept, order, src, more, sums[s], w_send.at[s], w_recv.at[s]))
    own = [place.row] + [bit(place.rest, m) for m in rest_bits]
    targets = [place.other_row()] + [place.other_rest(m) for m in rest_bits]
    state = {}

    def plan(group_step):
        far = list(range(ndim - 1))
        turn = group_step % len(far)
        return [ndim - 1] + far[turn:] + far[:turn]

    def copy_of(step, stage):
        order = plan(step)
        group = (place.group + step) % GROUPS
        done = order[:stage]
        p_now = order[stage]
        buf = bufs[stage].at[step]
        if stage == 0:
            index = (p_index(group, done, p_now))
            src = kv_ref.at[index]
        else:
            kept = [p for p in range(ndim) if p not in done]
            src = bufs[stage - 1].at[(step,) + tuple(1 - own[p] if p == p_now else slice(None) for p in kept)]
        return remote(src, buf, send_sem.at[stage, step], recv_sem.at[stage, step], targets[p_now])

    def p_index(group, done, p_now):
        index = [slice(None)] * ndim
        index[p_now] = 1 - own[p_now]
        return (index[0], group) + tuple(index[1:])

    def absorb(step, stage):
        order = plan(step)
        done, p_now = order[:stage], order[stage]
        buf = bufs[stage].at[step]
        group = (place.group + step) % GROUPS
        if stage == 0:
            index = [None] * ndim
            index[p_now] = own[p_now]
            add_blocks(buf, kv_ref, (index[0], group) + tuple(index[1:]), buf.shape)
        else:
            kept = [p for p in range(ndim) if p not in done]
            index = tuple(own[p] if p == p_now else None for p in kept)
            add_blocks(buf, bufs[stage - 1].at[step], index, buf.shape)

    steps = (2, 1, 3, 0)
    for step in steps:
        copy_of(step, 0).start()
    for s, stream in enumerate(streams):
        add_two(stream.src, pairs[2 * s], pairs[2 * s + 1])
        stream.copy(0).start()
    for stage in range(ndim):
        for step in steps:
            copy_of(step, stage).wait()
            absorb(step, stage)
            if stage < ndim - 1:
                copy_of(step, stage + 1).start()
            elif step:
                remote(bufs[stage].at[step], kvo_ref.at[place.group], z_send.at[step], z_recv.at[(GROUPS - step) % GROUPS], place.other_group(step)).start()
            else:
                kvo_ref[place.group] = bufs[stage][step]
        for stream in streams:
            if stage < len(stream.order):
                stream.copy(stage).wait()
                stream.absorb(stage)
                if stage < len(stream.order) - 1:
                    stream.copy(stage + 1).start()
    for step in (1, 3, 2):
        there = kvo_ref.at[(place.group + step) % GROUPS]
        remote(bufs[ndim - 1].at[step], there, z_send.at[step], z_recv.at[step], place.other_group(step)).wait()
    return_heads_wait(place, q_ref, qo_ref, q_send, q_recv)


def add_two(dst_ref, one_ref, two_ref):
    lead = dst_ref.shape[:-2]

    def one(step, _):
        place, left = [], step
        for size in reversed(lead):
            place.append(left % size)
            left = left // size
        place = tuple(reversed(place))
        dst_ref[place] = (one_ref[place].astype(jnp.float32) + two_ref[place].astype(jnp.float32)).astype(dst_ref.dtype)
        return 0

    lax.fori_loop(0, math.prod(lead), one, 0)


def reduce_all(shape, q_packed, kv_sums, orders, pairs):
    shards = shape["blk"]
    tokens_all, width = kv_sums.shape[1:]
    tokens = tokens_all // shards
    rest_bits = bits_of(shards // GROUPS)
    ndim = 1 + len(rest_bits)
    sem = pltpu.SemaphoreType.DMA
    scratch = [pltpu.VMEM((GROUPS,) + (2,) * (ndim - 1 - s) + (tokens, width), kv_sums.dtype) for s in range(ndim)]
    flat, sums = [], []
    for (kept, order), pair in zip(orders, pairs):
        rows, cols = pair[0].shape[-2:]
        flat += [part.reshape((2,) * len(kept) + (rows, cols)) for part in pair]
        sums.append(jax.ShapeDtypeStruct((rows, cols), jnp.float32))
        scratch.append(pltpu.VMEM((2,) * len(kept) + (rows, cols), jnp.bfloat16))
        scratch += stream_scratch(len(kept), order, rows, cols)
    stages = max([len(order) for _, order in orders], default=1)
    return pl.pallas_call(
        functools.partial(reduce_kernel, shards, bit_axes(shape), orders),
        out_shape=(
            jax.ShapeDtypeStruct((GROUPS,) + q_packed.shape[2:], q_packed.dtype),
            jax.ShapeDtypeStruct((GROUPS, tokens, width), kv_sums.dtype),
        ) + tuple(sums),
        in_specs=[VMEM_SPEC] * (2 + len(flat)),
        out_specs=(VMEM_SPEC,) * (2 + len(sums)),
        scratch_shapes=[sem((4,)), sem((4,)), sem((ndim, GROUPS)), sem((ndim, GROUPS)), sem((GROUPS,)), sem((GROUPS,)),
                        sem((max(len(orders), 1), stages)), sem((max(len(orders), 1), stages))] + scratch,
        compiler_params=pltpu.CompilerParams(collective_id=2, has_side_effects=True, vmem_limit_bytes=VMEM_BYTES),
        name="reduce_keys",
    )(q_packed, kv_sums.reshape((2, GROUPS) + (2,) * len(rest_bits) + (tokens, width)), *flat)


TQ = 256
TK = 512
NEAR_ROWS = 448
NEG = -1e30
FIRST_MAX = -1e29
NT = (((1,), (1,)), ((), ()))
NN = (((1,), (0,)), ((), ()))
BORDERS = (12, 16, 23, 32, 46, 64, 91)


def mxu(left, right, dims=NN):
    return lax.dot_general(left, right, dims, preferred_element_type=jnp.float32)


def turned(tile):
    return jnp.concatenate([tile[:, 64:], tile[:, :64]], axis=1)


def spread_lanes(packed, high):
    lane = lax.broadcasted_iota(jnp.int32, (1, 128), 1)
    keep = lane >= 64 if high else lane < 64
    zero = jnp.zeros((), packed.dtype)
    pair, last = packed[0:TQ], packed[TQ:]
    pick = lambda tile: jnp.where(keep, tile, zero)
    if high:
        return [pick(turned(pair)), pick(pair), jnp.concatenate([pick(turned(last)), pick(last)], axis=0)]
    return [pick(pair), pick(turned(pair)), jnp.concatenate([pick(last), pick(turned(last))], axis=0)]


def join_heads(parts):
    half = TQ // 2
    top = jnp.concatenate([parts[0], parts[1]], axis=1)
    low = jnp.concatenate([parts[2][:half], parts[2][half:]], axis=1)
    return jnp.concatenate([top, low], axis=0)


def valid_mask(se_ref, r, i, k0):
    kpos = k0 + lax.broadcasted_iota(jnp.int32, (TK, TQ), 0)
    return jnp.logical_and(kpos >= se_ref[r, i, 0:1, :], kpos < se_ref[r, i, 1:2, :])


def near_buckets(first, rows, parity):
    relative = (
        first - TK + TQ * parity
        + lax.broadcasted_iota(jnp.int32, (rows, TQ), 0)
        - lax.broadcasted_iota(jnp.int32, (rows, TQ), 1)
    )
    return buckets_of(relative)


def make_bias(table, parity, near_ref, tiles=(0, 1)):
    heads = near_ref.shape[0]
    for tile in tiles:
        def rows(step, _):
            start = pl.multiple_of(step * 32, 32)
            place = tile * TK + start
            after = place - near_start(parity)
            inside = jnp.logical_and(after >= 0, after < NEAR_ROWS)

            @pl.when(inside)
            def _():
                which = near_buckets(place, 32, parity)
                for h in range(heads):
                    value = jnp.zeros((32, TQ), jnp.float32)
                    for b in range(BUCKETS):
                        value = jnp.where(which == b, table[h, b], value)
                    near_ref[h, tile, pl.ds(start, 32)] = value.astype(jnp.bfloat16)

            @pl.when(jnp.logical_not(inside))
            def _():
                for h in range(heads):
                    value = jnp.where(after < 0, table[h, 15], table[h, 31])
                    near_ref[h, tile, pl.ds(start, 32)] = jnp.full((32, TQ), value, jnp.float32).astype(jnp.bfloat16)

            return 0
        lax.fori_loop(0, TK // 32, rows, 0)


def tile_kind(bounds, r, i, t):
    slot = jnp.clip(t - bounds[r, i, 2] + 1, 0, 3)
    away = jnp.logical_or(slot == 0, slot == 3)
    inside = jnp.logical_and(t >= bounds[r, i, 3], t < bounds[r, i, 4])
    return slot, jnp.logical_and(away, inside)


def fwd_kernel(alone, bounds, table, q_ref, kv_hbm, se_ref, *refs):
    if alone:
        near_ref, o_in, keep_in, lse_in, o_ref, keep_ref, lse_ref, vt, acc, mx, qp, kv_ref, kv_sem = refs
    else:
        o_ref, keep_ref, lse_ref, near_ref, vt, acc, mx, qp, kv_ref, kv_sem = refs
        make_bias(table, bounds[0, 0, 5], near_ref)
    heads = lse_ref.shape[2]
    base = 1 - bounds[0, 0, 6] if alone else 0

    def row_body(at, _):
        r = base + at
        lo_all = jnp.minimum(bounds[r, 0, 0], bounds[r, 1, 0])
        hi_all = jnp.maximum(bounds[r, 0, 1], bounds[r, 1, 1])

        def fetch(t):
            rows = pl.ds(pl.multiple_of(t * TK, TK), TK)
            return pltpu.make_async_copy(kv_hbm.at[r, rows], kv_ref.at[rows], kv_sem.at[t])

        def begin(t, _):
            fetch(t).start()
            return 0

        lax.fori_loop(lo_all, hi_all, begin, 0)
        for i in range(2):
            for h, tile in enumerate(spread_lanes(q_ref[r, i], False)):
                qp[i, h] = tile

        def turn(t, _):
            fetch(t).wait()
            k0 = pl.multiple_of(t * TK, TK)
            for h in range(heads):
                tile = kv_ref[pl.ds(k0, TK), h * 128 : h * 128 + 128]
                vt[h, 0:64, pl.ds(k0, TK)] = tile.T[64:128, :]
                vt[h, 64:80, pl.ds(k0, TK)] = jnp.ones((16, TK), jnp.bfloat16)
            return 0

        lax.fori_loop(lo_all, hi_all, turn, 0)

        def q_body(i, _):
            acc[...] = jnp.zeros_like(acc)
            mx[...] = jnp.full_like(mx, FIRST_MAX)

            def tile_body(t, _):
                k0 = pl.multiple_of(t * TK, TK)
                slot, plain = tile_kind(bounds, r, i, t)
                near = jnp.logical_and(slot > 0, slot < 3)

                def scores(h):
                    return mxu(kv_ref[pl.ds(k0, TK), h * 128 : h * 128 + 128], qp[i, h], NT)

                def finish(h, s, b):
                    m_old = mx[h]
                    m_new = jnp.maximum(m_old, jnp.max(s, axis=0, keepdims=True) + b)
                    p = jnp.exp(s - (m_new - b)).astype(jnp.bfloat16)
                    mx[h] = m_new
                    acc[h] = acc[h] * jnp.exp(m_old - m_new) + mxu(vt[h, :, pl.ds(k0, TK)], p)

                @pl.when(plain)
                def _():
                    found = [scores(h) for h in range(heads)]
                    for h in range(heads):
                        finish(h, found[h], jnp.where(slot == 0, table[h, 15], table[h, 31]))

                @pl.when(near)
                def _():
                    ok = valid_mask(se_ref, r, i, k0)
                    for h in range(heads):
                        s = scores(h) + near_ref[h, slot - 1].astype(jnp.float32)
                        finish(h, jnp.where(ok, s, NEG), 0.0)

                @pl.when(jnp.logical_not(jnp.logical_or(plain, near)))
                def _():
                    ok = valid_mask(se_ref, r, i, k0)
                    for h in range(heads):
                        s = scores(h) + jnp.where(slot == 0, table[h, 15], table[h, 31])
                        finish(h, jnp.where(ok, s, NEG), 0.0)

                return 0

            lax.fori_loop(bounds[r, i, 0], bounds[r, i, 1], tile_body, 0)
            parts = []
            for h in range(heads):
                total = acc[h, 64:65, :]
                parts.append((acc[h, 0:64, :] / total).T)
                lse_ref[r, i, h] = mx[h] + jnp.log(total)
            joined = join_heads(parts)
            o_ref[r, i] = joined.astype(jnp.bfloat16)
            keep_ref[r, i] = joined
            return 0

        lax.fori_loop(0, 2, q_body, 0)
        return 0

    lax.fori_loop(0, 1 if alone else 2, row_body, 0)
    if alone:
        o_ref[1 - base] = o_in[...]
        keep_ref[1 - base] = keep_in[...]
        lse_ref[1 - base] = lse_in[...]


def attention(bounds, table, q, kv, se, ready=()):
    heads, n = kv.shape[2] // 128, kv.shape[1]
    packed = q.shape
    outs = [
        jax.ShapeDtypeStruct(packed, jnp.bfloat16),
        jax.ShapeDtypeStruct(packed, jnp.float32),
        jax.ShapeDtypeStruct((2, 2, heads, 1, TQ), jnp.float32),
    ]
    if not ready:
        outs.append(jax.ShapeDtypeStruct((heads, 2, TK, TQ), jnp.bfloat16))
    return pl.pallas_call(
        functools.partial(fwd_kernel, bool(ready)),
        out_shape=tuple(outs),
        in_specs=[SMEM_SPEC] * 2 + [VMEM_SPEC, ANY_SPEC, VMEM_SPEC] + [VMEM_SPEC] * len(ready),
        out_specs=(VMEM_SPEC,) * len(outs),
        scratch_shapes=[
            pltpu.VMEM((heads, 80, n), jnp.bfloat16),
            pltpu.VMEM((heads, 80, TQ), jnp.float32),
            pltpu.VMEM((heads, 1, TQ), jnp.float32),
            pltpu.VMEM((2, heads, TQ, 128), jnp.bfloat16),
            pltpu.VMEM(kv.shape[1:], jnp.bfloat16),
            pltpu.SemaphoreType.DMA((n // TK,)),
        ],
        compiler_params=pltpu.CompilerParams(vmem_limit_bytes=VMEM_BYTES),
        name="attention",
    )(bounds, table, q, kv, se, *ready)


def prepare(q, do, q_out, do_out):
    for h, tile in enumerate(spread_lanes(q, False)):
        q_out[h] = tile
    for h, tile in enumerate(spread_lanes(do, True)):
        do_out[h] = tile


def row_deltas(do, keep, delta):
    prod = (do.astype(jnp.float32) * keep).T
    top, low = prod[:, 0:TQ], prod[:, TQ:]
    delta[0] = jnp.sum(top[0:64], axis=0, keepdims=True)
    delta[1] = jnp.sum(top[64:128], axis=0, keepdims=True)
    delta[2] = jnp.concatenate(
        [jnp.sum(low[0:64], axis=0, keepdims=True), jnp.sum(low[64:128], axis=0, keepdims=True)], axis=1
    )


def near_start(parity):
    return 416 - TQ * parity


def far_sums(grid, h, first, end):
    def one(step, total):
        rows = grid[h, pl.ds(pl.multiple_of(step * 32, 32), 32)]
        return total + jnp.sum(rows.reshape(4, 8, TQ), axis=0)
    total = lax.fori_loop(first // 32, end // 32, one, jnp.zeros((8, TQ), jnp.float32))
    return jnp.sum(total, axis=0, keepdims=True)


def bucket_sums(parity, near, side, tab_ref, tab8):
    heads = near.shape[0]
    tab8[...] = jnp.zeros_like(tab8)

    def inner(step, _):
        start = pl.multiple_of(step * 32, 32)
        which = near_buckets(near_start(parity) + start, 32, parity)
        for b in range(BUCKETS):
            here = which == b
            for h in range(heads):
                rows = jnp.where(here, near[h, pl.ds(start, 32)], 0.0)
                tab8[h, b] += jnp.sum(rows.reshape(4, 8, TQ), axis=0)
        return 0

    lax.fori_loop(0, NEAR_ROWS // 32, inner, 0)
    for h in range(heads):
        tab_ref[h] = jnp.sum(tab8[h], axis=1)
        tab_ref[h, 15:16] += side[h, 0:1]
        tab_ref[h, 31:32] += side[h, 1:2]


def bwd_kernel(alone, bounds, table, q_ref, do_ref, keep_ref, kv_hbm, bias_ref, se_ref, lse_ref,
               dq_ref, dkv_ref, near_ref, side, delta, *rest):
    tab_ref, tab8, rest = (None, None, rest) if alone else (rest[0], rest[-1], rest[1:-1])
    kt, dqt, dkv, grid, qp, dp_ref, kv_ref, kv_sem = rest
    heads = lse_ref.shape[2]
    n = kv_hbm.shape[1]
    grid[...] = jnp.zeros_like(grid)
    side[...] = jnp.zeros_like(side)
    base = 1 - bounds[0, 0, 6] if alone else 0
    for at in range(1 if alone else 2):
        for i in range(2):
            prepare(q_ref[base + at, i], do_ref[base + at, i], qp.at[at, i], dp_ref.at[at, i])
    for r in range(2):
        for i in range(2):
            row_deltas(do_ref[r, i], keep_ref[r, i], delta.at[r, i])

    def row_body(at, _):
        r = base + at
        lo_all = jnp.minimum(bounds[r, 0, 0], bounds[r, 1, 0])
        hi_all = jnp.maximum(bounds[r, 0, 1], bounds[r, 1, 1])

        def fetch(t):
            rows = pl.ds(pl.multiple_of(t * TK, TK), TK)
            return pltpu.make_async_copy(kv_hbm.at[r, rows], kv_ref.at[rows], kv_sem.at[t])

        def begin(t, _):
            fetch(t).start()
            return 0

        lax.fori_loop(lo_all, hi_all, begin, 0)

        def clear(t, _):
            k0 = pl.multiple_of(t * TK, TK)
            for h in range(heads):
                dkv[h, pl.ds(k0, TK), :] = jnp.zeros((TK, 128), jnp.float32)
            return 0

        lax.fori_loop(0, n // TK, clear, 0)

        def turn(t, _):
            fetch(t).wait()
            k0 = pl.multiple_of(t * TK, TK)
            for h in range(heads):
                tile = kv_ref[pl.ds(k0, TK), h * 128 : h * 128 + 128]
                kt[h, 0:64, pl.ds(k0, TK)] = tile.T[0:64, :]
                kt[h, 64:80, pl.ds(k0, TK)] = jnp.ones((16, TK), jnp.bfloat16)
            return 0

        lax.fori_loop(lo_all, hi_all, turn, 0)

        def q_body(i, _):
            dqt[...] = jnp.zeros_like(dqt)

            def tile_body(t, _):
                k0 = pl.multiple_of(t * TK, TK)
                slot, plain = tile_kind(bounds, r, i, t)

                def finish(h, p, ds, where):
                    ds_low = ds.astype(jnp.bfloat16)
                    two = jnp.concatenate([ds_low, p.astype(jnp.bfloat16)], axis=1)
                    both = jnp.concatenate([qp[at, i, h], dp_ref[at, i, h]], axis=0)
                    dkv[h, pl.ds(k0, TK), :] += mxu(two, both)
                    dqt[h, where] += mxu(kt[h, :, pl.ds(k0, TK)], ds_low)

                def products(h):
                    tile = kv_ref[pl.ds(k0, TK), h * 128 : h * 128 + 128]
                    return mxu(tile, qp[at, i, h], NT), mxu(tile, dp_ref[at, i, h], NT)

                @pl.when(plain)
                def _():
                    for h in range(heads):
                        s, d_probs = products(h)
                        p = jnp.exp(s - (lse_ref[r, i, h] - jnp.where(slot == 0, table[h, 15], table[h, 31])))
                        finish(h, p, p * (d_probs - delta[r, i, h]), jnp.where(slot == 0, 0, 2))

                def general(bias):
                    ok = valid_mask(se_ref, r, i, k0)
                    for h in range(heads):
                        s, d_probs = products(h)
                        s = s + bias(h)
                        p = jnp.where(ok, jnp.exp(jnp.where(ok, s, NEG) - lse_ref[r, i, h]), 0.0)
                        ds = p * (d_probs - delta[r, i, h])
                        grid[h, pl.ds(pl.multiple_of(slot * TK, TK), TK)] += ds
                        finish(h, p, ds, 1)

                near = jnp.logical_and(slot > 0, slot < 3)
                pl.when(near)(lambda: general(lambda h: bias_ref[h, slot - 1].astype(jnp.float32)))
                away = jnp.logical_not(jnp.logical_or(plain, near))
                pl.when(away)(lambda: general(lambda h: jnp.where(slot == 0, table[h, 15], table[h, 31])))
                return 0

            lax.fori_loop(bounds[r, i, 0], bounds[r, i, 1], tile_body, 0)
            parts = []
            for h in range(heads):
                parts.append((dqt[h, 0, 0:64] + dqt[h, 1, 0:64] + dqt[h, 2, 0:64]).T * 0.125)
                side[h, 0:1] += dqt[h, 0, 64:65]
                side[h, 1:2] += dqt[h, 2, 64:65]
            dq_ref[at, i] = join_heads(parts).astype(jnp.bfloat16)
            return 0

        lax.fori_loop(0, 2, q_body, 0)

        def put(t, _):
            k0 = pl.multiple_of(t * TK, TK)
            for h in range(heads):
                dkv_ref[at, pl.ds(k0, TK), h * 128 : h * 128 + 128] = dkv[h, pl.ds(k0, TK), :].astype(jnp.bfloat16)
            return 0

        lax.fori_loop(0, n // TK, put, 0)
        return 0

    lax.fori_loop(0, 1 if alone else 2, row_body, 0)

    parity = bounds[0, 0, 5]
    first = TK + near_start(parity)
    for h in range(heads):
        near_ref[h] = grid[h, pl.ds(pl.multiple_of(first, 32), NEAR_ROWS)]
        side[h, 0:1] += far_sums(grid, h, 0, first)
        side[h, 1:2] += far_sums(grid, h, first + NEAR_ROWS, 4 * TK)
    if not alone:
        bucket_sums(parity, near_ref, side, tab_ref, tab8)


def attention_back(alone, bounds, table, q, do, keep, kv, bias, se, lse):
    heads, n = kv.shape[2] // 128, kv.shape[1]
    count = 1 if alone else 2
    table_out = [] if alone else [jax.ShapeDtypeStruct((heads, BUCKETS, TQ), jnp.float32)]
    return pl.pallas_call(
        functools.partial(bwd_kernel, alone),
        out_shape=(
            jax.ShapeDtypeStruct((count,) + q.shape[1:], jnp.bfloat16),
            jax.ShapeDtypeStruct((count,) + kv.shape[1:], jnp.bfloat16),
            jax.ShapeDtypeStruct((heads, NEAR_ROWS, TQ), jnp.float32),
            jax.ShapeDtypeStruct((heads, 2, TQ), jnp.float32),
            jax.ShapeDtypeStruct((2, 2, heads, 1, TQ), jnp.float32),
        ) + tuple(table_out),
        in_specs=[SMEM_SPEC] * 2 + [VMEM_SPEC] * 3 + [ANY_SPEC] + [VMEM_SPEC] * 3,
        out_specs=(VMEM_SPEC,) * (5 + len(table_out)),
        scratch_shapes=[
            pltpu.VMEM((heads, 80, n), jnp.bfloat16),
            pltpu.VMEM((heads, 3, 80, TQ), jnp.float32),
            pltpu.VMEM((heads, n, 128), jnp.float32),
            pltpu.VMEM((heads, 4 * TK, TQ), jnp.float32),
            pltpu.VMEM((count, 2, heads, TQ, 128), jnp.bfloat16),
            pltpu.VMEM((count, 2, heads, TQ, 128), jnp.bfloat16),
            pltpu.VMEM(kv.shape[1:], jnp.bfloat16),
            pltpu.SemaphoreType.DMA((n // TK,)),
        ] + [pltpu.VMEM((heads, BUCKETS, 8, TQ), jnp.float32) for _ in table_out],
        compiler_params=pltpu.CompilerParams(vmem_limit_bytes=VMEM_BYTES),
        name="attention_back",
    )(bounds, table, q, do, keep, kv, bias, se, lse)


TAPS = tuple(range(-3, 5))
LEAD = 8


def pool_scalars(y_rows, lab_rows, first):
    tokens = y_rows[0].shape[1]
    t = lax.broadcasted_iota(jnp.int32, (1, tokens), 1)
    at = lambda rows, k: rows[k + 3]
    found = []
    for p in range(2):
        inside = {1: 0 * t, 2: 0 * t + p, 3: (first + 2 * t + p) % 3, 4: 2 * (t % 2) + p}
        weights, scores = {}, []
        for b in range(1, MAX_BLOCK + 1):
            keep = {}
            for o in range(1 - b, b):
                same = jnp.logical_and(inside[b] + o >= 0, inside[b] + o < b)
                same = jnp.logical_and(same, at(lab_rows, p + o) == at(lab_rows, p))
                keep[o] = same.astype(jnp.float32)
            inverse = 1.0 / sum(keep.values())
            for o in keep:
                weights[b, o] = keep[o] * inverse
            scores.append(sum(weights[b, o] * at(y_rows, p + o) for o in keep))
        top = functools.reduce(jnp.maximum, scores)
        grown = [jnp.exp(s - top) for s in scores]
        total = sum(grown)
        found.append(([g / total for g in grown], weights))
    return found


def tap_weights(found):
    rows = []
    for k in TAPS:
        row = 0.0
        for p, (probs, weights) in enumerate(found):
            for b in range(1, MAX_BLOCK + 1):
                if (b, k - p) in weights:
                    row = row + probs[b - 1] * weights[b, k - p]
        rows.append(0.5 * row)
    return rows


def as_columns(rows):
    tokens = rows[0].shape[1]
    return jnp.concatenate(list(rows) + [jnp.zeros((128 - len(rows), tokens), jnp.float32)], axis=0).T


def load_bytes(x_ref, before_ref, after_ref, xs):
    length, width = x_ref.shape
    for j in range(width // 128):
        cols = slice(j * 128, j * 128 + 128)
        xs[j, 0:LEAD, :] = jnp.zeros((LEAD, 128), jnp.float32)
        xs[j, LEAD + length :, :] = jnp.zeros((LEAD, 128), jnp.float32)
        xs[j, LEAD - 2 : LEAD, :] = before_ref[0:2, cols].astype(jnp.float32)
        xs[j, LEAD + length : LEAD + length + 2, :] = after_ref[0:2, cols].astype(jnp.float32)
        xs[j, LEAD : LEAD + length, :] = x_ref[:, cols].astype(jnp.float32)


def tap(xs, k, tokens):
    return jnp.concatenate([xs[j, pl.ds(LEAD + k, tokens, stride=2), :] for j in range(xs.shape[0])], axis=1)


def strips(buf, first, rows):
    return jnp.concatenate([buf[j, first : first + rows, :] for j in range(buf.shape[0])], axis=1)


def unit_rows(values):
    return lax.rsqrt(jnp.mean(values * values, axis=-1, keepdims=True) + 1e-06)


def pool_kernel(shards, scale, x_ref, before_ref, after_ref, lab_ref, score_ref, gain_ref, wq_ref, wk_ref, wv_ref,
                hidden_ref, n1_ref, y_ref, share_ref, q_ref, kv_ref, xs):
    tokens = hidden_ref.shape[0]
    width = hidden_ref.shape[1]
    load_bytes(x_ref, before_ref, after_ref, xs)
    score = jnp.broadcast_to(score_ref[...], (8, width))
    for k in TAPS:
        y_ref[k + 3 : k + 4, :] = mxu(score, tap(xs, k, tokens).astype(jnp.bfloat16), NT)[0:1]
    rows = [y_ref[j : j + 1, :] for j in range(8)]
    labels = [lab_ref[j : j + 1, :] for j in range(8)]
    first = (lax.axis_index("blk") * x_ref.shape[0]) % 3
    found = pool_scalars(rows, labels, first)
    lane = lax.broadcasted_iota(jnp.int32, (1, 128), 1)
    share = jnp.zeros((1, 128), jnp.float32)
    for b in range(MAX_BLOCK):
        share = jnp.where(lane == b, jnp.sum(found[0][0][b] + found[1][0][b], axis=1, keepdims=True) * scale, share)
    share_ref[...] = share
    columns = as_columns(tap_weights(found))
    hidden = sum(columns[:, k + 3 : k + 4] * tap(xs, k, tokens) for k in TAPS)
    hidden_ref[...] = hidden
    n1 = (hidden * unit_rows(hidden) * gain_ref[...].astype(jnp.float32)).astype(jnp.bfloat16)
    n1_ref[...] = n1
    keys = mxu(n1, wk_ref[...]).astype(jnp.bfloat16)
    values = mxu(n1, wv_ref[...]).astype(jnp.bfloat16)
    low = lane < 64
    for j in range(width // 128):
        k_pair, v_pair = keys[:, j * 128 : j * 128 + 128], values[:, j * 128 : j * 128 + 128]
        one = jnp.where(low, k_pair, turned(v_pair))
        two = jnp.where(low, turned(k_pair), v_pair)
        for head, tile in ((2 * j, one), (2 * j + 1, two)):
            kv_ref[head // 3, :, head % 3 * 128 : head % 3 * 128 + 128] = tile
    queries = mxu(n1, wq_ref[...]).astype(jnp.bfloat16) * jnp.bfloat16(0.125)
    put_packed(queries, q_ref)


def put_packed(array, out_ref):
    tokens = array.shape[0]
    half = tokens // 2
    for g in range(GROUPS):
        part = array[:, g * 192 : g * 192 + 192]
        out_ref[g, 0:tokens, :] = part[:, 0:128]
        out_ref[g, tokens:, :] = jnp.concatenate([part[:half, 128:], part[half:, 128:]], axis=1)


def get_packed(packed_ref):
    tokens = packed_ref.shape[1] * 2 // 3
    parts = []
    for g in range(GROUPS):
        last = packed_ref[g, tokens:, :]
        parts += [packed_ref[g, 0:tokens, :], jnp.concatenate([last[:, :64], last[:, 64:]], axis=0)]
    return jnp.concatenate(parts, axis=1)


def pool_and_project(shards, scale, x, before, after, labels, score, gain, wq, wk, wv):
    length, width = x.shape
    tokens = length // 2
    return pl.pallas_call(
        functools.partial(pool_kernel, shards, scale),
        out_shape=(
            jax.ShapeDtypeStruct((tokens, width), jnp.float32),
            jax.ShapeDtypeStruct((tokens, width), jnp.bfloat16),
            jax.ShapeDtypeStruct((8, tokens), jnp.float32),
            jax.ShapeDtypeStruct((1, 128), jnp.float32),
            jax.ShapeDtypeStruct((GROUPS, tokens * 3 // 2, 128), jnp.bfloat16),
            jax.ShapeDtypeStruct((GROUPS, tokens, width * 2 // GROUPS), jnp.bfloat16),
        ),
        in_specs=[VMEM_SPEC] * 9,
        out_specs=(VMEM_SPEC,) * 6,
        scratch_shapes=[pltpu.VMEM((width // 128, length + 2 * LEAD, 128), jnp.float32)],
        compiler_params=pltpu.CompilerParams(vmem_limit_bytes=VMEM_BYTES),
        name="pool_and_project",
    )(x, before, after, labels, score, gain, wq, wk, wv)


GELU_A = math.sqrt(2.0 / math.pi)
GELU_B = 0.044715


def norm_back(d_out, rows, gain):
    unit = unit_rows(rows)
    flat = rows * unit
    scaled = d_out * gain
    d_rows = unit * (scaled - flat * jnp.mean(scaled * flat, axis=-1, keepdims=True))
    return d_rows, jnp.sum(d_out * flat, axis=0, keepdims=True)


def feed_kernel(o_ref, hidden_ref, ct_ref, gain_ref, wo_ref, wg_ref, wu_ref, wd_ref,
                out_ref, dres_ref, da_ref, dgain_ref, n2_ref, att_ref, act_ref, dg_ref, du_ref, db_ref, acc, dn2):
    ff = wg_ref.shape[1]
    step = 512
    att = get_packed(o_ref)
    att_ref[...] = att
    residual = hidden_ref[...] + mxu(att, wo_ref[...])
    gain = gain_ref[...].astype(jnp.float32)
    n2_ref[...] = (residual * unit_rows(residual) * gain).astype(jnp.bfloat16)
    acc[...] = residual
    dn2[...] = jnp.zeros_like(dn2)

    for j in range(ff // step):
        cols = slice(j * step, j * step + step)
        n2 = n2_ref[...]
        gate = mxu(n2, wg_ref[:, cols])
        up = mxu(n2, wu_ref[:, cols])
        d_act = mxu(ct_ref[...], wd_ref[cols, :], NT)
        square = gate * gate
        curve = jnp.tanh(GELU_A * gate * (1.0 + GELU_B * square))
        half = 0.5 * (1.0 + curve)
        grown = gate * half
        slope = half + 0.5 * gate * (1.0 - curve * curve) * (GELU_A * (1.0 + 3.0 * GELU_B * square))
        act = (grown * up).astype(jnp.bfloat16)
        d_gate = (d_act * up * slope).astype(jnp.bfloat16)
        d_up = (d_act * grown).astype(jnp.bfloat16)
        act_ref[:, cols] = act
        dg_ref[:, cols] = d_gate
        du_ref[:, cols] = d_up
        acc[...] += mxu(act, wd_ref[cols, :])
        dn2[...] += mxu(d_gate, wg_ref[:, cols], NT) + mxu(d_up, wu_ref[:, cols], NT)

    out_ref[...] = acc[...].astype(jnp.bfloat16)
    residual = hidden_ref[...] + mxu(att_ref[...], wo_ref[...])
    d_rows, d_gain = norm_back(dn2[...], residual, gain)
    dgain_ref[...] = d_gain
    d_res = ct_ref[...].astype(jnp.float32) + d_rows
    dres_ref[...] = d_res
    d_branch = d_res.astype(jnp.bfloat16)
    db_ref[...] = d_branch
    put_packed(mxu(d_branch, wo_ref[...], NT).astype(jnp.bfloat16), da_ref)


def feed_forward(o_home, hidden, ct, gain, wo, wg, wu, wd):
    tokens, width = hidden.shape
    ff = wg.shape[1]
    low = lambda cols: jax.ShapeDtypeStruct((tokens, cols), jnp.bfloat16)
    return pl.pallas_call(
        feed_kernel,
        out_shape=(
            low(width),
            jax.ShapeDtypeStruct((tokens, width), jnp.float32),
            jax.ShapeDtypeStruct(o_home.shape, jnp.bfloat16),
            jax.ShapeDtypeStruct((1, width), jnp.float32),
            low(width), low(width), low(ff), low(ff), low(ff), low(width),
        ),
        in_specs=[VMEM_SPEC] * 8,
        out_specs=(VMEM_SPEC,) * 10,
        scratch_shapes=[pltpu.VMEM((tokens, width), jnp.float32)] * 2,
        compiler_params=pltpu.CompilerParams(vmem_limit_bytes=VMEM_BYTES),
        name="feed_forward",
    )(o_home, hidden, ct, gain, wo, wg, wu, wd)


def unpack_pairs(dkv_ref, width):
    low = lax.broadcasted_iota(jnp.int32, (1, 128), 1) < 64
    dk_parts, dv_parts = [], []
    for j in range(width // 128):
        one, two = [dkv_ref[h // 3, :, h % 3 * 128 : h % 3 * 128 + 128] for h in (2 * j, 2 * j + 1)]
        dk_parts.append(jnp.where(low, one, turned(two)))
        dv_parts.append(jnp.where(low, turned(one), two))
    return jnp.concatenate(dk_parts, axis=1), jnp.concatenate(dv_parts, axis=1)


def pool_back(d_hidden, x_refs, lab_ref, y_ref, score_ref, gb_ref, edge_ref, spill_ref, xs, gbuf):
    x_ref = x_refs[0]
    tokens, width = d_hidden.shape
    length = x_ref.shape[0]
    lane = lax.broadcasted_iota(jnp.int32, (1, 128), 1)
    met = jnp.zeros((tokens, 128), jnp.float32)
    for k in TAPS:
        met = jnp.where(lane == k + 3, jnp.sum(d_hidden * tap(xs, k, tokens), axis=-1, keepdims=True), met)
    met = met.T
    first = (lax.axis_index("blk") * length) % 3
    found = pool_scalars([y_ref[j : j + 1, :] for j in range(8)], [lab_ref[j : j + 1, :] for j in range(8)], first)
    touch = [0.0] * 8
    for p, (probs, weights) in enumerate(found):
        d_block = []
        for b in range(1, MAX_BLOCK + 1):
            d_block.append(0.5 * sum(weights[b, o] * met[p + o + 3 : p + o + 4] for o in range(1 - b, b)))
        mean = sum(q * d for q, d in zip(probs, d_block))
        for b in range(1, MAX_BLOCK + 1):
            d_score = probs[b - 1] * (d_block[b - 1] - mean)
            for o in range(1 - b, b):
                touch[p + o + 3] = touch[p + o + 3] + d_score * weights[b, o]
    share_cols = as_columns(tap_weights(found) + touch)
    score = score_ref[...].astype(jnp.float32)
    gbuf[...] = jnp.zeros_like(gbuf)
    d_score_vec = jnp.zeros((1, width), jnp.float32)
    for k in TAPS:
        own, via = share_cols[:, k + 3 : k + 4], share_cols[:, k + 11 : k + 12]
        added = own * d_hidden + via * score
        for j in range(gbuf.shape[0]):
            gbuf[j, pl.ds(LEAD + k, tokens, stride=2), :] += added[:, j * 128 : j * 128 + 128]
        d_score_vec = d_score_vec + jnp.sum(via * tap(xs, k, tokens), axis=0, keepdims=True)
    gb_ref[...] = strips(gbuf, LEAD, length).astype(jnp.bfloat16)
    edge_ref[0] = strips(gbuf, LEAD, 16)
    edge_ref[1] = strips(gbuf, LEAD + length - 16, 16)
    spill_ref[0] = strips(gbuf, 0, LEAD)
    spill_ref[1] = strips(gbuf, LEAD + length, LEAD)
    return d_score_vec


def put_small(small_ref, vectors, tab_ref, share_ref):
    small_ref[...] = jnp.zeros_like(small_ref)
    for row, vector in zip((0, 6, 12), vectors):
        for j in range(6):
            small_ref[row + j : row + j + 1, :] = vector[:, j * 128 : j * 128 + 128]
    heads = tab_ref.shape[0]
    group = lax.axis_index("blk") // (lax.axis_size("blk") // GROUPS)
    for h in range(heads):
        total = lax.dot_general(
            jnp.ones((8, tab_ref.shape[2]), jnp.float32), tab_ref[h], NT,
            precision=lax.Precision.HIGHEST, preferred_element_type=jnp.float32,
        )
        small_ref[pl.ds(18 + group * heads + h, 1), 0:BUCKETS] = total[0:1]
    small_ref[30:31, :] = share_ref[...]


def last_kernel(shards, axes, order, dq_ref, dkv_ref, hidden_ref, dres_ref, x_ref, before_ref, after_ref, lab_ref, y_ref, score_ref,
                gain_ref, wq_ref, wk_ref, wv_ref, dgain2_ref, share_ref, tab_ref, gb_ref, edge_ref, spill_out, small_out, parts_ref,
                w_send, w_recv, s_send, s_recv, xs, gbuf, spill_ref, small_ref, small_bufs):
    at = {"dp": lax.axis_index("dp"), "blk": lax.axis_index("blk")}
    width = hidden_ref.shape[1]
    whole = Whole(axes, at, order, small_ref, small_bufs, small_out, w_send, w_recv)
    left = (at["dp"], (at["blk"] + shards - 1) % shards)
    right = (at["dp"], (at["blk"] + 1) % shards)
    greet([whole.stream.target(p) for p in range(len(axes))] + [left, right])
    load_bytes(x_ref, before_ref, after_ref, xs)
    dq = get_packed(dq_ref)
    dk, dv = unpack_pairs(dkv_ref, width)
    parts_ref[0], parts_ref[1], parts_ref[2] = dq, dk, dv
    d_n1 = mxu(dq, wq_ref[...], NT) + mxu(dk, wk_ref[...], NT) + mxu(dv, wv_ref[...], NT)
    d_rows, d_gain1 = norm_back(d_n1, hidden_ref[...], gain_ref[...].astype(jnp.float32))
    d_hidden = dres_ref[...] + d_rows
    d_score = pool_back(d_hidden, (x_ref, before_ref, after_ref), lab_ref, y_ref, score_ref, gb_ref, edge_ref, spill_ref, xs, gbuf)
    put_small(small_ref, (d_score, d_gain1, dgain2_ref[...]), tab_ref, share_ref)
    spills = [
        remote(spill_ref.at[0], spill_out.at[1], s_send.at[0], s_recv.at[1], left),
        remote(spill_ref.at[1], spill_out.at[0], s_send.at[1], s_recv.at[0], right),
    ]
    whole.copy(0).start()
    for copy in spills:
        copy.start()
    for stage in range(len(axes)):
        advance(whole, stage)
    for copy in spills:
        copy.wait()


def last_part(shape, dq, dkv, hidden, dres, x, before, after, labels, y, score, gain, wq, wk, wv, dgain2, share, tab):
    tokens, width = hidden.shape
    length = x.shape[0]
    axes = bit_axes(shape)
    ndim = len(axes)
    full, sem, low = jax.ShapeDtypeStruct, pltpu.SemaphoreType.DMA, jnp.bfloat16
    strip = pltpu.VMEM((width // 128, length + 2 * LEAD, 128), jnp.float32)
    return pl.pallas_call(
        functools.partial(last_kernel, shape["blk"], axes, tuple(reversed(range(ndim)))),
        out_shape=(
            full((length, width), low),
            full((2, 16, width), jnp.float32),
            full((2, LEAD, width), jnp.float32),
            full((32, 128), jnp.float32),
            full((3, tokens, width), low),
        ),
        in_specs=[VMEM_SPEC] * 17,
        out_specs=(VMEM_SPEC,) * 5,
        scratch_shapes=[
            sem((ndim,)), sem((ndim,)), sem((2,)), sem((2,)), strip, strip,
            pltpu.VMEM((2, LEAD, width), jnp.float32), pltpu.VMEM((32, 128), jnp.float32), pltpu.VMEM((2, ndim, 32, 128), jnp.float32),
        ],
        compiler_params=pltpu.CompilerParams(collective_id=3, has_side_effects=True, vmem_limit_bytes=VMEM_BYTES),
        name="last_part",
    )(dq, dkv, hidden, dres, x, before, after, labels, y, score, gain, wq, wk, wv, dgain2, share, tab)


def finish_kernel(shards, heads_all, gb_ref, edge_ref, spill_ref, small_ref, *refs):
    position = lax.axis_index("blk")
    streams, outs = refs[: len(refs) - (5 if len(refs) == 5 else 12)], refs[len(refs) - (5 if len(refs) == 5 else 12) :]
    bytes_ref, score_ref, gain1_ref, gain2_ref, tab_ref = outs[:5]
    length = gb_ref.shape[0]
    bytes_ref[...] = gb_ref[...]
    zero = jnp.zeros((16 - LEAD, gb_ref.shape[1]), jnp.float32)
    left = jnp.where(position > 0, spill_ref[0], 0.0)
    right = jnp.where(position < shards - 1, spill_ref[1], 0.0)
    bytes_ref[0:16, :] = (edge_ref[0] + jnp.concatenate([left, zero], axis=0)).astype(jnp.bfloat16)
    bytes_ref[length - 16 :, :] = (edge_ref[1] + jnp.concatenate([zero, right], axis=0)).astype(jnp.bfloat16)
    for row, ref in ((0, score_ref), (6, gain1_ref), (12, gain2_ref)):
        for j in range(6):
            ref[j * 128 : j * 128 + 128] = small_ref[row + j, :]
    tab_ref[...] = small_ref[16:32, :]
    if streams:
        gq, gk, gv, go, gg, gu, gd = outs[5:]
        per, width = gq.shape
        half, ff = width // 2, gg.shape[1]
        one, two, down, *thirds = streams
        for ref, third in zip((gq, gk, gv), thirds):
            ref[:, :half] = third[:per, :]
            ref[:, half:] = third[per:, :]
        first = one.shape[1]
        for ref, rows in ((gg, slice(0, per)), (gu, slice(per, 2 * per))):
            ref[:, :first] = one[rows, :]
            ref[:, first:] = two[rows, : ff - first]
        go[:, :half] = two[:per, ff - first :]
        go[:, half:] = two[per:, ff - first :]
        gd[...] = down[...]


def finish(shards, heads_all, per, ff, gb, edge, spill, small, streams):
    width = gb.shape[1]
    full = jax.ShapeDtypeStruct
    line = full((width,), jnp.float32)
    outs = [full(gb.shape, jnp.bfloat16), line, line, line, full((16, 128), jnp.float32)]
    if streams:
        square, broad = full((per, width), jnp.float32), full((per, ff), jnp.float32)
        outs += [square] * 4 + [broad] * 2 + [full((streams[2].shape[0], width), jnp.float32)]
    return pl.pallas_call(
        functools.partial(finish_kernel, shards, heads_all),
        out_shape=tuple(outs),
        in_specs=[VMEM_SPEC] * (4 + len(streams)),
        out_specs=(VMEM_SPEC,) * len(outs),
        compiler_params=pltpu.CompilerParams(vmem_limit_bytes=VMEM_BYTES),
        name="finish",
    )(gb, edge, spill, small, *streams)


class NearRows:
    def __init__(self, grid, first):
        self.grid, self.first, self.shape = grid, first, grid.shape

    def __getitem__(self, index):
        h, rows = index
        return self.grid[h, pl.ds(pl.multiple_of(self.first + rows.start, 32), rows.size)]


class Refs:
    def __init__(self, **refs):
        self.__dict__.update(refs)


class Held:
    def __init__(self, array, space):
        self.array, self.space = array, space


def call(kernel, ident, ins, outs, scratch):
    leaf = lambda entry: isinstance(entry, Held) or isinstance(entry, tuple) or not isinstance(entry, (dict, list))
    parts = [jax.tree.flatten(part, is_leaf=leaf) for part in (ins, outs, scratch)]
    counts = [len(part[0]) for part in parts]
    given, wanted, kept = [part[0] for part in parts]

    def run(*refs):
        named, start = {}, 0
        for count, (_, tree) in zip(counts, parts):
            named.update(jax.tree.unflatten(tree, refs[start : start + count]))
            start += count
        kernel(Refs(**named))

    space = lambda entry, at: entry.space if isinstance(entry, Held) else entry[2] if isinstance(entry, tuple) and len(entry) > 2 else at
    found = pl.pallas_call(
        run,
        out_shape=tuple(jax.ShapeDtypeStruct(entry[0], entry[1]) for entry in wanted),
        in_specs=[pl.BlockSpec(memory_space=space(entry, pltpu.VMEM)) for entry in given],
        out_specs=tuple(pl.BlockSpec(memory_space=space(entry, pltpu.VMEM)) for entry in wanted),
        scratch_shapes=kept,
        compiler_params=pltpu.CompilerParams(collective_id=ident, has_side_effects=True, vmem_limit_bytes=VMEM_BYTES),
        name=kernel.func.__name__,
    )(*[entry.array if isinstance(entry, Held) else entry for entry in given])
    return Refs(**jax.tree.unflatten(parts[1][1], found))


wide = lambda value: value.astype(jnp.float32)
slim = lambda value: value.astype(jnp.bfloat16)


class RowBack:
    def __init__(self, place, r):
        self.place, self.r = place, r
        self.heads = r.lse.shape[1]
        self.tokens = TQ
        self.across, self.core_to = place.other_rest(2), place.other_rest(1)
        self.y, self.core = bit(place.rest, 2), place.rest % 2

    def group_of(self, n):
        return (self.place.group + 1 + n) % GROUPS

    def tile_start(self, m):
        place_y = jnp.where(m % 2 == 0, 1 - self.y, self.y)
        return pl.multiple_of((self.group_of(m // 2) * 2 + place_y) * TK, TK)

    def fetch(self, m):
        r = self.r
        rows = pl.ds(self.tile_start(m), TK)
        return (
            pltpu.make_async_copy(r.kv_hbm.at[rows], r.kv.at[m], r.kv_sem.at[m]),
            pltpu.make_async_copy(r.kl_hbm.at[rows], r.kl.at[m], r.kl_sem.at[m]),
        )

    def prepare(self):
        r = self.r
        for m in range(2 * GROUPS):
            for copy in self.fetch(m):
                copy.start()

        def one(i, _):
            for h, tile in enumerate(spread_lanes(r.q[i], False)):
                r.qp[i, h] = tile
            for h, tile in enumerate(spread_lanes(r.do[i], True)):
                r.dp[i, h] = tile
            row_deltas(r.do[i], r.keep[i], r.delta.at[i])
            return 0

        lax.fori_loop(0, GROUPS, one, 0)
        r.dqt[...] = jnp.zeros_like(r.dqt)
        r.grid[...] = jnp.zeros_like(r.grid)

    def core_copy(self, n, j):
        r = self.r
        return remote(r.held.at[n, j, 1 - self.core], r.core_in.at[n, j], r.core_send.at[n, j], r.core_recv.at[n, j], self.core_to)

    def y_copy(self, n):
        r = self.r
        return remote(r.y_out.at[n], r.y_in.at[n], r.y_send.at[n], r.y_recv.at[n], self.across)

    def z_copy(self, n):
        r, place = self.r, self.place
        return remote(r.z_out.at[n], r.dkv_home.at[place.group], r.z_send.at[n], r.z_recv.at[n], place.at(place.row, self.group_of(n), place.rest))

    def by_rows(self, one):
        def step(k, _):
            one(pl.ds(pl.multiple_of(k * 32, 32), 32))
            return 0
        lax.fori_loop(0, self.tokens // 32, step, 0)

    def own_sum(self, n, j, rows):
        return wide(self.r.held[n, j, self.core, rows]) + wide(self.r.core_in[n, j, rows])

    def send_y(self, n):
        r = self.r
        self.core_copy(n, 0).wait()

        def one(rows):
            r.y_out[n, rows] = slim(self.own_sum(n, 0, rows))

        self.by_rows(one)
        self.y_copy(n).start()

    def send_home(self, n):
        r = self.r
        self.core_copy(n, 1).wait()
        self.y_copy(n).wait()
        here = isinstance(n, int) and n == GROUPS - 1

        def one(rows):
            total = slim(self.own_sum(n, 1, rows) + wide(r.y_in[n, rows]))
            if here:
                r.dkv_home[self.place.group, rows] = total
            else:
                r.z_out[n, rows] = total

        self.by_rows(one)
        if not here:
            self.z_copy(n).start()

    def tile(self, m):
        r, place, heads = self.r, self.place, self.heads
        n, j = m // 2, m % 2
        t = self.tile_start(m) // TK
        for copy in self.fetch(m):
            copy.wait()
        r.acc[...] = jnp.zeros_like(r.acc)
        keys = lambda h: r.kv[m, :, h * 128 : h * 128 + 128]
        for h in range(heads):
            r.kt[h, 0:64] = keys(h).T[0:64]
            r.kt[h, 64:80] = jnp.ones((16, TK), jnp.bfloat16)

        def part(i, _):
            slot = near_slot(place, i, t)
            away = jnp.logical_or(slot == 0, slot == 3)

            def finish(h, p, ds, where):
                ds_low = ds.astype(jnp.bfloat16)
                two = jnp.concatenate([ds_low, p.astype(jnp.bfloat16)], axis=1)
                both = jnp.concatenate([r.qp[i, h], r.dp[i, h]], axis=0)
                r.acc[:, h * 128 : h * 128 + 128] += mxu(two, both)
                r.dqt[i, h, where] += mxu(r.kt[h], ds_low)

            def products(h):
                s = mxu(jnp.concatenate([keys(h), r.kl[m]], axis=1), jnp.concatenate([r.qp[i, h], r.ql[i]], axis=1), NT)
                return s, mxu(keys(h), r.dp[i, h], NT)

            @pl.when(away)
            def _():
                for h in range(heads):
                    s, d_probs = products(h)
                    p = jnp.exp(s - (r.lse[i, h] - jnp.where(slot == 0, r.table[h, 15], r.table[h, 31])))
                    finish(h, p, p * (d_probs - r.delta[i, h]), jnp.where(slot == 0, 0, 2))

            @pl.when(jnp.logical_not(away))
            def _():
                for h in range(heads):
                    s, d_probs = products(h)
                    p = jnp.exp(s + r.bias[h, slot - 1].astype(jnp.float32) - r.lse[i, h])
                    ds = p * (d_probs - r.delta[i, h])
                    r.grid[h, pl.ds(pl.multiple_of((slot - 1) * TK, TK), TK)] += ds
                    finish(h, p, ds, 1)

            return 0

        lax.fori_loop(0, GROUPS, part, 0)
        for half in range(2):
            r.held[n, j, half] = r.acc[half * self.tokens : half * self.tokens + self.tokens].astype(jnp.bfloat16)
        self.core_copy(n, j).start()

    def queries(self):
        r = self.r

        def one(i, _):
            parts = []
            for h in range(self.heads):
                parts.append((r.dqt[i, h, 0, 0:64] + r.dqt[i, h, 1, 0:64] + r.dqt[i, h, 2, 0:64]).T * 0.125)
            r.dq[i] = slim(join_heads(parts))
            return 0

        lax.fori_loop(0, GROUPS, one, 0)

    def buckets(self):
        r = self.r
        first = near_start(self.core)
        for h in range(self.heads):
            r.side[h, 0:1] = sum(r.dqt[i, h, 0, 64:65] for i in range(GROUPS)) + far_sums(r.grid, h, 0, first)
            r.side[h, 1:2] = sum(r.dqt[i, h, 2, 64:65] for i in range(GROUPS)) + far_sums(r.grid, h, first + NEAR_ROWS, 2 * TK)
        bucket_sums(self.core, NearRows(r.grid, first), r.side, r.tab, r.tab8)

    def wait_home(self):
        r, place = self.r, self.place
        for n in range(GROUPS - 1):
            there = r.dkv_home.at[(place.group - 1 - n + GROUPS) % GROUPS]
            remote(r.z_out.at[n], there, r.z_send.at[n], r.z_recv.at[n], self.core_to).wait()


def back_kernel(shards, axes, plans, r):
    place = Place(shards)
    at = {"dp": place.dp, "blk": place.blk}
    tokens, width = r.hidden.shape
    back = RowBack(place, r)
    streams = []
    for s, (kept, order) in enumerate(plans):
        src = r.early[s] if s < 3 else r.late[s - 3]
        streams.append(Stream(axes, at, kept, order, src, r.bufs[s], r.sums[s], r.w_send.at[s], r.w_recv.at[s]))
    early, late = streams[:3], streams[3:]
    whole = Whole(axes, at, (4, 0, 3, 2, 1), r.small, r.small_bufs, r.small_out, r.w_send.at[len(plans)], r.w_recv.at[len(plans)])
    left, right = (place.dp, (place.blk + shards - 1) % shards), (place.dp, (place.blk + 1) % shards)

    met = hail([place.other_group(step) for step in (1, 2, 3)] + [back.across, back.core_to, place.other_row(), left, right])
    back.prepare()
    await_all(met)
    for stream in early:
        stream.copy(0).start()

    def step(m, _):
        back.tile(m)
        for delay, action in ((1, back.send_y), (3, back.send_home)):
            then = m - delay + 2 * GROUPS
            n = then // 2 - GROUPS

            @pl.when(jnp.logical_and(then % 2 == 0, n >= 0))
            def _():
                action(n)

        @pl.when(m == 5)
        def _():
            for stream in early:
                advance(stream, 0)

        return 0

    lax.fori_loop(0, 2 * GROUPS, step, 0)
    back.queries()
    home = Line(place, r.dq, r.dq_home, r.q_send, r.q_recv)
    home.keep().start()
    home.start()
    back.send_home(3)
    for stream in early:
        advance(stream, 1)
    back.buckets()
    load_bytes(r.x, r.before, r.after, r.xs)
    n1_t = r.n1[...].T
    home.wait_all()
    dq = get_packed(r.dq_home)
    devices = 1 << len(axes)
    per = width // devices
    half = width // 2

    def weights(stream, part):
        r.total[...] = mxu(n1_t, part)

        def block(d, _):
            rows = pl.ds(pl.multiple_of(d * per, 8), per)
            index, rest = [], d
            for _ in axes:
                index.append(rest % 2)
                rest = rest // 2
            part = r.total[rows, :]
            stream.src[tuple(reversed(index))] = jnp.concatenate([part[:, :half], part[:, half:]], axis=0).astype(jnp.bfloat16)
            return 0

        lax.fori_loop(0, devices, block, 0)
        stream.copy(0).start()

    weights(late[0], dq)
    back.wait_home()
    dk, dv = unpack_pairs(r.dkv_home, width)
    weights(late[1], dk)
    weights(late[2], dv)
    d_n1 = mxu(dq, r.wq[...], NT) + mxu(dk, r.wk[...], NT) + mxu(dv, r.wv[...], NT)
    d_rows, d_gain1 = norm_back(d_n1, r.hidden[...], r.gain[...].astype(jnp.float32))
    d_hidden = r.dres[...] + d_rows
    for stream in late:
        advance(stream, 0)
    for stream in early:
        advance(stream, 2)
    d_score = pool_back(d_hidden, (r.x, r.before, r.after), r.labels, r.y, r.score, r.gb, r.edge, r.spill, r.xs, r.gbuf)
    put_small(r.small, (d_score, d_gain1, r.dgain2[...]), r.tab, r.share)
    whole.copy(0).start()
    spills = [
        remote(r.spill.at[0], r.spill_out.at[1], r.s2_send.at[0], r.s2_recv.at[1], left),
        remote(r.spill.at[1], r.spill_out.at[0], r.s2_send.at[1], r.s2_recv.at[0], right),
    ]
    for copy in spills:
        copy.start()
    for stage in range(1, len(axes)):
        for stream in late:
            advance(stream, stage)
        advance(whole, stage - 1)
        if stage == 1:
            for stream in early:
                advance(stream, 3)
    advance(whole, len(axes) - 1)
    for copy in spills:
        copy.wait()


def back_and_last(shape, early, inputs):
    shards = shape["blk"]
    axes = bit_axes(shape)
    ndim = len(axes)
    kv, q, hidden = inputs["kv_hbm"].array, inputs["q"], inputs["hidden"]
    heads, width = kv.shape[1] // 128, kv.shape[1]
    tokens, features = hidden.shape
    length = inputs["x"].shape[0]
    f32, low, sem = jnp.float32, jnp.bfloat16, pltpu.SemaphoreType.DMA
    chunk = (tokens, width)
    every = (0, 1, 2, 3, 4)
    four = (0, 1, 2, 3)
    plans = [
        (four, (0, 3, 2, 1)), (four, (0, 3, 2, 1)), (four, (3, 0, 2, 1)),
        (every, (4, 0, 3, 2, 1)), (every, (4, 3, 2, 0, 1)), (every, (4, 2, 0, 3, 1)),
    ]
    own = (2 * (features // (1 << ndim)), features // 2)
    blocks = [part.shape[-2:] for part in early] + [own] * 3
    ins = dict(inputs, early=[part.reshape((2, 2, 2, 2) + part.shape[-2:]) for part in early])
    outs = dict(
        gb=((length, features), low), edge=((2, 16, features), f32), spill_out=((2, LEAD, features), f32),
        small_out=((32, 128), f32), sums=[(block, f32) for block in blocks],
    )
    mem = lambda shape, dtype=low: pltpu.VMEM(shape, dtype)
    pairs, fours = sem((GROUPS, 2)), sem((GROUPS,))
    strip = mem((features // 128, length + 2 * LEAD, 128), f32)
    eights = sem((2 * GROUPS,))
    scratch = dict(
        kt=mem((heads, 80, TK)), dqt=mem((GROUPS, heads, 3, 80, TQ), f32), acc=mem((TK, width), f32),
        grid=mem((heads, 2 * TK, TQ), f32), side=mem((heads, 2, TQ), f32), tab8=mem((heads, BUCKETS, 8, TQ), f32),
        tab=mem((heads, BUCKETS, TQ), f32), delta=mem((GROUPS, heads, 1, TQ), f32),
        qp=mem((GROUPS, heads, TQ, 128)), dp=mem((GROUPS, heads, TQ, 128)),
        kv=mem((2 * GROUPS, TK, width)), kl=mem((2 * GROUPS, TK, 128)),
        held=mem((GROUPS, 2, 2) + chunk), core_in=mem((GROUPS, 2) + chunk),
        y_out=mem((GROUPS,) + chunk), y_in=mem((GROUPS,) + chunk), z_out=mem((GROUPS,) + chunk), dkv_home=mem((GROUPS,) + chunk),
        dq=mem(q.shape), dq_home=mem(q.shape),
        core_send=pairs, core_recv=pairs, y_send=fours, y_recv=fours, z_send=fours, z_recv=fours, q_send=fours, q_recv=fours,
        kv_sem=eights, kl_sem=eights,
        w_send=sem((len(plans) + 1, ndim)), w_recv=sem((len(plans) + 1, ndim)), s2_send=sem((2,)), s2_recv=sem((2,)),
        xs=strip, gbuf=strip, spill=mem((2, LEAD, features), f32), small=mem((32, 128), f32),
        small_bufs=mem((2, ndim, 32, 128), f32), total=mem((features, features), f32),
    )
    scratch["late"] = [mem((2,) * ndim + own)] * 3
    scratch["bufs"] = [stream_scratch(len(kept), order, *block) for (kept, order), block in zip(plans, blocks)]
    return call(functools.partial(back_kernel, shards, axes, plans), 6, ins, outs, scratch)


def label_features(line, unlike):
    rows = [(line != k if unlike else line == k).astype(jnp.float32) for k in range(8)]
    return slim(jnp.concatenate(rows + [jnp.zeros((120, line.shape[1]), jnp.float32)], axis=0).T)


class Line:
    def __init__(self, place, src, dst, send_sem, recv_sem):
        self.place, self.src, self.dst, self.send_sem, self.recv_sem = place, src, dst, send_sem, recv_sem

    def copy(self, step, slot):
        group = self.place.group
        return remote(
            self.src.at[(group + step) % GROUPS], self.dst.at[slot], self.send_sem.at[step], self.recv_sem.at[step],
            self.place.other_group(step),
        )

    def keep(self):
        group = self.place.group
        return pltpu.make_async_copy(self.src.at[group], self.dst.at[group], self.send_sem.at[0])

    def start(self, steps=(1, 3, 2)):
        for step in steps:
            self.copy(step, self.place.group).start()

    def wait(self, step):
        self.copy(step, (self.place.group - step + GROUPS) % GROUPS).wait()

    def wait_all(self):
        for step in (1, 3, 2):
            self.wait(step)
        self.keep().wait()


def near_slot(place, chunk, t):
    first = (chunk * place.rest_size + place.rest) * TQ
    return jnp.clip(t - (first // TK - 1 + place.rest % 2) + 1, 0, 3)


class RowForward:
    def __init__(self, place, r):
        self.place, self.r, self.heads = place, r, r.lse.shape[1]

    def clear(self):
        self.r.acc[...] = jnp.zeros_like(self.r.acc)
        self.r.mx[...] = jnp.full_like(self.r.mx, FIRST_MAX)

    def queries(self, chunk):
        r = self.r
        for h, tile in enumerate(spread_lanes(r.q_all[chunk], False)):
            r.qp[chunk, h] = jnp.concatenate([tile, r.ql[chunk]], axis=1)

    def tile(self, t, chunks, turn=True):
        r = self.r
        rows = pl.ds(pl.multiple_of(t * TK, TK), TK)
        keys = lambda h: r.kv_all[rows, h * 128 : h * 128 + 128]
        if turn:
            for h in range(self.heads):
                r.vt[h, 0:64] = keys(h).T[64:128]
                r.vt[h, 64:80] = jnp.ones((16, TK), jnp.bfloat16)

        def part(i, _):
            slot = near_slot(self.place, i, t)
            away = jnp.logical_or(slot == 0, slot == 3)

            def scores(h):
                return mxu(jnp.concatenate([keys(h), r.kl[rows, :]], axis=1), r.qp[i, h], NT)

            def finish(h, s, b):
                m_old = r.mx[i, h]
                m_new = jnp.maximum(m_old, jnp.max(s, axis=0, keepdims=True) + b)
                p = jnp.exp(s - (m_new - b)).astype(jnp.bfloat16)
                r.mx[i, h] = m_new
                r.acc[i, h] = r.acc[i, h] * jnp.exp(m_old - m_new) + mxu(r.vt[h], p)

            @pl.when(away)
            def _():
                found = [scores(h) for h in range(self.heads)]
                for h in range(self.heads):
                    finish(h, found[h], jnp.where(slot == 0, r.table[h, 15], r.table[h, 31]))

            @pl.when(jnp.logical_not(away))
            def _():
                for h in range(self.heads):
                    finish(h, scores(h) + r.near[h, slot - 1].astype(jnp.float32), 0.0)

            return 0

        lax.fori_loop(0, chunks, part, 0)

    def end(self):
        r = self.r

        def one(i, _):
            parts = []
            for h in range(self.heads):
                total = r.acc[i, h, 64:65, :]
                parts.append((r.acc[i, h, 0:64, :] / total).T)
                r.lse[i, h] = r.mx[i, h] + jnp.log(total)
            joined = join_heads(parts)
            r.o[i] = joined.astype(jnp.bfloat16)
            r.keep[i] = joined
            return 0

        lax.fori_loop(0, GROUPS, one, 0)


def front_kernel(shards, r):
    place = Place(shards)
    tokens = r.kv.shape[1]
    y, core = bit(place.rest, 2), place.rest % 2
    core_to, across = place.other_rest(1), place.other_rest(2)
    met = hail([place.other_group(step) for step in (1, 2, 3)] + [core_to, across])
    masks = bits_of(shards)
    lab_index = [bit(place.blk, m) for m in masks]

    def lab_copy(stage):
        index = tuple(slice(None) if p < stage else lab_index[p] for p in range(len(masks)))
        there = r.labels_all.at[index]
        return remote(there, there, r.lab_send.at[stage], r.lab_recv.at[stage], (place.dp, flipped(place.blk, masks[stage])))

    def label_stage(stage):
        lab_copy(stage).wait()
        if stage + 1 < len(masks):
            lab_copy(stage + 1).start()

    def held(dz, off, core_off):
        rest = flipped(place.rest, 2) if off else place.rest
        rest = flipped(rest, 1) if core_off else rest
        start = pl.multiple_of(place.chunk((place.group + dz) % GROUPS, rest) * tokens, tokens)
        return r.kv_all.at[pl.ds(start, tokens)]

    def sem_of(dz, off, core_off):
        return r.kv_recv.at[(core_off * 2 + off) * GROUPS + dz]

    waits = []

    def send(src, dz, off, came, target):
        copy = remote(src, held(dz, off, 0), r.kv_send.at[len(waits)], sem_of(*came), target)
        copy.start()
        waits.append(copy)

    def arrived(dz, off, core_off=0):
        here = held(dz, off, core_off)
        remote(here, here, r.kv_send.at[0], sem_of(dz, off, core_off), core_to).wait_recv()

    def pass_on(dz, off):
        mine = dz == 0 and off == 0
        if not mine:
            arrived(dz, off)
        src = r.kv.at[place.group] if mine else held(dz, off, 0)
        if not off:
            send(src, dz, off, (dz, 1, 0), across)
        send(src, dz, off, (dz, off, 1), core_to)

    def along(step):
        copy = remote(r.kv.at[(place.group + step) % GROUPS], held(0, 0, 0), r.z_send.at[step], sem_of((GROUPS - step) % GROUPS, 0, 0), place.other_group(step))
        copy.start()
        return copy

    work = RowForward(place, r)

    def tile(dz, off):
        arrived(dz, off, 1)
        work.tile((place.group + dz) % GROUPS * 2 + (1 - y if off else y), GROUPS)

    r.labels_all[tuple(lab_index)] = r.label[...]
    await_all(met)
    lab_copy(0).start()
    own = pltpu.make_async_copy(r.kv.at[place.group], held(0, 0, 0), r.own_sem)
    own.start()
    queries = Line(place, r.q, r.q_all, r.q_send, r.q_recv)
    queries.keep().start()
    queries.start()
    first = [along(1), along(3)]
    pass_on(0, 0)
    make_bias(r.table, core, r.near, (0,))
    label_stage(0)
    pass_on(0, 1)
    make_bias(r.table, core, r.near, (1,))
    label_stage(1)
    work.clear()
    label_stage(2)
    label_stage(3)
    blocks = r.labels_all[...].reshape(shards, 8, 128)
    for n in range(shards):
        line = jnp.concatenate([blocks[n, 0:1], blocks[n, 1:2]], axis=1)
        r.kl[n * tokens : n * tokens + tokens, :] = label_features(line, True)
    for z in range(GROUPS):
        chunk = r.labels_all[tuple([z // 2, z % 2] + [bit(place.rest, m) for m in bits_of(place.rest_size)])]
        line = jnp.concatenate([chunk[0:1], chunk[1:2]], axis=1)
        r.ql[z] = label_features(line, False) * jnp.bfloat16(NEG)
    queries.wait_all()
    for z in range(GROUPS):
        work.queries(z)
    own.wait()
    for copy in first:
        copy.wait_send()
    last = along(2)
    tile(0, 0)
    pass_on(1, 0)
    pass_on(3, 0)
    tile(0, 1)
    pass_on(1, 1)
    tile(1, 0)
    pass_on(3, 1)
    tile(3, 0)
    pass_on(2, 0)
    tile(1, 1)
    pass_on(2, 1)
    tile(3, 1)
    tile(2, 0)
    tile(2, 1)
    last.wait_send()
    work.end()
    for copy in waits:
        copy.wait_send()


def front(shards, table, q_packed, kv_parts, label):
    tokens, width = kv_parts.shape[1:]
    heads = width // 128
    nbits = len(bits_of(shards))
    sem, f32, low = pltpu.SemaphoreType.DMA, jnp.float32, jnp.bfloat16
    mem = lambda shape, dtype=low: pltpu.VMEM(shape, dtype)
    packed = q_packed.shape
    ins = dict(table=Held(table, pltpu.SMEM), q=q_packed, kv=kv_parts, label=label)
    outs = dict(
        q_all=(packed, low), kv_all=((shards * tokens, width), low), kl=((shards * tokens, 128), low), ql=((GROUPS, tokens, 128), low),
        near=((heads, 2, TK, TQ), low), o=(packed, low), keep=(packed, f32), lse=((GROUPS, heads, 1, TQ), f32),
    )
    scratch = dict(
        labels_all=mem((2,) * nbits + label.shape, label.dtype),
        qp=mem((GROUPS, heads, TQ, 256)), acc=mem((GROUPS, heads, 80, TQ), f32), mx=mem((GROUPS, heads, 1, TQ), f32), vt=mem((heads, 80, TK)),
        q_send=sem((4,)), q_recv=sem((4,)), kv_send=sem((12,)), z_send=sem((GROUPS,)), kv_recv=sem((16,)), own_sem=sem,
        lab_send=sem((nbits,)), lab_recv=sem((nbits,)),
    )
    return call(functools.partial(front_kernel, shards), 7, ins, outs, scratch)


def middle_kernel(shards, r):
    place = Place(shards)
    met = hail([place.other_group(step) for step in (1, 2, 3)] + [place.other_rest(1)])
    pairs = ((r.wo_hbm, r.wo), (r.wg_hbm, r.wg), (r.wu_hbm, r.wu), (r.wd_hbm, r.wd))
    fetches = [pltpu.make_async_copy(src, dst, r.w_sem.at[k]) for k, (src, dst) in enumerate(pairs)]
    for copy in fetches:
        copy.start()
    await_all(met)
    home = Line(place, r.o, r.o_home, r.o_send, r.o_recv)
    home.keep().start()
    home.start()
    for copy in fetches:
        copy.wait()
    home.wait_all()
    feed_kernel(r.o_home, r.hidden, r.ct, r.gain, r.wo, r.wg, r.wu, r.wd, r.block_out, r.dres, r.da, r.dgain,
                r.n2, r.att, r.act, r.dg, r.du, r.db, r.acc, r.dn2)
    away = Line(place, r.da, r.do, r.q_send, r.q_recv)
    away.keep().start()
    away.start()
    feed_weights(place, r.n2, r.att, r.act, r.dg, r.du, r.ct, r.db, r.sums,
                 r.core_send, r.core_recv, r.gate, r.up, r.down, r.out, r.wide_out, r.slim_out, r.wide_in, r.slim_in)
    away.wait_all()


def middle(shards, o_packed, hidden, ct, gain, wo, wg, wu, wd):
    tokens, width = hidden.shape
    ff = wg.shape[1]
    per, per_ff = width // 32, ff // 32
    sem, low, f32 = pltpu.SemaphoreType.DMA, jnp.bfloat16, jnp.float32
    half = o_packed.shape[1:]
    wide_cols = ff + width // 2
    first = (wide_cols // 256 + 1) * 128
    ins = dict(o=o_packed, hidden=hidden, ct=ct, gain=gain, wo_hbm=Held(wo, pl.ANY), wg_hbm=Held(wg, pl.ANY), wu_hbm=Held(wu, pl.ANY), wd_hbm=Held(wd, pl.ANY))
    outs = dict(
        block_out=((tokens, width), low), dres=((tokens, width), f32), dgain=((1, width), f32), do=((GROUPS,) + half, low),
        sums=[((16, 2 * per, first), low), ((16, 2 * per, wide_cols - first), low), ((16, per_ff, width), low)],
    )
    mem = lambda shape, dtype=low: pltpu.VMEM(shape, dtype)
    scratch = dict(
        o_home=mem((GROUPS,) + half), da=mem((GROUPS,) + half),
        n2=mem((tokens, width)), att=mem((tokens, width)), db=mem((tokens, width)),
        act=mem((tokens, ff)), dg=mem((tokens, ff)), du=mem((tokens, ff)),
        acc=mem((tokens, width), f32), dn2=mem((tokens, width), f32),
        wo=mem(wo.shape), wg=mem(wg.shape), wu=mem(wu.shape), wd=mem(wd.shape),
        gate=mem((width, ff), f32), up=mem((width, ff), f32), down=mem((ff, width), f32), out=mem((width, width), f32),
        wide_out=mem((16, 2 * per, wide_cols)), slim_out=mem((16, per_ff, width)),
        wide_in=mem((16, 2 * per, wide_cols)), slim_in=mem((16, per_ff, width)),
        w_sem=sem((4,)), o_send=sem((4,)), o_recv=sem((4,)), q_send=sem((4,)), q_recv=sem((4,)),
        core_send=sem((2,)), core_recv=sem((2,)),
    )
    return call(functools.partial(middle_kernel, shards), 8, ins, outs, scratch)


def neighbours(rows):
    peers = lax.axis_size("blk")
    up = [(i, i + 1) for i in range(peers - 1)]
    last, leading = rows
    return lax.ppermute(last, "blk", up), lax.ppermute(leading, "blk", [(j, i) for i, j in up])


def body(
    byte_embeds,
    segments,
    score_weight,
    norm_gain1,
    w_query,
    w_key,
    w_value,
    w_out,
    rel_bias,
    norm_gain2,
    w_gate,
    w_up,
    w_down,
    cotangent,
):
    row_count, length, width = byte_embeds.shape
    tokens = length // 2
    shards = lax.axis_size("blk")
    shape = {"dp": lax.axis_size("dp"), "blk": shards}
    devices = shards * shape["dp"]
    heads = rel_bias.shape[1] // GROUPS
    position = lax.axis_index("blk")
    rest_size = shards // GROUPS
    group, rest = position // rest_size, position % rest_size
    row = lax.axis_index("dp") % 2
    x, ids_here = byte_embeds[0], segments[0]

    marks = (ids_here + 1).astype(jnp.bfloat16)
    with_marks = lambda part, two: jnp.concatenate([part, jnp.pad(two, (0, width - 2))[None]], axis=0)
    before, after = neighbours((with_marks(x[-2:], marks[-2:]), with_marks(x[:2], marks[:2])))
    line = jnp.concatenate([before[2, :2], marks, after[2, :2]])
    line = jnp.pad(line, (1, 1)).astype(jnp.int32).reshape(tokens + 3, 2).T
    labels = jnp.stack([line[j % 2, j // 2 : j // 2 + tokens] for j in range(8)])

    score_row, gain1, gain2 = score_weight[None], norm_gain1[None], norm_gain2[None]
    hidden, n1, y, share, q_packed, kv_parts = pool_and_project(
        shards, 1.0 / (row_count * length * devices), x, before, after, labels, score_row, gain1, w_query, w_key, w_value
    )

    label_block = jnp.pad(ids_here[0::2].reshape(tokens // 128, 128), ((0, 8 - tokens // 128), (0, 0)), constant_values=-1)
    table = lax.dynamic_slice_in_dim(rel_bias.astype(jnp.float32).T, group * heads, heads, 0)
    if devices == 32:
        got = front(shards, table, q_packed, kv_parts, label_block)
        o_packed = got.o
    else:
        q_all, kv_all, labels_all = gather_all(shards, q_packed, kv_parts, label_block)
        labels_all = labels_all.reshape(2, shards, 8, 128)[:, :, : tokens // 128].reshape(2, shards * tokens)
        ids = jnp.arange(8, dtype=jnp.int32)
        counts = jnp.sum((labels_all[:, None, :] == ids[None, :, None]).astype(jnp.int32), axis=2)
        ends = jnp.sum(jnp.where(ids[None, :] <= ids[:, None], counts[:, None, :], 0), axis=2)
        begins = ends - counts
        query_labels = jnp.stack(
            [lax.dynamic_slice_in_dim(labels_all, ((2 * row + i) * rest_size + rest) * tokens, tokens, 1) for i in range(2)],
            axis=1,
        )
        chosen = query_labels[:, :, None, :] == ids[None, None, :, None]
        span = jnp.stack(
            [jnp.sum(jnp.where(chosen, edge[:, None, :, None], 0), axis=2) for edge in (begins, ends)], axis=2
        )
        parity = rest % 2
        firsts = jnp.stack([((2 * row + i) * rest_size + rest) * tokens for i in range(2)])
        near = jnp.broadcast_to((firsts // TK - 1 + parity)[None], (2, 2))
        bounds = jnp.stack(
            [
                jnp.min(span[:, :, 0], axis=-1) // TK,
                -(-jnp.max(span[:, :, 1], axis=-1) // TK),
                near,
                -(-jnp.max(span[:, :, 0], axis=-1) // TK),
                jnp.min(span[:, :, 1], axis=-1) // TK,
                jnp.broadcast_to(parity, (2, 2)),
                jnp.broadcast_to((labels_all[0, -1] > 0).astype(jnp.int32), (2, 2)),
            ],
            axis=-1,
        ).astype(jnp.int32)
        o_packed, o_kept, log_total, near_bias = attention(bounds, table, q_all, kv_all, span)
    ct = cotangent[0]
    if devices == 32:
        mid = middle(shards, o_packed, hidden, ct, gain2, w_out, w_gate, w_up, w_down)
        block_out, d_res, d_gain2 = mid.block_out, mid.dres, mid.dgain
        last = back_and_last(
            shape,
            mid.sums,
            dict(
                table=Held(table, pltpu.SMEM), q=got.q_all, do=mid.do, keep=got.keep, kv_hbm=Held(got.kv_all, pl.ANY),
                kl_hbm=Held(got.kl, pl.ANY), ql=got.ql, bias=got.near, lse=got.lse,
                hidden=hidden, dres=d_res, n1=n1, x=x, before=before, after=after,
                labels=labels, y=y, score=score_row, gain=gain1, wq=w_query, wk=w_key, wv=w_value, dgain2=d_gain2, share=share,
            ),
        )
        grad_bytes, edge, spill, small, sums = last.gb, last.edge, last.spill_out, last.small_out, last.sums
    else:
        o_home = move_heads(return_kernel, (GROUPS,), shards, 4, o_packed)
        block_out, d_res, da_packed, d_gain2, n2, att, act, d_gate, d_up, d_branch = feed_forward(
            o_home, hidden, ct, gain2, w_out, w_gate, w_up, w_down
        )
        do_all = move_heads(spread_kernel, (2, 2), shards, 5, da_packed)
        dq_packed, dkv_all, _, _, _, d_table_lanes = attention_back(
            False, bounds, table, q_all, do_all, o_kept, kv_all, near_bias, span, log_total
        )
        dq_home, dkv_home = reduce_all(shape, dq_packed, dkv_all, [], [])
        grad_bytes, edge, spill, small, last_parts = last_part(
            shape, dq_home, dkv_home, hidden, d_res, x, before, after, labels, y,
            score_row, gain1, w_query, w_key, w_value, d_gain2, share, d_table_lanes,
        )
        sums = []
    per = width // devices
    grad_bytes, g_score, g_gain1, g_gain2, rows, *grads = finish(
        shards, rel_bias.shape[1], per, w_gate.shape[1], grad_bytes, edge, spill, small, sums
    )
    if devices != 32:
        product = lambda left, right: jnp.einsum("td,te->de", left, right, preferred_element_type=jnp.float32)
        grads = [product(n1, last_parts[j]) for j in range(3)]
        grads += [product(att, d_branch), product(n2, d_gate), product(n2, d_up), product(act, ct)]
        grads = [lax.psum_scatter(grad, ("dp", "blk"), scatter_dimension=0, tiled=True) for grad in grads]
    return (
        block_out[None],
        grad_bytes[None],
        g_score,
        g_gain1,
        *grads[:4],
        rows[2 : 2 + rel_bias.shape[1], :BUCKETS].T,
        g_gain2,
        *grads[4:],
        rows[14, :MAX_BLOCK],
    )


def solution(mesh):
    placed = (
        P("dp", "blk", None),
        P("dp", "blk"),
        P(),
        P(),
        P(),
        P(),
        P(),
        P(),
        P(),
        P(),
        P(),
        P(),
        P(),
        P("dp", "blk", None),
    )
    return jax.shard_map(
        body,
        mesh=mesh,
        in_specs=placed,
        out_specs=(
            P("dp", "blk", None),
            P("dp", "blk", None),
            P(),
            P(),
            P(("dp", "blk"), None),
            P(("dp", "blk"), None),
            P(("dp", "blk"), None),
            P(("dp", "blk"), None),
            P(),
            P(),
            P(("dp", "blk"), None),
            P(("dp", "blk"), None),
            P(("dp", "blk"), None),
            P(),
        ),
        check_vma=False,
    )
```

```python
import functools
import math

import jax
import jax.numpy as jnp
from jax import lax
from jax.experimental import pallas as pl
from jax.experimental.pallas import tpu as pltpu
from jax.sharding import PartitionSpec as P

BUCKETS = 32
MAX_BLOCK = 4
VMEM_BYTES = 61 * 2**20


def buckets_of(relative):
    distance = jnp.abs(relative)
    beyond = jnp.zeros_like(distance)
    for border in (12, 16, 23, 32, 46, 64, 91):
        beyond = beyond + (distance >= border).astype(jnp.int32)
    nearer = jnp.where(distance < 8, distance, 8 + beyond)
    return nearer + BUCKETS // 2 * (relative > 0).astype(jnp.int32)


MESH_ID = pl.DeviceIdType.MESH
GROUPS = 4


def bits_of(size):
    return [1 << p for p in reversed(range(size.bit_length() - 1))]


def bit(value, mask):
    return (value // mask) % 2


def flipped(value, mask):
    return value + mask * (1 - 2 * bit(value, mask))


class Place:
    def __init__(self, shards):
        self.shards = shards
        self.rest_size = shards // GROUPS
        self.dp = lax.axis_index("dp")
        self.blk = lax.axis_index("blk")
        self.row = self.dp % 2
        self.group = self.blk // self.rest_size
        self.rest = self.blk % self.rest_size

    def at(self, row, group, rest):
        return (self.dp - self.row + row, group * self.rest_size + rest)

    def chunk(self, group, rest):
        return group * self.rest_size + rest

    def other_row(self):
        return self.at(1 - self.row, self.group, self.rest)

    def other_rest(self, mask):
        return self.at(self.row, self.group, flipped(self.rest, mask))

    def other_group(self, step):
        return self.at(self.row, (self.group + step) % GROUPS, self.rest)


def hail(targets):
    barrier = pltpu.get_barrier_semaphore()
    for target in targets:
        pl.semaphore_signal(barrier, inc=1, device_id=target, device_id_type=MESH_ID)
    return len(targets)


def await_all(count):
    pl.semaphore_wait(pltpu.get_barrier_semaphore(), count)


def greet(targets):
    await_all(hail(targets))


def remote(src, dst, send_sem, recv_sem, target):
    return pltpu.make_async_remote_copy(
        src_ref=src,
        dst_ref=dst,
        send_sem=send_sem,
        recv_sem=recv_sem,
        device_id=target,
        device_id_type=MESH_ID,
    )


def line_and_row(place):
    found = []
    for step in range(GROUPS):
        for flip in range(2):
            if step or flip:
                row = 1 - place.row if flip else place.row
                found.append(place.at(row, (place.group + step) % GROUPS, place.rest))
    return found


def spread_heads(place, q_ref, out_ref, send_sem, recv_sem):
    row_to = place.group // 2
    slot = place.group % 2
    dst = out_ref.at[place.row, slot]
    mine = recv_sem.at[place.row * 2 + slot]
    at_home = row_to == place.row
    for step in range(GROUPS):
        group = (place.group + step) % GROUPS
        src = q_ref.at[group]
        copy = remote(src, dst, send_sem.at[step], mine, place.at(row_to, group, place.rest))
        if step:
            copy.start()
        else:
            pl.when(jnp.logical_not(at_home))(copy.start)
            pl.when(at_home)(pltpu.make_async_copy(src, dst, mine).start)


def spread_heads_come(q_ref, out_ref, recv_sem):
    for row in range(2):
        for slot in range(2):
            pltpu.make_async_copy(q_ref.at[0], out_ref.at[row, slot], recv_sem.at[row * 2 + slot]).wait()


def spread_heads_gone(place, q_ref, out_ref, send_sem, recv_sem):
    at_home = place.group // 2 == place.row
    for step in range(GROUPS):
        copy = remote(q_ref.at[0], out_ref.at[0, 0], send_sem.at[step], recv_sem.at[0], place.other_row())
        if step:
            copy.wait_send()
        else:
            pl.when(jnp.logical_not(at_home))(copy.wait_send)


def spread_heads_wait(place, q_ref, out_ref, send_sem, recv_sem):
    spread_heads_come(q_ref, out_ref, recv_sem)
    spread_heads_gone(place, q_ref, out_ref, send_sem, recv_sem)


def return_heads(place, o_ref, out_ref, send_sem, recv_sem):
    for row in range(2):
        for slot in range(2):
            group = place.row * 2 + slot
            src = o_ref.at[row, slot]
            dst = out_ref.at[place.group]
            mine = recv_sem.at[place.group]
            at_home = jnp.logical_and(place.row == row, place.group == group)
            copy = remote(src, dst, send_sem.at[row * 2 + slot], mine, place.at(row, group, place.rest))
            pl.when(jnp.logical_not(at_home))(copy.start)
            pl.when(at_home)(pltpu.make_async_copy(src, dst, mine).start)


def return_heads_wait(place, o_ref, out_ref, send_sem, recv_sem):
    for group in range(GROUPS):
        pltpu.make_async_copy(o_ref.at[0, 0], out_ref.at[group], recv_sem.at[group]).wait()
    for row in range(2):
        for slot in range(2):
            group = place.row * 2 + slot
            at_home = jnp.logical_and(place.row == row, place.group == group)
            copy = remote(o_ref.at[0, 0], out_ref.at[0], send_sem.at[row * 2 + slot], recv_sem.at[0], place.other_row())
            pl.when(jnp.logical_not(at_home))(copy.wait_send)


def spread_kernel(shards, q_ref, out_ref, send_sem, recv_sem):
    place = Place(shards)
    greet(line_and_row(place))
    spread_heads(place, q_ref, out_ref, send_sem, recv_sem)
    spread_heads_wait(place, q_ref, out_ref, send_sem, recv_sem)


def return_kernel(shards, o_ref, out_ref, send_sem, recv_sem):
    place = Place(shards)
    greet(line_and_row(place))
    return_heads(place, o_ref, out_ref, send_sem, recv_sem)
    return_heads_wait(place, o_ref, out_ref, send_sem, recv_sem)


SMEM_SPEC = pl.BlockSpec(memory_space=pltpu.SMEM)
VMEM_SPEC = pl.BlockSpec(memory_space=pltpu.VMEM)
ANY_SPEC = pl.BlockSpec(memory_space=pl.ANY)


def move_heads(kernel, lead, shards, ident, packed):
    rows, lanes = packed.shape[-2:]
    return pl.pallas_call(
        functools.partial(kernel, shards),
        out_shape=jax.ShapeDtypeStruct(lead + (rows, lanes), packed.dtype),
        in_specs=[pl.BlockSpec(memory_space=pltpu.VMEM)],
        out_specs=pl.BlockSpec(memory_space=pltpu.VMEM),
        scratch_shapes=[pltpu.SemaphoreType.DMA((4,)), pltpu.SemaphoreType.DMA((4,))],
        compiler_params=pltpu.CompilerParams(collective_id=ident, has_side_effects=True, vmem_limit_bytes=VMEM_BYTES),
        name="move_heads_%d" % ident,
    )(packed)


def gather_kernel(shards, q_ref, kv_ref, label_ref, qo_ref, kvo_ref, labo_ref, q_send, q_recv, z_send, far_send, core_send, kv_recv, own_sem, lab_send, lab_recv):
    place = Place(shards)
    tokens = kv_ref.shape[1]
    rest_bits = bits_of(place.rest_size)
    core, far = rest_bits[-1], ["row"] + rest_bits[:-1]
    greet(line_and_row(place) + [place.other_rest(mask) for mask in rest_bits])

    dims = [("row", 1)] + [("blk", m) for m in bits_of(shards)]
    lab_index = [place.row] + [bit(place.blk, m) for _, m in dims[1:]]
    lab_order = list(range(len(dims)))

    def lab_copy(stage):
        index = tuple(slice(None) if p in lab_order[:stage] else lab_index[p] for p in range(len(dims)))
        axis, mask = dims[lab_order[stage]]
        target = place.other_row() if axis == "row" else (place.dp, flipped(place.blk, mask))
        there = labo_ref.at[index]
        return remote(there, there, lab_send.at[stage], lab_recv.at[stage], target)

    labo_ref[tuple(lab_index)] = label_ref[...]
    lab_copy(0).start()
    lab_stage = 0

    def slot(row, group, rest):
        start = pl.multiple_of(place.chunk(group, rest) * tokens, tokens)
        return kvo_ref.at[row, pl.ds(start, tokens)]

    def held(dz, offset, core_off):
        row = 1 - place.row if offset & 1 else place.row
        rest = place.rest
        for p, mask in enumerate(far[1:]):
            if offset >> (p + 1) & 1:
                rest = flipped(rest, mask)
        if core_off:
            rest = flipped(rest, core)
        return slot(row, (place.group + dz) % GROUPS, rest)

    count = 1 << len(far)

    def sem_of(dz, offset, core_off):
        return kv_recv.at[(core_off * count + offset) * GROUPS + dz]

    own = pltpu.make_async_copy(kv_ref.at[place.group], held(0, 0, 0), own_sem)
    own.start()
    waits = []
    for step in (1, 3, 2):
        copy = remote(kv_ref.at[(place.group + step) % GROUPS], held(0, 0, 0), z_send.at[step], sem_of((GROUPS - step) % GROUPS, 0, 0), place.other_group(step))
        copy.start()
        waits.append(copy)

    used = 0
    events = sorted(((dz, off) for dz in range(GROUPS) for off in range(count)), key=lambda e: (bin(e[1]).count("1"), (0, 1, 3, 2).index(e[0])))
    core_target = place.other_rest(core)
    for step, (dz, off) in enumerate(events):
        if step == GROUPS:
            spread_heads(place, q_ref, qo_ref, q_send, q_recv)
        here = held(dz, off, 0)
        if dz == 0 and off == 0:
            src = kv_ref.at[place.group]
        else:
            remote(here, here, z_send.at[0], sem_of(dz, off, 0), core_target).wait_recv()
            src = here
        order = [(p + dz) % len(far) for p in range(len(far))]
        last = max([order.index(p) for p in range(len(far)) if off >> p & 1], default=-1)
        for p in order[last + 1 :]:
            target = place.other_row() if p == 0 else place.other_rest(far[p])
            copy = remote(src, here, far_send.at[used], sem_of(dz, off | 1 << p, 0), target)
            copy.start()
            waits.append(copy)
            used += 1
        copy = remote(src, here, core_send.at[off * GROUPS + dz], sem_of(dz, off, 1), core_target)
        copy.start()
        waits.append(copy)
        if lab_stage < len(dims):
            lab_copy(lab_stage).wait()
            lab_stage += 1
            if lab_stage < len(dims):
                lab_copy(lab_stage).start()
    for dz, off in events:
        here = held(dz, off, 1)
        remote(here, here, z_send.at[0], sem_of(dz, off, 1), core_target).wait_recv()
    own.wait()
    for copy in waits:
        copy.wait_send()
    spread_heads_wait(place, q_ref, qo_ref, q_send, q_recv)


def gather_all(shards, q_packed, kv_parts, labels):
    tokens, width = kv_parts.shape[1:]
    far = 1 + len(bits_of(shards // GROUPS)) - 1
    count = 1 << far
    nbits = 1 + len(bits_of(shards))
    sem = pltpu.SemaphoreType.DMA
    return pl.pallas_call(
        functools.partial(gather_kernel, shards),
        out_shape=(
            jax.ShapeDtypeStruct((2, 2) + q_packed.shape[1:], q_packed.dtype),
            jax.ShapeDtypeStruct((2, shards * tokens, width), kv_parts.dtype),
            jax.ShapeDtypeStruct((2,) * nbits + labels.shape, labels.dtype),
        ),
        in_specs=[pl.BlockSpec(memory_space=pltpu.VMEM)] * 3,
        out_specs=(pl.BlockSpec(memory_space=pltpu.VMEM),) * 3,
        scratch_shapes=[
            sem((4,)), sem((4,)), sem((GROUPS,)), sem((GROUPS * (count - 1),)), sem((GROUPS * count,)), sem((GROUPS * count * 2,)),
            sem, sem((nbits,)), sem((nbits,)),
        ],
        compiler_params=pltpu.CompilerParams(collective_id=1, has_side_effects=True, vmem_limit_bytes=VMEM_BYTES),
        name="gather_keys",
    )(q_packed, kv_parts, labels)


def add_blocks(dst_ref, src_ref, index, shape):
    lead = shape[:-2]
    total = math.prod(lead)

    def one(step, _):
        place, left = [], step
        for size in reversed(lead):
            place.append(left % size)
            left = left // size
        place = tuple(reversed(place))
        full, k = [], 0
        for entry in index:
            if entry is None:
                full.append(place[k])
                k += 1
            else:
                full.append(entry)
        mine = src_ref[tuple(full)].astype(jnp.float32)
        dst_ref[place] = (dst_ref[place].astype(jnp.float32) + mine).astype(dst_ref.dtype)
        return 0

    lax.fori_loop(0, total, one, 0)


class Stream:
    def __init__(self, axes, at, kept, order, src, bufs, out, send_sem, recv_sem):
        self.axes, self.at, self.kept, self.order = axes, at, kept, order
        self.src, self.bufs, self.out = src, bufs, out
        self.send_sem, self.recv_sem = send_sem, recv_sem

    def own(self, p):
        axis, mask = self.axes[p]
        return bit(self.at[axis], mask)

    def target(self, p):
        axis, mask = self.axes[p]
        moved = dict(self.at)
        moved[axis] = flipped(self.at[axis], mask)
        return (moved["dp"], moved["blk"])

    def stage(self, k):
        kept = [p for p in self.kept if p not in self.order[:k]]
        return kept, self.src if k == 0 else self.bufs[k - 1], self.order[k]

    def copy(self, k):
        kept, src, now = self.stage(k)
        index = tuple(1 - self.own(p) if p == now else slice(None) for p in kept)
        return remote(src.at[index], self.bufs[k], self.send_sem.at[k], self.recv_sem.at[k], self.target(now))

    def absorb(self, k):
        kept, src, now = self.stage(k)
        buf = self.bufs[k]
        if k == len(self.order) - 1 and self.out is not None:
            mine = src[self.own(now)].astype(jnp.float32)
            self.out[...] = buf[...].astype(jnp.float32) + mine
        else:
            add_blocks(buf, src, tuple(self.own(p) if p == now else None for p in kept), buf.shape)


class Whole:
    def __init__(self, axes, at, order, src, bufs, out, send_sem, recv_sem):
        self.stream = Stream(axes, at, order, order, src, bufs, out, send_sem, recv_sem)
        self.order, self.src, self.bufs, self.out = order, src, bufs, out

    def held(self, k):
        return self.src if k == 0 else self.bufs.at[1, k - 1]

    def copy(self, k):
        s = self.stream
        return remote(self.held(k), self.bufs.at[0, k], s.send_sem.at[k], s.recv_sem.at[k], s.target(self.order[k]))

    def absorb(self, k):
        total = self.held(k)[...] + self.bufs[0, k]
        if k == len(self.order) - 1:
            self.out[...] = total
        else:
            self.bufs[1, k] = total


def advance(stream, stage):
    if stage < len(stream.order):
        stream.copy(stage).wait()
        stream.absorb(stage)
        if stage < len(stream.order) - 1:
            stream.copy(stage + 1).start()


def bit_axes(shape):
    return [("dp", m) for m in bits_of(shape["dp"])] + [("blk", m) for m in bits_of(shape["blk"])]


def stream_scratch(lead, order, rows, cols):
    return [pltpu.VMEM((2,) * (lead - 1 - k) + (rows, cols), jnp.bfloat16) for k in range(len(order))]


def feed_weights(place, n2_ref, att_ref, act_ref, dg_ref, du_ref, ct_ref, db_ref, sums,
                 core_send, core_recv, gate, up, down, out, wide_out, slim_out, wide_in, slim_in):
    core_target = place.other_rest(1)
    per = gate.shape[0] // 32
    per_ff = down.shape[0] // 32
    first = sums[0].shape[2]
    half = out.shape[1] // 2
    core = place.rest % 2

    n2_t = n2_ref[...].T
    step = 512
    for j in range(gate.shape[1] // step):
        cols = slice(j * step, j * step + step)
        gate[:, cols] = mxu(n2_t, dg_ref[:, cols])
        up[:, cols] = mxu(n2_t, du_ref[:, cols])
    out[...] = mxu(att_ref[...].T, db_ref[...])

    def wide_rows(block):
        rows = pl.ds(pl.multiple_of(block * per, 8), per)
        last = jnp.concatenate([out[rows, :half], out[rows, half:]], axis=0)
        return jnp.concatenate([jnp.concatenate([gate[rows, :], up[rows, :]], axis=0), last], axis=1)

    def slim_rows(block):
        return down[pl.ds(pl.multiple_of(block * per_ff, 8), per_ff), :]

    def send_wide(m, _):
        wide_out[m] = wide_rows(2 * m + 1 - core).astype(jnp.bfloat16)
        return 0

    lax.fori_loop(0, 16, send_wide, 0)
    wide_copy = remote(wide_out, wide_in, core_send.at[0], core_recv.at[0], core_target)
    wide_copy.start()
    for j in range(down.shape[0] // step):
        rows = slice(j * step, j * step + step)
        down[rows, :] = mxu(act_ref[:, rows].T, ct_ref[...])

    def send_slim(m, _):
        slim_out[m] = slim_rows(2 * m + 1 - core).astype(jnp.bfloat16)
        return 0

    lax.fori_loop(0, 16, send_slim, 0)
    slim_copy = remote(slim_out, slim_in, core_send.at[1], core_recv.at[1], core_target)
    slim_copy.start()

    wide_copy.wait()

    def sum_wide(m, _):
        total = wide_rows(2 * m + core) + wide_in[m].astype(jnp.float32)
        sums[0][m] = total[:, :first].astype(jnp.bfloat16)
        sums[1][m] = total[:, first:].astype(jnp.bfloat16)
        return 0

    lax.fori_loop(0, 16, sum_wide, 0)
    slim_copy.wait()

    def sum_slim(m, _):
        sums[2][m] = (slim_rows(2 * m + core) + slim_in[m].astype(jnp.float32)).astype(jnp.bfloat16)
        return 0

    lax.fori_loop(0, 16, sum_slim, 0)


def reduce_kernel(shards, axes, orders, *refs):
    count = len(orders)
    q_ref, kv_ref = refs[:2]
    pairs = refs[2 : 2 + 2 * count]
    qo_ref, kvo_ref = refs[2 + 2 * count : 4 + 2 * count]
    sums = refs[4 + 2 * count : 4 + 3 * count]
    q_send, q_recv, send_sem, recv_sem, z_send, z_recv, w_send, w_recv = refs[4 + 3 * count : 12 + 3 * count]
    bufs = refs[12 + 3 * count :]
    place = Place(shards)
    rest_bits = bits_of(place.rest_size)
    greet(line_and_row(place) + [place.other_rest(mask) for mask in rest_bits])
    return_heads(place, q_ref, qo_ref, q_send, q_recv)
    ndim = 1 + len(rest_bits)
    at = {"dp": place.dp, "blk": place.blk}
    streams, used = [], ndim
    for s, (kept, order) in enumerate(orders):
        src, more = bufs[used], bufs[used + 1 : used + 1 + len(order)]
        used += 1 + len(order)
        streams.append(Stream(axes, at, kept, order, src, more, sums[s], w_send.at[s], w_recv.at[s]))
    own = [place.row] + [bit(place.rest, m) for m in rest_bits]
    targets = [place.other_row()] + [place.other_rest(m) for m in rest_bits]
    state = {}

    def plan(group_step):
        far = list(range(ndim - 1))
        turn = group_step % len(far)
        return [ndim - 1] + far[turn:] + far[:turn]

    def copy_of(step, stage):
        order = plan(step)
        group = (place.group + step) % GROUPS
        done = order[:stage]
        p_now = order[stage]
        buf = bufs[stage].at[step]
        if stage == 0:
            index = (p_index(group, done, p_now))
            src = kv_ref.at[index]
        else:
            kept = [p for p in range(ndim) if p not in done]
            src = bufs[stage - 1].at[(step,) + tuple(1 - own[p] if p == p_now else slice(None) for p in kept)]
        return remote(src, buf, send_sem.at[stage, step], recv_sem.at[stage, step], targets[p_now])

    def p_index(group, done, p_now):
        index = [slice(None)] * ndim
        index[p_now] = 1 - own[p_now]
        return (index[0], group) + tuple(index[1:])

    def absorb(step, stage):
        order = plan(step)
        done, p_now = order[:stage], order[stage]
        buf = bufs[stage].at[step]
        group = (place.group + step) % GROUPS
        if stage == 0:
            index = [None] * ndim
            index[p_now] = own[p_now]
            add_blocks(buf, kv_ref, (index[0], group) + tuple(index[1:]), buf.shape)
        else:
            kept = [p for p in range(ndim) if p not in done]
            index = tuple(own[p] if p == p_now else None for p in kept)
            add_blocks(buf, bufs[stage - 1].at[step], index, buf.shape)

    steps = (2, 1, 3, 0)
    for step in steps:
        copy_of(step, 0).start()
    for s, stream in enumerate(streams):
        add_two(stream.src, pairs[2 * s], pairs[2 * s + 1])
        stream.copy(0).start()
    for stage in range(ndim):
        for step in steps:
            copy_of(step, stage).wait()
            absorb(step, stage)
            if stage < ndim - 1:
                copy_of(step, stage + 1).start()
            elif step:
                remote(bufs[stage].at[step], kvo_ref.at[place.group], z_send.at[step], z_recv.at[(GROUPS - step) % GROUPS], place.other_group(step)).start()
            else:
                kvo_ref[place.group] = bufs[stage][step]
        for stream in streams:
            if stage < len(stream.order):
                stream.copy(stage).wait()
                stream.absorb(stage)
                if stage < len(stream.order) - 1:
                    stream.copy(stage + 1).start()
    for step in (1, 3, 2):
        there = kvo_ref.at[(place.group + step) % GROUPS]
        remote(bufs[ndim - 1].at[step], there, z_send.at[step], z_recv.at[step], place.other_group(step)).wait()
    return_heads_wait(place, q_ref, qo_ref, q_send, q_recv)


def add_two(dst_ref, one_ref, two_ref):
    lead = dst_ref.shape[:-2]

    def one(step, _):
        place, left = [], step
        for size in reversed(lead):
            place.append(left % size)
            left = left // size
        place = tuple(reversed(place))
        dst_ref[place] = (one_ref[place].astype(jnp.float32) + two_ref[place].astype(jnp.float32)).astype(dst_ref.dtype)
        return 0

    lax.fori_loop(0, math.prod(lead), one, 0)


def reduce_all(shape, q_packed, kv_sums, orders, pairs):
    shards = shape["blk"]
    tokens_all, width = kv_sums.shape[1:]
    tokens = tokens_all // shards
    rest_bits = bits_of(shards // GROUPS)
    ndim = 1 + len(rest_bits)
    sem = pltpu.SemaphoreType.DMA
    scratch = [pltpu.VMEM((GROUPS,) + (2,) * (ndim - 1 - s) + (tokens, width), kv_sums.dtype) for s in range(ndim)]
    flat, sums = [], []
    for (kept, order), pair in zip(orders, pairs):
        rows, cols = pair[0].shape[-2:]
        flat += [part.reshape((2,) * len(kept) + (rows, cols)) for part in pair]
        sums.append(jax.ShapeDtypeStruct((rows, cols), jnp.float32))
        scratch.append(pltpu.VMEM((2,) * len(kept) + (rows, cols), jnp.bfloat16))
        scratch += stream_scratch(len(kept), order, rows, cols)
    stages = max([len(order) for _, order in orders], default=1)
    return pl.pallas_call(
        functools.partial(reduce_kernel, shards, bit_axes(shape), orders),
        out_shape=(
            jax.ShapeDtypeStruct((GROUPS,) + q_packed.shape[2:], q_packed.dtype),
            jax.ShapeDtypeStruct((GROUPS, tokens, width), kv_sums.dtype),
        ) + tuple(sums),
        in_specs=[VMEM_SPEC] * (2 + len(flat)),
        out_specs=(VMEM_SPEC,) * (2 + len(sums)),
        scratch_shapes=[sem((4,)), sem((4,)), sem((ndim, GROUPS)), sem((ndim, GROUPS)), sem((GROUPS,)), sem((GROUPS,)),
                        sem((max(len(orders), 1), stages)), sem((max(len(orders), 1), stages))] + scratch,
        compiler_params=pltpu.CompilerParams(collective_id=2, has_side_effects=True, vmem_limit_bytes=VMEM_BYTES),
        name="reduce_keys",
    )(q_packed, kv_sums.reshape((2, GROUPS) + (2,) * len(rest_bits) + (tokens, width)), *flat)


TQ = 256
TK = 512
NEAR_ROWS = 448
NEG = -1e30
FIRST_MAX = -1e29
NT = (((1,), (1,)), ((), ()))
NN = (((1,), (0,)), ((), ()))
BORDERS = (12, 16, 23, 32, 46, 64, 91)


def mxu(left, right, dims=NN):
    return lax.dot_general(left, right, dims, preferred_element_type=jnp.float32)


def turned(tile):
    return jnp.concatenate([tile[:, 64:], tile[:, :64]], axis=1)


def spread_lanes(packed, high):
    lane = lax.broadcasted_iota(jnp.int32, (1, 128), 1)
    keep = lane >= 64 if high else lane < 64
    zero = jnp.zeros((), packed.dtype)
    pair, last = packed[0:TQ], packed[TQ:]
    pick = lambda tile: jnp.where(keep, tile, zero)
    if high:
        return [pick(turned(pair)), pick(pair), jnp.concatenate([pick(turned(last)), pick(last)], axis=0)]
    return [pick(pair), pick(turned(pair)), jnp.concatenate([pick(last), pick(turned(last))], axis=0)]


def join_heads(parts):
    half = TQ // 2
    top = jnp.concatenate([parts[0], parts[1]], axis=1)
    low = jnp.concatenate([parts[2][:half], parts[2][half:]], axis=1)
    return jnp.concatenate([top, low], axis=0)


def valid_mask(se_ref, r, i, k0):
    kpos = k0 + lax.broadcasted_iota(jnp.int32, (TK, TQ), 0)
    return jnp.logical_and(kpos >= se_ref[r, i, 0:1, :], kpos < se_ref[r, i, 1:2, :])


def near_buckets(first, rows, parity):
    relative = (
        first - TK + TQ * parity
        + lax.broadcasted_iota(jnp.int32, (rows, TQ), 0)
        - lax.broadcasted_iota(jnp.int32, (rows, TQ), 1)
    )
    return buckets_of(relative)


def make_bias(table, parity, near_ref, tiles=(0, 1)):
    heads = near_ref.shape[0]
    for tile in tiles:
        def rows(step, _):
            start = pl.multiple_of(step * 32, 32)
            place = tile * TK + start
            after = place - near_start(parity)
            inside = jnp.logical_and(after >= 0, after < NEAR_ROWS)

            @pl.when(inside)
            def _():
                which = near_buckets(place, 32, parity)
                for h in range(heads):
                    value = jnp.zeros((32, TQ), jnp.float32)
                    for b in range(BUCKETS):
                        value = jnp.where(which == b, table[h, b], value)
                    near_ref[h, tile, pl.ds(start, 32)] = value.astype(jnp.bfloat16)

            @pl.when(jnp.logical_not(inside))
            def _():
                for h in range(heads):
                    value = jnp.where(after < 0, table[h, 15], table[h, 31])
                    near_ref[h, tile, pl.ds(start, 32)] = jnp.full((32, TQ), value, jnp.float32).astype(jnp.bfloat16)

            return 0
        lax.fori_loop(0, TK // 32, rows, 0)


def tile_kind(bounds, r, i, t):
    slot = jnp.clip(t - bounds[r, i, 2] + 1, 0, 3)
    away = jnp.logical_or(slot == 0, slot == 3)
    inside = jnp.logical_and(t >= bounds[r, i, 3], t < bounds[r, i, 4])
    return slot, jnp.logical_and(away, inside)


def fwd_kernel(alone, bounds, table, q_ref, kv_hbm, se_ref, *refs):
    if alone:
        near_ref, o_in, keep_in, lse_in, o_ref, keep_ref, lse_ref, vt, acc, mx, qp, kv_ref, kv_sem = refs
    else:
        o_ref, keep_ref, lse_ref, near_ref, vt, acc, mx, qp, kv_ref, kv_sem = refs
        make_bias(table, bounds[0, 0, 5], near_ref)
    heads = lse_ref.shape[2]
    base = 1 - bounds[0, 0, 6] if alone else 0

    def row_body(at, _):
        r = base + at
        lo_all = jnp.minimum(bounds[r, 0, 0], bounds[r, 1, 0])
        hi_all = jnp.maximum(bounds[r, 0, 1], bounds[r, 1, 1])

        def fetch(t):
            rows = pl.ds(pl.multiple_of(t * TK, TK), TK)
            return pltpu.make_async_copy(kv_hbm.at[r, rows], kv_ref.at[rows], kv_sem.at[t])

        def begin(t, _):
            fetch(t).start()
            return 0

        lax.fori_loop(lo_all, hi_all, begin, 0)
        for i in range(2):
            for h, tile in enumerate(spread_lanes(q_ref[r, i], False)):
                qp[i, h] = tile

        def turn(t, _):
            fetch(t).wait()
            k0 = pl.multiple_of(t * TK, TK)
            for h in range(heads):
                tile = kv_ref[pl.ds(k0, TK), h * 128 : h * 128 + 128]
                vt[h, 0:64, pl.ds(k0, TK)] = tile.T[64:128, :]
                vt[h, 64:80, pl.ds(k0, TK)] = jnp.ones((16, TK), jnp.bfloat16)
            return 0

        lax.fori_loop(lo_all, hi_all, turn, 0)

        def q_body(i, _):
            acc[...] = jnp.zeros_like(acc)
            mx[...] = jnp.full_like(mx, FIRST_MAX)

            def tile_body(t, _):
                k0 = pl.multiple_of(t * TK, TK)
                slot, plain = tile_kind(bounds, r, i, t)
                near = jnp.logical_and(slot > 0, slot < 3)

                def scores(h):
                    return mxu(kv_ref[pl.ds(k0, TK), h * 128 : h * 128 + 128], qp[i, h], NT)

                def finish(h, s, b):
                    m_old = mx[h]
                    m_new = jnp.maximum(m_old, jnp.max(s, axis=0, keepdims=True) + b)
                    p = jnp.exp(s - (m_new - b)).astype(jnp.bfloat16)
                    mx[h] = m_new
                    acc[h] = acc[h] * jnp.exp(m_old - m_new) + mxu(vt[h, :, pl.ds(k0, TK)], p)

                @pl.when(plain)
                def _():
                    found = [scores(h) for h in range(heads)]
                    for h in range(heads):
                        finish(h, found[h], jnp.where(slot == 0, table[h, 15], table[h, 31]))

                @pl.when(near)
                def _():
                    ok = valid_mask(se_ref, r, i, k0)
                    for h in range(heads):
                        s = scores(h) + near_ref[h, slot - 1].astype(jnp.float32)
                        finish(h, jnp.where(ok, s, NEG), 0.0)

                @pl.when(jnp.logical_not(jnp.logical_or(plain, near)))
                def _():
                    ok = valid_mask(se_ref, r, i, k0)
                    for h in range(heads):
                        s = scores(h) + jnp.where(slot == 0, table[h, 15], table[h, 31])
                        finish(h, jnp.where(ok, s, NEG), 0.0)

                return 0

            lax.fori_loop(bounds[r, i, 0], bounds[r, i, 1], tile_body, 0)
            parts = []
            for h in range(heads):
                total = acc[h, 64:65, :]
                parts.append((acc[h, 0:64, :] / total).T)
                lse_ref[r, i, h] = mx[h] + jnp.log(total)
            joined = join_heads(parts)
            o_ref[r, i] = joined.astype(jnp.bfloat16)
            keep_ref[r, i] = joined
            return 0

        lax.fori_loop(0, 2, q_body, 0)
        return 0

    lax.fori_loop(0, 1 if alone else 2, row_body, 0)
    if alone:
        o_ref[1 - base] = o_in[...]
        keep_ref[1 - base] = keep_in[...]
        lse_ref[1 - base] = lse_in[...]


def attention(bounds, table, q, kv, se, ready=()):
    heads, n = kv.shape[2] // 128, kv.shape[1]
    packed = q.shape
    outs = [
        jax.ShapeDtypeStruct(packed, jnp.bfloat16),
        jax.ShapeDtypeStruct(packed, jnp.float32),
        jax.ShapeDtypeStruct((2, 2, heads, 1, TQ), jnp.float32),
    ]
    if not ready:
        outs.append(jax.ShapeDtypeStruct((heads, 2, TK, TQ), jnp.bfloat16))
    return pl.pallas_call(
        functools.partial(fwd_kernel, bool(ready)),
        out_shape=tuple(outs),
        in_specs=[SMEM_SPEC] * 2 + [VMEM_SPEC, ANY_SPEC, VMEM_SPEC] + [VMEM_SPEC] * len(ready),
        out_specs=(VMEM_SPEC,) * len(outs),
        scratch_shapes=[
            pltpu.VMEM((heads, 80, n), jnp.bfloat16),
            pltpu.VMEM((heads, 80, TQ), jnp.float32),
            pltpu.VMEM((heads, 1, TQ), jnp.float32),
            pltpu.VMEM((2, heads, TQ, 128), jnp.bfloat16),
            pltpu.VMEM(kv.shape[1:], jnp.bfloat16),
            pltpu.SemaphoreType.DMA((n // TK,)),
        ],
        compiler_params=pltpu.CompilerParams(vmem_limit_bytes=VMEM_BYTES),
        name="attention",
    )(bounds, table, q, kv, se, *ready)


def prepare(q, do, q_out, do_out):
    for h, tile in enumerate(spread_lanes(q, False)):
        q_out[h] = tile
    for h, tile in enumerate(spread_lanes(do, True)):
        do_out[h] = tile


def row_deltas(do, keep, delta):
    prod = (do.astype(jnp.float32) * keep).T
    top, low = prod[:, 0:TQ], prod[:, TQ:]
    delta[0] = jnp.sum(top[0:64], axis=0, keepdims=True)
    delta[1] = jnp.sum(top[64:128], axis=0, keepdims=True)
    delta[2] = jnp.concatenate(
        [jnp.sum(low[0:64], axis=0, keepdims=True), jnp.sum(low[64:128], axis=0, keepdims=True)], axis=1
    )


def near_start(parity):
    return 416 - TQ * parity


def far_sums(grid, h, first, end):
    def one(step, total):
        rows = grid[h, pl.ds(pl.multiple_of(step * 32, 32), 32)]
        return total + jnp.sum(rows.reshape(4, 8, TQ), axis=0)
    total = lax.fori_loop(first // 32, end // 32, one, jnp.zeros((8, TQ), jnp.float32))
    return jnp.sum(total, axis=0, keepdims=True)


def bucket_sums(parity, near, side, tab_ref, tab8):
    heads = near.shape[0]
    tab8[...] = jnp.zeros_like(tab8)

    def inner(step, _):
        start = pl.multiple_of(step * 32, 32)
        which = near_buckets(near_start(parity) + start, 32, parity)
        for b in range(BUCKETS):
            here = which == b
            for h in range(heads):
                rows = jnp.where(here, near[h, pl.ds(start, 32)], 0.0)
                tab8[h, b] += jnp.sum(rows.reshape(4, 8, TQ), axis=0)
        return 0

    lax.fori_loop(0, NEAR_ROWS // 32, inner, 0)
    for h in range(heads):
        tab_ref[h] = jnp.sum(tab8[h], axis=1)
        tab_ref[h, 15:16] += side[h, 0:1]
        tab_ref[h, 31:32] += side[h, 1:2]


def bwd_kernel(alone, bounds, table, q_ref, do_ref, keep_ref, kv_hbm, bias_ref, se_ref, lse_ref,
               dq_ref, dkv_ref, near_ref, side, delta, *rest):
    tab_ref, tab8, rest = (None, None, rest) if alone else (rest[0], rest[-1], rest[1:-1])
    kt, dqt, dkv, grid, qp, dp_ref, kv_ref, kv_sem = rest
    heads = lse_ref.shape[2]
    n = kv_hbm.shape[1]
    grid[...] = jnp.zeros_like(grid)
    side[...] = jnp.zeros_like(side)
    base = 1 - bounds[0, 0, 6] if alone else 0
    for at in range(1 if alone else 2):
        for i in range(2):
            prepare(q_ref[base + at, i], do_ref[base + at, i], qp.at[at, i], dp_ref.at[at, i])
    for r in range(2):
        for i in range(2):
            row_deltas(do_ref[r, i], keep_ref[r, i], delta.at[r, i])

    def row_body(at, _):
        r = base + at
        lo_all = jnp.minimum(bounds[r, 0, 0], bounds[r, 1, 0])
        hi_all = jnp.maximum(bounds[r, 0, 1], bounds[r, 1, 1])

        def fetch(t):
            rows = pl.ds(pl.multiple_of(t * TK, TK), TK)
            return pltpu.make_async_copy(kv_hbm.at[r, rows], kv_ref.at[rows], kv_sem.at[t])

        def begin(t, _):
            fetch(t).start()
            return 0

        lax.fori_loop(lo_all, hi_all, begin, 0)

        def clear(t, _):
            k0 = pl.multiple_of(t * TK, TK)
            for h in range(heads):
                dkv[h, pl.ds(k0, TK), :] = jnp.zeros((TK, 128), jnp.float32)
            return 0

        lax.fori_loop(0, n // TK, clear, 0)

        def turn(t, _):
            fetch(t).wait()
            k0 = pl.multiple_of(t * TK, TK)
            for h in range(heads):
                tile = kv_ref[pl.ds(k0, TK), h * 128 : h * 128 + 128]
                kt[h, 0:64, pl.ds(k0, TK)] = tile.T[0:64, :]
                kt[h, 64:80, pl.ds(k0, TK)] = jnp.ones((16, TK), jnp.bfloat16)
            return 0

        lax.fori_loop(lo_all, hi_all, turn, 0)

        def q_body(i, _):
            dqt[...] = jnp.zeros_like(dqt)

            def tile_body(t, _):
                k0 = pl.multiple_of(t * TK, TK)
                slot, plain = tile_kind(bounds, r, i, t)

                def finish(h, p, ds, where):
                    ds_low = ds.astype(jnp.bfloat16)
                    two = jnp.concatenate([ds_low, p.astype(jnp.bfloat16)], axis=1)
                    both = jnp.concatenate([qp[at, i, h], dp_ref[at, i, h]], axis=0)
                    dkv[h, pl.ds(k0, TK), :] += mxu(two, both)
                    dqt[h, where] += mxu(kt[h, :, pl.ds(k0, TK)], ds_low)

                def products(h):
                    tile = kv_ref[pl.ds(k0, TK), h * 128 : h * 128 + 128]
                    return mxu(tile, qp[at, i, h], NT), mxu(tile, dp_ref[at, i, h], NT)

                @pl.when(plain)
                def _():
                    for h in range(heads):
                        s, d_probs = products(h)
                        p = jnp.exp(s - (lse_ref[r, i, h] - jnp.where(slot == 0, table[h, 15], table[h, 31])))
                        finish(h, p, p * (d_probs - delta[r, i, h]), jnp.where(slot == 0, 0, 2))

                def general(bias):
                    ok = valid_mask(se_ref, r, i, k0)
                    for h in range(heads):
                        s, d_probs = products(h)
                        s = s + bias(h)
                        p = jnp.where(ok, jnp.exp(jnp.where(ok, s, NEG) - lse_ref[r, i, h]), 0.0)
                        ds = p * (d_probs - delta[r, i, h])
                        grid[h, pl.ds(pl.multiple_of(slot * TK, TK), TK)] += ds
                        finish(h, p, ds, 1)

                near = jnp.logical_and(slot > 0, slot < 3)
                pl.when(near)(lambda: general(lambda h: bias_ref[h, slot - 1].astype(jnp.float32)))
                away = jnp.logical_not(jnp.logical_or(plain, near))
                pl.when(away)(lambda: general(lambda h: jnp.where(slot == 0, table[h, 15], table[h, 31])))
                return 0

            lax.fori_loop(bounds[r, i, 0], bounds[r, i, 1], tile_body, 0)
            parts = []
            for h in range(heads):
                parts.append((dqt[h, 0, 0:64] + dqt[h, 1, 0:64] + dqt[h, 2, 0:64]).T * 0.125)
                side[h, 0:1] += dqt[h, 0, 64:65]
                side[h, 1:2] += dqt[h, 2, 64:65]
            dq_ref[at, i] = join_heads(parts).astype(jnp.bfloat16)
            return 0

        lax.fori_loop(0, 2, q_body, 0)

        def put(t, _):
            k0 = pl.multiple_of(t * TK, TK)
            for h in range(heads):
                dkv_ref[at, pl.ds(k0, TK), h * 128 : h * 128 + 128] = dkv[h, pl.ds(k0, TK), :].astype(jnp.bfloat16)
            return 0

        lax.fori_loop(0, n // TK, put, 0)
        return 0

    lax.fori_loop(0, 1 if alone else 2, row_body, 0)

    parity = bounds[0, 0, 5]
    first = TK + near_start(parity)
    for h in range(heads):
        near_ref[h] = grid[h, pl.ds(pl.multiple_of(first, 32), NEAR_ROWS)]
        side[h, 0:1] += far_sums(grid, h, 0, first)
        side[h, 1:2] += far_sums(grid, h, first + NEAR_ROWS, 4 * TK)
    if not alone:
        bucket_sums(parity, near_ref, side, tab_ref, tab8)


def attention_back(alone, bounds, table, q, do, keep, kv, bias, se, lse):
    heads, n = kv.shape[2] // 128, kv.shape[1]
    count = 1 if alone else 2
    table_out = [] if alone else [jax.ShapeDtypeStruct((heads, BUCKETS, TQ), jnp.float32)]
    return pl.pallas_call(
        functools.partial(bwd_kernel, alone),
        out_shape=(
            jax.ShapeDtypeStruct((count,) + q.shape[1:], jnp.bfloat16),
            jax.ShapeDtypeStruct((count,) + kv.shape[1:], jnp.bfloat16),
            jax.ShapeDtypeStruct((heads, NEAR_ROWS, TQ), jnp.float32),
            jax.ShapeDtypeStruct((heads, 2, TQ), jnp.float32),
            jax.ShapeDtypeStruct((2, 2, heads, 1, TQ), jnp.float32),
        ) + tuple(table_out),
        in_specs=[SMEM_SPEC] * 2 + [VMEM_SPEC] * 3 + [ANY_SPEC] + [VMEM_SPEC] * 3,
        out_specs=(VMEM_SPEC,) * (5 + len(table_out)),
        scratch_shapes=[
            pltpu.VMEM((heads, 80, n), jnp.bfloat16),
            pltpu.VMEM((heads, 3, 80, TQ), jnp.float32),
            pltpu.VMEM((heads, n, 128), jnp.float32),
            pltpu.VMEM((heads, 4 * TK, TQ), jnp.float32),
            pltpu.VMEM((count, 2, heads, TQ, 128), jnp.bfloat16),
            pltpu.VMEM((count, 2, heads, TQ, 128), jnp.bfloat16),
            pltpu.VMEM(kv.shape[1:], jnp.bfloat16),
            pltpu.SemaphoreType.DMA((n // TK,)),
        ] + [pltpu.VMEM((heads, BUCKETS, 8, TQ), jnp.float32) for _ in table_out],
        compiler_params=pltpu.CompilerParams(vmem_limit_bytes=VMEM_BYTES),
        name="attention_back",
    )(bounds, table, q, do, keep, kv, bias, se, lse)


TAPS = tuple(range(-3, 5))
LEAD = 8


def pool_scalars(y_rows, lab_rows, first):
    tokens = y_rows[0].shape[1]
    t = lax.broadcasted_iota(jnp.int32, (1, tokens), 1)
    at = lambda rows, k: rows[k + 3]
    found = []
    for p in range(2):
        inside = {1: 0 * t, 2: 0 * t + p, 3: (first + 2 * t + p) % 3, 4: 2 * (t % 2) + p}
        weights, scores = {}, []
        for b in range(1, MAX_BLOCK + 1):
            keep = {}
            for o in range(1 - b, b):
                same = jnp.logical_and(inside[b] + o >= 0, inside[b] + o < b)
                same = jnp.logical_and(same, at(lab_rows, p + o) == at(lab_rows, p))
                keep[o] = same.astype(jnp.float32)
            inverse = 1.0 / sum(keep.values())
            for o in keep:
                weights[b, o] = keep[o] * inverse
            scores.append(sum(weights[b, o] * at(y_rows, p + o) for o in keep))
        top = functools.reduce(jnp.maximum, scores)
        grown = [jnp.exp(s - top) for s in scores]
        total = sum(grown)
        found.append(([g / total for g in grown], weights))
    return found


def tap_weights(found):
    rows = []
    for k in TAPS:
        row = 0.0
        for p, (probs, weights) in enumerate(found):
            for b in range(1, MAX_BLOCK + 1):
                if (b, k - p) in weights:
                    row = row + probs[b - 1] * weights[b, k - p]
        rows.append(0.5 * row)
    return rows


def as_columns(rows):
    tokens = rows[0].shape[1]
    return jnp.concatenate(list(rows) + [jnp.zeros((128 - len(rows), tokens), jnp.float32)], axis=0).T


def load_bytes(x_ref, before, after, xs):
    length, width = x_ref.shape
    for j in range(width // 128):
        cols = slice(j * 128, j * 128 + 128)
        xs[j, 0:LEAD, :] = jnp.zeros((LEAD, 128), jnp.float32)
        xs[j, LEAD + length :, :] = jnp.zeros((LEAD, 128), jnp.float32)
        xs[j, LEAD - 2 : LEAD, :] = before[:, cols].astype(jnp.float32)
        xs[j, LEAD + length : LEAD + length + 2, :] = after[:, cols].astype(jnp.float32)
        xs[j, LEAD : LEAD + length, :] = x_ref[:, cols].astype(jnp.float32)


def tap(xs, k, tokens):
    return jnp.concatenate([xs[j, pl.ds(LEAD + k, tokens, stride=2), :] for j in range(xs.shape[0])], axis=1)


def strips(buf, first, rows):
    return jnp.concatenate([buf[j, first : first + rows, :] for j in range(buf.shape[0])], axis=1)


def unit_rows(values):
    return lax.rsqrt(jnp.mean(values * values, axis=-1, keepdims=True) + 1e-06)


def pool_tokens(scale, xs, labels, score, gain, tokens, y_ref, share_ref):
    width = xs.shape[0] * 128
    score = jnp.broadcast_to(score, (8, width))
    for k in TAPS:
        y_ref[k + 3 : k + 4, :] = mxu(score, tap(xs, k, tokens).astype(jnp.bfloat16), NT)[0:1]
    rows = [y_ref[j : j + 1, :] for j in range(8)]
    first = (lax.axis_index("blk") * 2 * tokens) % 3
    found = pool_scalars(rows, labels, first)
    lane = lax.broadcasted_iota(jnp.int32, (1, 128), 1)
    share = jnp.zeros((1, 128), jnp.float32)
    for b in range(MAX_BLOCK):
        share = jnp.where(lane == b, jnp.sum(found[0][0][b] + found[1][0][b], axis=1, keepdims=True) * scale, share)
    share_ref[...] = share
    columns = as_columns(tap_weights(found))
    hidden = sum(columns[:, k + 3 : k + 4] * tap(xs, k, tokens) for k in TAPS)
    return hidden, (hidden * unit_rows(hidden) * gain.astype(jnp.float32)).astype(jnp.bfloat16)


def put_pairs(keys, values, kv_ref):
    low = lax.broadcasted_iota(jnp.int32, (1, 128), 1) < 64
    for j in range(keys.shape[1] // 128):
        k_pair, v_pair = keys[:, j * 128 : j * 128 + 128], values[:, j * 128 : j * 128 + 128]
        one = jnp.where(low, k_pair, turned(v_pair))
        two = jnp.where(low, turned(k_pair), v_pair)
        for head, tile in ((2 * j, one), (2 * j + 1, two)):
            kv_ref[head // 3, :, head % 3 * 128 : head % 3 * 128 + 128] = tile


def pool_kernel(shards, scale, x_ref, before_ref, after_ref, lab_ref, score_ref, gain_ref, wq_ref, wk_ref, wv_ref,
                hidden_ref, n1_ref, y_ref, share_ref, q_ref, kv_ref, xs):
    tokens = hidden_ref.shape[0]
    load_bytes(x_ref, before_ref[0:2, :], after_ref[0:2, :], xs)
    labels = [lab_ref[j : j + 1, :] for j in range(8)]
    hidden_ref[...], n1 = pool_tokens(scale, xs, labels, score_ref[...], gain_ref[...], tokens, y_ref, share_ref)
    n1_ref[...] = n1
    put_pairs(mxu(n1, wk_ref[...]).astype(jnp.bfloat16), mxu(n1, wv_ref[...]).astype(jnp.bfloat16), kv_ref)
    put_packed(mxu(n1, wq_ref[...]).astype(jnp.bfloat16) * jnp.bfloat16(0.125), q_ref)


def put_packed(array, out_ref):
    tokens = array.shape[0]
    half = tokens // 2
    for g in range(GROUPS):
        part = array[:, g * 192 : g * 192 + 192]
        out_ref[g, 0:tokens, :] = part[:, 0:128]
        out_ref[g, tokens:, :] = jnp.concatenate([part[:half, 128:], part[half:, 128:]], axis=1)


def get_packed(packed_ref):
    tokens = packed_ref.shape[1] * 2 // 3
    parts = []
    for g in range(GROUPS):
        last = packed_ref[g, tokens:, :]
        parts += [packed_ref[g, 0:tokens, :], jnp.concatenate([last[:, :64], last[:, 64:]], axis=0)]
    return jnp.concatenate(parts, axis=1)


def pool_and_project(shards, scale, x, before, after, labels, score, gain, wq, wk, wv):
    length, width = x.shape
    tokens = length // 2
    return pl.pallas_call(
        functools.partial(pool_kernel, shards, scale),
        out_shape=(
            jax.ShapeDtypeStruct((tokens, width), jnp.float32),
            jax.ShapeDtypeStruct((tokens, width), jnp.bfloat16),
            jax.ShapeDtypeStruct((8, tokens), jnp.float32),
            jax.ShapeDtypeStruct((1, 128), jnp.float32),
            jax.ShapeDtypeStruct((GROUPS, tokens * 3 // 2, 128), jnp.bfloat16),
            jax.ShapeDtypeStruct((GROUPS, tokens, width * 2 // GROUPS), jnp.bfloat16),
        ),
        in_specs=[VMEM_SPEC] * 9,
        out_specs=(VMEM_SPEC,) * 6,
        scratch_shapes=[pltpu.VMEM((width // 128, length + 2 * LEAD, 128), jnp.float32)],
        compiler_params=pltpu.CompilerParams(vmem_limit_bytes=VMEM_BYTES),
        name="pool_and_project",
    )(x, before, after, labels, score, gain, wq, wk, wv)


GELU_A = math.sqrt(2.0 / math.pi)
GELU_B = 0.044715


def norm_back(d_out, rows, gain):
    unit = unit_rows(rows)
    flat = rows * unit
    scaled = d_out * gain
    d_rows = unit * (scaled - flat * jnp.mean(scaled * flat, axis=-1, keepdims=True))
    return d_rows, jnp.sum(d_out * flat, axis=0, keepdims=True)


def feed_kernel(o_ref, hidden_ref, ct_ref, gain_ref, wo_ref, wg_ref, wu_ref, wd_ref,
                out_ref, dres_ref, da_ref, dgain_ref, n2_ref, att_ref, act_ref, dg_ref, du_ref, db_ref, acc, dn2):
    ff = wg_ref.shape[1]
    step = 512
    att = get_packed(o_ref)
    att_ref[...] = att
    residual = hidden_ref[...] + mxu(att, wo_ref[...])
    gain = gain_ref[...].astype(jnp.float32)
    n2_ref[...] = (residual * unit_rows(residual) * gain).astype(jnp.bfloat16)
    acc[...] = residual
    dn2[...] = jnp.zeros_like(dn2)

    for j in range(ff // step):
        cols = slice(j * step, j * step + step)
        n2 = n2_ref[...]
        gate = mxu(n2, wg_ref[:, cols])
        up = mxu(n2, wu_ref[:, cols])
        d_act = mxu(ct_ref[...], wd_ref[cols, :], NT)
        square = gate * gate
        curve = jnp.tanh(GELU_A * gate * (1.0 + GELU_B * square))
        half = 0.5 * (1.0 + curve)
        grown = gate * half
        slope = half + 0.5 * gate * (1.0 - curve * curve) * (GELU_A * (1.0 + 3.0 * GELU_B * square))
        act = (grown * up).astype(jnp.bfloat16)
        d_gate = (d_act * up * slope).astype(jnp.bfloat16)
        d_up = (d_act * grown).astype(jnp.bfloat16)
        act_ref[:, cols] = act
        dg_ref[:, cols] = d_gate
        du_ref[:, cols] = d_up
        acc[...] += mxu(act, wd_ref[cols, :])
        dn2[...] += mxu(d_gate, wg_ref[:, cols], NT) + mxu(d_up, wu_ref[:, cols], NT)

    out_ref[...] = acc[...].astype(jnp.bfloat16)
    residual = hidden_ref[...] + mxu(att_ref[...], wo_ref[...])
    d_rows, d_gain = norm_back(dn2[...], residual, gain)
    dgain_ref[...] = d_gain
    d_res = ct_ref[...].astype(jnp.float32) + d_rows
    dres_ref[...] = d_res
    d_branch = d_res.astype(jnp.bfloat16)
    db_ref[...] = d_branch
    put_packed(mxu(d_branch, wo_ref[...], NT).astype(jnp.bfloat16), da_ref)


def feed_forward(o_home, hidden, ct, gain, wo, wg, wu, wd):
    tokens, width = hidden.shape
    ff = wg.shape[1]
    low = lambda cols: jax.ShapeDtypeStruct((tokens, cols), jnp.bfloat16)
    return pl.pallas_call(
        feed_kernel,
        out_shape=(
            low(width),
            jax.ShapeDtypeStruct((tokens, width), jnp.float32),
            jax.ShapeDtypeStruct(o_home.shape, jnp.bfloat16),
            jax.ShapeDtypeStruct((1, width), jnp.float32),
            low(width), low(width), low(ff), low(ff), low(ff), low(width),
        ),
        in_specs=[VMEM_SPEC] * 8,
        out_specs=(VMEM_SPEC,) * 10,
        scratch_shapes=[pltpu.VMEM((tokens, width), jnp.float32)] * 2,
        compiler_params=pltpu.CompilerParams(vmem_limit_bytes=VMEM_BYTES),
        name="feed_forward",
    )(o_home, hidden, ct, gain, wo, wg, wu, wd)


def unpack_pairs(dkv_ref, width):
    low = lax.broadcasted_iota(jnp.int32, (1, 128), 1) < 64
    dk_parts, dv_parts = [], []
    for j in range(width // 128):
        one, two = [dkv_ref[h // 3, :, h % 3 * 128 : h % 3 * 128 + 128] for h in (2 * j, 2 * j + 1)]
        dk_parts.append(jnp.where(low, one, turned(two)))
        dv_parts.append(jnp.where(low, turned(one), two))
    return jnp.concatenate(dk_parts, axis=1), jnp.concatenate(dv_parts, axis=1)


def pool_back(d_hidden, length, lab_ref, y_ref, score, gb_ref, edge_ref, spill_ref, xs, gbuf):
    tokens, width = d_hidden.shape
    lane = lax.broadcasted_iota(jnp.int32, (1, 128), 1)
    met = jnp.zeros((tokens, 128), jnp.float32)
    for k in TAPS:
        met = jnp.where(lane == k + 3, jnp.sum(d_hidden * tap(xs, k, tokens), axis=-1, keepdims=True), met)
    met = met.T
    first = (lax.axis_index("blk") * length) % 3
    found = pool_scalars([y_ref[j : j + 1, :] for j in range(8)], [lab_ref[j : j + 1, :] for j in range(8)], first)
    touch = [0.0] * 8
    for p, (probs, weights) in enumerate(found):
        d_block = []
        for b in range(1, MAX_BLOCK + 1):
            d_block.append(0.5 * sum(weights[b, o] * met[p + o + 3 : p + o + 4] for o in range(1 - b, b)))
        mean = sum(q * d for q, d in zip(probs, d_block))
        for b in range(1, MAX_BLOCK + 1):
            d_score = probs[b - 1] * (d_block[b - 1] - mean)
            for o in range(1 - b, b):
                touch[p + o + 3] = touch[p + o + 3] + d_score * weights[b, o]
    share_cols = as_columns(tap_weights(found) + touch)
    score = score.astype(jnp.float32)
    gbuf[...] = jnp.zeros_like(gbuf)
    d_score_vec = jnp.zeros((1, width), jnp.float32)
    for k in TAPS:
        own, via = share_cols[:, k + 3 : k + 4], share_cols[:, k + 11 : k + 12]
        added = own * d_hidden + via * score
        for j in range(gbuf.shape[0]):
            gbuf[j, pl.ds(LEAD + k, tokens, stride=2), :] += added[:, j * 128 : j * 128 + 128]
        d_score_vec = d_score_vec + jnp.sum(via * tap(xs, k, tokens), axis=0, keepdims=True)
    gb_ref[...] = strips(gbuf, LEAD, length).astype(jnp.bfloat16)
    edge_ref[0] = strips(gbuf, LEAD, 16)
    edge_ref[1] = strips(gbuf, LEAD + length - 16, 16)
    spill_ref[0] = strips(gbuf, 0, LEAD)
    spill_ref[1] = strips(gbuf, LEAD + length, LEAD)
    return d_score_vec


def put_small(small_ref, vectors, tab_ref, share_ref):
    small_ref[...] = jnp.zeros_like(small_ref)
    for row, vector in zip((0, 6, 12), vectors):
        for j in range(6):
            small_ref[row + j : row + j + 1, :] = vector[:, j * 128 : j * 128 + 128]
    heads = tab_ref.shape[0]
    group = lax.axis_index("blk") // (lax.axis_size("blk") // GROUPS)
    for h in range(heads):
        total = lax.dot_general(
            jnp.ones((8, tab_ref.shape[2]), jnp.float32), tab_ref[h], NT,
            precision=lax.Precision.HIGHEST, preferred_element_type=jnp.float32,
        )
        small_ref[pl.ds(18 + group * heads + h, 1), 0:BUCKETS] = total[0:1]
    small_ref[30:31, :] = share_ref[...]


def last_kernel(shards, axes, order, dq_ref, dkv_ref, hidden_ref, dres_ref, x_ref, before_ref, after_ref, lab_ref, y_ref, score_ref,
                gain_ref, wq_ref, wk_ref, wv_ref, dgain2_ref, share_ref, tab_ref, gb_ref, edge_ref, spill_out, small_out, parts_ref,
                w_send, w_recv, s_send, s_recv, xs, gbuf, spill_ref, small_ref, small_bufs):
    at = {"dp": lax.axis_index("dp"), "blk": lax.axis_index("blk")}
    width = hidden_ref.shape[1]
    whole = Whole(axes, at, order, small_ref, small_bufs, small_out, w_send, w_recv)
    left = (at["dp"], (at["blk"] + shards - 1) % shards)
    right = (at["dp"], (at["blk"] + 1) % shards)
    greet([whole.stream.target(p) for p in range(len(axes))] + [left, right])
    load_bytes(x_ref, before_ref[0:2, :], after_ref[0:2, :], xs)
    dq = get_packed(dq_ref)
    dk, dv = unpack_pairs(dkv_ref, width)
    parts_ref[0], parts_ref[1], parts_ref[2] = dq, dk, dv
    d_n1 = mxu(dq, wq_ref[...], NT) + mxu(dk, wk_ref[...], NT) + mxu(dv, wv_ref[...], NT)
    d_rows, d_gain1 = norm_back(d_n1, hidden_ref[...], gain_ref[...].astype(jnp.float32))
    d_hidden = dres_ref[...] + d_rows
    d_score = pool_back(d_hidden, x_ref.shape[0], lab_ref, y_ref, score_ref[...], gb_ref, edge_ref, spill_ref, xs, gbuf)
    put_small(small_ref, (d_score, d_gain1, dgain2_ref[...]), tab_ref, share_ref)
    spills = [
        remote(spill_ref.at[0], spill_out.at[1], s_send.at[0], s_recv.at[1], left),
        remote(spill_ref.at[1], spill_out.at[0], s_send.at[1], s_recv.at[0], right),
    ]
    whole.copy(0).start()
    for copy in spills:
        copy.start()
    for stage in range(len(axes)):
        advance(whole, stage)
    for copy in spills:
        copy.wait()


def last_part(shape, dq, dkv, hidden, dres, x, before, after, labels, y, score, gain, wq, wk, wv, dgain2, share, tab):
    tokens, width = hidden.shape
    length = x.shape[0]
    axes = bit_axes(shape)
    ndim = len(axes)
    full, sem, low = jax.ShapeDtypeStruct, pltpu.SemaphoreType.DMA, jnp.bfloat16
    strip = pltpu.VMEM((width // 128, length + 2 * LEAD, 128), jnp.float32)
    return pl.pallas_call(
        functools.partial(last_kernel, shape["blk"], axes, tuple(reversed(range(ndim)))),
        out_shape=(
            full((length, width), low),
            full((2, 16, width), jnp.float32),
            full((2, LEAD, width), jnp.float32),
            full((32, 128), jnp.float32),
            full((3, tokens, width), low),
        ),
        in_specs=[VMEM_SPEC] * 17,
        out_specs=(VMEM_SPEC,) * 5,
        scratch_shapes=[
            sem((ndim,)), sem((ndim,)), sem((2,)), sem((2,)), strip, strip,
            pltpu.VMEM((2, LEAD, width), jnp.float32), pltpu.VMEM((32, 128), jnp.float32), pltpu.VMEM((2, ndim, 32, 128), jnp.float32),
        ],
        compiler_params=pltpu.CompilerParams(collective_id=3, has_side_effects=True, vmem_limit_bytes=VMEM_BYTES),
        name="last_part",
    )(dq, dkv, hidden, dres, x, before, after, labels, y, score, gain, wq, wk, wv, dgain2, share, tab)


def finish_kernel(shards, block_ref, gb_ref, edge_ref, spill_ref, small_ref, *refs):
    position = lax.axis_index("blk")
    count = 7 if len(refs) == 7 else 14
    streams, outs = refs[: len(refs) - count], refs[len(refs) - count :]
    out_ref, bytes_ref, score_ref, gain1_ref, gain2_ref, tab_ref, share_ref = outs[:7]
    out_ref[...] = block_ref[...]
    length = gb_ref.shape[0]
    bytes_ref[...] = gb_ref[...]
    zero = jnp.zeros((16 - LEAD, gb_ref.shape[1]), jnp.float32)
    left = jnp.where(position > 0, spill_ref[0], 0.0)
    right = jnp.where(position < shards - 1, spill_ref[1], 0.0)
    bytes_ref[0:16, :] = (edge_ref[0] + jnp.concatenate([left, zero], axis=0)).astype(jnp.bfloat16)
    bytes_ref[length - 16 :, :] = (edge_ref[1] + jnp.concatenate([zero, right], axis=0)).astype(jnp.bfloat16)
    for row, ref in ((0, score_ref), (6, gain1_ref), (12, gain2_ref)):
        for j in range(6):
            ref[j * 128 : j * 128 + 128] = small_ref[row + j, :]
    tab_ref[...] = small_ref[16:32, :].T[: tab_ref.shape[0], 2 : 2 + tab_ref.shape[1]]
    share_ref[...] = small_ref[30, 0:MAX_BLOCK]
    if streams:
        gq, gk, gv, go, gg, gu, gd = outs[7:]
        per, width = gq.shape
        half, ff = width // 2, gg.shape[1]
        one, two, down, *thirds = streams
        for ref, third in zip((gq, gk, gv), thirds):
            ref[:, :half] = third[:per, :]
            ref[:, half:] = third[per:, :]
        first = one.shape[1]
        for ref, rows in ((gg, slice(0, per)), (gu, slice(per, 2 * per))):
            ref[:, :first] = one[rows, :]
            ref[:, first:] = two[rows, : ff - first]
        go[:, :half] = two[:per, ff - first :]
        go[:, half:] = two[per:, ff - first :]
        gd[...] = down[...]


def finish(shards, heads_all, per, ff, block_out, gb, edge, spill, small, streams):
    width = gb.shape[1]
    full = jax.ShapeDtypeStruct
    line = full((width,), jnp.float32)
    outs = [full(block_out.shape, jnp.bfloat16), full(gb.shape, jnp.bfloat16), line, line, line]
    outs += [full((BUCKETS, heads_all), jnp.float32), full((MAX_BLOCK,), jnp.float32)]
    if streams:
        square, broad = full((per, width), jnp.float32), full((per, ff), jnp.float32)
        outs += [square] * 4 + [broad] * 2 + [full(streams[2].shape, jnp.float32)]
    return pl.pallas_call(
        functools.partial(finish_kernel, shards),
        out_shape=tuple(outs),
        in_specs=[VMEM_SPEC] * (5 + len(streams)),
        out_specs=(VMEM_SPEC,) * len(outs),
        compiler_params=pltpu.CompilerParams(vmem_limit_bytes=VMEM_BYTES),
        name="finish",
    )(block_out, gb, edge, spill, small, *streams)


class NearRows:
    def __init__(self, grid, first):
        self.grid, self.first, self.shape = grid, first, grid.shape

    def __getitem__(self, index):
        h, rows = index
        return self.grid[h, pl.ds(pl.multiple_of(self.first + rows.start, 32), rows.size)]


class Refs:
    def __init__(self, **refs):
        self.__dict__.update(refs)


class BiasTable:
    def __init__(self, ref, place, heads):
        self.ref, self.first = ref, place.group * heads

    def __getitem__(self, index):
        head, bucket = index
        return self.ref[bucket, self.first + head]


class Held:
    def __init__(self, array, space):
        self.array, self.space = array, space


def call(kernel, ident, ins, outs, scratch):
    leaf = lambda entry: isinstance(entry, Held) or isinstance(entry, tuple) or not isinstance(entry, (dict, list))
    parts = [jax.tree.flatten(part, is_leaf=leaf) for part in (ins, outs, scratch)]
    counts = [len(part[0]) for part in parts]
    given, wanted, kept = [part[0] for part in parts]

    def run(*refs):
        named, start = {}, 0
        for count, (_, tree) in zip(counts, parts):
            named.update(jax.tree.unflatten(tree, refs[start : start + count]))
            start += count
        kernel(Refs(**named))

    space = lambda entry, at: entry.space if isinstance(entry, Held) else entry[2] if isinstance(entry, tuple) and len(entry) > 2 else at
    found = pl.pallas_call(
        run,
        out_shape=tuple(jax.ShapeDtypeStruct(entry[0], entry[1]) for entry in wanted),
        in_specs=[pl.BlockSpec(memory_space=space(entry, pltpu.VMEM)) for entry in given],
        out_specs=tuple(pl.BlockSpec(memory_space=space(entry, pltpu.VMEM)) for entry in wanted),
        scratch_shapes=kept,
        compiler_params=pltpu.CompilerParams(collective_id=ident, has_side_effects=True, vmem_limit_bytes=VMEM_BYTES),
        name=kernel.func.__name__,
    )(*[entry.array if isinstance(entry, Held) else entry for entry in given])
    return Refs(**jax.tree.unflatten(parts[1][1], found))


wide = lambda value: value.astype(jnp.float32)
slim = lambda value: value.astype(jnp.bfloat16)


class RowBack:
    def __init__(self, place, r):
        self.place, self.r = place, r
        self.heads = r.lse.shape[1]
        self.table = BiasTable(r.table, place, self.heads)
        self.tokens = TQ
        self.across, self.core_to = place.other_rest(2), place.other_rest(1)
        self.y, self.core = bit(place.rest, 2), place.rest % 2

    def group_of(self, n):
        return (self.place.group + 1 + n) % GROUPS

    def tile_start(self, m):
        place_y = jnp.where(m % 2 == 0, 1 - self.y, self.y)
        return pl.multiple_of((self.group_of(m // 2) * 2 + place_y) * TK, TK)

    def fetch(self, m):
        r = self.r
        rows = pl.ds(self.tile_start(m), TK)
        return (
            pltpu.make_async_copy(r.kv_hbm.at[rows], r.kv.at[m], r.kv_sem.at[m]),
            pltpu.make_async_copy(r.kl_hbm.at[rows], r.kl.at[m], r.kl_sem.at[m]),
        )

    def prepare(self):
        r = self.r
        for m in range(2 * GROUPS):
            for copy in self.fetch(m):
                copy.start()

        def one(i, _):
            for h, tile in enumerate(spread_lanes(r.q[i], False)):
                r.qp[i, h] = tile
            for h, tile in enumerate(spread_lanes(r.do[i], True)):
                r.dp[i, h] = tile
            row_deltas(r.do[i], r.keep[i], r.delta.at[i])
            return 0

        lax.fori_loop(0, GROUPS, one, 0)
        r.dqt[...] = jnp.zeros_like(r.dqt)
        r.grid[...] = jnp.zeros_like(r.grid)

    def core_copy(self, n, j):
        r = self.r
        return remote(r.held.at[n, j, 1 - self.core], r.core_in.at[n, j], r.core_send.at[n, j], r.core_recv.at[n, j], self.core_to)

    def y_copy(self, n):
        r = self.r
        return remote(r.y_out.at[n], r.y_in.at[n], r.y_send.at[n], r.y_recv.at[n], self.across)

    def z_copy(self, n):
        r, place = self.r, self.place
        return remote(r.z_out.at[n], r.dkv_home.at[place.group], r.z_send.at[n], r.z_recv.at[n], place.at(place.row, self.group_of(n), place.rest))

    def by_rows(self, one):
        def step(k, _):
            one(pl.ds(pl.multiple_of(k * 32, 32), 32))
            return 0
        lax.fori_loop(0, self.tokens // 32, step, 0)

    def own_sum(self, n, j, rows):
        return wide(self.r.held[n, j, self.core, rows]) + wide(self.r.core_in[n, j, rows])

    def send_y(self, n):
        r = self.r
        self.core_copy(n, 0).wait()

        def one(rows):
            r.y_out[n, rows] = slim(self.own_sum(n, 0, rows))

        self.by_rows(one)
        self.y_copy(n).start()

    def send_home(self, n):
        r = self.r
        self.core_copy(n, 1).wait()
        self.y_copy(n).wait()
        here = isinstance(n, int) and n == GROUPS - 1

        def one(rows):
            total = slim(self.own_sum(n, 1, rows) + wide(r.y_in[n, rows]))
            if here:
                r.dkv_home[self.place.group, rows] = total
            else:
                r.z_out[n, rows] = total

        self.by_rows(one)
        if not here:
            self.z_copy(n).start()

    def tile(self, m):
        r, place, heads = self.r, self.place, self.heads
        n, j = m // 2, m % 2
        t = self.tile_start(m) // TK
        for copy in self.fetch(m):
            copy.wait()
        r.acc[...] = jnp.zeros_like(r.acc)
        keys = lambda h: r.kv[m, :, h * 128 : h * 128 + 128]
        for h in range(heads):
            r.kt[h, 0:64] = keys(h).T[0:64]
            r.kt[h, 64:80] = jnp.ones((16, TK), jnp.bfloat16)

        def part(i, _):
            slot = near_slot(place, i, t)
            away = jnp.logical_or(slot == 0, slot == 3)

            def finish(h, p, ds, where):
                ds_low = ds.astype(jnp.bfloat16)
                two = jnp.concatenate([ds_low, p.astype(jnp.bfloat16)], axis=1)
                both = jnp.concatenate([r.qp[i, h], r.dp[i, h]], axis=0)
                r.acc[:, h * 128 : h * 128 + 128] += mxu(two, both)
                r.dqt[i, h, where] += mxu(r.kt[h], ds_low)

            def products(h):
                s = mxu(jnp.concatenate([keys(h), r.kl[m]], axis=1), jnp.concatenate([r.qp[i, h], r.ql[i]], axis=1), NT)
                return s, mxu(keys(h), r.dp[i, h], NT)

            @pl.when(away)
            def _():
                for h in range(heads):
                    s, d_probs = products(h)
                    p = jnp.exp(s - (r.lse[i, h] - jnp.where(slot == 0, self.table[h, 15], self.table[h, 31])))
                    finish(h, p, p * (d_probs - r.delta[i, h]), jnp.where(slot == 0, 0, 2))

            @pl.when(jnp.logical_not(away))
            def _():
                for h in range(heads):
                    s, d_probs = products(h)
                    p = jnp.exp(s + r.bias[h, slot - 1].astype(jnp.float32) - r.lse[i, h])
                    ds = p * (d_probs - r.delta[i, h])
                    r.grid[h, pl.ds(pl.multiple_of((slot - 1) * TK, TK), TK)] += ds
                    finish(h, p, ds, 1)

            return 0

        lax.fori_loop(0, GROUPS, part, 0)
        for half in range(2):
            r.held[n, j, half] = r.acc[half * self.tokens : half * self.tokens + self.tokens].astype(jnp.bfloat16)
        self.core_copy(n, j).start()

    def queries(self):
        r = self.r

        def one(i, _):
            parts = []
            for h in range(self.heads):
                parts.append((r.dqt[i, h, 0, 0:64] + r.dqt[i, h, 1, 0:64] + r.dqt[i, h, 2, 0:64]).T * 0.125)
            r.dq[i] = slim(join_heads(parts))
            return 0

        lax.fori_loop(0, GROUPS, one, 0)

    def buckets(self):
        r = self.r
        first = near_start(self.core)
        for h in range(self.heads):
            r.side[h, 0:1] = sum(r.dqt[i, h, 0, 64:65] for i in range(GROUPS)) + far_sums(r.grid, h, 0, first)
            r.side[h, 1:2] = sum(r.dqt[i, h, 2, 64:65] for i in range(GROUPS)) + far_sums(r.grid, h, first + NEAR_ROWS, 2 * TK)
        bucket_sums(self.core, NearRows(r.grid, first), r.side, r.tab, r.tab8)

    def wait_home(self):
        r, place = self.r, self.place
        for n in range(GROUPS - 1):
            there = r.dkv_home.at[(place.group - 1 - n + GROUPS) % GROUPS]
            remote(r.z_out.at[n], there, r.z_send.at[n], r.z_recv.at[n], self.core_to).wait()


def back_kernel(shards, axes, plans, r):
    place = Place(shards)
    at = {"dp": place.dp, "blk": place.blk}
    tokens, width = r.hidden.shape
    back = RowBack(place, r)
    streams = []
    for s, (kept, order) in enumerate(plans):
        src = r.early[s] if s < 3 else r.late[s - 3]
        streams.append(Stream(axes, at, kept, order, src, r.bufs[s], r.sums[s], r.w_send.at[s], r.w_recv.at[s]))
    early, late = streams[:3], streams[3:]
    whole = Whole(axes, at, (4, 0, 3, 2, 1), r.small, r.small_bufs, r.small_out, r.w_send.at[len(plans)], r.w_recv.at[len(plans)])
    left, right = (place.dp, (place.blk + shards - 1) % shards), (place.dp, (place.blk + 1) % shards)

    met = hail([place.other_group(step) for step in (1, 2, 3)] + [back.across, back.core_to, place.other_row(), left, right])
    back.prepare()
    await_all(met)
    for stream in early:
        stream.copy(0).start()

    def step(m, _):
        back.tile(m)
        for delay, action in ((1, back.send_y), (3, back.send_home)):
            then = m - delay + 2 * GROUPS
            n = then // 2 - GROUPS

            @pl.when(jnp.logical_and(then % 2 == 0, n >= 0))
            def _():
                action(n)

        for when, s in ((5, 0), (5, 2), (6, 1)):
            pl.when(m == when)(functools.partial(advance, early[s], 0))

        return 0

    lax.fori_loop(0, 2 * GROUPS, step, 0)
    back.queries()
    home = Line(place, r.dq, r.dq_home, r.q_send, r.q_recv)
    home.keep().start()
    home.start()
    back.send_home(3)
    for stream in early:
        advance(stream, 1)
    back.buckets()
    load_bytes(r.x, r.before[14:16, :], r.after[0:2, :], r.xs)
    n1_t = r.n1[...].T
    home.wait_all()
    dq = get_packed(r.dq_home)
    devices = 1 << len(axes)
    per = width // devices
    half = width // 2

    def weights(stream, part):
        r.total[...] = mxu(n1_t, part)

        def block(d, _):
            rows = pl.ds(pl.multiple_of(d * per, 8), per)
            index, rest = [], d
            for _ in axes:
                index.append(rest % 2)
                rest = rest // 2
            part = r.total[rows, :]
            stream.src[tuple(reversed(index))] = jnp.concatenate([part[:, :half], part[:, half:]], axis=0).astype(jnp.bfloat16)
            return 0

        lax.fori_loop(0, devices, block, 0)
        stream.copy(0).start()

    weights(late[0], dq)
    back.wait_home()
    dk, dv = unpack_pairs(r.dkv_home, width)
    weights(late[1], dk)
    weights(late[2], dv)
    d_n1 = mxu(dq, r.wq[...], NT) + mxu(dk, r.wk[...], NT) + mxu(dv, r.wv[...], NT)
    d_rows, d_gain1 = norm_back(d_n1, r.hidden[...], r.vectors[1:2, :].astype(jnp.float32))
    d_hidden = r.dres[...] + d_rows
    for stream in late:
        advance(stream, 0)
    for stream in early:
        advance(stream, 2)
    d_score = pool_back(d_hidden, r.x.shape[0], r.labels, r.y, r.vectors[0:1, :], r.gb, r.edge, r.spill, r.xs, r.gbuf)
    put_small(r.small, (d_score, d_gain1, r.dgain2[...]), r.tab, r.share)
    whole.copy(0).start()
    spills = [
        remote(r.spill.at[0], r.spill_out.at[1], r.s2_send.at[0], r.s2_recv.at[1], left),
        remote(r.spill.at[1], r.spill_out.at[0], r.s2_send.at[1], r.s2_recv.at[0], right),
    ]
    for copy in spills:
        copy.start()
    for stage in range(1, len(axes)):
        for stream in late:
            advance(stream, stage)
        advance(whole, stage - 1)
        if stage == 1:
            for stream in early:
                advance(stream, 3)
    advance(whole, len(axes) - 1)
    for copy in spills:
        copy.wait()


def back_and_last(shape, early, inputs):
    shards = shape["blk"]
    axes = bit_axes(shape)
    ndim = len(axes)
    kv, q, hidden = inputs["kv_hbm"].array, inputs["q"], inputs["hidden"]
    heads, width = kv.shape[1] // 128, kv.shape[1]
    tokens, features = hidden.shape
    length = inputs["x"].shape[0]
    f32, low, sem = jnp.float32, jnp.bfloat16, pltpu.SemaphoreType.DMA
    chunk = (tokens, width)
    every = (0, 1, 2, 3, 4)
    four = (0, 1, 2, 3)
    plans = [
        (four, (0, 3, 2, 1)), (four, (3, 0, 2, 1)), (four, (2, 0, 3, 1)),
        (every, (4, 0, 3, 2, 1)), (every, (4, 3, 2, 0, 1)), (every, (4, 2, 0, 3, 1)),
    ]
    own = (2 * (features // (1 << ndim)), features // 2)
    blocks = [part.shape[-2:] for part in early] + [own] * 3
    ins = dict(inputs, early=[part.reshape((2, 2, 2, 2) + part.shape[-2:]) for part in early])
    outs = dict(
        gb=((length, features), low), edge=((2, 16, features), f32), spill_out=((2, LEAD, features), f32),
        small_out=((32, 128), f32), sums=[(block, f32) for block in blocks],
    )
    mem = lambda shape, dtype=low: pltpu.VMEM(shape, dtype)
    pairs, fours = sem((GROUPS, 2)), sem((GROUPS,))
    strip = mem((features // 128, length + 2 * LEAD, 128), f32)
    eights = sem((2 * GROUPS,))
    scratch = dict(
        kt=mem((heads, 80, TK)), dqt=mem((GROUPS, heads, 3, 80, TQ), f32), acc=mem((TK, width), f32),
        grid=mem((heads, 2 * TK, TQ), f32), side=mem((heads, 2, TQ), f32), tab8=mem((heads, BUCKETS, 8, TQ), f32),
        tab=mem((heads, BUCKETS, TQ), f32), delta=mem((GROUPS, heads, 1, TQ), f32),
        qp=mem((GROUPS, heads, TQ, 128)), dp=mem((GROUPS, heads, TQ, 128)),
        kv=mem((2 * GROUPS, TK, width)), kl=mem((2 * GROUPS, TK, 128)),
        held=mem((GROUPS, 2, 2) + chunk), core_in=mem((GROUPS, 2) + chunk),
        y_out=mem((GROUPS,) + chunk), y_in=mem((GROUPS,) + chunk), z_out=mem((GROUPS,) + chunk), dkv_home=mem((GROUPS,) + chunk),
        dq=mem(q.shape), dq_home=mem(q.shape),
        core_send=pairs, core_recv=pairs, y_send=fours, y_recv=fours, z_send=fours, z_recv=fours, q_send=fours, q_recv=fours,
        kv_sem=eights, kl_sem=eights,
        w_send=sem((len(plans) + 1, ndim)), w_recv=sem((len(plans) + 1, ndim)), s2_send=sem((2,)), s2_recv=sem((2,)),
        xs=strip, gbuf=strip, spill=mem((2, LEAD, features), f32), small=mem((32, 128), f32),
        small_bufs=mem((2, ndim, 32, 128), f32), total=mem((features, features), f32),
    )
    scratch["late"] = [mem((2,) * ndim + own)] * 3
    scratch["bufs"] = [stream_scratch(len(kept), order, *block) for (kept, order), block in zip(plans, blocks)]
    return call(functools.partial(back_kernel, shards, axes, plans), 6, ins, outs, scratch)


def label_features(line, unlike):
    rows = [(line != k if unlike else line == k).astype(jnp.float32) for k in range(8)]
    return slim(jnp.concatenate(rows + [jnp.zeros((120, line.shape[1]), jnp.float32)], axis=0).T)


class Line:
    def __init__(self, place, src, dst, send_sem, recv_sem):
        self.place, self.src, self.dst, self.send_sem, self.recv_sem = place, src, dst, send_sem, recv_sem

    def copy(self, step, slot):
        group = self.place.group
        return remote(
            self.src.at[(group + step) % GROUPS], self.dst.at[slot], self.send_sem.at[step], self.recv_sem.at[step],
            self.place.other_group(step),
        )

    def keep(self):
        group = self.place.group
        return pltpu.make_async_copy(self.src.at[group], self.dst.at[group], self.send_sem.at[0])

    def start(self, steps=(1, 3, 2)):
        for step in steps:
            self.copy(step, self.place.group).start()

    def wait(self, step):
        self.copy(step, (self.place.group - step + GROUPS) % GROUPS).wait()

    def wait_all(self):
        for step in (1, 3, 2):
            self.wait(step)
        self.keep().wait()

    def gone(self, step):
        self.copy(step, self.place.group).wait_send()

    def come_all(self):
        for step in (1, 3, 2):
            self.copy(step, (self.place.group - step + GROUPS) % GROUPS).wait_recv()
        self.keep().wait()


def near_slot(place, chunk, t):
    first = (chunk * place.rest_size + place.rest) * TQ
    return jnp.clip(t - (first // TK - 1 + place.rest % 2) + 1, 0, 3)


class RowForward:
    def __init__(self, place, r):
        self.place, self.r, self.heads = place, r, r.lse.shape[1]
        self.table = BiasTable(r.table, place, self.heads)

    def clear(self):
        self.r.acc[...] = jnp.zeros_like(self.r.acc)
        self.r.mx[...] = jnp.full_like(self.r.mx, FIRST_MAX)

    def queries(self, chunk):
        r = self.r
        for h, tile in enumerate(spread_lanes(r.q_all[chunk], False)):
            r.qp[chunk, h] = jnp.concatenate([tile, r.ql[chunk]], axis=1)

    def tile(self, t):
        r = self.r
        rows = pl.ds(pl.multiple_of(t * TK, TK), TK)
        keys = lambda h: r.kv_all[rows, h * 128 : h * 128 + 128]
        for h in range(self.heads):
            r.vt[h, 0:64] = keys(h).T[64:128]
            r.vt[h, 64:80] = jnp.ones((16, TK), jnp.bfloat16)

        def scores(i, h):
            return mxu(jnp.concatenate([keys(h), r.kl[rows, :]], axis=1), r.qp[i, h], NT)

        def finish(i, h, s, b):
            m_old = r.mx[i, h]
            m_new = jnp.maximum(m_old, jnp.max(s, axis=0, keepdims=True) + b)
            p = jnp.exp(s - (m_new - b)).astype(jnp.bfloat16)
            r.mx[i, h] = m_new
            r.acc[i, h] = r.acc[i, h] * jnp.exp(m_old - m_new) + mxu(r.vt[h], p)

        def part(i, _):
            slot = near_slot(self.place, i, t)
            away = jnp.logical_or(slot == 0, slot == 3)

            @pl.when(away)
            def _():
                found = [scores(i, h) for h in range(self.heads)]
                for h in range(self.heads):
                    finish(i, h, found[h], jnp.where(slot == 0, self.table[h, 15], self.table[h, 31]))

            @pl.when(jnp.logical_not(away))
            def _():
                for h in range(self.heads):
                    finish(i, h, scores(i, h) + r.near[h, slot - 1].astype(jnp.float32), 0.0)

            return 0

        def pair(p, _):
            slots = [near_slot(self.place, 2 * p + k, t) for k in range(2)]
            far = [jnp.logical_or(slot == 0, slot == 3) for slot in slots]
            both = jnp.logical_and(far[0], far[1])

            @pl.when(both)
            def _():
                items = [(2 * p + k, h, jnp.where(slots[k] == 0, self.table[h, 15], self.table[h, 31])) for h in range(self.heads) for k in range(2)]
                found = [scores(i, h) for i, h, _ in items]
                for (i, h, b), s in zip(items, found):
                    finish(i, h, s, b)

            @pl.when(jnp.logical_not(both))
            def _():
                lax.fori_loop(2 * p, 2 * p + 2, part, 0)

            return 0

        lax.fori_loop(0, GROUPS // 2, pair, 0)

    def end(self):
        r = self.r

        def one(i, _):
            parts = []
            for h in range(self.heads):
                total = r.acc[i, h, 64:65, :]
                parts.append((r.acc[i, h, 0:64, :] / total).T)
                r.lse[i, h] = r.mx[i, h] + jnp.log(total)
            joined = join_heads(parts)
            r.o[i] = joined.astype(jnp.bfloat16)
            r.keep[i] = joined
            return 0

        lax.fori_loop(0, GROUPS, one, 0)


def label_taps(place, own, left, right):
    at_left, at_right = place.blk == 0, place.blk == place.shards - 1
    even, odd = jnp.concatenate([own[0:1], own[1:2]], axis=1), jnp.concatenate([own[2:3], own[3:4]], axis=1)
    none = jnp.full((1, 1), -1, jnp.int32)
    before = [jnp.where(at_left, none, left[row : row + 1, 127:128]) for row in (1, 3)]
    after = [jnp.where(at_right, none, right[row : row + 1, 0:1]) for row in (0, 2)]
    join = lambda *parts: jnp.concatenate(parts, axis=1)
    return [
        join(none, before[1], odd[:, :-2]), join(before[0], even[:, :-1]), join(before[1], odd[:, :-1]), even, odd,
        join(even[:, 1:], after[0]), join(odd[:, 1:], after[1]), join(even[:, 2:], after[0], none),
    ]


def front_kernel(shards, scale, r):
    place = Place(shards)
    tokens = r.kv.shape[1]
    y, core = bit(place.rest, 2), place.rest % 2
    core_to, across = place.other_rest(1), place.other_rest(2)
    peers = [(place.dp, (place.blk + step) % shards) for step in range(1, shards)]
    met = hail(peers)
    length = r.x.shape[0]

    def label_copy(step, block):
        return remote(r.label, r.labels_all.at[block], r.lab_send.at[step], r.lab_recv.at[step], peers[step - 1])

    def label_come(step):
        back = (place.blk + shards - step) % shards
        label_copy(step, back).wait_recv()
        return r.labels_all[back]

    r.labels_all[place.blk] = r.label[...]
    await_all(met)
    halo = [
        remote(r.x.at[pl.ds(0, 16)], r.after, r.x_send.at[0], r.x_recv.at[0], peers[shards - 2]),
        remote(r.x.at[pl.ds(length - 16, 16)], r.before, r.x_send.at[1], r.x_recv.at[1], peers[0]),
    ]
    for copy in halo:
        copy.start()
    for step in [1, shards - 1] + list(range(2, shards - 1)):
        label_copy(step, place.blk).start()
    weights = [pltpu.make_async_copy(src, dst, r.w_sem.at[k]) for k, (src, dst) in enumerate(((r.wq_hbm, r.wq), (r.wk_hbm, r.wk), (r.wv_hbm, r.wv)))]
    for copy in weights:
        copy.start()
    work = RowForward(place, r)
    make_bias(work.table, core, r.near, (0,))
    left, right = label_come(1), label_come(shards - 1)
    taps = label_taps(place, r.label[...], left, right)
    for j in range(8):
        r.labels[j : j + 1, :] = taps[j]
    for copy in halo:
        copy.wait()
    load_bytes(r.x, r.before[14:16, :], r.after[0:2, :], r.xs)
    r.hidden[...], n1 = pool_tokens(scale, r.xs, taps, r.vectors[0:1, :], r.vectors[1:2, :], tokens, r.y, r.share)
    r.n1[...] = n1
    for copy in weights:
        copy.wait()
    put_packed(mxu(n1, r.wq[...]).astype(jnp.bfloat16) * jnp.bfloat16(0.125), r.q)
    queries = Line(place, r.q, r.q_all, r.q_send, r.q_recv)
    queries.keep().start()
    queries.start()
    put_pairs(mxu(n1, r.wk[...]).astype(jnp.bfloat16), mxu(n1, r.wv[...]).astype(jnp.bfloat16), r.kv)

    def held(dz, off, core_off):
        rest = flipped(place.rest, 2) if off else place.rest
        rest = flipped(rest, 1) if core_off else rest
        start = pl.multiple_of(place.chunk((place.group + dz) % GROUPS, rest) * tokens, tokens)
        return r.kv_all.at[pl.ds(start, tokens)]

    def sem_of(dz, off, core_off):
        return r.kv_recv.at[(core_off * 2 + off) * GROUPS + dz]

    waits = []

    def send(src, dz, off, came, target):
        copy = remote(src, held(dz, off, 0), r.kv_send.at[len(waits)], sem_of(*came), target)
        copy.start()
        waits.append(copy)

    def arrived(dz, off, core_off=0):
        here = held(dz, off, core_off)
        remote(here, here, r.kv_send.at[0], sem_of(dz, off, core_off), core_to).wait_recv()

    def pass_on(dz, off):
        mine = dz == 0 and off == 0
        if not mine:
            arrived(dz, off)
        src = r.kv.at[place.group] if mine else held(dz, off, 0)
        if not off:
            send(src, dz, off, (dz, 1, 0), across)
        send(src, dz, off, (dz, off, 1), core_to)

    def along(step):
        copy = remote(r.kv.at[(place.group + step) % GROUPS], held(0, 0, 0), r.z_send.at[step], sem_of((GROUPS - step) % GROUPS, 0, 0), place.other_group(step))
        copy.start()
        return copy

    def line_of(block):
        return jnp.concatenate([block[0:1], block[1:2]], axis=1)

    def tile(dz, off):
        group = (place.group + dz) % GROUPS
        for c in range(2):
            number = place.chunk(group, (1 - y if off else y) * 2 + c)
            rows = pl.ds(pl.multiple_of(number * tokens, tokens), tokens)
            r.kl[rows, :] = label_features(line_of(r.labels_all[number]), True)
        arrived(dz, off, 1)
        work.tile(group * 2 + (1 - y if off else y))

    own = pltpu.make_async_copy(r.kv.at[place.group], held(0, 0, 0), r.own_sem)
    own.start()
    pass_on(0, 0)
    make_bias(work.table, core, r.near, (1,))
    work.clear()
    for step in range(2, shards - 1):
        label_copy(step, (place.blk + shards - step) % shards).wait_recv()
    for z in range(GROUPS):
        r.ql[z] = label_features(line_of(r.labels_all[place.chunk(z, place.rest)]), False) * jnp.bfloat16(NEG)
    pass_on(0, 1)
    for step in (1, 3, 2):
        queries.gone(step)
    first = [along(1), along(3)]
    queries.come_all()
    for z in range(GROUPS):
        work.queries(z)
    own.wait()
    tile(0, 0)
    tile(0, 1)
    for copy in first:
        copy.wait_send()
    last = along(2)
    pass_on(1, 0)
    pass_on(3, 0)
    tile(1, 0)
    pass_on(1, 1)
    pass_on(3, 1)
    tile(3, 0)
    tile(1, 1)
    pass_on(2, 0)
    tile(3, 1)
    pass_on(2, 1)
    tile(2, 0)
    tile(2, 1)
    last.wait_send()
    work.end()
    for copy in waits:
        copy.wait_send()
    for step in range(1, shards):
        label_copy(step, place.blk).wait_send()


def front(shards, scale, table, x, label, vectors, wq, wk, wv):
    length, features = x.shape
    tokens, heads = length // 2, features // 64 // GROUPS
    width = heads * 128
    sem, f32, low = pltpu.SemaphoreType.DMA, jnp.float32, jnp.bfloat16
    mem = lambda shape, dtype=low: pltpu.VMEM(shape, dtype)
    packed = (GROUPS, tokens * 3 // 2, 128)
    ins = dict(
        table=Held(table, pltpu.SMEM), x=x, label=label, vectors=vectors,
        wq_hbm=Held(wq, pl.ANY), wk_hbm=Held(wk, pl.ANY), wv_hbm=Held(wv, pl.ANY),
    )
    outs = dict(
        q_all=(packed, low), kv_all=((shards * tokens, width), low), kl=((shards * tokens, 128), low), ql=((GROUPS, tokens, 128), low),
        near=((heads, 2, TK, TQ), low), o=(packed, low), keep=(packed, f32), lse=((GROUPS, heads, 1, TQ), f32),
        hidden=((tokens, features), f32), n1=((tokens, features), low), y=((8, tokens), f32), share=((1, 128), f32),
        labels=((8, tokens), jnp.int32), before=((16, features), low), after=((16, features), low),
    )
    scratch = dict(
        q=mem(packed), kv=mem((GROUPS, tokens, width)), xs=mem((features // 128, length + 2 * LEAD, 128), f32),
        wq=mem(wq.shape), wk=mem(wk.shape), wv=mem(wv.shape), labels_all=mem((shards,) + label.shape, label.dtype),
        qp=mem((GROUPS, heads, TQ, 256)), acc=mem((GROUPS, heads, 80, TQ), f32), mx=mem((GROUPS, heads, 1, TQ), f32), vt=mem((heads, 80, TK)),
        q_send=sem((4,)), q_recv=sem((4,)), kv_send=sem((12,)), z_send=sem((GROUPS,)), kv_recv=sem((16,)), own_sem=sem,
        lab_send=sem((shards,)), lab_recv=sem((shards,)), x_send=sem((2,)), x_recv=sem((2,)), w_sem=sem((3,)),
    )
    return call(functools.partial(front_kernel, shards, scale), 7, ins, outs, scratch)


def middle_kernel(shards, r):
    place = Place(shards)
    met = hail([place.other_group(step) for step in (1, 2, 3)] + [place.other_rest(1)])
    pairs = ((r.wo_hbm, r.wo), (r.wg_hbm, r.wg), (r.wu_hbm, r.wu), (r.wd_hbm, r.wd))
    fetches = [pltpu.make_async_copy(src, dst, r.w_sem.at[k]) for k, (src, dst) in enumerate(pairs)]
    for copy in fetches:
        copy.start()
    await_all(met)
    home = Line(place, r.o, r.o_home, r.o_send, r.o_recv)
    home.keep().start()
    home.start()
    for copy in fetches:
        copy.wait()
    home.wait_all()
    feed_kernel(r.o_home, r.hidden, r.ct, r.vectors.at[pl.ds(2, 1)], r.wo, r.wg, r.wu, r.wd, r.block_out, r.dres, r.da, r.dgain,
                r.n2, r.att, r.act, r.dg, r.du, r.db, r.acc, r.dn2)
    away = Line(place, r.da, r.do, r.q_send, r.q_recv)
    away.keep().start()
    away.start()
    feed_weights(place, r.n2, r.att, r.act, r.dg, r.du, r.ct, r.db, r.sums,
                 r.core_send, r.core_recv, r.gate, r.up, r.down, r.out, r.wide_out, r.slim_out, r.wide_in, r.slim_in)
    away.wait_all()


def middle(shards, o_packed, hidden, ct, vectors, wo, wg, wu, wd):
    tokens, width = hidden.shape
    ff = wg.shape[1]
    per, per_ff = width // 32, ff // 32
    sem, low, f32 = pltpu.SemaphoreType.DMA, jnp.bfloat16, jnp.float32
    half = o_packed.shape[1:]
    wide_cols = ff + width // 2
    first = (wide_cols // 256 + 1) * 128
    ins = dict(o=o_packed, hidden=hidden, ct=ct, vectors=vectors, wo_hbm=Held(wo, pl.ANY), wg_hbm=Held(wg, pl.ANY), wu_hbm=Held(wu, pl.ANY), wd_hbm=Held(wd, pl.ANY))
    outs = dict(
        block_out=((tokens, width), low), dres=((tokens, width), f32), dgain=((1, width), f32), do=((GROUPS,) + half, low),
        sums=[((16, 2 * per, first), low), ((16, 2 * per, wide_cols - first), low), ((16, per_ff, width), low)],
    )
    mem = lambda shape, dtype=low: pltpu.VMEM(shape, dtype)
    scratch = dict(
        o_home=mem((GROUPS,) + half), da=mem((GROUPS,) + half),
        n2=mem((tokens, width)), att=mem((tokens, width)), db=mem((tokens, width)),
        act=mem((tokens, ff)), dg=mem((tokens, ff)), du=mem((tokens, ff)),
        acc=mem((tokens, width), f32), dn2=mem((tokens, width), f32),
        wo=mem(wo.shape), wg=mem(wg.shape), wu=mem(wu.shape), wd=mem(wd.shape),
        gate=mem((width, ff), f32), up=mem((width, ff), f32), down=mem((ff, width), f32), out=mem((width, width), f32),
        wide_out=mem((16, 2 * per, wide_cols)), slim_out=mem((16, per_ff, width)),
        wide_in=mem((16, 2 * per, wide_cols)), slim_in=mem((16, per_ff, width)),
        w_sem=sem((4,)), o_send=sem((4,)), o_recv=sem((4,)), q_send=sem((4,)), q_recv=sem((4,)),
        core_send=sem((2,)), core_recv=sem((2,)),
    )
    return call(functools.partial(middle_kernel, shards), 8, ins, outs, scratch)


def neighbours(rows):
    peers = lax.axis_size("blk")
    up = [(i, i + 1) for i in range(peers - 1)]
    last, leading = rows
    return lax.ppermute(last, "blk", up), lax.ppermute(leading, "blk", [(j, i) for i, j in up])


def body(
    byte_embeds,
    segments,
    score_weight,
    norm_gain1,
    w_query,
    w_key,
    w_value,
    w_out,
    rel_bias,
    norm_gain2,
    w_gate,
    w_up,
    w_down,
    cotangent,
):
    row_count, length, width = byte_embeds.shape
    tokens = length // 2
    shards = lax.axis_size("blk")
    shape = {"dp": lax.axis_size("dp"), "blk": shards}
    devices = shards * shape["dp"]
    heads = rel_bias.shape[1] // GROUPS
    position = lax.axis_index("blk")
    rest_size = shards // GROUPS
    group, rest = position // rest_size, position % rest_size
    row = lax.axis_index("dp") % 2
    x, ids_here = byte_embeds[0], segments[0]

    ct = cotangent[0]
    scale = 1.0 / (row_count * length * devices)
    if devices == 32:
        label_block = jnp.pad(ids_here.reshape(tokens, 2).T.reshape(4, 128), ((0, 4), (0, 0)))
        vectors = jnp.stack([score_weight, norm_gain1, norm_gain2])
        table = rel_bias.astype(jnp.float32)
        got = front(shards, scale, table, x, label_block, vectors, w_query, w_key, w_value)
        mid = middle(shards, got.o, got.hidden, ct, vectors, w_out, w_gate, w_up, w_down)
        block_out, d_res, d_gain2 = mid.block_out, mid.dres, mid.dgain
        last = back_and_last(
            shape,
            mid.sums,
            dict(
                table=Held(table, pltpu.SMEM), q=got.q_all, do=mid.do, keep=got.keep, kv_hbm=Held(got.kv_all, pl.ANY),
                kl_hbm=Held(got.kl, pl.ANY), ql=got.ql, bias=got.near, lse=got.lse,
                hidden=got.hidden, dres=d_res, n1=got.n1, x=x, before=got.before, after=got.after,
                labels=got.labels, y=got.y, vectors=vectors, wq=w_query, wk=w_key, wv=w_value, dgain2=d_gain2, share=got.share,
            ),
        )
        grad_bytes, edge, spill, small, sums = last.gb, last.edge, last.spill_out, last.small_out, last.sums
    else:
        marks = (ids_here + 1).astype(jnp.bfloat16)
        with_marks = lambda part, two: jnp.concatenate([part, jnp.pad(two, (0, width - 2))[None]], axis=0)
        before, after = neighbours((with_marks(x[-2:], marks[-2:]), with_marks(x[:2], marks[:2])))
        line = jnp.concatenate([before[2, :2], marks, after[2, :2]])
        line = jnp.pad(line, (1, 1)).astype(jnp.int32).reshape(tokens + 3, 2).T
        labels = jnp.stack([line[j % 2, j // 2 : j // 2 + tokens] for j in range(8)])

        score_row, gain1, gain2 = score_weight[None], norm_gain1[None], norm_gain2[None]
        hidden, n1, y, share, q_packed, kv_parts = pool_and_project(
            shards, scale, x, before, after, labels, score_row, gain1, w_query, w_key, w_value
        )

        label_block = jnp.pad(ids_here[0::2].reshape(tokens // 128, 128), ((0, 8 - tokens // 128), (0, 0)), constant_values=-1)
        table = lax.dynamic_slice_in_dim(rel_bias.astype(jnp.float32).T, group * heads, heads, 0)
        q_all, kv_all, labels_all = gather_all(shards, q_packed, kv_parts, label_block)
        labels_all = labels_all.reshape(2, shards, 8, 128)[:, :, : tokens // 128].reshape(2, shards * tokens)
        ids = jnp.arange(8, dtype=jnp.int32)
        counts = jnp.sum((labels_all[:, None, :] == ids[None, :, None]).astype(jnp.int32), axis=2)
        ends = jnp.sum(jnp.where(ids[None, :] <= ids[:, None], counts[:, None, :], 0), axis=2)
        begins = ends - counts
        query_labels = jnp.stack(
            [lax.dynamic_slice_in_dim(labels_all, ((2 * row + i) * rest_size + rest) * tokens, tokens, 1) for i in range(2)],
            axis=1,
        )
        chosen = query_labels[:, :, None, :] == ids[None, None, :, None]
        span = jnp.stack(
            [jnp.sum(jnp.where(chosen, edge[:, None, :, None], 0), axis=2) for edge in (begins, ends)], axis=2
        )
        parity = rest % 2
        firsts = jnp.stack([((2 * row + i) * rest_size + rest) * tokens for i in range(2)])
        near = jnp.broadcast_to((firsts // TK - 1 + parity)[None], (2, 2))
        bounds = jnp.stack(
            [
                jnp.min(span[:, :, 0], axis=-1) // TK,
                -(-jnp.max(span[:, :, 1], axis=-1) // TK),
                near,
                -(-jnp.max(span[:, :, 0], axis=-1) // TK),
                jnp.min(span[:, :, 1], axis=-1) // TK,
                jnp.broadcast_to(parity, (2, 2)),
                jnp.broadcast_to((labels_all[0, -1] > 0).astype(jnp.int32), (2, 2)),
            ],
            axis=-1,
        ).astype(jnp.int32)
        o_packed, o_kept, log_total, near_bias = attention(bounds, table, q_all, kv_all, span)
        o_home = move_heads(return_kernel, (GROUPS,), shards, 4, o_packed)
        block_out, d_res, da_packed, d_gain2, n2, att, act, d_gate, d_up, d_branch = feed_forward(
            o_home, hidden, ct, gain2, w_out, w_gate, w_up, w_down
        )
        do_all = move_heads(spread_kernel, (2, 2), shards, 5, da_packed)
        dq_packed, dkv_all, _, _, _, d_table_lanes = attention_back(
            False, bounds, table, q_all, do_all, o_kept, kv_all, near_bias, span, log_total
        )
        dq_home, dkv_home = reduce_all(shape, dq_packed, dkv_all, [], [])
        grad_bytes, edge, spill, small, last_parts = last_part(
            shape, dq_home, dkv_home, hidden, d_res, x, before, after, labels, y,
            score_row, gain1, w_query, w_key, w_value, d_gain2, share, d_table_lanes,
        )
        sums = []
    per = width // devices
    block_out, grad_bytes, g_score, g_gain1, g_gain2, g_bias, shares, *grads = finish(
        shards, rel_bias.shape[1], per, w_gate.shape[1], block_out, grad_bytes, edge, spill, small, sums
    )
    if devices != 32:
        product = lambda left, right: jnp.einsum("td,te->de", left, right, preferred_element_type=jnp.float32)
        grads = [product(n1, last_parts[j]) for j in range(3)]
        grads += [product(att, d_branch), product(n2, d_gate), product(n2, d_up), product(act, ct)]
        grads = [lax.psum_scatter(grad, ("dp", "blk"), scatter_dimension=0, tiled=True) for grad in grads]
    return (
        block_out[None],
        grad_bytes[None],
        g_score,
        g_gain1,
        *grads[:4],
        g_bias,
        g_gain2,
        *grads[4:],
        shares,
    )


def solution(mesh):
    placed = (
        P("dp", "blk", None),
        P("dp", "blk"),
        P(),
        P(),
        P(),
        P(),
        P(),
        P(),
        P(),
        P(),
        P(),
        P(),
        P(),
        P("dp", "blk", None),
    )
    return jax.shard_map(
        body,
        mesh=mesh,
        in_specs=placed,
        out_specs=(
            P("dp", "blk", None),
            P("dp", "blk", None),
            P(),
            P(),
            P(("dp", "blk"), None),
            P(("dp", "blk"), None),
            P(("dp", "blk"), None),
            P(("dp", "blk"), None),
            P(),
            P(),
            P(("dp", "blk"), None),
            P(("dp", "blk"), None),
            P(("dp", "blk"), None),
            P(),
        ),
        check_vma=False,
    )
```

```python
import functools
import math

import jax
import jax.numpy as jnp
from jax import lax
from jax.experimental import pallas as pl
from jax.experimental.pallas import tpu as pltpu
from jax.sharding import PartitionSpec as P

BUCKETS = 32
MAX_BLOCK = 4
VMEM_BYTES = 61 * 2**20


def buckets_of(relative):
    distance = jnp.abs(relative)
    beyond = jnp.zeros_like(distance)
    for border in (12, 16, 23, 32, 46, 64, 91):
        beyond = beyond + (distance >= border).astype(jnp.int32)
    nearer = jnp.where(distance < 8, distance, 8 + beyond)
    return nearer + BUCKETS // 2 * (relative > 0).astype(jnp.int32)


MESH_ID = pl.DeviceIdType.MESH
GROUPS = 4


def bits_of(size):
    return [1 << p for p in reversed(range(size.bit_length() - 1))]


def bit(value, mask):
    return (value // mask) % 2


def flipped(value, mask):
    return value + mask * (1 - 2 * bit(value, mask))


class Place:
    def __init__(self, shards):
        self.shards = shards
        self.rest_size = shards // GROUPS
        self.dp = lax.axis_index("dp")
        self.blk = lax.axis_index("blk")
        self.row = self.dp % 2
        self.group = self.blk // self.rest_size
        self.rest = self.blk % self.rest_size

    def at(self, row, group, rest):
        return (self.dp - self.row + row, group * self.rest_size + rest)

    def chunk(self, group, rest):
        return group * self.rest_size + rest

    def other_row(self):
        return self.at(1 - self.row, self.group, self.rest)

    def other_rest(self, mask):
        return self.at(self.row, self.group, flipped(self.rest, mask))

    def other_group(self, step):
        return self.at(self.row, (self.group + step) % GROUPS, self.rest)


def hail(targets):
    barrier = pltpu.get_barrier_semaphore()
    for target in targets:
        pl.semaphore_signal(barrier, inc=1, device_id=target, device_id_type=MESH_ID)
    return len(targets)


def await_all(count):
    pl.semaphore_wait(pltpu.get_barrier_semaphore(), count)


def greet(targets):
    await_all(hail(targets))


def remote(src, dst, send_sem, recv_sem, target):
    return pltpu.make_async_remote_copy(
        src_ref=src,
        dst_ref=dst,
        send_sem=send_sem,
        recv_sem=recv_sem,
        device_id=target,
        device_id_type=MESH_ID,
    )


def line_and_row(place):
    found = []
    for step in range(GROUPS):
        for flip in range(2):
            if step or flip:
                row = 1 - place.row if flip else place.row
                found.append(place.at(row, (place.group + step) % GROUPS, place.rest))
    return found


def spread_heads(place, q_ref, out_ref, send_sem, recv_sem):
    row_to = place.group // 2
    slot = place.group % 2
    dst = out_ref.at[place.row, slot]
    mine = recv_sem.at[place.row * 2 + slot]
    at_home = row_to == place.row
    for step in range(GROUPS):
        group = (place.group + step) % GROUPS
        src = q_ref.at[group]
        copy = remote(src, dst, send_sem.at[step], mine, place.at(row_to, group, place.rest))
        if step:
            copy.start()
        else:
            pl.when(jnp.logical_not(at_home))(copy.start)
            pl.when(at_home)(pltpu.make_async_copy(src, dst, mine).start)


def spread_heads_come(q_ref, out_ref, recv_sem):
    for row in range(2):
        for slot in range(2):
            pltpu.make_async_copy(q_ref.at[0], out_ref.at[row, slot], recv_sem.at[row * 2 + slot]).wait()


def spread_heads_gone(place, q_ref, out_ref, send_sem, recv_sem):
    at_home = place.group // 2 == place.row
    for step in range(GROUPS):
        copy = remote(q_ref.at[0], out_ref.at[0, 0], send_sem.at[step], recv_sem.at[0], place.other_row())
        if step:
            copy.wait_send()
        else:
            pl.when(jnp.logical_not(at_home))(copy.wait_send)


def spread_heads_wait(place, q_ref, out_ref, send_sem, recv_sem):
    spread_heads_come(q_ref, out_ref, recv_sem)
    spread_heads_gone(place, q_ref, out_ref, send_sem, recv_sem)


def return_heads(place, o_ref, out_ref, send_sem, recv_sem):
    for row in range(2):
        for slot in range(2):
            group = place.row * 2 + slot
            src = o_ref.at[row, slot]
            dst = out_ref.at[place.group]
            mine = recv_sem.at[place.group]
            at_home = jnp.logical_and(place.row == row, place.group == group)
            copy = remote(src, dst, send_sem.at[row * 2 + slot], mine, place.at(row, group, place.rest))
            pl.when(jnp.logical_not(at_home))(copy.start)
            pl.when(at_home)(pltpu.make_async_copy(src, dst, mine).start)


def return_heads_wait(place, o_ref, out_ref, send_sem, recv_sem):
    for group in range(GROUPS):
        pltpu.make_async_copy(o_ref.at[0, 0], out_ref.at[group], recv_sem.at[group]).wait()
    for row in range(2):
        for slot in range(2):
            group = place.row * 2 + slot
            at_home = jnp.logical_and(place.row == row, place.group == group)
            copy = remote(o_ref.at[0, 0], out_ref.at[0], send_sem.at[row * 2 + slot], recv_sem.at[0], place.other_row())
            pl.when(jnp.logical_not(at_home))(copy.wait_send)


def spread_kernel(shards, q_ref, out_ref, send_sem, recv_sem):
    place = Place(shards)
    greet(line_and_row(place))
    spread_heads(place, q_ref, out_ref, send_sem, recv_sem)
    spread_heads_wait(place, q_ref, out_ref, send_sem, recv_sem)


def return_kernel(shards, o_ref, out_ref, send_sem, recv_sem):
    place = Place(shards)
    greet(line_and_row(place))
    return_heads(place, o_ref, out_ref, send_sem, recv_sem)
    return_heads_wait(place, o_ref, out_ref, send_sem, recv_sem)


SMEM_SPEC = pl.BlockSpec(memory_space=pltpu.SMEM)
VMEM_SPEC = pl.BlockSpec(memory_space=pltpu.VMEM)
ANY_SPEC = pl.BlockSpec(memory_space=pl.ANY)


def move_heads(kernel, lead, shards, ident, packed):
    rows, lanes = packed.shape[-2:]
    return pl.pallas_call(
        functools.partial(kernel, shards),
        out_shape=jax.ShapeDtypeStruct(lead + (rows, lanes), packed.dtype),
        in_specs=[pl.BlockSpec(memory_space=pltpu.VMEM)],
        out_specs=pl.BlockSpec(memory_space=pltpu.VMEM),
        scratch_shapes=[pltpu.SemaphoreType.DMA((4,)), pltpu.SemaphoreType.DMA((4,))],
        compiler_params=pltpu.CompilerParams(collective_id=ident, has_side_effects=True, vmem_limit_bytes=VMEM_BYTES),
        name="move_heads_%d" % ident,
    )(packed)


def gather_kernel(shards, q_ref, kv_ref, label_ref, qo_ref, kvo_ref, labo_ref, q_send, q_recv, z_send, far_send, core_send, kv_recv, own_sem, lab_send, lab_recv):
    place = Place(shards)
    tokens = kv_ref.shape[1]
    rest_bits = bits_of(place.rest_size)
    core, far = rest_bits[-1], ["row"] + rest_bits[:-1]
    greet(line_and_row(place) + [place.other_rest(mask) for mask in rest_bits])

    dims = [("row", 1)] + [("blk", m) for m in bits_of(shards)]
    lab_index = [place.row] + [bit(place.blk, m) for _, m in dims[1:]]
    lab_order = list(range(len(dims)))

    def lab_copy(stage):
        index = tuple(slice(None) if p in lab_order[:stage] else lab_index[p] for p in range(len(dims)))
        axis, mask = dims[lab_order[stage]]
        target = place.other_row() if axis == "row" else (place.dp, flipped(place.blk, mask))
        there = labo_ref.at[index]
        return remote(there, there, lab_send.at[stage], lab_recv.at[stage], target)

    labo_ref[tuple(lab_index)] = label_ref[...]
    lab_copy(0).start()
    lab_stage = 0

    def slot(row, group, rest):
        start = pl.multiple_of(place.chunk(group, rest) * tokens, tokens)
        return kvo_ref.at[row, pl.ds(start, tokens)]

    def held(dz, offset, core_off):
        row = 1 - place.row if offset & 1 else place.row
        rest = place.rest
        for p, mask in enumerate(far[1:]):
            if offset >> (p + 1) & 1:
                rest = flipped(rest, mask)
        if core_off:
            rest = flipped(rest, core)
        return slot(row, (place.group + dz) % GROUPS, rest)

    count = 1 << len(far)

    def sem_of(dz, offset, core_off):
        return kv_recv.at[(core_off * count + offset) * GROUPS + dz]

    own = pltpu.make_async_copy(kv_ref.at[place.group], held(0, 0, 0), own_sem)
    own.start()
    waits = []
    for step in (1, 3, 2):
        copy = remote(kv_ref.at[(place.group + step) % GROUPS], held(0, 0, 0), z_send.at[step], sem_of((GROUPS - step) % GROUPS, 0, 0), place.other_group(step))
        copy.start()
        waits.append(copy)

    used = 0
    events = sorted(((dz, off) for dz in range(GROUPS) for off in range(count)), key=lambda e: (bin(e[1]).count("1"), (0, 1, 3, 2).index(e[0])))
    core_target = place.other_rest(core)
    for step, (dz, off) in enumerate(events):
        if step == GROUPS:
            spread_heads(place, q_ref, qo_ref, q_send, q_recv)
        here = held(dz, off, 0)
        if dz == 0 and off == 0:
            src = kv_ref.at[place.group]
        else:
            remote(here, here, z_send.at[0], sem_of(dz, off, 0), core_target).wait_recv()
            src = here
        order = [(p + dz) % len(far) for p in range(len(far))]
        last = max([order.index(p) for p in range(len(far)) if off >> p & 1], default=-1)
        for p in order[last + 1 :]:
            target = place.other_row() if p == 0 else place.other_rest(far[p])
            copy = remote(src, here, far_send.at[used], sem_of(dz, off | 1 << p, 0), target)
            copy.start()
            waits.append(copy)
            used += 1
        copy = remote(src, here, core_send.at[off * GROUPS + dz], sem_of(dz, off, 1), core_target)
        copy.start()
        waits.append(copy)
        if lab_stage < len(dims):
            lab_copy(lab_stage).wait()
            lab_stage += 1
            if lab_stage < len(dims):
                lab_copy(lab_stage).start()
    for dz, off in events:
        here = held(dz, off, 1)
        remote(here, here, z_send.at[0], sem_of(dz, off, 1), core_target).wait_recv()
    own.wait()
    for copy in waits:
        copy.wait_send()
    spread_heads_wait(place, q_ref, qo_ref, q_send, q_recv)


def gather_all(shards, q_packed, kv_parts, labels):
    tokens, width = kv_parts.shape[1:]
    far = 1 + len(bits_of(shards // GROUPS)) - 1
    count = 1 << far
    nbits = 1 + len(bits_of(shards))
    sem = pltpu.SemaphoreType.DMA
    return pl.pallas_call(
        functools.partial(gather_kernel, shards),
        out_shape=(
            jax.ShapeDtypeStruct((2, 2) + q_packed.shape[1:], q_packed.dtype),
            jax.ShapeDtypeStruct((2, shards * tokens, width), kv_parts.dtype),
            jax.ShapeDtypeStruct((2,) * nbits + labels.shape, labels.dtype),
        ),
        in_specs=[pl.BlockSpec(memory_space=pltpu.VMEM)] * 3,
        out_specs=(pl.BlockSpec(memory_space=pltpu.VMEM),) * 3,
        scratch_shapes=[
            sem((4,)), sem((4,)), sem((GROUPS,)), sem((GROUPS * (count - 1),)), sem((GROUPS * count,)), sem((GROUPS * count * 2,)),
            sem, sem((nbits,)), sem((nbits,)),
        ],
        compiler_params=pltpu.CompilerParams(collective_id=1, has_side_effects=True, vmem_limit_bytes=VMEM_BYTES),
        name="gather_keys",
    )(q_packed, kv_parts, labels)


def add_blocks(dst_ref, src_ref, index, shape):
    lead = shape[:-2]
    total = math.prod(lead)

    def one(step, _):
        place, left = [], step
        for size in reversed(lead):
            place.append(left % size)
            left = left // size
        place = tuple(reversed(place))
        full, k = [], 0
        for entry in index:
            if entry is None:
                full.append(place[k])
                k += 1
            else:
                full.append(entry)
        dst_ref[place] = dst_ref[place] + src_ref[tuple(full)]
        return 0

    lax.fori_loop(0, total, one, 0)


class Stream:
    def __init__(self, axes, at, kept, order, src, half, bufs, out, send_sem, recv_sem):
        self.axes, self.at, self.kept, self.order = axes, at, kept, order
        self.half = half
        self.src, self.bufs, self.out = src, bufs, out
        self.send_sem, self.recv_sem = send_sem, recv_sem

    def own(self, p):
        axis, mask = self.axes[p]
        return bit(self.at[axis], mask)

    def target(self, p):
        axis, mask = self.axes[p]
        moved = dict(self.at)
        moved[axis] = flipped(self.at[axis], mask)
        return (moved["dp"], moved["blk"])

    def stage(self, k):
        kept = [p for p in self.kept if p not in self.order[:k]]
        return kept, self.src if k == 0 else self.bufs[k - 1], self.order[k]

    def copy(self, k):
        kept, src, now = self.stage(k)
        index = tuple(1 - self.own(p) if p == now else slice(None) for p in kept)
        return remote(src.at[index], self.bufs[k], self.send_sem.at[k], self.recv_sem.at[k], self.target(now))

    def absorb(self, k):
        kept, src, now = self.stage(k)
        buf = self.bufs[k]
        if k == len(self.order) - 1 and self.out is not None:
            mine = src[self.own(now)].astype(jnp.float32)
            self.out[...] = buf[...].astype(jnp.float32) + mine
        else:
            half = k == 0 and self.half is not None
            index = tuple(self.own(p) if p == now else None for p in kept if p != now or not half)
            add_blocks(buf, self.half if half else src, index, buf.shape)


class Whole:
    def __init__(self, axes, at, order, src, bufs, out, send_sem, recv_sem):
        self.stream = Stream(axes, at, order, order, src, None, bufs, out, send_sem, recv_sem)
        self.order, self.src, self.bufs, self.out = order, src, bufs, out

    def held(self, k):
        return self.src if k == 0 else self.bufs.at[1, k - 1]

    def copy(self, k):
        s = self.stream
        return remote(self.held(k), self.bufs.at[0, k], s.send_sem.at[k], s.recv_sem.at[k], s.target(self.order[k]))

    def absorb(self, k):
        total = self.held(k)[...] + self.bufs[0, k]
        if k == len(self.order) - 1:
            self.out[...] = total
        else:
            self.bufs[1, k] = total


def advance(stream, stage):
    if stage < len(stream.order):
        stream.copy(stage).wait()
        stream.absorb(stage)
        if stage < len(stream.order) - 1:
            stream.copy(stage + 1).start()


def bit_axes(shape):
    return [("dp", m) for m in bits_of(shape["dp"])] + [("blk", m) for m in bits_of(shape["blk"])]


def stream_scratch(lead, order, rows, cols):
    return [pltpu.VMEM((2,) * (lead - 1 - k) + (rows, cols), jnp.bfloat16) for k in range(len(order))]


def feed_weights(place, n2_ref, att_ref, act_ref, dg_ref, du_ref, ct_ref, db_ref, sums,
                 core_send, core_recv, gate, up, down, out, wide_out, slim_out, wide_in, slim_in):
    core_target = place.other_rest(1)
    per = gate.shape[0] // 32
    per_ff = down.shape[0] // 32
    first = sums[0].shape[2]
    half = out.shape[1] // 2
    core = place.rest % 2

    n2_t = n2_ref[...].T
    step = 512
    for j in range(gate.shape[1] // step):
        cols = slice(j * step, j * step + step)
        gate[:, cols] = mxu(n2_t, dg_ref[:, cols])
        up[:, cols] = mxu(n2_t, du_ref[:, cols])
    out[...] = mxu(att_ref[...].T, db_ref[...])

    def wide_rows(block):
        rows = pl.ds(pl.multiple_of(block * per, 8), per)
        last = jnp.concatenate([out[rows, :half], out[rows, half:]], axis=0)
        return jnp.concatenate([jnp.concatenate([gate[rows, :], up[rows, :]], axis=0), last], axis=1)

    def slim_rows(block):
        return down[pl.ds(pl.multiple_of(block * per_ff, 8), per_ff), :]

    def send_wide(m, _):
        wide_out[m] = wide_rows(2 * m + 1 - core).astype(jnp.bfloat16)
        return 0

    lax.fori_loop(0, 16, send_wide, 0)
    wide_copy = remote(wide_out, wide_in, core_send.at[0], core_recv.at[0], core_target)
    wide_copy.start()
    for j in range(down.shape[0] // step):
        rows = slice(j * step, j * step + step)
        down[rows, :] = mxu(act_ref[:, rows].T, ct_ref[...])

    def send_slim(m, _):
        slim_out[m] = slim_rows(2 * m + 1 - core).astype(jnp.bfloat16)
        return 0

    lax.fori_loop(0, 16, send_slim, 0)
    slim_copy = remote(slim_out, slim_in, core_send.at[1], core_recv.at[1], core_target)
    slim_copy.start()

    wide_copy.wait()

    def sum_wide(m, _):
        total = wide_rows(2 * m + core) + wide_in[m].astype(jnp.float32)
        sums[0][m] = total[:, :first].astype(jnp.bfloat16)
        sums[1][m] = total[:, first:].astype(jnp.bfloat16)
        return 0

    lax.fori_loop(0, 16, sum_wide, 0)
    slim_copy.wait()

    def sum_slim(m, _):
        sums[2][m] = (slim_rows(2 * m + core) + slim_in[m].astype(jnp.float32)).astype(jnp.bfloat16)
        return 0

    lax.fori_loop(0, 16, sum_slim, 0)


def reduce_kernel(shards, axes, orders, *refs):
    count = len(orders)
    q_ref, kv_ref = refs[:2]
    pairs = refs[2 : 2 + 2 * count]
    qo_ref, kvo_ref = refs[2 + 2 * count : 4 + 2 * count]
    sums = refs[4 + 2 * count : 4 + 3 * count]
    q_send, q_recv, send_sem, recv_sem, z_send, z_recv, w_send, w_recv = refs[4 + 3 * count : 12 + 3 * count]
    bufs = refs[12 + 3 * count :]
    place = Place(shards)
    rest_bits = bits_of(place.rest_size)
    greet(line_and_row(place) + [place.other_rest(mask) for mask in rest_bits])
    return_heads(place, q_ref, qo_ref, q_send, q_recv)
    ndim = 1 + len(rest_bits)
    at = {"dp": place.dp, "blk": place.blk}
    streams, used = [], ndim
    for s, (kept, order) in enumerate(orders):
        src, more = bufs[used], bufs[used + 1 : used + 1 + len(order)]
        used += 1 + len(order)
        streams.append(Stream(axes, at, kept, order, src, more, sums[s], w_send.at[s], w_recv.at[s]))
    own = [place.row] + [bit(place.rest, m) for m in rest_bits]
    targets = [place.other_row()] + [place.other_rest(m) for m in rest_bits]
    state = {}

    def plan(group_step):
        far = list(range(ndim - 1))
        turn = group_step % len(far)
        return [ndim - 1] + far[turn:] + far[:turn]

    def copy_of(step, stage):
        order = plan(step)
        group = (place.group + step) % GROUPS
        done = order[:stage]
        p_now = order[stage]
        buf = bufs[stage].at[step]
        if stage == 0:
            index = (p_index(group, done, p_now))
            src = kv_ref.at[index]
        else:
            kept = [p for p in range(ndim) if p not in done]
            src = bufs[stage - 1].at[(step,) + tuple(1 - own[p] if p == p_now else slice(None) for p in kept)]
        return remote(src, buf, send_sem.at[stage, step], recv_sem.at[stage, step], targets[p_now])

    def p_index(group, done, p_now):
        index = [slice(None)] * ndim
        index[p_now] = 1 - own[p_now]
        return (index[0], group) + tuple(index[1:])

    def absorb(step, stage):
        order = plan(step)
        done, p_now = order[:stage], order[stage]
        buf = bufs[stage].at[step]
        group = (place.group + step) % GROUPS
        if stage == 0:
            index = [None] * ndim
            index[p_now] = own[p_now]
            add_blocks(buf, kv_ref, (index[0], group) + tuple(index[1:]), buf.shape)
        else:
            kept = [p for p in range(ndim) if p not in done]
            index = tuple(own[p] if p == p_now else None for p in kept)
            add_blocks(buf, bufs[stage - 1].at[step], index, buf.shape)

    steps = (2, 1, 3, 0)
    for step in steps:
        copy_of(step, 0).start()
    for s, stream in enumerate(streams):
        add_two(stream.src, pairs[2 * s], pairs[2 * s + 1])
        stream.copy(0).start()
    for stage in range(ndim):
        for step in steps:
            copy_of(step, stage).wait()
            absorb(step, stage)
            if stage < ndim - 1:
                copy_of(step, stage + 1).start()
            elif step:
                remote(bufs[stage].at[step], kvo_ref.at[place.group], z_send.at[step], z_recv.at[(GROUPS - step) % GROUPS], place.other_group(step)).start()
            else:
                kvo_ref[place.group] = bufs[stage][step]
        for stream in streams:
            if stage < len(stream.order):
                stream.copy(stage).wait()
                stream.absorb(stage)
                if stage < len(stream.order) - 1:
                    stream.copy(stage + 1).start()
    for step in (1, 3, 2):
        there = kvo_ref.at[(place.group + step) % GROUPS]
        remote(bufs[ndim - 1].at[step], there, z_send.at[step], z_recv.at[step], place.other_group(step)).wait()
    return_heads_wait(place, q_ref, qo_ref, q_send, q_recv)


def add_two(dst_ref, one_ref, two_ref):
    lead = dst_ref.shape[:-2]

    def one(step, _):
        place, left = [], step
        for size in reversed(lead):
            place.append(left % size)
            left = left // size
        place = tuple(reversed(place))
        dst_ref[place] = (one_ref[place].astype(jnp.float32) + two_ref[place].astype(jnp.float32)).astype(dst_ref.dtype)
        return 0

    lax.fori_loop(0, math.prod(lead), one, 0)


def reduce_all(shape, q_packed, kv_sums, orders, pairs):
    shards = shape["blk"]
    tokens_all, width = kv_sums.shape[1:]
    tokens = tokens_all // shards
    rest_bits = bits_of(shards // GROUPS)
    ndim = 1 + len(rest_bits)
    sem = pltpu.SemaphoreType.DMA
    scratch = [pltpu.VMEM((GROUPS,) + (2,) * (ndim - 1 - s) + (tokens, width), kv_sums.dtype) for s in range(ndim)]
    flat, sums = [], []
    for (kept, order), pair in zip(orders, pairs):
        rows, cols = pair[0].shape[-2:]
        flat += [part.reshape((2,) * len(kept) + (rows, cols)) for part in pair]
        sums.append(jax.ShapeDtypeStruct((rows, cols), jnp.float32))
        scratch.append(pltpu.VMEM((2,) * len(kept) + (rows, cols), jnp.bfloat16))
        scratch += stream_scratch(len(kept), order, rows, cols)
    stages = max([len(order) for _, order in orders], default=1)
    return pl.pallas_call(
        functools.partial(reduce_kernel, shards, bit_axes(shape), orders),
        out_shape=(
            jax.ShapeDtypeStruct((GROUPS,) + q_packed.shape[2:], q_packed.dtype),
            jax.ShapeDtypeStruct((GROUPS, tokens, width), kv_sums.dtype),
        ) + tuple(sums),
        in_specs=[VMEM_SPEC] * (2 + len(flat)),
        out_specs=(VMEM_SPEC,) * (2 + len(sums)),
        scratch_shapes=[sem((4,)), sem((4,)), sem((ndim, GROUPS)), sem((ndim, GROUPS)), sem((GROUPS,)), sem((GROUPS,)),
                        sem((max(len(orders), 1), stages)), sem((max(len(orders), 1), stages))] + scratch,
        compiler_params=pltpu.CompilerParams(collective_id=2, has_side_effects=True, vmem_limit_bytes=VMEM_BYTES),
        name="reduce_keys",
    )(q_packed, kv_sums.reshape((2, GROUPS) + (2,) * len(rest_bits) + (tokens, width)), *flat)


TQ = 256
TK = 512
NEAR_ROWS = 448
NEG = -1e30
FIRST_MAX = -1e29
NT = (((1,), (1,)), ((), ()))
NN = (((1,), (0,)), ((), ()))
BORDERS = (12, 16, 23, 32, 46, 64, 91)


def mxu(left, right, dims=NN):
    return lax.dot_general(left, right, dims, preferred_element_type=jnp.float32)


def turned(tile):
    return jnp.concatenate([tile[:, 64:], tile[:, :64]], axis=1)


def spread_lanes(packed, high):
    lane = lax.broadcasted_iota(jnp.int32, (1, 128), 1)
    keep = lane >= 64 if high else lane < 64
    zero = jnp.zeros((), packed.dtype)
    pair, last = packed[0:TQ], packed[TQ:]
    pick = lambda tile: jnp.where(keep, tile, zero)
    if high:
        return [pick(turned(pair)), pick(pair), jnp.concatenate([pick(turned(last)), pick(last)], axis=0)]
    return [pick(pair), pick(turned(pair)), jnp.concatenate([pick(last), pick(turned(last))], axis=0)]


def join_heads(parts):
    half = TQ // 2
    top = jnp.concatenate([parts[0], parts[1]], axis=1)
    low = jnp.concatenate([parts[2][:half], parts[2][half:]], axis=1)
    return jnp.concatenate([top, low], axis=0)


def valid_mask(se_ref, r, i, k0):
    kpos = k0 + lax.broadcasted_iota(jnp.int32, (TK, TQ), 0)
    return jnp.logical_and(kpos >= se_ref[r, i, 0:1, :], kpos < se_ref[r, i, 1:2, :])


def near_buckets(first, rows, parity):
    relative = (
        first - TK + TQ * parity
        + lax.broadcasted_iota(jnp.int32, (rows, TQ), 0)
        - lax.broadcasted_iota(jnp.int32, (rows, TQ), 1)
    )
    return buckets_of(relative)


def make_bias(table, parity, near_ref, tiles=(0, 1)):
    heads = near_ref.shape[0]
    for tile in tiles:
        def rows(step, _):
            start = pl.multiple_of(step * 32, 32)
            place = tile * TK + start
            after = place - near_start(parity)
            inside = jnp.logical_and(after >= 0, after < NEAR_ROWS)

            @pl.when(inside)
            def _():
                which = near_buckets(place, 32, parity)
                for h in range(heads):
                    value = jnp.zeros((32, TQ), jnp.float32)
                    for b in range(BUCKETS):
                        value = jnp.where(which == b, table[h, b], value)
                    near_ref[h, tile, pl.ds(start, 32)] = value.astype(jnp.bfloat16)

            @pl.when(jnp.logical_not(inside))
            def _():
                for h in range(heads):
                    value = jnp.where(after < 0, table[h, 15], table[h, 31])
                    near_ref[h, tile, pl.ds(start, 32)] = jnp.full((32, TQ), value, jnp.float32).astype(jnp.bfloat16)

            return 0
        lax.fori_loop(0, TK // 32, rows, 0)


def tile_kind(bounds, r, i, t):
    slot = jnp.clip(t - bounds[r, i, 2] + 1, 0, 3)
    away = jnp.logical_or(slot == 0, slot == 3)
    inside = jnp.logical_and(t >= bounds[r, i, 3], t < bounds[r, i, 4])
    return slot, jnp.logical_and(away, inside)


def fwd_kernel(alone, bounds, table, q_ref, kv_hbm, se_ref, *refs):
    if alone:
        near_ref, o_in, keep_in, lse_in, o_ref, keep_ref, lse_ref, vt, acc, mx, qp, kv_ref, kv_sem = refs
    else:
        o_ref, keep_ref, lse_ref, near_ref, vt, acc, mx, qp, kv_ref, kv_sem = refs
        make_bias(table, bounds[0, 0, 5], near_ref)
    heads = lse_ref.shape[2]
    base = 1 - bounds[0, 0, 6] if alone else 0

    def row_body(at, _):
        r = base + at
        lo_all = jnp.minimum(bounds[r, 0, 0], bounds[r, 1, 0])
        hi_all = jnp.maximum(bounds[r, 0, 1], bounds[r, 1, 1])

        def fetch(t):
            rows = pl.ds(pl.multiple_of(t * TK, TK), TK)
            return pltpu.make_async_copy(kv_hbm.at[r, rows], kv_ref.at[rows], kv_sem.at[t])

        def begin(t, _):
            fetch(t).start()
            return 0

        lax.fori_loop(lo_all, hi_all, begin, 0)
        for i in range(2):
            for h, tile in enumerate(spread_lanes(q_ref[r, i], False)):
                qp[i, h] = tile

        def turn(t, _):
            fetch(t).wait()
            k0 = pl.multiple_of(t * TK, TK)
            for h in range(heads):
                tile = kv_ref[pl.ds(k0, TK), h * 128 : h * 128 + 128]
                vt[h, 0:64, pl.ds(k0, TK)] = tile.T[64:128, :]
                vt[h, 64:80, pl.ds(k0, TK)] = jnp.ones((16, TK), jnp.bfloat16)
            return 0

        lax.fori_loop(lo_all, hi_all, turn, 0)

        def q_body(i, _):
            acc[...] = jnp.zeros_like(acc)
            mx[...] = jnp.full_like(mx, FIRST_MAX)

            def tile_body(t, _):
                k0 = pl.multiple_of(t * TK, TK)
                slot, plain = tile_kind(bounds, r, i, t)
                near = jnp.logical_and(slot > 0, slot < 3)

                def scores(h):
                    return mxu(kv_ref[pl.ds(k0, TK), h * 128 : h * 128 + 128], qp[i, h], NT)

                def finish(h, s, b):
                    m_old = mx[h]
                    m_new = jnp.maximum(m_old, jnp.max(s, axis=0, keepdims=True) + b)
                    p = jnp.exp(s - (m_new - b)).astype(jnp.bfloat16)
                    mx[h] = m_new
                    acc[h] = acc[h] * jnp.exp(m_old - m_new) + mxu(vt[h, :, pl.ds(k0, TK)], p)

                @pl.when(plain)
                def _():
                    found = [scores(h) for h in range(heads)]
                    for h in range(heads):
                        finish(h, found[h], jnp.where(slot == 0, table[h, 15], table[h, 31]))

                @pl.when(near)
                def _():
                    ok = valid_mask(se_ref, r, i, k0)
                    for h in range(heads):
                        s = scores(h) + near_ref[h, slot - 1].astype(jnp.float32)
                        finish(h, jnp.where(ok, s, NEG), 0.0)

                @pl.when(jnp.logical_not(jnp.logical_or(plain, near)))
                def _():
                    ok = valid_mask(se_ref, r, i, k0)
                    for h in range(heads):
                        s = scores(h) + jnp.where(slot == 0, table[h, 15], table[h, 31])
                        finish(h, jnp.where(ok, s, NEG), 0.0)

                return 0

            lax.fori_loop(bounds[r, i, 0], bounds[r, i, 1], tile_body, 0)
            parts = []
            for h in range(heads):
                total = acc[h, 64:65, :]
                parts.append((acc[h, 0:64, :] / total).T)
                lse_ref[r, i, h] = mx[h] + jnp.log(total)
            joined = join_heads(parts)
            o_ref[r, i] = joined.astype(jnp.bfloat16)
            keep_ref[r, i] = joined
            return 0

        lax.fori_loop(0, 2, q_body, 0)
        return 0

    lax.fori_loop(0, 1 if alone else 2, row_body, 0)
    if alone:
        o_ref[1 - base] = o_in[...]
        keep_ref[1 - base] = keep_in[...]
        lse_ref[1 - base] = lse_in[...]


def attention(bounds, table, q, kv, se, ready=()):
    heads, n = kv.shape[2] // 128, kv.shape[1]
    packed = q.shape
    outs = [
        jax.ShapeDtypeStruct(packed, jnp.bfloat16),
        jax.ShapeDtypeStruct(packed, jnp.float32),
        jax.ShapeDtypeStruct((2, 2, heads, 1, TQ), jnp.float32),
    ]
    if not ready:
        outs.append(jax.ShapeDtypeStruct((heads, 2, TK, TQ), jnp.bfloat16))
    return pl.pallas_call(
        functools.partial(fwd_kernel, bool(ready)),
        out_shape=tuple(outs),
        in_specs=[SMEM_SPEC] * 2 + [VMEM_SPEC, ANY_SPEC, VMEM_SPEC] + [VMEM_SPEC] * len(ready),
        out_specs=(VMEM_SPEC,) * len(outs),
        scratch_shapes=[
            pltpu.VMEM((heads, 80, n), jnp.bfloat16),
            pltpu.VMEM((heads, 80, TQ), jnp.float32),
            pltpu.VMEM((heads, 1, TQ), jnp.float32),
            pltpu.VMEM((2, heads, TQ, 128), jnp.bfloat16),
            pltpu.VMEM(kv.shape[1:], jnp.bfloat16),
            pltpu.SemaphoreType.DMA((n // TK,)),
        ],
        compiler_params=pltpu.CompilerParams(vmem_limit_bytes=VMEM_BYTES),
        name="attention",
    )(bounds, table, q, kv, se, *ready)


def prepare(q, do, q_out, do_out):
    for h, tile in enumerate(spread_lanes(q, False)):
        q_out[h] = tile
    for h, tile in enumerate(spread_lanes(do, True)):
        do_out[h] = tile


def row_deltas(do, keep, delta):
    prod = (do.astype(jnp.float32) * keep).T
    top, low = prod[:, 0:TQ], prod[:, TQ:]
    delta[0] = jnp.sum(top[0:64], axis=0, keepdims=True)
    delta[1] = jnp.sum(top[64:128], axis=0, keepdims=True)
    delta[2] = jnp.concatenate(
        [jnp.sum(low[0:64], axis=0, keepdims=True), jnp.sum(low[64:128], axis=0, keepdims=True)], axis=1
    )


def near_start(parity):
    return 416 - TQ * parity


def far_sums(grid, h, first, end):
    def one(step, total):
        rows = grid[h, pl.ds(pl.multiple_of(step * 32, 32), 32)]
        return total + jnp.sum(rows.reshape(4, 8, TQ), axis=0)
    total = lax.fori_loop(first // 32, end // 32, one, jnp.zeros((8, TQ), jnp.float32))
    return jnp.sum(total, axis=0, keepdims=True)


def bucket_sums(parity, near, side, tab_ref, tab8):
    heads = near.shape[0]
    tab8[...] = jnp.zeros_like(tab8)

    def inner(step, _):
        start = pl.multiple_of(step * 32, 32)
        which = near_buckets(near_start(parity) + start, 32, parity)
        for b in range(BUCKETS):
            here = which == b
            for h in range(heads):
                rows = jnp.where(here, near[h, pl.ds(start, 32)], 0.0)
                tab8[h, b] += jnp.sum(rows.reshape(4, 8, TQ), axis=0)
        return 0

    lax.fori_loop(0, NEAR_ROWS // 32, inner, 0)
    for h in range(heads):
        tab_ref[h] = jnp.sum(tab8[h], axis=1)
        tab_ref[h, 15:16] += side[h, 0:1]
        tab_ref[h, 31:32] += side[h, 1:2]


def bwd_kernel(alone, bounds, table, q_ref, do_ref, keep_ref, kv_hbm, bias_ref, se_ref, lse_ref,
               dq_ref, dkv_ref, near_ref, side, delta, *rest):
    tab_ref, tab8, rest = (None, None, rest) if alone else (rest[0], rest[-1], rest[1:-1])
    kt, dqt, dkv, grid, qp, dp_ref, kv_ref, kv_sem = rest
    heads = lse_ref.shape[2]
    n = kv_hbm.shape[1]
    grid[...] = jnp.zeros_like(grid)
    side[...] = jnp.zeros_like(side)
    base = 1 - bounds[0, 0, 6] if alone else 0
    for at in range(1 if alone else 2):
        for i in range(2):
            prepare(q_ref[base + at, i], do_ref[base + at, i], qp.at[at, i], dp_ref.at[at, i])
    for r in range(2):
        for i in range(2):
            row_deltas(do_ref[r, i], keep_ref[r, i], delta.at[r, i])

    def row_body(at, _):
        r = base + at
        lo_all = jnp.minimum(bounds[r, 0, 0], bounds[r, 1, 0])
        hi_all = jnp.maximum(bounds[r, 0, 1], bounds[r, 1, 1])

        def fetch(t):
            rows = pl.ds(pl.multiple_of(t * TK, TK), TK)
            return pltpu.make_async_copy(kv_hbm.at[r, rows], kv_ref.at[rows], kv_sem.at[t])

        def begin(t, _):
            fetch(t).start()
            return 0

        lax.fori_loop(lo_all, hi_all, begin, 0)

        def clear(t, _):
            k0 = pl.multiple_of(t * TK, TK)
            for h in range(heads):
                dkv[h, pl.ds(k0, TK), :] = jnp.zeros((TK, 128), jnp.float32)
            return 0

        lax.fori_loop(0, n // TK, clear, 0)

        def turn(t, _):
            fetch(t).wait()
            k0 = pl.multiple_of(t * TK, TK)
            for h in range(heads):
                tile = kv_ref[pl.ds(k0, TK), h * 128 : h * 128 + 128]
                kt[h, 0:64, pl.ds(k0, TK)] = tile.T[0:64, :]
                kt[h, 64:80, pl.ds(k0, TK)] = jnp.ones((16, TK), jnp.bfloat16)
            return 0

        lax.fori_loop(lo_all, hi_all, turn, 0)

        def q_body(i, _):
            dqt[...] = jnp.zeros_like(dqt)

            def tile_body(t, _):
                k0 = pl.multiple_of(t * TK, TK)
                slot, plain = tile_kind(bounds, r, i, t)

                def finish(h, p, ds, where):
                    ds_low = ds.astype(jnp.bfloat16)
                    two = jnp.concatenate([ds_low, p.astype(jnp.bfloat16)], axis=1)
                    both = jnp.concatenate([qp[at, i, h], dp_ref[at, i, h]], axis=0)
                    dkv[h, pl.ds(k0, TK), :] += mxu(two, both)
                    dqt[h, where] += mxu(kt[h, :, pl.ds(k0, TK)], ds_low)

                def products(h):
                    tile = kv_ref[pl.ds(k0, TK), h * 128 : h * 128 + 128]
                    return mxu(tile, qp[at, i, h], NT), mxu(tile, dp_ref[at, i, h], NT)

                @pl.when(plain)
                def _():
                    for h in range(heads):
                        s, d_probs = products(h)
                        p = jnp.exp(s - (lse_ref[r, i, h] - jnp.where(slot == 0, table[h, 15], table[h, 31])))
                        finish(h, p, p * (d_probs - delta[r, i, h]), jnp.where(slot == 0, 0, 2))

                def general(bias):
                    ok = valid_mask(se_ref, r, i, k0)
                    for h in range(heads):
                        s, d_probs = products(h)
                        s = s + bias(h)
                        p = jnp.where(ok, jnp.exp(jnp.where(ok, s, NEG) - lse_ref[r, i, h]), 0.0)
                        ds = p * (d_probs - delta[r, i, h])
                        grid[h, pl.ds(pl.multiple_of(slot * TK, TK), TK)] += ds
                        finish(h, p, ds, 1)

                near = jnp.logical_and(slot > 0, slot < 3)
                pl.when(near)(lambda: general(lambda h: bias_ref[h, slot - 1].astype(jnp.float32)))
                away = jnp.logical_not(jnp.logical_or(plain, near))
                pl.when(away)(lambda: general(lambda h: jnp.where(slot == 0, table[h, 15], table[h, 31])))
                return 0

            lax.fori_loop(bounds[r, i, 0], bounds[r, i, 1], tile_body, 0)
            parts = []
            for h in range(heads):
                parts.append((dqt[h, 0, 0:64] + dqt[h, 1, 0:64] + dqt[h, 2, 0:64]).T * 0.125)
                side[h, 0:1] += dqt[h, 0, 64:65]
                side[h, 1:2] += dqt[h, 2, 64:65]
            dq_ref[at, i] = join_heads(parts).astype(jnp.bfloat16)
            return 0

        lax.fori_loop(0, 2, q_body, 0)

        def put(t, _):
            k0 = pl.multiple_of(t * TK, TK)
            for h in range(heads):
                dkv_ref[at, pl.ds(k0, TK), h * 128 : h * 128 + 128] = dkv[h, pl.ds(k0, TK), :].astype(jnp.bfloat16)
            return 0

        lax.fori_loop(0, n // TK, put, 0)
        return 0

    lax.fori_loop(0, 1 if alone else 2, row_body, 0)

    parity = bounds[0, 0, 5]
    first = TK + near_start(parity)
    for h in range(heads):
        near_ref[h] = grid[h, pl.ds(pl.multiple_of(first, 32), NEAR_ROWS)]
        side[h, 0:1] += far_sums(grid, h, 0, first)
        side[h, 1:2] += far_sums(grid, h, first + NEAR_ROWS, 4 * TK)
    if not alone:
        bucket_sums(parity, near_ref, side, tab_ref, tab8)


def attention_back(alone, bounds, table, q, do, keep, kv, bias, se, lse):
    heads, n = kv.shape[2] // 128, kv.shape[1]
    count = 1 if alone else 2
    table_out = [] if alone else [jax.ShapeDtypeStruct((heads, BUCKETS, TQ), jnp.float32)]
    return pl.pallas_call(
        functools.partial(bwd_kernel, alone),
        out_shape=(
            jax.ShapeDtypeStruct((count,) + q.shape[1:], jnp.bfloat16),
            jax.ShapeDtypeStruct((count,) + kv.shape[1:], jnp.bfloat16),
            jax.ShapeDtypeStruct((heads, NEAR_ROWS, TQ), jnp.float32),
            jax.ShapeDtypeStruct((heads, 2, TQ), jnp.float32),
            jax.ShapeDtypeStruct((2, 2, heads, 1, TQ), jnp.float32),
        ) + tuple(table_out),
        in_specs=[SMEM_SPEC] * 2 + [VMEM_SPEC] * 3 + [ANY_SPEC] + [VMEM_SPEC] * 3,
        out_specs=(VMEM_SPEC,) * (5 + len(table_out)),
        scratch_shapes=[
            pltpu.VMEM((heads, 80, n), jnp.bfloat16),
            pltpu.VMEM((heads, 3, 80, TQ), jnp.float32),
            pltpu.VMEM((heads, n, 128), jnp.float32),
            pltpu.VMEM((heads, 4 * TK, TQ), jnp.float32),
            pltpu.VMEM((count, 2, heads, TQ, 128), jnp.bfloat16),
            pltpu.VMEM((count, 2, heads, TQ, 128), jnp.bfloat16),
            pltpu.VMEM(kv.shape[1:], jnp.bfloat16),
            pltpu.SemaphoreType.DMA((n // TK,)),
        ] + [pltpu.VMEM((heads, BUCKETS, 8, TQ), jnp.float32) for _ in table_out],
        compiler_params=pltpu.CompilerParams(vmem_limit_bytes=VMEM_BYTES),
        name="attention_back",
    )(bounds, table, q, do, keep, kv, bias, se, lse)


TAPS = tuple(range(-3, 5))
LEAD = 8


def pool_scalars(y_rows, lab_rows, first):
    tokens = y_rows[0].shape[1]
    t = lax.broadcasted_iota(jnp.int32, (1, tokens), 1)
    at = lambda rows, k: rows[k + 3]
    found = []
    for p in range(2):
        inside = {1: 0 * t, 2: 0 * t + p, 3: (first + 2 * t + p) % 3, 4: 2 * (t % 2) + p}
        weights, scores = {}, []
        for b in range(1, MAX_BLOCK + 1):
            keep = {}
            for o in range(1 - b, b):
                same = jnp.logical_and(inside[b] + o >= 0, inside[b] + o < b)
                same = jnp.logical_and(same, at(lab_rows, p + o) == at(lab_rows, p))
                keep[o] = same.astype(jnp.float32)
            inverse = 1.0 / sum(keep.values())
            for o in keep:
                weights[b, o] = keep[o] * inverse
            scores.append(sum(weights[b, o] * at(y_rows, p + o) for o in keep))
        top = functools.reduce(jnp.maximum, scores)
        grown = [jnp.exp(s - top) for s in scores]
        total = sum(grown)
        found.append(([g / total for g in grown], weights))
    return found


def tap_weights(found):
    rows = []
    for k in TAPS:
        row = 0.0
        for p, (probs, weights) in enumerate(found):
            for b in range(1, MAX_BLOCK + 1):
                if (b, k - p) in weights:
                    row = row + probs[b - 1] * weights[b, k - p]
        rows.append(0.5 * row)
    return rows


def as_columns(rows):
    tokens = rows[0].shape[1]
    return jnp.concatenate(list(rows) + [jnp.zeros((128 - len(rows), tokens), jnp.float32)], axis=0).T


def load_bytes(x_ref, before, after, xs):
    length, width = x_ref.shape
    for j in range(width // 128):
        cols = slice(j * 128, j * 128 + 128)
        xs[j, 0:LEAD, :] = jnp.zeros((LEAD, 128), jnp.float32)
        xs[j, LEAD + length :, :] = jnp.zeros((LEAD, 128), jnp.float32)
        xs[j, LEAD - 2 : LEAD, :] = before[:, cols].astype(jnp.float32)
        xs[j, LEAD + length : LEAD + length + 2, :] = after[:, cols].astype(jnp.float32)
        xs[j, LEAD : LEAD + length, :] = x_ref[:, cols].astype(jnp.float32)


def tap(xs, k, tokens):
    return jnp.concatenate([xs[j, pl.ds(LEAD + k, tokens, stride=2), :] for j in range(xs.shape[0])], axis=1)


def strips(buf, first, rows):
    return jnp.concatenate([buf[j, first : first + rows, :] for j in range(buf.shape[0])], axis=1)


def unit_rows(values):
    return lax.rsqrt(jnp.mean(values * values, axis=-1, keepdims=True) + 1e-06)


def pool_tokens(scale, xs, labels, score, gain, tokens, y_ref, share_ref):
    width = xs.shape[0] * 128
    score = jnp.broadcast_to(score, (8, width))
    for k in TAPS:
        y_ref[k + 3 : k + 4, :] = mxu(score, tap(xs, k, tokens).astype(jnp.bfloat16), NT)[0:1]
    rows = [y_ref[j : j + 1, :] for j in range(8)]
    first = (lax.axis_index("blk") * 2 * tokens) % 3
    found = pool_scalars(rows, labels, first)
    lane = lax.broadcasted_iota(jnp.int32, (1, 128), 1)
    share = jnp.zeros((1, 128), jnp.float32)
    for b in range(MAX_BLOCK):
        share = jnp.where(lane == b, jnp.sum(found[0][0][b] + found[1][0][b], axis=1, keepdims=True) * scale, share)
    share_ref[...] = share
    columns = as_columns(tap_weights(found))
    hidden = sum(columns[:, k + 3 : k + 4] * tap(xs, k, tokens) for k in TAPS)
    return hidden, (hidden * unit_rows(hidden) * gain.astype(jnp.float32)).astype(jnp.bfloat16)


def put_pairs(keys, values, kv_ref):
    low = lax.broadcasted_iota(jnp.int32, (1, 128), 1) < 64
    for j in range(keys.shape[1] // 128):
        k_pair, v_pair = keys[:, j * 128 : j * 128 + 128], values[:, j * 128 : j * 128 + 128]
        one = jnp.where(low, k_pair, turned(v_pair))
        two = jnp.where(low, turned(k_pair), v_pair)
        for head, tile in ((2 * j, one), (2 * j + 1, two)):
            kv_ref[head // 3, :, head % 3 * 128 : head % 3 * 128 + 128] = tile


def pool_kernel(shards, scale, x_ref, before_ref, after_ref, lab_ref, score_ref, gain_ref, wq_ref, wk_ref, wv_ref,
                hidden_ref, n1_ref, y_ref, share_ref, q_ref, kv_ref, xs):
    tokens = hidden_ref.shape[0]
    load_bytes(x_ref, before_ref[0:2, :], after_ref[0:2, :], xs)
    labels = [lab_ref[j : j + 1, :] for j in range(8)]
    hidden_ref[...], n1 = pool_tokens(scale, xs, labels, score_ref[...], gain_ref[...], tokens, y_ref, share_ref)
    n1_ref[...] = n1
    put_pairs(mxu(n1, wk_ref[...]).astype(jnp.bfloat16), mxu(n1, wv_ref[...]).astype(jnp.bfloat16), kv_ref)
    put_packed(mxu(n1, wq_ref[...]).astype(jnp.bfloat16) * jnp.bfloat16(0.125), q_ref)


def put_packed(array, out_ref):
    tokens = array.shape[0]
    half = tokens // 2
    for g in range(GROUPS):
        part = array[:, g * 192 : g * 192 + 192]
        out_ref[g, 0:tokens, :] = part[:, 0:128]
        out_ref[g, tokens:, :] = jnp.concatenate([part[:half, 128:], part[half:, 128:]], axis=1)


def get_packed(packed_ref):
    tokens = packed_ref.shape[1] * 2 // 3
    parts = []
    for g in range(GROUPS):
        last = packed_ref[g, tokens:, :]
        parts += [packed_ref[g, 0:tokens, :], jnp.concatenate([last[:, :64], last[:, 64:]], axis=0)]
    return jnp.concatenate(parts, axis=1)


def pool_and_project(shards, scale, x, before, after, labels, score, gain, wq, wk, wv):
    length, width = x.shape
    tokens = length // 2
    return pl.pallas_call(
        functools.partial(pool_kernel, shards, scale),
        out_shape=(
            jax.ShapeDtypeStruct((tokens, width), jnp.float32),
            jax.ShapeDtypeStruct((tokens, width), jnp.bfloat16),
            jax.ShapeDtypeStruct((8, tokens), jnp.float32),
            jax.ShapeDtypeStruct((1, 128), jnp.float32),
            jax.ShapeDtypeStruct((GROUPS, tokens * 3 // 2, 128), jnp.bfloat16),
            jax.ShapeDtypeStruct((GROUPS, tokens, width * 2 // GROUPS), jnp.bfloat16),
        ),
        in_specs=[VMEM_SPEC] * 9,
        out_specs=(VMEM_SPEC,) * 6,
        scratch_shapes=[pltpu.VMEM((width // 128, length + 2 * LEAD, 128), jnp.float32)],
        compiler_params=pltpu.CompilerParams(vmem_limit_bytes=VMEM_BYTES),
        name="pool_and_project",
    )(x, before, after, labels, score, gain, wq, wk, wv)


GELU_A = math.sqrt(2.0 / math.pi)
GELU_B = 0.044715


def norm_back(d_out, rows, gain):
    unit = unit_rows(rows)
    flat = rows * unit
    scaled = d_out * gain
    d_rows = unit * (scaled - flat * jnp.mean(scaled * flat, axis=-1, keepdims=True))
    return d_rows, jnp.sum(d_out * flat, axis=0, keepdims=True)


def feed_kernel(o_ref, hidden_ref, ct_ref, gain_ref, wo_ref, wg_ref, wu_ref, wd_ref,
                out_ref, dres_ref, da_ref, dgain_ref, n2_ref, att_ref, act_ref, dg_ref, du_ref, db_ref, acc, dn2):
    ff = wg_ref.shape[1]
    step = 512
    att = get_packed(o_ref)
    att_ref[...] = att
    residual = hidden_ref[...] + mxu(att, wo_ref[...])
    gain = gain_ref[...].astype(jnp.float32)
    n2_ref[...] = (residual * unit_rows(residual) * gain).astype(jnp.bfloat16)
    acc[...] = residual
    dn2[...] = jnp.zeros_like(dn2)

    for j in range(ff // step):
        cols = slice(j * step, j * step + step)
        n2 = n2_ref[...]
        gate = mxu(n2, wg_ref[:, cols])
        up = mxu(n2, wu_ref[:, cols])
        d_act = mxu(ct_ref[...], wd_ref[cols, :], NT)
        square = gate * gate
        curve = jnp.tanh(GELU_A * gate * (1.0 + GELU_B * square))
        half = 0.5 * (1.0 + curve)
        grown = gate * half
        slope = half + 0.5 * gate * (1.0 - curve * curve) * (GELU_A * (1.0 + 3.0 * GELU_B * square))
        act = (grown * up).astype(jnp.bfloat16)
        d_gate = (d_act * up * slope).astype(jnp.bfloat16)
        d_up = (d_act * grown).astype(jnp.bfloat16)
        act_ref[:, cols] = act
        dg_ref[:, cols] = d_gate
        du_ref[:, cols] = d_up
        acc[...] += mxu(act, wd_ref[cols, :])
        dn2[...] += mxu(d_gate, wg_ref[:, cols], NT) + mxu(d_up, wu_ref[:, cols], NT)

    out_ref[...] = acc[...].astype(jnp.bfloat16)
    residual = hidden_ref[...] + mxu(att_ref[...], wo_ref[...])
    d_rows, d_gain = norm_back(dn2[...], residual, gain)
    dgain_ref[...] = d_gain
    d_res = ct_ref[...].astype(jnp.float32) + d_rows
    dres_ref[...] = d_res
    d_branch = d_res.astype(jnp.bfloat16)
    db_ref[...] = d_branch
    put_packed(mxu(d_branch, wo_ref[...], NT).astype(jnp.bfloat16), da_ref)


def feed_forward(o_home, hidden, ct, gain, wo, wg, wu, wd):
    tokens, width = hidden.shape
    ff = wg.shape[1]
    low = lambda cols: jax.ShapeDtypeStruct((tokens, cols), jnp.bfloat16)
    return pl.pallas_call(
        feed_kernel,
        out_shape=(
            low(width),
            jax.ShapeDtypeStruct((tokens, width), jnp.float32),
            jax.ShapeDtypeStruct(o_home.shape, jnp.bfloat16),
            jax.ShapeDtypeStruct((1, width), jnp.float32),
            low(width), low(width), low(ff), low(ff), low(ff), low(width),
        ),
        in_specs=[VMEM_SPEC] * 8,
        out_specs=(VMEM_SPEC,) * 10,
        scratch_shapes=[pltpu.VMEM((tokens, width), jnp.float32)] * 2,
        compiler_params=pltpu.CompilerParams(vmem_limit_bytes=VMEM_BYTES),
        name="feed_forward",
    )(o_home, hidden, ct, gain, wo, wg, wu, wd)


def unpack_pairs(dkv_ref, width):
    low = lax.broadcasted_iota(jnp.int32, (1, 128), 1) < 64
    dk_parts, dv_parts = [], []
    for j in range(width // 128):
        one, two = [dkv_ref[h // 3, :, h % 3 * 128 : h % 3 * 128 + 128] for h in (2 * j, 2 * j + 1)]
        dk_parts.append(jnp.where(low, one, turned(two)))
        dv_parts.append(jnp.where(low, turned(one), two))
    return jnp.concatenate(dk_parts, axis=1), jnp.concatenate(dv_parts, axis=1)


def pool_back(d_hidden, length, lab_ref, y_ref, score, gb_ref, edge_ref, spill_ref, xs, gbuf):
    tokens, width = d_hidden.shape
    lane = lax.broadcasted_iota(jnp.int32, (1, 128), 1)
    met = jnp.zeros((tokens, 128), jnp.float32)
    for k in TAPS:
        met = jnp.where(lane == k + 3, jnp.sum(d_hidden * tap(xs, k, tokens), axis=-1, keepdims=True), met)
    met = met.T
    first = (lax.axis_index("blk") * length) % 3
    found = pool_scalars([y_ref[j : j + 1, :] for j in range(8)], [lab_ref[j : j + 1, :] for j in range(8)], first)
    touch = [0.0] * 8
    for p, (probs, weights) in enumerate(found):
        d_block = []
        for b in range(1, MAX_BLOCK + 1):
            d_block.append(0.5 * sum(weights[b, o] * met[p + o + 3 : p + o + 4] for o in range(1 - b, b)))
        mean = sum(q * d for q, d in zip(probs, d_block))
        for b in range(1, MAX_BLOCK + 1):
            d_score = probs[b - 1] * (d_block[b - 1] - mean)
            for o in range(1 - b, b):
                touch[p + o + 3] = touch[p + o + 3] + d_score * weights[b, o]
    share_cols = as_columns(tap_weights(found) + touch)
    score = score.astype(jnp.float32)
    gbuf[...] = jnp.zeros_like(gbuf)
    d_score_vec = jnp.zeros((1, width), jnp.float32)
    for k in TAPS:
        own, via = share_cols[:, k + 3 : k + 4], share_cols[:, k + 11 : k + 12]
        added = own * d_hidden + via * score
        for j in range(gbuf.shape[0]):
            gbuf[j, pl.ds(LEAD + k, tokens, stride=2), :] += added[:, j * 128 : j * 128 + 128]
        d_score_vec = d_score_vec + jnp.sum(via * tap(xs, k, tokens), axis=0, keepdims=True)
    gb_ref[...] = strips(gbuf, LEAD, length).astype(jnp.bfloat16)
    edge_ref[0] = strips(gbuf, LEAD, 16)
    edge_ref[1] = strips(gbuf, LEAD + length - 16, 16)
    spill_ref[0] = strips(gbuf, 0, LEAD)
    spill_ref[1] = strips(gbuf, LEAD + length, LEAD)
    return d_score_vec


def put_small(small_ref, vectors, tab_ref, share_ref):
    small_ref[...] = jnp.zeros_like(small_ref)
    for row, vector in zip((0, 6, 12), vectors):
        for j in range(6):
            small_ref[row + j : row + j + 1, :] = vector[:, j * 128 : j * 128 + 128]
    heads = tab_ref.shape[0]
    group = lax.axis_index("blk") // (lax.axis_size("blk") // GROUPS)
    for h in range(heads):
        total = lax.dot_general(
            jnp.ones((8, tab_ref.shape[2]), jnp.float32), tab_ref[h], NT,
            precision=lax.Precision.HIGHEST, preferred_element_type=jnp.float32,
        )
        small_ref[pl.ds(18 + group * heads + h, 1), 0:BUCKETS] = total[0:1]
    small_ref[30:31, :] = share_ref[...]


def last_kernel(shards, axes, order, dq_ref, dkv_ref, hidden_ref, dres_ref, x_ref, before_ref, after_ref, lab_ref, y_ref, score_ref,
                gain_ref, wq_ref, wk_ref, wv_ref, dgain2_ref, share_ref, tab_ref, gb_ref, edge_ref, spill_out, small_out, parts_ref,
                w_send, w_recv, s_send, s_recv, xs, gbuf, spill_ref, small_ref, small_bufs):
    at = {"dp": lax.axis_index("dp"), "blk": lax.axis_index("blk")}
    width = hidden_ref.shape[1]
    whole = Whole(axes, at, order, small_ref, small_bufs, small_out, w_send, w_recv)
    left = (at["dp"], (at["blk"] + shards - 1) % shards)
    right = (at["dp"], (at["blk"] + 1) % shards)
    greet([whole.stream.target(p) for p in range(len(axes))] + [left, right])
    load_bytes(x_ref, before_ref[0:2, :], after_ref[0:2, :], xs)
    dq = get_packed(dq_ref)
    dk, dv = unpack_pairs(dkv_ref, width)
    parts_ref[0], parts_ref[1], parts_ref[2] = dq, dk, dv
    d_n1 = mxu(dq, wq_ref[...], NT) + mxu(dk, wk_ref[...], NT) + mxu(dv, wv_ref[...], NT)
    d_rows, d_gain1 = norm_back(d_n1, hidden_ref[...], gain_ref[...].astype(jnp.float32))
    d_hidden = dres_ref[...] + d_rows
    d_score = pool_back(d_hidden, x_ref.shape[0], lab_ref, y_ref, score_ref[...], gb_ref, edge_ref, spill_ref, xs, gbuf)
    put_small(small_ref, (d_score, d_gain1, dgain2_ref[...]), tab_ref, share_ref)
    spills = [
        remote(spill_ref.at[0], spill_out.at[1], s_send.at[0], s_recv.at[1], left),
        remote(spill_ref.at[1], spill_out.at[0], s_send.at[1], s_recv.at[0], right),
    ]
    whole.copy(0).start()
    for copy in spills:
        copy.start()
    for stage in range(len(axes)):
        advance(whole, stage)
    for copy in spills:
        copy.wait()


def last_part(shape, dq, dkv, hidden, dres, x, before, after, labels, y, score, gain, wq, wk, wv, dgain2, share, tab):
    tokens, width = hidden.shape
    length = x.shape[0]
    axes = bit_axes(shape)
    ndim = len(axes)
    full, sem, low = jax.ShapeDtypeStruct, pltpu.SemaphoreType.DMA, jnp.bfloat16
    strip = pltpu.VMEM((width // 128, length + 2 * LEAD, 128), jnp.float32)
    return pl.pallas_call(
        functools.partial(last_kernel, shape["blk"], axes, tuple(reversed(range(ndim)))),
        out_shape=(
            full((length, width), low),
            full((2, 16, width), jnp.float32),
            full((2, LEAD, width), jnp.float32),
            full((32, 128), jnp.float32),
            full((3, tokens, width), low),
        ),
        in_specs=[VMEM_SPEC] * 17,
        out_specs=(VMEM_SPEC,) * 5,
        scratch_shapes=[
            sem((ndim,)), sem((ndim,)), sem((2,)), sem((2,)), strip, strip,
            pltpu.VMEM((2, LEAD, width), jnp.float32), pltpu.VMEM((32, 128), jnp.float32), pltpu.VMEM((2, ndim, 32, 128), jnp.float32),
        ],
        compiler_params=pltpu.CompilerParams(collective_id=3, has_side_effects=True, vmem_limit_bytes=VMEM_BYTES),
        name="last_part",
    )(dq, dkv, hidden, dres, x, before, after, labels, y, score, gain, wq, wk, wv, dgain2, share, tab)


def finish_kernel(shards, block_ref, gb_ref, edge_ref, spill_ref, small_ref, *refs):
    position = lax.axis_index("blk")
    count = 7 if len(refs) == 7 else 14
    streams, outs = refs[: len(refs) - count], refs[len(refs) - count :]
    out_ref, bytes_ref, score_ref, gain1_ref, gain2_ref, tab_ref, share_ref = outs[:7]
    out_ref[...] = block_ref[...]
    length = gb_ref.shape[0]
    bytes_ref[...] = gb_ref[...]
    zero = jnp.zeros((16 - LEAD, gb_ref.shape[1]), jnp.float32)
    left = jnp.where(position > 0, spill_ref[0], 0.0)
    right = jnp.where(position < shards - 1, spill_ref[1], 0.0)
    bytes_ref[0:16, :] = (edge_ref[0] + jnp.concatenate([left, zero], axis=0)).astype(jnp.bfloat16)
    bytes_ref[length - 16 :, :] = (edge_ref[1] + jnp.concatenate([zero, right], axis=0)).astype(jnp.bfloat16)
    for row, ref in ((0, score_ref), (6, gain1_ref), (12, gain2_ref)):
        for j in range(6):
            ref[j * 128 : j * 128 + 128] = small_ref[row + j, :]
    tab_ref[...] = small_ref[18 : 18 + tab_ref.shape[0], 0 : tab_ref.shape[1]]
    share_ref[...] = small_ref[30, 0:MAX_BLOCK]
    if streams:
        gq, gk, gv, go, gg, gu, gd = outs[7:]
        per, width = gq.shape
        half, ff = width // 2, gg.shape[1]
        one, two, down, *thirds = streams
        for ref, third in zip((gq, gk, gv), thirds):
            ref[:, :half] = third[:per, :]
            ref[:, half:] = third[per:, :]
        first = one.shape[1]
        for ref, rows in ((gg, slice(0, per)), (gu, slice(per, 2 * per))):
            ref[:, :first] = one[rows, :]
            ref[:, first:] = two[rows, : ff - first]
        go[:, :half] = two[:per, ff - first :]
        go[:, half:] = two[per:, ff - first :]
        gd[...] = down[...]


def finish(shards, heads_all, per, ff, block_out, gb, edge, spill, small, streams):
    width = gb.shape[1]
    full = jax.ShapeDtypeStruct
    line = full((width,), jnp.float32)
    outs = [full(block_out.shape, jnp.bfloat16), full(gb.shape, jnp.bfloat16), line, line, line]
    outs += [full((heads_all, BUCKETS), jnp.float32), full((MAX_BLOCK,), jnp.float32)]
    if streams:
        square, broad = full((per, width), jnp.float32), full((per, ff), jnp.float32)
        outs += [square] * 4 + [broad] * 2 + [full(streams[2].shape, jnp.float32)]
    return pl.pallas_call(
        functools.partial(finish_kernel, shards),
        out_shape=tuple(outs),
        in_specs=[VMEM_SPEC] * (5 + len(streams)),
        out_specs=(VMEM_SPEC,) * len(outs),
        compiler_params=pltpu.CompilerParams(vmem_limit_bytes=VMEM_BYTES),
        name="finish",
    )(block_out, gb, edge, spill, small, *streams)


class NearRows:
    def __init__(self, grid, first):
        self.grid, self.first, self.shape = grid, first, grid.shape

    def __getitem__(self, index):
        h, rows = index
        return self.grid[h, pl.ds(pl.multiple_of(self.first + rows.start, 32), rows.size)]


class Refs:
    def __init__(self, **refs):
        self.__dict__.update(refs)


def row_of(vectors, k):
    return jnp.concatenate([vectors[6 * k + j : 6 * k + j + 1, :] for j in range(6)], axis=1)


class BiasTable:
    def __init__(self, ref, place, heads):
        self.ref, self.first = ref, place.group * heads

    def __getitem__(self, index):
        head, bucket = index
        return self.ref[self.first + head, bucket]


class Held:
    def __init__(self, array, space):
        self.array, self.space = array, space


def call(kernel, ident, ins, outs, scratch):
    leaf = lambda entry: isinstance(entry, Held) or isinstance(entry, tuple) or not isinstance(entry, (dict, list))
    parts = [jax.tree.flatten(part, is_leaf=leaf) for part in (ins, outs, scratch)]
    counts = [len(part[0]) for part in parts]
    given, wanted, kept = [part[0] for part in parts]

    def run(*refs):
        named, start = {}, 0
        for count, (_, tree) in zip(counts, parts):
            named.update(jax.tree.unflatten(tree, refs[start : start + count]))
            start += count
        kernel(Refs(**named))

    space = lambda entry, at: entry.space if isinstance(entry, Held) else entry[2] if isinstance(entry, tuple) and len(entry) > 2 else at
    found = pl.pallas_call(
        run,
        out_shape=tuple(jax.ShapeDtypeStruct(entry[0], entry[1]) for entry in wanted),
        in_specs=[pl.BlockSpec(memory_space=space(entry, pltpu.VMEM)) for entry in given],
        out_specs=tuple(pl.BlockSpec(memory_space=space(entry, pltpu.VMEM)) for entry in wanted),
        scratch_shapes=kept,
        compiler_params=pltpu.CompilerParams(collective_id=ident, has_side_effects=True, vmem_limit_bytes=VMEM_BYTES),
        name=kernel.func.__name__,
    )(*[entry.array if isinstance(entry, Held) else entry for entry in given])
    return Refs(**jax.tree.unflatten(parts[1][1], found))


wide = lambda value: value.astype(jnp.float32)
slim = lambda value: value.astype(jnp.bfloat16)


class RowBack:
    def __init__(self, place, r):
        self.place, self.r = place, r
        self.heads = r.lse.shape[1]
        self.table = BiasTable(r.table, place, self.heads)
        self.tokens = TQ
        self.across, self.core_to = place.other_rest(2), place.other_rest(1)
        self.y, self.core = bit(place.rest, 2), place.rest % 2

    def group_of(self, n):
        return (self.place.group + 1 + n) % GROUPS

    def tile_start(self, m):
        place_y = jnp.where(m % 2 == 0, 1 - self.y, self.y)
        return pl.multiple_of((self.group_of(m // 2) * 2 + place_y) * TK, TK)

    def fetch(self, m):
        r = self.r
        rows = pl.ds(self.tile_start(m), TK)
        return (
            pltpu.make_async_copy(r.kv_hbm.at[rows], r.kv.at[m], r.kv_sem.at[m]),
            pltpu.make_async_copy(r.kl_hbm.at[rows], r.kl.at[m], r.kl_sem.at[m]),
        )

    def fetch_all(self):
        for m in range(2 * GROUPS):
            for copy in self.fetch(m):
                copy.start()

    def prepare(self):
        r = self.r

        def one(i, _):
            for h, tile in enumerate(spread_lanes(r.q[i], False)):
                r.qp[i, h] = tile
            for h, tile in enumerate(spread_lanes(r.do[i], True)):
                r.dp[i, h] = tile
            row_deltas(r.do[i], r.keep[i], r.delta.at[i])
            return 0

        lax.fori_loop(0, GROUPS, one, 0)

    def clear(self):
        r = self.r
        r.dqt[...] = jnp.zeros_like(r.dqt)
        r.grid[...] = jnp.zeros_like(r.grid)

    def core_copy(self, n, j):
        r = self.r
        return remote(r.held.at[n, j, 1 - self.core], r.core_in.at[n, j], r.core_send.at[n, j], r.core_recv.at[n, j], self.core_to)

    def y_copy(self, n):
        r = self.r
        return remote(r.y_out.at[n], r.y_in.at[n], r.y_send.at[n], r.y_recv.at[n], self.across)

    def z_copy(self, n):
        r, place = self.r, self.place
        return remote(r.z_out.at[n], r.dkv_home.at[place.group], r.z_send.at[n], r.z_recv.at[n], place.at(place.row, self.group_of(n), place.rest))

    def by_rows(self, one):
        def step(k, _):
            one(pl.ds(pl.multiple_of(k * 32, 32), 32))
            return 0
        lax.fori_loop(0, self.tokens // 32, step, 0)

    def own_sum(self, n, j, rows):
        return wide(self.r.held[n, j, self.core, rows]) + wide(self.r.core_in[n, j, rows])

    def send_y(self, n):
        r = self.r
        self.core_copy(n, 0).wait()

        def one(rows):
            r.y_out[n, rows] = slim(self.own_sum(n, 0, rows))

        self.by_rows(one)
        self.y_copy(n).start()

    def send_home(self, n):
        r = self.r
        self.core_copy(n, 1).wait()
        self.y_copy(n).wait()
        here = isinstance(n, int) and n == GROUPS - 1

        def one(rows):
            total = slim(self.own_sum(n, 1, rows) + wide(r.y_in[n, rows]))
            if here:
                r.dkv_home[self.place.group, rows] = total
            else:
                r.z_out[n, rows] = total

        self.by_rows(one)
        if not here:
            self.z_copy(n).start()

    def begin(self, m, a):
        r = self.r
        for copy in self.fetch(m):
            copy.wait()
        r.acc[a] = jnp.zeros_like(r.acc[a])
        for h in range(self.heads):
            r.kt[a, h, 0:64] = r.kv[m, :, h * 128 : h * 128 + 128].T[0:64]
            r.kt[a, h, 64:80] = jnp.ones((16, TK), jnp.bfloat16)

    def part(self, m, i, a):
        r, heads = self.r, self.heads
        t = self.tile_start(m) // TK
        keys = lambda h: r.kv[m, :, h * 128 : h * 128 + 128]
        slot = near_slot(self.place, i, t)
        away = jnp.logical_or(slot == 0, slot == 3)

        def finish(h, p, ds, where):
            ds_low = ds.astype(jnp.bfloat16)
            two = jnp.concatenate([ds_low, p.astype(jnp.bfloat16)], axis=1)
            both = jnp.concatenate([r.qp[i, h], r.dp[i, h]], axis=0)
            r.acc[a, :, h * 128 : h * 128 + 128] += mxu(two, both)
            r.dqt[i, h, where] += mxu(r.kt[a, h], ds_low)

        def products(h):
            s = mxu(jnp.concatenate([keys(h), r.kl[m]], axis=1), jnp.concatenate([r.qp[i, h], r.ql[i]], axis=1), NT)
            return s, mxu(keys(h), r.dp[i, h], NT)

        @pl.when(away)
        def _():
            for h in range(heads):
                s, d_probs = products(h)
                p = jnp.exp(s - (r.lse[i, h] - jnp.where(slot == 0, self.table[h, 15], self.table[h, 31])))
                finish(h, p, p * (d_probs - r.delta[i, h]), jnp.where(slot == 0, 0, 2))

        @pl.when(jnp.logical_not(away))
        def _():
            for h in range(heads):
                s, d_probs = products(h)
                p = jnp.exp(s + r.bias[h, slot - 1].astype(jnp.float32) - r.lse[i, h])
                ds = p * (d_probs - r.delta[i, h])
                r.grid[h, pl.ds(pl.multiple_of((slot - 1) * TK, TK), TK)] += ds
                finish(h, p, ds, 1)

    def end(self, m, a):
        r = self.r
        n, j = m // 2, m % 2
        for half in range(2):
            r.held[n, j, half] = r.acc[a, half * self.tokens : half * self.tokens + self.tokens].astype(jnp.bfloat16)
        self.core_copy(n, j).start()

    def query(self, i):
        r, place = self.r, self.place
        parts = []
        for h in range(self.heads):
            parts.append((r.dqt[i, h, 0, 0:64] + r.dqt[i, h, 1, 0:64] + r.dqt[i, h, 2, 0:64]).T * 0.125)
        r.dq[i] = slim(join_heads(parts))
        step = (i - place.group + GROUPS) % GROUPS
        copy = remote(r.dq.at[i], r.dq_home.at[place.group], r.q_send.at[step], r.q_recv.at[step], place.at(place.row, i, place.rest))
        pl.when(step > 0)(copy.start)

    def buckets(self):
        r = self.r
        first = near_start(self.core)
        for h in range(self.heads):
            r.side[h, 0:1] = sum(r.dqt[i, h, 0, 64:65] for i in range(GROUPS)) + far_sums(r.grid, h, 0, first)
            r.side[h, 1:2] = sum(r.dqt[i, h, 2, 64:65] for i in range(GROUPS)) + far_sums(r.grid, h, first + NEAR_ROWS, 2 * TK)
        bucket_sums(self.core, NearRows(r.grid, first), r.side, r.tab, r.tab8)

    def wait_home(self):
        r, place = self.r, self.place
        for n in range(GROUPS - 1):
            there = r.dkv_home.at[(place.group - 1 - n + GROUPS) % GROUPS]
            remote(r.z_out.at[n], there, r.z_send.at[n], r.z_recv.at[n], self.core_to).wait()


def back_kernel(shards, axes, plans, r):
    place = Place(shards)
    at = {"dp": place.dp, "blk": place.blk}
    tokens, width = r.hidden.shape
    back = RowBack(place, r)
    streams = []
    for s, (kept, order) in enumerate(plans):
        src = r.early_hbm[s] if s < 3 else r.late[s - 3]
        own = r.early_own[s] if s < 3 else None
        streams.append(Stream(axes, at, kept, order, src, own, r.bufs[s], r.sums[s], r.w_send.at[s], r.w_recv.at[s]))
    early, late = streams[:3], streams[3:]
    whole = Whole(axes, at, (4, 0, 3, 2, 1), r.small, r.small_bufs, r.small_out, r.w_send.at[len(plans)], r.w_recv.at[len(plans)])
    left, right = (place.dp, (place.blk + shards - 1) % shards), (place.dp, (place.blk + 1) % shards)

    met = hail([place.other_group(step) for step in (1, 2, 3)] + [back.across, back.core_to, place.other_row(), left, right])
    back.fetch_all()
    halves = []
    for s, stream in enumerate(early):
        (now,) = stream.order[:1]
        index = tuple(stream.own(p) if p == now else slice(None) for p in stream.kept)
        halves.append(pltpu.make_async_copy(r.early_hbm[s].at[index], r.early_own[s], r.own_sem.at[s]))
        halves[-1].start()
    later = [pltpu.make_async_copy(src, dst, r.later_sem.at[k]) for k, (src, dst) in enumerate((
        (r.hidden_hbm, r.hidden), (r.dres_hbm, r.dres), (r.n1_hbm, r.n1), (r.x_hbm, r.x), (r.wq_hbm, r.wq), (r.wk_hbm, r.wk), (r.wv_hbm, r.wv),
    ))]
    for copy in later:
        copy.start()
    back.prepare()
    await_all(met)
    for stream in early:
        stream.copy(0).start()
    back.clear()

    def halve(s):
        halves[s].wait()
        advance(early[s], 0)

    def step(m, _):
        back.begin(m, 0)

        def one(i, _):
            back.part(m, i, 0)
            return 0

        lax.fori_loop(0, GROUPS, one, 0)
        back.end(m, 0)
        for delay, action in ((1, back.send_y), (3, back.send_home)):
            then = m - delay + 2 * GROUPS
            n = then // 2 - GROUPS

            @pl.when(jnp.logical_and(then % 2 == 0, n >= 0))
            def _():
                action(n)

        for when, s in ((4, 0), (5, 2)):
            pl.when(m == when)(functools.partial(halve, s))
        return 0

    lax.fori_loop(0, 2 * GROUPS - 2, step, 0)
    back.begin(6, 0)
    back.begin(7, 1)

    def chunk(k, _):
        i = (place.group + 1 + k) % GROUPS
        back.part(6, i, 0)
        back.part(7, i, 1)
        back.query(i)
        pl.when(k == 3)(functools.partial(back.send_home, 2))
        return 0

    lax.fori_loop(0, GROUPS, chunk, 0)
    back.end(6, 0)
    back.end(7, 1)
    home = Line(place, r.dq, r.dq_home, r.q_send, r.q_recv)
    home.keep().start()
    halve(1)
    back.send_y(3)
    back.buckets()
    back.send_home(3)
    for copy in later:
        copy.wait()
    load_bytes(r.x, r.before[14:16, :], r.after[0:2, :], r.xs)
    n1_t = r.n1[...].T
    for s in (2, 0, 1):
        advance(early[s], 1)
    home.wait_all()
    dq = get_packed(r.dq_home)
    devices = 1 << len(axes)
    per = width // devices
    half = width // 2

    def weights(stream, part):
        r.total[...] = mxu(n1_t, part)

        def block(d, _):
            rows = pl.ds(pl.multiple_of(d * per, 8), per)
            index, rest = [], d
            for _ in axes:
                index.append(rest % 2)
                rest = rest // 2
            part = r.total[rows, :]
            stream.src[tuple(reversed(index))] = jnp.concatenate([part[:, :half], part[:, half:]], axis=0).astype(jnp.bfloat16)
            return 0

        lax.fori_loop(0, devices, block, 0)
        stream.copy(0).start()

    weights(late[0], dq)
    back.wait_home()
    dk, dv = unpack_pairs(r.dkv_home, width)
    weights(late[1], dk)
    weights(late[2], dv)
    d_n1 = mxu(dq, r.wq[...], NT) + mxu(dk, r.wk[...], NT) + mxu(dv, r.wv[...], NT)
    d_rows, d_gain1 = norm_back(d_n1, r.hidden[...], row_of(r.vectors, 1))
    d_hidden = r.dres[...] + d_rows
    for stream in late:
        advance(stream, 0)
    for stream in early:
        advance(stream, 2)
    d_score = pool_back(d_hidden, r.x.shape[0], r.labels, r.y, row_of(r.vectors, 0), r.gb, r.edge, r.spill, r.xs, r.gbuf)
    put_small(r.small, (d_score, d_gain1, r.dgain2[...]), r.tab, r.share)
    whole.copy(0).start()
    spills = [
        remote(r.spill.at[0], r.spill_out.at[1], r.s2_send.at[0], r.s2_recv.at[1], left),
        remote(r.spill.at[1], r.spill_out.at[0], r.s2_send.at[1], r.s2_recv.at[0], right),
    ]
    for copy in spills:
        copy.start()
    for stage in range(1, len(axes)):
        for stream in late:
            advance(stream, stage)
        advance(whole, stage - 1)
        if stage == 1:
            for stream in early:
                advance(stream, 3)
    advance(whole, len(axes) - 1)
    for copy in spills:
        copy.wait()


def back_and_last(shape, early, inputs):
    shards = shape["blk"]
    axes = bit_axes(shape)
    ndim = len(axes)
    kv, q, hidden = inputs["kv_hbm"].array, inputs["q"], inputs["hidden_hbm"].array
    heads, width = kv.shape[1] // 128, kv.shape[1]
    tokens, features = hidden.shape
    length = inputs["x_hbm"].array.shape[0]
    f32, low, sem = jnp.float32, jnp.bfloat16, pltpu.SemaphoreType.DMA
    chunk = (tokens, width)
    every = (0, 1, 2, 3, 4)
    four = (0, 1, 2, 3)
    plans = [
        (four, (0, 3, 2, 1)), (four, (3, 0, 2, 1)), (four, (2, 0, 3, 1)),
        (every, (4, 0, 3, 2, 1)), (every, (4, 3, 2, 0, 1)), (every, (4, 2, 0, 3, 1)),
    ]
    own = (2 * (features // (1 << ndim)), features // 2)
    blocks = [part.shape[-2:] for part in early] + [own] * 3
    ins = dict(inputs, early_hbm=[Held(part.reshape((2, 2, 2, 2) + part.shape[-2:]), pl.ANY) for part in early])
    outs = dict(
        gb=((length, features), low), edge=((2, 16, features), f32), spill_out=((2, LEAD, features), f32),
        small_out=((32, 128), f32), sums=[(block, f32) for block in blocks],
    )
    mem = lambda shape, dtype=low: pltpu.VMEM(shape, dtype)
    pairs, fours = sem((GROUPS, 2)), sem((GROUPS,))
    strip = mem((features // 128, length + 2 * LEAD, 128), f32)
    eights = sem((2 * GROUPS,))
    scratch = dict(
        kt=mem((2, heads, 80, TK)), dqt=mem((GROUPS, heads, 3, 80, TQ), f32), acc=mem((2, TK, width), f32),
        grid=mem((heads, 2 * TK, TQ), f32), side=mem((heads, 2, TQ), f32), tab8=mem((heads, BUCKETS, 8, TQ), f32),
        tab=mem((heads, BUCKETS, TQ), f32), delta=mem((GROUPS, heads, 1, TQ), f32),
        qp=mem((GROUPS, heads, TQ, 128)), dp=mem((GROUPS, heads, TQ, 128)),
        kv=mem((2 * GROUPS, TK, width)), kl=mem((2 * GROUPS, TK, 128)),
        held=mem((GROUPS, 2, 2) + chunk), core_in=mem((GROUPS, 2) + chunk),
        y_out=mem((GROUPS,) + chunk), y_in=mem((GROUPS,) + chunk), z_out=mem((GROUPS,) + chunk), dkv_home=mem((GROUPS,) + chunk),
        dq=mem(q.shape), dq_home=mem(q.shape),
        core_send=pairs, core_recv=pairs, y_send=fours, y_recv=fours, z_send=fours, z_recv=fours, q_send=fours, q_recv=fours,
        kv_sem=eights, kl_sem=eights, own_sem=sem((3,)), later_sem=sem((7,)),
        hidden=mem((tokens, features), f32), dres=mem((tokens, features), f32), n1=mem((tokens, features)), x=mem((length, features)),
        wq=mem((features, features)), wk=mem((features, features)), wv=mem((features, features)),
        w_send=sem((len(plans) + 1, ndim)), w_recv=sem((len(plans) + 1, ndim)), s2_send=sem((2,)), s2_recv=sem((2,)),
        xs=strip, gbuf=strip, spill=mem((2, LEAD, features), f32), small=mem((32, 128), f32),
        small_bufs=mem((2, ndim, 32, 128), f32), total=mem((features, features), f32),
    )
    scratch["early_own"] = [mem((2, 2, 2) + block) for block in blocks[:3]]
    scratch["late"] = [mem((2,) * ndim + own)] * 3
    scratch["bufs"] = [stream_scratch(len(kept), order, *block) for (kept, order), block in zip(plans, blocks)]
    return call(functools.partial(back_kernel, shards, axes, plans), 6, ins, outs, scratch)


def label_features(line, unlike):
    rows = [(line != k if unlike else line == k).astype(jnp.float32) for k in range(8)]
    return slim(jnp.concatenate(rows + [jnp.zeros((120, line.shape[1]), jnp.float32)], axis=0).T)


class Line:
    def __init__(self, place, src, dst, send_sem, recv_sem):
        self.place, self.src, self.dst, self.send_sem, self.recv_sem = place, src, dst, send_sem, recv_sem

    def copy(self, step, slot):
        group = self.place.group
        return remote(
            self.src.at[(group + step) % GROUPS], self.dst.at[slot], self.send_sem.at[step], self.recv_sem.at[step],
            self.place.other_group(step),
        )

    def keep(self):
        group = self.place.group
        return pltpu.make_async_copy(self.src.at[group], self.dst.at[group], self.send_sem.at[0])

    def start(self, steps=(1, 3, 2)):
        for step in steps:
            self.copy(step, self.place.group).start()

    def wait(self, step):
        self.copy(step, (self.place.group - step + GROUPS) % GROUPS).wait()

    def wait_all(self):
        for step in (1, 3, 2):
            self.wait(step)
        self.keep().wait()

    def gone(self, step):
        self.copy(step, self.place.group).wait_send()

    def come_all(self):
        for step in (1, 3, 2):
            self.copy(step, (self.place.group - step + GROUPS) % GROUPS).wait_recv()
        self.keep().wait()


def near_slot(place, chunk, t):
    first = (chunk * place.rest_size + place.rest) * TQ
    return jnp.clip(t - (first // TK - 1 + place.rest % 2) + 1, 0, 3)


class RowForward:
    def __init__(self, place, r):
        self.place, self.r, self.heads = place, r, r.lse.shape[1]
        self.table = BiasTable(r.table, place, self.heads)

    def clear(self):
        self.r.acc[...] = jnp.zeros_like(self.r.acc)
        self.r.mx[...] = jnp.full_like(self.r.mx, FIRST_MAX)

    def queries(self, chunk):
        r = self.r
        for h, tile in enumerate(spread_lanes(r.q_all[chunk], False)):
            r.qp[chunk, h] = jnp.concatenate([tile, r.ql[chunk]], axis=1)

    def tile(self, t):
        r = self.r
        rows = pl.ds(pl.multiple_of(t * TK, TK), TK)
        keys = lambda h: r.kv_all[rows, h * 128 : h * 128 + 128]
        for h in range(self.heads):
            r.vt[h, 0:64] = keys(h).T[64:128]
            r.vt[h, 64:80] = jnp.ones((16, TK), jnp.bfloat16)

        def scores(i, h):
            return mxu(jnp.concatenate([keys(h), r.kl[rows, :]], axis=1), r.qp[i, h], NT)

        def finish(i, h, s, b):
            m_old = r.mx[i, h]
            m_new = jnp.maximum(m_old, jnp.max(s, axis=0, keepdims=True) + b)
            p = jnp.exp(s - (m_new - b)).astype(jnp.bfloat16)
            r.mx[i, h] = m_new
            r.acc[i, h] = r.acc[i, h] * jnp.exp(m_old - m_new) + mxu(r.vt[h], p)

        def part(i, _):
            slot = near_slot(self.place, i, t)
            away = jnp.logical_or(slot == 0, slot == 3)

            @pl.when(away)
            def _():
                found = [scores(i, h) for h in range(self.heads)]
                for h in range(self.heads):
                    finish(i, h, found[h], jnp.where(slot == 0, self.table[h, 15], self.table[h, 31]))

            @pl.when(jnp.logical_not(away))
            def _():
                for h in range(self.heads):
                    finish(i, h, scores(i, h) + r.near[h, slot - 1].astype(jnp.float32), 0.0)

            return 0

        def pair(p, _):
            slots = [near_slot(self.place, 2 * p + k, t) for k in range(2)]
            far = [jnp.logical_or(slot == 0, slot == 3) for slot in slots]
            both = jnp.logical_and(far[0], far[1])

            @pl.when(both)
            def _():
                items = [(2 * p + k, h, jnp.where(slots[k] == 0, self.table[h, 15], self.table[h, 31])) for h in range(self.heads) for k in range(2)]
                found = [scores(i, h) for i, h, _ in items]
                for (i, h, b), s in zip(items, found):
                    finish(i, h, s, b)

            @pl.when(jnp.logical_not(both))
            def _():
                lax.fori_loop(2 * p, 2 * p + 2, part, 0)

            return 0

        lax.fori_loop(0, GROUPS // 2, pair, 0)

    def end(self):
        r = self.r

        def one(i, _):
            parts = []
            for h in range(self.heads):
                total = r.acc[i, h, 64:65, :]
                parts.append((r.acc[i, h, 0:64, :] / total).T)
                r.lse[i, h] = r.mx[i, h] + jnp.log(total)
            joined = join_heads(parts)
            r.o[i] = joined.astype(jnp.bfloat16)
            r.keep[i] = joined
            return 0

        lax.fori_loop(0, GROUPS, one, 0)


def label_taps(place, own, left, right):
    at_left, at_right = place.blk == 0, place.blk == place.shards - 1
    even, odd = jnp.concatenate([own[0:1], own[1:2]], axis=1), jnp.concatenate([own[2:3], own[3:4]], axis=1)
    none = jnp.full((1, 1), -1, jnp.int32)
    before = [jnp.where(at_left, none, left[row : row + 1, 127:128]) for row in (1, 3)]
    after = [jnp.where(at_right, none, right[row : row + 1, 0:1]) for row in (0, 2)]
    join = lambda *parts: jnp.concatenate(parts, axis=1)
    return [
        join(none, before[1], odd[:, :-2]), join(before[0], even[:, :-1]), join(before[1], odd[:, :-1]), even, odd,
        join(even[:, 1:], after[0]), join(odd[:, 1:], after[1]), join(even[:, 2:], after[0], none),
    ]


def front_kernel(shards, scale, r):
    place = Place(shards)
    tokens = r.kv.shape[1]
    y, core = bit(place.rest, 2), place.rest % 2
    core_to, across = place.other_rest(1), place.other_rest(2)
    peers = [(place.dp, (place.blk + step) % shards) for step in range(1, shards)]
    met = hail(peers)
    length = r.x.shape[0]

    def label_copy(step, block):
        return remote(r.label, r.labels_all.at[block], r.lab_send.at[step], r.lab_recv.at[step], peers[step - 1])

    def label_come(step):
        back = (place.blk + shards - step) % shards
        label_copy(step, back).wait_recv()
        return r.labels_all[back]

    lane = lax.broadcasted_iota(jnp.int32, (128, 128), 0)
    to = lax.broadcasted_iota(jnp.int32, (128, 128), 1)
    apart = (lane == jnp.where(to < 64, 2 * to, 2 * to - 127)).astype(jnp.float32).astype(jnp.bfloat16)
    flat = jnp.concatenate([r.segments[0:1, j * 128 : j * 128 + 128] for j in range(4)] + [jnp.zeros((4, 128), jnp.int32)], axis=0)
    flat = mxu(flat.astype(jnp.float32).astype(jnp.bfloat16), apart).astype(jnp.int32)
    for j, (row, cols) in enumerate(((0, slice(0, 64)), (2, slice(0, 64)), (0, slice(64, 128)), (2, slice(64, 128)))):
        r.label[j : j + 1, :] = jnp.concatenate([flat[row : row + 1, cols], flat[row + 1 : row + 2, cols]], axis=1)
    r.label[4:8, :] = jnp.zeros((4, 128), jnp.int32)
    r.labels_all[place.blk] = r.label[...]
    await_all(met)
    halo = [
        remote(r.x.at[pl.ds(0, 16)], r.after, r.x_send.at[0], r.x_recv.at[0], peers[shards - 2]),
        remote(r.x.at[pl.ds(length - 16, 16)], r.before, r.x_send.at[1], r.x_recv.at[1], peers[0]),
    ]
    for copy in halo:
        copy.start()
    for step in [1, shards - 1] + list(range(2, shards - 1)):
        label_copy(step, place.blk).start()
    weights = [pltpu.make_async_copy(src, dst, r.w_sem.at[k]) for k, (src, dst) in enumerate(((r.wq_hbm, r.wq), (r.wk_hbm, r.wk), (r.wv_hbm, r.wv)))]
    for copy in weights:
        copy.start()
    work = RowForward(place, r)
    make_bias(work.table, core, r.near, (0,))
    left, right = label_come(1), label_come(shards - 1)
    taps = label_taps(place, r.label[...], left, right)
    for j in range(8):
        r.labels[j : j + 1, :] = taps[j]
    for copy in halo:
        copy.wait()
    load_bytes(r.x, r.before[14:16, :], r.after[0:2, :], r.xs)
    r.hidden[...], n1 = pool_tokens(scale, r.xs, taps, row_of(r.vectors, 0).astype(jnp.bfloat16), row_of(r.vectors, 1), tokens, r.y, r.share)
    r.n1[...] = n1
    for copy in weights:
        copy.wait()
    put_packed(mxu(n1, r.wq[...]).astype(jnp.bfloat16) * jnp.bfloat16(0.125), r.q)
    queries = Line(place, r.q, r.q_all, r.q_send, r.q_recv)
    queries.keep().start()
    queries.start()
    put_pairs(mxu(n1, r.wk[...]).astype(jnp.bfloat16), mxu(n1, r.wv[...]).astype(jnp.bfloat16), r.kv)

    def held(dz, off, core_off):
        rest = flipped(place.rest, 2) if off else place.rest
        rest = flipped(rest, 1) if core_off else rest
        start = pl.multiple_of(place.chunk((place.group + dz) % GROUPS, rest) * tokens, tokens)
        return r.kv_all.at[pl.ds(start, tokens)]

    def sem_of(dz, off, core_off):
        return r.kv_recv.at[(core_off * 2 + off) * GROUPS + dz]

    waits = []

    def send(src, dz, off, came, target):
        copy = remote(src, held(dz, off, 0), r.kv_send.at[len(waits)], sem_of(*came), target)
        copy.start()
        waits.append(copy)

    def arrived(dz, off, core_off=0):
        here = held(dz, off, core_off)
        remote(here, here, r.kv_send.at[0], sem_of(dz, off, core_off), core_to).wait_recv()

    def pass_on(dz, off):
        mine = dz == 0 and off == 0
        if not mine:
            arrived(dz, off)
        src = r.kv.at[place.group] if mine else held(dz, off, 0)
        if not off:
            send(src, dz, off, (dz, 1, 0), across)
        send(src, dz, off, (dz, off, 1), core_to)

    def along(step):
        copy = remote(r.kv.at[(place.group + step) % GROUPS], held(0, 0, 0), r.z_send.at[step], sem_of((GROUPS - step) % GROUPS, 0, 0), place.other_group(step))
        copy.start()
        return copy

    def line_of(block):
        return jnp.concatenate([block[0:1], block[1:2]], axis=1)

    def tile(dz, off):
        group = (place.group + dz) % GROUPS
        for c in range(2):
            number = place.chunk(group, (1 - y if off else y) * 2 + c)
            rows = pl.ds(pl.multiple_of(number * tokens, tokens), tokens)
            r.kl[rows, :] = label_features(line_of(r.labels_all[number]), True)
        arrived(dz, off, 1)
        work.tile(group * 2 + (1 - y if off else y))

    own = pltpu.make_async_copy(r.kv.at[place.group], held(0, 0, 0), r.own_sem)
    own.start()
    pass_on(0, 0)
    make_bias(work.table, core, r.near, (1,))
    work.clear()
    for step in range(2, shards - 1):
        label_copy(step, (place.blk + shards - step) % shards).wait_recv()
    for z in range(GROUPS):
        r.ql[z] = label_features(line_of(r.labels_all[place.chunk(z, place.rest)]), False) * jnp.bfloat16(NEG)
    pass_on(0, 1)
    for step in (1, 3, 2):
        queries.gone(step)
    first = [along(1), along(3)]
    queries.come_all()
    for z in range(GROUPS):
        work.queries(z)
    own.wait()
    tile(0, 0)
    tile(0, 1)
    for copy in first:
        copy.wait_send()
    last = along(2)
    pass_on(1, 0)
    pass_on(3, 0)
    tile(1, 0)
    pass_on(1, 1)
    pass_on(3, 1)
    tile(3, 0)
    tile(1, 1)
    pass_on(2, 0)
    tile(3, 1)
    pass_on(2, 1)
    tile(2, 0)
    tile(2, 1)
    last.wait_send()
    work.end()
    for copy in waits:
        copy.wait_send()
    for step in range(1, shards):
        label_copy(step, place.blk).wait_send()


def front(shards, scale, table, x, segments, vectors, wq, wk, wv):
    length, features = x.shape
    tokens, heads = length // 2, features // 64 // GROUPS
    width = heads * 128
    sem, f32, low = pltpu.SemaphoreType.DMA, jnp.float32, jnp.bfloat16
    mem = lambda shape, dtype=low: pltpu.VMEM(shape, dtype)
    packed = (GROUPS, tokens * 3 // 2, 128)
    ins = dict(
        table=Held(table, pltpu.SMEM), x=x, segments=segments, vectors=vectors,
        wq_hbm=Held(wq, pl.ANY), wk_hbm=Held(wk, pl.ANY), wv_hbm=Held(wv, pl.ANY),
    )
    outs = dict(
        q_all=(packed, low), kv_all=((shards * tokens, width), low), kl=((shards * tokens, 128), low), ql=((GROUPS, tokens, 128), low),
        near=((heads, 2, TK, TQ), low), o=(packed, low), keep=(packed, f32), lse=((GROUPS, heads, 1, TQ), f32),
        hidden=((tokens, features), f32), n1=((tokens, features), low), y=((8, tokens), f32), share=((1, 128), f32),
        labels=((8, tokens), jnp.int32), before=((16, features), low), after=((16, features), low),
    )
    scratch = dict(
        q=mem(packed), kv=mem((GROUPS, tokens, width)), xs=mem((features // 128, length + 2 * LEAD, 128), f32),
        wq=mem(wq.shape), wk=mem(wk.shape), wv=mem(wv.shape), label=mem((8, 128), jnp.int32), labels_all=mem((shards, 8, 128), jnp.int32),
        qp=mem((GROUPS, heads, TQ, 256)), acc=mem((GROUPS, heads, 80, TQ), f32), mx=mem((GROUPS, heads, 1, TQ), f32), vt=mem((heads, 80, TK)),
        q_send=sem((4,)), q_recv=sem((4,)), kv_send=sem((12,)), z_send=sem((GROUPS,)), kv_recv=sem((16,)), own_sem=sem,
        lab_send=sem((shards,)), lab_recv=sem((shards,)), x_send=sem((2,)), x_recv=sem((2,)), w_sem=sem((3,)),
    )
    return call(functools.partial(front_kernel, shards, scale), 7, ins, outs, scratch)


def middle_kernel(shards, r):
    place = Place(shards)
    met = hail([place.other_group(step) for step in (1, 2, 3)] + [place.other_rest(1)])
    pairs = ((r.wo_hbm, r.wo), (r.wg_hbm, r.wg), (r.wu_hbm, r.wu), (r.wd_hbm, r.wd))
    fetches = [pltpu.make_async_copy(src, dst, r.w_sem.at[k]) for k, (src, dst) in enumerate(pairs)]
    for copy in fetches:
        copy.start()
    await_all(met)
    home = Line(place, r.o, r.o_home, r.o_send, r.o_recv)
    home.keep().start()
    home.start()
    for copy in fetches:
        copy.wait()
    home.wait_all()
    r.gain[...] = row_of(r.vectors, 2)
    feed_kernel(r.o_home, r.hidden, r.ct, r.gain, r.wo, r.wg, r.wu, r.wd, r.block_out, r.dres, r.da, r.dgain,
                r.n2, r.att, r.act, r.dg, r.du, r.db, r.acc, r.dn2)
    away = Line(place, r.da, r.do, r.q_send, r.q_recv)
    away.keep().start()
    away.start()
    feed_weights(place, r.n2, r.att, r.act, r.dg, r.du, r.ct, r.db, r.sums,
                 r.core_send, r.core_recv, r.gate, r.up, r.down, r.out, r.wide_out, r.slim_out, r.wide_in, r.slim_in)
    away.wait_all()


def middle(shards, o_packed, hidden, ct, vectors, wo, wg, wu, wd):
    tokens, width = hidden.shape
    ff = wg.shape[1]
    per, per_ff = width // 32, ff // 32
    sem, low, f32 = pltpu.SemaphoreType.DMA, jnp.bfloat16, jnp.float32
    half = o_packed.shape[1:]
    wide_cols = ff + width // 2
    first = (wide_cols // 256 + 1) * 128
    ins = dict(o=o_packed, hidden=hidden, ct=ct, vectors=vectors, wo_hbm=Held(wo, pl.ANY), wg_hbm=Held(wg, pl.ANY), wu_hbm=Held(wu, pl.ANY), wd_hbm=Held(wd, pl.ANY))
    outs = dict(
        block_out=((tokens, width), low), dres=((tokens, width), f32), dgain=((1, width), f32), do=((GROUPS,) + half, low),
        sums=[((16, 2 * per, first), low), ((16, 2 * per, wide_cols - first), low), ((16, per_ff, width), low)],
    )
    mem = lambda shape, dtype=low: pltpu.VMEM(shape, dtype)
    scratch = dict(
        gain=mem((1, width), f32), o_home=mem((GROUPS,) + half), da=mem((GROUPS,) + half),
        n2=mem((tokens, width)), att=mem((tokens, width)), db=mem((tokens, width)),
        act=mem((tokens, ff)), dg=mem((tokens, ff)), du=mem((tokens, ff)),
        acc=mem((tokens, width), f32), dn2=mem((tokens, width), f32),
        wo=mem(wo.shape), wg=mem(wg.shape), wu=mem(wu.shape), wd=mem(wd.shape),
        gate=mem((width, ff), f32), up=mem((width, ff), f32), down=mem((ff, width), f32), out=mem((width, width), f32),
        wide_out=mem((16, 2 * per, wide_cols)), slim_out=mem((16, per_ff, width)),
        wide_in=mem((16, 2 * per, wide_cols)), slim_in=mem((16, per_ff, width)),
        w_sem=sem((4,)), o_send=sem((4,)), o_recv=sem((4,)), q_send=sem((4,)), q_recv=sem((4,)),
        core_send=sem((2,)), core_recv=sem((2,)),
    )
    return call(functools.partial(middle_kernel, shards), 8, ins, outs, scratch)


def neighbours(rows):
    peers = lax.axis_size("blk")
    up = [(i, i + 1) for i in range(peers - 1)]
    last, leading = rows
    return lax.ppermute(last, "blk", up), lax.ppermute(leading, "blk", [(j, i) for i, j in up])


def body(
    byte_embeds,
    segments,
    score_weight,
    norm_gain1,
    w_query,
    w_key,
    w_value,
    w_out,
    rel_bias,
    norm_gain2,
    w_gate,
    w_up,
    w_down,
    cotangent,
):
    row_count, length, width = byte_embeds.shape
    tokens = length // 2
    shards = lax.axis_size("blk")
    shape = {"dp": lax.axis_size("dp"), "blk": shards}
    devices = shards * shape["dp"]
    heads = rel_bias.shape[1] // GROUPS
    position = lax.axis_index("blk")
    rest_size = shards // GROUPS
    group, rest = position // rest_size, position % rest_size
    row = lax.axis_index("dp") % 2
    x, ids_here = byte_embeds[0], segments[0]

    ct = cotangent[0]
    scale = 1.0 / (row_count * length * devices)
    if devices == 32:
        vectors = jnp.concatenate([score_weight, norm_gain1, norm_gain2]).astype(jnp.float32).reshape(-1, 128)
        table = rel_bias.T.astype(jnp.float32)
        got = front(shards, scale, table, x, segments, vectors, w_query, w_key, w_value)
        mid = middle(shards, got.o, got.hidden, ct, vectors, w_out, w_gate, w_up, w_down)
        block_out, d_res, d_gain2 = mid.block_out, mid.dres, mid.dgain
        last = back_and_last(
            shape,
            mid.sums,
            dict(
                table=Held(table, pltpu.SMEM), q=got.q_all, do=mid.do, keep=got.keep, kv_hbm=Held(got.kv_all, pl.ANY),
                kl_hbm=Held(got.kl, pl.ANY), ql=got.ql, bias=got.near, lse=got.lse,
                hidden_hbm=Held(got.hidden, pl.ANY), dres_hbm=Held(d_res, pl.ANY), n1_hbm=Held(got.n1, pl.ANY), x_hbm=Held(x, pl.ANY), before=got.before, after=got.after,
                labels=got.labels, y=got.y, vectors=vectors,
                wq_hbm=Held(w_query, pl.ANY), wk_hbm=Held(w_key, pl.ANY), wv_hbm=Held(w_value, pl.ANY), dgain2=d_gain2, share=got.share,
            ),
        )
        grad_bytes, edge, spill, small, sums = last.gb, last.edge, last.spill_out, last.small_out, last.sums
    else:
        marks = (ids_here + 1).astype(jnp.bfloat16)
        with_marks = lambda part, two: jnp.concatenate([part, jnp.pad(two, (0, width - 2))[None]], axis=0)
        before, after = neighbours((with_marks(x[-2:], marks[-2:]), with_marks(x[:2], marks[:2])))
        line = jnp.concatenate([before[2, :2], marks, after[2, :2]])
        line = jnp.pad(line, (1, 1)).astype(jnp.int32).reshape(tokens + 3, 2).T
        labels = jnp.stack([line[j % 2, j // 2 : j // 2 + tokens] for j in range(8)])

        score_row, gain1, gain2 = score_weight[None], norm_gain1[None], norm_gain2[None]
        hidden, n1, y, share, q_packed, kv_parts = pool_and_project(
            shards, scale, x, before, after, labels, score_row, gain1, w_query, w_key, w_value
        )

        label_block = jnp.pad(ids_here[0::2].reshape(tokens // 128, 128), ((0, 8 - tokens // 128), (0, 0)), constant_values=-1)
        table = lax.dynamic_slice_in_dim(rel_bias.astype(jnp.float32).T, group * heads, heads, 0)
        q_all, kv_all, labels_all = gather_all(shards, q_packed, kv_parts, label_block)
        labels_all = labels_all.reshape(2, shards, 8, 128)[:, :, : tokens // 128].reshape(2, shards * tokens)
        ids = jnp.arange(8, dtype=jnp.int32)
        counts = jnp.sum((labels_all[:, None, :] == ids[None, :, None]).astype(jnp.int32), axis=2)
        ends = jnp.sum(jnp.where(ids[None, :] <= ids[:, None], counts[:, None, :], 0), axis=2)
        begins = ends - counts
        query_labels = jnp.stack(
            [lax.dynamic_slice_in_dim(labels_all, ((2 * row + i) * rest_size + rest) * tokens, tokens, 1) for i in range(2)],
            axis=1,
        )
        chosen = query_labels[:, :, None, :] == ids[None, None, :, None]
        span = jnp.stack(
            [jnp.sum(jnp.where(chosen, edge[:, None, :, None], 0), axis=2) for edge in (begins, ends)], axis=2
        )
        parity = rest % 2
        firsts = jnp.stack([((2 * row + i) * rest_size + rest) * tokens for i in range(2)])
        near = jnp.broadcast_to((firsts // TK - 1 + parity)[None], (2, 2))
        bounds = jnp.stack(
            [
                jnp.min(span[:, :, 0], axis=-1) // TK,
                -(-jnp.max(span[:, :, 1], axis=-1) // TK),
                near,
                -(-jnp.max(span[:, :, 0], axis=-1) // TK),
                jnp.min(span[:, :, 1], axis=-1) // TK,
                jnp.broadcast_to(parity, (2, 2)),
                jnp.broadcast_to((labels_all[0, -1] > 0).astype(jnp.int32), (2, 2)),
            ],
            axis=-1,
        ).astype(jnp.int32)
        o_packed, o_kept, log_total, near_bias = attention(bounds, table, q_all, kv_all, span)
        o_home = move_heads(return_kernel, (GROUPS,), shards, 4, o_packed)
        block_out, d_res, da_packed, d_gain2, n2, att, act, d_gate, d_up, d_branch = feed_forward(
            o_home, hidden, ct, gain2, w_out, w_gate, w_up, w_down
        )
        do_all = move_heads(spread_kernel, (2, 2), shards, 5, da_packed)
        dq_packed, dkv_all, _, _, _, d_table_lanes = attention_back(
            False, bounds, table, q_all, do_all, o_kept, kv_all, near_bias, span, log_total
        )
        dq_home, dkv_home = reduce_all(shape, dq_packed, dkv_all, [], [])
        grad_bytes, edge, spill, small, last_parts = last_part(
            shape, dq_home, dkv_home, hidden, d_res, x, before, after, labels, y,
            score_row, gain1, w_query, w_key, w_value, d_gain2, share, d_table_lanes,
        )
        sums = []
    per = width // devices
    block_out, grad_bytes, g_score, g_gain1, g_gain2, g_bias, shares, *grads = finish(
        shards, rel_bias.shape[1], per, w_gate.shape[1], block_out, grad_bytes, edge, spill, small, sums
    )
    if devices != 32:
        product = lambda left, right: jnp.einsum("td,te->de", left, right, preferred_element_type=jnp.float32)
        grads = [product(n1, last_parts[j]) for j in range(3)]
        grads += [product(att, d_branch), product(n2, d_gate), product(n2, d_up), product(act, ct)]
        grads = [lax.psum_scatter(grad, ("dp", "blk"), scatter_dimension=0, tiled=True) for grad in grads]
    return (
        block_out[None],
        grad_bytes[None],
        g_score,
        g_gain1,
        *grads[:4],
        g_bias.T,
        g_gain2,
        *grads[4:],
        shares,
    )


def solution(mesh):
    placed = (
        P("dp", "blk", None),
        P("dp", "blk"),
        P(),
        P(),
        P(),
        P(),
        P(),
        P(),
        P(),
        P(),
        P(),
        P(),
        P(),
        P("dp", "blk", None),
    )
    return jax.shard_map(
        body,
        mesh=mesh,
        in_specs=placed,
        out_specs=(
            P("dp", "blk", None),
            P("dp", "blk", None),
            P(),
            P(),
            P(("dp", "blk"), None),
            P(("dp", "blk"), None),
            P(("dp", "blk"), None),
            P(("dp", "blk"), None),
            P(),
            P(),
            P(("dp", "blk"), None),
            P(("dp", "blk"), None),
            P(("dp", "blk"), None),
            P(),
        ),
        check_vma=False,
    )
```

```python
import functools
import math

import jax
import jax.numpy as jnp
from jax import lax
from jax.experimental import pallas as pl
from jax.experimental.pallas import tpu as pltpu
from jax.sharding import PartitionSpec as P

BUCKETS = 32
MAX_BLOCK = 4
VMEM_BYTES = 61 * 2**20


def buckets_of(relative):
    distance = jnp.abs(relative)
    beyond = jnp.zeros_like(distance)
    for border in (12, 16, 23, 32, 46, 64, 91):
        beyond = beyond + (distance >= border).astype(jnp.int32)
    nearer = jnp.where(distance < 8, distance, 8 + beyond)
    return nearer + BUCKETS // 2 * (relative > 0).astype(jnp.int32)


MESH_ID = pl.DeviceIdType.MESH
GROUPS = 4


def bits_of(size):
    return [1 << p for p in reversed(range(size.bit_length() - 1))]


def bit(value, mask):
    return (value // mask) % 2


def flipped(value, mask):
    return value + mask * (1 - 2 * bit(value, mask))


class Place:
    def __init__(self, shards):
        self.shards = shards
        self.rest_size = shards // GROUPS
        self.dp = lax.axis_index("dp")
        self.blk = lax.axis_index("blk")
        self.row = self.dp % 2
        self.group = self.blk // self.rest_size
        self.rest = self.blk % self.rest_size

    def at(self, row, group, rest):
        return (self.dp - self.row + row, group * self.rest_size + rest)

    def chunk(self, group, rest):
        return group * self.rest_size + rest

    def other_row(self):
        return self.at(1 - self.row, self.group, self.rest)

    def other_rest(self, mask):
        return self.at(self.row, self.group, flipped(self.rest, mask))

    def other_group(self, step):
        return self.at(self.row, (self.group + step) % GROUPS, self.rest)


def hail(targets):
    barrier = pltpu.get_barrier_semaphore()
    for target in targets:
        pl.semaphore_signal(barrier, inc=1, device_id=target, device_id_type=MESH_ID)
    return len(targets)


def await_all(count):
    pl.semaphore_wait(pltpu.get_barrier_semaphore(), count)


def greet(targets):
    await_all(hail(targets))


def remote(src, dst, send_sem, recv_sem, target):
    return pltpu.make_async_remote_copy(
        src_ref=src,
        dst_ref=dst,
        send_sem=send_sem,
        recv_sem=recv_sem,
        device_id=target,
        device_id_type=MESH_ID,
    )


def line_and_row(place):
    found = []
    for step in range(GROUPS):
        for flip in range(2):
            if step or flip:
                row = 1 - place.row if flip else place.row
                found.append(place.at(row, (place.group + step) % GROUPS, place.rest))
    return found


def spread_heads(place, q_ref, out_ref, send_sem, recv_sem):
    row_to = place.group // 2
    slot = place.group % 2
    dst = out_ref.at[place.row, slot]
    mine = recv_sem.at[place.row * 2 + slot]
    at_home = row_to == place.row
    for step in range(GROUPS):
        group = (place.group + step) % GROUPS
        src = q_ref.at[group]
        copy = remote(src, dst, send_sem.at[step], mine, place.at(row_to, group, place.rest))
        if step:
            copy.start()
        else:
            pl.when(jnp.logical_not(at_home))(copy.start)
            pl.when(at_home)(pltpu.make_async_copy(src, dst, mine).start)


def spread_heads_come(q_ref, out_ref, recv_sem):
    for row in range(2):
        for slot in range(2):
            pltpu.make_async_copy(q_ref.at[0], out_ref.at[row, slot], recv_sem.at[row * 2 + slot]).wait()


def spread_heads_gone(place, q_ref, out_ref, send_sem, recv_sem):
    at_home = place.group // 2 == place.row
    for step in range(GROUPS):
        copy = remote(q_ref.at[0], out_ref.at[0, 0], send_sem.at[step], recv_sem.at[0], place.other_row())
        if step:
            copy.wait_send()
        else:
            pl.when(jnp.logical_not(at_home))(copy.wait_send)


def spread_heads_wait(place, q_ref, out_ref, send_sem, recv_sem):
    spread_heads_come(q_ref, out_ref, recv_sem)
    spread_heads_gone(place, q_ref, out_ref, send_sem, recv_sem)


def return_heads(place, o_ref, out_ref, send_sem, recv_sem):
    for row in range(2):
        for slot in range(2):
            group = place.row * 2 + slot
            src = o_ref.at[row, slot]
            dst = out_ref.at[place.group]
            mine = recv_sem.at[place.group]
            at_home = jnp.logical_and(place.row == row, place.group == group)
            copy = remote(src, dst, send_sem.at[row * 2 + slot], mine, place.at(row, group, place.rest))
            pl.when(jnp.logical_not(at_home))(copy.start)
            pl.when(at_home)(pltpu.make_async_copy(src, dst, mine).start)


def return_heads_wait(place, o_ref, out_ref, send_sem, recv_sem):
    for group in range(GROUPS):
        pltpu.make_async_copy(o_ref.at[0, 0], out_ref.at[group], recv_sem.at[group]).wait()
    for row in range(2):
        for slot in range(2):
            group = place.row * 2 + slot
            at_home = jnp.logical_and(place.row == row, place.group == group)
            copy = remote(o_ref.at[0, 0], out_ref.at[0], send_sem.at[row * 2 + slot], recv_sem.at[0], place.other_row())
            pl.when(jnp.logical_not(at_home))(copy.wait_send)


def spread_kernel(shards, q_ref, out_ref, send_sem, recv_sem):
    place = Place(shards)
    greet(line_and_row(place))
    spread_heads(place, q_ref, out_ref, send_sem, recv_sem)
    spread_heads_wait(place, q_ref, out_ref, send_sem, recv_sem)


def return_kernel(shards, o_ref, out_ref, send_sem, recv_sem):
    place = Place(shards)
    greet(line_and_row(place))
    return_heads(place, o_ref, out_ref, send_sem, recv_sem)
    return_heads_wait(place, o_ref, out_ref, send_sem, recv_sem)


SMEM_SPEC = pl.BlockSpec(memory_space=pltpu.SMEM)
VMEM_SPEC = pl.BlockSpec(memory_space=pltpu.VMEM)
ANY_SPEC = pl.BlockSpec(memory_space=pl.ANY)


def move_heads(kernel, lead, shards, ident, packed):
    rows, lanes = packed.shape[-2:]
    return pl.pallas_call(
        functools.partial(kernel, shards),
        out_shape=jax.ShapeDtypeStruct(lead + (rows, lanes), packed.dtype),
        in_specs=[pl.BlockSpec(memory_space=pltpu.VMEM)],
        out_specs=pl.BlockSpec(memory_space=pltpu.VMEM),
        scratch_shapes=[pltpu.SemaphoreType.DMA((4,)), pltpu.SemaphoreType.DMA((4,))],
        compiler_params=pltpu.CompilerParams(collective_id=ident, has_side_effects=True, vmem_limit_bytes=VMEM_BYTES),
        name="move_heads_%d" % ident,
    )(packed)


def gather_kernel(shards, q_ref, kv_ref, label_ref, qo_ref, kvo_ref, labo_ref, q_send, q_recv, z_send, far_send, core_send, kv_recv, own_sem, lab_send, lab_recv):
    place = Place(shards)
    tokens = kv_ref.shape[1]
    rest_bits = bits_of(place.rest_size)
    core, far = rest_bits[-1], ["row"] + rest_bits[:-1]
    greet(line_and_row(place) + [place.other_rest(mask) for mask in rest_bits])

    dims = [("row", 1)] + [("blk", m) for m in bits_of(shards)]
    lab_index = [place.row] + [bit(place.blk, m) for _, m in dims[1:]]
    lab_order = list(range(len(dims)))

    def lab_copy(stage):
        index = tuple(slice(None) if p in lab_order[:stage] else lab_index[p] for p in range(len(dims)))
        axis, mask = dims[lab_order[stage]]
        target = place.other_row() if axis == "row" else (place.dp, flipped(place.blk, mask))
        there = labo_ref.at[index]
        return remote(there, there, lab_send.at[stage], lab_recv.at[stage], target)

    labo_ref[tuple(lab_index)] = label_ref[...]
    lab_copy(0).start()
    lab_stage = 0

    def slot(row, group, rest):
        start = pl.multiple_of(place.chunk(group, rest) * tokens, tokens)
        return kvo_ref.at[row, pl.ds(start, tokens)]

    def held(dz, offset, core_off):
        row = 1 - place.row if offset & 1 else place.row
        rest = place.rest
        for p, mask in enumerate(far[1:]):
            if offset >> (p + 1) & 1:
                rest = flipped(rest, mask)
        if core_off:
            rest = flipped(rest, core)
        return slot(row, (place.group + dz) % GROUPS, rest)

    count = 1 << len(far)

    def sem_of(dz, offset, core_off):
        return kv_recv.at[(core_off * count + offset) * GROUPS + dz]

    own = pltpu.make_async_copy(kv_ref.at[place.group], held(0, 0, 0), own_sem)
    own.start()
    waits = []
    for step in (1, 3, 2):
        copy = remote(kv_ref.at[(place.group + step) % GROUPS], held(0, 0, 0), z_send.at[step], sem_of((GROUPS - step) % GROUPS, 0, 0), place.other_group(step))
        copy.start()
        waits.append(copy)

    used = 0
    events = sorted(((dz, off) for dz in range(GROUPS) for off in range(count)), key=lambda e: (bin(e[1]).count("1"), (0, 1, 3, 2).index(e[0])))
    core_target = place.other_rest(core)
    for step, (dz, off) in enumerate(events):
        if step == GROUPS:
            spread_heads(place, q_ref, qo_ref, q_send, q_recv)
        here = held(dz, off, 0)
        if dz == 0 and off == 0:
            src = kv_ref.at[place.group]
        else:
            remote(here, here, z_send.at[0], sem_of(dz, off, 0), core_target).wait_recv()
            src = here
        order = [(p + dz) % len(far) for p in range(len(far))]
        last = max([order.index(p) for p in range(len(far)) if off >> p & 1], default=-1)
        for p in order[last + 1 :]:
            target = place.other_row() if p == 0 else place.other_rest(far[p])
            copy = remote(src, here, far_send.at[used], sem_of(dz, off | 1 << p, 0), target)
            copy.start()
            waits.append(copy)
            used += 1
        copy = remote(src, here, core_send.at[off * GROUPS + dz], sem_of(dz, off, 1), core_target)
        copy.start()
        waits.append(copy)
        if lab_stage < len(dims):
            lab_copy(lab_stage).wait()
            lab_stage += 1
            if lab_stage < len(dims):
                lab_copy(lab_stage).start()
    for dz, off in events:
        here = held(dz, off, 1)
        remote(here, here, z_send.at[0], sem_of(dz, off, 1), core_target).wait_recv()
    own.wait()
    for copy in waits:
        copy.wait_send()
    spread_heads_wait(place, q_ref, qo_ref, q_send, q_recv)


def gather_all(shards, q_packed, kv_parts, labels):
    tokens, width = kv_parts.shape[1:]
    far = 1 + len(bits_of(shards // GROUPS)) - 1
    count = 1 << far
    nbits = 1 + len(bits_of(shards))
    sem = pltpu.SemaphoreType.DMA
    return pl.pallas_call(
        functools.partial(gather_kernel, shards),
        out_shape=(
            jax.ShapeDtypeStruct((2, 2) + q_packed.shape[1:], q_packed.dtype),
            jax.ShapeDtypeStruct((2, shards * tokens, width), kv_parts.dtype),
            jax.ShapeDtypeStruct((2,) * nbits + labels.shape, labels.dtype),
        ),
        in_specs=[pl.BlockSpec(memory_space=pltpu.VMEM)] * 3,
        out_specs=(pl.BlockSpec(memory_space=pltpu.VMEM),) * 3,
        scratch_shapes=[
            sem((4,)), sem((4,)), sem((GROUPS,)), sem((GROUPS * (count - 1),)), sem((GROUPS * count,)), sem((GROUPS * count * 2,)),
            sem, sem((nbits,)), sem((nbits,)),
        ],
        compiler_params=pltpu.CompilerParams(collective_id=1, has_side_effects=True, vmem_limit_bytes=VMEM_BYTES),
        name="gather_keys",
    )(q_packed, kv_parts, labels)


def add_blocks(dst_ref, src_ref, index, shape):
    lead = shape[:-2]
    total = math.prod(lead)

    def one(step, _):
        place, left = [], step
        for size in reversed(lead):
            place.append(left % size)
            left = left // size
        place = tuple(reversed(place))
        full, k = [], 0
        for entry in index:
            if entry is None:
                full.append(place[k])
                k += 1
            else:
                full.append(entry)
        dst_ref[place] = dst_ref[place] + src_ref[tuple(full)]
        return 0

    lax.fori_loop(0, total, one, 0)


class Stream:
    def __init__(self, axes, at, kept, order, src, half, bufs, out, send_sem, recv_sem):
        self.axes, self.at, self.kept, self.order = axes, at, kept, order
        self.half = half
        self.src, self.bufs, self.out = src, bufs, out
        self.send_sem, self.recv_sem = send_sem, recv_sem

    def own(self, p):
        axis, mask = self.axes[p]
        return bit(self.at[axis], mask)

    def target(self, p):
        axis, mask = self.axes[p]
        moved = dict(self.at)
        moved[axis] = flipped(self.at[axis], mask)
        return (moved["dp"], moved["blk"])

    def stage(self, k):
        kept = [p for p in self.kept if p not in self.order[:k]]
        return kept, self.src if k == 0 else self.bufs[k - 1], self.order[k]

    def copy(self, k):
        kept, src, now = self.stage(k)
        index = tuple(1 - self.own(p) if p == now else slice(None) for p in kept)
        return remote(src.at[index], self.bufs[k], self.send_sem.at[k], self.recv_sem.at[k], self.target(now))

    def absorb(self, k):
        kept, src, now = self.stage(k)
        buf = self.bufs[k]
        if k == len(self.order) - 1 and self.out is not None:
            mine = src[self.own(now)].astype(jnp.float32)
            self.out[...] = buf[...].astype(jnp.float32) + mine
        else:
            half = k == 0 and self.half is not None
            index = tuple(self.own(p) if p == now else None for p in kept if p != now or not half)
            add_blocks(buf, self.half if half else src, index, buf.shape)


class Whole:
    def __init__(self, axes, at, order, src, bufs, out, send_sem, recv_sem):
        self.stream = Stream(axes, at, order, order, src, None, bufs, out, send_sem, recv_sem)
        self.order, self.src, self.bufs, self.out = order, src, bufs, out

    def held(self, k):
        return self.src if k == 0 else self.bufs.at[1, k - 1]

    def copy(self, k):
        s = self.stream
        return remote(self.held(k), self.bufs.at[0, k], s.send_sem.at[k], s.recv_sem.at[k], s.target(self.order[k]))

    def absorb(self, k):
        total = self.held(k)[...] + self.bufs[0, k]
        if k == len(self.order) - 1:
            self.out[...] = total
        else:
            self.bufs[1, k] = total


def advance(stream, stage):
    if stage < len(stream.order):
        stream.copy(stage).wait()
        stream.absorb(stage)
        if stage < len(stream.order) - 1:
            stream.copy(stage + 1).start()


def bit_axes(shape):
    return [("dp", m) for m in bits_of(shape["dp"])] + [("blk", m) for m in bits_of(shape["blk"])]


def stream_scratch(lead, order, rows, cols):
    return [pltpu.VMEM((2,) * (lead - 1 - k) + (rows, cols), jnp.bfloat16) for k in range(len(order))]


def feed_weights(place, n2_ref, att_ref, act_ref, dg_ref, du_ref, ct_ref, db_ref, sums,
                 core_send, core_recv, gate, up, down, out, wide_out, slim_out, wide_in, slim_in):
    core_target = place.other_rest(1)
    per = gate.shape[0] // 32
    per_ff = down.shape[0] // 32
    first = sums[0].shape[2]
    half = out.shape[1] // 2
    core = place.rest % 2

    n2_t = n2_ref[...].T
    step = 512
    for j in range(gate.shape[1] // step):
        cols = slice(j * step, j * step + step)
        gate[:, cols] = mxu(n2_t, dg_ref[:, cols])
        up[:, cols] = mxu(n2_t, du_ref[:, cols])
    out[...] = mxu(att_ref[...].T, db_ref[...])

    def wide_rows(block):
        rows = pl.ds(pl.multiple_of(block * per, 8), per)
        last = jnp.concatenate([out[rows, :half], out[rows, half:]], axis=0)
        return jnp.concatenate([jnp.concatenate([gate[rows, :], up[rows, :]], axis=0), last], axis=1)

    def slim_rows(block):
        return down[pl.ds(pl.multiple_of(block * per_ff, 8), per_ff), :]

    def send_wide(m, _):
        wide_out[m] = wide_rows(2 * m + 1 - core).astype(jnp.bfloat16)
        return 0

    lax.fori_loop(0, 16, send_wide, 0)
    wide_copy = remote(wide_out, wide_in, core_send.at[0], core_recv.at[0], core_target)
    wide_copy.start()
    for j in range(down.shape[0] // step):
        rows = slice(j * step, j * step + step)
        down[rows, :] = mxu(act_ref[:, rows].T, ct_ref[...])

    def send_slim(m, _):
        slim_out[m] = slim_rows(2 * m + 1 - core).astype(jnp.bfloat16)
        return 0

    lax.fori_loop(0, 16, send_slim, 0)
    slim_copy = remote(slim_out, slim_in, core_send.at[1], core_recv.at[1], core_target)
    slim_copy.start()

    wide_copy.wait()

    def sum_wide(m, _):
        total = wide_rows(2 * m + core) + wide_in[m].astype(jnp.float32)
        sums[0][m] = total[:, :first].astype(jnp.bfloat16)
        sums[1][m] = total[:, first:].astype(jnp.bfloat16)
        return 0

    lax.fori_loop(0, 16, sum_wide, 0)
    slim_copy.wait()

    def sum_slim(m, _):
        sums[2][m] = (slim_rows(2 * m + core) + slim_in[m].astype(jnp.float32)).astype(jnp.bfloat16)
        return 0

    lax.fori_loop(0, 16, sum_slim, 0)


def reduce_kernel(shards, axes, orders, *refs):
    count = len(orders)
    q_ref, kv_ref = refs[:2]
    pairs = refs[2 : 2 + 2 * count]
    qo_ref, kvo_ref = refs[2 + 2 * count : 4 + 2 * count]
    sums = refs[4 + 2 * count : 4 + 3 * count]
    q_send, q_recv, send_sem, recv_sem, z_send, z_recv, w_send, w_recv = refs[4 + 3 * count : 12 + 3 * count]
    bufs = refs[12 + 3 * count :]
    place = Place(shards)
    rest_bits = bits_of(place.rest_size)
    greet(line_and_row(place) + [place.other_rest(mask) for mask in rest_bits])
    return_heads(place, q_ref, qo_ref, q_send, q_recv)
    ndim = 1 + len(rest_bits)
    at = {"dp": place.dp, "blk": place.blk}
    streams, used = [], ndim
    for s, (kept, order) in enumerate(orders):
        src, more = bufs[used], bufs[used + 1 : used + 1 + len(order)]
        used += 1 + len(order)
        streams.append(Stream(axes, at, kept, order, src, more, sums[s], w_send.at[s], w_recv.at[s]))
    own = [place.row] + [bit(place.rest, m) for m in rest_bits]
    targets = [place.other_row()] + [place.other_rest(m) for m in rest_bits]
    state = {}

    def plan(group_step):
        far = list(range(ndim - 1))
        turn = group_step % len(far)
        return [ndim - 1] + far[turn:] + far[:turn]

    def copy_of(step, stage):
        order = plan(step)
        group = (place.group + step) % GROUPS
        done = order[:stage]
        p_now = order[stage]
        buf = bufs[stage].at[step]
        if stage == 0:
            index = (p_index(group, done, p_now))
            src = kv_ref.at[index]
        else:
            kept = [p for p in range(ndim) if p not in done]
            src = bufs[stage - 1].at[(step,) + tuple(1 - own[p] if p == p_now else slice(None) for p in kept)]
        return remote(src, buf, send_sem.at[stage, step], recv_sem.at[stage, step], targets[p_now])

    def p_index(group, done, p_now):
        index = [slice(None)] * ndim
        index[p_now] = 1 - own[p_now]
        return (index[0], group) + tuple(index[1:])

    def absorb(step, stage):
        order = plan(step)
        done, p_now = order[:stage], order[stage]
        buf = bufs[stage].at[step]
        group = (place.group + step) % GROUPS
        if stage == 0:
            index = [None] * ndim
            index[p_now] = own[p_now]
            add_blocks(buf, kv_ref, (index[0], group) + tuple(index[1:]), buf.shape)
        else:
            kept = [p for p in range(ndim) if p not in done]
            index = tuple(own[p] if p == p_now else None for p in kept)
            add_blocks(buf, bufs[stage - 1].at[step], index, buf.shape)

    steps = (2, 1, 3, 0)
    for step in steps:
        copy_of(step, 0).start()
    for s, stream in enumerate(streams):
        add_two(stream.src, pairs[2 * s], pairs[2 * s + 1])
        stream.copy(0).start()
    for stage in range(ndim):
        for step in steps:
            copy_of(step, stage).wait()
            absorb(step, stage)
            if stage < ndim - 1:
                copy_of(step, stage + 1).start()
            elif step:
                remote(bufs[stage].at[step], kvo_ref.at[place.group], z_send.at[step], z_recv.at[(GROUPS - step) % GROUPS], place.other_group(step)).start()
            else:
                kvo_ref[place.group] = bufs[stage][step]
        for stream in streams:
            if stage < len(stream.order):
                stream.copy(stage).wait()
                stream.absorb(stage)
                if stage < len(stream.order) - 1:
                    stream.copy(stage + 1).start()
    for step in (1, 3, 2):
        there = kvo_ref.at[(place.group + step) % GROUPS]
        remote(bufs[ndim - 1].at[step], there, z_send.at[step], z_recv.at[step], place.other_group(step)).wait()
    return_heads_wait(place, q_ref, qo_ref, q_send, q_recv)


def add_two(dst_ref, one_ref, two_ref):
    lead = dst_ref.shape[:-2]

    def one(step, _):
        place, left = [], step
        for size in reversed(lead):
            place.append(left % size)
            left = left // size
        place = tuple(reversed(place))
        dst_ref[place] = (one_ref[place].astype(jnp.float32) + two_ref[place].astype(jnp.float32)).astype(dst_ref.dtype)
        return 0

    lax.fori_loop(0, math.prod(lead), one, 0)


def reduce_all(shape, q_packed, kv_sums, orders, pairs):
    shards = shape["blk"]
    tokens_all, width = kv_sums.shape[1:]
    tokens = tokens_all // shards
    rest_bits = bits_of(shards // GROUPS)
    ndim = 1 + len(rest_bits)
    sem = pltpu.SemaphoreType.DMA
    scratch = [pltpu.VMEM((GROUPS,) + (2,) * (ndim - 1 - s) + (tokens, width), kv_sums.dtype) for s in range(ndim)]
    flat, sums = [], []
    for (kept, order), pair in zip(orders, pairs):
        rows, cols = pair[0].shape[-2:]
        flat += [part.reshape((2,) * len(kept) + (rows, cols)) for part in pair]
        sums.append(jax.ShapeDtypeStruct((rows, cols), jnp.float32))
        scratch.append(pltpu.VMEM((2,) * len(kept) + (rows, cols), jnp.bfloat16))
        scratch += stream_scratch(len(kept), order, rows, cols)
    stages = max([len(order) for _, order in orders], default=1)
    return pl.pallas_call(
        functools.partial(reduce_kernel, shards, bit_axes(shape), orders),
        out_shape=(
            jax.ShapeDtypeStruct((GROUPS,) + q_packed.shape[2:], q_packed.dtype),
            jax.ShapeDtypeStruct((GROUPS, tokens, width), kv_sums.dtype),
        ) + tuple(sums),
        in_specs=[VMEM_SPEC] * (2 + len(flat)),
        out_specs=(VMEM_SPEC,) * (2 + len(sums)),
        scratch_shapes=[sem((4,)), sem((4,)), sem((ndim, GROUPS)), sem((ndim, GROUPS)), sem((GROUPS,)), sem((GROUPS,)),
                        sem((max(len(orders), 1), stages)), sem((max(len(orders), 1), stages))] + scratch,
        compiler_params=pltpu.CompilerParams(collective_id=2, has_side_effects=True, vmem_limit_bytes=VMEM_BYTES),
        name="reduce_keys",
    )(q_packed, kv_sums.reshape((2, GROUPS) + (2,) * len(rest_bits) + (tokens, width)), *flat)


TQ = 256
TK = 512
NEAR_ROWS = 448
NEG = -1e30
FIRST_MAX = -1e29
NT = (((1,), (1,)), ((), ()))
NN = (((1,), (0,)), ((), ()))
BORDERS = (12, 16, 23, 32, 46, 64, 91)


def mxu(left, right, dims=NN):
    return lax.dot_general(left, right, dims, preferred_element_type=jnp.float32)


def turned(tile):
    return jnp.concatenate([tile[:, 64:], tile[:, :64]], axis=1)


def spread_lanes(packed, high):
    lane = lax.broadcasted_iota(jnp.int32, (1, 128), 1)
    keep = lane >= 64 if high else lane < 64
    zero = jnp.zeros((), packed.dtype)
    pair, last = packed[0:TQ], packed[TQ:]
    pick = lambda tile: jnp.where(keep, tile, zero)
    if high:
        return [pick(turned(pair)), pick(pair), jnp.concatenate([pick(turned(last)), pick(last)], axis=0)]
    return [pick(pair), pick(turned(pair)), jnp.concatenate([pick(last), pick(turned(last))], axis=0)]


def join_heads(parts):
    half = TQ // 2
    top = jnp.concatenate([parts[0], parts[1]], axis=1)
    low = jnp.concatenate([parts[2][:half], parts[2][half:]], axis=1)
    return jnp.concatenate([top, low], axis=0)


def valid_mask(se_ref, r, i, k0):
    kpos = k0 + lax.broadcasted_iota(jnp.int32, (TK, TQ), 0)
    return jnp.logical_and(kpos >= se_ref[r, i, 0:1, :], kpos < se_ref[r, i, 1:2, :])


def near_buckets(first, rows, parity):
    relative = (
        first - TK + TQ * parity
        + lax.broadcasted_iota(jnp.int32, (rows, TQ), 0)
        - lax.broadcasted_iota(jnp.int32, (rows, TQ), 1)
    )
    return buckets_of(relative)


def make_bias(table, parity, near_ref, tiles=(0, 1)):
    heads = near_ref.shape[0]
    for tile in tiles:
        def rows(step, _):
            start = pl.multiple_of(step * 32, 32)
            place = tile * TK + start
            after = place - near_start(parity)
            inside = jnp.logical_and(after >= 0, after < NEAR_ROWS)

            @pl.when(inside)
            def _():
                which = near_buckets(place, 32, parity)
                for h in range(heads):
                    value = jnp.zeros((32, TQ), jnp.float32)
                    for b in range(BUCKETS):
                        value = jnp.where(which == b, table[h, b], value)
                    near_ref[h, tile, pl.ds(start, 32)] = value.astype(jnp.bfloat16)

            @pl.when(jnp.logical_not(inside))
            def _():
                for h in range(heads):
                    value = jnp.where(after < 0, table[h, 15], table[h, 31])
                    near_ref[h, tile, pl.ds(start, 32)] = jnp.full((32, TQ), value, jnp.float32).astype(jnp.bfloat16)

            return 0
        lax.fori_loop(0, TK // 32, rows, 0)


def tile_kind(bounds, r, i, t):
    slot = jnp.clip(t - bounds[r, i, 2] + 1, 0, 3)
    away = jnp.logical_or(slot == 0, slot == 3)
    inside = jnp.logical_and(t >= bounds[r, i, 3], t < bounds[r, i, 4])
    return slot, jnp.logical_and(away, inside)


def fwd_kernel(alone, bounds, table, q_ref, kv_hbm, se_ref, *refs):
    if alone:
        near_ref, o_in, keep_in, lse_in, o_ref, keep_ref, lse_ref, vt, acc, mx, qp, kv_ref, kv_sem = refs
    else:
        o_ref, keep_ref, lse_ref, near_ref, vt, acc, mx, qp, kv_ref, kv_sem = refs
        make_bias(table, bounds[0, 0, 5], near_ref)
    heads = lse_ref.shape[2]
    base = 1 - bounds[0, 0, 6] if alone else 0

    def row_body(at, _):
        r = base + at
        lo_all = jnp.minimum(bounds[r, 0, 0], bounds[r, 1, 0])
        hi_all = jnp.maximum(bounds[r, 0, 1], bounds[r, 1, 1])

        def fetch(t):
            rows = pl.ds(pl.multiple_of(t * TK, TK), TK)
            return pltpu.make_async_copy(kv_hbm.at[r, rows], kv_ref.at[rows], kv_sem.at[t])

        def begin(t, _):
            fetch(t).start()
            return 0

        lax.fori_loop(lo_all, hi_all, begin, 0)
        for i in range(2):
            for h, tile in enumerate(spread_lanes(q_ref[r, i], False)):
                qp[i, h] = tile

        def turn(t, _):
            fetch(t).wait()
            k0 = pl.multiple_of(t * TK, TK)
            for h in range(heads):
                tile = kv_ref[pl.ds(k0, TK), h * 128 : h * 128 + 128]
                vt[h, 0:64, pl.ds(k0, TK)] = tile.T[64:128, :]
                vt[h, 64:80, pl.ds(k0, TK)] = jnp.ones((16, TK), jnp.bfloat16)
            return 0

        lax.fori_loop(lo_all, hi_all, turn, 0)

        def q_body(i, _):
            acc[...] = jnp.zeros_like(acc)
            mx[...] = jnp.full_like(mx, FIRST_MAX)

            def tile_body(t, _):
                k0 = pl.multiple_of(t * TK, TK)
                slot, plain = tile_kind(bounds, r, i, t)
                near = jnp.logical_and(slot > 0, slot < 3)

                def scores(h):
                    return mxu(kv_ref[pl.ds(k0, TK), h * 128 : h * 128 + 128], qp[i, h], NT)

                def finish(h, s, b):
                    m_old = mx[h]
                    m_new = jnp.maximum(m_old, jnp.max(s, axis=0, keepdims=True) + b)
                    p = jnp.exp(s - (m_new - b)).astype(jnp.bfloat16)
                    mx[h] = m_new
                    acc[h] = acc[h] * jnp.exp(m_old - m_new) + mxu(vt[h, :, pl.ds(k0, TK)], p)

                @pl.when(plain)
                def _():
                    found = [scores(h) for h in range(heads)]
                    for h in range(heads):
                        finish(h, found[h], jnp.where(slot == 0, table[h, 15], table[h, 31]))

                @pl.when(near)
                def _():
                    ok = valid_mask(se_ref, r, i, k0)
                    for h in range(heads):
                        s = scores(h) + near_ref[h, slot - 1].astype(jnp.float32)
                        finish(h, jnp.where(ok, s, NEG), 0.0)

                @pl.when(jnp.logical_not(jnp.logical_or(plain, near)))
                def _():
                    ok = valid_mask(se_ref, r, i, k0)
                    for h in range(heads):
                        s = scores(h) + jnp.where(slot == 0, table[h, 15], table[h, 31])
                        finish(h, jnp.where(ok, s, NEG), 0.0)

                return 0

            lax.fori_loop(bounds[r, i, 0], bounds[r, i, 1], tile_body, 0)
            parts = []
            for h in range(heads):
                total = acc[h, 64:65, :]
                parts.append((acc[h, 0:64, :] / total).T)
                lse_ref[r, i, h] = mx[h] + jnp.log(total)
            joined = join_heads(parts)
            o_ref[r, i] = joined.astype(jnp.bfloat16)
            keep_ref[r, i] = joined
            return 0

        lax.fori_loop(0, 2, q_body, 0)
        return 0

    lax.fori_loop(0, 1 if alone else 2, row_body, 0)
    if alone:
        o_ref[1 - base] = o_in[...]
        keep_ref[1 - base] = keep_in[...]
        lse_ref[1 - base] = lse_in[...]


def attention(bounds, table, q, kv, se, ready=()):
    heads, n = kv.shape[2] // 128, kv.shape[1]
    packed = q.shape
    outs = [
        jax.ShapeDtypeStruct(packed, jnp.bfloat16),
        jax.ShapeDtypeStruct(packed, jnp.float32),
        jax.ShapeDtypeStruct((2, 2, heads, 1, TQ), jnp.float32),
    ]
    if not ready:
        outs.append(jax.ShapeDtypeStruct((heads, 2, TK, TQ), jnp.bfloat16))
    return pl.pallas_call(
        functools.partial(fwd_kernel, bool(ready)),
        out_shape=tuple(outs),
        in_specs=[SMEM_SPEC] * 2 + [VMEM_SPEC, ANY_SPEC, VMEM_SPEC] + [VMEM_SPEC] * len(ready),
        out_specs=(VMEM_SPEC,) * len(outs),
        scratch_shapes=[
            pltpu.VMEM((heads, 80, n), jnp.bfloat16),
            pltpu.VMEM((heads, 80, TQ), jnp.float32),
            pltpu.VMEM((heads, 1, TQ), jnp.float32),
            pltpu.VMEM((2, heads, TQ, 128), jnp.bfloat16),
            pltpu.VMEM(kv.shape[1:], jnp.bfloat16),
            pltpu.SemaphoreType.DMA((n // TK,)),
        ],
        compiler_params=pltpu.CompilerParams(vmem_limit_bytes=VMEM_BYTES),
        name="attention",
    )(bounds, table, q, kv, se, *ready)


def prepare(q, do, q_out, do_out):
    for h, tile in enumerate(spread_lanes(q, False)):
        q_out[h] = tile
    for h, tile in enumerate(spread_lanes(do, True)):
        do_out[h] = tile


def row_deltas(do, keep, delta):
    prod = (do.astype(jnp.float32) * keep).T
    top, low = prod[:, 0:TQ], prod[:, TQ:]
    delta[0] = jnp.sum(top[0:64], axis=0, keepdims=True)
    delta[1] = jnp.sum(top[64:128], axis=0, keepdims=True)
    delta[2] = jnp.concatenate(
        [jnp.sum(low[0:64], axis=0, keepdims=True), jnp.sum(low[64:128], axis=0, keepdims=True)], axis=1
    )


def near_start(parity):
    return 416 - TQ * parity


def far_sums(grid, h, first, end):
    def one(step, total):
        rows = grid[h, pl.ds(pl.multiple_of(step * 32, 32), 32)]
        return total + jnp.sum(rows.reshape(4, 8, TQ), axis=0)
    total = lax.fori_loop(first // 32, end // 32, one, jnp.zeros((8, TQ), jnp.float32))
    return jnp.sum(total, axis=0, keepdims=True)


def bucket_sums(parity, near, side, tab_ref, tab8):
    heads = near.shape[0]
    tab8[...] = jnp.zeros_like(tab8)

    def inner(step, _):
        start = pl.multiple_of(step * 32, 32)
        which = near_buckets(near_start(parity) + start, 32, parity)
        for b in range(BUCKETS):
            here = which == b
            for h in range(heads):
                rows = jnp.where(here, near[h, pl.ds(start, 32)], 0.0)
                tab8[h, b] += jnp.sum(rows.reshape(4, 8, TQ), axis=0)
        return 0

    lax.fori_loop(0, NEAR_ROWS // 32, inner, 0)
    for h in range(heads):
        tab_ref[h] = jnp.sum(tab8[h], axis=1)
        tab_ref[h, 15:16] += side[h, 0:1]
        tab_ref[h, 31:32] += side[h, 1:2]


def bwd_kernel(alone, bounds, table, q_ref, do_ref, keep_ref, kv_hbm, bias_ref, se_ref, lse_ref,
               dq_ref, dkv_ref, near_ref, side, delta, *rest):
    tab_ref, tab8, rest = (None, None, rest) if alone else (rest[0], rest[-1], rest[1:-1])
    kt, dqt, dkv, grid, qp, dp_ref, kv_ref, kv_sem = rest
    heads = lse_ref.shape[2]
    n = kv_hbm.shape[1]
    grid[...] = jnp.zeros_like(grid)
    side[...] = jnp.zeros_like(side)
    base = 1 - bounds[0, 0, 6] if alone else 0
    for at in range(1 if alone else 2):
        for i in range(2):
            prepare(q_ref[base + at, i], do_ref[base + at, i], qp.at[at, i], dp_ref.at[at, i])
    for r in range(2):
        for i in range(2):
            row_deltas(do_ref[r, i], keep_ref[r, i], delta.at[r, i])

    def row_body(at, _):
        r = base + at
        lo_all = jnp.minimum(bounds[r, 0, 0], bounds[r, 1, 0])
        hi_all = jnp.maximum(bounds[r, 0, 1], bounds[r, 1, 1])

        def fetch(t):
            rows = pl.ds(pl.multiple_of(t * TK, TK), TK)
            return pltpu.make_async_copy(kv_hbm.at[r, rows], kv_ref.at[rows], kv_sem.at[t])

        def begin(t, _):
            fetch(t).start()
            return 0

        lax.fori_loop(lo_all, hi_all, begin, 0)

        def clear(t, _):
            k0 = pl.multiple_of(t * TK, TK)
            for h in range(heads):
                dkv[h, pl.ds(k0, TK), :] = jnp.zeros((TK, 128), jnp.float32)
            return 0

        lax.fori_loop(0, n // TK, clear, 0)

        def turn(t, _):
            fetch(t).wait()
            k0 = pl.multiple_of(t * TK, TK)
            for h in range(heads):
                tile = kv_ref[pl.ds(k0, TK), h * 128 : h * 128 + 128]
                kt[h, 0:64, pl.ds(k0, TK)] = tile.T[0:64, :]
                kt[h, 64:80, pl.ds(k0, TK)] = jnp.ones((16, TK), jnp.bfloat16)
            return 0

        lax.fori_loop(lo_all, hi_all, turn, 0)

        def q_body(i, _):
            dqt[...] = jnp.zeros_like(dqt)

            def tile_body(t, _):
                k0 = pl.multiple_of(t * TK, TK)
                slot, plain = tile_kind(bounds, r, i, t)

                def finish(h, p, ds, where):
                    ds_low = ds.astype(jnp.bfloat16)
                    two = jnp.concatenate([ds_low, p.astype(jnp.bfloat16)], axis=1)
                    both = jnp.concatenate([qp[at, i, h], dp_ref[at, i, h]], axis=0)
                    dkv[h, pl.ds(k0, TK), :] += mxu(two, both)
                    dqt[h, where] += mxu(kt[h, :, pl.ds(k0, TK)], ds_low)

                def products(h):
                    tile = kv_ref[pl.ds(k0, TK), h * 128 : h * 128 + 128]
                    return mxu(tile, qp[at, i, h], NT), mxu(tile, dp_ref[at, i, h], NT)

                @pl.when(plain)
                def _():
                    for h in range(heads):
                        s, d_probs = products(h)
                        p = jnp.exp(s - (lse_ref[r, i, h] - jnp.where(slot == 0, table[h, 15], table[h, 31])))
                        finish(h, p, p * (d_probs - delta[r, i, h]), jnp.where(slot == 0, 0, 2))

                def general(bias):
                    ok = valid_mask(se_ref, r, i, k0)
                    for h in range(heads):
                        s, d_probs = products(h)
                        s = s + bias(h)
                        p = jnp.where(ok, jnp.exp(jnp.where(ok, s, NEG) - lse_ref[r, i, h]), 0.0)
                        ds = p * (d_probs - delta[r, i, h])
                        grid[h, pl.ds(pl.multiple_of(slot * TK, TK), TK)] += ds
                        finish(h, p, ds, 1)

                near = jnp.logical_and(slot > 0, slot < 3)
                pl.when(near)(lambda: general(lambda h: bias_ref[h, slot - 1].astype(jnp.float32)))
                away = jnp.logical_not(jnp.logical_or(plain, near))
                pl.when(away)(lambda: general(lambda h: jnp.where(slot == 0, table[h, 15], table[h, 31])))
                return 0

            lax.fori_loop(bounds[r, i, 0], bounds[r, i, 1], tile_body, 0)
            parts = []
            for h in range(heads):
                parts.append((dqt[h, 0, 0:64] + dqt[h, 1, 0:64] + dqt[h, 2, 0:64]).T * 0.125)
                side[h, 0:1] += dqt[h, 0, 64:65]
                side[h, 1:2] += dqt[h, 2, 64:65]
            dq_ref[at, i] = join_heads(parts).astype(jnp.bfloat16)
            return 0

        lax.fori_loop(0, 2, q_body, 0)

        def put(t, _):
            k0 = pl.multiple_of(t * TK, TK)
            for h in range(heads):
                dkv_ref[at, pl.ds(k0, TK), h * 128 : h * 128 + 128] = dkv[h, pl.ds(k0, TK), :].astype(jnp.bfloat16)
            return 0

        lax.fori_loop(0, n // TK, put, 0)
        return 0

    lax.fori_loop(0, 1 if alone else 2, row_body, 0)

    parity = bounds[0, 0, 5]
    first = TK + near_start(parity)
    for h in range(heads):
        near_ref[h] = grid[h, pl.ds(pl.multiple_of(first, 32), NEAR_ROWS)]
        side[h, 0:1] += far_sums(grid, h, 0, first)
        side[h, 1:2] += far_sums(grid, h, first + NEAR_ROWS, 4 * TK)
    if not alone:
        bucket_sums(parity, near_ref, side, tab_ref, tab8)


def attention_back(alone, bounds, table, q, do, keep, kv, bias, se, lse):
    heads, n = kv.shape[2] // 128, kv.shape[1]
    count = 1 if alone else 2
    table_out = [] if alone else [jax.ShapeDtypeStruct((heads, BUCKETS, TQ), jnp.float32)]
    return pl.pallas_call(
        functools.partial(bwd_kernel, alone),
        out_shape=(
            jax.ShapeDtypeStruct((count,) + q.shape[1:], jnp.bfloat16),
            jax.ShapeDtypeStruct((count,) + kv.shape[1:], jnp.bfloat16),
            jax.ShapeDtypeStruct((heads, NEAR_ROWS, TQ), jnp.float32),
            jax.ShapeDtypeStruct((heads, 2, TQ), jnp.float32),
            jax.ShapeDtypeStruct((2, 2, heads, 1, TQ), jnp.float32),
        ) + tuple(table_out),
        in_specs=[SMEM_SPEC] * 2 + [VMEM_SPEC] * 3 + [ANY_SPEC] + [VMEM_SPEC] * 3,
        out_specs=(VMEM_SPEC,) * (5 + len(table_out)),
        scratch_shapes=[
            pltpu.VMEM((heads, 80, n), jnp.bfloat16),
            pltpu.VMEM((heads, 3, 80, TQ), jnp.float32),
            pltpu.VMEM((heads, n, 128), jnp.float32),
            pltpu.VMEM((heads, 4 * TK, TQ), jnp.float32),
            pltpu.VMEM((count, 2, heads, TQ, 128), jnp.bfloat16),
            pltpu.VMEM((count, 2, heads, TQ, 128), jnp.bfloat16),
            pltpu.VMEM(kv.shape[1:], jnp.bfloat16),
            pltpu.SemaphoreType.DMA((n // TK,)),
        ] + [pltpu.VMEM((heads, BUCKETS, 8, TQ), jnp.float32) for _ in table_out],
        compiler_params=pltpu.CompilerParams(vmem_limit_bytes=VMEM_BYTES),
        name="attention_back",
    )(bounds, table, q, do, keep, kv, bias, se, lse)


TAPS = tuple(range(-3, 5))
LEAD = 8


def pool_scalars(y_rows, lab_rows, first):
    tokens = y_rows[0].shape[1]
    t = lax.broadcasted_iota(jnp.int32, (1, tokens), 1)
    at = lambda rows, k: rows[k + 3]
    found = []
    for p in range(2):
        inside = {1: 0 * t, 2: 0 * t + p, 3: (first + 2 * t + p) % 3, 4: 2 * (t % 2) + p}
        weights, scores = {}, []
        for b in range(1, MAX_BLOCK + 1):
            keep = {}
            for o in range(1 - b, b):
                same = jnp.logical_and(inside[b] + o >= 0, inside[b] + o < b)
                same = jnp.logical_and(same, at(lab_rows, p + o) == at(lab_rows, p))
                keep[o] = same.astype(jnp.float32)
            inverse = 1.0 / sum(keep.values())
            for o in keep:
                weights[b, o] = keep[o] * inverse
            scores.append(sum(weights[b, o] * at(y_rows, p + o) for o in keep))
        top = functools.reduce(jnp.maximum, scores)
        grown = [jnp.exp(s - top) for s in scores]
        total = sum(grown)
        found.append(([g / total for g in grown], weights))
    return found


def tap_weights(found):
    rows = []
    for k in TAPS:
        row = 0.0
        for p, (probs, weights) in enumerate(found):
            for b in range(1, MAX_BLOCK + 1):
                if (b, k - p) in weights:
                    row = row + probs[b - 1] * weights[b, k - p]
        rows.append(0.5 * row)
    return rows


def as_columns(rows):
    tokens = rows[0].shape[1]
    return jnp.concatenate(list(rows) + [jnp.zeros((128 - len(rows), tokens), jnp.float32)], axis=0).T


def load_bytes(x_ref, before, after, xs):
    length, width = x_ref.shape
    for j in range(width // 128):
        cols = slice(j * 128, j * 128 + 128)
        xs[j, 0:LEAD, :] = jnp.zeros((LEAD, 128), jnp.float32)
        xs[j, LEAD + length :, :] = jnp.zeros((LEAD, 128), jnp.float32)
        xs[j, LEAD - 2 : LEAD, :] = before[:, cols].astype(jnp.float32)
        xs[j, LEAD + length : LEAD + length + 2, :] = after[:, cols].astype(jnp.float32)
        xs[j, LEAD : LEAD + length, :] = x_ref[:, cols].astype(jnp.float32)


def tap(xs, k, tokens):
    return jnp.concatenate([xs[j, pl.ds(LEAD + k, tokens, stride=2), :] for j in range(xs.shape[0])], axis=1)


def strips(buf, first, rows):
    return jnp.concatenate([buf[j, first : first + rows, :] for j in range(buf.shape[0])], axis=1)


def unit_rows(values):
    return lax.rsqrt(jnp.mean(values * values, axis=-1, keepdims=True) + 1e-06)


def pool_tokens(scale, xs, labels, score, gain, tokens, y_ref, share_ref):
    width = xs.shape[0] * 128
    score = jnp.broadcast_to(score, (8, width))
    for k in TAPS:
        y_ref[k + 3 : k + 4, :] = mxu(score, tap(xs, k, tokens).astype(jnp.bfloat16), NT)[0:1]
    rows = [y_ref[j : j + 1, :] for j in range(8)]
    first = (lax.axis_index("blk") * 2 * tokens) % 3
    found = pool_scalars(rows, labels, first)
    lane = lax.broadcasted_iota(jnp.int32, (1, 128), 1)
    share = jnp.zeros((1, 128), jnp.float32)
    for b in range(MAX_BLOCK):
        share = jnp.where(lane == b, jnp.sum(found[0][0][b] + found[1][0][b], axis=1, keepdims=True) * scale, share)
    share_ref[...] = share
    columns = as_columns(tap_weights(found))
    hidden = sum(columns[:, k + 3 : k + 4] * tap(xs, k, tokens) for k in TAPS)
    return hidden, (hidden * unit_rows(hidden) * gain.astype(jnp.float32)).astype(jnp.bfloat16)


def put_pairs(keys, values, kv_ref):
    low = lax.broadcasted_iota(jnp.int32, (1, 128), 1) < 64
    for j in range(keys.shape[1] // 128):
        k_pair, v_pair = keys[:, j * 128 : j * 128 + 128], values[:, j * 128 : j * 128 + 128]
        one = jnp.where(low, k_pair, turned(v_pair))
        two = jnp.where(low, turned(k_pair), v_pair)
        for head, tile in ((2 * j, one), (2 * j + 1, two)):
            kv_ref[head // 3, :, head % 3 * 128 : head % 3 * 128 + 128] = tile


def pool_kernel(shards, scale, x_ref, before_ref, after_ref, lab_ref, score_ref, gain_ref, wq_ref, wk_ref, wv_ref,
                hidden_ref, n1_ref, y_ref, share_ref, q_ref, kv_ref, xs):
    tokens = hidden_ref.shape[0]
    load_bytes(x_ref, before_ref[0:2, :], after_ref[0:2, :], xs)
    labels = [lab_ref[j : j + 1, :] for j in range(8)]
    hidden_ref[...], n1 = pool_tokens(scale, xs, labels, score_ref[...], gain_ref[...], tokens, y_ref, share_ref)
    n1_ref[...] = n1
    put_pairs(mxu(n1, wk_ref[...]).astype(jnp.bfloat16), mxu(n1, wv_ref[...]).astype(jnp.bfloat16), kv_ref)
    put_packed(mxu(n1, wq_ref[...]).astype(jnp.bfloat16) * jnp.bfloat16(0.125), q_ref)


def put_packed(array, out_ref):
    tokens = array.shape[0]
    half = tokens // 2
    for g in range(GROUPS):
        part = array[:, g * 192 : g * 192 + 192]
        out_ref[g, 0:tokens, :] = part[:, 0:128]
        out_ref[g, tokens:, :] = jnp.concatenate([part[:half, 128:], part[half:, 128:]], axis=1)


def get_packed(packed_ref):
    tokens = packed_ref.shape[1] * 2 // 3
    parts = []
    for g in range(GROUPS):
        last = packed_ref[g, tokens:, :]
        parts += [packed_ref[g, 0:tokens, :], jnp.concatenate([last[:, :64], last[:, 64:]], axis=0)]
    return jnp.concatenate(parts, axis=1)


def pool_and_project(shards, scale, x, before, after, labels, score, gain, wq, wk, wv):
    length, width = x.shape
    tokens = length // 2
    return pl.pallas_call(
        functools.partial(pool_kernel, shards, scale),
        out_shape=(
            jax.ShapeDtypeStruct((tokens, width), jnp.float32),
            jax.ShapeDtypeStruct((tokens, width), jnp.bfloat16),
            jax.ShapeDtypeStruct((8, tokens), jnp.float32),
            jax.ShapeDtypeStruct((1, 128), jnp.float32),
            jax.ShapeDtypeStruct((GROUPS, tokens * 3 // 2, 128), jnp.bfloat16),
            jax.ShapeDtypeStruct((GROUPS, tokens, width * 2 // GROUPS), jnp.bfloat16),
        ),
        in_specs=[VMEM_SPEC] * 9,
        out_specs=(VMEM_SPEC,) * 6,
        scratch_shapes=[pltpu.VMEM((width // 128, length + 2 * LEAD, 128), jnp.float32)],
        compiler_params=pltpu.CompilerParams(vmem_limit_bytes=VMEM_BYTES),
        name="pool_and_project",
    )(x, before, after, labels, score, gain, wq, wk, wv)


GELU_A = math.sqrt(2.0 / math.pi)
GELU_B = 0.044715


def norm_back(d_out, rows, gain):
    unit = unit_rows(rows)
    flat = rows * unit
    scaled = d_out * gain
    d_rows = unit * (scaled - flat * jnp.mean(scaled * flat, axis=-1, keepdims=True))
    return d_rows, jnp.sum(d_out * flat, axis=0, keepdims=True)


def feed_kernel(o_ref, hidden_ref, ct_ref, gain_ref, wo_ref, wg_ref, wu_ref, wd_ref,
                out_ref, dres_ref, da_ref, dgain_ref, n2_ref, att_ref, act_ref, dg_ref, du_ref, db_ref, acc, dn2):
    ff = wg_ref.shape[1]
    step = 512
    att = get_packed(o_ref)
    att_ref[...] = att
    residual = hidden_ref[...] + mxu(att, wo_ref[...])
    gain = gain_ref[...].astype(jnp.float32)
    n2_ref[...] = (residual * unit_rows(residual) * gain).astype(jnp.bfloat16)
    acc[...] = residual
    dn2[...] = jnp.zeros_like(dn2)

    for j in range(ff // step):
        cols = slice(j * step, j * step + step)
        n2 = n2_ref[...]
        gate = mxu(n2, wg_ref[:, cols])
        up = mxu(n2, wu_ref[:, cols])
        d_act = mxu(ct_ref[...], wd_ref[cols, :], NT)
        square = gate * gate
        curve = jnp.tanh(GELU_A * gate * (1.0 + GELU_B * square))
        half = 0.5 * (1.0 + curve)
        grown = gate * half
        slope = half + 0.5 * gate * (1.0 - curve * curve) * (GELU_A * (1.0 + 3.0 * GELU_B * square))
        act = (grown * up).astype(jnp.bfloat16)
        d_gate = (d_act * up * slope).astype(jnp.bfloat16)
        d_up = (d_act * grown).astype(jnp.bfloat16)
        act_ref[:, cols] = act
        dg_ref[:, cols] = d_gate
        du_ref[:, cols] = d_up
        acc[...] += mxu(act, wd_ref[cols, :])
        dn2[...] += mxu(d_gate, wg_ref[:, cols], NT) + mxu(d_up, wu_ref[:, cols], NT)

    out_ref[...] = acc[...].astype(jnp.bfloat16)
    residual = hidden_ref[...] + mxu(att_ref[...], wo_ref[...])
    d_rows, d_gain = norm_back(dn2[...], residual, gain)
    dgain_ref[...] = d_gain
    d_res = ct_ref[...].astype(jnp.float32) + d_rows
    dres_ref[...] = d_res
    d_branch = d_res.astype(jnp.bfloat16)
    db_ref[...] = d_branch
    put_packed(mxu(d_branch, wo_ref[...], NT).astype(jnp.bfloat16), da_ref)


def feed_forward(o_home, hidden, ct, gain, wo, wg, wu, wd):
    tokens, width = hidden.shape
    ff = wg.shape[1]
    low = lambda cols: jax.ShapeDtypeStruct((tokens, cols), jnp.bfloat16)
    return pl.pallas_call(
        feed_kernel,
        out_shape=(
            low(width),
            jax.ShapeDtypeStruct((tokens, width), jnp.float32),
            jax.ShapeDtypeStruct(o_home.shape, jnp.bfloat16),
            jax.ShapeDtypeStruct((1, width), jnp.float32),
            low(width), low(width), low(ff), low(ff), low(ff), low(width),
        ),
        in_specs=[VMEM_SPEC] * 8,
        out_specs=(VMEM_SPEC,) * 10,
        scratch_shapes=[pltpu.VMEM((tokens, width), jnp.float32)] * 2,
        compiler_params=pltpu.CompilerParams(vmem_limit_bytes=VMEM_BYTES),
        name="feed_forward",
    )(o_home, hidden, ct, gain, wo, wg, wu, wd)


def unpack_pairs(dkv_ref, width):
    low = lax.broadcasted_iota(jnp.int32, (1, 128), 1) < 64
    dk_parts, dv_parts = [], []
    for j in range(width // 128):
        one, two = [dkv_ref[h // 3, :, h % 3 * 128 : h % 3 * 128 + 128] for h in (2 * j, 2 * j + 1)]
        dk_parts.append(jnp.where(low, one, turned(two)))
        dv_parts.append(jnp.where(low, turned(one), two))
    return jnp.concatenate(dk_parts, axis=1), jnp.concatenate(dv_parts, axis=1)


def pool_back(d_hidden, length, lab_ref, y_ref, score, gb_ref, edge_ref, spill_ref, xs, gbuf):
    tokens, width = d_hidden.shape
    lane = lax.broadcasted_iota(jnp.int32, (1, 128), 1)
    met = jnp.zeros((tokens, 128), jnp.float32)
    for k in TAPS:
        met = jnp.where(lane == k + 3, jnp.sum(d_hidden * tap(xs, k, tokens), axis=-1, keepdims=True), met)
    met = met.T
    first = (lax.axis_index("blk") * length) % 3
    found = pool_scalars([y_ref[j : j + 1, :] for j in range(8)], [lab_ref[j : j + 1, :] for j in range(8)], first)
    touch = [0.0] * 8
    for p, (probs, weights) in enumerate(found):
        d_block = []
        for b in range(1, MAX_BLOCK + 1):
            d_block.append(0.5 * sum(weights[b, o] * met[p + o + 3 : p + o + 4] for o in range(1 - b, b)))
        mean = sum(q * d for q, d in zip(probs, d_block))
        for b in range(1, MAX_BLOCK + 1):
            d_score = probs[b - 1] * (d_block[b - 1] - mean)
            for o in range(1 - b, b):
                touch[p + o + 3] = touch[p + o + 3] + d_score * weights[b, o]
    share_cols = as_columns(tap_weights(found) + touch)
    score = score.astype(jnp.float32)
    gbuf[...] = jnp.zeros_like(gbuf)
    d_score_vec = jnp.zeros((1, width), jnp.float32)
    for k in TAPS:
        own, via = share_cols[:, k + 3 : k + 4], share_cols[:, k + 11 : k + 12]
        added = own * d_hidden + via * score
        for j in range(gbuf.shape[0]):
            gbuf[j, pl.ds(LEAD + k, tokens, stride=2), :] += added[:, j * 128 : j * 128 + 128]
        d_score_vec = d_score_vec + jnp.sum(via * tap(xs, k, tokens), axis=0, keepdims=True)
    gb_ref[...] = strips(gbuf, LEAD, length).astype(jnp.bfloat16)
    edge_ref[0] = strips(gbuf, LEAD, 16)
    edge_ref[1] = strips(gbuf, LEAD + length - 16, 16)
    spill_ref[0] = strips(gbuf, 0, LEAD)
    spill_ref[1] = strips(gbuf, LEAD + length, LEAD)
    return d_score_vec


def put_small(small_ref, vectors, tab_ref, share_ref):
    small_ref[...] = jnp.zeros_like(small_ref)
    for row, vector in zip((0, 6, 12), vectors):
        for j in range(6):
            small_ref[row + j : row + j + 1, :] = vector[:, j * 128 : j * 128 + 128]
    heads = tab_ref.shape[0]
    group = lax.axis_index("blk") // (lax.axis_size("blk") // GROUPS)
    for h in range(heads):
        total = lax.dot_general(
            jnp.ones((8, tab_ref.shape[2]), jnp.float32), tab_ref[h], NT,
            precision=lax.Precision.HIGHEST, preferred_element_type=jnp.float32,
        )
        small_ref[pl.ds(18 + group * heads + h, 1), 0:BUCKETS] = total[0:1]
    small_ref[30:31, :] = share_ref[...]


def last_kernel(shards, axes, order, dq_ref, dkv_ref, hidden_ref, dres_ref, x_ref, before_ref, after_ref, lab_ref, y_ref, score_ref,
                gain_ref, wq_ref, wk_ref, wv_ref, dgain2_ref, share_ref, tab_ref, gb_ref, edge_ref, spill_out, small_out, parts_ref,
                w_send, w_recv, s_send, s_recv, xs, gbuf, spill_ref, small_ref, small_bufs):
    at = {"dp": lax.axis_index("dp"), "blk": lax.axis_index("blk")}
    width = hidden_ref.shape[1]
    whole = Whole(axes, at, order, small_ref, small_bufs, small_out, w_send, w_recv)
    left = (at["dp"], (at["blk"] + shards - 1) % shards)
    right = (at["dp"], (at["blk"] + 1) % shards)
    greet([whole.stream.target(p) for p in range(len(axes))] + [left, right])
    load_bytes(x_ref, before_ref[0:2, :], after_ref[0:2, :], xs)
    dq = get_packed(dq_ref)
    dk, dv = unpack_pairs(dkv_ref, width)
    parts_ref[0], parts_ref[1], parts_ref[2] = dq, dk, dv
    d_n1 = mxu(dq, wq_ref[...], NT) + mxu(dk, wk_ref[...], NT) + mxu(dv, wv_ref[...], NT)
    d_rows, d_gain1 = norm_back(d_n1, hidden_ref[...], gain_ref[...].astype(jnp.float32))
    d_hidden = dres_ref[...] + d_rows
    d_score = pool_back(d_hidden, x_ref.shape[0], lab_ref, y_ref, score_ref[...], gb_ref, edge_ref, spill_ref, xs, gbuf)
    put_small(small_ref, (d_score, d_gain1, dgain2_ref[...]), tab_ref, share_ref)
    spills = [
        remote(spill_ref.at[0], spill_out.at[1], s_send.at[0], s_recv.at[1], left),
        remote(spill_ref.at[1], spill_out.at[0], s_send.at[1], s_recv.at[0], right),
    ]
    whole.copy(0).start()
    for copy in spills:
        copy.start()
    for stage in range(len(axes)):
        advance(whole, stage)
    for copy in spills:
        copy.wait()


def last_part(shape, dq, dkv, hidden, dres, x, before, after, labels, y, score, gain, wq, wk, wv, dgain2, share, tab):
    tokens, width = hidden.shape
    length = x.shape[0]
    axes = bit_axes(shape)
    ndim = len(axes)
    full, sem, low = jax.ShapeDtypeStruct, pltpu.SemaphoreType.DMA, jnp.bfloat16
    strip = pltpu.VMEM((width // 128, length + 2 * LEAD, 128), jnp.float32)
    return pl.pallas_call(
        functools.partial(last_kernel, shape["blk"], axes, tuple(reversed(range(ndim)))),
        out_shape=(
            full((length, width), low),
            full((2, 16, width), jnp.float32),
            full((2, LEAD, width), jnp.float32),
            full((32, 128), jnp.float32),
            full((3, tokens, width), low),
        ),
        in_specs=[VMEM_SPEC] * 17,
        out_specs=(VMEM_SPEC,) * 5,
        scratch_shapes=[
            sem((ndim,)), sem((ndim,)), sem((2,)), sem((2,)), strip, strip,
            pltpu.VMEM((2, LEAD, width), jnp.float32), pltpu.VMEM((32, 128), jnp.float32), pltpu.VMEM((2, ndim, 32, 128), jnp.float32),
        ],
        compiler_params=pltpu.CompilerParams(collective_id=3, has_side_effects=True, vmem_limit_bytes=VMEM_BYTES),
        name="last_part",
    )(dq, dkv, hidden, dres, x, before, after, labels, y, score, gain, wq, wk, wv, dgain2, share, tab)


def finish_kernel(shards, block_ref, gb_ref, edge_ref, spill_ref, small_ref, *refs):
    position = lax.axis_index("blk")
    count = 7 if len(refs) == 7 else 14
    streams, outs = refs[: len(refs) - count], refs[len(refs) - count :]
    out_ref, bytes_ref, score_ref, gain1_ref, gain2_ref, tab_ref, share_ref = outs[:7]
    out_ref[...] = block_ref[...]
    length = gb_ref.shape[0]
    bytes_ref[...] = gb_ref[...]
    zero = jnp.zeros((16 - LEAD, gb_ref.shape[1]), jnp.float32)
    left = jnp.where(position > 0, spill_ref[0], 0.0)
    right = jnp.where(position < shards - 1, spill_ref[1], 0.0)
    bytes_ref[0:16, :] = (edge_ref[0] + jnp.concatenate([left, zero], axis=0)).astype(jnp.bfloat16)
    bytes_ref[length - 16 :, :] = (edge_ref[1] + jnp.concatenate([zero, right], axis=0)).astype(jnp.bfloat16)
    for row, ref in ((0, score_ref), (6, gain1_ref), (12, gain2_ref)):
        for j in range(6):
            ref[j * 128 : j * 128 + 128] = small_ref[row + j, :]
    tab_ref[...] = small_ref[18 : 18 + tab_ref.shape[0], 0 : tab_ref.shape[1]]
    share_ref[...] = small_ref[30, 0:MAX_BLOCK]
    if streams:
        gq, gk, gv, go, gg, gu, gd = outs[7:]
        per, width = gq.shape
        half, ff = width // 2, gg.shape[1]
        one, two, down, *thirds = streams
        for ref, third in zip((gq, gk, gv), thirds):
            ref[:, :half] = third[:per, :]
            ref[:, half:] = third[per:, :]
        first = one.shape[1]
        for ref, rows in ((gg, slice(0, per)), (gu, slice(per, 2 * per))):
            ref[:, :first] = one[rows, :]
            ref[:, first:] = two[rows, : ff - first]
        go[:, :half] = two[:per, ff - first :]
        go[:, half:] = two[per:, ff - first :]
        gd[...] = down[...]


def finish(shards, heads_all, per, ff, block_out, gb, edge, spill, small, streams):
    width = gb.shape[1]
    full = jax.ShapeDtypeStruct
    line = full((width,), jnp.float32)
    outs = [full(block_out.shape, jnp.bfloat16), full(gb.shape, jnp.bfloat16), line, line, line]
    outs += [full((heads_all, BUCKETS), jnp.float32), full((MAX_BLOCK,), jnp.float32)]
    if streams:
        square, broad = full((per, width), jnp.float32), full((per, ff), jnp.float32)
        outs += [square] * 4 + [broad] * 2 + [full(streams[2].shape, jnp.float32)]
    return pl.pallas_call(
        functools.partial(finish_kernel, shards),
        out_shape=tuple(outs),
        in_specs=[VMEM_SPEC] * (5 + len(streams)),
        out_specs=(VMEM_SPEC,) * len(outs),
        compiler_params=pltpu.CompilerParams(vmem_limit_bytes=VMEM_BYTES),
        name="finish",
    )(block_out, gb, edge, spill, small, *streams)


class NearRows:
    def __init__(self, grid, first):
        self.grid, self.first, self.shape = grid, first, grid.shape

    def __getitem__(self, index):
        h, rows = index
        return self.grid[h, pl.ds(pl.multiple_of(self.first + rows.start, 32), rows.size)]


class Refs:
    def __init__(self, **refs):
        self.__dict__.update(refs)


def row_of(vectors, k):
    return jnp.concatenate([vectors[6 * k + j : 6 * k + j + 1, :] for j in range(6)], axis=1)


class BiasTable:
    def __init__(self, ref, place, heads):
        self.ref, self.first = ref, place.group * heads

    def __getitem__(self, index):
        head, bucket = index
        return self.ref[self.first + head, bucket]


class Held:
    def __init__(self, array, space):
        self.array, self.space = array, space


def call(kernel, ident, ins, outs, scratch):
    leaf = lambda entry: isinstance(entry, Held) or isinstance(entry, tuple) or not isinstance(entry, (dict, list))
    parts = [jax.tree.flatten(part, is_leaf=leaf) for part in (ins, outs, scratch)]
    counts = [len(part[0]) for part in parts]
    given, wanted, kept = [part[0] for part in parts]

    def run(*refs):
        named, start = {}, 0
        for count, (_, tree) in zip(counts, parts):
            named.update(jax.tree.unflatten(tree, refs[start : start + count]))
            start += count
        kernel(Refs(**named))

    space = lambda entry, at: entry.space if isinstance(entry, Held) else entry[2] if isinstance(entry, tuple) and len(entry) > 2 else at
    found = pl.pallas_call(
        run,
        out_shape=tuple(jax.ShapeDtypeStruct(entry[0], entry[1]) for entry in wanted),
        in_specs=[pl.BlockSpec(memory_space=space(entry, pltpu.VMEM)) for entry in given],
        out_specs=tuple(pl.BlockSpec(memory_space=space(entry, pltpu.VMEM)) for entry in wanted),
        scratch_shapes=kept,
        compiler_params=pltpu.CompilerParams(collective_id=ident, has_side_effects=True, vmem_limit_bytes=VMEM_BYTES),
        name=kernel.func.__name__,
    )(*[entry.array if isinstance(entry, Held) else entry for entry in given])
    return Refs(**jax.tree.unflatten(parts[1][1], found))


wide = lambda value: value.astype(jnp.float32)
slim = lambda value: value.astype(jnp.bfloat16)


class RowBack:
    def __init__(self, place, r):
        self.place, self.r = place, r
        self.heads = r.lse.shape[1]
        self.table = BiasTable(r.table, place, self.heads)
        self.tokens = TQ
        self.across, self.core_to = place.other_rest(2), place.other_rest(1)
        self.y, self.core = bit(place.rest, 2), place.rest % 2

    def group_of(self, n):
        return (self.place.group + 1 + n) % GROUPS

    def tile_start(self, m):
        place_y = jnp.where(m % 2 == 0, 1 - self.y, self.y)
        return pl.multiple_of((self.group_of(m // 2) * 2 + place_y) * TK, TK)

    def fetch(self, m):
        r = self.r
        rows = pl.ds(self.tile_start(m), TK)
        return (
            pltpu.make_async_copy(r.kv_hbm.at[rows], r.kv.at[m], r.kv_sem.at[m]),
            pltpu.make_async_copy(r.kl_hbm.at[rows], r.kl.at[m], r.kl_sem.at[m]),
        )

    def fetch_all(self):
        for m in range(2 * GROUPS):
            for copy in self.fetch(m):
                copy.start()

    def prepare(self):
        r = self.r

        def one(i, _):
            for h, tile in enumerate(spread_lanes(r.q[i], False)):
                r.qp[i, h] = tile
            for h, tile in enumerate(spread_lanes(r.do[i], True)):
                r.dp[i, h] = tile
            row_deltas(r.do[i], r.keep[i], r.delta.at[i])
            return 0

        lax.fori_loop(0, GROUPS, one, 0)

    def clear(self):
        r = self.r
        r.dqt[...] = jnp.zeros_like(r.dqt)
        r.grid[...] = jnp.zeros_like(r.grid)

    def core_copy(self, n, j):
        r = self.r
        return remote(r.held.at[n, j, 1 - self.core], r.core_in.at[n, j], r.core_send.at[n, j], r.core_recv.at[n, j], self.core_to)

    def y_copy(self, n):
        r = self.r
        return remote(r.y_out.at[n], r.y_in.at[n], r.y_send.at[n], r.y_recv.at[n], self.across)

    def z_copy(self, n):
        r, place = self.r, self.place
        return remote(r.z_out.at[n], r.dkv_home.at[place.group], r.z_send.at[n], r.z_recv.at[n], place.at(place.row, self.group_of(n), place.rest))

    def by_rows(self, one):
        def step(k, _):
            one(pl.ds(pl.multiple_of(k * 32, 32), 32))
            return 0
        lax.fori_loop(0, self.tokens // 32, step, 0)

    def own_sum(self, n, j, rows):
        return wide(self.r.held[n, j, self.core, rows]) + wide(self.r.core_in[n, j, rows])

    def send_y(self, n):
        r = self.r
        self.core_copy(n, 0).wait()

        def one(rows):
            r.y_out[n, rows] = slim(self.own_sum(n, 0, rows))

        self.by_rows(one)
        self.y_copy(n).start()

    def send_home(self, n):
        r = self.r
        self.core_copy(n, 1).wait()
        self.y_copy(n).wait()
        here = isinstance(n, int) and n == GROUPS - 1

        def one(rows):
            total = slim(self.own_sum(n, 1, rows) + wide(r.y_in[n, rows]))
            if here:
                r.dkv_home[self.place.group, rows] = total
            else:
                r.z_out[n, rows] = total

        self.by_rows(one)
        if not here:
            self.z_copy(n).start()

    def begin(self, m, a):
        r = self.r
        for copy in self.fetch(m):
            copy.wait()
        r.acc[a] = jnp.zeros_like(r.acc[a])
        for h in range(self.heads):
            r.kt[a, h, 0:64] = r.kv[m, :, h * 128 : h * 128 + 128].T[0:64]
            r.kt[a, h, 64:80] = jnp.ones((16, TK), jnp.bfloat16)

    def part(self, m, i, a):
        r, heads = self.r, self.heads
        t = self.tile_start(m) // TK
        keys = lambda h: r.kv[m, :, h * 128 : h * 128 + 128]
        slot = near_slot(self.place, i, t)
        away = jnp.logical_or(slot == 0, slot == 3)

        def finish(h, p, ds, where):
            ds_low = ds.astype(jnp.bfloat16)
            two = jnp.concatenate([ds_low, p.astype(jnp.bfloat16)], axis=1)
            both = jnp.concatenate([r.qp[i, h], r.dp[i, h]], axis=0)
            r.acc[a, :, h * 128 : h * 128 + 128] += mxu(two, both)
            r.dqt[i, h, where] += mxu(r.kt[a, h], ds_low)

        def products(h):
            s = mxu(jnp.concatenate([keys(h), r.kl[m]], axis=1), jnp.concatenate([r.qp[i, h], r.ql[i]], axis=1), NT)
            return s, mxu(keys(h), r.dp[i, h], NT)

        @pl.when(away)
        def _():
            for h in range(heads):
                s, d_probs = products(h)
                p = jnp.exp(s - (r.lse[i, h] - jnp.where(slot == 0, self.table[h, 15], self.table[h, 31])))
                finish(h, p, p * (d_probs - r.delta[i, h]), jnp.where(slot == 0, 0, 2))

        @pl.when(jnp.logical_not(away))
        def _():
            for h in range(heads):
                s, d_probs = products(h)
                p = jnp.exp(s + r.bias[h, slot - 1].astype(jnp.float32) - r.lse[i, h])
                ds = p * (d_probs - r.delta[i, h])
                r.grid[h, pl.ds(pl.multiple_of((slot - 1) * TK, TK), TK)] += ds
                finish(h, p, ds, 1)

    def end(self, m, a):
        r = self.r
        n, j = m // 2, m % 2
        for half in range(2):
            r.held[n, j, half] = r.acc[a, half * self.tokens : half * self.tokens + self.tokens].astype(jnp.bfloat16)
        self.core_copy(n, j).start()

    def query(self, i):
        r, place = self.r, self.place
        parts = []
        for h in range(self.heads):
            parts.append((r.dqt[i, h, 0, 0:64] + r.dqt[i, h, 1, 0:64] + r.dqt[i, h, 2, 0:64]).T * 0.125)
        r.dq[i] = slim(join_heads(parts))
        step = (i - place.group + GROUPS) % GROUPS
        copy = remote(r.dq.at[i], r.dq_home.at[place.group], r.q_send.at[step], r.q_recv.at[step], place.at(place.row, i, place.rest))
        pl.when(step > 0)(copy.start)

    def buckets(self):
        r = self.r
        first = near_start(self.core)
        for h in range(self.heads):
            r.side[h, 0:1] = sum(r.dqt[i, h, 0, 64:65] for i in range(GROUPS)) + far_sums(r.grid, h, 0, first)
            r.side[h, 1:2] = sum(r.dqt[i, h, 2, 64:65] for i in range(GROUPS)) + far_sums(r.grid, h, first + NEAR_ROWS, 2 * TK)
        bucket_sums(self.core, NearRows(r.grid, first), r.side, r.tab, r.tab8)

    def wait_home(self):
        r, place = self.r, self.place
        for n in range(GROUPS - 1):
            there = r.dkv_home.at[(place.group - 1 - n + GROUPS) % GROUPS]
            remote(r.z_out.at[n], there, r.z_send.at[n], r.z_recv.at[n], self.core_to).wait()


def back_kernel(shards, axes, plans, r):
    place = Place(shards)
    at = {"dp": place.dp, "blk": place.blk}
    tokens, width = r.hidden.shape
    back = RowBack(place, r)
    streams = []
    for s, (kept, order) in enumerate(plans):
        src = r.early_hbm[s] if s < 3 else r.late[s - 3]
        own = r.early_own[s] if s < 3 else None
        streams.append(Stream(axes, at, kept, order, src, own, r.bufs[s], r.sums[s], r.w_send.at[s], r.w_recv.at[s]))
    early, late = streams[:3], streams[3:]
    whole = Whole(axes, at, (4, 0, 3, 2, 1), r.small, r.small_bufs, r.small_out, r.w_send.at[len(plans)], r.w_recv.at[len(plans)])
    left, right = (place.dp, (place.blk + shards - 1) % shards), (place.dp, (place.blk + 1) % shards)

    met = hail([place.other_group(step) for step in (1, 2, 3)] + [back.across, back.core_to, place.other_row(), left, right])
    back.fetch_all()
    halves = []
    for s, stream in enumerate(early):
        (now,) = stream.order[:1]
        index = tuple(stream.own(p) if p == now else slice(None) for p in stream.kept)
        halves.append(pltpu.make_async_copy(r.early_hbm[s].at[index], r.early_own[s], r.own_sem.at[s]))
        halves[-1].start()
    later = [pltpu.make_async_copy(src, dst, r.later_sem.at[k]) for k, (src, dst) in enumerate((
        (r.hidden_hbm, r.hidden), (r.dres_hbm, r.dres), (r.n1_hbm, r.n1), (r.x_hbm, r.x), (r.wq_hbm, r.wq), (r.wk_hbm, r.wk), (r.wv_hbm, r.wv),
    ))]
    for copy in later:
        copy.start()
    back.prepare()
    await_all(met)
    for stream in early:
        stream.copy(0).start()
    back.clear()

    def halve(s):
        halves[s].wait()
        advance(early[s], 0)

    def step(m, _):
        back.begin(m, 0)

        def one(i, _):
            back.part(m, i, 0)
            return 0

        lax.fori_loop(0, GROUPS, one, 0)
        back.end(m, 0)
        for delay, action in ((1, back.send_y), (3, back.send_home)):
            then = m - delay + 2 * GROUPS
            n = then // 2 - GROUPS

            @pl.when(jnp.logical_and(then % 2 == 0, n >= 0))
            def _():
                action(n)

        for when, s in ((4, 0), (5, 2)):
            pl.when(m == when)(functools.partial(halve, s))
        return 0

    lax.fori_loop(0, 2 * GROUPS - 2, step, 0)
    back.begin(6, 0)
    back.begin(7, 1)

    def chunk(k, _):
        i = (place.group + 1 + k) % GROUPS
        back.part(6, i, 0)
        back.part(7, i, 1)
        back.query(i)
        pl.when(k == 3)(functools.partial(back.send_home, 2))
        return 0

    lax.fori_loop(0, GROUPS, chunk, 0)
    back.end(6, 0)
    back.end(7, 1)
    home = Line(place, r.dq, r.dq_home, r.q_send, r.q_recv)
    home.keep().start()
    halve(1)
    back.send_y(3)
    back.buckets()
    back.send_home(3)
    for copy in later:
        copy.wait()
    load_bytes(r.x, r.before[14:16, :], r.after[0:2, :], r.xs)
    n1_t = r.n1[...].T
    for s in (2, 0, 1):
        advance(early[s], 1)
    home.wait_all()
    dq = get_packed(r.dq_home)
    devices = 1 << len(axes)
    per = width // devices
    half = width // 2

    def weights(stream, part):
        r.total[...] = mxu(n1_t, part)

        def block(d, _):
            rows = pl.ds(pl.multiple_of(d * per, 8), per)
            index, rest = [], d
            for _ in axes:
                index.append(rest % 2)
                rest = rest // 2
            part = r.total[rows, :]
            stream.src[tuple(reversed(index))] = jnp.concatenate([part[:, :half], part[:, half:]], axis=0).astype(jnp.bfloat16)
            return 0

        lax.fori_loop(0, devices, block, 0)
        stream.copy(0).start()

    weights(late[0], dq)
    back.wait_home()
    dk, dv = unpack_pairs(r.dkv_home, width)
    weights(late[1], dk)
    weights(late[2], dv)
    d_n1 = mxu(dq, r.wq[...], NT) + mxu(dk, r.wk[...], NT) + mxu(dv, r.wv[...], NT)
    d_rows, d_gain1 = norm_back(d_n1, r.hidden[...], row_of(r.vectors, 1))
    d_hidden = r.dres[...] + d_rows
    for stream in late:
        advance(stream, 0)
    for stream in early:
        advance(stream, 2)
    d_score = pool_back(d_hidden, r.x.shape[0], r.labels, r.y, row_of(r.vectors, 0), r.gb, r.edge, r.spill, r.xs, r.gbuf)
    put_small(r.small, (d_score, d_gain1, r.dgain2[...]), r.tab, r.share)
    whole.copy(0).start()
    spills = [
        remote(r.spill.at[0], r.spill_out.at[1], r.s2_send.at[0], r.s2_recv.at[1], left),
        remote(r.spill.at[1], r.spill_out.at[0], r.s2_send.at[1], r.s2_recv.at[0], right),
    ]
    for copy in spills:
        copy.start()
    for stage in range(1, len(axes)):
        for stream in late:
            advance(stream, stage)
        advance(whole, stage - 1)
        if stage == 1:
            for stream in early:
                advance(stream, 3)
    advance(whole, len(axes) - 1)
    for copy in spills:
        copy.wait()


def back_and_last(shape, early, inputs):
    shards = shape["blk"]
    axes = bit_axes(shape)
    ndim = len(axes)
    kv, q, hidden = inputs["kv_hbm"].array, inputs["q"], inputs["hidden_hbm"].array
    heads, width = kv.shape[1] // 128, kv.shape[1]
    tokens, features = hidden.shape
    length = inputs["x_hbm"].array.shape[0]
    f32, low, sem = jnp.float32, jnp.bfloat16, pltpu.SemaphoreType.DMA
    chunk = (tokens, width)
    every = (0, 1, 2, 3, 4)
    four = (0, 1, 2, 3)
    plans = [
        (four, (0, 3, 2, 1)), (four, (3, 0, 2, 1)), (four, (2, 0, 3, 1)),
        (every, (4, 0, 3, 2, 1)), (every, (4, 3, 2, 0, 1)), (every, (4, 2, 0, 3, 1)),
    ]
    own = (2 * (features // (1 << ndim)), features // 2)
    blocks = [part.shape[-2:] for part in early] + [own] * 3
    ins = dict(inputs, early_hbm=[Held(part.reshape((2, 2, 2, 2) + part.shape[-2:]), pl.ANY) for part in early])
    outs = dict(
        gb=((length, features), low), edge=((2, 16, features), f32), spill_out=((2, LEAD, features), f32),
        small_out=((32, 128), f32), sums=[(block, f32) for block in blocks],
    )
    mem = lambda shape, dtype=low: pltpu.VMEM(shape, dtype)
    pairs, fours = sem((GROUPS, 2)), sem((GROUPS,))
    strip = mem((features // 128, length + 2 * LEAD, 128), f32)
    eights = sem((2 * GROUPS,))
    scratch = dict(
        kt=mem((2, heads, 80, TK)), dqt=mem((GROUPS, heads, 3, 80, TQ), f32), acc=mem((2, TK, width), f32),
        grid=mem((heads, 2 * TK, TQ), f32), side=mem((heads, 2, TQ), f32), tab8=mem((heads, BUCKETS, 8, TQ), f32),
        tab=mem((heads, BUCKETS, TQ), f32), delta=mem((GROUPS, heads, 1, TQ), f32),
        qp=mem((GROUPS, heads, TQ, 128)), dp=mem((GROUPS, heads, TQ, 128)),
        kv=mem((2 * GROUPS, TK, width)), kl=mem((2 * GROUPS, TK, 128)),
        held=mem((GROUPS, 2, 2) + chunk), core_in=mem((GROUPS, 2) + chunk),
        y_out=mem((GROUPS,) + chunk), y_in=mem((GROUPS,) + chunk), z_out=mem((GROUPS,) + chunk), dkv_home=mem((GROUPS,) + chunk),
        dq=mem(q.shape), dq_home=mem(q.shape),
        core_send=pairs, core_recv=pairs, y_send=fours, y_recv=fours, z_send=fours, z_recv=fours, q_send=fours, q_recv=fours,
        kv_sem=eights, kl_sem=eights, own_sem=sem((3,)), later_sem=sem((7,)),
        hidden=mem((tokens, features), f32), dres=mem((tokens, features), f32), n1=mem((tokens, features)), x=mem((length, features)),
        wq=mem((features, features)), wk=mem((features, features)), wv=mem((features, features)),
        w_send=sem((len(plans) + 1, ndim)), w_recv=sem((len(plans) + 1, ndim)), s2_send=sem((2,)), s2_recv=sem((2,)),
        xs=strip, gbuf=strip, spill=mem((2, LEAD, features), f32), small=mem((32, 128), f32),
        small_bufs=mem((2, ndim, 32, 128), f32), total=mem((features, features), f32),
    )
    scratch["early_own"] = [mem((2, 2, 2) + block) for block in blocks[:3]]
    scratch["late"] = [mem((2,) * ndim + own)] * 3
    scratch["bufs"] = [stream_scratch(len(kept), order, *block) for (kept, order), block in zip(plans, blocks)]
    return call(functools.partial(back_kernel, shards, axes, plans), 6, ins, outs, scratch)


def label_features(line, unlike):
    rows = [(line != k if unlike else line == k).astype(jnp.float32) for k in range(8)]
    return slim(jnp.concatenate(rows + [jnp.zeros((120, line.shape[1]), jnp.float32)], axis=0).T)


class Line:
    def __init__(self, place, src, dst, send_sem, recv_sem):
        self.place, self.src, self.dst, self.send_sem, self.recv_sem = place, src, dst, send_sem, recv_sem

    def copy(self, step, slot):
        group = self.place.group
        return remote(
            self.src.at[(group + step) % GROUPS], self.dst.at[slot], self.send_sem.at[step], self.recv_sem.at[step],
            self.place.other_group(step),
        )

    def keep(self):
        group = self.place.group
        return pltpu.make_async_copy(self.src.at[group], self.dst.at[group], self.send_sem.at[0])

    def start(self, steps=(1, 3, 2)):
        for step in steps:
            self.copy(step, self.place.group).start()

    def wait(self, step):
        self.copy(step, (self.place.group - step + GROUPS) % GROUPS).wait()

    def wait_all(self):
        for step in (1, 3, 2):
            self.wait(step)
        self.keep().wait()

    def gone(self, step):
        self.copy(step, self.place.group).wait_send()

    def come_all(self):
        for step in (1, 3, 2):
            self.copy(step, (self.place.group - step + GROUPS) % GROUPS).wait_recv()
        self.keep().wait()


def near_slot(place, chunk, t):
    first = (chunk * place.rest_size + place.rest) * TQ
    return jnp.clip(t - (first // TK - 1 + place.rest % 2) + 1, 0, 3)


class RowForward:
    def __init__(self, place, r):
        self.place, self.r, self.heads = place, r, r.lse.shape[1]
        self.table = BiasTable(r.table, place, self.heads)

    def clear(self):
        self.r.acc[...] = jnp.zeros_like(self.r.acc)
        self.r.mx[...] = jnp.full_like(self.r.mx, FIRST_MAX)

    def queries(self, chunk):
        r = self.r
        for h, tile in enumerate(spread_lanes(r.q_all[chunk], False)):
            r.qp[chunk, h] = jnp.concatenate([tile, r.ql[chunk]], axis=1)

    def tile(self, t):
        r = self.r
        rows = pl.ds(pl.multiple_of(t * TK, TK), TK)
        keys = lambda h: r.kv_all[rows, h * 128 : h * 128 + 128]
        for h in range(self.heads):
            r.vt[h, 0:64] = keys(h).T[64:128]
            r.vt[h, 64:80] = jnp.ones((16, TK), jnp.bfloat16)

        def scores(i, h):
            return mxu(jnp.concatenate([keys(h), r.kl[rows, :]], axis=1), r.qp[i, h], NT)

        def finish(i, h, s, b):
            m_old = r.mx[i, h]
            m_new = jnp.maximum(m_old, jnp.max(s, axis=0, keepdims=True) + b)
            p = jnp.exp(s - (m_new - b)).astype(jnp.bfloat16)
            r.mx[i, h] = m_new
            r.acc[i, h] = r.acc[i, h] * jnp.exp(m_old - m_new) + mxu(r.vt[h], p)

        def part(i, _):
            slot = near_slot(self.place, i, t)
            away = jnp.logical_or(slot == 0, slot == 3)

            @pl.when(away)
            def _():
                found = [scores(i, h) for h in range(self.heads)]
                for h in range(self.heads):
                    finish(i, h, found[h], jnp.where(slot == 0, self.table[h, 15], self.table[h, 31]))

            @pl.when(jnp.logical_not(away))
            def _():
                for h in range(self.heads):
                    finish(i, h, scores(i, h) + r.near[h, slot - 1].astype(jnp.float32), 0.0)

            return 0

        def pair(p, _):
            slots = [near_slot(self.place, 2 * p + k, t) for k in range(2)]
            far = [jnp.logical_or(slot == 0, slot == 3) for slot in slots]
            both = jnp.logical_and(far[0], far[1])

            @pl.when(both)
            def _():
                items = [(2 * p + k, h, jnp.where(slots[k] == 0, self.table[h, 15], self.table[h, 31])) for h in range(self.heads) for k in range(2)]
                found = [scores(i, h) for i, h, _ in items]
                for (i, h, b), s in zip(items, found):
                    finish(i, h, s, b)

            @pl.when(jnp.logical_not(both))
            def _():
                lax.fori_loop(2 * p, 2 * p + 2, part, 0)

            return 0

        lax.fori_loop(0, GROUPS // 2, pair, 0)

    def end(self):
        r = self.r

        def one(i, _):
            parts = []
            for h in range(self.heads):
                total = r.acc[i, h, 64:65, :]
                parts.append((r.acc[i, h, 0:64, :] / total).T)
                r.lse[i, h] = r.mx[i, h] + jnp.log(total)
            joined = join_heads(parts)
            r.o[i] = joined.astype(jnp.bfloat16)
            r.keep[i] = joined
            return 0

        lax.fori_loop(0, GROUPS, one, 0)


def label_taps(place, own, left, right):
    at_left, at_right = place.blk == 0, place.blk == place.shards - 1
    even, odd = jnp.concatenate([own[0:1], own[1:2]], axis=1), jnp.concatenate([own[2:3], own[3:4]], axis=1)
    none = jnp.full((1, 1), -1, jnp.int32)
    before = [jnp.where(at_left, none, left[row : row + 1, 127:128]) for row in (1, 3)]
    after = [jnp.where(at_right, none, right[row : row + 1, 0:1]) for row in (0, 2)]
    join = lambda *parts: jnp.concatenate(parts, axis=1)
    return [
        join(none, before[1], odd[:, :-2]), join(before[0], even[:, :-1]), join(before[1], odd[:, :-1]), even, odd,
        join(even[:, 1:], after[0]), join(odd[:, 1:], after[1]), join(even[:, 2:], after[0], none),
    ]


def front_kernel(shards, scale, r):
    place = Place(shards)
    tokens = r.kv.shape[1]
    y, core = bit(place.rest, 2), place.rest % 2
    core_to, across = place.other_rest(1), place.other_rest(2)
    peers = [(place.dp, (place.blk + step) % shards) for step in range(1, shards)]
    met = hail(peers)
    length = r.x.shape[0]

    def label_copy(step, block):
        return remote(r.label, r.labels_all.at[block], r.lab_send.at[step], r.lab_recv.at[step], peers[step - 1])

    def label_come(step):
        back = (place.blk + shards - step) % shards
        label_copy(step, back).wait_recv()
        return r.labels_all[back]

    lane = lax.broadcasted_iota(jnp.int32, (128, 128), 0)
    to = lax.broadcasted_iota(jnp.int32, (128, 128), 1)
    apart = (lane == jnp.where(to < 64, 2 * to, 2 * to - 127)).astype(jnp.float32).astype(jnp.bfloat16)
    flat = jnp.concatenate([r.segments[0:1, j * 128 : j * 128 + 128] for j in range(4)] + [jnp.zeros((4, 128), jnp.int32)], axis=0)
    flat = mxu(flat.astype(jnp.float32).astype(jnp.bfloat16), apart).astype(jnp.int32)
    for j, (row, cols) in enumerate(((0, slice(0, 64)), (2, slice(0, 64)), (0, slice(64, 128)), (2, slice(64, 128)))):
        r.label[j : j + 1, :] = jnp.concatenate([flat[row : row + 1, cols], flat[row + 1 : row + 2, cols]], axis=1)
    r.label[4:8, :] = jnp.zeros((4, 128), jnp.int32)
    r.labels_all[place.blk] = r.label[...]
    await_all(met)
    halo = [
        remote(r.x.at[pl.ds(0, 16)], r.after, r.x_send.at[0], r.x_recv.at[0], peers[shards - 2]),
        remote(r.x.at[pl.ds(length - 16, 16)], r.before, r.x_send.at[1], r.x_recv.at[1], peers[0]),
    ]
    for copy in halo:
        copy.start()
    for step in [1, shards - 1] + list(range(2, shards - 1)):
        label_copy(step, place.blk).start()
    weights = [pltpu.make_async_copy(src, dst, r.w_sem.at[k]) for k, (src, dst) in enumerate(((r.wq_hbm, r.wq), (r.wk_hbm, r.wk), (r.wv_hbm, r.wv)))]
    for copy in weights:
        copy.start()
    work = RowForward(place, r)
    make_bias(work.table, core, r.near, (0,))
    left, right = label_come(1), label_come(shards - 1)
    taps = label_taps(place, r.label[...], left, right)
    for j in range(8):
        r.labels[j : j + 1, :] = taps[j]
    for copy in halo:
        copy.wait()
    load_bytes(r.x, r.before[14:16, :], r.after[0:2, :], r.xs)
    r.hidden[...], n1 = pool_tokens(scale, r.xs, taps, row_of(r.vectors, 0).astype(jnp.bfloat16), row_of(r.vectors, 1), tokens, r.y, r.share)
    r.n1[...] = n1
    for copy in weights:
        copy.wait()
    put_packed(mxu(n1, r.wq[...]).astype(jnp.bfloat16) * jnp.bfloat16(0.125), r.q)
    queries = Line(place, r.q, r.q_all, r.q_send, r.q_recv)
    queries.keep().start()
    queries.start()
    put_pairs(mxu(n1, r.wk[...]).astype(jnp.bfloat16), mxu(n1, r.wv[...]).astype(jnp.bfloat16), r.kv)

    def held(dz, off, core_off):
        rest = flipped(place.rest, 2) if off else place.rest
        rest = flipped(rest, 1) if core_off else rest
        start = pl.multiple_of(place.chunk((place.group + dz) % GROUPS, rest) * tokens, tokens)
        return r.kv_all.at[pl.ds(start, tokens)]

    def sem_of(dz, off, core_off):
        return r.kv_recv.at[(core_off * 2 + off) * GROUPS + dz]

    waits = []

    def send(src, dz, off, came, target):
        copy = remote(src, held(dz, off, 0), r.kv_send.at[len(waits)], sem_of(*came), target)
        copy.start()
        waits.append(copy)

    def arrived(dz, off, core_off=0):
        here = held(dz, off, core_off)
        remote(here, here, r.kv_send.at[0], sem_of(dz, off, core_off), core_to).wait_recv()

    def pass_on(dz, off):
        mine = dz == 0 and off == 0
        if not mine:
            arrived(dz, off)
        src = r.kv.at[place.group] if mine else held(dz, off, 0)
        if not off:
            send(src, dz, off, (dz, 1, 0), across)
        send(src, dz, off, (dz, off, 1), core_to)

    def along(step):
        copy = remote(r.kv.at[(place.group + step) % GROUPS], held(0, 0, 0), r.z_send.at[step], sem_of((GROUPS - step) % GROUPS, 0, 0), place.other_group(step))
        copy.start()
        return copy

    left_over = []

    def leave(src, dst):
        copy = pltpu.make_async_copy(src, dst, r.out_sem.at[len(left_over)])
        copy.start()
        left_over.append(copy)

    def line_of(block):
        return jnp.concatenate([block[0:1], block[1:2]], axis=1)

    def tile(dz, off):
        group = (place.group + dz) % GROUPS
        for c in range(2):
            number = place.chunk(group, (1 - y if off else y) * 2 + c)
            rows = pl.ds(pl.multiple_of(number * tokens, tokens), tokens)
            r.kl[rows, :] = label_features(line_of(r.labels_all[number]), True)
        arrived(dz, off, 1)
        t = group * 2 + (1 - y if off else y)
        rows = pl.ds(pl.multiple_of(t * TK, TK), TK)
        leave(r.kv_all.at[rows], r.kv_out.at[rows])
        leave(r.kl.at[rows], r.kl_out.at[rows])
        work.tile(t)

    leave(r.hidden, r.hidden_out)
    leave(r.n1, r.n1_out)
    own = pltpu.make_async_copy(r.kv.at[place.group], held(0, 0, 0), r.own_sem)
    own.start()
    pass_on(0, 0)
    make_bias(work.table, core, r.near, (1,))
    leave(r.near, r.near_out)
    work.clear()
    for step in range(2, shards - 1):
        label_copy(step, (place.blk + shards - step) % shards).wait_recv()
    for z in range(GROUPS):
        r.ql[z] = label_features(line_of(r.labels_all[place.chunk(z, place.rest)]), False) * jnp.bfloat16(NEG)
    pass_on(0, 1)
    for step in (1, 3, 2):
        queries.gone(step)
    first = [along(1), along(3)]
    queries.come_all()
    for z in range(GROUPS):
        work.queries(z)
    own.wait()
    tile(0, 0)
    for copy in first:
        copy.wait_send()
    last = along(2)
    pass_on(1, 0)
    pass_on(3, 0)
    tile(0, 1)
    tile(1, 0)
    pass_on(1, 1)
    pass_on(3, 1)
    tile(3, 0)
    tile(1, 1)
    pass_on(2, 0)
    tile(3, 1)
    pass_on(2, 1)
    tile(2, 0)
    tile(2, 1)
    last.wait_send()
    work.end()
    for copy in waits:
        copy.wait_send()
    for step in range(1, shards):
        label_copy(step, place.blk).wait_send()
    for copy in left_over:
        copy.wait()


def front(shards, scale, table, x, segments, vectors, wq, wk, wv):
    length, features = x.shape
    tokens, heads = length // 2, features // 64 // GROUPS
    width = heads * 128
    sem, f32, low = pltpu.SemaphoreType.DMA, jnp.float32, jnp.bfloat16
    mem = lambda shape, dtype=low: pltpu.VMEM(shape, dtype)
    packed = (GROUPS, tokens * 3 // 2, 128)
    ins = dict(
        table=Held(table, pltpu.SMEM), x=x, segments=segments, vectors=vectors,
        wq_hbm=Held(wq, pl.ANY), wk_hbm=Held(wk, pl.ANY), wv_hbm=Held(wv, pl.ANY),
    )
    outs = dict(
        q_all=(packed, low), kv_out=((shards * tokens, width), low, pl.ANY), kl_out=((shards * tokens, 128), low, pl.ANY), ql=((GROUPS, tokens, 128), low),
        near_out=((heads, 2, TK, TQ), low, pl.ANY), o=(packed, low), keep=(packed, f32), lse=((GROUPS, heads, 1, TQ), f32),
        hidden_out=((tokens, features), f32, pl.ANY), n1_out=((tokens, features), low, pl.ANY), y=((8, tokens), f32), share=((1, 128), f32),
        labels=((8, tokens), jnp.int32), before=((16, features), low), after=((16, features), low),
    )
    scratch = dict(
        kv_all=mem((shards * tokens, width)), kl=mem((shards * tokens, 128)), near=mem((heads, 2, TK, TQ)),
        hidden=mem((tokens, features), f32), n1=mem((tokens, features)), out_sem=sem((19,)),
        q=mem(packed), kv=mem((GROUPS, tokens, width)), xs=mem((features // 128, length + 2 * LEAD, 128), f32),
        wq=mem(wq.shape), wk=mem(wk.shape), wv=mem(wv.shape), label=mem((8, 128), jnp.int32), labels_all=mem((shards, 8, 128), jnp.int32),
        qp=mem((GROUPS, heads, TQ, 256)), acc=mem((GROUPS, heads, 80, TQ), f32), mx=mem((GROUPS, heads, 1, TQ), f32), vt=mem((heads, 80, TK)),
        q_send=sem((4,)), q_recv=sem((4,)), kv_send=sem((12,)), z_send=sem((GROUPS,)), kv_recv=sem((16,)), own_sem=sem,
        lab_send=sem((shards,)), lab_recv=sem((shards,)), x_send=sem((2,)), x_recv=sem((2,)), w_sem=sem((3,)),
    )
    return call(functools.partial(front_kernel, shards, scale), 7, ins, outs, scratch)


def middle_kernel(shards, r):
    place = Place(shards)
    met = hail([place.other_group(step) for step in (1, 2, 3)] + [place.other_rest(1)])
    pairs = ((r.wo_hbm, r.wo), (r.wg_hbm, r.wg), (r.wu_hbm, r.wu), (r.wd_hbm, r.wd))
    fetches = [pltpu.make_async_copy(src, dst, r.w_sem.at[k]) for k, (src, dst) in enumerate(pairs)]
    for copy in fetches:
        copy.start()
    await_all(met)
    home = Line(place, r.o, r.o_home, r.o_send, r.o_recv)
    home.keep().start()
    home.start()
    for copy in fetches:
        copy.wait()
    home.wait_all()
    r.gain[...] = row_of(r.vectors, 2)
    feed_kernel(r.o_home, r.hidden, r.ct, r.gain, r.wo, r.wg, r.wu, r.wd, r.block_out, r.dres, r.da, r.dgain,
                r.n2, r.att, r.act, r.dg, r.du, r.db, r.acc, r.dn2)
    away = Line(place, r.da, r.do, r.q_send, r.q_recv)
    away.keep().start()
    away.start()
    feed_weights(place, r.n2, r.att, r.act, r.dg, r.du, r.ct, r.db, r.sums,
                 r.core_send, r.core_recv, r.gate, r.up, r.down, r.out, r.wide_out, r.slim_out, r.wide_in, r.slim_in)
    away.wait_all()


def middle(shards, o_packed, hidden, ct, vectors, wo, wg, wu, wd):
    tokens, width = hidden.shape
    ff = wg.shape[1]
    per, per_ff = width // 32, ff // 32
    sem, low, f32 = pltpu.SemaphoreType.DMA, jnp.bfloat16, jnp.float32
    half = o_packed.shape[1:]
    wide_cols = ff + width // 2
    first = (wide_cols // 256 + 1) * 128
    ins = dict(o=o_packed, hidden=hidden, ct=ct, vectors=vectors, wo_hbm=Held(wo, pl.ANY), wg_hbm=Held(wg, pl.ANY), wu_hbm=Held(wu, pl.ANY), wd_hbm=Held(wd, pl.ANY))
    outs = dict(
        block_out=((tokens, width), low), dres=((tokens, width), f32), dgain=((1, width), f32), do=((GROUPS,) + half, low),
        sums=[((16, 2 * per, first), low), ((16, 2 * per, wide_cols - first), low), ((16, per_ff, width), low)],
    )
    mem = lambda shape, dtype=low: pltpu.VMEM(shape, dtype)
    scratch = dict(
        gain=mem((1, width), f32), o_home=mem((GROUPS,) + half), da=mem((GROUPS,) + half),
        n2=mem((tokens, width)), att=mem((tokens, width)), db=mem((tokens, width)),
        act=mem((tokens, ff)), dg=mem((tokens, ff)), du=mem((tokens, ff)),
        acc=mem((tokens, width), f32), dn2=mem((tokens, width), f32),
        wo=mem(wo.shape), wg=mem(wg.shape), wu=mem(wu.shape), wd=mem(wd.shape),
        gate=mem((width, ff), f32), up=mem((width, ff), f32), down=mem((ff, width), f32), out=mem((width, width), f32),
        wide_out=mem((16, 2 * per, wide_cols)), slim_out=mem((16, per_ff, width)),
        wide_in=mem((16, 2 * per, wide_cols)), slim_in=mem((16, per_ff, width)),
        w_sem=sem((4,)), o_send=sem((4,)), o_recv=sem((4,)), q_send=sem((4,)), q_recv=sem((4,)),
        core_send=sem((2,)), core_recv=sem((2,)),
    )
    return call(functools.partial(middle_kernel, shards), 8, ins, outs, scratch)


def neighbours(rows):
    peers = lax.axis_size("blk")
    up = [(i, i + 1) for i in range(peers - 1)]
    last, leading = rows
    return lax.ppermute(last, "blk", up), lax.ppermute(leading, "blk", [(j, i) for i, j in up])


def body(
    byte_embeds,
    segments,
    score_weight,
    norm_gain1,
    w_query,
    w_key,
    w_value,
    w_out,
    rel_bias,
    norm_gain2,
    w_gate,
    w_up,
    w_down,
    cotangent,
):
    row_count, length, width = byte_embeds.shape
    tokens = length // 2
    shards = lax.axis_size("blk")
    shape = {"dp": lax.axis_size("dp"), "blk": shards}
    devices = shards * shape["dp"]
    heads = rel_bias.shape[1] // GROUPS
    position = lax.axis_index("blk")
    rest_size = shards // GROUPS
    group, rest = position // rest_size, position % rest_size
    row = lax.axis_index("dp") % 2
    x, ids_here = byte_embeds[0], segments[0]

    ct = cotangent[0]
    scale = 1.0 / (row_count * length * devices)
    if devices == 32:
        vectors = jnp.concatenate([score_weight, norm_gain1, norm_gain2]).astype(jnp.float32).reshape(-1, 128)
        table = rel_bias.T.astype(jnp.float32)
        got = front(shards, scale, table, x, segments, vectors, w_query, w_key, w_value)
        mid = middle(shards, got.o, got.hidden_out, ct, vectors, w_out, w_gate, w_up, w_down)
        block_out, d_res, d_gain2 = mid.block_out, mid.dres, mid.dgain
        last = back_and_last(
            shape,
            mid.sums,
            dict(
                table=Held(table, pltpu.SMEM), q=got.q_all, do=mid.do, keep=got.keep, kv_hbm=Held(got.kv_out, pl.ANY),
                kl_hbm=Held(got.kl_out, pl.ANY), ql=got.ql, bias=got.near_out, lse=got.lse,
                hidden_hbm=Held(got.hidden_out, pl.ANY), dres_hbm=Held(d_res, pl.ANY), n1_hbm=Held(got.n1_out, pl.ANY), x_hbm=Held(x, pl.ANY), before=got.before, after=got.after,
                labels=got.labels, y=got.y, vectors=vectors,
                wq_hbm=Held(w_query, pl.ANY), wk_hbm=Held(w_key, pl.ANY), wv_hbm=Held(w_value, pl.ANY), dgain2=d_gain2, share=got.share,
            ),
        )
        grad_bytes, edge, spill, small, sums = last.gb, last.edge, last.spill_out, last.small_out, last.sums
    else:
        marks = (ids_here + 1).astype(jnp.bfloat16)
        with_marks = lambda part, two: jnp.concatenate([part, jnp.pad(two, (0, width - 2))[None]], axis=0)
        before, after = neighbours((with_marks(x[-2:], marks[-2:]), with_marks(x[:2], marks[:2])))
        line = jnp.concatenate([before[2, :2], marks, after[2, :2]])
        line = jnp.pad(line, (1, 1)).astype(jnp.int32).reshape(tokens + 3, 2).T
        labels = jnp.stack([line[j % 2, j // 2 : j // 2 + tokens] for j in range(8)])

        score_row, gain1, gain2 = score_weight[None], norm_gain1[None], norm_gain2[None]
        hidden, n1, y, share, q_packed, kv_parts = pool_and_project(
            shards, scale, x, before, after, labels, score_row, gain1, w_query, w_key, w_value
        )

        label_block = jnp.pad(ids_here[0::2].reshape(tokens // 128, 128), ((0, 8 - tokens // 128), (0, 0)), constant_values=-1)
        table = lax.dynamic_slice_in_dim(rel_bias.astype(jnp.float32).T, group * heads, heads, 0)
        q_all, kv_all, labels_all = gather_all(shards, q_packed, kv_parts, label_block)
        labels_all = labels_all.reshape(2, shards, 8, 128)[:, :, : tokens // 128].reshape(2, shards * tokens)
        ids = jnp.arange(8, dtype=jnp.int32)
        counts = jnp.sum((labels_all[:, None, :] == ids[None, :, None]).astype(jnp.int32), axis=2)
        ends = jnp.sum(jnp.where(ids[None, :] <= ids[:, None], counts[:, None, :], 0), axis=2)
        begins = ends - counts
        query_labels = jnp.stack(
            [lax.dynamic_slice_in_dim(labels_all, ((2 * row + i) * rest_size + rest) * tokens, tokens, 1) for i in range(2)],
            axis=1,
        )
        chosen = query_labels[:, :, None, :] == ids[None, None, :, None]
        span = jnp.stack(
            [jnp.sum(jnp.where(chosen, edge[:, None, :, None], 0), axis=2) for edge in (begins, ends)], axis=2
        )
        parity = rest % 2
        firsts = jnp.stack([((2 * row + i) * rest_size + rest) * tokens for i in range(2)])
        near = jnp.broadcast_to((firsts // TK - 1 + parity)[None], (2, 2))
        bounds = jnp.stack(
            [
                jnp.min(span[:, :, 0], axis=-1) // TK,
                -(-jnp.max(span[:, :, 1], axis=-1) // TK),
                near,
                -(-jnp.max(span[:, :, 0], axis=-1) // TK),
                jnp.min(span[:, :, 1], axis=-1) // TK,
                jnp.broadcast_to(parity, (2, 2)),
                jnp.broadcast_to((labels_all[0, -1] > 0).astype(jnp.int32), (2, 2)),
            ],
            axis=-1,
        ).astype(jnp.int32)
        o_packed, o_kept, log_total, near_bias = attention(bounds, table, q_all, kv_all, span)
        o_home = move_heads(return_kernel, (GROUPS,), shards, 4, o_packed)
        block_out, d_res, da_packed, d_gain2, n2, att, act, d_gate, d_up, d_branch = feed_forward(
            o_home, hidden, ct, gain2, w_out, w_gate, w_up, w_down
        )
        do_all = move_heads(spread_kernel, (2, 2), shards, 5, da_packed)
        dq_packed, dkv_all, _, _, _, d_table_lanes = attention_back(
            False, bounds, table, q_all, do_all, o_kept, kv_all, near_bias, span, log_total
        )
        dq_home, dkv_home = reduce_all(shape, dq_packed, dkv_all, [], [])
        grad_bytes, edge, spill, small, last_parts = last_part(
            shape, dq_home, dkv_home, hidden, d_res, x, before, after, labels, y,
            score_row, gain1, w_query, w_key, w_value, d_gain2, share, d_table_lanes,
        )
        sums = []
    per = width // devices
    block_out, grad_bytes, g_score, g_gain1, g_gain2, g_bias, shares, *grads = finish(
        shards, rel_bias.shape[1], per, w_gate.shape[1], block_out, grad_bytes, edge, spill, small, sums
    )
    if devices != 32:
        product = lambda left, right: jnp.einsum("td,te->de", left, right, preferred_element_type=jnp.float32)
        grads = [product(n1, last_parts[j]) for j in range(3)]
        grads += [product(att, d_branch), product(n2, d_gate), product(n2, d_up), product(act, ct)]
        grads = [lax.psum_scatter(grad, ("dp", "blk"), scatter_dimension=0, tiled=True) for grad in grads]
    return (
        block_out[None],
        grad_bytes[None],
        g_score,
        g_gain1,
        *grads[:4],
        g_bias.T,
        g_gain2,
        *grads[4:],
        shares,
    )


def solution(mesh):
    placed = (
        P("dp", "blk", None),
        P("dp", "blk"),
        P(),
        P(),
        P(),
        P(),
        P(),
        P(),
        P(),
        P(),
        P(),
        P(),
        P(),
        P("dp", "blk", None),
    )
    return jax.shard_map(
        body,
        mesh=mesh,
        in_specs=placed,
        out_specs=(
            P("dp", "blk", None),
            P("dp", "blk", None),
            P(),
            P(),
            P(("dp", "blk"), None),
            P(("dp", "blk"), None),
            P(("dp", "blk"), None),
            P(("dp", "blk"), None),
            P(),
            P(),
            P(("dp", "blk"), None),
            P(("dp", "blk"), None),
            P(("dp", "blk"), None),
            P(),
        ),
        check_vma=False,
    )
```

```python
import functools
import math

import jax
import jax.numpy as jnp
from jax import lax
from jax.experimental import pallas as pl
from jax.experimental.pallas import tpu as pltpu
from jax.sharding import PartitionSpec as P

BUCKETS = 32
MAX_BLOCK = 4
VMEM_BYTES = 61 * 2**20


def buckets_of(relative):
    distance = jnp.abs(relative)
    beyond = jnp.zeros_like(distance)
    for border in (12, 16, 23, 32, 46, 64, 91):
        beyond = beyond + (distance >= border).astype(jnp.int32)
    nearer = jnp.where(distance < 8, distance, 8 + beyond)
    return nearer + BUCKETS // 2 * (relative > 0).astype(jnp.int32)


MESH_ID = pl.DeviceIdType.MESH
GROUPS = 4


def bits_of(size):
    return [1 << p for p in reversed(range(size.bit_length() - 1))]


def bit(value, mask):
    return (value // mask) % 2


def flipped(value, mask):
    return value + mask * (1 - 2 * bit(value, mask))


class Place:
    def __init__(self, shards):
        self.shards = shards
        self.rest_size = shards // GROUPS
        self.dp = lax.axis_index("dp")
        self.blk = lax.axis_index("blk")
        self.row = self.dp % 2
        self.group = self.blk // self.rest_size
        self.rest = self.blk % self.rest_size

    def at(self, row, group, rest):
        return (self.dp - self.row + row, group * self.rest_size + rest)

    def chunk(self, group, rest):
        return group * self.rest_size + rest

    def other_row(self):
        return self.at(1 - self.row, self.group, self.rest)

    def other_rest(self, mask):
        return self.at(self.row, self.group, flipped(self.rest, mask))

    def other_group(self, step):
        return self.at(self.row, (self.group + step) % GROUPS, self.rest)


def hail(targets):
    barrier = pltpu.get_barrier_semaphore()
    for target in targets:
        pl.semaphore_signal(barrier, inc=1, device_id=target, device_id_type=MESH_ID)
    return len(targets)


def await_all(count):
    pl.semaphore_wait(pltpu.get_barrier_semaphore(), count)


def greet(targets):
    await_all(hail(targets))


def remote(src, dst, send_sem, recv_sem, target):
    return pltpu.make_async_remote_copy(
        src_ref=src,
        dst_ref=dst,
        send_sem=send_sem,
        recv_sem=recv_sem,
        device_id=target,
        device_id_type=MESH_ID,
    )


def line_and_row(place):
    found = []
    for step in range(GROUPS):
        for flip in range(2):
            if step or flip:
                row = 1 - place.row if flip else place.row
                found.append(place.at(row, (place.group + step) % GROUPS, place.rest))
    return found


def spread_heads(place, q_ref, out_ref, send_sem, recv_sem):
    row_to = place.group // 2
    slot = place.group % 2
    dst = out_ref.at[place.row, slot]
    mine = recv_sem.at[place.row * 2 + slot]
    at_home = row_to == place.row
    for step in range(GROUPS):
        group = (place.group + step) % GROUPS
        src = q_ref.at[group]
        copy = remote(src, dst, send_sem.at[step], mine, place.at(row_to, group, place.rest))
        if step:
            copy.start()
        else:
            pl.when(jnp.logical_not(at_home))(copy.start)
            pl.when(at_home)(pltpu.make_async_copy(src, dst, mine).start)


def spread_heads_come(q_ref, out_ref, recv_sem):
    for row in range(2):
        for slot in range(2):
            pltpu.make_async_copy(q_ref.at[0], out_ref.at[row, slot], recv_sem.at[row * 2 + slot]).wait()


def spread_heads_gone(place, q_ref, out_ref, send_sem, recv_sem):
    at_home = place.group // 2 == place.row
    for step in range(GROUPS):
        copy = remote(q_ref.at[0], out_ref.at[0, 0], send_sem.at[step], recv_sem.at[0], place.other_row())
        if step:
            copy.wait_send()
        else:
            pl.when(jnp.logical_not(at_home))(copy.wait_send)


def spread_heads_wait(place, q_ref, out_ref, send_sem, recv_sem):
    spread_heads_come(q_ref, out_ref, recv_sem)
    spread_heads_gone(place, q_ref, out_ref, send_sem, recv_sem)


def return_heads(place, o_ref, out_ref, send_sem, recv_sem):
    for row in range(2):
        for slot in range(2):
            group = place.row * 2 + slot
            src = o_ref.at[row, slot]
            dst = out_ref.at[place.group]
            mine = recv_sem.at[place.group]
            at_home = jnp.logical_and(place.row == row, place.group == group)
            copy = remote(src, dst, send_sem.at[row * 2 + slot], mine, place.at(row, group, place.rest))
            pl.when(jnp.logical_not(at_home))(copy.start)
            pl.when(at_home)(pltpu.make_async_copy(src, dst, mine).start)


def return_heads_wait(place, o_ref, out_ref, send_sem, recv_sem):
    for group in range(GROUPS):
        pltpu.make_async_copy(o_ref.at[0, 0], out_ref.at[group], recv_sem.at[group]).wait()
    for row in range(2):
        for slot in range(2):
            group = place.row * 2 + slot
            at_home = jnp.logical_and(place.row == row, place.group == group)
            copy = remote(o_ref.at[0, 0], out_ref.at[0], send_sem.at[row * 2 + slot], recv_sem.at[0], place.other_row())
            pl.when(jnp.logical_not(at_home))(copy.wait_send)


def spread_kernel(shards, q_ref, out_ref, send_sem, recv_sem):
    place = Place(shards)
    greet(line_and_row(place))
    spread_heads(place, q_ref, out_ref, send_sem, recv_sem)
    spread_heads_wait(place, q_ref, out_ref, send_sem, recv_sem)


def return_kernel(shards, o_ref, out_ref, send_sem, recv_sem):
    place = Place(shards)
    greet(line_and_row(place))
    return_heads(place, o_ref, out_ref, send_sem, recv_sem)
    return_heads_wait(place, o_ref, out_ref, send_sem, recv_sem)


SMEM_SPEC = pl.BlockSpec(memory_space=pltpu.SMEM)
VMEM_SPEC = pl.BlockSpec(memory_space=pltpu.VMEM)
ANY_SPEC = pl.BlockSpec(memory_space=pl.ANY)


def move_heads(kernel, lead, shards, ident, packed):
    rows, lanes = packed.shape[-2:]
    return pl.pallas_call(
        functools.partial(kernel, shards),
        out_shape=jax.ShapeDtypeStruct(lead + (rows, lanes), packed.dtype),
        in_specs=[pl.BlockSpec(memory_space=pltpu.VMEM)],
        out_specs=pl.BlockSpec(memory_space=pltpu.VMEM),
        scratch_shapes=[pltpu.SemaphoreType.DMA((4,)), pltpu.SemaphoreType.DMA((4,))],
        compiler_params=pltpu.CompilerParams(collective_id=ident, has_side_effects=True, vmem_limit_bytes=VMEM_BYTES),
        name="move_heads_%d" % ident,
    )(packed)


def gather_kernel(shards, q_ref, kv_ref, label_ref, qo_ref, kvo_ref, labo_ref, q_send, q_recv, z_send, far_send, core_send, kv_recv, own_sem, lab_send, lab_recv):
    place = Place(shards)
    tokens = kv_ref.shape[1]
    rest_bits = bits_of(place.rest_size)
    core, far = rest_bits[-1], ["row"] + rest_bits[:-1]
    greet(line_and_row(place) + [place.other_rest(mask) for mask in rest_bits])

    dims = [("row", 1)] + [("blk", m) for m in bits_of(shards)]
    lab_index = [place.row] + [bit(place.blk, m) for _, m in dims[1:]]
    lab_order = list(range(len(dims)))

    def lab_copy(stage):
        index = tuple(slice(None) if p in lab_order[:stage] else lab_index[p] for p in range(len(dims)))
        axis, mask = dims[lab_order[stage]]
        target = place.other_row() if axis == "row" else (place.dp, flipped(place.blk, mask))
        there = labo_ref.at[index]
        return remote(there, there, lab_send.at[stage], lab_recv.at[stage], target)

    labo_ref[tuple(lab_index)] = label_ref[...]
    lab_copy(0).start()
    lab_stage = 0

    def slot(row, group, rest):
        start = pl.multiple_of(place.chunk(group, rest) * tokens, tokens)
        return kvo_ref.at[row, pl.ds(start, tokens)]

    def held(dz, offset, core_off):
        row = 1 - place.row if offset & 1 else place.row
        rest = place.rest
        for p, mask in enumerate(far[1:]):
            if offset >> (p + 1) & 1:
                rest = flipped(rest, mask)
        if core_off:
            rest = flipped(rest, core)
        return slot(row, (place.group + dz) % GROUPS, rest)

    count = 1 << len(far)

    def sem_of(dz, offset, core_off):
        return kv_recv.at[(core_off * count + offset) * GROUPS + dz]

    own = pltpu.make_async_copy(kv_ref.at[place.group], held(0, 0, 0), own_sem)
    own.start()
    waits = []
    for step in (1, 3, 2):
        copy = remote(kv_ref.at[(place.group + step) % GROUPS], held(0, 0, 0), z_send.at[step], sem_of((GROUPS - step) % GROUPS, 0, 0), place.other_group(step))
        copy.start()
        waits.append(copy)

    used = 0
    events = sorted(((dz, off) for dz in range(GROUPS) for off in range(count)), key=lambda e: (bin(e[1]).count("1"), (0, 1, 3, 2).index(e[0])))
    core_target = place.other_rest(core)
    for step, (dz, off) in enumerate(events):
        if step == GROUPS:
            spread_heads(place, q_ref, qo_ref, q_send, q_recv)
        here = held(dz, off, 0)
        if dz == 0 and off == 0:
            src = kv_ref.at[place.group]
        else:
            remote(here, here, z_send.at[0], sem_of(dz, off, 0), core_target).wait_recv()
            src = here
        order = [(p + dz) % len(far) for p in range(len(far))]
        last = max([order.index(p) for p in range(len(far)) if off >> p & 1], default=-1)
        for p in order[last + 1 :]:
            target = place.other_row() if p == 0 else place.other_rest(far[p])
            copy = remote(src, here, far_send.at[used], sem_of(dz, off | 1 << p, 0), target)
            copy.start()
            waits.append(copy)
            used += 1
        copy = remote(src, here, core_send.at[off * GROUPS + dz], sem_of(dz, off, 1), core_target)
        copy.start()
        waits.append(copy)
        if lab_stage < len(dims):
            lab_copy(lab_stage).wait()
            lab_stage += 1
            if lab_stage < len(dims):
                lab_copy(lab_stage).start()
    for dz, off in events:
        here = held(dz, off, 1)
        remote(here, here, z_send.at[0], sem_of(dz, off, 1), core_target).wait_recv()
    own.wait()
    for copy in waits:
        copy.wait_send()
    spread_heads_wait(place, q_ref, qo_ref, q_send, q_recv)


def gather_all(shards, q_packed, kv_parts, labels):
    tokens, width = kv_parts.shape[1:]
    far = 1 + len(bits_of(shards // GROUPS)) - 1
    count = 1 << far
    nbits = 1 + len(bits_of(shards))
    sem = pltpu.SemaphoreType.DMA
    return pl.pallas_call(
        functools.partial(gather_kernel, shards),
        out_shape=(
            jax.ShapeDtypeStruct((2, 2) + q_packed.shape[1:], q_packed.dtype),
            jax.ShapeDtypeStruct((2, shards * tokens, width), kv_parts.dtype),
            jax.ShapeDtypeStruct((2,) * nbits + labels.shape, labels.dtype),
        ),
        in_specs=[pl.BlockSpec(memory_space=pltpu.VMEM)] * 3,
        out_specs=(pl.BlockSpec(memory_space=pltpu.VMEM),) * 3,
        scratch_shapes=[
            sem((4,)), sem((4,)), sem((GROUPS,)), sem((GROUPS * (count - 1),)), sem((GROUPS * count,)), sem((GROUPS * count * 2,)),
            sem, sem((nbits,)), sem((nbits,)),
        ],
        compiler_params=pltpu.CompilerParams(collective_id=1, has_side_effects=True, vmem_limit_bytes=VMEM_BYTES),
        name="gather_keys",
    )(q_packed, kv_parts, labels)


def add_blocks(dst_ref, src_ref, index, shape):
    lead = shape[:-2]
    total = math.prod(lead)

    def one(step, _):
        place, left = [], step
        for size in reversed(lead):
            place.append(left % size)
            left = left // size
        place = tuple(reversed(place))
        full, k = [], 0
        for entry in index:
            if entry is None:
                full.append(place[k])
                k += 1
            else:
                full.append(entry)
        dst_ref[place] = dst_ref[place] + src_ref[tuple(full)]
        return 0

    lax.fori_loop(0, total, one, 0)


class Stream:
    def __init__(self, axes, at, kept, order, src, half, bufs, out, send_sem, recv_sem):
        self.axes, self.at, self.kept, self.order = axes, at, kept, order
        self.half = half
        self.src, self.bufs, self.out = src, bufs, out
        self.send_sem, self.recv_sem = send_sem, recv_sem

    def own(self, p):
        axis, mask = self.axes[p]
        return bit(self.at[axis], mask)

    def target(self, p):
        axis, mask = self.axes[p]
        moved = dict(self.at)
        moved[axis] = flipped(self.at[axis], mask)
        return (moved["dp"], moved["blk"])

    def stage(self, k):
        kept = [p for p in self.kept if p not in self.order[:k]]
        return kept, self.src if k == 0 else self.bufs[k - 1], self.order[k]

    def copy(self, k):
        kept, src, now = self.stage(k)
        index = tuple(1 - self.own(p) if p == now else slice(None) for p in kept)
        return remote(src.at[index], self.bufs[k], self.send_sem.at[k], self.recv_sem.at[k], self.target(now))

    def absorb(self, k):
        kept, src, now = self.stage(k)
        buf = self.bufs[k]
        if k == len(self.order) - 1 and self.out is not None:
            mine = src[self.own(now)].astype(jnp.float32)
            self.out[...] = buf[...].astype(jnp.float32) + mine
        else:
            half = k == 0 and self.half is not None
            index = tuple(self.own(p) if p == now else None for p in kept if p != now or not half)
            add_blocks(buf, self.half if half else src, index, buf.shape)


class Whole:
    def __init__(self, axes, at, order, src, bufs, out, send_sem, recv_sem):
        self.stream = Stream(axes, at, order, order, src, None, bufs, out, send_sem, recv_sem)
        self.order, self.src, self.bufs, self.out = order, src, bufs, out

    def held(self, k):
        return self.src if k == 0 else self.bufs.at[1, k - 1]

    def copy(self, k):
        s = self.stream
        return remote(self.held(k), self.bufs.at[0, k], s.send_sem.at[k], s.recv_sem.at[k], s.target(self.order[k]))

    def absorb(self, k):
        total = self.held(k)[...] + self.bufs[0, k]
        if k == len(self.order) - 1:
            self.out[...] = total
        else:
            self.bufs[1, k] = total


def advance(stream, stage):
    if stage < len(stream.order):
        stream.copy(stage).wait()
        stream.absorb(stage)
        if stage < len(stream.order) - 1:
            stream.copy(stage + 1).start()


def bit_axes(shape):
    return [("dp", m) for m in bits_of(shape["dp"])] + [("blk", m) for m in bits_of(shape["blk"])]


def stream_scratch(lead, order, rows, cols):
    return [pltpu.VMEM((2,) * (lead - 1 - k) + (rows, cols), jnp.bfloat16) for k in range(len(order))]


def feed_weights(place, n2_ref, att_ref, act_ref, dg_ref, du_ref, ct_ref, db_ref, sums, outs, out_sem,
                 core_send, core_recv, gate, up, down, out, wide_out, slim_out, wide_in, slim_in):
    core_target = place.other_rest(1)
    per = gate.shape[0] // 32
    per_ff = down.shape[0] // 32
    first = sums[0].shape[2]
    half = out.shape[1] // 2
    core = place.rest % 2

    n2_t = n2_ref[...].T
    step = 512
    for j in range(gate.shape[1] // step):
        cols = slice(j * step, j * step + step)
        gate[:, cols] = mxu(n2_t, dg_ref[:, cols])
        up[:, cols] = mxu(n2_t, du_ref[:, cols])
    out[...] = mxu(att_ref[...].T, db_ref[...])

    def wide_rows(block):
        rows = pl.ds(pl.multiple_of(block * per, 8), per)
        last = jnp.concatenate([out[rows, :half], out[rows, half:]], axis=0)
        return jnp.concatenate([jnp.concatenate([gate[rows, :], up[rows, :]], axis=0), last], axis=1)

    def slim_rows(block):
        return down[pl.ds(pl.multiple_of(block * per_ff, 8), per_ff), :]

    def quarter(ref, k):
        return ref.at[pl.ds(4 * k, 4)]

    def send_wide(m, _):
        wide_out[m] = wide_rows(2 * m + 1 - core).astype(jnp.bfloat16)
        return 0

    def send_slim(m, _):
        slim_out[m] = slim_rows(2 * m + 1 - core).astype(jnp.bfloat16)
        return 0

    wide_copies, slim_copies = [], []
    for k in range(4):
        lax.fori_loop(4 * k, 4 * k + 4, send_wide, 0)
        wide_copies.append(remote(quarter(wide_out, k), quarter(wide_in, k), core_send.at[k], core_recv.at[k], core_target))
        wide_copies[-1].start()
    for j in range(down.shape[0] // step):
        rows = slice(j * step, j * step + step)
        down[rows, :] = mxu(act_ref[:, rows].T, ct_ref[...])
    for k in range(4):
        lax.fori_loop(4 * k, 4 * k + 4, send_slim, 0)
        slim_copies.append(remote(quarter(slim_out, k), quarter(slim_in, k), core_send.at[4 + k], core_recv.at[4 + k], core_target))
        slim_copies[-1].start()

    def sum_wide(m, _):
        total = wide_rows(2 * m + core) + wide_in[m].astype(jnp.float32)
        sums[0][m] = total[:, :first].astype(jnp.bfloat16)
        sums[1][m] = total[:, first:].astype(jnp.bfloat16)
        return 0

    def sum_slim(m, _):
        sums[2][m] = (slim_rows(2 * m + core) + slim_in[m].astype(jnp.float32)).astype(jnp.bfloat16)
        return 0

    gone = []

    def leave(s, k):
        gone.append(pltpu.make_async_copy(quarter(sums[s], k), quarter(outs[s], k), out_sem.at[len(gone)]))
        gone[-1].start()

    for k in range(4):
        wide_copies[k].wait()
        lax.fori_loop(4 * k, 4 * k + 4, sum_wide, 0)
        leave(0, k)
        leave(1, k)
    for k in range(4):
        slim_copies[k].wait()
        lax.fori_loop(4 * k, 4 * k + 4, sum_slim, 0)
        leave(2, k)
    for copy in gone:
        copy.wait()


def reduce_kernel(shards, axes, orders, *refs):
    count = len(orders)
    q_ref, kv_ref = refs[:2]
    pairs = refs[2 : 2 + 2 * count]
    qo_ref, kvo_ref = refs[2 + 2 * count : 4 + 2 * count]
    sums = refs[4 + 2 * count : 4 + 3 * count]
    q_send, q_recv, send_sem, recv_sem, z_send, z_recv, w_send, w_recv = refs[4 + 3 * count : 12 + 3 * count]
    bufs = refs[12 + 3 * count :]
    place = Place(shards)
    rest_bits = bits_of(place.rest_size)
    greet(line_and_row(place) + [place.other_rest(mask) for mask in rest_bits])
    return_heads(place, q_ref, qo_ref, q_send, q_recv)
    ndim = 1 + len(rest_bits)
    at = {"dp": place.dp, "blk": place.blk}
    streams, used = [], ndim
    for s, (kept, order) in enumerate(orders):
        src, more = bufs[used], bufs[used + 1 : used + 1 + len(order)]
        used += 1 + len(order)
        streams.append(Stream(axes, at, kept, order, src, more, sums[s], w_send.at[s], w_recv.at[s]))
    own = [place.row] + [bit(place.rest, m) for m in rest_bits]
    targets = [place.other_row()] + [place.other_rest(m) for m in rest_bits]
    state = {}

    def plan(group_step):
        far = list(range(ndim - 1))
        turn = group_step % len(far)
        return [ndim - 1] + far[turn:] + far[:turn]

    def copy_of(step, stage):
        order = plan(step)
        group = (place.group + step) % GROUPS
        done = order[:stage]
        p_now = order[stage]
        buf = bufs[stage].at[step]
        if stage == 0:
            index = (p_index(group, done, p_now))
            src = kv_ref.at[index]
        else:
            kept = [p for p in range(ndim) if p not in done]
            src = bufs[stage - 1].at[(step,) + tuple(1 - own[p] if p == p_now else slice(None) for p in kept)]
        return remote(src, buf, send_sem.at[stage, step], recv_sem.at[stage, step], targets[p_now])

    def p_index(group, done, p_now):
        index = [slice(None)] * ndim
        index[p_now] = 1 - own[p_now]
        return (index[0], group) + tuple(index[1:])

    def absorb(step, stage):
        order = plan(step)
        done, p_now = order[:stage], order[stage]
        buf = bufs[stage].at[step]
        group = (place.group + step) % GROUPS
        if stage == 0:
            index = [None] * ndim
            index[p_now] = own[p_now]
            add_blocks(buf, kv_ref, (index[0], group) + tuple(index[1:]), buf.shape)
        else:
            kept = [p for p in range(ndim) if p not in done]
            index = tuple(own[p] if p == p_now else None for p in kept)
            add_blocks(buf, bufs[stage - 1].at[step], index, buf.shape)

    steps = (2, 1, 3, 0)
    for step in steps:
        copy_of(step, 0).start()
    for s, stream in enumerate(streams):
        add_two(stream.src, pairs[2 * s], pairs[2 * s + 1])
        stream.copy(0).start()
    for stage in range(ndim):
        for step in steps:
            copy_of(step, stage).wait()
            absorb(step, stage)
            if stage < ndim - 1:
                copy_of(step, stage + 1).start()
            elif step:
                remote(bufs[stage].at[step], kvo_ref.at[place.group], z_send.at[step], z_recv.at[(GROUPS - step) % GROUPS], place.other_group(step)).start()
            else:
                kvo_ref[place.group] = bufs[stage][step]
        for stream in streams:
            if stage < len(stream.order):
                stream.copy(stage).wait()
                stream.absorb(stage)
                if stage < len(stream.order) - 1:
                    stream.copy(stage + 1).start()
    for step in (1, 3, 2):
        there = kvo_ref.at[(place.group + step) % GROUPS]
        remote(bufs[ndim - 1].at[step], there, z_send.at[step], z_recv.at[step], place.other_group(step)).wait()
    return_heads_wait(place, q_ref, qo_ref, q_send, q_recv)


def add_two(dst_ref, one_ref, two_ref):
    lead = dst_ref.shape[:-2]

    def one(step, _):
        place, left = [], step
        for size in reversed(lead):
            place.append(left % size)
            left = left // size
        place = tuple(reversed(place))
        dst_ref[place] = (one_ref[place].astype(jnp.float32) + two_ref[place].astype(jnp.float32)).astype(dst_ref.dtype)
        return 0

    lax.fori_loop(0, math.prod(lead), one, 0)


def reduce_all(shape, q_packed, kv_sums, orders, pairs):
    shards = shape["blk"]
    tokens_all, width = kv_sums.shape[1:]
    tokens = tokens_all // shards
    rest_bits = bits_of(shards // GROUPS)
    ndim = 1 + len(rest_bits)
    sem = pltpu.SemaphoreType.DMA
    scratch = [pltpu.VMEM((GROUPS,) + (2,) * (ndim - 1 - s) + (tokens, width), kv_sums.dtype) for s in range(ndim)]
    flat, sums = [], []
    for (kept, order), pair in zip(orders, pairs):
        rows, cols = pair[0].shape[-2:]
        flat += [part.reshape((2,) * len(kept) + (rows, cols)) for part in pair]
        sums.append(jax.ShapeDtypeStruct((rows, cols), jnp.float32))
        scratch.append(pltpu.VMEM((2,) * len(kept) + (rows, cols), jnp.bfloat16))
        scratch += stream_scratch(len(kept), order, rows, cols)
    stages = max([len(order) for _, order in orders], default=1)
    return pl.pallas_call(
        functools.partial(reduce_kernel, shards, bit_axes(shape), orders),
        out_shape=(
            jax.ShapeDtypeStruct((GROUPS,) + q_packed.shape[2:], q_packed.dtype),
            jax.ShapeDtypeStruct((GROUPS, tokens, width), kv_sums.dtype),
        ) + tuple(sums),
        in_specs=[VMEM_SPEC] * (2 + len(flat)),
        out_specs=(VMEM_SPEC,) * (2 + len(sums)),
        scratch_shapes=[sem((4,)), sem((4,)), sem((ndim, GROUPS)), sem((ndim, GROUPS)), sem((GROUPS,)), sem((GROUPS,)),
                        sem((max(len(orders), 1), stages)), sem((max(len(orders), 1), stages))] + scratch,
        compiler_params=pltpu.CompilerParams(collective_id=2, has_side_effects=True, vmem_limit_bytes=VMEM_BYTES),
        name="reduce_keys",
    )(q_packed, kv_sums.reshape((2, GROUPS) + (2,) * len(rest_bits) + (tokens, width)), *flat)


TQ = 256
TK = 512
NEAR_ROWS = 448
NEG = -1e30
FIRST_MAX = -1e29
NT = (((1,), (1,)), ((), ()))
NN = (((1,), (0,)), ((), ()))
BORDERS = (12, 16, 23, 32, 46, 64, 91)


def mxu(left, right, dims=NN):
    return lax.dot_general(left, right, dims, preferred_element_type=jnp.float32)


def turned(tile):
    return jnp.concatenate([tile[:, 64:], tile[:, :64]], axis=1)


def spread_lanes(packed, high):
    lane = lax.broadcasted_iota(jnp.int32, (1, 128), 1)
    keep = lane >= 64 if high else lane < 64
    zero = jnp.zeros((), packed.dtype)
    pair, last = packed[0:TQ], packed[TQ:]
    pick = lambda tile: jnp.where(keep, tile, zero)
    if high:
        return [pick(turned(pair)), pick(pair), jnp.concatenate([pick(turned(last)), pick(last)], axis=0)]
    return [pick(pair), pick(turned(pair)), jnp.concatenate([pick(last), pick(turned(last))], axis=0)]


def join_heads(parts):
    half = TQ // 2
    top = jnp.concatenate([parts[0], parts[1]], axis=1)
    low = jnp.concatenate([parts[2][:half], parts[2][half:]], axis=1)
    return jnp.concatenate([top, low], axis=0)


def valid_mask(se_ref, r, i, k0):
    kpos = k0 + lax.broadcasted_iota(jnp.int32, (TK, TQ), 0)
    return jnp.logical_and(kpos >= se_ref[r, i, 0:1, :], kpos < se_ref[r, i, 1:2, :])


def near_buckets(first, rows, parity):
    relative = (
        first - TK + TQ * parity
        + lax.broadcasted_iota(jnp.int32, (rows, TQ), 0)
        - lax.broadcasted_iota(jnp.int32, (rows, TQ), 1)
    )
    return buckets_of(relative)


def make_bias(table, parity, near_ref, tiles=(0, 1)):
    heads = near_ref.shape[0]
    for tile in tiles:
        def rows(step, _):
            start = pl.multiple_of(step * 32, 32)
            place = tile * TK + start
            after = place - near_start(parity)
            inside = jnp.logical_and(after >= 0, after < NEAR_ROWS)

            @pl.when(inside)
            def _():
                which = near_buckets(place, 32, parity)
                for h in range(heads):
                    value = jnp.zeros((32, TQ), jnp.float32)
                    for b in range(BUCKETS):
                        value = jnp.where(which == b, table[h, b], value)
                    near_ref[h, tile, pl.ds(start, 32)] = value.astype(jnp.bfloat16)

            @pl.when(jnp.logical_not(inside))
            def _():
                for h in range(heads):
                    value = jnp.where(after < 0, table[h, 15], table[h, 31])
                    near_ref[h, tile, pl.ds(start, 32)] = jnp.full((32, TQ), value, jnp.float32).astype(jnp.bfloat16)

            return 0
        lax.fori_loop(0, TK // 32, rows, 0)


def tile_kind(bounds, r, i, t):
    slot = jnp.clip(t - bounds[r, i, 2] + 1, 0, 3)
    away = jnp.logical_or(slot == 0, slot == 3)
    inside = jnp.logical_and(t >= bounds[r, i, 3], t < bounds[r, i, 4])
    return slot, jnp.logical_and(away, inside)


def fwd_kernel(alone, bounds, table, q_ref, kv_hbm, se_ref, *refs):
    if alone:
        near_ref, o_in, keep_in, lse_in, o_ref, keep_ref, lse_ref, vt, acc, mx, qp, kv_ref, kv_sem = refs
    else:
        o_ref, keep_ref, lse_ref, near_ref, vt, acc, mx, qp, kv_ref, kv_sem = refs
        make_bias(table, bounds[0, 0, 5], near_ref)
    heads = lse_ref.shape[2]
    base = 1 - bounds[0, 0, 6] if alone else 0

    def row_body(at, _):
        r = base + at
        lo_all = jnp.minimum(bounds[r, 0, 0], bounds[r, 1, 0])
        hi_all = jnp.maximum(bounds[r, 0, 1], bounds[r, 1, 1])

        def fetch(t):
            rows = pl.ds(pl.multiple_of(t * TK, TK), TK)
            return pltpu.make_async_copy(kv_hbm.at[r, rows], kv_ref.at[rows], kv_sem.at[t])

        def begin(t, _):
            fetch(t).start()
            return 0

        lax.fori_loop(lo_all, hi_all, begin, 0)
        for i in range(2):
            for h, tile in enumerate(spread_lanes(q_ref[r, i], False)):
                qp[i, h] = tile

        def turn(t, _):
            fetch(t).wait()
            k0 = pl.multiple_of(t * TK, TK)
            for h in range(heads):
                tile = kv_ref[pl.ds(k0, TK), h * 128 : h * 128 + 128]
                vt[h, 0:64, pl.ds(k0, TK)] = tile.T[64:128, :]
                vt[h, 64:80, pl.ds(k0, TK)] = jnp.ones((16, TK), jnp.bfloat16)
            return 0

        lax.fori_loop(lo_all, hi_all, turn, 0)

        def q_body(i, _):
            acc[...] = jnp.zeros_like(acc)
            mx[...] = jnp.full_like(mx, FIRST_MAX)

            def tile_body(t, _):
                k0 = pl.multiple_of(t * TK, TK)
                slot, plain = tile_kind(bounds, r, i, t)
                near = jnp.logical_and(slot > 0, slot < 3)

                def scores(h):
                    return mxu(kv_ref[pl.ds(k0, TK), h * 128 : h * 128 + 128], qp[i, h], NT)

                def finish(h, s, b):
                    m_old = mx[h]
                    m_new = jnp.maximum(m_old, jnp.max(s, axis=0, keepdims=True) + b)
                    p = jnp.exp(s - (m_new - b)).astype(jnp.bfloat16)
                    mx[h] = m_new
                    acc[h] = acc[h] * jnp.exp(m_old - m_new) + mxu(vt[h, :, pl.ds(k0, TK)], p)

                @pl.when(plain)
                def _():
                    found = [scores(h) for h in range(heads)]
                    for h in range(heads):
                        finish(h, found[h], jnp.where(slot == 0, table[h, 15], table[h, 31]))

                @pl.when(near)
                def _():
                    ok = valid_mask(se_ref, r, i, k0)
                    for h in range(heads):
                        s = scores(h) + near_ref[h, slot - 1].astype(jnp.float32)
                        finish(h, jnp.where(ok, s, NEG), 0.0)

                @pl.when(jnp.logical_not(jnp.logical_or(plain, near)))
                def _():
                    ok = valid_mask(se_ref, r, i, k0)
                    for h in range(heads):
                        s = scores(h) + jnp.where(slot == 0, table[h, 15], table[h, 31])
                        finish(h, jnp.where(ok, s, NEG), 0.0)

                return 0

            lax.fori_loop(bounds[r, i, 0], bounds[r, i, 1], tile_body, 0)
            parts = []
            for h in range(heads):
                total = acc[h, 64:65, :]
                parts.append((acc[h, 0:64, :] / total).T)
                lse_ref[r, i, h] = mx[h] + jnp.log(total)
            joined = join_heads(parts)
            o_ref[r, i] = joined.astype(jnp.bfloat16)
            keep_ref[r, i] = joined
            return 0

        lax.fori_loop(0, 2, q_body, 0)
        return 0

    lax.fori_loop(0, 1 if alone else 2, row_body, 0)
    if alone:
        o_ref[1 - base] = o_in[...]
        keep_ref[1 - base] = keep_in[...]
        lse_ref[1 - base] = lse_in[...]


def attention(bounds, table, q, kv, se, ready=()):
    heads, n = kv.shape[2] // 128, kv.shape[1]
    packed = q.shape
    outs = [
        jax.ShapeDtypeStruct(packed, jnp.bfloat16),
        jax.ShapeDtypeStruct(packed, jnp.float32),
        jax.ShapeDtypeStruct((2, 2, heads, 1, TQ), jnp.float32),
    ]
    if not ready:
        outs.append(jax.ShapeDtypeStruct((heads, 2, TK, TQ), jnp.bfloat16))
    return pl.pallas_call(
        functools.partial(fwd_kernel, bool(ready)),
        out_shape=tuple(outs),
        in_specs=[SMEM_SPEC] * 2 + [VMEM_SPEC, ANY_SPEC, VMEM_SPEC] + [VMEM_SPEC] * len(ready),
        out_specs=(VMEM_SPEC,) * len(outs),
        scratch_shapes=[
            pltpu.VMEM((heads, 80, n), jnp.bfloat16),
            pltpu.VMEM((heads, 80, TQ), jnp.float32),
            pltpu.VMEM((heads, 1, TQ), jnp.float32),
            pltpu.VMEM((2, heads, TQ, 128), jnp.bfloat16),
            pltpu.VMEM(kv.shape[1:], jnp.bfloat16),
            pltpu.SemaphoreType.DMA((n // TK,)),
        ],
        compiler_params=pltpu.CompilerParams(vmem_limit_bytes=VMEM_BYTES),
        name="attention",
    )(bounds, table, q, kv, se, *ready)


def prepare(q, do, q_out, do_out):
    for h, tile in enumerate(spread_lanes(q, False)):
        q_out[h] = tile
    for h, tile in enumerate(spread_lanes(do, True)):
        do_out[h] = tile


def row_deltas(do, keep, delta):
    prod = (do.astype(jnp.float32) * keep).T
    top, low = prod[:, 0:TQ], prod[:, TQ:]
    delta[0] = jnp.sum(top[0:64], axis=0, keepdims=True)
    delta[1] = jnp.sum(top[64:128], axis=0, keepdims=True)
    delta[2] = jnp.concatenate(
        [jnp.sum(low[0:64], axis=0, keepdims=True), jnp.sum(low[64:128], axis=0, keepdims=True)], axis=1
    )


def near_start(parity):
    return 416 - TQ * parity


def far_sums(grid, h, first, end):
    def one(step, total):
        rows = grid[h, pl.ds(pl.multiple_of(step * 32, 32), 32)]
        return total + jnp.sum(rows.reshape(4, 8, TQ), axis=0)
    total = lax.fori_loop(first // 32, end // 32, one, jnp.zeros((8, TQ), jnp.float32))
    return jnp.sum(total, axis=0, keepdims=True)


def bucket_sums(parity, near, side, tab_ref, tab8):
    heads = near.shape[0]
    tab8[...] = jnp.zeros_like(tab8)

    def inner(step, _):
        start = pl.multiple_of(step * 32, 32)
        which = near_buckets(near_start(parity) + start, 32, parity)
        for b in range(BUCKETS):
            here = which == b
            for h in range(heads):
                rows = jnp.where(here, near[h, pl.ds(start, 32)], 0.0)
                tab8[h, b] += jnp.sum(rows.reshape(4, 8, TQ), axis=0)
        return 0

    lax.fori_loop(0, NEAR_ROWS // 32, inner, 0)
    for h in range(heads):
        tab_ref[h] = jnp.sum(tab8[h], axis=1)
        tab_ref[h, 15:16] += side[h, 0:1]
        tab_ref[h, 31:32] += side[h, 1:2]


def bwd_kernel(alone, bounds, table, q_ref, do_ref, keep_ref, kv_hbm, bias_ref, se_ref, lse_ref,
               dq_ref, dkv_ref, near_ref, side, delta, *rest):
    tab_ref, tab8, rest = (None, None, rest) if alone else (rest[0], rest[-1], rest[1:-1])
    kt, dqt, dkv, grid, qp, dp_ref, kv_ref, kv_sem = rest
    heads = lse_ref.shape[2]
    n = kv_hbm.shape[1]
    grid[...] = jnp.zeros_like(grid)
    side[...] = jnp.zeros_like(side)
    base = 1 - bounds[0, 0, 6] if alone else 0
    for at in range(1 if alone else 2):
        for i in range(2):
            prepare(q_ref[base + at, i], do_ref[base + at, i], qp.at[at, i], dp_ref.at[at, i])
    for r in range(2):
        for i in range(2):
            row_deltas(do_ref[r, i], keep_ref[r, i], delta.at[r, i])

    def row_body(at, _):
        r = base + at
        lo_all = jnp.minimum(bounds[r, 0, 0], bounds[r, 1, 0])
        hi_all = jnp.maximum(bounds[r, 0, 1], bounds[r, 1, 1])

        def fetch(t):
            rows = pl.ds(pl.multiple_of(t * TK, TK), TK)
            return pltpu.make_async_copy(kv_hbm.at[r, rows], kv_ref.at[rows], kv_sem.at[t])

        def begin(t, _):
            fetch(t).start()
            return 0

        lax.fori_loop(lo_all, hi_all, begin, 0)

        def clear(t, _):
            k0 = pl.multiple_of(t * TK, TK)
            for h in range(heads):
                dkv[h, pl.ds(k0, TK), :] = jnp.zeros((TK, 128), jnp.float32)
            return 0

        lax.fori_loop(0, n // TK, clear, 0)

        def turn(t, _):
            fetch(t).wait()
            k0 = pl.multiple_of(t * TK, TK)
            for h in range(heads):
                tile = kv_ref[pl.ds(k0, TK), h * 128 : h * 128 + 128]
                kt[h, 0:64, pl.ds(k0, TK)] = tile.T[0:64, :]
                kt[h, 64:80, pl.ds(k0, TK)] = jnp.ones((16, TK), jnp.bfloat16)
            return 0

        lax.fori_loop(lo_all, hi_all, turn, 0)

        def q_body(i, _):
            dqt[...] = jnp.zeros_like(dqt)

            def tile_body(t, _):
                k0 = pl.multiple_of(t * TK, TK)
                slot, plain = tile_kind(bounds, r, i, t)

                def finish(h, p, ds, where):
                    ds_low = ds.astype(jnp.bfloat16)
                    two = jnp.concatenate([ds_low, p.astype(jnp.bfloat16)], axis=1)
                    both = jnp.concatenate([qp[at, i, h], dp_ref[at, i, h]], axis=0)
                    dkv[h, pl.ds(k0, TK), :] += mxu(two, both)
                    dqt[h, where] += mxu(kt[h, :, pl.ds(k0, TK)], ds_low)

                def products(h):
                    tile = kv_ref[pl.ds(k0, TK), h * 128 : h * 128 + 128]
                    return mxu(tile, qp[at, i, h], NT), mxu(tile, dp_ref[at, i, h], NT)

                @pl.when(plain)
                def _():
                    for h in range(heads):
                        s, d_probs = products(h)
                        p = jnp.exp(s - (lse_ref[r, i, h] - jnp.where(slot == 0, table[h, 15], table[h, 31])))
                        finish(h, p, p * (d_probs - delta[r, i, h]), jnp.where(slot == 0, 0, 2))

                def general(bias):
                    ok = valid_mask(se_ref, r, i, k0)
                    for h in range(heads):
                        s, d_probs = products(h)
                        s = s + bias(h)
                        p = jnp.where(ok, jnp.exp(jnp.where(ok, s, NEG) - lse_ref[r, i, h]), 0.0)
                        ds = p * (d_probs - delta[r, i, h])
                        grid[h, pl.ds(pl.multiple_of(slot * TK, TK), TK)] += ds
                        finish(h, p, ds, 1)

                near = jnp.logical_and(slot > 0, slot < 3)
                pl.when(near)(lambda: general(lambda h: bias_ref[h, slot - 1].astype(jnp.float32)))
                away = jnp.logical_not(jnp.logical_or(plain, near))
                pl.when(away)(lambda: general(lambda h: jnp.where(slot == 0, table[h, 15], table[h, 31])))
                return 0

            lax.fori_loop(bounds[r, i, 0], bounds[r, i, 1], tile_body, 0)
            parts = []
            for h in range(heads):
                parts.append((dqt[h, 0, 0:64] + dqt[h, 1, 0:64] + dqt[h, 2, 0:64]).T * 0.125)
                side[h, 0:1] += dqt[h, 0, 64:65]
                side[h, 1:2] += dqt[h, 2, 64:65]
            dq_ref[at, i] = join_heads(parts).astype(jnp.bfloat16)
            return 0

        lax.fori_loop(0, 2, q_body, 0)

        def put(t, _):
            k0 = pl.multiple_of(t * TK, TK)
            for h in range(heads):
                dkv_ref[at, pl.ds(k0, TK), h * 128 : h * 128 + 128] = dkv[h, pl.ds(k0, TK), :].astype(jnp.bfloat16)
            return 0

        lax.fori_loop(0, n // TK, put, 0)
        return 0

    lax.fori_loop(0, 1 if alone else 2, row_body, 0)

    parity = bounds[0, 0, 5]
    first = TK + near_start(parity)
    for h in range(heads):
        near_ref[h] = grid[h, pl.ds(pl.multiple_of(first, 32), NEAR_ROWS)]
        side[h, 0:1] += far_sums(grid, h, 0, first)
        side[h, 1:2] += far_sums(grid, h, first + NEAR_ROWS, 4 * TK)
    if not alone:
        bucket_sums(parity, near_ref, side, tab_ref, tab8)


def attention_back(alone, bounds, table, q, do, keep, kv, bias, se, lse):
    heads, n = kv.shape[2] // 128, kv.shape[1]
    count = 1 if alone else 2
    table_out = [] if alone else [jax.ShapeDtypeStruct((heads, BUCKETS, TQ), jnp.float32)]
    return pl.pallas_call(
        functools.partial(bwd_kernel, alone),
        out_shape=(
            jax.ShapeDtypeStruct((count,) + q.shape[1:], jnp.bfloat16),
            jax.ShapeDtypeStruct((count,) + kv.shape[1:], jnp.bfloat16),
            jax.ShapeDtypeStruct((heads, NEAR_ROWS, TQ), jnp.float32),
            jax.ShapeDtypeStruct((heads, 2, TQ), jnp.float32),
            jax.ShapeDtypeStruct((2, 2, heads, 1, TQ), jnp.float32),
        ) + tuple(table_out),
        in_specs=[SMEM_SPEC] * 2 + [VMEM_SPEC] * 3 + [ANY_SPEC] + [VMEM_SPEC] * 3,
        out_specs=(VMEM_SPEC,) * (5 + len(table_out)),
        scratch_shapes=[
            pltpu.VMEM((heads, 80, n), jnp.bfloat16),
            pltpu.VMEM((heads, 3, 80, TQ), jnp.float32),
            pltpu.VMEM((heads, n, 128), jnp.float32),
            pltpu.VMEM((heads, 4 * TK, TQ), jnp.float32),
            pltpu.VMEM((count, 2, heads, TQ, 128), jnp.bfloat16),
            pltpu.VMEM((count, 2, heads, TQ, 128), jnp.bfloat16),
            pltpu.VMEM(kv.shape[1:], jnp.bfloat16),
            pltpu.SemaphoreType.DMA((n // TK,)),
        ] + [pltpu.VMEM((heads, BUCKETS, 8, TQ), jnp.float32) for _ in table_out],
        compiler_params=pltpu.CompilerParams(vmem_limit_bytes=VMEM_BYTES),
        name="attention_back",
    )(bounds, table, q, do, keep, kv, bias, se, lse)


TAPS = tuple(range(-3, 5))
LEAD = 8


def pool_scalars(y_rows, lab_rows, first):
    tokens = y_rows[0].shape[1]
    t = lax.broadcasted_iota(jnp.int32, (1, tokens), 1)
    at = lambda rows, k: rows[k + 3]
    found = []
    for p in range(2):
        inside = {1: 0 * t, 2: 0 * t + p, 3: (first + 2 * t + p) % 3, 4: 2 * (t % 2) + p}
        weights, scores = {}, []
        for b in range(1, MAX_BLOCK + 1):
            keep = {}
            for o in range(1 - b, b):
                same = jnp.logical_and(inside[b] + o >= 0, inside[b] + o < b)
                same = jnp.logical_and(same, at(lab_rows, p + o) == at(lab_rows, p))
                keep[o] = same.astype(jnp.float32)
            inverse = 1.0 / sum(keep.values())
            for o in keep:
                weights[b, o] = keep[o] * inverse
            scores.append(sum(weights[b, o] * at(y_rows, p + o) for o in keep))
        top = functools.reduce(jnp.maximum, scores)
        grown = [jnp.exp(s - top) for s in scores]
        total = sum(grown)
        found.append(([g / total for g in grown], weights))
    return found


def tap_weights(found):
    rows = []
    for k in TAPS:
        row = 0.0
        for p, (probs, weights) in enumerate(found):
            for b in range(1, MAX_BLOCK + 1):
                if (b, k - p) in weights:
                    row = row + probs[b - 1] * weights[b, k - p]
        rows.append(0.5 * row)
    return rows


def as_columns(rows):
    tokens = rows[0].shape[1]
    return jnp.concatenate(list(rows) + [jnp.zeros((128 - len(rows), tokens), jnp.float32)], axis=0).T


def load_bytes(x_ref, before, after, xs):
    length, width = x_ref.shape
    for j in range(width // 128):
        cols = slice(j * 128, j * 128 + 128)
        xs[j, 0:LEAD, :] = jnp.zeros((LEAD, 128), jnp.float32)
        xs[j, LEAD + length :, :] = jnp.zeros((LEAD, 128), jnp.float32)
        xs[j, LEAD - 2 : LEAD, :] = before[:, cols].astype(jnp.float32)
        xs[j, LEAD + length : LEAD + length + 2, :] = after[:, cols].astype(jnp.float32)
        xs[j, LEAD : LEAD + length, :] = x_ref[:, cols].astype(jnp.float32)


def tap(xs, k, tokens):
    return jnp.concatenate([xs[j, pl.ds(LEAD + k, tokens, stride=2), :] for j in range(xs.shape[0])], axis=1)


def strips(buf, first, rows):
    return jnp.concatenate([buf[j, first : first + rows, :] for j in range(buf.shape[0])], axis=1)


def unit_rows(values):
    return lax.rsqrt(jnp.mean(values * values, axis=-1, keepdims=True) + 1e-06)


def pool_tokens(scale, xs, labels, score, gain, tokens, y_ref, share_ref):
    width = xs.shape[0] * 128
    score = jnp.broadcast_to(score, (8, width))
    for k in TAPS:
        y_ref[k + 3 : k + 4, :] = mxu(score, tap(xs, k, tokens).astype(jnp.bfloat16), NT)[0:1]
    rows = [y_ref[j : j + 1, :] for j in range(8)]
    first = (lax.axis_index("blk") * 2 * tokens) % 3
    found = pool_scalars(rows, labels, first)
    lane = lax.broadcasted_iota(jnp.int32, (1, 128), 1)
    share = jnp.zeros((1, 128), jnp.float32)
    for b in range(MAX_BLOCK):
        share = jnp.where(lane == b, jnp.sum(found[0][0][b] + found[1][0][b], axis=1, keepdims=True) * scale, share)
    share_ref[...] = share
    columns = as_columns(tap_weights(found))
    hidden = sum(columns[:, k + 3 : k + 4] * tap(xs, k, tokens) for k in TAPS)
    return hidden, (hidden * unit_rows(hidden) * gain.astype(jnp.float32)).astype(jnp.bfloat16)


def put_pairs(keys, values, kv_ref):
    low = lax.broadcasted_iota(jnp.int32, (1, 128), 1) < 64
    for j in range(keys.shape[1] // 128):
        k_pair, v_pair = keys[:, j * 128 : j * 128 + 128], values[:, j * 128 : j * 128 + 128]
        one = jnp.where(low, k_pair, turned(v_pair))
        two = jnp.where(low, turned(k_pair), v_pair)
        for head, tile in ((2 * j, one), (2 * j + 1, two)):
            kv_ref[head // 3, :, head % 3 * 128 : head % 3 * 128 + 128] = tile


def pool_kernel(shards, scale, x_ref, before_ref, after_ref, lab_ref, score_ref, gain_ref, wq_ref, wk_ref, wv_ref,
                hidden_ref, n1_ref, y_ref, share_ref, q_ref, kv_ref, xs):
    tokens = hidden_ref.shape[0]
    load_bytes(x_ref, before_ref[0:2, :], after_ref[0:2, :], xs)
    labels = [lab_ref[j : j + 1, :] for j in range(8)]
    hidden_ref[...], n1 = pool_tokens(scale, xs, labels, score_ref[...], gain_ref[...], tokens, y_ref, share_ref)
    n1_ref[...] = n1
    put_pairs(mxu(n1, wk_ref[...]).astype(jnp.bfloat16), mxu(n1, wv_ref[...]).astype(jnp.bfloat16), kv_ref)
    put_packed(mxu(n1, wq_ref[...]).astype(jnp.bfloat16) * jnp.bfloat16(0.125), q_ref)


def put_packed(array, out_ref):
    tokens = array.shape[0]
    half = tokens // 2
    for g in range(GROUPS):
        part = array[:, g * 192 : g * 192 + 192]
        out_ref[g, 0:tokens, :] = part[:, 0:128]
        out_ref[g, tokens:, :] = jnp.concatenate([part[:half, 128:], part[half:, 128:]], axis=1)


def get_packed(packed_ref):
    tokens = packed_ref.shape[1] * 2 // 3
    parts = []
    for g in range(GROUPS):
        last = packed_ref[g, tokens:, :]
        parts += [packed_ref[g, 0:tokens, :], jnp.concatenate([last[:, :64], last[:, 64:]], axis=0)]
    return jnp.concatenate(parts, axis=1)


def pool_and_project(shards, scale, x, before, after, labels, score, gain, wq, wk, wv):
    length, width = x.shape
    tokens = length // 2
    return pl.pallas_call(
        functools.partial(pool_kernel, shards, scale),
        out_shape=(
            jax.ShapeDtypeStruct((tokens, width), jnp.float32),
            jax.ShapeDtypeStruct((tokens, width), jnp.bfloat16),
            jax.ShapeDtypeStruct((8, tokens), jnp.float32),
            jax.ShapeDtypeStruct((1, 128), jnp.float32),
            jax.ShapeDtypeStruct((GROUPS, tokens * 3 // 2, 128), jnp.bfloat16),
            jax.ShapeDtypeStruct((GROUPS, tokens, width * 2 // GROUPS), jnp.bfloat16),
        ),
        in_specs=[VMEM_SPEC] * 9,
        out_specs=(VMEM_SPEC,) * 6,
        scratch_shapes=[pltpu.VMEM((width // 128, length + 2 * LEAD, 128), jnp.float32)],
        compiler_params=pltpu.CompilerParams(vmem_limit_bytes=VMEM_BYTES),
        name="pool_and_project",
    )(x, before, after, labels, score, gain, wq, wk, wv)


GELU_A = math.sqrt(2.0 / math.pi)
GELU_B = 0.044715


def norm_back(d_out, rows, gain):
    unit = unit_rows(rows)
    flat = rows * unit
    scaled = d_out * gain
    d_rows = unit * (scaled - flat * jnp.mean(scaled * flat, axis=-1, keepdims=True))
    return d_rows, jnp.sum(d_out * flat, axis=0, keepdims=True)


def feed_kernel(o_ref, hidden_ref, ct_ref, gain_ref, wo_ref, wg_ref, wu_ref, wd_ref,
                out_ref, dres_ref, da_ref, dgain_ref, n2_ref, att_ref, act_ref, dg_ref, du_ref, db_ref, acc, dn2):
    ff = wg_ref.shape[1]
    step = 512
    att = get_packed(o_ref)
    att_ref[...] = att
    residual = hidden_ref[...] + mxu(att, wo_ref[...])
    gain = gain_ref[...].astype(jnp.float32)
    n2_ref[...] = (residual * unit_rows(residual) * gain).astype(jnp.bfloat16)
    acc[...] = residual
    dn2[...] = jnp.zeros_like(dn2)

    for j in range(ff // step):
        cols = slice(j * step, j * step + step)
        n2 = n2_ref[...]
        gate = mxu(n2, wg_ref[:, cols])
        up = mxu(n2, wu_ref[:, cols])
        d_act = mxu(ct_ref[...], wd_ref[cols, :], NT)
        square = gate * gate
        curve = jnp.tanh(GELU_A * gate * (1.0 + GELU_B * square))
        half = 0.5 * (1.0 + curve)
        grown = gate * half
        slope = half + 0.5 * gate * (1.0 - curve * curve) * (GELU_A * (1.0 + 3.0 * GELU_B * square))
        act = (grown * up).astype(jnp.bfloat16)
        d_gate = (d_act * up * slope).astype(jnp.bfloat16)
        d_up = (d_act * grown).astype(jnp.bfloat16)
        act_ref[:, cols] = act
        dg_ref[:, cols] = d_gate
        du_ref[:, cols] = d_up
        acc[...] += mxu(act, wd_ref[cols, :])
        dn2[...] += mxu(d_gate, wg_ref[:, cols], NT) + mxu(d_up, wu_ref[:, cols], NT)

    out_ref[...] = acc[...].astype(jnp.bfloat16)
    residual = hidden_ref[...] + mxu(att_ref[...], wo_ref[...])
    d_rows, d_gain = norm_back(dn2[...], residual, gain)
    dgain_ref[...] = d_gain
    d_res = ct_ref[...].astype(jnp.float32) + d_rows
    dres_ref[...] = d_res
    d_branch = d_res.astype(jnp.bfloat16)
    db_ref[...] = d_branch
    put_packed(mxu(d_branch, wo_ref[...], NT).astype(jnp.bfloat16), da_ref)


def feed_forward(o_home, hidden, ct, gain, wo, wg, wu, wd):
    tokens, width = hidden.shape
    ff = wg.shape[1]
    low = lambda cols: jax.ShapeDtypeStruct((tokens, cols), jnp.bfloat16)
    return pl.pallas_call(
        feed_kernel,
        out_shape=(
            low(width),
            jax.ShapeDtypeStruct((tokens, width), jnp.float32),
            jax.ShapeDtypeStruct(o_home.shape, jnp.bfloat16),
            jax.ShapeDtypeStruct((1, width), jnp.float32),
            low(width), low(width), low(ff), low(ff), low(ff), low(width),
        ),
        in_specs=[VMEM_SPEC] * 8,
        out_specs=(VMEM_SPEC,) * 10,
        scratch_shapes=[pltpu.VMEM((tokens, width), jnp.float32)] * 2,
        compiler_params=pltpu.CompilerParams(vmem_limit_bytes=VMEM_BYTES),
        name="feed_forward",
    )(o_home, hidden, ct, gain, wo, wg, wu, wd)


def unpack_pairs(dkv_ref, width):
    low = lax.broadcasted_iota(jnp.int32, (1, 128), 1) < 64
    dk_parts, dv_parts = [], []
    for j in range(width // 128):
        one, two = [dkv_ref[h // 3, :, h % 3 * 128 : h % 3 * 128 + 128] for h in (2 * j, 2 * j + 1)]
        dk_parts.append(jnp.where(low, one, turned(two)))
        dv_parts.append(jnp.where(low, turned(one), two))
    return jnp.concatenate(dk_parts, axis=1), jnp.concatenate(dv_parts, axis=1)


def pool_back(d_hidden, length, lab_ref, y_ref, score, gb_ref, edge_ref, spill_ref, xs, gbuf):
    tokens, width = d_hidden.shape
    lane = lax.broadcasted_iota(jnp.int32, (1, 128), 1)
    met = jnp.zeros((tokens, 128), jnp.float32)
    for k in TAPS:
        met = jnp.where(lane == k + 3, jnp.sum(d_hidden * tap(xs, k, tokens), axis=-1, keepdims=True), met)
    met = met.T
    first = (lax.axis_index("blk") * length) % 3
    found = pool_scalars([y_ref[j : j + 1, :] for j in range(8)], [lab_ref[j : j + 1, :] for j in range(8)], first)
    touch = [0.0] * 8
    for p, (probs, weights) in enumerate(found):
        d_block = []
        for b in range(1, MAX_BLOCK + 1):
            d_block.append(0.5 * sum(weights[b, o] * met[p + o + 3 : p + o + 4] for o in range(1 - b, b)))
        mean = sum(q * d for q, d in zip(probs, d_block))
        for b in range(1, MAX_BLOCK + 1):
            d_score = probs[b - 1] * (d_block[b - 1] - mean)
            for o in range(1 - b, b):
                touch[p + o + 3] = touch[p + o + 3] + d_score * weights[b, o]
    share_cols = as_columns(tap_weights(found) + touch)
    score = score.astype(jnp.float32)
    gbuf[...] = jnp.zeros_like(gbuf)
    d_score_vec = jnp.zeros((1, width), jnp.float32)
    for k in TAPS:
        own, via = share_cols[:, k + 3 : k + 4], share_cols[:, k + 11 : k + 12]
        added = own * d_hidden + via * score
        for j in range(gbuf.shape[0]):
            gbuf[j, pl.ds(LEAD + k, tokens, stride=2), :] += added[:, j * 128 : j * 128 + 128]
        d_score_vec = d_score_vec + jnp.sum(via * tap(xs, k, tokens), axis=0, keepdims=True)
    gb_ref[...] = strips(gbuf, LEAD, length).astype(jnp.bfloat16)
    edge_ref[0] = strips(gbuf, LEAD, 16)
    edge_ref[1] = strips(gbuf, LEAD + length - 16, 16)
    spill_ref[0] = strips(gbuf, 0, LEAD)
    spill_ref[1] = strips(gbuf, LEAD + length, LEAD)
    return d_score_vec


def put_small(small_ref, vectors, tab_ref, share_ref):
    small_ref[...] = jnp.zeros_like(small_ref)
    for row, vector in zip((0, 6, 12), vectors):
        for j in range(6):
            small_ref[row + j : row + j + 1, :] = vector[:, j * 128 : j * 128 + 128]
    heads = tab_ref.shape[0]
    group = lax.axis_index("blk") // (lax.axis_size("blk") // GROUPS)
    for h in range(heads):
        total = lax.dot_general(
            jnp.ones((8, tab_ref.shape[2]), jnp.float32), tab_ref[h], NT,
            precision=lax.Precision.HIGHEST, preferred_element_type=jnp.float32,
        )
        small_ref[pl.ds(18 + group * heads + h, 1), 0:BUCKETS] = total[0:1]
    small_ref[30:31, :] = share_ref[...]


def last_kernel(shards, axes, order, dq_ref, dkv_ref, hidden_ref, dres_ref, x_ref, before_ref, after_ref, lab_ref, y_ref, score_ref,
                gain_ref, wq_ref, wk_ref, wv_ref, dgain2_ref, share_ref, tab_ref, gb_ref, edge_ref, spill_out, small_out, parts_ref,
                w_send, w_recv, s_send, s_recv, xs, gbuf, spill_ref, small_ref, small_bufs):
    at = {"dp": lax.axis_index("dp"), "blk": lax.axis_index("blk")}
    width = hidden_ref.shape[1]
    whole = Whole(axes, at, order, small_ref, small_bufs, small_out, w_send, w_recv)
    left = (at["dp"], (at["blk"] + shards - 1) % shards)
    right = (at["dp"], (at["blk"] + 1) % shards)
    greet([whole.stream.target(p) for p in range(len(axes))] + [left, right])
    load_bytes(x_ref, before_ref[0:2, :], after_ref[0:2, :], xs)
    dq = get_packed(dq_ref)
    dk, dv = unpack_pairs(dkv_ref, width)
    parts_ref[0], parts_ref[1], parts_ref[2] = dq, dk, dv
    d_n1 = mxu(dq, wq_ref[...], NT) + mxu(dk, wk_ref[...], NT) + mxu(dv, wv_ref[...], NT)
    d_rows, d_gain1 = norm_back(d_n1, hidden_ref[...], gain_ref[...].astype(jnp.float32))
    d_hidden = dres_ref[...] + d_rows
    d_score = pool_back(d_hidden, x_ref.shape[0], lab_ref, y_ref, score_ref[...], gb_ref, edge_ref, spill_ref, xs, gbuf)
    put_small(small_ref, (d_score, d_gain1, dgain2_ref[...]), tab_ref, share_ref)
    spills = [
        remote(spill_ref.at[0], spill_out.at[1], s_send.at[0], s_recv.at[1], left),
        remote(spill_ref.at[1], spill_out.at[0], s_send.at[1], s_recv.at[0], right),
    ]
    whole.copy(0).start()
    for copy in spills:
        copy.start()
    for stage in range(len(axes)):
        advance(whole, stage)
    for copy in spills:
        copy.wait()


def last_part(shape, dq, dkv, hidden, dres, x, before, after, labels, y, score, gain, wq, wk, wv, dgain2, share, tab):
    tokens, width = hidden.shape
    length = x.shape[0]
    axes = bit_axes(shape)
    ndim = len(axes)
    full, sem, low = jax.ShapeDtypeStruct, pltpu.SemaphoreType.DMA, jnp.bfloat16
    strip = pltpu.VMEM((width // 128, length + 2 * LEAD, 128), jnp.float32)
    return pl.pallas_call(
        functools.partial(last_kernel, shape["blk"], axes, tuple(reversed(range(ndim)))),
        out_shape=(
            full((length, width), low),
            full((2, 16, width), jnp.float32),
            full((2, LEAD, width), jnp.float32),
            full((32, 128), jnp.float32),
            full((3, tokens, width), low),
        ),
        in_specs=[VMEM_SPEC] * 17,
        out_specs=(VMEM_SPEC,) * 5,
        scratch_shapes=[
            sem((ndim,)), sem((ndim,)), sem((2,)), sem((2,)), strip, strip,
            pltpu.VMEM((2, LEAD, width), jnp.float32), pltpu.VMEM((32, 128), jnp.float32), pltpu.VMEM((2, ndim, 32, 128), jnp.float32),
        ],
        compiler_params=pltpu.CompilerParams(collective_id=3, has_side_effects=True, vmem_limit_bytes=VMEM_BYTES),
        name="last_part",
    )(dq, dkv, hidden, dres, x, before, after, labels, y, score, gain, wq, wk, wv, dgain2, share, tab)


def finish_kernel(shards, block_ref, gb_ref, edge_ref, spill_ref, small_ref, *refs):
    position = lax.axis_index("blk")
    count = 7 if len(refs) == 7 else 14
    streams, outs = refs[: len(refs) - count], refs[len(refs) - count :]
    out_ref, bytes_ref, score_ref, gain1_ref, gain2_ref, tab_ref, share_ref = outs[:7]
    out_ref[...] = block_ref[...]
    length = gb_ref.shape[0]
    bytes_ref[...] = gb_ref[...]
    zero = jnp.zeros((16 - LEAD, gb_ref.shape[1]), jnp.float32)
    left = jnp.where(position > 0, spill_ref[0], 0.0)
    right = jnp.where(position < shards - 1, spill_ref[1], 0.0)
    bytes_ref[0:16, :] = (edge_ref[0] + jnp.concatenate([left, zero], axis=0)).astype(jnp.bfloat16)
    bytes_ref[length - 16 :, :] = (edge_ref[1] + jnp.concatenate([zero, right], axis=0)).astype(jnp.bfloat16)
    for row, ref in ((0, score_ref), (6, gain1_ref), (12, gain2_ref)):
        for j in range(6):
            ref[j * 128 : j * 128 + 128] = small_ref[row + j, :]
    tab_ref[...] = small_ref[18 : 18 + tab_ref.shape[0], 0 : tab_ref.shape[1]]
    share_ref[...] = small_ref[30, 0:MAX_BLOCK]
    if streams:
        gq, gk, gv, go, gg, gu, gd = outs[7:]
        per, width = gq.shape
        half, ff = width // 2, gg.shape[1]
        one, two, down, *thirds = streams
        for ref, third in zip((gq, gk, gv), thirds):
            ref[:, :half] = third[:per, :]
            ref[:, half:] = third[per:, :]
        first = one.shape[1]
        for ref, rows in ((gg, slice(0, per)), (gu, slice(per, 2 * per))):
            ref[:, :first] = one[rows, :]
            ref[:, first:] = two[rows, : ff - first]
        go[:, :half] = two[:per, ff - first :]
        go[:, half:] = two[per:, ff - first :]
        gd[...] = down[...]


def finish(shards, heads_all, per, ff, block_out, gb, edge, spill, small, streams):
    width = gb.shape[1]
    full = jax.ShapeDtypeStruct
    line = full((width,), jnp.float32)
    outs = [full(block_out.shape, jnp.bfloat16), full(gb.shape, jnp.bfloat16), line, line, line]
    outs += [full((heads_all, BUCKETS), jnp.float32), full((MAX_BLOCK,), jnp.float32)]
    if streams:
        square, broad = full((per, width), jnp.float32), full((per, ff), jnp.float32)
        outs += [square] * 4 + [broad] * 2 + [full(streams[2].shape, jnp.float32)]
    return pl.pallas_call(
        functools.partial(finish_kernel, shards),
        out_shape=tuple(outs),
        in_specs=[VMEM_SPEC] * (5 + len(streams)),
        out_specs=(VMEM_SPEC,) * len(outs),
        compiler_params=pltpu.CompilerParams(vmem_limit_bytes=VMEM_BYTES),
        name="finish",
    )(block_out, gb, edge, spill, small, *streams)


class NearRows:
    def __init__(self, grid, first):
        self.grid, self.first, self.shape = grid, first, grid.shape

    def __getitem__(self, index):
        h, rows = index
        return self.grid[h, pl.ds(pl.multiple_of(self.first + rows.start, 32), rows.size)]


class Refs:
    def __init__(self, **refs):
        self.__dict__.update(refs)


def row_of(vectors, k):
    return jnp.concatenate([vectors[6 * k + j : 6 * k + j + 1, :] for j in range(6)], axis=1)


class BiasTable:
    def __init__(self, ref, place, heads):
        self.ref, self.first = ref, place.group * heads

    def __getitem__(self, index):
        head, bucket = index
        return self.ref[self.first + head, bucket]


class Held:
    def __init__(self, array, space):
        self.array, self.space = array, space


def call(kernel, ident, ins, outs, scratch):
    leaf = lambda entry: isinstance(entry, Held) or isinstance(entry, tuple) or not isinstance(entry, (dict, list))
    parts = [jax.tree.flatten(part, is_leaf=leaf) for part in (ins, outs, scratch)]
    counts = [len(part[0]) for part in parts]
    given, wanted, kept = [part[0] for part in parts]

    def run(*refs):
        named, start = {}, 0
        for count, (_, tree) in zip(counts, parts):
            named.update(jax.tree.unflatten(tree, refs[start : start + count]))
            start += count
        kernel(Refs(**named))

    space = lambda entry, at: entry.space if isinstance(entry, Held) else entry[2] if isinstance(entry, tuple) and len(entry) > 2 else at
    found = pl.pallas_call(
        run,
        out_shape=tuple(jax.ShapeDtypeStruct(entry[0], entry[1]) for entry in wanted),
        in_specs=[pl.BlockSpec(memory_space=space(entry, pltpu.VMEM)) for entry in given],
        out_specs=tuple(pl.BlockSpec(memory_space=space(entry, pltpu.VMEM)) for entry in wanted),
        scratch_shapes=kept,
        compiler_params=pltpu.CompilerParams(collective_id=ident, has_side_effects=True, vmem_limit_bytes=VMEM_BYTES),
        name=kernel.func.__name__,
    )(*[entry.array if isinstance(entry, Held) else entry for entry in given])
    return Refs(**jax.tree.unflatten(parts[1][1], found))


wide = lambda value: value.astype(jnp.float32)
slim = lambda value: value.astype(jnp.bfloat16)


class RowBack:
    def __init__(self, place, r):
        self.place, self.r = place, r
        self.heads = r.lse.shape[1]
        self.table = BiasTable(r.table, place, self.heads)
        self.tokens = TQ
        self.across, self.core_to = place.other_rest(2), place.other_rest(1)
        self.y, self.core = bit(place.rest, 2), place.rest % 2

    def group_of(self, n):
        return (self.place.group + 1 + n) % GROUPS

    def tile_start(self, m):
        place_y = jnp.where(m % 2 == 0, 1 - self.y, self.y)
        return pl.multiple_of((self.group_of(m // 2) * 2 + place_y) * TK, TK)

    def fetch(self, m):
        r = self.r
        rows = pl.ds(self.tile_start(m), TK)
        return (
            pltpu.make_async_copy(r.kv_hbm.at[rows], r.kv.at[m], r.kv_sem.at[m]),
            pltpu.make_async_copy(r.kl_hbm.at[rows], r.kl.at[m], r.kl_sem.at[m]),
        )

    def fetch_all(self):
        for m in range(2 * GROUPS):
            for copy in self.fetch(m):
                copy.start()

    def prepare(self):
        r = self.r

        def one(i, _):
            for h, tile in enumerate(spread_lanes(r.q[i], False)):
                r.qp[i, h] = tile
            for h, tile in enumerate(spread_lanes(r.do[i], True)):
                r.dp[i, h] = tile
            row_deltas(r.do[i], r.keep[i], r.delta.at[i])
            return 0

        lax.fori_loop(0, GROUPS, one, 0)

    def clear(self):
        r = self.r
        r.dqt[...] = jnp.zeros_like(r.dqt)
        r.grid[...] = jnp.zeros_like(r.grid)

    def core_copy(self, n, j):
        r = self.r
        return remote(r.held.at[n, j, 1 - self.core], r.core_in.at[n, j], r.core_send.at[n, j], r.core_recv.at[n, j], self.core_to)

    def y_copy(self, n):
        r = self.r
        return remote(r.y_out.at[n], r.y_in.at[n], r.y_send.at[n], r.y_recv.at[n], self.across)

    def z_copy(self, n):
        r, place = self.r, self.place
        return remote(r.z_out.at[n], r.dkv_home.at[place.group], r.z_send.at[n], r.z_recv.at[n], place.at(place.row, self.group_of(n), place.rest))

    def by_rows(self, one):
        def step(k, _):
            one(pl.ds(pl.multiple_of(k * 32, 32), 32))
            return 0
        lax.fori_loop(0, self.tokens // 32, step, 0)

    def own_sum(self, n, j, rows):
        return wide(self.r.held[n, j, self.core, rows]) + wide(self.r.core_in[n, j, rows])

    def send_y(self, n):
        r = self.r
        self.core_copy(n, 0).wait()

        def one(rows):
            r.y_out[n, rows] = slim(self.own_sum(n, 0, rows))

        self.by_rows(one)
        self.y_copy(n).start()

    def send_home(self, n):
        r = self.r
        self.core_copy(n, 1).wait()
        self.y_copy(n).wait()
        here = isinstance(n, int) and n == GROUPS - 1

        def one(rows):
            total = slim(self.own_sum(n, 1, rows) + wide(r.y_in[n, rows]))
            if here:
                r.dkv_home[self.place.group, rows] = total
            else:
                r.z_out[n, rows] = total

        self.by_rows(one)
        if not here:
            self.z_copy(n).start()

    def begin(self, m, a):
        r = self.r
        for copy in self.fetch(m):
            copy.wait()
        r.acc[a] = jnp.zeros_like(r.acc[a])
        for h in range(self.heads):
            r.kt[a, h, 0:64] = r.kv[m, :, h * 128 : h * 128 + 128].T[0:64]
            r.kt[a, h, 64:80] = jnp.ones((16, TK), jnp.bfloat16)

    def part(self, m, i, a):
        r, heads = self.r, self.heads
        t = self.tile_start(m) // TK
        keys = lambda h: r.kv[m, :, h * 128 : h * 128 + 128]
        slot = near_slot(self.place, i, t)
        away = jnp.logical_or(slot == 0, slot == 3)

        def finish(h, p, ds, where):
            ds_low = ds.astype(jnp.bfloat16)
            two = jnp.concatenate([ds_low, p.astype(jnp.bfloat16)], axis=1)
            both = jnp.concatenate([r.qp[i, h], r.dp[i, h]], axis=0)
            r.acc[a, :, h * 128 : h * 128 + 128] += mxu(two, both)
            r.dqt[i, h, where] += mxu(r.kt[a, h], ds_low)

        def products(h):
            s = mxu(jnp.concatenate([keys(h), r.kl[m]], axis=1), jnp.concatenate([r.qp[i, h], r.ql[i]], axis=1), NT)
            return s, mxu(keys(h), r.dp[i, h], NT)

        @pl.when(away)
        def _():
            for h in range(heads):
                s, d_probs = products(h)
                p = jnp.exp(s - (r.lse[i, h] - jnp.where(slot == 0, self.table[h, 15], self.table[h, 31])))
                finish(h, p, p * (d_probs - r.delta[i, h]), jnp.where(slot == 0, 0, 2))

        @pl.when(jnp.logical_not(away))
        def _():
            for h in range(heads):
                s, d_probs = products(h)
                p = jnp.exp(s + r.bias[h, slot - 1].astype(jnp.float32) - r.lse[i, h])
                ds = p * (d_probs - r.delta[i, h])
                r.grid[h, pl.ds(pl.multiple_of((slot - 1) * TK, TK), TK)] += ds
                finish(h, p, ds, 1)

    def end(self, m, a):
        r = self.r
        n, j = m // 2, m % 2
        for half in range(2):
            r.held[n, j, half] = r.acc[a, half * self.tokens : half * self.tokens + self.tokens].astype(jnp.bfloat16)
        self.core_copy(n, j).start()

    def query(self, i):
        r, place = self.r, self.place
        parts = []
        for h in range(self.heads):
            parts.append((r.dqt[i, h, 0, 0:64] + r.dqt[i, h, 1, 0:64] + r.dqt[i, h, 2, 0:64]).T * 0.125)
        r.dq[i] = slim(join_heads(parts))
        step = (i - place.group + GROUPS) % GROUPS
        copy = remote(r.dq.at[i], r.dq_home.at[place.group], r.q_send.at[step], r.q_recv.at[step], place.at(place.row, i, place.rest))
        pl.when(step > 0)(copy.start)

    def buckets(self):
        r = self.r
        first = near_start(self.core)
        for h in range(self.heads):
            r.side[h, 0:1] = sum(r.dqt[i, h, 0, 64:65] for i in range(GROUPS)) + far_sums(r.grid, h, 0, first)
            r.side[h, 1:2] = sum(r.dqt[i, h, 2, 64:65] for i in range(GROUPS)) + far_sums(r.grid, h, first + NEAR_ROWS, 2 * TK)
        bucket_sums(self.core, NearRows(r.grid, first), r.side, r.tab, r.tab8)

    def wait_home(self):
        r, place = self.r, self.place
        for n in range(GROUPS - 1):
            there = r.dkv_home.at[(place.group - 1 - n + GROUPS) % GROUPS]
            remote(r.z_out.at[n], there, r.z_send.at[n], r.z_recv.at[n], self.core_to).wait()


def back_kernel(shards, axes, plans, r):
    place = Place(shards)
    at = {"dp": place.dp, "blk": place.blk}
    tokens, width = r.hidden.shape
    back = RowBack(place, r)
    streams = []
    for s, (kept, order) in enumerate(plans):
        src = r.early_hbm[s] if s < 3 else r.late[s - 3]
        own = r.early_own[s] if s < 3 else None
        streams.append(Stream(axes, at, kept, order, src, own, r.bufs[s], r.sums[s], r.w_send.at[s], r.w_recv.at[s]))
    early, late = streams[:3], streams[3:]
    whole = Whole(axes, at, (4, 0, 3, 2, 1), r.small, r.small_bufs, r.small_out, r.w_send.at[len(plans)], r.w_recv.at[len(plans)])
    left, right = (place.dp, (place.blk + shards - 1) % shards), (place.dp, (place.blk + 1) % shards)

    met = hail([place.other_group(step) for step in (1, 2, 3)] + [back.across, back.core_to, place.other_row(), left, right])
    back.fetch_all()
    halves = []
    for s, stream in enumerate(early):
        (now,) = stream.order[:1]
        index = tuple(stream.own(p) if p == now else slice(None) for p in stream.kept)
        halves.append(pltpu.make_async_copy(r.early_hbm[s].at[index], r.early_own[s], r.own_sem.at[s]))
        halves[-1].start()
    later = [pltpu.make_async_copy(src, dst, r.later_sem.at[k]) for k, (src, dst) in enumerate((
        (r.hidden_hbm, r.hidden), (r.dres_hbm, r.dres), (r.n1_hbm, r.n1), (r.x_hbm, r.x), (r.wq_hbm, r.wq), (r.wk_hbm, r.wk), (r.wv_hbm, r.wv),
    ))]
    for copy in later:
        copy.start()
    back.prepare()
    await_all(met)
    for stream in early:
        stream.copy(0).start()
    back.clear()

    def halve(s):
        halves[s].wait()
        advance(early[s], 0)

    def step(m, _):
        back.begin(m, 0)

        def one(i, _):
            back.part(m, i, 0)
            return 0

        lax.fori_loop(0, GROUPS, one, 0)
        back.end(m, 0)
        for delay, action in ((1, back.send_y), (3, back.send_home)):
            then = m - delay + 2 * GROUPS
            n = then // 2 - GROUPS

            @pl.when(jnp.logical_and(then % 2 == 0, n >= 0))
            def _():
                action(n)

        for when, s in ((4, 0), (5, 2)):
            pl.when(m == when)(functools.partial(halve, s))
        return 0

    lax.fori_loop(0, 2 * GROUPS - 2, step, 0)
    back.begin(6, 0)
    back.begin(7, 1)

    def chunk(k, _):
        i = (place.group + 1 + k) % GROUPS
        back.part(6, i, 0)
        back.part(7, i, 1)
        back.query(i)
        pl.when(k == 3)(functools.partial(back.send_home, 2))
        return 0

    lax.fori_loop(0, GROUPS, chunk, 0)
    back.end(6, 0)
    back.end(7, 1)
    home = Line(place, r.dq, r.dq_home, r.q_send, r.q_recv)
    home.keep().start()
    halve(1)
    back.send_y(3)
    back.buckets()
    back.send_home(3)
    for copy in later:
        copy.wait()
    load_bytes(r.x, r.before[14:16, :], r.after[0:2, :], r.xs)
    n1_t = r.n1[...].T
    for s in (2, 0, 1):
        advance(early[s], 1)
    home.wait_all()
    dq = get_packed(r.dq_home)
    devices = 1 << len(axes)
    per = width // devices
    half = width // 2

    def weights(stream, part):
        r.total[...] = mxu(n1_t, part)

        def block(d, _):
            rows = pl.ds(pl.multiple_of(d * per, 8), per)
            index, rest = [], d
            for _ in axes:
                index.append(rest % 2)
                rest = rest // 2
            part = r.total[rows, :]
            stream.src[tuple(reversed(index))] = jnp.concatenate([part[:, :half], part[:, half:]], axis=0).astype(jnp.bfloat16)
            return 0

        lax.fori_loop(0, devices, block, 0)
        stream.copy(0).start()

    weights(late[0], dq)
    back.wait_home()
    dk, dv = unpack_pairs(r.dkv_home, width)
    weights(late[1], dk)
    weights(late[2], dv)
    d_n1 = mxu(dq, r.wq[...], NT) + mxu(dk, r.wk[...], NT) + mxu(dv, r.wv[...], NT)
    d_rows, d_gain1 = norm_back(d_n1, r.hidden[...], row_of(r.vectors, 1))
    d_hidden = r.dres[...] + d_rows
    for stream in late:
        advance(stream, 0)
    for stream in early:
        advance(stream, 2)
    d_score = pool_back(d_hidden, r.x.shape[0], r.labels, r.y, row_of(r.vectors, 0), r.gb, r.edge, r.spill, r.xs, r.gbuf)
    put_small(r.small, (d_score, d_gain1, r.dgain2[...]), r.tab, r.share)
    whole.copy(0).start()
    spills = [
        remote(r.spill.at[0], r.spill_out.at[1], r.s2_send.at[0], r.s2_recv.at[1], left),
        remote(r.spill.at[1], r.spill_out.at[0], r.s2_send.at[1], r.s2_recv.at[0], right),
    ]
    for copy in spills:
        copy.start()
    for stage in range(1, len(axes)):
        for stream in late:
            advance(stream, stage)
        advance(whole, stage - 1)
        if stage == 1:
            for stream in early:
                advance(stream, 3)
    advance(whole, len(axes) - 1)
    for copy in spills:
        copy.wait()


def back_and_last(shape, early, inputs):
    shards = shape["blk"]
    axes = bit_axes(shape)
    ndim = len(axes)
    kv, q, hidden = inputs["kv_hbm"].array, inputs["q"], inputs["hidden_hbm"].array
    heads, width = kv.shape[1] // 128, kv.shape[1]
    tokens, features = hidden.shape
    length = inputs["x_hbm"].array.shape[0]
    f32, low, sem = jnp.float32, jnp.bfloat16, pltpu.SemaphoreType.DMA
    chunk = (tokens, width)
    every = (0, 1, 2, 3, 4)
    four = (0, 1, 2, 3)
    plans = [
        (four, (0, 3, 2, 1)), (four, (3, 0, 2, 1)), (four, (2, 0, 3, 1)),
        (every, (4, 0, 3, 2, 1)), (every, (4, 3, 0, 2, 1)), (every, (4, 2, 0, 3, 1)),
    ]
    own = (2 * (features // (1 << ndim)), features // 2)
    blocks = [part.shape[-2:] for part in early] + [own] * 3
    ins = dict(inputs, early_hbm=[Held(part.reshape((2, 2, 2, 2) + part.shape[-2:]), pl.ANY) for part in early])
    outs = dict(
        gb=((length, features), low), edge=((2, 16, features), f32), spill_out=((2, LEAD, features), f32),
        small_out=((32, 128), f32), sums=[(block, f32) for block in blocks],
    )
    mem = lambda shape, dtype=low: pltpu.VMEM(shape, dtype)
    pairs, fours = sem((GROUPS, 2)), sem((GROUPS,))
    strip = mem((features // 128, length + 2 * LEAD, 128), f32)
    eights = sem((2 * GROUPS,))
    scratch = dict(
        kt=mem((2, heads, 80, TK)), dqt=mem((GROUPS, heads, 3, 80, TQ), f32), acc=mem((2, TK, width), f32),
        grid=mem((heads, 2 * TK, TQ), f32), side=mem((heads, 2, TQ), f32), tab8=mem((heads, BUCKETS, 8, TQ), f32),
        tab=mem((heads, BUCKETS, TQ), f32), delta=mem((GROUPS, heads, 1, TQ), f32),
        qp=mem((GROUPS, heads, TQ, 128)), dp=mem((GROUPS, heads, TQ, 128)),
        kv=mem((2 * GROUPS, TK, width)), kl=mem((2 * GROUPS, TK, 128)),
        held=mem((GROUPS, 2, 2) + chunk), core_in=mem((GROUPS, 2) + chunk),
        y_out=mem((GROUPS,) + chunk), y_in=mem((GROUPS,) + chunk), z_out=mem((GROUPS,) + chunk), dkv_home=mem((GROUPS,) + chunk),
        dq=mem(q.shape), dq_home=mem(q.shape),
        core_send=pairs, core_recv=pairs, y_send=fours, y_recv=fours, z_send=fours, z_recv=fours, q_send=fours, q_recv=fours,
        kv_sem=eights, kl_sem=eights, own_sem=sem((3,)), later_sem=sem((7,)),
        hidden=mem((tokens, features), f32), dres=mem((tokens, features), f32), n1=mem((tokens, features)), x=mem((length, features)),
        wq=mem((features, features)), wk=mem((features, features)), wv=mem((features, features)),
        w_send=sem((len(plans) + 1, ndim)), w_recv=sem((len(plans) + 1, ndim)), s2_send=sem((2,)), s2_recv=sem((2,)),
        xs=strip, gbuf=strip, spill=mem((2, LEAD, features), f32), small=mem((32, 128), f32),
        small_bufs=mem((2, ndim, 32, 128), f32), total=mem((features, features), f32),
    )
    scratch["early_own"] = [mem((2, 2, 2) + block) for block in blocks[:3]]
    scratch["late"] = [mem((2,) * ndim + own)] * 3
    scratch["bufs"] = [stream_scratch(len(kept), order, *block) for (kept, order), block in zip(plans, blocks)]
    return call(functools.partial(back_kernel, shards, axes, plans), 6, ins, outs, scratch)


def label_features(line, unlike):
    rows = [(line != k if unlike else line == k).astype(jnp.float32) for k in range(8)]
    return slim(jnp.concatenate(rows + [jnp.zeros((120, line.shape[1]), jnp.float32)], axis=0).T)


class Line:
    def __init__(self, place, src, dst, send_sem, recv_sem):
        self.place, self.src, self.dst, self.send_sem, self.recv_sem = place, src, dst, send_sem, recv_sem

    def copy(self, step, slot):
        group = self.place.group
        return remote(
            self.src.at[(group + step) % GROUPS], self.dst.at[slot], self.send_sem.at[step], self.recv_sem.at[step],
            self.place.other_group(step),
        )

    def keep(self):
        group = self.place.group
        return pltpu.make_async_copy(self.src.at[group], self.dst.at[group], self.send_sem.at[0])

    def start(self, steps=(1, 3, 2)):
        for step in steps:
            self.copy(step, self.place.group).start()

    def wait(self, step):
        self.copy(step, (self.place.group - step + GROUPS) % GROUPS).wait()

    def wait_all(self):
        for step in (1, 3, 2):
            self.wait(step)
        self.keep().wait()

    def gone(self, step):
        self.copy(step, self.place.group).wait_send()

    def come_all(self):
        for step in (1, 3, 2):
            self.copy(step, (self.place.group - step + GROUPS) % GROUPS).wait_recv()
        self.keep().wait()


def near_slot(place, chunk, t):
    first = (chunk * place.rest_size + place.rest) * TQ
    return jnp.clip(t - (first // TK - 1 + place.rest % 2) + 1, 0, 3)


class RowForward:
    def __init__(self, place, r):
        self.place, self.r, self.heads = place, r, r.lse.shape[1]
        self.table = BiasTable(r.table, place, self.heads)

    def clear(self):
        self.r.acc[...] = jnp.zeros_like(self.r.acc)
        self.r.mx[...] = jnp.full_like(self.r.mx, FIRST_MAX)

    def queries(self, chunk):
        r = self.r
        for h, tile in enumerate(spread_lanes(r.q_all[chunk], False)):
            r.qp[chunk, h] = jnp.concatenate([tile, r.ql[chunk]], axis=1)

    def tile(self, t):
        r = self.r
        rows = pl.ds(pl.multiple_of(t * TK, TK), TK)
        keys = lambda h: r.kv_all[rows, h * 128 : h * 128 + 128]
        for h in range(self.heads):
            r.vt[h, 0:64] = keys(h).T[64:128]
            r.vt[h, 64:80] = jnp.ones((16, TK), jnp.bfloat16)

        def scores(i, h):
            return mxu(jnp.concatenate([keys(h), r.kl[rows, :]], axis=1), r.qp[i, h], NT)

        def finish(i, h, s, b):
            m_old = r.mx[i, h]
            m_new = jnp.maximum(m_old, jnp.max(s, axis=0, keepdims=True) + b)
            p = jnp.exp(s - (m_new - b)).astype(jnp.bfloat16)
            r.mx[i, h] = m_new
            r.acc[i, h] = r.acc[i, h] * jnp.exp(m_old - m_new) + mxu(r.vt[h], p)

        def part(i, _):
            slot = near_slot(self.place, i, t)
            away = jnp.logical_or(slot == 0, slot == 3)

            @pl.when(away)
            def _():
                found = [scores(i, h) for h in range(self.heads)]
                for h in range(self.heads):
                    finish(i, h, found[h], jnp.where(slot == 0, self.table[h, 15], self.table[h, 31]))

            @pl.when(jnp.logical_not(away))
            def _():
                for h in range(self.heads):
                    finish(i, h, scores(i, h) + r.near[h, slot - 1].astype(jnp.float32), 0.0)

            return 0

        def pair(p, _):
            slots = [near_slot(self.place, 2 * p + k, t) for k in range(2)]
            far = [jnp.logical_or(slot == 0, slot == 3) for slot in slots]
            both = jnp.logical_and(far[0], far[1])

            @pl.when(both)
            def _():
                items = [(2 * p + k, h, jnp.where(slots[k] == 0, self.table[h, 15], self.table[h, 31])) for h in range(self.heads) for k in range(2)]
                found = [scores(i, h) for i, h, _ in items]
                for (i, h, b), s in zip(items, found):
                    finish(i, h, s, b)

            @pl.when(jnp.logical_not(both))
            def _():
                lax.fori_loop(2 * p, 2 * p + 2, part, 0)

            return 0

        lax.fori_loop(0, GROUPS // 2, pair, 0)

    def end(self):
        r = self.r

        def one(i, _):
            parts = []
            for h in range(self.heads):
                total = r.acc[i, h, 64:65, :]
                parts.append((r.acc[i, h, 0:64, :] / total).T)
                r.lse[i, h] = r.mx[i, h] + jnp.log(total)
            joined = join_heads(parts)
            r.o[i] = joined.astype(jnp.bfloat16)
            r.keep[i] = joined
            return 0

        lax.fori_loop(0, GROUPS, one, 0)


def label_taps(place, own, left, right):
    at_left, at_right = place.blk == 0, place.blk == place.shards - 1
    even, odd = jnp.concatenate([own[0:1], own[1:2]], axis=1), jnp.concatenate([own[2:3], own[3:4]], axis=1)
    none = jnp.full((1, 1), -1, jnp.int32)
    before = [jnp.where(at_left, none, left[row : row + 1, 127:128]) for row in (1, 3)]
    after = [jnp.where(at_right, none, right[row : row + 1, 0:1]) for row in (0, 2)]
    join = lambda *parts: jnp.concatenate(parts, axis=1)
    return [
        join(none, before[1], odd[:, :-2]), join(before[0], even[:, :-1]), join(before[1], odd[:, :-1]), even, odd,
        join(even[:, 1:], after[0]), join(odd[:, 1:], after[1]), join(even[:, 2:], after[0], none),
    ]


def front_kernel(shards, scale, r):
    place = Place(shards)
    tokens = r.kv.shape[1]
    y, core = bit(place.rest, 2), place.rest % 2
    core_to, across = place.other_rest(1), place.other_rest(2)
    peers = [(place.dp, (place.blk + step) % shards) for step in range(1, shards)]
    met = hail(peers)
    length = r.x.shape[0]

    def label_copy(step, block):
        return remote(r.label, r.labels_all.at[block], r.lab_send.at[step], r.lab_recv.at[step], peers[step - 1])

    def label_come(step):
        back = (place.blk + shards - step) % shards
        label_copy(step, back).wait_recv()
        return r.labels_all[back]

    lane = lax.broadcasted_iota(jnp.int32, (128, 128), 0)
    to = lax.broadcasted_iota(jnp.int32, (128, 128), 1)
    apart = (lane == jnp.where(to < 64, 2 * to, 2 * to - 127)).astype(jnp.float32).astype(jnp.bfloat16)
    flat = jnp.concatenate([r.segments[0:1, j * 128 : j * 128 + 128] for j in range(4)] + [jnp.zeros((4, 128), jnp.int32)], axis=0)
    flat = mxu(flat.astype(jnp.float32).astype(jnp.bfloat16), apart).astype(jnp.int32)
    for j, (row, cols) in enumerate(((0, slice(0, 64)), (2, slice(0, 64)), (0, slice(64, 128)), (2, slice(64, 128)))):
        r.label[j : j + 1, :] = jnp.concatenate([flat[row : row + 1, cols], flat[row + 1 : row + 2, cols]], axis=1)
    r.label[4:8, :] = jnp.zeros((4, 128), jnp.int32)
    r.labels_all[place.blk] = r.label[...]
    await_all(met)
    halo = [
        remote(r.x.at[pl.ds(0, 16)], r.after, r.x_send.at[0], r.x_recv.at[0], peers[shards - 2]),
        remote(r.x.at[pl.ds(length - 16, 16)], r.before, r.x_send.at[1], r.x_recv.at[1], peers[0]),
    ]
    for copy in halo:
        copy.start()
    for step in [1, shards - 1] + list(range(2, shards - 1)):
        label_copy(step, place.blk).start()
    weights = [pltpu.make_async_copy(src, dst, r.w_sem.at[k]) for k, (src, dst) in enumerate(((r.wq_hbm, r.wq), (r.wk_hbm, r.wk), (r.wv_hbm, r.wv)))]
    for copy in weights:
        copy.start()
    work = RowForward(place, r)
    make_bias(work.table, core, r.near, (0,))
    left, right = label_come(1), label_come(shards - 1)
    taps = label_taps(place, r.label[...], left, right)
    for j in range(8):
        r.labels[j : j + 1, :] = taps[j]
    for copy in halo:
        copy.wait()
    load_bytes(r.x, r.before[14:16, :], r.after[0:2, :], r.xs)
    r.hidden[...], n1 = pool_tokens(scale, r.xs, taps, row_of(r.vectors, 0).astype(jnp.bfloat16), row_of(r.vectors, 1), tokens, r.y, r.share)
    r.n1[...] = n1
    for copy in weights:
        copy.wait()
    put_packed(mxu(n1, r.wq[...]).astype(jnp.bfloat16) * jnp.bfloat16(0.125), r.q)
    queries = Line(place, r.q, r.q_all, r.q_send, r.q_recv)
    queries.keep().start()
    queries.start()
    put_pairs(mxu(n1, r.wk[...]).astype(jnp.bfloat16), mxu(n1, r.wv[...]).astype(jnp.bfloat16), r.kv)

    def held(dz, off, core_off):
        rest = flipped(place.rest, 2) if off else place.rest
        rest = flipped(rest, 1) if core_off else rest
        start = pl.multiple_of(place.chunk((place.group + dz) % GROUPS, rest) * tokens, tokens)
        return r.kv_all.at[pl.ds(start, tokens)]

    def sem_of(dz, off, core_off):
        return r.kv_recv.at[(core_off * 2 + off) * GROUPS + dz]

    waits = []

    def send(src, dz, off, came, target):
        copy = remote(src, held(dz, off, 0), r.kv_send.at[len(waits)], sem_of(*came), target)
        copy.start()
        waits.append(copy)

    def arrived(dz, off, core_off=0):
        here = held(dz, off, core_off)
        remote(here, here, r.kv_send.at[0], sem_of(dz, off, core_off), core_to).wait_recv()

    def pass_on(dz, off):
        mine = dz == 0 and off == 0
        if not mine:
            arrived(dz, off)
        src = r.kv.at[place.group] if mine else held(dz, off, 0)
        if not off:
            send(src, dz, off, (dz, 1, 0), across)
        send(src, dz, off, (dz, off, 1), core_to)

    def along(step):
        copy = remote(r.kv.at[(place.group + step) % GROUPS], held(0, 0, 0), r.z_send.at[step], sem_of((GROUPS - step) % GROUPS, 0, 0), place.other_group(step))
        copy.start()
        return copy

    left_over = []

    def leave(src, dst):
        copy = pltpu.make_async_copy(src, dst, r.out_sem.at[len(left_over)])
        copy.start()
        left_over.append(copy)

    def line_of(block):
        return jnp.concatenate([block[0:1], block[1:2]], axis=1)

    def tile(dz, off):
        group = (place.group + dz) % GROUPS
        for c in range(2):
            number = place.chunk(group, (1 - y if off else y) * 2 + c)
            rows = pl.ds(pl.multiple_of(number * tokens, tokens), tokens)
            r.kl[rows, :] = label_features(line_of(r.labels_all[number]), True)
        arrived(dz, off, 1)
        t = group * 2 + (1 - y if off else y)
        rows = pl.ds(pl.multiple_of(t * TK, TK), TK)
        leave(r.kv_all.at[rows], r.kv_out.at[rows])
        leave(r.kl.at[rows], r.kl_out.at[rows])
        work.tile(t)

    leave(r.hidden, r.hidden_out)
    leave(r.n1, r.n1_out)
    own = pltpu.make_async_copy(r.kv.at[place.group], held(0, 0, 0), r.own_sem)
    own.start()
    pass_on(0, 0)
    make_bias(work.table, core, r.near, (1,))
    leave(r.near, r.near_out)
    work.clear()
    for step in range(2, shards - 1):
        label_copy(step, (place.blk + shards - step) % shards).wait_recv()
    for z in range(GROUPS):
        r.ql[z] = label_features(line_of(r.labels_all[place.chunk(z, place.rest)]), False) * jnp.bfloat16(NEG)
    pass_on(0, 1)
    for step in (1, 3, 2):
        queries.gone(step)
    first = [along(1), along(3)]
    queries.come_all()
    for z in range(GROUPS):
        work.queries(z)
    own.wait()
    tile(0, 0)
    for copy in first:
        copy.wait_send()
    last = along(2)
    pass_on(1, 0)
    pass_on(3, 0)
    tile(0, 1)
    tile(1, 0)
    pass_on(1, 1)
    pass_on(3, 1)
    tile(3, 0)
    tile(1, 1)
    pass_on(2, 0)
    tile(3, 1)
    pass_on(2, 1)
    tile(2, 0)
    tile(2, 1)
    last.wait_send()
    work.end()
    for copy in waits:
        copy.wait_send()
    for step in range(1, shards):
        label_copy(step, place.blk).wait_send()
    for copy in left_over:
        copy.wait()


def front(shards, scale, table, x, segments, vectors, wq, wk, wv):
    length, features = x.shape
    tokens, heads = length // 2, features // 64 // GROUPS
    width = heads * 128
    sem, f32, low = pltpu.SemaphoreType.DMA, jnp.float32, jnp.bfloat16
    mem = lambda shape, dtype=low: pltpu.VMEM(shape, dtype)
    packed = (GROUPS, tokens * 3 // 2, 128)
    ins = dict(
        table=Held(table, pltpu.SMEM), x=x, segments=segments, vectors=vectors,
        wq_hbm=Held(wq, pl.ANY), wk_hbm=Held(wk, pl.ANY), wv_hbm=Held(wv, pl.ANY),
    )
    outs = dict(
        q_all=(packed, low), kv_out=((shards * tokens, width), low, pl.ANY), kl_out=((shards * tokens, 128), low, pl.ANY), ql=((GROUPS, tokens, 128), low),
        near_out=((heads, 2, TK, TQ), low, pl.ANY), o=(packed, low), keep=(packed, f32), lse=((GROUPS, heads, 1, TQ), f32),
        hidden_out=((tokens, features), f32, pl.ANY), n1_out=((tokens, features), low, pl.ANY), y=((8, tokens), f32), share=((1, 128), f32),
        labels=((8, tokens), jnp.int32), before=((16, features), low), after=((16, features), low),
    )
    scratch = dict(
        kv_all=mem((shards * tokens, width)), kl=mem((shards * tokens, 128)), near=mem((heads, 2, TK, TQ)),
        hidden=mem((tokens, features), f32), n1=mem((tokens, features)), out_sem=sem((19,)),
        q=mem(packed), kv=mem((GROUPS, tokens, width)), xs=mem((features // 128, length + 2 * LEAD, 128), f32),
        wq=mem(wq.shape), wk=mem(wk.shape), wv=mem(wv.shape), label=mem((8, 128), jnp.int32), labels_all=mem((shards, 8, 128), jnp.int32),
        qp=mem((GROUPS, heads, TQ, 256)), acc=mem((GROUPS, heads, 80, TQ), f32), mx=mem((GROUPS, heads, 1, TQ), f32), vt=mem((heads, 80, TK)),
        q_send=sem((4,)), q_recv=sem((4,)), kv_send=sem((12,)), z_send=sem((GROUPS,)), kv_recv=sem((16,)), own_sem=sem,
        lab_send=sem((shards,)), lab_recv=sem((shards,)), x_send=sem((2,)), x_recv=sem((2,)), w_sem=sem((3,)),
    )
    return call(functools.partial(front_kernel, shards, scale), 7, ins, outs, scratch)


def middle_kernel(shards, r):
    place = Place(shards)
    met = hail([place.other_group(step) for step in (1, 2, 3)] + [place.other_rest(1)])
    pairs = ((r.wo_hbm, r.wo), (r.wg_hbm, r.wg), (r.wu_hbm, r.wu), (r.wd_hbm, r.wd))
    fetches = [pltpu.make_async_copy(src, dst, r.w_sem.at[k]) for k, (src, dst) in enumerate(pairs)]
    for copy in fetches:
        copy.start()
    await_all(met)
    home = Line(place, r.o, r.o_home, r.o_send, r.o_recv)
    home.keep().start()
    home.start()
    for copy in fetches:
        copy.wait()
    home.wait_all()
    r.gain[...] = row_of(r.vectors, 2)
    feed_kernel(r.o_home, r.hidden, r.ct, r.gain, r.wo, r.wg, r.wu, r.wd, r.block_out, r.dres, r.da, r.dgain,
                r.n2, r.att, r.act, r.dg, r.du, r.db, r.acc, r.dn2)
    away = Line(place, r.da, r.do, r.q_send, r.q_recv)
    away.keep().start()
    away.start()
    feed_weights(place, r.n2, r.att, r.act, r.dg, r.du, r.ct, r.db, r.sums, r.sums_out, r.out_sem,
                 r.core_send, r.core_recv, r.gate, r.up, r.down, r.out, r.wide_out, r.slim_out, r.wide_in, r.slim_in)
    away.wait_all()


def middle(shards, o_packed, hidden, ct, vectors, wo, wg, wu, wd):
    tokens, width = hidden.shape
    ff = wg.shape[1]
    per, per_ff = width // 32, ff // 32
    sem, low, f32 = pltpu.SemaphoreType.DMA, jnp.bfloat16, jnp.float32
    half = o_packed.shape[1:]
    wide_cols = ff + width // 2
    first = (wide_cols // 256 + 1) * 128
    blocks = [(16, 2 * per, first), (16, 2 * per, wide_cols - first), (16, per_ff, width)]
    ins = dict(o=o_packed, hidden=hidden, ct=ct, vectors=vectors, wo_hbm=Held(wo, pl.ANY), wg_hbm=Held(wg, pl.ANY), wu_hbm=Held(wu, pl.ANY), wd_hbm=Held(wd, pl.ANY))
    outs = dict(
        block_out=((tokens, width), low), dres=((tokens, width), f32), dgain=((1, width), f32), do=((GROUPS,) + half, low),
        sums_out=[(block, low, pl.ANY) for block in blocks],
    )
    mem = lambda shape, dtype=low: pltpu.VMEM(shape, dtype)
    scratch = dict(
        gain=mem((1, width), f32), o_home=mem((GROUPS,) + half), da=mem((GROUPS,) + half),
        n2=mem((tokens, width)), att=mem((tokens, width)), db=mem((tokens, width)),
        act=mem((tokens, ff)), dg=mem((tokens, ff)), du=mem((tokens, ff)),
        acc=mem((tokens, width), f32), dn2=mem((tokens, width), f32),
        wo=mem(wo.shape), wg=mem(wg.shape), wu=mem(wu.shape), wd=mem(wd.shape),
        gate=mem((width, ff), f32), up=mem((width, ff), f32), down=mem((ff, width), f32), out=mem((width, width), f32),
        wide_out=mem((16, 2 * per, wide_cols)), slim_out=mem((16, per_ff, width)),
        wide_in=mem((16, 2 * per, wide_cols)), slim_in=mem((16, per_ff, width)),
        w_sem=sem((4,)), o_send=sem((4,)), o_recv=sem((4,)), q_send=sem((4,)), q_recv=sem((4,)),
        core_send=sem((8,)), core_recv=sem((8,)), sums=[mem(block) for block in blocks], out_sem=sem((12,)),
    )
    return call(functools.partial(middle_kernel, shards), 8, ins, outs, scratch)


def neighbours(rows):
    peers = lax.axis_size("blk")
    up = [(i, i + 1) for i in range(peers - 1)]
    last, leading = rows
    return lax.ppermute(last, "blk", up), lax.ppermute(leading, "blk", [(j, i) for i, j in up])


def body(
    byte_embeds,
    segments,
    score_weight,
    norm_gain1,
    w_query,
    w_key,
    w_value,
    w_out,
    rel_bias,
    norm_gain2,
    w_gate,
    w_up,
    w_down,
    cotangent,
):
    row_count, length, width = byte_embeds.shape
    tokens = length // 2
    shards = lax.axis_size("blk")
    shape = {"dp": lax.axis_size("dp"), "blk": shards}
    devices = shards * shape["dp"]
    heads = rel_bias.shape[1] // GROUPS
    position = lax.axis_index("blk")
    rest_size = shards // GROUPS
    group, rest = position // rest_size, position % rest_size
    row = lax.axis_index("dp") % 2
    x, ids_here = byte_embeds[0], segments[0]

    ct = cotangent[0]
    scale = 1.0 / (row_count * length * devices)
    if devices == 32:
        vectors = jnp.concatenate([score_weight, norm_gain1, norm_gain2]).astype(jnp.float32).reshape(-1, 128)
        table = rel_bias.T.astype(jnp.float32)
        got = front(shards, scale, table, x, segments, vectors, w_query, w_key, w_value)
        mid = middle(shards, got.o, got.hidden_out, ct, vectors, w_out, w_gate, w_up, w_down)
        block_out, d_res, d_gain2 = mid.block_out, mid.dres, mid.dgain
        last = back_and_last(
            shape,
            mid.sums_out,
            dict(
                table=Held(table, pltpu.SMEM), q=got.q_all, do=mid.do, keep=got.keep, kv_hbm=Held(got.kv_out, pl.ANY),
                kl_hbm=Held(got.kl_out, pl.ANY), ql=got.ql, bias=got.near_out, lse=got.lse,
                hidden_hbm=Held(got.hidden_out, pl.ANY), dres_hbm=Held(d_res, pl.ANY), n1_hbm=Held(got.n1_out, pl.ANY), x_hbm=Held(x, pl.ANY), before=got.before, after=got.after,
                labels=got.labels, y=got.y, vectors=vectors,
                wq_hbm=Held(w_query, pl.ANY), wk_hbm=Held(w_key, pl.ANY), wv_hbm=Held(w_value, pl.ANY), dgain2=d_gain2, share=got.share,
            ),
        )
        grad_bytes, edge, spill, small, sums = last.gb, last.edge, last.spill_out, last.small_out, last.sums
    else:
        marks = (ids_here + 1).astype(jnp.bfloat16)
        with_marks = lambda part, two: jnp.concatenate([part, jnp.pad(two, (0, width - 2))[None]], axis=0)
        before, after = neighbours((with_marks(x[-2:], marks[-2:]), with_marks(x[:2], marks[:2])))
        line = jnp.concatenate([before[2, :2], marks, after[2, :2]])
        line = jnp.pad(line, (1, 1)).astype(jnp.int32).reshape(tokens + 3, 2).T
        labels = jnp.stack([line[j % 2, j // 2 : j // 2 + tokens] for j in range(8)])

        score_row, gain1, gain2 = score_weight[None], norm_gain1[None], norm_gain2[None]
        hidden, n1, y, share, q_packed, kv_parts = pool_and_project(
            shards, scale, x, before, after, labels, score_row, gain1, w_query, w_key, w_value
        )

        label_block = jnp.pad(ids_here[0::2].reshape(tokens // 128, 128), ((0, 8 - tokens // 128), (0, 0)), constant_values=-1)
        table = lax.dynamic_slice_in_dim(rel_bias.astype(jnp.float32).T, group * heads, heads, 0)
        q_all, kv_all, labels_all = gather_all(shards, q_packed, kv_parts, label_block)
        labels_all = labels_all.reshape(2, shards, 8, 128)[:, :, : tokens // 128].reshape(2, shards * tokens)
        ids = jnp.arange(8, dtype=jnp.int32)
        counts = jnp.sum((labels_all[:, None, :] == ids[None, :, None]).astype(jnp.int32), axis=2)
        ends = jnp.sum(jnp.where(ids[None, :] <= ids[:, None], counts[:, None, :], 0), axis=2)
        begins = ends - counts
        query_labels = jnp.stack(
            [lax.dynamic_slice_in_dim(labels_all, ((2 * row + i) * rest_size + rest) * tokens, tokens, 1) for i in range(2)],
            axis=1,
        )
        chosen = query_labels[:, :, None, :] == ids[None, None, :, None]
        span = jnp.stack(
            [jnp.sum(jnp.where(chosen, edge[:, None, :, None], 0), axis=2) for edge in (begins, ends)], axis=2
        )
        parity = rest % 2
        firsts = jnp.stack([((2 * row + i) * rest_size + rest) * tokens for i in range(2)])
        near = jnp.broadcast_to((firsts // TK - 1 + parity)[None], (2, 2))
        bounds = jnp.stack(
            [
                jnp.min(span[:, :, 0], axis=-1) // TK,
                -(-jnp.max(span[:, :, 1], axis=-1) // TK),
                near,
                -(-jnp.max(span[:, :, 0], axis=-1) // TK),
                jnp.min(span[:, :, 1], axis=-1) // TK,
                jnp.broadcast_to(parity, (2, 2)),
                jnp.broadcast_to((labels_all[0, -1] > 0).astype(jnp.int32), (2, 2)),
            ],
            axis=-1,
        ).astype(jnp.int32)
        o_packed, o_kept, log_total, near_bias = attention(bounds, table, q_all, kv_all, span)
        o_home = move_heads(return_kernel, (GROUPS,), shards, 4, o_packed)
        block_out, d_res, da_packed, d_gain2, n2, att, act, d_gate, d_up, d_branch = feed_forward(
            o_home, hidden, ct, gain2, w_out, w_gate, w_up, w_down
        )
        do_all = move_heads(spread_kernel, (2, 2), shards, 5, da_packed)
        dq_packed, dkv_all, _, _, _, d_table_lanes = attention_back(
            False, bounds, table, q_all, do_all, o_kept, kv_all, near_bias, span, log_total
        )
        dq_home, dkv_home = reduce_all(shape, dq_packed, dkv_all, [], [])
        grad_bytes, edge, spill, small, last_parts = last_part(
            shape, dq_home, dkv_home, hidden, d_res, x, before, after, labels, y,
            score_row, gain1, w_query, w_key, w_value, d_gain2, share, d_table_lanes,
        )
        sums = []
    per = width // devices
    block_out, grad_bytes, g_score, g_gain1, g_gain2, g_bias, shares, *grads = finish(
        shards, rel_bias.shape[1], per, w_gate.shape[1], block_out, grad_bytes, edge, spill, small, sums
    )
    if devices != 32:
        product = lambda left, right: jnp.einsum("td,te->de", left, right, preferred_element_type=jnp.float32)
        grads = [product(n1, last_parts[j]) for j in range(3)]
        grads += [product(att, d_branch), product(n2, d_gate), product(n2, d_up), product(act, ct)]
        grads = [lax.psum_scatter(grad, ("dp", "blk"), scatter_dimension=0, tiled=True) for grad in grads]
    return (
        block_out[None],
        grad_bytes[None],
        g_score,
        g_gain1,
        *grads[:4],
        g_bias.T,
        g_gain2,
        *grads[4:],
        shares,
    )


def solution(mesh):
    placed = (
        P("dp", "blk", None),
        P("dp", "blk"),
        P(),
        P(),
        P(),
        P(),
        P(),
        P(),
        P(),
        P(),
        P(),
        P(),
        P(),
        P("dp", "blk", None),
    )
    return jax.shard_map(
        body,
        mesh=mesh,
        in_specs=placed,
        out_specs=(
            P("dp", "blk", None),
            P("dp", "blk", None),
            P(),
            P(),
            P(("dp", "blk"), None),
            P(("dp", "blk"), None),
            P(("dp", "blk"), None),
            P(("dp", "blk"), None),
            P(),
            P(),
            P(("dp", "blk"), None),
            P(("dp", "blk"), None),
            P(("dp", "blk"), None),
            P(),
        ),
        check_vma=False,
    )
```
